32 devices in a mesh: dp: 8 (over z, y), section: 4 (over x, core).
Axes of the slice: x: 2, y: 2, z: 4, core: 2. Of those that a mesh axis runs over, the one named last changes fastest.
Arguments:
- char_ids: int32 [64, 35, 21], P('dp'), may hold values from 0 to 50
- target_ids: int32 [64, 35], P('dp'), may hold values from 0 to 9999
- remaining: int32 [64], P('dp'), may hold values from 1 to 279
- resets: int32 [64, 35], P('dp'), may hold values 0 or 1
- start_state: float32 [2, 2, 64, 650], P(None, None, 'dp'), may hold values from -3 to 3
- section_params: bfloat16 [4, 6512640], P('section'), may hold values from -3 to 3, as said below
Outputs:
- mean_loss: float32 [], replicated
- param_grads: float32 [4, 6512640], P('section', 'dp')
- gate_bias_grad: float32 [1100], replicated
The draws below stay inside these ranges and needn't reach their ends.
Inputs may be any that keep to these rules, and one draw needn't show every extreme that they name: `section_params`: row s holds section s's parameters laid out as the steps give; entries after them are zero.
All inputs are finite; a program needn't handle non-finite values. No bound on the sum of `resets` on one device may be relied on, other than what follows from the above.
Results may differ from the reference program's by a relative error of at most 0.007.
Values may be sent and summed in bfloat16 or wider, within the bound.
A program may use at most 256 MiB of HBM per device.

```python
import math
import jax
import jax.numpy as jnp
import numpy as np
from jax import lax

D_CHAR = 15
CHAR_V = 51
WORD_CHARS = 21
F_UNIT = 50
HID = 650
VOCAB = 10000
STEPS = 35
FILT = 1100
ROWS_ALL = 64
PACKED = 6512640


def section_shapes_drawn(section_number):
    if section_number == 0:
        shapes = [(CHAR_V, D_CHAR)]
        for kernel_width in range(1, 8):
            channels = F_UNIT * min(kernel_width, 4)
            shapes = shapes + [(kernel_width * D_CHAR, channels), (channels,)]
        for layer_index in range(2):
            shapes = shapes + [(FILT, FILT), (FILT,), (FILT, FILT), (FILT,)]
        return shapes
    if section_number == 1:
        return [(FILT, 4 * HID), (HID, 4 * HID), (4 * HID,)]
    if section_number == 2:
        return [(HID, 4 * HID), (HID, 4 * HID), (4 * HID,)]
    return [(HID, VOCAB), (VOCAB,)]


def scale_list(section_number):
    if section_number == 0:
        scales = [1.0]
        for kernel_width in range(1, 8):
            scales = scales + [(kernel_width * D_CHAR) ** (-0.5), 0.5]
        scales = scales + [FILT ** (-0.5), 0.5, FILT ** (-0.5), 0.5] * 2
        return scales
    if section_number == 1:
        return [(FILT + HID) ** (-0.5), (FILT + HID) ** (-0.5), 0.5]
    if section_number == 2:
        return [(2 * HID) ** (-0.5), (2 * HID) ** (-0.5), 0.5]
    return [3.0 * HID ** (-0.5), 0.5]


def draw_section_params(key, part):
    key = jax.random.fold_in(key, 11)
    rows_list = []
    for section_number in range(4):
        pieces = []
        for piece_shape, factor in zip(section_shapes_drawn(section_number), scale_list(section_number)):
            pieces.append(jnp.full((math.prod(piece_shape),), factor, jnp.float32))
        scale_row = jnp.concatenate(pieces)
        scale_row = jnp.pad(scale_row, (0, PACKED - scale_row.shape[0]))
        section_key = jax.random.fold_in(key, section_number)
        noise = jnp.clip(jax.random.normal(section_key, (PACKED,), jnp.float32), -3.0, 3.0)
        rows_list.append(noise * scale_row)
    return jnp.stack(rows_list).astype(jnp.bfloat16)


def with_ends(drawn, rng, least, high):
    dims = drawn.shape
    place = [jax.random.randint(jax.random.fold_in(rng, axis), (), 0, dims[axis]) for axis in range(len(dims))]
    drawn = drawn.at[tuple(place)].set(least)
    longest = dims.index(max(dims))
    place[longest] = (place[longest] + 1) % dims[longest]
    return drawn.at[tuple(place)].set(high)


def levels(rng, dims, cuts, smallest, high):
    gain, own = 1.0, jax.random.fold_in(rng, 6)
    for axis_at, parts in cuts:
        heights = jnp.exp(jax.random.uniform(jax.random.fold_in(own, axis_at), (parts,), jnp.float32, smallest / len(cuts), high / len(cuts)))
        gain = gain * jnp.repeat(heights, dims[axis_at] // parts).reshape([-1 if axis == axis_at else 1 for axis in range(len(dims))])
    return gain


def rank_bounds(number_of, skew):
    weights = [(1 << 20) // math.isqrt(standing ** skew) + 1 for standing in range(1, number_of + 1)]
    spread = 1 + sum(weights) // (1 << 30)
    return np.cumsum(np.array([max(1, weight // spread) for weight in weights]))


def ranked(key, dims, number_of, skew):
    grid = rank_bounds(number_of, skew)
    ticket = jax.random.randint(jax.random.fold_in(key, 1), dims, 0, int(grid[number_of - 1]))
    grade = jnp.searchsorted(jnp.asarray(grid, jnp.int32), ticket, side="right")
    return jax.random.permutation(jax.random.fold_in(key, 2), number_of)[grade].astype(jnp.int32)


def scatter_about(key, extent, scale, most, shards=(), kind=jnp.bfloat16):
    drawn = scale * jax.random.normal(key, extent, jnp.float32)
    if shards:
        drawn = drawn * levels(key, extent, shards, -0.22, 0.18)
    return jnp.clip(drawn, -most, most).astype(kind)


def setup_inputs(seed: int = 0) -> dict:
    splits = jax.random.split(jax.random.key(seed), 7)
    return {
        "char_ids": with_ends(jax.random.randint(splits[0], (ROWS_ALL, STEPS, WORD_CHARS), 0, CHAR_V), jax.random.fold_in(splits[0], 1), 0, CHAR_V - 1).astype(jnp.int32),
        "target_ids": with_ends(ranked(splits[1], (ROWS_ALL, STEPS), VOCAB, 2), jax.random.fold_in(splits[1], 3), 0, VOCAB - 1).astype(jnp.int32),
        "remaining": with_ends(jax.random.randint(splits[2], (ROWS_ALL,), 1, 8 * STEPS), jax.random.fold_in(splits[2], 1), 1, (8 * STEPS) - 1).astype(jnp.int32),
        "resets": with_ends((jax.random.randint(splits[3], (ROWS_ALL, STEPS), 0, 35) < 1).astype(jnp.int32), jax.random.fold_in(splits[3], 1), 0, 1),
        "start_state": scatter_about(splits[4], (2, 2, ROWS_ALL, HID), 0.5, 3.0, ((2, 8),), jnp.float32),
        "section_params": draw_section_params(jax.random.fold_in(splits[6], 71), 0),
    }


@jax.custom_vjp
def low(v):
    return lax.optimization_barrier(v.astype(jnp.bfloat16)).astype(jnp.float32)

@jax.custom_vjp
def low_back(v):
    return v

def low_keep(v):
    return (low(v), None)

def low_pass(kept, grad):
    return (grad,)

def back_keep(v):
    return (v, None)

def back_low(kept, grad):
    return (low(grad),)
low.defvjp(low_keep, low_pass)
low_back.defvjp(back_keep, back_low)

def section_shapes(section_number):
    if section_number == 0:
        shapes = [(CHAR_V, D_CHAR)]
        for kernel_width in range(1, 8):
            channels = F_UNIT * min(kernel_width, 4)
            shapes = shapes + [(kernel_width * D_CHAR, channels), (channels,)]
        for layer_index in range(2):
            shapes = shapes + [(FILT, FILT), (FILT,), (FILT, FILT), (FILT,)]
        return shapes
    if section_number == 1:
        return [(FILT, 4 * HID), (HID, 4 * HID), (4 * HID,)]
    if section_number == 2:
        return [(HID, 4 * HID), (HID, 4 * HID), (4 * HID,)]
    return [(HID, VOCAB), (VOCAB,)]

def piece_offset(section_number, piece_index):
    return sum((math.prod(piece_shape) for piece_shape in section_shapes(section_number)[:piece_index]))

def unpack(vector, section_number):
    pieces = []
    offset = 0
    for piece_shape in section_shapes(section_number):
        length = math.prod(piece_shape)
        pieces.append(vector[offset:offset + length].reshape(piece_shape))
        offset = offset + length
    return pieces

def char_network(pieces, word_chars):
    embedded = jnp.take(pieces[0], word_chars, axis=0)
    pooled = []
    for number in range(7):
        kernel_width = number + 1
        kernel = pieces[1 + 2 * number]
        bias_row = pieces[2 + 2 * number]
        positions = WORD_CHARS - kernel_width + 1
        windows = jnp.concatenate([embedded[:, offset:offset + positions, :] for offset in range(kernel_width)], axis=2)
        preact = low_back(jnp.einsum('wlk,kc->wlc', windows, kernel, precision=lax.Precision.HIGHEST) + bias_row)
        pooled.append(jax.nn.logsumexp(jnp.tanh(preact), axis=1) - math.log(positions))
    hidden_in = low(jnp.concatenate(pooled, axis=1))
    for layer_index in range(2):
        transform_weight, transform_bias, hidden_weight, hidden_bias = pieces[15 + 4 * layer_index:19 + 4 * layer_index]
        gate_value = jax.nn.sigmoid(low_back(jnp.dot(hidden_in, transform_weight, precision=lax.Precision.HIGHEST) + transform_bias))
        hidden_value = jax.nn.silu(low_back(jnp.dot(hidden_in, hidden_weight, precision=lax.Precision.HIGHEST) + hidden_bias))
        hidden_in = low(gate_value * hidden_value + (1.0 - gate_value) * hidden_in)
    return hidden_in

def lstm_layer(pieces, layer_in, start_hidden, start_cell, keep_mask):
    input_weight, recurrent_weight, bias_row = pieces
    projected = jnp.einsum('rtf,fg->trg', layer_in, input_weight, precision=lax.Precision.HIGHEST)

    def advance(loop_state, sliced):
        hidden_state, cell_state = loop_state
        proj_step, keep_step = sliced
        hidden_prev = hidden_state * keep_step[:, None]
        cell_prev = cell_state * keep_step[:, None]
        preact = low_back(proj_step + jnp.dot(hidden_prev, recurrent_weight, precision=lax.Precision.HIGHEST) + bias_row)
        quarter = preact.shape[1] // 4
        in_gate = jax.nn.sigmoid(preact[:, :quarter])
        forget_gate = jax.nn.sigmoid(preact[:, quarter:2 * quarter])
        out_gate = jax.nn.sigmoid(preact[:, 2 * quarter:3 * quarter])
        cell_input = jnp.tanh(preact[:, 3 * quarter:])
        cell_next = forget_gate * cell_prev + in_gate * cell_input
        hidden_next = low(out_gate * jnp.tanh(cell_next))
        return ((hidden_next, cell_next), hidden_next)
    ignored, hidden_seq = lax.scan(advance, (low(start_hidden), start_cell), (projected, keep_mask.T))
    return low_back(hidden_seq.transpose(1, 0, 2))

def output_total(pieces, hidden_seq, target_ids, valid_mask):
    output_weight, output_bias = pieces
    logits = low_back(jnp.einsum('rth,hv->rtv', hidden_seq, output_weight, precision=lax.Precision.HIGHEST) + output_bias)
    log_total = jax.nn.logsumexp(logits, axis=-1)
    picked = jnp.take_along_axis(logits, target_ids[:, :, None], axis=-1)[:, :, 0]
    return jnp.sum((log_total - picked) * valid_mask)

def reference(char_ids, target_ids, remaining, resets, start_state, section_params):
    params_float = section_params.astype(jnp.float32)
    keep_mask = 1.0 - resets.astype(jnp.float32)
    valid_mask = (jnp.arange(STEPS, dtype=jnp.int32)[None, :] < remaining[:, None]).astype(jnp.float32)
    row_count = char_ids.shape[0]
    word_chars = char_ids.reshape(row_count * STEPS, WORD_CHARS)

    def total_loss(params_all):
        features = low_back(char_network(unpack(params_all[0], 0), word_chars))
        layer_in = features.reshape(row_count, STEPS, FILT)
        for layer_index in range(2):
            layer_in = lstm_layer(unpack(params_all[layer_index + 1], layer_index + 1), layer_in, start_state[layer_index, 0], start_state[layer_index, 1], keep_mask)
        return output_total(unpack(params_all[3], 3), layer_in, target_ids, valid_mask)
    loss_sum, pull_back = jax.vjp(total_loss, params_float)
    gradients, = pull_back(jnp.ones((), jnp.float32))
    bias_start = piece_offset(0, 16)
    return (loss_sum / (row_count * STEPS), gradients, gradients[0, bias_start:bias_start + FILT])
```

```python
import functools
import math

import jax
import jax.numpy as jnp
from jax import lax
from jax.experimental import pallas as pl
from jax.experimental.pallas import tpu as pltpu
from jax.sharding import PartitionSpec as P

D_CHAR = 15
CHAR_V = 51
F_UNIT = 50
WORD_CHARS = 21
HID = 650
VOCAB = 10000
FILT = 1100
F32 = jnp.float32
BF16 = jnp.bfloat16

NFILT = [F_UNIT * min(k, 4) for k in range(1, 8)]
COLS = [sum(NFILT[:k]) for k in range(8)]
KOFF = [CHAR_V * D_CHAR + sum((j * D_CHAR + 1) * NFILT[j - 1] for j in range(1, k)) for k in range(1, 9)]
CONV_END = KOFF[7]
HIGH_STRIDE = FILT * (FILT + 1)
FW = 1152
GW = 768
ZW = 4 * GW
VW = 10112
LANE = 128
LENS = (2240, 2624, 2624, 5056)


def roll_lanes(x, shift):
    return pltpu.roll(x, shift, 1)


def lanes(rows=8):
    return lax.broadcasted_iota(jnp.int32, (rows, LANE), 1)


def sublanes():
    return lax.broadcasted_iota(jnp.int32, (8, LANE), 0)


def widen(raw, slot, rows, wide):
    def body(i, carry):
        piece = raw[slot, 0:1, pl.ds(pl.multiple_of(i * 8192, 8192), 8192)]
        wide[pl.ds(pl.multiple_of(i * 64, 64), 64), :] = piece.astype(F32).reshape(64, LANE)
        return carry

    lax.fori_loop(0, rows // 64, body, 0)


def stream_blocks(count, length, total, chunk_of, src, raw, sem, wide, work):
    def start_of(i):
        first = chunk_of(i)
        return jnp.minimum(first // 8 * 8, total - length)

    def copy(i, slot):
        at = pl.multiple_of(start_of(i) * LANE, 8 * LANE)
        return pltpu.make_async_copy(
            src.at[:, pl.ds(at, length * LANE)], raw.at[slot, :, pl.ds(0, length * LANE)], sem.at[slot]
        )

    copy(0, 0).start()

    def body(i, carry):
        slot = lax.rem(i, 2)

        @pl.when(i + 1 < count)
        def _():
            copy(i + 1, 1 - slot).start()

        copy(i, slot).wait()
        widen(raw, slot, length, wide)
        work(i, chunk_of(i) - start_of(i))
        return carry

    lax.fori_loop(0, count, body, 0)


def take_rows(wide, dest, first, shift, tiles, cols, stride, put, keep_row):
    turn = lax.rem(LANE - shift, LANE)
    split = lanes() < LANE - shift
    here = roll_lanes(wide[pl.ds(first, 8, stride=stride), :], turn)
    for c in range(tiles):
        after = roll_lanes(wide[pl.ds(first + c + 1, 8, stride=stride), :], turn)
        out = jnp.where(split, here, after)
        keep = keep_row
        if cols - c * LANE < LANE:
            keep = keep & (lanes() < cols - c * LANE)
        put(c, jnp.where(keep, out, 0.0))
        here = after


def unpack_kernel(
    src, km, e8, ab, ur, rt, wt, raw, wide, dest, kstage, stage0, stage1, stage_t, stage3, sem_in, sem_out, sem_t
):
    role = lax.axis_index("section")
    total = src.shape[1] // LANE

    def out_copy(stage, slot, target):
        return pltpu.make_async_copy(stage.at[slot], target, sem_out.at[slot])

    @pl.when(role == 0)
    def _():
        length = 640
        copy = pltpu.make_async_copy(
            src.at[:, pl.ds(0, length * LANE)], raw.at[0, :, pl.ds(0, length * LANE)], sem_in.at[0]
        )
        copy.start()
        copy.wait()
        widen(raw, 0, length, wide)
        lane1 = lanes(1)
        dest[pl.ds(0, 64), :] = jnp.zeros((64, LANE), F32)
        for a in range(CHAR_V):
            flat = D_CHAR * a
            q, s = flat // LANE, flat % LANE
            here = wide[q : q + 1, :]
            out = roll_lanes(here, (LANE - s) % LANE) if s else here
            if s + D_CHAR > LANE:
                out = jnp.where(lane1 < LANE - s, out, roll_lanes(wide[q + 1 : q + 2, :], LANE - s))
            dest[a : a + 1, :] = jnp.where(lane1 < D_CHAR, out, jnp.where(lane1 == D_CHAR, 1.0, 0.0))
        table = dest[pl.ds(0, 64), :]
        for m in range(8):
            kstage[pl.ds(64 * m, 64), pl.ds(0, LANE)] = (
                pltpu.roll(table, 16 * m, 1) if m else table
            ).astype(BF16)
        copy = pltpu.make_async_copy(kstage.at[pl.ds(0, 512), pl.ds(0, LANE)], e8, sem_out.at[0])
        copy.start()
        copy.wait()
        tiles = FW // LANE
        rows = 112
        dest[pl.ds(0, rows * tiles), :] = jnp.zeros((rows * tiles, LANE), F32)

        def kernel_row(k, i, row):
            n, base = NFILT[k - 1], COLS[k - 1]
            edge = KOFF[k - 1] + n * i - base
            q, s = edge // LANE, edge % LANE
            turn = lax.rem(LANE - s, LANE)
            first = base // LANE
            here = roll_lanes(wide[pl.ds(q + first, 1), :], turn)
            for ct in range(first, (base + n - 1) // LANE + 1):
                after = roll_lanes(wide[pl.ds(q + ct + 1, 1), :], turn)
                out = jnp.where(lane1 < LANE - s, here, after)
                at = pl.ds(ct * rows + row, 1)
                mask = (lane1 + ct * LANE >= base) & (lane1 + ct * LANE < base + n)
                dest[at, :] = jnp.where(mask, out, dest[at, :])
                here = after

        for k in range(1, 8):

            def offset_rows(o, carry, k=k):
                for d in range(D_CHAR):
                    kernel_row(k, o * D_CHAR + d, 16 * o + d)
                return carry

            lax.fori_loop(0, k, offset_rows, 0)
            kernel_row(k, jnp.int32(k * D_CHAR), 15)
        kstage[...] = jnp.zeros_like(kstage)
        for ct in range(tiles):
            kstage[pl.ds(112, rows), pl.ds(ct * LANE, LANE)] = dest[pl.ds(ct * rows, rows), :].astype(BF16)
        copy = pltpu.make_async_copy(kstage.at[pl.ds(0, 368)], km, sem_out.at[0])
        copy.start()
        copy.wait()

        blocks = 5

        def flat_of(i):
            return CONV_END + HIGH_STRIDE * (i // blocks)

        def chunk_of(i):
            return flat_of(i) // LANE + 2200 * lax.rem(i, blocks)

        def target(i):
            return ab.at[i // blocks, pl.ds(pl.multiple_of(lax.rem(i, blocks) * 256, 256), 256)]

        def work(i, extra):
            block = lax.rem(i, blocks)
            inner = lax.rem(flat_of(i), LANE)

            def rows_of(n, carry):
                flat = inner + FILT * n
                keep = 32 * (8 * block + sublanes()) + n <= FILT

                def put(c, value):
                    dest[pl.ds(256 * c + n, 8, stride=32), :] = value

                take_rows(wide, dest, flat // LANE + extra, lax.rem(flat, LANE), tiles, FILT, 275, put, keep)
                return carry

            lax.fori_loop(0, 32, rows_of, 0, unroll=2)
            slot = lax.rem(i, 2)

            @pl.when(i >= 2)
            def _():
                out_copy(stage0, slot, target(i - 2)).wait()

            for c in range(tiles):
                stage0[slot, :, pl.ds(c * LANE, LANE)] = dest[pl.ds(256 * c, 256), :].astype(BF16)
            out_copy(stage0, slot, target(i)).start()

        count = 4 * blocks
        stream_blocks(count, LENS[0], total, chunk_of, src, raw, sem_in, wide, work)
        for i in (count - 2, count - 1):
            out_copy(stage0, i % 2, target(i)).wait()

    for layer in (1, 2):

        @pl.when(role == layer)
        def _(layer=layer):
            depth = FILT if layer == 1 else HID
            blocks = -(-depth // 128)
            recurrent = depth * 4 * HID
            count = blocks + 6

            def chunk_of(i):
                return jnp.where(i < blocks, 2600 * i, recurrent // LANE + 2600 * (i - blocks))

            def target(i):
                at = jnp.where(i < blocks, i, i - blocks + 9)
                return ur.at[pl.ds(pl.multiple_of(at * 128, 128), 128)]

            def work(i, extra):
                inner = jnp.where(i < blocks, 0, recurrent % LANE)
                block = jnp.where(i < blocks, i, i - blocks)
                limit = jnp.where(i < blocks, depth, HID + 1)

                def rows_of(n, carry):
                    keep = 16 * (8 * block + sublanes()) + n < limit
                    for b in range(4):
                        flat = inner + 4 * HID * n + HID * b

                        def put(c, value, b=b):
                            dest[pl.ds(128 * (6 * b + c) + n, 8, stride=16), :] = value

                        take_rows(wide, dest, flat // LANE + extra, lax.rem(flat, LANE), 6, HID, 325, put, keep)
                    return carry

                lax.fori_loop(0, 16, rows_of, 0)
                slot = lax.rem(i, 2)

                @pl.when(i >= 2)
                def _():
                    out_copy(stage1, slot, target(i - 2)).wait()

                for c in range(24):
                    stage1[slot, :, pl.ds(c * LANE, LANE)] = dest[pl.ds(128 * c, 128), :].astype(BF16)
                out_copy(stage1, slot, target(i)).start()

                @pl.when(i >= blocks)
                def _():
                    @pl.when(i >= blocks + 2)
                    def _():
                        turned_copy(i - 2).wait()

                    k = LANE * block + lanes(LANE)
                    for c in range(24):
                        turned = jnp.transpose(dest[pl.ds(128 * c, 128), :])
                        stage_t[slot, pl.ds(128 * c, 128), :] = jnp.where(k < HID, turned, 0.0).astype(BF16)
                    turned_copy(i).start()

            def turned_copy(i):
                slot = lax.rem(i, 2)
                at = pl.multiple_of((i - blocks) * LANE, LANE)
                return pltpu.make_async_copy(stage_t.at[slot], rt.at[:, pl.ds(at, LANE)], sem_t.at[slot])

            stream_blocks(count, LENS[1], total, chunk_of, src, raw, sem_in, wide, work)
            for i in (count - 2, count - 1):
                out_copy(stage1, i % 2, target(jnp.int32(i))).wait()
                turned_copy(jnp.int32(i)).wait()

    @pl.when(role == 3)
    def _():
        count = 11
        tiles = VW // LANE

        def chunk_of(i):
            return 5000 * i

        def target(i):
            return wt.at[pl.ds(pl.multiple_of(i * 64, 64), 64)]

        def work(i, extra):
            def rows_of(n, carry):
                flat = VOCAB * n
                keep = 8 * (8 * i + sublanes()) + n < HID + 1

                def put(c, value):
                    dest[pl.ds(64 * c + n, 8, stride=8), :] = value

                take_rows(wide, dest, flat // LANE + extra, lax.rem(flat, LANE), tiles, VOCAB, 625, put, keep)
                return carry

            lax.fori_loop(0, 8, rows_of, 0)
            slot = lax.rem(i, 2)

            @pl.when(i >= 2)
            def _():
                out_copy(stage3, slot, target(i - 2)).wait()

            for c in range(tiles):
                stage3[slot, :, pl.ds(c * LANE, LANE)] = dest[pl.ds(64 * c, 64), :].astype(BF16)
            out_copy(stage3, slot, target(i)).start()

        stream_blocks(count, LENS[3], total, chunk_of, src, raw, sem_in, wide, work)
        for i in (count - 2, count - 1):
            out_copy(stage3, i % 2, target(jnp.int32(i))).wait()


def unpack_all(section_params):
    anywhere = pl.BlockSpec(memory_space=pl.ANY)
    return pl.pallas_call(
        unpack_kernel,
        out_shape=[
            jax.ShapeDtypeStruct((368, FW), BF16),
            jax.ShapeDtypeStruct((512, LANE), BF16),
            jax.ShapeDtypeStruct((4, 1280, FW), BF16),
            jax.ShapeDtypeStruct((15 * 128, ZW), BF16),
            jax.ShapeDtypeStruct((ZW, GW), BF16),
            jax.ShapeDtypeStruct((11 * 64, VW), BF16),
        ],
        in_specs=[anywhere],
        out_specs=[anywhere] * 6,
        scratch_shapes=[
            pltpu.VMEM((2, 1, LENS[3] * LANE), BF16),
            pltpu.VMEM((9312, LANE), F32),
            pltpu.VMEM((5056, LANE), F32),
            pltpu.VMEM((512, FW), BF16),
            pltpu.VMEM((2, 256, FW), BF16),
            pltpu.VMEM((2, 128, ZW), BF16),
            pltpu.VMEM((2, ZW, LANE), BF16),
            pltpu.VMEM((2, 64, VW), BF16),
            pltpu.SemaphoreType.DMA((2,)),
            pltpu.SemaphoreType.DMA((2,)),
            pltpu.SemaphoreType.DMA((2,)),
        ],
        compiler_params=pltpu.CompilerParams(vmem_limit_bytes=56 << 20),
        name="unpack",
    )(section_params)


def fblocks(width, step=256):
    return [(at, min(step, width - at)) for at in range(0, width, step)]


def mm(a, b):
    return jnp.dot(a, b, preferred_element_type=F32)


def mm_tn(a, b):
    return lax.dot_general(a, b, (((0,), (0,)), ((), ())), preferred_element_type=F32)


def mm_nt(a, b):
    return lax.dot_general(a, b, (((1,), (1,)), ((), ())), preferred_element_type=F32)


def sigmoid(x):
    return 0.5 * jnp.tanh(0.5 * x) + 0.5


def load(pairs, sem):
    copies = [pltpu.make_async_copy(a, b, sem.at[i]) for i, (a, b) in enumerate(pairs)]
    for copy in copies:
        copy.start()
    for copy in copies:
        copy.wait()


def column_mask(at, width, limit, rows):
    return lax.broadcasted_iota(jnp.int32, (rows, width), 1) + at < limit


def char_onehot(ids, t):
    rows = ids.shape[0]
    lane = lanes(rows)
    pieces = []
    for pair in range(4):
        j = 8 * t + 2 * pair
        left = ids[:, j : j + 1]
        right = ids[:, j + 1 : j + 2]
        hit = jnp.where(lane < 64, left, right) == lax.rem(lane, 64)
        pieces.append(jnp.where(hit, 1.0, 0.0).astype(BF16))
    return jnp.concatenate(pieces, axis=1)


def conv_steps(body):
    def step(p, carry):
        body(p, p // 8, True, lax.rem(p, 8), FILT)
        return carry

    lax.fori_loop(0, 15, step, 0)
    body(15, 1, True, 7, COLS[6])
    for p in range(16, WORD_CHARS):
        body(p, 2, False, p - 16, COLS[WORD_CHARS - p])


def conv_at(emb, km, tile, second, within, at, width):
    first = 112 - 16 * within
    if not isinstance(first, int):
        first = pl.multiple_of(first, 16)
    if second:
        window = jnp.concatenate([emb[tile], emb[tile + 1]], axis=1)
    else:
        window = emb[tile]
    return mm(window, km[pl.ds(first, window.shape[1]), pl.ds(at, width)])


def char_forward(ids, e8, km, ab, emb, total, feats, pres, out):
    rows = ids.shape[0]
    for t in range(3):
        emb[t] = mm(char_onehot(ids, t), e8[...]).astype(BF16)
    total[...] = jnp.zeros_like(total)

    def step(p, tile, second, within, limit):
        for at, width in fblocks(FW):
            if at >= limit:
                continue
            value = jnp.exp(jnp.tanh(conv_at(emb, km, tile, second, within, at, width)))
            if at + width > limit and limit < FILT:
                value = jnp.where(column_mask(at, width, limit, rows), value, 0.0)
            total[:, pl.ds(at, width)] += value

    conv_steps(step)
    for at, width in fblocks(FW):
        col = lax.broadcasted_iota(jnp.int32, (rows, width), 1) + at
        count = jnp.full((rows, width), float(WORD_CHARS), F32)
        for k in range(1, 7):
            count = jnp.where(col >= COLS[k], float(WORD_CHARS - k), count)
        value = jnp.log(total[:, pl.ds(at, width)]) - jnp.log(count)
        value = jnp.where(col < FILT, value, jnp.where(col == FILT, 1.0, 0.0))
        feats[0, :, pl.ds(at, width)] = value.astype(BF16)
    for layer in range(2):
        for at, width in fblocks(FW):
            cols = pl.ds(at, width)
            t_pre = mm(feats[layer], ab[2 * layer, pl.ds(0, FW), cols])
            h_pre = mm(feats[layer], ab[2 * layer + 1, pl.ds(0, FW), cols])
            pres[2 * layer, :, cols] = t_pre
            pres[2 * layer + 1, :, cols] = h_pre
            gate = sigmoid(t_pre)
            y = feats[layer, :, cols].astype(F32)
            value = gate * (h_pre * sigmoid(h_pre)) + (1.0 - gate) * y
            col = lax.broadcasted_iota(jnp.int32, (rows, width), 1) + at
            if layer == 0:
                value = jnp.where(col < FILT, value, jnp.where(col == FILT, 1.0, 0.0))
                feats[1, :, cols] = value.astype(BF16)
            else:
                out[:, cols] = jnp.where(col < FILT, value, 0.0).astype(BF16)


def highway_backward(dy, ab, feats, pres, grad, dpre):
    rows = grad.shape[0]
    for at, width in fblocks(FW):
        cols = pl.ds(at, width)
        grad[:, cols] = jnp.where(column_mask(at, width, FILT, rows), dy[:, cols].astype(F32), 0.0)
    for layer in (1, 0):
        for at, width in fblocks(FW):
            cols = pl.ds(at, width)
            g = grad[:, cols]
            gate = sigmoid(pres[2 * layer, :, cols])
            q = pres[2 * layer + 1, :, cols]
            sig = sigmoid(q)
            y = feats[layer, :, cols].astype(F32)
            dpre[2 * layer, :, cols] = (g * (q * sig - y) * gate * (1.0 - gate)).astype(BF16)
            dpre[2 * layer + 1, :, cols] = (g * gate * sig * (1.0 + q * (1.0 - sig))).astype(BF16)
            grad[:, cols] = g * (1.0 - gate)
        for at, width in fblocks(FW):
            cols = pl.ds(at, width)
            value = (
                grad[:, cols]
                + mm_nt(dpre[2 * layer], ab[2 * layer, cols, :])
                + mm_nt(dpre[2 * layer + 1], ab[2 * layer + 1, cols, :])
            )
            if at + width > FILT:
                value = jnp.where(column_mask(at, width, FILT, rows), value, 0.0)
            grad[:, cols] = value


def conv_backward(ids, km, kt, emb, emb_t, total, grad, dk, demb):
    rows = grad.shape[0]
    kt[...] = jnp.transpose(km[pl.ds(112, LANE), :])
    for t in range(3):
        emb_t[pl.ds(LANE * t, LANE), :] = jnp.transpose(emb[t])
    emb_t[pl.ds(3 * LANE, LANE), :] = jnp.zeros((LANE, rows), BF16)
    dk[...] = jnp.zeros_like(dk)
    demb[...] = jnp.zeros_like(demb)
    for at, width in fblocks(FW):
        cols = pl.ds(at, width)
        grad[:, cols] = grad[:, cols] / total[:, cols]

    def step(p, tile, second, within, limit):
        window_t = emb_t[pl.ds(p * 16 if isinstance(p, int) else pl.multiple_of(p * 16, 16), LANE), :]
        back = jnp.zeros((rows, LANE), F32)
        for at, width in fblocks(FW):
            if at >= limit:
                continue
            cols = pl.ds(at, width)
            act = jnp.tanh(conv_at(emb, km, tile, second, within, at, width))
            dz = grad[:, cols] * jnp.exp(act) * (1.0 - act * act)
            if at + width > limit and limit < FILT:
                dz = jnp.where(column_mask(at, width, limit, rows), dz, 0.0)
            dz = dz.astype(BF16)
            dk[:, cols] += mm(window_t, dz)
            back = back + mm(dz, kt[cols, :])
        lane = lanes(rows)
        back = jnp.where(lane < 112, back, 0.0)
        turned = pltpu.roll(back, 16 * within, 1)
        demb[tile] += jnp.where(lane >= 16 * within, turned, 0.0)
        if second:
            demb[tile + 1] += jnp.where(lane < 16 * within, turned, 0.0)

    conv_steps(step)


def table_backward(ids, demb, table):
    acc = jnp.zeros((64, LANE), F32)
    for t in range(3):
        hot = char_onehot(ids, t)
        value = demb[t]
        high = value.astype(BF16)
        low = (value - high.astype(F32)).astype(BF16)
        grads = mm_tn(hot, high) + mm_tn(hot, low)
        for m in range(8):
            block = grads[64 * m : 64 * m + 64, :]
            acc = acc + (pltpu.roll(block, LANE - 16 * m, 1) if m else block)
    table[...] = acc


def tile_rows(stage, base, value, row_tiles, col_tiles, first_col=0, pitch=None):
    pitch = col_tiles if pitch is None else pitch
    for r in range(row_tiles):
        for c in range(col_tiles):
            stage[base + r * pitch + first_col + c] = value[16 * r : 16 * r + 16, LANE * c : LANE * c + LANE].astype(BF16)


def lstm_project(x, depth, u, bias, gates):
    for at, width in fblocks(ZW):
        cols = pl.ds(at, width)
        gates[:, cols] = mm(x[:, pl.ds(0, depth)], u[pl.ds(0, depth), cols]) + bias[:, cols].astype(F32)


def six(x):
    return jnp.concatenate([x] * 6, axis=1)


def lstm_forward_loop(steps, keep, h0, c0, r, gates, cells, prevs, hiddens):
    def step(t, carry):
        h, c = carry
        at = pl.ds(pl.multiple_of(t * 8, 8), 8)
        k = six(keep[at, :])
        hp = h * k
        cp = c * k
        prevs[at, :] = hp
        z = gates[at, :] + mm(hp.astype(BF16), r[...])
        i = sigmoid(z[:, 0:GW])
        f = sigmoid(z[:, GW : 2 * GW])
        o = sigmoid(z[:, 2 * GW : 3 * GW])
        g = jnp.tanh(z[:, 3 * GW :])
        c = f * cp + i * g
        h = (o * jnp.tanh(c)).astype(BF16).astype(F32)
        gates[at, :] = jnp.concatenate([i, f, o, g], axis=1)
        cells[at, :] = c
        hiddens[at, :] = h
        return h, c

    lax.fori_loop(0, steps, step, (h0.astype(BF16).astype(F32), c0))


def lstm_backward_loop(steps, keep, c0, rt, gates, cells, dhs):
    def step(s, carry):
        dh_next, dc_next = carry
        t = steps - 1 - s
        at = pl.ds(pl.multiple_of(t * 8, 8), 8)
        before = pl.ds(pl.multiple_of(jnp.maximum(t - 1, 0) * 8, 8), 8)
        k = six(keep[at, :])
        saved = gates[at, :]
        i, f, o, g = [saved[:, GW * b : GW * b + GW] for b in range(4)]
        cp = jnp.where(t > 0, cells[before, :], c0) * k
        ct = jnp.tanh(cells[at, :])
        dh = dhs[at, :] + dh_next
        dc = dc_next + dh * o * (1.0 - ct * ct)
        dz = jnp.concatenate(
            [dc * g * i * (1.0 - i), dc * cp * f * (1.0 - f), dh * ct * o * (1.0 - o), dc * i * (1.0 - g * g)], axis=1
        ).astype(BF16)
        gates[at, :] = dz.astype(F32)
        return k * mm(dz, rt[...]), k * dc * f

    zero = jnp.zeros((8, GW), F32)
    lax.fori_loop(0, steps, step, (zero, zero))


ANYWHERE = pl.BlockSpec(memory_space=pl.ANY)
ON_CHIP = pl.BlockSpec(memory_space=pltpu.VMEM)
LIMIT = 56 << 20


def call(kernel, name, ins, specs, outs, scratch, aliases=None):
    return pl.pallas_call(
        kernel,
        out_shape=[jax.ShapeDtypeStruct(shape, dtype) for shape, dtype in outs],
        in_specs=specs,
        out_specs=[ANYWHERE] * len(outs),
        scratch_shapes=scratch,
        input_output_aliases=aliases or {},
        compiler_params=pltpu.CompilerParams(vmem_limit_bytes=LIMIT),
        name=name,
    )(*ins)


def vmem(shape, dtype):
    return pltpu.VMEM(shape, dtype)


def dmas(count):
    return pltpu.SemaphoreType.DMA((count,))


def char_forward_call(ids, km, e8, ab):
    n = ids.shape[0]

    def kernel(ids, km, e8, ab, y2_o, feats_o, pres_o, total_o, emb_o, km_v, e8_v, ab_v, y2, feats, pres, total, emb, sem):
        @pl.when(lax.axis_index("section") == 0)
        def _():
            load([(km, km_v), (e8, e8_v), (ab, ab_v)], sem)
            char_forward(ids, e8_v, km_v, ab_v, emb, total, feats, pres, y2)
            load([(y2, y2_o), (feats, feats_o), (pres, pres_o), (total, total_o), (emb, emb_o)], sem)

    outs = [
        ((n, FW), BF16),
        ((2, n, FW), BF16),
        ((4, n, FW), F32),
        ((n, FW), F32),
        ((3, n, LANE), BF16),
    ]
    scratch = [vmem(km.shape, BF16), vmem(e8.shape, BF16), vmem(ab.shape, BF16)]
    scratch += [vmem(shape, dtype) for shape, dtype in outs] + [dmas(5)]
    return call(kernel, "char_forward", (ids, km, e8, ab), [ON_CHIP] + [ANYWHERE] * 3, outs, scratch)


def char_backward_call(ids, dy, km, ab, saved, tiles):
    n = ids.shape[0]
    feats, pres, total, emb = saved

    def kernel(
        ids, dy, km, ab, feats, pres, total, emb, tiles, tiles_o, bias_o,
        dy_v, km_v, ab_v, feats_v, pres_v, total_v, emb_v, grad, dpre, kt, emb_t, dk, demb, table, y_t, stage, bias, sem,
    ):
        @pl.when(lax.axis_index("section") == 0)
        def _():
            load(
                [(dy, dy_v), (km, km_v), (ab, ab_v), (feats, feats_v), (pres, pres_v), (total, total_v), (emb, emb_v)],
                sem,
            )
            highway_backward(dy_v, ab_v, feats_v, pres_v, grad, dpre)
            conv_backward(ids, km_v, kt, emb_v, emb_t, total_v, grad, dk, demb)
            table_backward(ids, demb, table)
            tile_rows(stage, 0, dk[...], 8, 9)
            tile_rows(stage, 72, table[...], 4, 1)
            highway_weights(feats_v, dpre, y_t, stage, CONV_TILES, bias)
            load([(stage, tiles_o.at[pl.ds(0, stage.shape[0])]), (bias, bias_o)], sem)

    outs = [(tiles.shape, BF16), ((8, FW), F32)]
    scratch = [
        vmem(dy.shape, BF16), vmem(km.shape, BF16), vmem(ab.shape, BF16), vmem(feats.shape, BF16),
        vmem(pres.shape, F32), vmem(total.shape, F32), vmem(emb.shape, BF16),
        vmem((n, FW), F32), vmem((4, n, FW), BF16), vmem((FW, LANE), BF16), vmem((4 * LANE, n), BF16),
        vmem((LANE, FW), F32), vmem((3, n, LANE), F32), vmem((64, LANE), F32), vmem((10 * LANE, n), BF16),
        vmem((CONV_TILES + 35 * 72, 16, LANE), BF16), vmem((8, FW), F32), dmas(7),
    ]
    return call(
        kernel, "char_backward", (ids, dy, km, ab, feats, pres, total, emb, tiles),
        [ON_CHIP] + [ANYWHERE] * 8, outs, scratch, {8: 0},
    )


CONV_TILES = 76
TILES = 3648


def turned_tile(left, right, shift):
    rows = right.shape[0]
    if shift:
        mixed = jnp.where(
            lanes(rows) < shift, pltpu.roll(left.astype(F32), shift, 1), pltpu.roll(right.astype(F32), shift, 1)
        )
        right = mixed.astype(BF16)
    return jnp.transpose(right)


def highway_weights(feats, dpre, y_t, stage, base, bias):
    n = feats.shape[1]
    zero = jnp.zeros((n, LANE), BF16)
    for segment in range(4):
        start = segment * (FILT + 1)
        shift, first, last = start % LANE, start // LANE, (start + FILT) // LANE
        for c in range(10):
            left = feats[segment // 2, :, pl.ds(LANE * (c - 1), LANE)] if c > 0 else zero
            right = feats[segment // 2, :, pl.ds(LANE * c, LANE)] if c < 9 else zero
            y_t[pl.ds(LANE * c, LANE), :] = turned_tile(left, right, shift)

        def block(b, joined):
            rows_t = y_t[pl.ds(pl.multiple_of(LANE * b, LANE), LANE), :]
            at = base + 72 * (first + b)
            for col, width in fblocks(FW):
                value = mm(rows_t, dpre[segment, :, pl.ds(col, width)])
                for r in range(8):
                    for c in range(width // LANE):
                        tile = value[16 * r : 16 * r + 16, LANE * c : LANE * c + LANE].astype(BF16)
                        where = at + 9 * r + col // LANE + c
                        if joined:
                            tile = stage[where] + tile
                        stage[where] = tile
                if segment == 0 and joined is None:
                    row = FILT % LANE
                    bias[:, pl.ds(col, width)] = value[row // 8 * 8 : row // 8 * 8 + 8, :]

        def body(b, carry):
            block(b, False)
            return carry

        if segment == 0:
            lax.fori_loop(0, last, body, 0)
            block(last, None)
        else:
            block(0, True)
            lax.fori_loop(1, last - first + 1, body, 0)


def lstm_forward_call(layer, x, ur, keep, state):
    n = x.shape[0]
    depth = x.shape[1]
    steps = n // 8 - 1

    def kernel(x, ur, keep, state, h_o, gates_o, cells_o, prevs_o, x_v, u_v, r_v, state_v, gates, cells, prevs, hs, h16, sem):
        @pl.when(lax.axis_index("section") == layer)
        def _():
            load(
                [
                    (x, x_v),
                    (ur.at[pl.ds(0, depth)], u_v),
                    (ur.at[pl.ds(1152, GW)], r_v),
                    (state.at[layer - 1], state_v),
                ],
                sem,
            )
            lstm_project(x_v, depth, u_v, r_v[pl.ds(HID, 1), :], gates)
            last = pl.ds(8 * steps, 8)
            prevs[last, :] = jnp.zeros((8, GW), F32)
            hs[last, :] = jnp.zeros((8, GW), F32)
            lstm_forward_loop(steps, keep, state_v[0], state_v[1], r_v, gates, cells, prevs, hs)
            h16[...] = hs[...].astype(BF16)
            load([(h16, h_o), (gates, gates_o), (cells, cells_o), (prevs, prevs_o)], sem)

    outs = [((n, GW), BF16), ((n, ZW), F32), ((n, GW), F32), ((n, GW), F32)]
    scratch = [
        vmem(x.shape, BF16), vmem((depth, ZW), BF16), vmem((GW, ZW), BF16), vmem((2, 8, GW), F32),
        vmem((n, ZW), F32), vmem((n, GW), F32), vmem((n, GW), F32), vmem((n, GW), F32), vmem((n, GW), BF16), dmas(4),
    ]
    return call(
        kernel, f"lstm_forward{layer}", (x, ur, keep, state), [ANYWHERE, ANYWHERE, ON_CHIP, ANYWHERE], outs, scratch
    )


def lstm_backward_call(layer, dh, ur, rt, keep, state, saved, depth_pad):
    n = dh.shape[0]
    steps = n // 8 - 1
    depth = FILT if layer == 1 else HID
    gates, cells, _ = saved

    def kernel(dh, ur, rt, keep, state, gates, cells, dx_o, dz_o, dh_v, u_v, rt_v, state_v, gates_v, cells_v, dhs, dx, dz, sem):
        @pl.when(lax.axis_index("section") == layer)
        def _():
            load(
                [
                    (dh, dh_v),
                    (ur.at[pl.ds(0, depth_pad)], u_v),
                    (rt, rt_v),
                    (state.at[layer - 1], state_v),
                    (gates, gates_v),
                    (cells, cells_v),
                ],
                sem,
            )
            dhs[...] = dh_v[...].astype(F32)
            lstm_backward_loop(steps, keep, state_v[1], rt_v, gates_v, cells_v, dhs)
            gates_v[pl.ds(8 * steps, 8), :] = jnp.zeros((8, ZW), F32)
            dz[...] = gates_v[...].astype(BF16)
            for at, width in fblocks(depth_pad):
                value = mm_nt(dz[...], u_v[pl.ds(at, width), :])
                if at + width > depth:
                    value = jnp.where(column_mask(at, width, depth, n), value, 0.0)
                dx[:, pl.ds(at, width)] = value.astype(BF16)
            load([(dx, dx_o), (dz, dz_o)], sem)

    outs = [((n, depth_pad), BF16), ((n, ZW), BF16)]
    scratch = [
        vmem((n, GW), BF16), vmem((depth_pad, ZW), BF16), vmem((ZW, GW), BF16), vmem((2, 8, GW), F32),
        vmem((n, ZW), F32), vmem((n, GW), F32), vmem((n, GW), F32), vmem((n, depth_pad), BF16), vmem((n, ZW), BF16),
        dmas(6),
    ]
    return call(
        kernel, f"lstm_backward{layer}", (dh, ur, rt, keep, state, gates, cells),
        [ANYWHERE] * 3 + [ON_CHIP] + [ANYWHERE] * 3, outs, scratch,
    )


def lstm_weights_call(layer, x, prevs, dz, tiles):
    n, width_in = x.shape
    depth = FILT if layer == 1 else HID
    blocks = 7 if layer == 1 else 6

    def kernel(x, prevs, dz, tiles, tiles_o, x_v, prevs_v, dz_v, xh_t, stage, sem):
        @pl.when(lax.axis_index("section") == layer)
        def _():
            load([(x, x_v), (prevs, prevs_v), (dz, dz_v)], sem)
            first, shift = depth // LANE, depth % LANE
            zero = jnp.zeros((n, LANE), F32)
            lane = lanes(n)
            end = depth + HID
            for c in range(2 * blocks):
                if c < first:
                    mixed = x_v[:, pl.ds(LANE * c, LANE)]
                else:
                    k = c - first
                    left = prevs_v[:, pl.ds(LANE * (k - 1), LANE)] if 0 < k < 7 else zero
                    right = prevs_v[:, pl.ds(LANE * k, LANE)] if k < 6 else zero
                    before = pltpu.roll(left, shift, 1) if k else x_v[:, pl.ds(LANE * c, LANE)].astype(F32)
                    mixed = jnp.where(lane < shift, before, pltpu.roll(right, shift, 1))
                    mixed = jnp.where(lane + c * LANE == end, 1.0, mixed).astype(BF16)
                xh_t[pl.ds(LANE * c, LANE), :] = jnp.transpose(mixed)

            def body(b, carry):
                rows_t = xh_t[pl.ds(pl.multiple_of(256 * b, 256), 256), :]
                for col, width in fblocks(ZW):
                    value = mm(rows_t, dz_v[:, pl.ds(col, width)])
                    tile_rows(stage, 16 * 24 * b, value, 16, 2, col // LANE, 24)
                return carry

            lax.fori_loop(0, blocks, body, 0)
            count = blocks * 16 * 24
            load([(stage.at[pl.ds(0, count)], tiles_o.at[pl.ds(0, count)])], sem)

    scratch = [
        vmem(x.shape, BF16), vmem((n, GW), F32), vmem((n, ZW), BF16), vmem((blocks * 256, n), BF16),
        vmem((blocks * 16 * 24, 16, LANE), BF16), dmas(3),
    ]
    return call(
        kernel, f"lstm_weights{layer}", (x, prevs, dz, tiles), [ANYWHERE] * 4, [(tiles.shape, BF16)], scratch, {3: 0}
    )[0]


VBLOCKS = VW // 256
VTAIL = VBLOCKS * 256


def each_vocab(body):
    def step(i, carry):
        body(pl.multiple_of(i * 256, 256), 256)
        return carry

    lax.fori_loop(0, VBLOCKS, step, 0)
    body(VTAIL, VW - VTAIL)


def output_call(h, wt, targets, valid):
    n = h.shape[0]
    depth = wt.shape[0]

    def kernel(h, wt, targets, valid, dh_o, dl_o, loss_o, h_v, w_v, logits, dl, top, part, dh, dh16, loss, sem):
        loss[...] = jnp.zeros_like(loss)

        @pl.when(lax.axis_index("section") == 3)
        def _():
            load([(h, h_v), (wt, w_v)], sem)
            col = lax.broadcasted_iota(jnp.int32, (n, GW), 1)
            he = jnp.where(col == HID, 1.0, h_v[...].astype(F32)).astype(BF16)
            h_v[...] = he
            top[...] = jnp.full((n, LANE), -jnp.inf, F32)

            def forward(at, width):
                z = mm(h_v[:, pl.ds(0, depth)], w_v[:, pl.ds(at, width)])
                if width < 256:
                    z = jnp.where(column_mask(at, width, VOCAB, n), z, -jnp.inf)
                logits[:, pl.ds(at, width)] = z
                best = top[...]
                for c in range(width // LANE):
                    best = jnp.maximum(best, z[:, LANE * c : LANE * c + LANE])
                top[...] = best

            each_vocab(forward)
            best = jnp.max(top[...], axis=1, keepdims=True)
            part[...] = jnp.zeros((2, n, LANE), F32)

            def exponents(at, width):
                z = logits[:, pl.ds(at, width)]
                e = jnp.exp(z - best)
                logits[:, pl.ds(at, width)] = e
                for c in range(width // LANE):
                    part[0] += e[:, LANE * c : LANE * c + LANE]
                    hit = lanes(n) + (at + LANE * c) == targets[...]
                    part[1] += jnp.where(hit, z[:, LANE * c : LANE * c + LANE], 0.0)

            each_vocab(exponents)
            total = jnp.sum(part[0], axis=1, keepdims=True)
            picked = jnp.sum(part[1], axis=1, keepdims=True)
            each = valid[...] * (best + jnp.log(total) - picked)
            loss[...] = jnp.sum(each, axis=0, keepdims=True)
            share = 1.0 / total
            dh[...] = jnp.zeros_like(dh)

            def backward(at, width):
                e = logits[:, pl.ds(at, width)]
                pieces = []
                for c in range(width // LANE):
                    hit = lanes(n) + (at + LANE * c) == targets[...]
                    grad = (e[:, LANE * c : LANE * c + LANE] * share - jnp.where(hit, 1.0, 0.0)) * valid[...]
                    pieces.append(grad.astype(BF16))
                grad = jnp.concatenate(pieces, axis=1)
                dl[:, pl.ds(at, width)] = grad
                dh[...] += mm_nt(grad, w_v[:, pl.ds(at, width)])

            each_vocab(backward)
            for at, width in fblocks(depth):
                value = dh[:, pl.ds(at, width)]
                dh16[:, pl.ds(at, width)] = jnp.where(column_mask(at, width, HID, n), value, 0.0).astype(BF16)
            dh16[:, pl.ds(depth, GW - depth)] = jnp.zeros((n, GW - depth), BF16)
            load([(dh16, dh_o), (dl, dl_o)], sem)

        load([(loss, loss_o)], sem)

    outs = [((n, GW), BF16), ((n, VW), BF16), ((1, LANE), F32)]
    scratch = [
        vmem((n, GW), BF16), vmem(wt.shape, BF16), vmem((n, VW), F32), vmem((n, VW), BF16), vmem((n, LANE), F32),
        vmem((2, n, LANE), F32), vmem((n, depth), F32), vmem((n, GW), BF16), vmem((1, LANE), F32), dmas(2),
    ]
    return call(kernel, "output", (h, wt, targets, valid), [ANYWHERE] * 2 + [ON_CHIP] * 2, outs, scratch)


def output_weights_call(h, dl):
    n = h.shape[0]
    rows = 704
    pitch = VW // LANE

    def kernel(h, dl, tiles_o, h_v, dl_v, h_t, stage, sem):
        @pl.when(lax.axis_index("section") == 3)
        def _():
            load([(h, h_v), (dl, dl_v)], sem)
            lane = lanes(n)
            for c in range(6):
                value = h_v[:, pl.ds(LANE * c, LANE)].astype(F32)
                value = jnp.where(lane + c * LANE == HID, 1.0, value).astype(BF16)
                h_t[pl.ds(LANE * c, LANE), :] = jnp.transpose(value)

            def body(at, width):
                first = at // LANE
                for top, count in fblocks(rows):
                    value = mm(h_t[pl.ds(top, count), :], dl_v[:, pl.ds(at, width)])
                    for r in range(count // 16):
                        for c in range(width // LANE):
                            stage[(top // 16 + r) * pitch + first + c] = value[
                                16 * r : 16 * r + 16, LANE * c : LANE * c + LANE
                            ].astype(BF16)

            each_vocab(body)
            count = rows // 16 * pitch
            load([(stage.at[pl.ds(0, count)], tiles_o.at[pl.ds(0, count)])], sem)

    scratch = [
        vmem((n, GW), BF16), vmem((n, VW), BF16), vmem((6 * LANE, n), BF16),
        vmem((rows // 16 * pitch, 16, LANE), BF16), dmas(2),
    ]
    return call(
        kernel, "output_weights", (h, dl), [ANYWHERE] * 2, [((TILES, 16, LANE), BF16)], scratch
    )[0]


FORM = (
    (FILT, 9, 4 * (FILT + 1), CONV_END, CONV_TILES, 32),
    (4 * HID, 24, FILT + HID + 1, 0, 0, 16),
    (4 * HID, 24, 2 * HID + 1, 0, 0, 16),
    (VOCAB, 79, HID + 1, 0, 0, 16),
)


def slab(role, dest, share):
    width, pitch, rows, before, lead, period = FORM[role]
    low = lax.max if not isinstance(dest, int) else max
    high = lax.min if not isinstance(dest, int) else min
    one = (lambda v: v) if isinstance(dest, int) else jnp.int32
    start = low(one(share) * dest - before, one(0))
    first = start // width // period * period
    end = high((share * (dest + 1) - before + width - 1) // width, one(rows))
    count = low((end - first + 15) // 16, one(0)) * pitch
    tile = lead + first // 16 * pitch
    if lead:
        if isinstance(dest, int):
            if dest == 0:
                tile, count = 0, count + lead
        else:
            head = lax.max(1 - dest, 0)
            tile = tile - lead * head
            count = count + lead * head
    return first, tile, count


def slab_pieces(count, size):
    return (count + size - 1) // size


def most_pieces(groups, share, size):
    return max(slab_pieces(slab(role, dest, share)[2], size) for role in range(4) for dest in range(groups))


def gather_sum_call(tiles, groups, share):
    pair = 2
    across = groups // pair
    size = 64 if across <= 4 else 32
    pieces = most_pieces(groups, share, size)
    room = pieces * size

    def kernel(tiles, out, own, got1, got2, acc, own_sem, send1, recv1, send2, recv2, out_sem):
        role = lax.axis_index("section")
        me = lax.axis_index("dp")
        mine, side = me // pair, lax.rem(me, pair)
        other = mine * pair + (1 - side)

        barrier = pltpu.get_barrier_semaphore()
        pl.semaphore_signal(barrier, inc=1, device_id={"dp": other}, device_id_type=pl.DeviceIdType.MESH)
        for k in range(1, across):
            peer = lax.rem(mine + k, across) * pair + side
            pl.semaphore_signal(barrier, inc=1, device_id={"dp": peer}, device_id_type=pl.DeviceIdType.MESH)
        pl.semaphore_wait(barrier, across)

        def part(ref, slot, p):
            return ref.at[slot, pl.ds(pl.multiple_of(p * size, size), size)]

        def run(shape_of):
            def dest(k):
                return lax.rem(mine + k, across)

            def own_copy(k, p):
                tile, _ = shape_of(dest(k) * pair + side)
                return pltpu.make_async_copy(tiles.at[pl.ds(tile + p * size, size)], part(own, k, p), own_sem.at[k, p])

            def first_copy(k, p):
                tile, _ = shape_of(dest(k) * pair + 1 - side)
                return pltpu.make_async_remote_copy(
                    tiles.at[pl.ds(tile + p * size, size)], part(got1, k, p), send1.at[k, p], recv1.at[k, p],
                    device_id={"dp": other}, device_id_type=pl.DeviceIdType.MESH,
                )

            def second_copy(k, p):
                return pltpu.make_async_remote_copy(
                    part(own, k, p), part(got2, k - 1, p), send2.at[k - 1, p], recv2.at[k - 1, p],
                    device_id={"dp": dest(k) * pair + side}, device_id_type=pl.DeviceIdType.MESH,
                )

            def loop(count, body):
                def step(p, carry):
                    body(p)
                    return carry

                lax.fori_loop(0, count, step, 0)

            order = list(range(1, across)) + [0]

            def count_to(k, which):
                return shape_of(dest(k) * pair + which)[1]

            for k in order:
                loop(count_to(k, 1 - side), lambda p, k=k: first_copy(k, p).start())
                loop(count_to(k, side), lambda p, k=k: own_copy(k, p).start())
            for k in order[:-1]:

                def join(p, k=k):
                    own_copy(k, p).wait()
                    first_copy(k, p).wait_recv()
                    at = pl.ds(pl.multiple_of(p * size, size), size)
                    own[k, at] = (own[k, at].astype(F32) + got1[k, at].astype(F32)).astype(BF16)
                    second_copy(k, p).start()

                loop(count_to(k, side), join)

            def settle(p):
                own_copy(0, p).wait()
                first_copy(0, p).wait_recv()
                at = pl.ds(pl.multiple_of(p * size, size), size)
                acc[at] = own[0, at].astype(F32) + got1[0, at].astype(F32)

            mine_count = count_to(0, side)
            loop(mine_count, settle)
            for k in order[:-1]:

                def add(p, k=k):
                    second_copy(k, p).wait_recv()
                    at = pl.ds(pl.multiple_of(p * size, size), size)
                    acc[at] += got2[k - 1, at].astype(F32)

                loop(mine_count, add)

            def out_copy(p):
                at = pl.ds(pl.multiple_of(p * size, size), size)
                return pltpu.make_async_copy(acc.at[at], out.at[at], out_sem.at[p])

            loop(mine_count, lambda p: out_copy(p).start())
            loop(mine_count, lambda p: out_copy(p).wait())
            for k in order:
                loop(count_to(k, 1 - side), lambda p, k=k: first_copy(k, p).wait_send())
            for k in order[:-1]:
                loop(count_to(k, side), lambda p, k=k: second_copy(k, p).wait_send())

        for which in range(4):

            @pl.when(role == which)
            def _(which=which):
                def shape_of(dest):
                    _, tile, count = slab(which, dest, share)
                    return tile, slab_pieces(count, size)

                run(shape_of)

    sems = pltpu.SemaphoreType.DMA
    return pl.pallas_call(
        kernel,
        out_shape=jax.ShapeDtypeStruct((room, 16, LANE), F32),
        in_specs=[ANYWHERE],
        out_specs=ANYWHERE,
        scratch_shapes=[
            vmem((across, room, 16, LANE), BF16), vmem((across, room, 16, LANE), BF16),
            vmem((across - 1, room, 16, LANE), BF16), vmem((room, 16, LANE), F32),
            sems((across, pieces)), sems((across, pieces)), sems((across, pieces)),
            sems((across - 1, pieces)), sems((across - 1, pieces)), sems((pieces,)),
        ],
        compiler_params=pltpu.CompilerParams(vmem_limit_bytes=62 << 20, collective_id=1, has_side_effects=True),
        name="gather_sum",
    )(tiles)


def pack_call(summed, groups, share):
    room = summed.shape[0] * 16
    chunks = share // LANE
    margin = 1280
    slab_rows = 10624
    flat_rows = margin + max(10752, chunks + 1280)

    def kernel(summed, out, rows_v, flat, sem):
        role = lax.axis_index("section")
        me = lax.axis_index("dp")
        zero = jnp.zeros((64, LANE), F32)

        def clear(i, carry):
            flat[pl.ds(pl.multiple_of(i * 64, 64), 64), :] = zero
            return carry

        copy = pltpu.make_async_copy(summed, rows_v.at[pl.ds(0, room)], sem.at[0])
        copy.start()
        lax.fori_loop(0, flat_rows // 64, clear, 0)
        copy.wait()
        lane = lanes()

        def put(at, stride, value, mask):
            where = pl.ds(at, 8, stride=stride)
            if mask is not None:
                value = jnp.where(mask, value, flat[where, :])
            flat[where, :] = value

        for which in range(4):
            width, pitch, rows, before, lead, period = FORM[which]
            if which == 0:
                blocks, cols, tiles = 1, FILT, 9
            elif which == 3:
                blocks, cols, tiles = 1, VOCAB, 79
            else:
                blocks, cols, tiles = 4, HID, 6
            stride = period * width // LANE
            most = max(slab(which, dest, share)[2] for dest in range(groups))
            groups8 = -(-(-(-most // pitch) * 16) // (8 * period))

            @pl.when(role == which)
            def _(which=which):
                first, _, count = slab(which, me, share)
                skip = lead * lax.max(1 - me, 0)
                base = margin + before // LANE + stride * (first // period) - chunks * me

                def row(i, carry):
                    group, n = i // period, lax.rem(i, period)
                    number = first + period * (8 * group + sublanes()) + n
                    keep = number < rows
                    for b in range(blocks):
                        flat_at = before % LANE + width * n + cols * b
                        turn = lax.rem(flat_at, LANE)
                        to = base + flat_at // LANE + stride * 8 * group
                        source = (skip + n // 16 * pitch + tiles * b) * 16 + lax.rem(n, 16) + 8 * group * period * pitch
                        last = jnp.zeros((8, LANE), F32)
                        for j in range(tiles + 1):
                            if j < tiles:
                                here = rows_v[pl.ds(source + 16 * j, 8, stride=period * pitch), :]
                                here = pltpu.roll(jnp.where(keep, here, 0.0), turn, 1)
                            else:
                                here = last
                            value = jnp.where(lane >= turn, here, last)
                            mask = None
                            if j == 0:
                                mask = lane >= turn
                            elif j >= tiles - 1:
                                mask = lane + LANE * j - turn < cols
                            put(to + j, stride, value, mask)
                            last = here
                    return carry

                @pl.when(count > 0)
                def _():
                    lax.fori_loop(0, period * groups8, row, 0)

        @pl.when((role == 0) & (me == 0))
        def _():
            lane1 = lanes(1)

            def piece(row_at, flat_at, low, size):
                edge = flat_at - low
                turn = lax.rem(edge + 128 * LANE, LANE)
                to = margin + (edge - turn) // LANE
                first, end = low // LANE, (low + size - 1) // LANE
                last = jnp.zeros((1, LANE), F32)
                for j in range(first, end + 2):
                    here = last
                    if j <= end:
                        here = pltpu.roll(rows_v[pl.ds(row_at + 16 * j, 1), :], turn, 1)
                    value = jnp.where(lane1 >= turn, here, last)
                    at = lane1 + LANE * j - turn
                    where = pl.ds(to + j, 1)
                    flat[where, :] = jnp.where((at >= low) & (at < low + size), value, flat[where, :])
                    last = here

            def conv_rows(k, i, number):
                n = NFILT[k - 1]
                piece(number // 16 * 144 + lax.rem(number, 16), KOFF[k - 1] + n * i, COLS[k - 1], n)

            for k in range(1, 8):

                def offset_rows(o, carry, k=k):
                    for d in range(D_CHAR):
                        conv_rows(k, o * D_CHAR + d, 16 * o + d)
                    return carry

                lax.fori_loop(0, k, offset_rows, 0)
                conv_rows(k, jnp.int32(k * D_CHAR), jnp.int32(15))

            def table_row(a, carry):
                piece(72 * 16 + a, D_CHAR * a, 0, D_CHAR)
                return carry

            lax.fori_loop(0, CHAR_V, table_row, 0, unroll=3)

        copy = pltpu.make_async_copy(flat.at[pl.ds(margin, chunks)], out, sem.at[0])
        copy.start()
        copy.wait()

    return pl.pallas_call(
        kernel,
        out_shape=jax.ShapeDtypeStruct((chunks, LANE), F32),
        in_specs=[ANYWHERE],
        out_specs=ANYWHERE,
        scratch_shapes=[vmem((slab_rows, LANE), F32), vmem((flat_rows, LANE), F32), pltpu.SemaphoreType.DMA((1,))],
        compiler_params=pltpu.CompilerParams(vmem_limit_bytes=LIMIT),
        name="pack",
    )(summed.reshape(room, LANE))


def shards(char_ids, target_ids, remaining, resets, start_state, section_params):
    rows, steps = char_ids.shape[:2]
    section = lax.axis_index("section")
    groups = lax.axis_size("dp")
    packed = section_params.shape[1]
    share = packed // groups
    n = rows * (steps + 1)

    def by_step(x, fill):
        x = jnp.pad(x.T, ((0, 1), (0, 0)), constant_values=fill)
        return jnp.broadcast_to(x.reshape(n, 1), (n, LANE))

    ids = jnp.pad(
        char_ids.transpose(1, 0, 2), ((0, 1), (0, 0), (0, LANE - WORD_CHARS)), constant_values=-1
    ).reshape(n, LANE)
    targets = by_step(target_ids, -1)
    keep = by_step(1.0 - resets.astype(F32), 0.0)
    valid = by_step((jnp.arange(steps, dtype=jnp.int32)[None, :] < remaining[:, None]).astype(F32), 0.0)
    state = jnp.pad(start_state, ((0, 0), (0, 0), (0, 0), (0, GW - HID)))

    km, e8, ab, ur, rt, wt = unpack_all(section_params)
    y2, *char_saved = char_forward_call(ids, km, e8, ab)
    x1 = lax.ppermute(y2, "section", [(0, 1)])
    h1, *saved1 = lstm_forward_call(1, x1, ur, keep, state)
    x2 = lax.ppermute(h1, "section", [(1, 2)])
    h2, *saved2 = lstm_forward_call(2, x2, ur, keep, state)
    x3 = lax.ppermute(h2, "section", [(2, 3)])
    dh2, dl, loss = output_call(x3, wt, targets, valid)
    g2 = lax.ppermute(dh2, "section", [(3, 2)])
    tiles = output_weights_call(x3, dl)
    dx2, dz2 = lstm_backward_call(2, g2, ur, rt, keep, state, saved2, GW)
    g1 = lax.ppermute(dx2, "section", [(2, 1)])
    tiles = lstm_weights_call(2, x2, saved2[2], dz2, tiles)
    dx1, dz1 = lstm_backward_call(1, g1, ur, rt, keep, state, saved1, FW)
    g0 = lax.ppermute(dx1, "section", [(1, 0)])
    tiles = lstm_weights_call(1, x1, saved1[2], dz1, tiles)
    tiles, bias = char_backward_call(ids, g0, km, ab, char_saved, tiles)
    summed = gather_sum_call(tiles, groups, share)
    flat = pack_call(summed, groups, share)
    bias_row = jnp.where(section == 0, bias[FILT % LANE % 8, :FILT], 0.0)
    total_loss, bias_total = lax.psum((loss[0, 0], bias_row), ("dp", "section"))
    mean_loss = total_loss / (groups * rows * steps)
    return mean_loss, flat.reshape(1, share), bias_total


def solution(mesh):
    in_specs = (
        P("dp", None, None),
        P("dp", None),
        P("dp"),
        P("dp", None),
        P(None, None, "dp", None),
        P("section", None),
    )
    out_specs = (P(), P("section", "dp"), P())
    return jax.shard_map(shards, mesh=mesh, in_specs=in_specs, out_specs=out_specs, check_vma=False)
```

```python
import functools
import math

import jax
import jax.numpy as jnp
from jax import lax
from jax.experimental import pallas as pl
from jax.experimental.pallas import tpu as pltpu
from jax.sharding import PartitionSpec as P

D_CHAR = 15
CHAR_V = 51
F_UNIT = 50
WORD_CHARS = 21
HID = 650
VOCAB = 10000
FILT = 1100
F32 = jnp.float32
BF16 = jnp.bfloat16

NFILT = [F_UNIT * min(k, 4) for k in range(1, 8)]
COLS = [sum(NFILT[:k]) for k in range(8)]
KOFF = [CHAR_V * D_CHAR + sum((j * D_CHAR + 1) * NFILT[j - 1] for j in range(1, k)) for k in range(1, 9)]
CONV_END = KOFF[7]
HIGH_STRIDE = FILT * (FILT + 1)
FW = 1152
GW = 768
ZW = 4 * GW
VW = 10112
LANE = 128
LENS = (2304, 2688, 2688, 5120)


def roll_lanes(x, shift):
    return pltpu.roll(x, shift, 1)


def lanes(rows=8):
    return lax.broadcasted_iota(jnp.int32, (rows, LANE), 1)


def sublanes():
    return lax.broadcasted_iota(jnp.int32, (8, LANE), 0)


def widen(raw, slot, rows, wide):
    def body(i, carry):
        piece = raw[slot, 0:1, pl.ds(pl.multiple_of(i * 16384, 16384), 16384)]
        wide[pl.ds(pl.multiple_of(i * 128, 128), 128), :] = piece.astype(F32).reshape(128, LANE)
        return carry

    lax.fori_loop(0, rows // 128, body, 0)


def stream_blocks(count, length, total, chunk_of, src, raw, sem, wide, work):
    def start_of(i):
        first = chunk_of(i)
        return jnp.minimum(first // 8 * 8, total - length)

    def copy(i, slot):
        at = pl.multiple_of(start_of(i) * LANE, 8 * LANE)
        return pltpu.make_async_copy(
            src.at[:, pl.ds(at, length * LANE)], raw.at[slot, :, pl.ds(0, length * LANE)], sem.at[slot]
        )

    copy(0, 0).start()

    def body(i, carry):
        slot = lax.rem(i, 2)

        @pl.when(i + 1 < count)
        def _():
            copy(i + 1, 1 - slot).start()

        copy(i, slot).wait()
        widen(raw, slot, length, wide)
        work(i, chunk_of(i) - start_of(i))
        return carry

    lax.fori_loop(0, count, body, 0)


def take_rows(wide, starts, tiles, cols, stride, put):
    step = max(1, 28 // len(starts))
    lane = lanes()
    for low in range(0, tiles, step):
        high = min(tiles, low + step)
        loaded = [
            [wide[pl.ds(first + c, 8, stride=stride), :] for c in range(low, high + 1)] for _, first, _, _ in starts
        ]
        results = []
        for (_, _, shift, keep_row), pieces in zip(starts, loaded):
            turn = lax.rem(LANE - shift, LANE)
            split = lane < LANE - shift
            turned = [roll_lanes(piece, turn) for piece in pieces]
            for c in range(low, high):
                out = jnp.where(split, turned[c - low], turned[c - low + 1])
                keep = keep_row
                if cols - c * LANE < LANE:
                    keep = keep & (lane < cols - c * LANE)
                results.append(jnp.where(keep, out, 0.0))
        at = 0
        for tag, _, _, _ in starts:
            for c in range(low, high):
                put(tag, c, results[at])
                at += 1


def unpack_kernel(
    src, km, e8, ab, ur, rt, wt, raw, wide, dest, kstage, stage0, stage1, stage_t, stage3, sem_in, sem_out, sem_t
):
    role = lax.axis_index("section")
    total = src.shape[1] // LANE

    def out_copy(stage, slot, target):
        return pltpu.make_async_copy(stage.at[slot], target, sem_out.at[slot])

    @pl.when(role == 0)
    def _():
        length = 640
        copy = pltpu.make_async_copy(
            src.at[:, pl.ds(0, length * LANE)], raw.at[0, :, pl.ds(0, length * LANE)], sem_in.at[0]
        )
        copy.start()
        copy.wait()
        widen(raw, 0, length, wide)
        lane1 = lanes(1)
        dest[pl.ds(0, 64), :] = jnp.zeros((64, LANE), F32)
        for a in range(CHAR_V):
            flat = D_CHAR * a
            q, s = flat // LANE, flat % LANE
            here = wide[q : q + 1, :]
            out = roll_lanes(here, (LANE - s) % LANE) if s else here
            if s + D_CHAR > LANE:
                out = jnp.where(lane1 < LANE - s, out, roll_lanes(wide[q + 1 : q + 2, :], LANE - s))
            dest[a : a + 1, :] = jnp.where(lane1 < D_CHAR, out, jnp.where(lane1 == D_CHAR, 1.0, 0.0))
        table = dest[pl.ds(0, 64), :]
        for m in range(8):
            kstage[pl.ds(64 * m, 64), pl.ds(0, LANE)] = (
                pltpu.roll(table, 16 * m, 1) if m else table
            ).astype(BF16)
        copy = pltpu.make_async_copy(kstage.at[pl.ds(0, 512), pl.ds(0, LANE)], e8, sem_out.at[0])
        copy.start()
        copy.wait()
        tiles = FW // LANE
        rows = 112
        dest[pl.ds(0, rows * tiles), :] = jnp.zeros((rows * tiles, LANE), F32)

        def kernel_row(k, i, row):
            n, base = NFILT[k - 1], COLS[k - 1]
            edge = KOFF[k - 1] + n * i - base
            q, s = edge // LANE, edge % LANE
            for ct in range(base // LANE, (base + n - 1) // LANE + 1):
                out = wide[q + ct : q + ct + 1, :]
                if s:
                    after = roll_lanes(wide[q + ct + 1 : q + ct + 2, :], LANE - s)
                    out = jnp.where(lane1 < LANE - s, roll_lanes(out, LANE - s), after)
                at = ct * rows + row
                low, high = max(base - ct * LANE, 0), min(base + n - ct * LANE, LANE)
                if low > 0 or high < LANE:
                    out = jnp.where((lane1 >= low) & (lane1 < high), out, dest[at : at + 1, :])
                dest[at : at + 1, :] = out

        for k in range(1, 8):
            for i in range(k * D_CHAR):
                kernel_row(k, i, i + i // D_CHAR)
            kernel_row(k, k * D_CHAR, 15)
        kstage[...] = jnp.zeros_like(kstage)
        for ct in range(tiles):
            kstage[pl.ds(112, rows), pl.ds(ct * LANE, LANE)] = dest[pl.ds(ct * rows, rows), :].astype(BF16)
        copy = pltpu.make_async_copy(kstage.at[pl.ds(0, 368)], km, sem_out.at[0])
        copy.start()
        copy.wait()

        blocks = 5

        def flat_of(i):
            return CONV_END + HIGH_STRIDE * (i // blocks)

        def chunk_of(i):
            return flat_of(i) // LANE + 2200 * lax.rem(i, blocks)

        def target(i):
            return ab.at[i // blocks, pl.ds(pl.multiple_of(lax.rem(i, blocks) * 256, 256), 256)]

        def work(i, extra):
            block = lax.rem(i, blocks)
            inner = lax.rem(flat_of(i), LANE)

            def rows_of(i, carry):
                starts = []
                for n in (2 * i, 2 * i + 1):
                    flat = inner + FILT * n
                    keep = 32 * (8 * block + sublanes()) + n <= FILT
                    starts.append((n, flat // LANE + extra, lax.rem(flat, LANE), keep))

                def put(n, c, value):
                    dest[pl.ds(256 * c + n, 8, stride=32), :] = value

                take_rows(wide, starts, tiles, FILT, 275, put)
                return carry

            lax.fori_loop(0, 16, rows_of, 0)
            slot = lax.rem(i, 2)

            @pl.when(i >= 2)
            def _():
                out_copy(stage0, slot, target(i - 2)).wait()

            for c in range(tiles):
                stage0[slot, :, pl.ds(c * LANE, LANE)] = dest[pl.ds(256 * c, 256), :].astype(BF16)
            out_copy(stage0, slot, target(i)).start()

        count = 4 * blocks
        stream_blocks(count, LENS[0], total, chunk_of, src, raw, sem_in, wide, work)
        for i in (count - 2, count - 1):
            out_copy(stage0, i % 2, target(i)).wait()

    for layer in (1, 2):

        @pl.when(role == layer)
        def _(layer=layer):
            depth = FILT if layer == 1 else HID
            blocks = -(-depth // 128)
            recurrent = depth * 4 * HID
            count = blocks + 6

            def chunk_of(i):
                return jnp.where(i < blocks, 2600 * i, recurrent // LANE + 2600 * (i - blocks))

            def target(i):
                at = jnp.where(i < blocks, i, i - blocks + 9)
                return ur.at[pl.ds(pl.multiple_of(at * 128, 128), 128)]

            def work(i, extra):
                inner = jnp.where(i < blocks, 0, recurrent % LANE)
                block = jnp.where(i < blocks, i, i - blocks)
                limit = jnp.where(i < blocks, depth, HID + 1)

                def rows_of(n, carry):
                    keep = 16 * (8 * block + sublanes()) + n < limit
                    flats = [inner + 4 * HID * n + HID * b for b in range(4)]

                    def put(b, c, value):
                        dest[pl.ds(128 * (6 * b + c) + n, 8, stride=16), :] = value

                    starts = [(b, flat // LANE + extra, lax.rem(flat, LANE), keep) for b, flat in enumerate(flats)]
                    take_rows(wide, starts, 6, HID, 325, put)
                    return carry

                lax.fori_loop(0, 16, rows_of, 0)
                slot = lax.rem(i, 2)

                @pl.when(i >= 2)
                def _():
                    out_copy(stage1, slot, target(i - 2)).wait()

                for c in range(24):
                    stage1[slot, :, pl.ds(c * LANE, LANE)] = dest[pl.ds(128 * c, 128), :].astype(BF16)
                out_copy(stage1, slot, target(i)).start()

                @pl.when(i >= blocks)
                def _():
                    @pl.when(i >= blocks + 2)
                    def _():
                        turned_copy(i - 2).wait()

                    k = LANE * block + lanes(LANE)
                    for c in range(24):
                        turned = jnp.transpose(dest[pl.ds(128 * c, 128), :])
                        stage_t[slot, pl.ds(128 * c, 128), :] = jnp.where(k < HID, turned, 0.0).astype(BF16)
                    turned_copy(i).start()

            def turned_copy(i):
                slot = lax.rem(i, 2)
                at = pl.multiple_of((i - blocks) * LANE, LANE)
                return pltpu.make_async_copy(stage_t.at[slot], rt.at[:, pl.ds(at, LANE)], sem_t.at[slot])

            stream_blocks(count, LENS[1], total, chunk_of, src, raw, sem_in, wide, work)
            for i in (count - 2, count - 1):
                out_copy(stage1, i % 2, target(jnp.int32(i))).wait()
                turned_copy(jnp.int32(i)).wait()

    @pl.when(role == 3)
    def _():
        count = 11
        tiles = VW // LANE

        def chunk_of(i):
            return 5000 * i

        def target(i):
            return wt.at[pl.ds(pl.multiple_of(i * 64, 64), 64)]

        def work(i, extra):
            def rows_of(n, carry):
                flat = VOCAB * n
                keep = 8 * (8 * i + sublanes()) + n < HID + 1

                def put(n, c, value):
                    dest[pl.ds(64 * c + n, 8, stride=8), :] = value

                take_rows(wide, [(n, flat // LANE + extra, lax.rem(flat, LANE), keep)], tiles, VOCAB, 625, put)
                return carry

            lax.fori_loop(0, 8, rows_of, 0)
            slot = lax.rem(i, 2)

            @pl.when(i >= 2)
            def _():
                out_copy(stage3, slot, target(i - 2)).wait()

            for c in range(tiles):
                stage3[slot, :, pl.ds(c * LANE, LANE)] = dest[pl.ds(64 * c, 64), :].astype(BF16)
            out_copy(stage3, slot, target(i)).start()

        stream_blocks(count, LENS[3], total, chunk_of, src, raw, sem_in, wide, work)
        for i in (count - 2, count - 1):
            out_copy(stage3, i % 2, target(jnp.int32(i))).wait()


def unpack_all(section_params):
    anywhere = pl.BlockSpec(memory_space=pl.ANY)
    return pl.pallas_call(
        unpack_kernel,
        out_shape=[
            jax.ShapeDtypeStruct((368, FW), BF16),
            jax.ShapeDtypeStruct((512, LANE), BF16),
            jax.ShapeDtypeStruct((4, 1280, FW), BF16),
            jax.ShapeDtypeStruct((15 * 128, ZW), BF16),
            jax.ShapeDtypeStruct((ZW, GW), BF16),
            jax.ShapeDtypeStruct((11 * 64, VW), BF16),
        ],
        in_specs=[anywhere],
        out_specs=[anywhere] * 6,
        scratch_shapes=[
            pltpu.VMEM((2, 1, LENS[3] * LANE), BF16),
            pltpu.VMEM((9312, LANE), F32),
            pltpu.VMEM((5056, LANE), F32),
            pltpu.VMEM((512, FW), BF16),
            pltpu.VMEM((2, 256, FW), BF16),
            pltpu.VMEM((2, 128, ZW), BF16),
            pltpu.VMEM((2, ZW, LANE), BF16),
            pltpu.VMEM((2, 64, VW), BF16),
            pltpu.SemaphoreType.DMA((2,)),
            pltpu.SemaphoreType.DMA((2,)),
            pltpu.SemaphoreType.DMA((2,)),
        ],
        compiler_params=pltpu.CompilerParams(vmem_limit_bytes=56 << 20),
        name="unpack",
    )(section_params)


def fblocks(width, step=256):
    return [(at, min(step, width - at)) for at in range(0, width, step)]


def mm(a, b):
    return jnp.dot(a, b, preferred_element_type=F32)


def mm_tn(a, b):
    return lax.dot_general(a, b, (((0,), (0,)), ((), ())), preferred_element_type=F32)


def mm_nt(a, b):
    return lax.dot_general(a, b, (((1,), (1,)), ((), ())), preferred_element_type=F32)


def sigmoid(x):
    return 0.5 * jnp.tanh(0.5 * x) + 0.5


def load(pairs, sem):
    copies = [pltpu.make_async_copy(a, b, sem.at[i]) for i, (a, b) in enumerate(pairs)]
    for copy in copies:
        copy.start()
    for copy in copies:
        copy.wait()


def column_mask(at, width, limit, rows):
    return lax.broadcasted_iota(jnp.int32, (rows, width), 1) + at < limit


def char_onehot(ids, t):
    rows = ids.shape[0]
    lane = lanes(rows)
    pieces = []
    for pair in range(4):
        j = 8 * t + 2 * pair
        left = ids[:, j : j + 1]
        right = ids[:, j + 1 : j + 2]
        hit = jnp.where(lane < 64, left, right) == lax.rem(lane, 64)
        pieces.append(jnp.where(hit, 1.0, 0.0).astype(BF16))
    return jnp.concatenate(pieces, axis=1)


def conv_steps(body):
    def step(p, carry):
        body(p, p // 8, True, lax.rem(p, 8), FILT)
        return carry

    lax.fori_loop(0, 15, step, 0)
    body(15, 1, True, 7, COLS[6])
    for p in range(16, WORD_CHARS):
        body(p, 2, False, p - 16, COLS[WORD_CHARS - p])


def conv_at(emb, km, tile, second, within, at, width):
    first = 112 - 16 * within
    if not isinstance(first, int):
        first = pl.multiple_of(first, 16)
    if second:
        window = jnp.concatenate([emb[tile], emb[tile + 1]], axis=1)
    else:
        window = emb[tile]
    return mm(window, km[pl.ds(first, window.shape[1]), pl.ds(at, width)])


def char_forward(ids, e8, km, ab, emb, total, feats, pres, out):
    rows = ids.shape[0]
    for t in range(3):
        emb[t] = mm(char_onehot(ids, t), e8[...]).astype(BF16)
    total[...] = jnp.zeros_like(total)

    def step(p, tile, second, within, limit):
        for at, width in fblocks(FW):
            if at >= limit:
                continue
            value = jnp.exp(jnp.tanh(conv_at(emb, km, tile, second, within, at, width)))
            if at + width > limit and limit < FILT:
                value = jnp.where(column_mask(at, width, limit, rows), value, 0.0)
            total[:, pl.ds(at, width)] += value

    conv_steps(step)
    for at, width in fblocks(FW):
        col = lax.broadcasted_iota(jnp.int32, (rows, width), 1) + at
        count = jnp.full((rows, width), float(WORD_CHARS), F32)
        for k in range(1, 7):
            count = jnp.where(col >= COLS[k], float(WORD_CHARS - k), count)
        value = jnp.log(total[:, pl.ds(at, width)]) - jnp.log(count)
        value = jnp.where(col < FILT, value, jnp.where(col == FILT, 1.0, 0.0))
        feats[0, :, pl.ds(at, width)] = value.astype(BF16)
    for layer in range(2):
        for at, width in fblocks(FW):
            cols = pl.ds(at, width)
            t_pre = mm(feats[layer], ab[2 * layer, pl.ds(0, FW), cols])
            h_pre = mm(feats[layer], ab[2 * layer + 1, pl.ds(0, FW), cols])
            pres[2 * layer, :, cols] = t_pre
            pres[2 * layer + 1, :, cols] = h_pre
            gate = sigmoid(t_pre)
            y = feats[layer, :, cols].astype(F32)
            value = gate * (h_pre * sigmoid(h_pre)) + (1.0 - gate) * y
            col = lax.broadcasted_iota(jnp.int32, (rows, width), 1) + at
            if layer == 0:
                value = jnp.where(col < FILT, value, jnp.where(col == FILT, 1.0, 0.0))
                feats[1, :, cols] = value.astype(BF16)
            else:
                out[:, cols] = jnp.where(col < FILT, value, 0.0).astype(BF16)


def highway_backward(dy, ab, feats, pres, grad, dpre):
    rows = grad.shape[0]
    for at, width in fblocks(FW):
        cols = pl.ds(at, width)
        grad[:, cols] = jnp.where(column_mask(at, width, FILT, rows), dy[:, cols].astype(F32), 0.0)
    for layer in (1, 0):
        for at, width in fblocks(FW):
            cols = pl.ds(at, width)
            g = grad[:, cols]
            gate = sigmoid(pres[2 * layer, :, cols])
            q = pres[2 * layer + 1, :, cols]
            sig = sigmoid(q)
            y = feats[layer, :, cols].astype(F32)
            dpre[2 * layer, :, cols] = (g * (q * sig - y) * gate * (1.0 - gate)).astype(BF16)
            dpre[2 * layer + 1, :, cols] = (g * gate * sig * (1.0 + q * (1.0 - sig))).astype(BF16)
            grad[:, cols] = g * (1.0 - gate)
        for at, width in fblocks(FW):
            cols = pl.ds(at, width)
            value = (
                grad[:, cols]
                + mm_nt(dpre[2 * layer], ab[2 * layer, cols, :])
                + mm_nt(dpre[2 * layer + 1], ab[2 * layer + 1, cols, :])
            )
            if at + width > FILT:
                value = jnp.where(column_mask(at, width, FILT, rows), value, 0.0)
            grad[:, cols] = value


def conv_backward(ids, km, kt, emb, emb_t, total, grad, dk, demb):
    rows = grad.shape[0]
    kt[...] = jnp.transpose(km[pl.ds(112, LANE), :])
    for t in range(3):
        emb_t[pl.ds(LANE * t, LANE), :] = jnp.transpose(emb[t])
    emb_t[pl.ds(3 * LANE, LANE), :] = jnp.zeros((LANE, rows), BF16)
    dk[...] = jnp.zeros_like(dk)
    demb[...] = jnp.zeros_like(demb)
    for at, width in fblocks(FW):
        cols = pl.ds(at, width)
        grad[:, cols] = grad[:, cols] / total[:, cols]

    def step(p, tile, second, within, limit):
        window_t = emb_t[pl.ds(p * 16 if isinstance(p, int) else pl.multiple_of(p * 16, 16), LANE), :]
        back = jnp.zeros((rows, LANE), F32)
        for at, width in fblocks(FW):
            if at >= limit:
                continue
            cols = pl.ds(at, width)
            act = jnp.tanh(conv_at(emb, km, tile, second, within, at, width))
            dz = grad[:, cols] * jnp.exp(act) * (1.0 - act * act)
            if at + width > limit and limit < FILT:
                dz = jnp.where(column_mask(at, width, limit, rows), dz, 0.0)
            dz = dz.astype(BF16)
            dk[:, cols] += mm(window_t, dz)
            back = back + mm(dz, kt[cols, :])
        lane = lanes(rows)
        back = jnp.where(lane < 112, back, 0.0)
        turned = pltpu.roll(back, 16 * within, 1)
        demb[tile] += jnp.where(lane >= 16 * within, turned, 0.0)
        if second:
            demb[tile + 1] += jnp.where(lane < 16 * within, turned, 0.0)

    conv_steps(step)


def table_backward(ids, demb, table):
    acc = jnp.zeros((64, LANE), F32)
    for t in range(3):
        hot = char_onehot(ids, t)
        value = demb[t]
        high = value.astype(BF16)
        low = (value - high.astype(F32)).astype(BF16)
        grads = mm_tn(hot, high) + mm_tn(hot, low)
        for m in range(8):
            block = grads[64 * m : 64 * m + 64, :]
            acc = acc + (pltpu.roll(block, LANE - 16 * m, 1) if m else block)
    table[...] = acc


def tile_rows(stage, base, value, row_tiles, col_tiles, first_col=0, pitch=None):
    pitch = col_tiles if pitch is None else pitch
    for r in range(row_tiles):
        for c in range(col_tiles):
            stage[base + r * pitch + first_col + c] = value[16 * r : 16 * r + 16, LANE * c : LANE * c + LANE].astype(BF16)


def lstm_project(x, depth, u, bias, gates):
    for at, width in fblocks(ZW):
        cols = pl.ds(at, width)
        gates[:, cols] = mm(x[:, pl.ds(0, depth)], u[pl.ds(0, depth), cols]) + bias[:, cols].astype(F32)


def six(x):
    return jnp.concatenate([x] * 6, axis=1)


def lstm_forward_loop(steps, keep, h0, c0, r, gates, cells, prevs, hiddens):
    def step(t, carry):
        h, c = carry
        at = pl.ds(pl.multiple_of(t * 8, 8), 8)
        k = six(keep[at, :])
        hp = h * k
        cp = c * k
        prevs[at, :] = hp
        z = gates[at, :] + mm(hp.astype(BF16), r[...])
        i = sigmoid(z[:, 0:GW])
        f = sigmoid(z[:, GW : 2 * GW])
        o = sigmoid(z[:, 2 * GW : 3 * GW])
        g = jnp.tanh(z[:, 3 * GW :])
        c = f * cp + i * g
        h = (o * jnp.tanh(c)).astype(BF16).astype(F32)
        gates[at, :] = jnp.concatenate([i, f, o, g], axis=1)
        cells[at, :] = c
        hiddens[at, :] = h
        return h, c

    lax.fori_loop(0, steps, step, (h0.astype(BF16).astype(F32), c0))


def lstm_backward_loop(steps, keep, c0, rt, gates, cells, dhs):
    def step(s, carry):
        dh_next, dc_next = carry
        t = steps - 1 - s
        at = pl.ds(pl.multiple_of(t * 8, 8), 8)
        before = pl.ds(pl.multiple_of(jnp.maximum(t - 1, 0) * 8, 8), 8)
        k = six(keep[at, :])
        saved = gates[at, :]
        i, f, o, g = [saved[:, GW * b : GW * b + GW] for b in range(4)]
        cp = jnp.where(t > 0, cells[before, :], c0) * k
        ct = jnp.tanh(cells[at, :])
        dh = dhs[at, :] + dh_next
        dc = dc_next + dh * o * (1.0 - ct * ct)
        dz = jnp.concatenate(
            [dc * g * i * (1.0 - i), dc * cp * f * (1.0 - f), dh * ct * o * (1.0 - o), dc * i * (1.0 - g * g)], axis=1
        ).astype(BF16)
        gates[at, :] = dz.astype(F32)
        return k * mm(dz, rt[...]), k * dc * f

    zero = jnp.zeros((8, GW), F32)
    lax.fori_loop(0, steps, step, (zero, zero))


ANYWHERE = pl.BlockSpec(memory_space=pl.ANY)
ON_CHIP = pl.BlockSpec(memory_space=pltpu.VMEM)
LIMIT = 56 << 20


def call(kernel, name, ins, specs, outs, scratch, aliases=None):
    return pl.pallas_call(
        kernel,
        out_shape=[jax.ShapeDtypeStruct(shape, dtype) for shape, dtype in outs],
        in_specs=specs,
        out_specs=[ANYWHERE] * len(outs),
        scratch_shapes=scratch,
        input_output_aliases=aliases or {},
        compiler_params=pltpu.CompilerParams(vmem_limit_bytes=LIMIT),
        name=name,
    )(*ins)


def vmem(shape, dtype):
    return pltpu.VMEM(shape, dtype)


def dmas(count):
    return pltpu.SemaphoreType.DMA((count,))


def char_forward_call(ids, km, e8, ab):
    n = ids.shape[0]

    def kernel(ids, km, e8, ab, y2_o, feats_o, pres_o, total_o, emb_o, km_v, e8_v, ab_v, y2, feats, pres, total, emb, sem):
        @pl.when(lax.axis_index("section") == 0)
        def _():
            load([(km, km_v), (e8, e8_v), (ab, ab_v)], sem)
            char_forward(ids, e8_v, km_v, ab_v, emb, total, feats, pres, y2)
            load([(y2, y2_o), (feats, feats_o), (pres, pres_o), (total, total_o), (emb, emb_o)], sem)

    outs = [
        ((n, FW), BF16),
        ((2, n, FW), BF16),
        ((4, n, FW), F32),
        ((n, FW), F32),
        ((3, n, LANE), BF16),
    ]
    scratch = [vmem(km.shape, BF16), vmem(e8.shape, BF16), vmem(ab.shape, BF16)]
    scratch += [vmem(shape, dtype) for shape, dtype in outs] + [dmas(5)]
    return call(kernel, "char_forward", (ids, km, e8, ab), [ON_CHIP] + [ANYWHERE] * 3, outs, scratch)


def char_backward_call(ids, dy, km, ab, saved, tiles):
    n = ids.shape[0]
    feats, pres, total, emb = saved

    def kernel(
        ids, dy, km, ab, feats, pres, total, emb, tiles, tiles_o, bias_o,
        dy_v, km_v, ab_v, feats_v, pres_v, total_v, emb_v, grad, dpre, kt, emb_t, dk, demb, table, y_t, stage, bias, sem,
    ):
        @pl.when(lax.axis_index("section") == 0)
        def _():
            load(
                [(dy, dy_v), (km, km_v), (ab, ab_v), (feats, feats_v), (pres, pres_v), (total, total_v), (emb, emb_v)],
                sem,
            )
            highway_backward(dy_v, ab_v, feats_v, pres_v, grad, dpre)
            conv_backward(ids, km_v, kt, emb_v, emb_t, total_v, grad, dk, demb)
            table_backward(ids, demb, table)
            tile_rows(stage, 0, dk[...], 8, 9)
            tile_rows(stage, 72, table[...], 4, 1)
            highway_weights(feats_v, dpre, y_t, stage, CONV_TILES, bias)
            load([(stage, tiles_o.at[pl.ds(0, stage.shape[0])]), (bias, bias_o)], sem)

    outs = [(tiles.shape, BF16), ((8, FW), F32)]
    scratch = [
        vmem(dy.shape, BF16), vmem(km.shape, BF16), vmem(ab.shape, BF16), vmem(feats.shape, BF16),
        vmem(pres.shape, F32), vmem(total.shape, F32), vmem(emb.shape, BF16),
        vmem((n, FW), F32), vmem((4, n, FW), BF16), vmem((FW, LANE), BF16), vmem((4 * LANE, n), BF16),
        vmem((LANE, FW), F32), vmem((3, n, LANE), F32), vmem((64, LANE), F32), vmem((10 * LANE, n), BF16),
        vmem((CONV_TILES + 35 * 72, 16, LANE), BF16), vmem((8, FW), F32), dmas(7),
    ]
    return call(
        kernel, "char_backward", (ids, dy, km, ab, feats, pres, total, emb, tiles),
        [ON_CHIP] + [ANYWHERE] * 8, outs, scratch, {8: 0},
    )


CONV_TILES = 76
TILES = 3648


def turned_tile(left, right, shift):
    rows = right.shape[0]
    if shift:
        mixed = jnp.where(
            lanes(rows) < shift, pltpu.roll(left.astype(F32), shift, 1), pltpu.roll(right.astype(F32), shift, 1)
        )
        right = mixed.astype(BF16)
    return jnp.transpose(right)


def highway_weights(feats, dpre, y_t, stage, base, bias):
    n = feats.shape[1]
    zero = jnp.zeros((n, LANE), BF16)
    for segment in range(4):
        start = segment * (FILT + 1)
        shift, first, last = start % LANE, start // LANE, (start + FILT) // LANE
        for c in range(10):
            left = feats[segment // 2, :, pl.ds(LANE * (c - 1), LANE)] if c > 0 else zero
            right = feats[segment // 2, :, pl.ds(LANE * c, LANE)] if c < 9 else zero
            y_t[pl.ds(LANE * c, LANE), :] = turned_tile(left, right, shift)

        def block(b, joined):
            rows_t = y_t[pl.ds(pl.multiple_of(LANE * b, LANE), LANE), :]
            at = base + 72 * (first + b)
            for col, width in fblocks(FW):
                value = mm(rows_t, dpre[segment, :, pl.ds(col, width)])
                for r in range(8):
                    for c in range(width // LANE):
                        tile = value[16 * r : 16 * r + 16, LANE * c : LANE * c + LANE].astype(BF16)
                        where = at + 9 * r + col // LANE + c
                        if joined:
                            tile = stage[where] + tile
                        stage[where] = tile
                if segment == 0 and joined is None:
                    row = FILT % LANE
                    bias[:, pl.ds(col, width)] = value[row // 8 * 8 : row // 8 * 8 + 8, :]

        def body(b, carry):
            block(b, False)
            return carry

        if segment == 0:
            lax.fori_loop(0, last, body, 0)
            block(last, None)
        else:
            block(0, True)
            lax.fori_loop(1, last - first + 1, body, 0)


def lstm_forward_call(layer, x, ur, keep, state):
    n = x.shape[0]
    depth = x.shape[1]
    steps = n // 8 - 1

    def kernel(x, ur, keep, state, h_o, gates_o, cells_o, prevs_o, x_v, u_v, r_v, state_v, gates, cells, prevs, hs, h16, sem):
        @pl.when(lax.axis_index("section") == layer)
        def _():
            load(
                [
                    (x, x_v),
                    (ur.at[pl.ds(0, depth)], u_v),
                    (ur.at[pl.ds(1152, GW)], r_v),
                    (state.at[layer - 1], state_v),
                ],
                sem,
            )
            lstm_project(x_v, depth, u_v, r_v[pl.ds(HID, 1), :], gates)
            last = pl.ds(8 * steps, 8)
            prevs[last, :] = jnp.zeros((8, GW), F32)
            hs[last, :] = jnp.zeros((8, GW), F32)
            lstm_forward_loop(steps, keep, state_v[0], state_v[1], r_v, gates, cells, prevs, hs)
            h16[...] = hs[...].astype(BF16)
            load([(h16, h_o), (gates, gates_o), (cells, cells_o), (prevs, prevs_o)], sem)

    outs = [((n, GW), BF16), ((n, ZW), F32), ((n, GW), F32), ((n, GW), F32)]
    scratch = [
        vmem(x.shape, BF16), vmem((depth, ZW), BF16), vmem((GW, ZW), BF16), vmem((2, 8, GW), F32),
        vmem((n, ZW), F32), vmem((n, GW), F32), vmem((n, GW), F32), vmem((n, GW), F32), vmem((n, GW), BF16), dmas(4),
    ]
    return call(
        kernel, f"lstm_forward{layer}", (x, ur, keep, state), [ANYWHERE, ANYWHERE, ON_CHIP, ANYWHERE], outs, scratch
    )


def lstm_backward_call(layer, dh, ur, rt, keep, state, saved, depth_pad):
    n = dh.shape[0]
    steps = n // 8 - 1
    depth = FILT if layer == 1 else HID
    gates, cells, _ = saved

    def kernel(dh, ur, rt, keep, state, gates, cells, dx_o, dz_o, dh_v, u_v, rt_v, state_v, gates_v, cells_v, dhs, dx, dz, sem):
        @pl.when(lax.axis_index("section") == layer)
        def _():
            load(
                [
                    (dh, dh_v),
                    (ur.at[pl.ds(0, depth_pad)], u_v),
                    (rt, rt_v),
                    (state.at[layer - 1], state_v),
                    (gates, gates_v),
                    (cells, cells_v),
                ],
                sem,
            )
            dhs[...] = dh_v[...].astype(F32)
            lstm_backward_loop(steps, keep, state_v[1], rt_v, gates_v, cells_v, dhs)
            gates_v[pl.ds(8 * steps, 8), :] = jnp.zeros((8, ZW), F32)
            dz[...] = gates_v[...].astype(BF16)
            for at, width in fblocks(depth_pad):
                value = mm_nt(dz[...], u_v[pl.ds(at, width), :])
                if at + width > depth:
                    value = jnp.where(column_mask(at, width, depth, n), value, 0.0)
                dx[:, pl.ds(at, width)] = value.astype(BF16)
            load([(dx, dx_o), (dz, dz_o)], sem)

    outs = [((n, depth_pad), BF16), ((n, ZW), BF16)]
    scratch = [
        vmem((n, GW), BF16), vmem((depth_pad, ZW), BF16), vmem((ZW, GW), BF16), vmem((2, 8, GW), F32),
        vmem((n, ZW), F32), vmem((n, GW), F32), vmem((n, GW), F32), vmem((n, depth_pad), BF16), vmem((n, ZW), BF16),
        dmas(6),
    ]
    return call(
        kernel, f"lstm_backward{layer}", (dh, ur, rt, keep, state, gates, cells),
        [ANYWHERE] * 3 + [ON_CHIP] + [ANYWHERE] * 3, outs, scratch,
    )


def lstm_weights_call(layer, x, prevs, dz, tiles):
    n, width_in = x.shape
    depth = FILT if layer == 1 else HID
    blocks = 7 if layer == 1 else 6

    def kernel(x, prevs, dz, tiles, tiles_o, x_v, prevs_v, dz_v, xh_t, stage, sem):
        @pl.when(lax.axis_index("section") == layer)
        def _():
            load([(x, x_v), (prevs, prevs_v), (dz, dz_v)], sem)
            first, shift = depth // LANE, depth % LANE
            zero = jnp.zeros((n, LANE), F32)
            lane = lanes(n)
            end = depth + HID
            for c in range(2 * blocks):
                if c < first:
                    mixed = x_v[:, pl.ds(LANE * c, LANE)]
                else:
                    k = c - first
                    left = prevs_v[:, pl.ds(LANE * (k - 1), LANE)] if 0 < k < 7 else zero
                    right = prevs_v[:, pl.ds(LANE * k, LANE)] if k < 6 else zero
                    before = pltpu.roll(left, shift, 1) if k else x_v[:, pl.ds(LANE * c, LANE)].astype(F32)
                    mixed = jnp.where(lane < shift, before, pltpu.roll(right, shift, 1))
                    mixed = jnp.where(lane + c * LANE == end, 1.0, mixed).astype(BF16)
                xh_t[pl.ds(LANE * c, LANE), :] = jnp.transpose(mixed)

            def body(b, carry):
                rows_t = xh_t[pl.ds(pl.multiple_of(256 * b, 256), 256), :]
                for col, width in fblocks(ZW):
                    value = mm(rows_t, dz_v[:, pl.ds(col, width)])
                    tile_rows(stage, 16 * 24 * b, value, 16, 2, col // LANE, 24)
                return carry

            lax.fori_loop(0, blocks, body, 0)
            count = blocks * 16 * 24
            load([(stage.at[pl.ds(0, count)], tiles_o.at[pl.ds(0, count)])], sem)

    scratch = [
        vmem(x.shape, BF16), vmem((n, GW), F32), vmem((n, ZW), BF16), vmem((blocks * 256, n), BF16),
        vmem((blocks * 16 * 24, 16, LANE), BF16), dmas(3),
    ]
    return call(
        kernel, f"lstm_weights{layer}", (x, prevs, dz, tiles), [ANYWHERE] * 4, [(tiles.shape, BF16)], scratch, {3: 0}
    )[0]


VBLOCKS = VW // 256
VTAIL = VBLOCKS * 256


def each_vocab(body):
    def step(i, carry):
        body(pl.multiple_of(i * 256, 256), 256)
        return carry

    lax.fori_loop(0, VBLOCKS, step, 0)
    body(VTAIL, VW - VTAIL)


def output_call(h, wt, targets, valid):
    n = h.shape[0]
    depth = wt.shape[0]

    def kernel(h, wt, targets, valid, dh_o, dl_o, loss_o, h_v, w_v, logits, dl, top, part, dh, dh16, loss, sem):
        loss[...] = jnp.zeros_like(loss)

        @pl.when(lax.axis_index("section") == 3)
        def _():
            load([(h, h_v), (wt, w_v)], sem)
            col = lax.broadcasted_iota(jnp.int32, (n, GW), 1)
            he = jnp.where(col == HID, 1.0, h_v[...].astype(F32)).astype(BF16)
            h_v[...] = he
            top[...] = jnp.full((n, LANE), -jnp.inf, F32)

            def forward(at, width):
                z = mm(h_v[:, pl.ds(0, depth)], w_v[:, pl.ds(at, width)])
                if width < 256:
                    z = jnp.where(column_mask(at, width, VOCAB, n), z, -jnp.inf)
                logits[:, pl.ds(at, width)] = z
                best = top[...]
                for c in range(width // LANE):
                    best = jnp.maximum(best, z[:, LANE * c : LANE * c + LANE])
                top[...] = best

            each_vocab(forward)
            best = jnp.max(top[...], axis=1, keepdims=True)
            part[...] = jnp.zeros((2, n, LANE), F32)

            def exponents(at, width):
                z = logits[:, pl.ds(at, width)]
                e = jnp.exp(z - best)
                logits[:, pl.ds(at, width)] = e
                for c in range(width // LANE):
                    part[0] += e[:, LANE * c : LANE * c + LANE]
                    hit = lanes(n) + (at + LANE * c) == targets[...]
                    part[1] += jnp.where(hit, z[:, LANE * c : LANE * c + LANE], 0.0)

            each_vocab(exponents)
            total = jnp.sum(part[0], axis=1, keepdims=True)
            picked = jnp.sum(part[1], axis=1, keepdims=True)
            each = valid[...] * (best + jnp.log(total) - picked)
            loss[...] = jnp.sum(each, axis=0, keepdims=True)
            share = 1.0 / total
            dh[...] = jnp.zeros_like(dh)

            def backward(at, width):
                e = logits[:, pl.ds(at, width)]
                pieces = []
                for c in range(width // LANE):
                    hit = lanes(n) + (at + LANE * c) == targets[...]
                    grad = (e[:, LANE * c : LANE * c + LANE] * share - jnp.where(hit, 1.0, 0.0)) * valid[...]
                    pieces.append(grad.astype(BF16))
                grad = jnp.concatenate(pieces, axis=1)
                dl[:, pl.ds(at, width)] = grad
                dh[...] += mm_nt(grad, w_v[:, pl.ds(at, width)])

            each_vocab(backward)
            for at, width in fblocks(depth):
                value = dh[:, pl.ds(at, width)]
                dh16[:, pl.ds(at, width)] = jnp.where(column_mask(at, width, HID, n), value, 0.0).astype(BF16)
            dh16[:, pl.ds(depth, GW - depth)] = jnp.zeros((n, GW - depth), BF16)
            load([(dh16, dh_o), (dl, dl_o)], sem)

        load([(loss, loss_o)], sem)

    outs = [((n, GW), BF16), ((n, VW), BF16), ((1, LANE), F32)]
    scratch = [
        vmem((n, GW), BF16), vmem(wt.shape, BF16), vmem((n, VW), F32), vmem((n, VW), BF16), vmem((n, LANE), F32),
        vmem((2, n, LANE), F32), vmem((n, depth), F32), vmem((n, GW), BF16), vmem((1, LANE), F32), dmas(2),
    ]
    return call(kernel, "output", (h, wt, targets, valid), [ANYWHERE] * 2 + [ON_CHIP] * 2, outs, scratch)


def output_weights_call(h, dl):
    n = h.shape[0]
    rows = 704
    pitch = VW // LANE

    def kernel(h, dl, tiles_o, h_v, dl_v, h_t, stage, sem):
        @pl.when(lax.axis_index("section") == 3)
        def _():
            load([(h, h_v), (dl, dl_v)], sem)
            lane = lanes(n)
            for c in range(6):
                value = h_v[:, pl.ds(LANE * c, LANE)].astype(F32)
                value = jnp.where(lane + c * LANE == HID, 1.0, value).astype(BF16)
                h_t[pl.ds(LANE * c, LANE), :] = jnp.transpose(value)

            def body(at, width):
                first = at // LANE
                for top, count in fblocks(rows):
                    value = mm(h_t[pl.ds(top, count), :], dl_v[:, pl.ds(at, width)])
                    for r in range(count // 16):
                        for c in range(width // LANE):
                            stage[(top // 16 + r) * pitch + first + c] = value[
                                16 * r : 16 * r + 16, LANE * c : LANE * c + LANE
                            ].astype(BF16)

            each_vocab(body)
            count = rows // 16 * pitch
            load([(stage.at[pl.ds(0, count)], tiles_o.at[pl.ds(0, count)])], sem)

    scratch = [
        vmem((n, GW), BF16), vmem((n, VW), BF16), vmem((6 * LANE, n), BF16),
        vmem((rows // 16 * pitch, 16, LANE), BF16), dmas(2),
    ]
    return call(
        kernel, "output_weights", (h, dl), [ANYWHERE] * 2, [((TILES, 16, LANE), BF16)], scratch
    )[0]


FORM = (
    (FILT, 9, 4 * (FILT + 1), CONV_END, CONV_TILES, 32),
    (4 * HID, 24, FILT + HID + 1, 0, 0, 16),
    (4 * HID, 24, 2 * HID + 1, 0, 0, 16),
    (VOCAB, 79, HID + 1, 0, 0, 16),
)


def slab(role, dest, share):
    width, pitch, rows, before, lead, period = FORM[role]
    low = lax.max if not isinstance(dest, int) else max
    high = lax.min if not isinstance(dest, int) else min
    one = (lambda v: v) if isinstance(dest, int) else jnp.int32
    start = low(one(share) * dest - before, one(0))
    first = start // width // period * period
    end = high((share * (dest + 1) - before + width - 1) // width, one(rows))
    count = low((end - first + 15) // 16, one(0)) * pitch
    tile = lead + first // 16 * pitch
    if lead:
        if isinstance(dest, int):
            if dest == 0:
                tile, count = 0, count + lead
        else:
            head = lax.max(1 - dest, 0)
            tile = tile - lead * head
            count = count + lead * head
    return first, tile, count


def slab_pieces(count, size):
    return (count + size - 1) // size


def most_pieces(groups, share, size):
    return max(slab_pieces(slab(role, dest, share)[2], size) for role in range(4) for dest in range(groups))


def gather_sum_call(tiles, bias, loss, groups, share):
    pair = 2
    across = groups // pair
    size = 64 if across <= 4 else 32
    pieces = most_pieces(groups, share, size)
    room = pieces * size
    line = across <= 4
    slots = across + 1 if line else across - 1
    MESH = pl.DeviceIdType.MESH

    def kernel(
        tiles, bias, loss, out, small_out, own, got1, got2, acc, small, got_small,
        own_sem, send1, recv1, send2, recv2, out_sem, small_send, small_recv,
    ):
        role = lax.axis_index("section")
        me = lax.axis_index("dp")
        mine, side = me // pair, lax.rem(me, pair)
        other = mine * pair + (1 - side)

        def at_place(place):
            return {"dp": place * pair + side}

        barrier = pltpu.get_barrier_semaphore()
        pl.semaphore_signal(barrier, inc=1, device_id={"dp": other}, device_id_type=MESH)
        for k in range(1, across):
            peer = at_place(lax.rem(mine + k, across))
            pl.semaphore_signal(barrier, inc=1, device_id=peer, device_id_type=MESH)
        pl.semaphore_wait(barrier, across)

        def part(ref, slot, p):
            return ref.at[slot, pl.ds(pl.multiple_of(p * size, size), size)]

        def span(p):
            return pl.ds(pl.multiple_of(p * size, size), size)

        def loop(count, body):
            def step(p, carry):
                body(p)
                return carry

            lax.fori_loop(0, count, step, 0)

        def small_copy(k):
            if k == 0:
                source, target = small.at[0], {"dp": other}
            else:
                source, target = small.at[1], at_place(lax.rem(mine + k, across))
            return pltpu.make_async_remote_copy(
                source, got_small.at[k], small_send.at[k], small_recv.at[k], device_id=target, device_id_type=MESH
            )

        small[...] = jnp.zeros_like(small)

        @pl.when(role == 0)
        def _():
            row = FILT % LANE % 8
            for at in range(0, FW, LANE):
                small[0, :, pl.ds(at, LANE)] = bias[row : row + 1, pl.ds(at, LANE)]

        @pl.when(role == 3)
        def _():
            small[0, :, pl.ds(FW, LANE)] = loss[...]

        small_copy(0).start()

        def run(shape_of):
            def count_to(place, which):
                return shape_of(place * pair + which)[1]

            def own_copy(place, p):
                tile, _ = shape_of(place * pair + side)
                return pltpu.make_async_copy(
                    tiles.at[pl.ds(tile + p * size, size)], part(own, place, p), own_sem.at[place, p]
                )

            def first_copy(place, p):
                tile, _ = shape_of(place * pair + 1 - side)
                return pltpu.make_async_remote_copy(
                    tiles.at[pl.ds(tile + p * size, size)], part(got1, place, p), send1.at[place, p], recv1.at[place, p],
                    device_id={"dp": other}, device_id_type=MESH,
                )

            def begin(place):
                loop(count_to(place, 1 - side), lambda p: first_copy(place, p).start())
                loop(count_to(place, side), lambda p: own_copy(place, p).start())

            def hop_copy(place, up, p):
                if line:
                    target = mine + 1 if up else mine - 1
                    slot = jnp.where(place == mine + 1, across, place) if up else place
                else:
                    target = place
                    slot = lax.rem(place - mine + across, across) - 1
                return pltpu.make_async_remote_copy(
                    part(own, place, p), part(got2, slot, p), send2.at[place, p], recv2.at[slot, p],
                    device_id=at_place(target), device_id_type=MESH,
                )

            def arrived(slot, p):
                return pltpu.make_async_remote_copy(
                    part(own, 0, p), part(got2, slot, p), send2.at[0, p], recv2.at[slot, p],
                    device_id=at_place(lax.rem(mine + 1, across)), device_id_type=MESH,
                )

            def forward(place, up, has_before):
                def body(p):
                    own_copy(place, p).wait()
                    first_copy(place, p).wait_recv()
                    at = span(p)
                    own[place, at] = (own[place, at].astype(F32) + got1[place, at].astype(F32)).astype(BF16)
                    hop_copy(place, up, p).start()

                def body_sum(p):
                    own_copy(place, p).wait()
                    first_copy(place, p).wait_recv()
                    arrived(place, p).wait_recv()
                    at = span(p)
                    total = own[place, at].astype(F32) + got1[place, at].astype(F32) + got2[place, at].astype(F32)
                    own[place, at] = total.astype(BF16)
                    hop_copy(place, up, p).start()

                count = count_to(place, side)
                if not line:
                    loop(count, body)
                    return

                @pl.when(has_before)
                def _():
                    loop(count, body_sum)

                @pl.when(jnp.logical_not(has_before))
                def _():
                    loop(count, body)

            if line:
                for k in range(across - 1):

                    @pl.when(k < mine)
                    def _(k=k):
                        begin(k)

                    @pl.when(k < across - 1 - mine)
                    def _(k=k):
                        begin(across - 1 - k)

                begin(mine)
                for k in range(across - 1):

                    @pl.when(k < mine)
                    def _(k=k):
                        forward(k, False, mine < across - 1)

                    @pl.when(k < across - 1 - mine)
                    def _(k=k):
                        forward(across - 1 - k, True, mine > 0)

            else:
                for k in range(1, across):
                    begin(lax.rem(mine + k, across))
                begin(mine)
                for k in range(1, across):
                    forward(lax.rem(mine + k, across), True, None)

            small_copy(0).wait_recv()
            small[1] = small[0] + got_small[0]
            for k in range(1, across):
                small_copy(k).start()

            def settle(p):
                own_copy(mine, p).wait()
                first_copy(mine, p).wait_recv()
                at = span(p)
                acc[at] = own[mine, at].astype(F32) + got1[mine, at].astype(F32)

            def add(slot):
                def body(p):
                    arrived(slot, p).wait_recv()
                    at = span(p)
                    acc[at] += got2[slot, at].astype(F32)

                return body

            mine_count = count_to(mine, side)
            loop(mine_count, settle)
            if line:

                @pl.when(mine < across - 1)
                def _():
                    loop(mine_count, add(mine))

                @pl.when(mine > 0)
                def _():
                    loop(mine_count, add(across))

            else:
                for k in range(1, across):
                    loop(mine_count, add(k - 1))

            def out_copy(p):
                return pltpu.make_async_copy(acc.at[span(p)], out.at[span(p)], out_sem.at[p])

            loop(mine_count, lambda p: out_copy(p).start())
            loop(mine_count, lambda p: out_copy(p).wait())
            for place in range(across):
                loop(count_to(place, 1 - side), lambda p, place=place: first_copy(place, p).wait_send())

                @pl.when(place != mine)
                def _(place=place):
                    loop(count_to(place, side), lambda p: hop_copy(place, True, p).wait_send())

        for which in range(4):

            @pl.when(role == which)
            def _(which=which):
                def shape_of(dest):
                    _, tile, count = slab(which, dest, share)
                    return tile, slab_pieces(count, size)

                run(shape_of)

        total = small[1]
        for k in range(1, across):
            small_copy(k).wait_recv()
            total = total + got_small[k]
        small_out[...] = total
        for k in range(across):
            small_copy(k).wait_send()

    sems = pltpu.SemaphoreType.DMA
    return pl.pallas_call(
        kernel,
        out_shape=[
            jax.ShapeDtypeStruct((room, 16, LANE), F32),
            jax.ShapeDtypeStruct((1, FW + LANE), F32),
        ],
        in_specs=[ANYWHERE, ON_CHIP, ON_CHIP],
        out_specs=[ANYWHERE, ON_CHIP],
        scratch_shapes=[
            vmem((across, room, 16, LANE), BF16), vmem((across, room, 16, LANE), BF16),
            vmem((slots, room, 16, LANE), BF16), vmem((room, 16, LANE), F32),
            vmem((2, 1, FW + LANE), F32), vmem((across, 1, FW + LANE), F32),
            sems((across, pieces)), sems((across, pieces)), sems((across, pieces)),
            sems((across, pieces)), sems((slots, pieces)), sems((pieces,)), sems((across,)), sems((across,)),
        ],
        compiler_params=pltpu.CompilerParams(vmem_limit_bytes=62 << 20, collective_id=1, has_side_effects=True),
        name="gather_sum",
    )(tiles, bias, loss)


def sections_sum_call(small):
    count = lax.axis_size("section")

    def kernel(mine, out, held, send, recv):
        me = lax.axis_index("section")
        barrier = pltpu.get_barrier_semaphore()

        def peer(k):
            return {"section": lax.rem(me + k, count)}

        for k in range(1, count):
            pl.semaphore_signal(barrier, inc=1, device_id=peer(k), device_id_type=pl.DeviceIdType.MESH)
        pl.semaphore_wait(barrier, count - 1)
        copies = [
            pltpu.make_async_remote_copy(
                mine, held.at[k], send.at[k], recv.at[k], device_id=peer(k), device_id_type=pl.DeviceIdType.MESH
            )
            for k in range(1, count)
        ]
        for copy in copies:
            copy.start()
        total = mine[...]
        for k, copy in enumerate(copies):
            copy.wait_recv()
            total = total + held[k + 1]
        out[...] = total
        for copy in copies:
            copy.wait_send()

    return pl.pallas_call(
        kernel,
        out_shape=jax.ShapeDtypeStruct(small.shape, F32),
        in_specs=[ON_CHIP],
        out_specs=ON_CHIP,
        scratch_shapes=[vmem((count,) + small.shape, F32), dmas(count), dmas(count)],
        compiler_params=pltpu.CompilerParams(collective_id=2, has_side_effects=True),
        name="sections_sum",
    )(small)


def pack_call(summed, groups, share):
    room = summed.shape[0] * 16
    chunks = share // LANE
    margin = 1280
    slab_rows = 10624
    flat_rows = margin + max(10752, chunks + 1280)

    def kernel(summed, out, rows_v, flat, sem):
        role = lax.axis_index("section")
        me = lax.axis_index("dp")
        zero = jnp.zeros((64, LANE), F32)

        def clear(i, carry):
            flat[pl.ds(pl.multiple_of(i * 64, 64), 64), :] = zero
            return carry

        copy = pltpu.make_async_copy(summed, rows_v.at[pl.ds(0, room)], sem.at[0])
        copy.start()
        lax.fori_loop(0, flat_rows // 64, clear, 0)
        copy.wait()
        lane = lanes()

        for which in range(4):
            width, pitch, rows, before, lead, period = FORM[which]
            if which == 0:
                blocks, cols, tiles = 1, FILT, 9
            elif which == 3:
                blocks, cols, tiles = 1, VOCAB, 79
            else:
                blocks, cols, tiles = 4, HID, 6
            stride = period * width // LANE
            most = max(slab(which, dest, share)[2] for dest in range(groups))
            groups8 = -(-(-(-most // pitch) * 16) // (8 * period))

            @pl.when(role == which)
            def _(which=which):
                first, _, count = slab(which, me, share)
                skip = lead * lax.max(1 - me, 0)
                base = margin + before // LANE + stride * (first // period) - chunks * me

                def row(i, carry):
                    group, n = i // period, lax.rem(i, period)
                    number = first + period * (8 * group + sublanes()) + n
                    keep = number < rows
                    place = skip + n // 16 * pitch
                    source = place * 16 + lax.rem(n, 16) + 8 * group * period * pitch
                    step = 27
                    for b in range(blocks):
                        flat_at = before % LANE + width * n + cols * b
                        turn = lax.rem(flat_at, LANE)
                        to = base + flat_at // LANE + stride * 8 * group
                        last = jnp.zeros((8, LANE), F32)
                        for low in range(0, tiles, step):
                            high = min(low + step, tiles)
                            taken = [
                                rows_v[pl.ds(source + 16 * (tiles * b + j), 8, stride=period * pitch), :]
                                for j in range(low, high)
                            ]
                            turned = [last] + [pltpu.roll(jnp.where(keep, x, 0.0), turn, 1) for x in taken]
                            for j in range(low, high):
                                value = jnp.where(lane >= turn, turned[j - low + 1], turned[j - low])
                                where = pl.ds(to + j, 8, stride=stride)
                                if j == 0:
                                    value = jnp.where(lane >= turn, value, flat[where, :])
                                flat[where, :] = value
                            last = turned[-1]
                        where = pl.ds(to + tiles, 8, stride=stride)
                        flat[where, :] = jnp.where(lane + LANE * tiles - turn < cols, last, flat[where, :])
                    return carry

                @pl.when(count > 0)
                def _():
                    lax.fori_loop(0, period * groups8, row, 0)

        @pl.when((role == 0) & (me == 0))
        def _():
            lane1 = lanes(1)

            def piece(row_at, flat_at, low, size):
                edge = flat_at - low
                turn = edge % LANE
                to = margin + (edge - turn) // LANE
                first, end = low // LANE, (low + size - 1) // LANE
                last = jnp.zeros((1, LANE), F32)
                for j in range(first, end + 2):
                    least, most = max(low + turn - LANE * j, 0), min(low + size + turn - LANE * j, LANE)
                    here = last
                    if j <= end:
                        here = rows_v[row_at + 16 * j : row_at + 16 * j + 1, :]
                        here = pltpu.roll(here, turn, 1) if turn else here
                    if most > least:
                        value = jnp.where(lane1 >= turn, here, last) if turn else here
                        at = to + j
                        if least > 0 or most < LANE:
                            value = jnp.where((lane1 >= least) & (lane1 < most), value, flat[at : at + 1, :])
                        flat[at : at + 1, :] = value
                    last = here

            for k in range(1, 8):
                n = NFILT[k - 1]
                for i in range(k * D_CHAR + 1):
                    number = i + i // D_CHAR if i < k * D_CHAR else 15
                    piece(number // 16 * 144 + number % 16, KOFF[k - 1] + n * i, COLS[k - 1], n)
            for a in range(CHAR_V):
                piece(72 * 16 + a, D_CHAR * a, 0, D_CHAR)

        copy = pltpu.make_async_copy(flat.at[pl.ds(margin, chunks)], out, sem.at[0])
        copy.start()
        copy.wait()

    return pl.pallas_call(
        kernel,
        out_shape=jax.ShapeDtypeStruct((chunks, LANE), F32),
        in_specs=[ANYWHERE],
        out_specs=ANYWHERE,
        scratch_shapes=[vmem((slab_rows, LANE), F32), vmem((flat_rows, LANE), F32), pltpu.SemaphoreType.DMA((1,))],
        compiler_params=pltpu.CompilerParams(vmem_limit_bytes=LIMIT),
        name="pack",
    )(summed.reshape(room, LANE))


def shards(char_ids, target_ids, remaining, resets, start_state, section_params):
    rows, steps = char_ids.shape[:2]
    groups = lax.axis_size("dp")
    packed = section_params.shape[1]
    share = packed // groups
    n = rows * (steps + 1)

    def by_step(x, fill):
        x = jnp.pad(x.T, ((0, 1), (0, 0)), constant_values=fill)
        return jnp.broadcast_to(x.reshape(n, 1), (n, LANE))

    ids = jnp.pad(
        char_ids.transpose(1, 0, 2), ((0, 1), (0, 0), (0, LANE - WORD_CHARS)), constant_values=-1
    ).reshape(n, LANE)
    targets = by_step(target_ids, -1)
    keep = by_step(1.0 - resets.astype(F32), 0.0)
    valid = by_step((jnp.arange(steps, dtype=jnp.int32)[None, :] < remaining[:, None]).astype(F32), 0.0)
    state = jnp.pad(start_state, ((0, 0), (0, 0), (0, 0), (0, GW - HID)))

    km, e8, ab, ur, rt, wt = unpack_all(section_params)
    y2, *char_saved = char_forward_call(ids, km, e8, ab)
    x1 = lax.ppermute(y2, "section", [(0, 1)])
    h1, *saved1 = lstm_forward_call(1, x1, ur, keep, state)
    x2 = lax.ppermute(h1, "section", [(1, 2)])
    h2, *saved2 = lstm_forward_call(2, x2, ur, keep, state)
    x3 = lax.ppermute(h2, "section", [(2, 3)])
    dh2, dl, loss = output_call(x3, wt, targets, valid)
    g2 = lax.ppermute(dh2, "section", [(3, 2)])
    tiles = output_weights_call(x3, dl)
    dx2, dz2 = lstm_backward_call(2, g2, ur, rt, keep, state, saved2, GW)
    g1 = lax.ppermute(dx2, "section", [(2, 1)])
    tiles = lstm_weights_call(2, x2, saved2[2], dz2, tiles)
    dx1, dz1 = lstm_backward_call(1, g1, ur, rt, keep, state, saved1, FW)
    g0 = lax.ppermute(dx1, "section", [(1, 0)])
    tiles = lstm_weights_call(1, x1, saved1[2], dz1, tiles)
    tiles, bias = char_backward_call(ids, g0, km, ab, char_saved, tiles)
    summed, small = gather_sum_call(tiles, bias, loss, groups, share)
    flat = pack_call(summed, groups, share)
    small = sections_sum_call(small)
    mean_loss = small[0, FW] / (groups * rows * steps)
    return mean_loss, flat.reshape(1, share), small[0, :FILT]


def solution(mesh):
    in_specs = (
        P("dp", None, None),
        P("dp", None),
        P("dp"),
        P("dp", None),
        P(None, None, "dp", None),
        P("section", None),
    )
    out_specs = (P(), P("section", "dp"), P())
    return jax.shard_map(shards, mesh=mesh, in_specs=in_specs, out_specs=out_specs, check_vma=False)
```

```python
import functools
import math

import jax
import jax.numpy as jnp
from jax import lax
from jax.experimental import pallas as pl
from jax.experimental.pallas import tpu as pltpu
from jax.sharding import PartitionSpec as P

D_CHAR = 15
CHAR_V = 51
F_UNIT = 50
WORD_CHARS = 21
HID = 650
VOCAB = 10000
FILT = 1100
F32 = jnp.float32
BF16 = jnp.bfloat16

NFILT = [F_UNIT * min(k, 4) for k in range(1, 8)]
COLS = [sum(NFILT[:k]) for k in range(8)]
KOFF = [CHAR_V * D_CHAR + sum((j * D_CHAR + 1) * NFILT[j - 1] for j in range(1, k)) for k in range(1, 9)]
CONV_END = KOFF[7]
HIGH_STRIDE = FILT * (FILT + 1)
FW = 1152
GW = 768
ZW = 4 * GW
VW = 10112
LANE = 128
LENS = (2304, 2688, 2688, 5120)


def roll_lanes(x, shift):
    return pltpu.roll(x, shift, 1)


def lanes(rows=8):
    return lax.broadcasted_iota(jnp.int32, (rows, LANE), 1)


def sublanes():
    return lax.broadcasted_iota(jnp.int32, (8, LANE), 0)


def widen(raw, slot, rows, wide):
    def body(i, carry):
        piece = raw[slot, 0:1, pl.ds(pl.multiple_of(i * 16384, 16384), 16384)]
        wide[pl.ds(pl.multiple_of(i * 128, 128), 128), :] = piece.astype(F32).reshape(128, LANE)
        return carry

    lax.fori_loop(0, rows // 128, body, 0)


def stream_blocks(count, length, total, chunk_of, src, raw, sem, wide, work):
    def start_of(i):
        first = chunk_of(i)
        return jnp.minimum(first // 8 * 8, total - length)

    def copy(i, slot):
        at = pl.multiple_of(start_of(i) * LANE, 8 * LANE)
        return pltpu.make_async_copy(
            src.at[:, pl.ds(at, length * LANE)], raw.at[slot, :, pl.ds(0, length * LANE)], sem.at[slot]
        )

    copy(0, 0).start()

    def body(i, carry):
        slot = lax.rem(i, 2)

        @pl.when(i + 1 < count)
        def _():
            copy(i + 1, 1 - slot).start()

        copy(i, slot).wait()
        widen(raw, slot, length, wide)
        work(i, chunk_of(i) - start_of(i))
        return carry

    lax.fori_loop(0, count, body, 0)


def take_rows(wide, starts, tiles, cols, stride, put):
    step = max(1, 28 // len(starts))
    lane = lanes()
    for low in range(0, tiles, step):
        high = min(tiles, low + step)
        loaded = [
            [wide[pl.ds(first + c, 8, stride=stride), :] for c in range(low, high + 1)] for _, first, _, _ in starts
        ]
        results = []
        for (_, _, shift, keep_row), pieces in zip(starts, loaded):
            turn = lax.rem(LANE - shift, LANE)
            split = lane < LANE - shift
            turned = [roll_lanes(piece, turn) for piece in pieces]
            for c in range(low, high):
                out = jnp.where(split, turned[c - low], turned[c - low + 1])
                keep = keep_row
                if cols - c * LANE < LANE:
                    keep = keep & (lane < cols - c * LANE)
                results.append(jnp.where(keep, out, 0.0))
        at = 0
        for tag, _, _, _ in starts:
            for c in range(low, high):
                put(tag, c, results[at])
                at += 1


def spread(c, n, period):
    return pl.ds((c * period + n) * 25, 8, stride=3)


def collect(dest, c, period):
    return [
        dest[pl.ds((c * period + 8 * m) * 25 + 3 * j, 8, stride=25), :] for j in range(8) for m in range(period // 8)
    ]


def stage_tile(stage, slot, c, blocks):
    for i in range(0, len(blocks), 2):
        pair = jnp.concatenate([blocks[i], blocks[i + 1]], axis=0).astype(BF16)
        stage[slot, pl.ds(8 * i, 16), pl.ds(c * LANE, LANE)] = pair


def unpack_kernel(
    src, km, e8, ab, ur, rt, wt, raw, wide, dest, kstage, stage0, stage1, stage_t, stage3, sem_in, sem_out, sem_t
):
    role = lax.axis_index("section")
    total = src.shape[1] // LANE

    def out_copy(stage, slot, target):
        return pltpu.make_async_copy(stage.at[slot], target, sem_out.at[slot])

    @pl.when(role == 0)
    def _():
        length = 640
        copy = pltpu.make_async_copy(
            src.at[:, pl.ds(0, length * LANE)], raw.at[0, :, pl.ds(0, length * LANE)], sem_in.at[0]
        )
        copy.start()
        copy.wait()
        widen(raw, 0, length, wide)
        lane1 = lanes(1)
        dest[pl.ds(0, 64), :] = jnp.zeros((64, LANE), F32)
        for a in range(CHAR_V):
            flat = D_CHAR * a
            q, s = flat // LANE, flat % LANE
            here = wide[q : q + 1, :]
            out = roll_lanes(here, (LANE - s) % LANE) if s else here
            if s + D_CHAR > LANE:
                out = jnp.where(lane1 < LANE - s, out, roll_lanes(wide[q + 1 : q + 2, :], LANE - s))
            dest[a : a + 1, :] = jnp.where(lane1 < D_CHAR, out, jnp.where(lane1 == D_CHAR, 1.0, 0.0))
        table = dest[pl.ds(0, 64), :]
        for m in range(8):
            kstage[pl.ds(64 * m, 64), pl.ds(0, LANE)] = (
                pltpu.roll(table, 16 * m, 1) if m else table
            ).astype(BF16)
        copy = pltpu.make_async_copy(kstage.at[pl.ds(0, 512), pl.ds(0, LANE)], e8, sem_out.at[0])
        copy.start()
        copy.wait()
        tiles = FW // LANE
        rows = 112
        dest[pl.ds(0, rows * tiles), :] = jnp.zeros((rows * tiles, LANE), F32)

        def kernel_row(k, i, row):
            n, base = NFILT[k - 1], COLS[k - 1]
            edge = KOFF[k - 1] + n * i - base
            q, s = edge // LANE, edge % LANE
            for ct in range(base // LANE, (base + n - 1) // LANE + 1):
                out = wide[q + ct : q + ct + 1, :]
                if s:
                    after = roll_lanes(wide[q + ct + 1 : q + ct + 2, :], LANE - s)
                    out = jnp.where(lane1 < LANE - s, roll_lanes(out, LANE - s), after)
                at = ct * rows + row
                low, high = max(base - ct * LANE, 0), min(base + n - ct * LANE, LANE)
                if low > 0 or high < LANE:
                    out = jnp.where((lane1 >= low) & (lane1 < high), out, dest[at : at + 1, :])
                dest[at : at + 1, :] = out

        for k in range(1, 8):
            for i in range(k * D_CHAR):
                kernel_row(k, i, i + i // D_CHAR)
            kernel_row(k, k * D_CHAR, 15)
        kstage[...] = jnp.zeros_like(kstage)
        for ct in range(tiles):
            kstage[pl.ds(112, rows), pl.ds(ct * LANE, LANE)] = dest[pl.ds(ct * rows, rows), :].astype(BF16)
        copy = pltpu.make_async_copy(kstage.at[pl.ds(0, 368)], km, sem_out.at[0])
        copy.start()
        copy.wait()

        blocks = 5

        def flat_of(i):
            return CONV_END + HIGH_STRIDE * (i // blocks)

        def chunk_of(i):
            return flat_of(i) // LANE + 2200 * lax.rem(i, blocks)

        def target(i):
            return ab.at[i // blocks, pl.ds(pl.multiple_of(lax.rem(i, blocks) * 256, 256), 256)]

        def work(i, extra):
            block = lax.rem(i, blocks)
            inner = lax.rem(flat_of(i), LANE)

            def rows_of(i, carry):
                starts = []
                for n in (2 * i, 2 * i + 1):
                    flat = inner + FILT * n
                    keep = 32 * (8 * block + sublanes()) + n <= FILT
                    starts.append((n, flat // LANE + extra, lax.rem(flat, LANE), keep))

                def put(n, c, value):
                    dest[spread(c, n, 32), :] = value

                take_rows(wide, starts, tiles, FILT, 275, put)
                return carry

            lax.fori_loop(0, 16, rows_of, 0)
            slot = lax.rem(i, 2)

            @pl.when(i >= 2)
            def _():
                out_copy(stage0, slot, target(i - 2)).wait()

            for c in range(tiles):
                stage_tile(stage0, slot, c, collect(dest, c, 32))
            out_copy(stage0, slot, target(i)).start()

        count = 4 * blocks
        stream_blocks(count, LENS[0], total, chunk_of, src, raw, sem_in, wide, work)
        for i in (count - 2, count - 1):
            out_copy(stage0, i % 2, target(i)).wait()

    for layer in (1, 2):

        @pl.when(role == layer)
        def _(layer=layer):
            depth = FILT if layer == 1 else HID
            blocks = -(-depth // 128)
            recurrent = depth * 4 * HID
            count = blocks + 6

            def chunk_of(i):
                return jnp.where(i < blocks, 2600 * i, recurrent // LANE + 2600 * (i - blocks))

            def target(i):
                at = jnp.where(i < blocks, i, i - blocks + 9)
                return ur.at[pl.ds(pl.multiple_of(at * 128, 128), 128)]

            def work(i, extra):
                inner = jnp.where(i < blocks, 0, recurrent % LANE)
                block = jnp.where(i < blocks, i, i - blocks)
                limit = jnp.where(i < blocks, depth, HID + 1)

                def rows_of(n, carry):
                    keep = 16 * (8 * block + sublanes()) + n < limit
                    flats = [inner + 4 * HID * n + HID * b for b in range(4)]

                    def put(b, c, value):
                        dest[spread(6 * b + c, n, 16), :] = value

                    starts = [(b, flat // LANE + extra, lax.rem(flat, LANE), keep) for b, flat in enumerate(flats)]
                    take_rows(wide, starts, 6, HID, 325, put)
                    return carry

                lax.fori_loop(0, 16, rows_of, 0)
                slot = lax.rem(i, 2)

                @pl.when(i >= 2)
                def _():
                    out_copy(stage1, slot, target(i - 2)).wait()

                for c in range(24):
                    stage_tile(stage1, slot, c, collect(dest, c, 16))
                out_copy(stage1, slot, target(i)).start()

                @pl.when(i >= blocks)
                def _():
                    @pl.when(i >= blocks + 2)
                    def _():
                        turned_copy(i - 2).wait()

                    k = LANE * block + lanes(LANE)
                    for c in range(24):
                        turned = jnp.transpose(jnp.concatenate(collect(dest, c, 16), axis=0))
                        stage_t[slot, pl.ds(128 * c, 128), :] = jnp.where(k < HID, turned, 0.0).astype(BF16)
                    turned_copy(i).start()

            def turned_copy(i):
                slot = lax.rem(i, 2)
                at = pl.multiple_of((i - blocks) * LANE, LANE)
                return pltpu.make_async_copy(stage_t.at[slot], rt.at[:, pl.ds(at, LANE)], sem_t.at[slot])

            stream_blocks(count, LENS[1], total, chunk_of, src, raw, sem_in, wide, work)
            for i in (count - 2, count - 1):
                out_copy(stage1, i % 2, target(jnp.int32(i))).wait()
                turned_copy(jnp.int32(i)).wait()

    @pl.when(role == 3)
    def _():
        count = 11
        tiles = VW // LANE

        def chunk_of(i):
            return 5000 * i

        def target(i):
            return wt.at[pl.ds(pl.multiple_of(i * 64, 64), 64)]

        def work(i, extra):
            def rows_of(n, carry):
                flat = VOCAB * n
                keep = 8 * (8 * i + sublanes()) + n < HID + 1

                def put(n, c, value):
                    dest[spread(c, n, 8), :] = value

                take_rows(wide, [(n, flat // LANE + extra, lax.rem(flat, LANE), keep)], tiles, VOCAB, 625, put)
                return carry

            lax.fori_loop(0, 8, rows_of, 0)
            slot = lax.rem(i, 2)

            @pl.when(i >= 2)
            def _():
                out_copy(stage3, slot, target(i - 2)).wait()

            for c in range(tiles):
                stage_tile(stage3, slot, c, collect(dest, c, 8))
            out_copy(stage3, slot, target(i)).start()

        stream_blocks(count, LENS[3], total, chunk_of, src, raw, sem_in, wide, work)
        for i in (count - 2, count - 1):
            out_copy(stage3, i % 2, target(jnp.int32(i))).wait()


def unpack_all(section_params):
    anywhere = pl.BlockSpec(memory_space=pl.ANY)
    return pl.pallas_call(
        unpack_kernel,
        out_shape=[
            jax.ShapeDtypeStruct((368, FW), BF16),
            jax.ShapeDtypeStruct((512, LANE), BF16),
            jax.ShapeDtypeStruct((4, 1280, FW), BF16),
            jax.ShapeDtypeStruct((15 * 128, ZW), BF16),
            jax.ShapeDtypeStruct((ZW, GW), BF16),
            jax.ShapeDtypeStruct((11 * 64, VW), BF16),
        ],
        in_specs=[anywhere],
        out_specs=[anywhere] * 6,
        scratch_shapes=[
            pltpu.VMEM((2, 1, LENS[3] * LANE), BF16),
            pltpu.VMEM((9312, LANE), F32),
            pltpu.VMEM((79 * 200, LANE), F32),
            pltpu.VMEM((512, FW), BF16),
            pltpu.VMEM((2, 256, FW), BF16),
            pltpu.VMEM((2, 128, ZW), BF16),
            pltpu.VMEM((2, ZW, LANE), BF16),
            pltpu.VMEM((2, 64, VW), BF16),
            pltpu.SemaphoreType.DMA((2,)),
            pltpu.SemaphoreType.DMA((2,)),
            pltpu.SemaphoreType.DMA((2,)),
        ],
        compiler_params=pltpu.CompilerParams(vmem_limit_bytes=56 << 20),
        name="unpack",
    )(section_params)


def fblocks(width, step=256):
    return [(at, min(step, width - at)) for at in range(0, width, step)]


def mm(a, b):
    return jnp.dot(a, b, preferred_element_type=F32)


def mm_tn(a, b):
    return lax.dot_general(a, b, (((0,), (0,)), ((), ())), preferred_element_type=F32)


def mm_nt(a, b):
    return lax.dot_general(a, b, (((1,), (1,)), ((), ())), preferred_element_type=F32)


def sigmoid(x):
    return 0.5 * jnp.tanh(0.5 * x) + 0.5


def load(pairs, sem):
    copies = [pltpu.make_async_copy(a, b, sem.at[i]) for i, (a, b) in enumerate(pairs)]
    for copy in copies:
        copy.start()
    for copy in copies:
        copy.wait()


def column_mask(at, width, limit, rows):
    return lax.broadcasted_iota(jnp.int32, (rows, width), 1) + at < limit


def char_onehot(ids, t):
    rows = ids.shape[0]
    lane = lanes(rows)
    pieces = []
    for pair in range(4):
        j = 8 * t + 2 * pair
        left = ids[:, j : j + 1]
        right = ids[:, j + 1 : j + 2]
        hit = jnp.where(lane < 64, left, right) == lax.rem(lane, 64)
        pieces.append(jnp.where(hit, 1.0, 0.0).astype(BF16))
    return jnp.concatenate(pieces, axis=1)


def conv_steps(body):
    def step(p, carry):
        body(p, p // 8, True, lax.rem(p, 8), FILT)
        return carry

    lax.fori_loop(0, 15, step, 0)
    body(15, 1, True, 7, COLS[6])
    for p in range(16, WORD_CHARS):
        body(p, 2, False, p - 16, COLS[WORD_CHARS - p])


def conv_at(emb, km, tile, second, within, at, width):
    first = 112 - 16 * within
    if not isinstance(first, int):
        first = pl.multiple_of(first, 16)
    if second:
        window = jnp.concatenate([emb[tile], emb[tile + 1]], axis=1)
    else:
        window = emb[tile]
    return mm(window, km[pl.ds(first, window.shape[1]), pl.ds(at, width)])


def char_forward(ids, e8, km, ab, emb, total, feats, pres, out):
    rows = ids.shape[0]
    for t in range(3):
        emb[t] = mm(char_onehot(ids, t), e8[...]).astype(BF16)
    total[...] = jnp.zeros_like(total)

    def step(p, tile, second, within, limit):
        for at, width in fblocks(FW):
            if at >= limit:
                continue
            value = jnp.exp(jnp.tanh(conv_at(emb, km, tile, second, within, at, width)))
            if at + width > limit and limit < FILT:
                value = jnp.where(column_mask(at, width, limit, rows), value, 0.0)
            total[:, pl.ds(at, width)] += value

    conv_steps(step)
    for at, width in fblocks(FW):
        col = lax.broadcasted_iota(jnp.int32, (rows, width), 1) + at
        count = jnp.full((rows, width), float(WORD_CHARS), F32)
        for k in range(1, 7):
            count = jnp.where(col >= COLS[k], float(WORD_CHARS - k), count)
        value = jnp.log(total[:, pl.ds(at, width)]) - jnp.log(count)
        value = jnp.where(col < FILT, value, jnp.where(col == FILT, 1.0, 0.0))
        feats[0, :, pl.ds(at, width)] = value.astype(BF16)
    for layer in range(2):
        for at, width in fblocks(FW):
            cols = pl.ds(at, width)
            t_pre = mm(feats[layer], ab[2 * layer, pl.ds(0, FW), cols])
            h_pre = mm(feats[layer], ab[2 * layer + 1, pl.ds(0, FW), cols])
            pres[2 * layer, :, cols] = t_pre
            pres[2 * layer + 1, :, cols] = h_pre
            gate = sigmoid(t_pre)
            y = feats[layer, :, cols].astype(F32)
            value = gate * (h_pre * sigmoid(h_pre)) + (1.0 - gate) * y
            col = lax.broadcasted_iota(jnp.int32, (rows, width), 1) + at
            if layer == 0:
                value = jnp.where(col < FILT, value, jnp.where(col == FILT, 1.0, 0.0))
                feats[1, :, cols] = value.astype(BF16)
            else:
                out[:, cols] = jnp.where(col < FILT, value, 0.0).astype(BF16)


def highway_backward(dy, ab, feats, pres, grad, dpre):
    rows = grad.shape[0]
    for at, width in fblocks(FW):
        cols = pl.ds(at, width)
        grad[:, cols] = jnp.where(column_mask(at, width, FILT, rows), dy[:, cols].astype(F32), 0.0)
    for layer in (1, 0):
        for at, width in fblocks(FW):
            cols = pl.ds(at, width)
            g = grad[:, cols]
            gate = sigmoid(pres[2 * layer, :, cols])
            q = pres[2 * layer + 1, :, cols]
            sig = sigmoid(q)
            y = feats[layer, :, cols].astype(F32)
            dpre[2 * layer, :, cols] = (g * (q * sig - y) * gate * (1.0 - gate)).astype(BF16)
            dpre[2 * layer + 1, :, cols] = (g * gate * sig * (1.0 + q * (1.0 - sig))).astype(BF16)
            grad[:, cols] = g * (1.0 - gate)
        for at, width in fblocks(FW):
            cols = pl.ds(at, width)
            value = (
                grad[:, cols]
                + mm_nt(dpre[2 * layer], ab[2 * layer, cols, :])
                + mm_nt(dpre[2 * layer + 1], ab[2 * layer + 1, cols, :])
            )
            if at + width > FILT:
                value = jnp.where(column_mask(at, width, FILT, rows), value, 0.0)
            grad[:, cols] = value


def conv_backward(ids, km, kt, emb, emb_t, total, grad, dk, demb):
    rows = grad.shape[0]
    kt[...] = jnp.transpose(km[pl.ds(112, LANE), :])
    for t in range(3):
        emb_t[pl.ds(LANE * t, LANE), :] = jnp.transpose(emb[t])
    emb_t[pl.ds(3 * LANE, LANE), :] = jnp.zeros((LANE, rows), BF16)
    dk[...] = jnp.zeros_like(dk)
    demb[...] = jnp.zeros_like(demb)
    for at, width in fblocks(FW):
        cols = pl.ds(at, width)
        grad[:, cols] = grad[:, cols] / total[:, cols]

    def step(p, tile, second, within, limit):
        window_t = emb_t[pl.ds(p * 16 if isinstance(p, int) else pl.multiple_of(p * 16, 16), LANE), :]
        back = jnp.zeros((rows, LANE), F32)
        for at, width in fblocks(FW):
            if at >= limit:
                continue
            cols = pl.ds(at, width)
            act = jnp.tanh(conv_at(emb, km, tile, second, within, at, width))
            dz = grad[:, cols] * jnp.exp(act) * (1.0 - act * act)
            if at + width > limit and limit < FILT:
                dz = jnp.where(column_mask(at, width, limit, rows), dz, 0.0)
            dz = dz.astype(BF16)
            dk[:, cols] += mm(window_t, dz)
            back = back + mm(dz, kt[cols, :])
        lane = lanes(rows)
        back = jnp.where(lane < 112, back, 0.0)
        turned = pltpu.roll(back, 16 * within, 1)
        demb[tile] += jnp.where(lane >= 16 * within, turned, 0.0)
        if second:
            demb[tile + 1] += jnp.where(lane < 16 * within, turned, 0.0)

    conv_steps(step)


def table_backward(ids, demb, table):
    acc = jnp.zeros((64, LANE), F32)
    for t in range(3):
        hot = char_onehot(ids, t)
        value = demb[t]
        high = value.astype(BF16)
        low = (value - high.astype(F32)).astype(BF16)
        grads = mm_tn(hot, high) + mm_tn(hot, low)
        for m in range(8):
            block = grads[64 * m : 64 * m + 64, :]
            acc = acc + (pltpu.roll(block, LANE - 16 * m, 1) if m else block)
    table[...] = acc


def tile_rows(stage, base, value, row_tiles, col_tiles, first_col=0, pitch=None):
    pitch = col_tiles if pitch is None else pitch
    for r in range(row_tiles):
        for c in range(col_tiles):
            stage[base + r * pitch + first_col + c] = value[16 * r : 16 * r + 16, LANE * c : LANE * c + LANE].astype(BF16)


def six(x):
    return jnp.concatenate([x] * 6, axis=1)


ANYWHERE = pl.BlockSpec(memory_space=pl.ANY)
ON_CHIP = pl.BlockSpec(memory_space=pltpu.VMEM)
LIMIT = 56 << 20


def call(kernel, name, ins, specs, outs, scratch, aliases=None):
    return pl.pallas_call(
        kernel,
        out_shape=[jax.ShapeDtypeStruct(shape, dtype) for shape, dtype in outs],
        in_specs=specs,
        out_specs=[ANYWHERE] * len(outs),
        scratch_shapes=scratch,
        input_output_aliases=aliases or {},
        compiler_params=pltpu.CompilerParams(vmem_limit_bytes=LIMIT),
        name=name,
    )(*ins)


def vmem(shape, dtype):
    return pltpu.VMEM(shape, dtype)


def dmas(count):
    return pltpu.SemaphoreType.DMA((count,))


def char_forward_call(ids, km, e8, ab):
    n = ids.shape[0]

    def kernel(ids, km, e8, ab, y2_o, feats_o, pres_o, total_o, emb_o, km_v, e8_v, ab_v, y2, feats, pres, total, emb, sem):
        @pl.when(lax.axis_index("section") == 0)
        def _():
            load([(km, km_v), (e8, e8_v), (ab, ab_v)], sem)
            char_forward(ids, e8_v, km_v, ab_v, emb, total, feats, pres, y2)
            load([(y2, y2_o), (feats, feats_o), (pres, pres_o), (total, total_o), (emb, emb_o)], sem)

    outs = [
        ((n, FW), BF16),
        ((2, n, FW), BF16),
        ((4, n, FW), F32),
        ((n, FW), F32),
        ((3, n, LANE), BF16),
    ]
    scratch = [vmem(km.shape, BF16), vmem(e8.shape, BF16), vmem(ab.shape, BF16)]
    scratch += [vmem(shape, dtype) for shape, dtype in outs] + [dmas(5)]
    return call(kernel, "char_forward", (ids, km, e8, ab), [ON_CHIP] + [ANYWHERE] * 3, outs, scratch)


def char_backward_call(ids, dy, km, ab, saved, tiles):
    n = ids.shape[0]
    feats, pres, total, emb = saved

    def kernel(
        ids, dy, km, ab, feats, pres, total, emb, tiles, tiles_o, bias_o,
        dy_v, km_v, ab_v, feats_v, pres_v, total_v, emb_v, grad, dpre, kt, emb_t, dk, demb, table, y_t, stage, bias, sem,
    ):
        @pl.when(lax.axis_index("section") == 0)
        def _():
            load(
                [(dy, dy_v), (km, km_v), (ab, ab_v), (feats, feats_v), (pres, pres_v), (total, total_v), (emb, emb_v)],
                sem,
            )
            highway_backward(dy_v, ab_v, feats_v, pres_v, grad, dpre)
            conv_backward(ids, km_v, kt, emb_v, emb_t, total_v, grad, dk, demb)
            table_backward(ids, demb, table)
            tile_rows(stage, 0, dk[...], 8, 9)
            tile_rows(stage, 72, table[...], 4, 1)
            highway_weights(feats_v, dpre, y_t, stage, CONV_TILES, bias)
            load([(stage, tiles_o.at[pl.ds(0, stage.shape[0])]), (bias, bias_o)], sem)

    outs = [(tiles.shape, BF16), ((8, FW), F32)]
    scratch = [
        vmem(dy.shape, BF16), vmem(km.shape, BF16), vmem(ab.shape, BF16), vmem(feats.shape, BF16),
        vmem(pres.shape, F32), vmem(total.shape, F32), vmem(emb.shape, BF16),
        vmem((n, FW), F32), vmem((4, n, FW), BF16), vmem((FW, LANE), BF16), vmem((4 * LANE, n), BF16),
        vmem((LANE, FW), F32), vmem((3, n, LANE), F32), vmem((64, LANE), F32), vmem((10 * LANE, n), BF16),
        vmem((CONV_TILES + 35 * 72, 16, LANE), BF16), vmem((8, FW), F32), dmas(7),
    ]
    return call(
        kernel, "char_backward", (ids, dy, km, ab, feats, pres, total, emb, tiles),
        [ON_CHIP] + [ANYWHERE] * 8, outs, scratch, {8: 0},
    )


CONV_TILES = 76
TILES = 3648


def turned_tile(left, right, shift):
    rows = right.shape[0]
    if shift:
        mixed = jnp.where(
            lanes(rows) < shift, pltpu.roll(left.astype(F32), shift, 1), pltpu.roll(right.astype(F32), shift, 1)
        )
        right = mixed.astype(BF16)
    return jnp.transpose(right)


def highway_weights(feats, dpre, y_t, stage, base, bias):
    n = feats.shape[1]
    zero = jnp.zeros((n, LANE), BF16)
    for segment in range(4):
        start = segment * (FILT + 1)
        shift, first, last = start % LANE, start // LANE, (start + FILT) // LANE
        for c in range(10):
            left = feats[segment // 2, :, pl.ds(LANE * (c - 1), LANE)] if c > 0 else zero
            right = feats[segment // 2, :, pl.ds(LANE * c, LANE)] if c < 9 else zero
            y_t[pl.ds(LANE * c, LANE), :] = turned_tile(left, right, shift)

        def block(b, joined):
            rows_t = y_t[pl.ds(pl.multiple_of(LANE * b, LANE), LANE), :]
            at = base + 72 * (first + b)
            for col, width in fblocks(FW):
                value = mm(rows_t, dpre[segment, :, pl.ds(col, width)])
                for r in range(8):
                    for c in range(width // LANE):
                        tile = value[16 * r : 16 * r + 16, LANE * c : LANE * c + LANE].astype(BF16)
                        where = at + 9 * r + col // LANE + c
                        if joined:
                            tile = stage[where] + tile
                        stage[where] = tile
                if segment == 0 and joined is None:
                    row = FILT % LANE
                    bias[:, pl.ds(col, width)] = value[row // 8 * 8 : row // 8 * 8 + 8, :]

        def body(b, carry):
            block(b, False)
            return carry

        if segment == 0:
            lax.fori_loop(0, last, body, 0)
            block(last, None)
        else:
            block(0, True)
            lax.fori_loop(1, last - first + 1, body, 0)


def lstm_weights_call(layer, x, prevs, dz, tiles):
    n, width_in = x.shape
    depth = FILT if layer == 1 else HID
    blocks = 7 if layer == 1 else 6

    def kernel(x, prevs, dz, tiles, tiles_o, x_v, prevs_v, dz_v, xh_t, stage, sem):
        @pl.when(lax.axis_index("section") == layer)
        def _():
            load([(x, x_v), (prevs, prevs_v), (dz, dz_v)], sem)
            first, shift = depth // LANE, depth % LANE
            zero = jnp.zeros((n, LANE), F32)
            lane = lanes(n)
            end = depth + HID
            for c in range(2 * blocks):
                if c < first:
                    mixed = x_v[:, pl.ds(LANE * c, LANE)]
                else:
                    k = c - first
                    left = prevs_v[:, pl.ds(LANE * (k - 1), LANE)] if 0 < k < 7 else zero
                    right = prevs_v[:, pl.ds(LANE * k, LANE)] if k < 6 else zero
                    before = pltpu.roll(left, shift, 1) if k else x_v[:, pl.ds(LANE * c, LANE)].astype(F32)
                    mixed = jnp.where(lane < shift, before, pltpu.roll(right, shift, 1))
                    mixed = jnp.where(lane + c * LANE == end, 1.0, mixed).astype(BF16)
                xh_t[pl.ds(LANE * c, LANE), :] = jnp.transpose(mixed)

            def body(b, carry):
                rows_t = xh_t[pl.ds(pl.multiple_of(256 * b, 256), 256), :]
                for col, width in fblocks(ZW):
                    value = mm(rows_t, dz_v[:, pl.ds(col, width)])
                    tile_rows(stage, 16 * 24 * b, value, 16, 2, col // LANE, 24)
                return carry

            lax.fori_loop(0, blocks, body, 0)
            count = blocks * 16 * 24
            load([(stage.at[pl.ds(0, count)], tiles_o.at[pl.ds(0, count)])], sem)

    scratch = [
        vmem(x.shape, BF16), vmem((n, GW), F32), vmem((n, ZW), BF16), vmem((blocks * 256, n), BF16),
        vmem((blocks * 16 * 24, 16, LANE), BF16), dmas(3),
    ]
    return call(
        kernel, f"lstm_weights{layer}", (x, prevs, dz, tiles), [ANYWHERE] * 4, [(tiles.shape, BF16)], scratch, {3: 0}
    )[0]


VBLOCKS = VW // 256
VTAIL = VBLOCKS * 256


def each_vocab(body):
    def step(i, carry):
        body(pl.multiple_of(i * 256, 256), 256)
        return carry

    lax.fori_loop(0, VBLOCKS, step, 0)
    body(VTAIL, VW - VTAIL)


def output_weights_call(h, dl):
    n = h.shape[0]
    rows = 704
    pitch = VW // LANE

    def kernel(h, dl, tiles_o, h_v, dl_v, h_t, stage, sem):
        @pl.when(lax.axis_index("section") == 3)
        def _():
            load([(h, h_v), (dl, dl_v)], sem)
            lane = lanes(n)
            for c in range(6):
                value = h_v[:, pl.ds(LANE * c, LANE)].astype(F32)
                value = jnp.where(lane + c * LANE == HID, 1.0, value).astype(BF16)
                h_t[pl.ds(LANE * c, LANE), :] = jnp.transpose(value)

            def body(at, width):
                first = at // LANE
                for top, count in fblocks(rows):
                    value = mm(h_t[pl.ds(top, count), :], dl_v[:, pl.ds(at, width)])
                    for r in range(count // 16):
                        for c in range(width // LANE):
                            stage[(top // 16 + r) * pitch + first + c] = value[
                                16 * r : 16 * r + 16, LANE * c : LANE * c + LANE
                            ].astype(BF16)

            each_vocab(body)
            count = rows // 16 * pitch
            load([(stage.at[pl.ds(0, count)], tiles_o.at[pl.ds(0, count)])], sem)

    scratch = [
        vmem((n, GW), BF16), vmem((n, VW), BF16), vmem((6 * LANE, n), BF16),
        vmem((rows // 16 * pitch, 16, LANE), BF16), dmas(2),
    ]
    return call(
        kernel, "output_weights", (h, dl), [ANYWHERE] * 2, [((TILES, 16, LANE), BF16)], scratch
    )[0]


CHUNK = 32
GROUPS_OUT = (3, 3, 2, 1)


def lstm_steps(first, count, keep, carry, r, gates, cells, prevs, hiddens):
    def step(s, carry):
        h, c = carry
        at = pl.ds(pl.multiple_of((first + s) * 8, 8), 8)
        k = six(keep[at, :])
        hp = h * k
        cp = c * k
        prevs[at, :] = hp
        z = gates[at, :] + mm(hp.astype(BF16), r[...])
        i = sigmoid(z[:, 0:GW])
        f = sigmoid(z[:, GW : 2 * GW])
        o = sigmoid(z[:, 2 * GW : 3 * GW])
        g = jnp.tanh(z[:, 3 * GW :])
        c = f * cp + i * g
        h = (o * jnp.tanh(c)).astype(BF16).astype(F32)
        gates[at, :] = jnp.concatenate([i, f, o, g], axis=1)
        cells[at, :] = c
        hiddens[at, :] = h
        return h, c

    return lax.fori_loop(0, count, step, carry)


def lstm_back_steps(first, count, keep, c0, carry, rt, gates, cells, dhs):
    def step(s, carry):
        dh_next, dc_next = carry
        t = first + count - 1 - s
        at = pl.ds(pl.multiple_of(t * 8, 8), 8)
        before = pl.ds(pl.multiple_of(jnp.maximum(t - 1, 0) * 8, 8), 8)
        k = six(keep[at, :])
        saved = gates[at, :]
        i, f, o, g = [saved[:, GW * b : GW * b + GW] for b in range(4)]
        cp = jnp.where(t > 0, cells[before, :], c0[...]) * k
        ct = jnp.tanh(cells[at, :])
        dh = dhs[at, :] + dh_next
        dc = dc_next + dh * o * (1.0 - ct * ct)
        dz = jnp.concatenate(
            [dc * g * i * (1.0 - i), dc * cp * f * (1.0 - f), dh * ct * o * (1.0 - o), dc * i * (1.0 - g * g)], axis=1
        ).astype(BF16)
        gates[at, :] = dz.astype(F32)
        return k * mm(dz, rt[...]), k * dc * f

    return lax.fori_loop(0, count, step, carry)


def output_rows(first, count, h, w, targets, valid, logits, dl, top, part, dh, loss, dh16):
    at_rows = pl.ds(first, count)
    depth = w.shape[0]
    own = pl.ds(0, count)
    top[own, :] = jnp.full((count, LANE), -jnp.inf, F32)

    def forward(at, width):
        z = mm(h[at_rows, pl.ds(0, depth)], w[:, pl.ds(at, width)])
        if width < 256:
            z = jnp.where(column_mask(at, width, VOCAB, count), z, -jnp.inf)
        logits[own, pl.ds(at, width)] = z
        best = top[own, :]
        for c in range(width // LANE):
            best = jnp.maximum(best, z[:, LANE * c : LANE * c + LANE])
        top[own, :] = best

    each_vocab(forward)
    best = jnp.max(top[own, :], axis=1, keepdims=True)
    part[:, own, :] = jnp.zeros((2, count, LANE), F32)
    wanted = targets[at_rows, :]

    def exponents(at, width):
        z = logits[own, pl.ds(at, width)]
        e = jnp.exp(z - best)
        logits[own, pl.ds(at, width)] = e
        for c in range(width // LANE):
            part[0, own, :] += e[:, LANE * c : LANE * c + LANE]
            hit = lanes(count) + (at + LANE * c) == wanted
            part[1, own, :] += jnp.where(hit, z[:, LANE * c : LANE * c + LANE], 0.0)

    each_vocab(exponents)
    total = jnp.sum(part[0, own, :], axis=1, keepdims=True)
    picked = jnp.sum(part[1, own, :], axis=1, keepdims=True)
    counts = valid[at_rows, :]
    loss[...] += jnp.sum(counts * (best + jnp.log(total) - picked), axis=0, keepdims=True)
    share = counts / total
    dh[own, :] = jnp.zeros((count, depth), F32)

    def backward(at, width):
        e = logits[own, pl.ds(at, width)]
        pieces = []
        for c in range(width // LANE):
            hit = lanes(count) + (at + LANE * c) == wanted
            grad = e[:, LANE * c : LANE * c + LANE] * share - jnp.where(hit, counts, 0.0)
            pieces.append(grad.astype(BF16))
        grad = jnp.concatenate(pieces, axis=1)
        dl[at_rows, pl.ds(at, width)] = grad
        dh[own, :] += mm_nt(grad, w[:, pl.ds(at, width)])

    each_vocab(backward)
    for at, width in fblocks(depth):
        value = dh[own, pl.ds(at, width)]
        dh16[at_rows, pl.ds(at, width)] = jnp.where(column_mask(at, width, HID, count), value, 0.0).astype(BF16)


def recurrent_call(y2, ur, rt, wt, keep, targets, valid, state):
    n = y2.shape[0]
    chunks = n // CHUNK
    steps = CHUNK // 8
    depth_w = wt.shape[0]
    MESH = pl.DeviceIdType.MESH

    def kernel(
        y2, ur, rt, wt, keep, targets, valid, state,
        dy_o, x1_o, xb_o, prevs_o, dz_o, dl_o, loss_o,
        x1, xb, hb, db, ob, dy, u, r, r_t, w, start, gates, cells, prevs, hs, dhs, dz16,
        logits, dl, top, part, dh, loss,
        sem_in, sem_out, send_y, recv_y, send_f, recv_f, send_b, recv_b, send_d, recv_d,
    ):
        role = lax.axis_index("section")
        loss[...] = jnp.zeros_like(loss)

        def to(step, source, target, send, recv):
            return pltpu.make_async_remote_copy(
                source, target, send, recv, device_id={"section": role + step}, device_id_type=MESH
            )

        def span(c):
            return pl.ds(pl.multiple_of(c * CHUNK, CHUNK), CHUNK)

        def forward_copy(c, step):
            return to(step, hb.at[span(c)], xb.at[span(c)], send_f.at[c], recv_f.at[c])

        def backward_copy(c, step):
            return to(step, ob.at[span(c)], db.at[span(c)], send_b.at[c], recv_b.at[c])

        def feature_copy(step):
            return to(step, y2, x1, send_y.at[0], recv_y.at[0])

        def last_copy(step):
            return to(step, dy, dy, send_d.at[0], recv_d.at[0])

        def inputs(which):
            if which == 3:
                pairs = [(wt, w)]
            else:
                depth = FW if which == 1 else GW
                pairs = [
                    (ur.at[pl.ds(0, depth)], u.at[pl.ds(0, depth)]),
                    (ur.at[pl.ds(FW, GW)], r),
                    (rt, r_t),
                    (state.at[which - 1], start),
                ]
            return [pltpu.make_async_copy(a, b, sem_in.at[i]) for i, (a, b) in enumerate(pairs)]

        for which in (1, 2, 3):

            @pl.when(role == which)
            def _(which=which):
                for copy in inputs(which):
                    copy.start()

        barrier = pltpu.get_barrier_semaphore()

        @pl.when(role > 0)
        def _():
            pl.semaphore_signal(barrier, inc=1, device_id={"section": role - 1}, device_id_type=MESH)

        @pl.when(role < 3)
        def _():
            pl.semaphore_signal(barrier, inc=1, device_id={"section": role + 1}, device_id_type=MESH)

        pl.semaphore_wait(barrier, lax.min(role, 1) + lax.min(3 - role, 1))

        @pl.when(role == 0)
        def _():
            feature_copy(1).start()
            feature_copy(1).wait_send()
            last_copy(1).wait_recv()
            copy = pltpu.make_async_copy(dy, dy_o, sem_out.at[0])
            copy.start()
            copy.wait()

        @pl.when((role == 1) | (role == 2))
        def _():
            for which in (1, 2):

                @pl.when(role == which)
                def _(which=which):
                    for copy in inputs(which):
                        copy.wait()

            bias = r[pl.ds(HID, 1), :].astype(F32)

            @pl.when(role == 1)
            def _():
                feature_copy(-1).wait_recv()
                for at, width in fblocks(ZW):
                    cols = pl.ds(at, width)
                    gates[:, cols] = mm(x1[...], u[:, cols]) + bias[:, at : at + width]

            def chunk_forward(c, carry):
                @pl.when(role == 2)
                def _():
                    forward_copy(c, -1).wait_recv()
                    for at, width in fblocks(ZW):
                        cols = pl.ds(at, width)
                        gates[span(c), cols] = mm(xb[span(c), :], u[pl.ds(0, GW), cols]) + bias[:, at : at + width]

                carry = lstm_steps(c * steps, steps, keep, carry, r, gates, cells, prevs, hs)
                hb[span(c), :] = hs[span(c), :].astype(BF16)
                forward_copy(c, 1).start()
                return carry

            h0 = start[0].astype(BF16).astype(F32)
            lax.fori_loop(0, chunks, chunk_forward, (h0, start[1]))

            def chunk_backward(i, carry):
                c = chunks - 1 - i
                backward_copy(c, 1).wait_recv()
                dhs[span(c), :] = db[span(c), :].astype(F32)
                carry = lstm_back_steps(c * steps, steps, keep, start.at[1], carry, r_t, gates, cells, dhs)
                dz16[span(c), :] = gates[span(c), :].astype(BF16)

                @pl.when(role == 2)
                def _():
                    for at, width in fblocks(GW):
                        value = mm_nt(dz16[span(c), :], u[pl.ds(at, width), :])
                        if at + width > HID:
                            value = jnp.where(column_mask(at, width, HID, CHUNK), value, 0.0)
                        ob[span(c), pl.ds(at, width)] = value.astype(BF16)
                    backward_copy(c, -1).start()

                return carry

            zero = jnp.zeros((8, GW), F32)
            lax.fori_loop(0, chunks, chunk_backward, (zero, zero))

            def saves():
                plain = pltpu.make_async_copy
                return [plain(prevs, prevs_o, sem_out.at[0]), plain(dz16, dz_o, sem_out.at[1])]

            for copy in saves():
                copy.start()

            @pl.when(role == 1)
            def _():
                for at, width in fblocks(FW):
                    value = mm_nt(dz16[...], u[pl.ds(at, width), :])
                    if at + width > FILT:
                        value = jnp.where(column_mask(at, width, FILT, n), value, 0.0)
                    dy[:, pl.ds(at, width)] = value.astype(BF16)
                last_copy(-1).start()
                copy = pltpu.make_async_copy(x1, x1_o, sem_out.at[2])
                copy.start()
                copy.wait()
                last_copy(-1).wait_send()

            @pl.when(role == 2)
            def _():
                copy = pltpu.make_async_copy(xb, xb_o, sem_out.at[2])
                copy.start()
                copy.wait()

                def sent(c, carry):
                    backward_copy(c, -1).wait_send()
                    return carry

                lax.fori_loop(0, chunks, sent, 0)

            for copy in saves():
                copy.wait()

            def sent(c, carry):
                forward_copy(c, 1).wait_send()
                return carry

            lax.fori_loop(0, chunks, sent, 0)

        @pl.when(role == 3)
        def _():
            for copy in inputs(3):
                copy.wait()
            ob[...] = jnp.zeros_like(ob)
            done = 0
            for count in GROUPS_OUT:
                rows = pl.ds(done * CHUNK, count * CHUNK)
                for c in range(done, done + count):
                    forward_copy(c, -1).wait_recv()
                value = xb[rows, pl.ds(5 * LANE, LANE)].astype(F32)
                value = jnp.where(lanes(count * CHUNK) + 5 * LANE == HID, 1.0, value)
                xb[rows, pl.ds(5 * LANE, LANE)] = value.astype(BF16)
                output_rows(
                    done * CHUNK, count * CHUNK, xb, w, targets, valid, logits, dl, top, part, dh, loss, ob
                )
                for c in range(done, done + count):
                    backward_copy(c, -1).start()
                done += count
            copies = [
                pltpu.make_async_copy(xb, xb_o, sem_out.at[0]),
                pltpu.make_async_copy(dl, dl_o, sem_out.at[1]),
            ]
            for copy in copies:
                copy.start()
            for c in range(chunks):
                backward_copy(c, -1).wait_send()
            for copy in copies:
                copy.wait()

        loss_o[...] = loss[...]

    most = max(GROUPS_OUT) * CHUNK
    outs = [
        ((n, FW), BF16), ((n, FW), BF16), ((n, GW), BF16), ((n, GW), F32), ((n, ZW), BF16), ((n, VW), BF16),
    ]
    scratch = [
        vmem((n, FW), BF16), vmem((n, GW), BF16), vmem((n, GW), BF16), vmem((n, GW), BF16), vmem((n, GW), BF16),
        vmem((n, FW), BF16), vmem((FW, ZW), BF16), vmem((GW, ZW), BF16), vmem((ZW, GW), BF16), vmem(wt.shape, BF16),
        vmem((2, 8, GW), F32), vmem((n, ZW), F32), vmem((n, GW), F32), vmem((n, GW), F32), vmem((n, GW), F32),
        vmem((n, GW), F32), vmem((n, ZW), BF16),
        vmem((most, VW), F32), vmem((n, VW), BF16), vmem((most, LANE), F32), vmem((2, most, LANE), F32),
        vmem((most, depth_w), F32), vmem((1, LANE), F32),
        dmas(4), dmas(3), dmas(1), dmas(1), dmas(chunks), dmas(chunks), dmas(chunks), dmas(chunks), dmas(1), dmas(1),
    ]
    return pl.pallas_call(
        kernel,
        out_shape=[jax.ShapeDtypeStruct(shape, dtype) for shape, dtype in outs]
        + [jax.ShapeDtypeStruct((1, LANE), F32)],
        in_specs=[ANYWHERE] * 4 + [ON_CHIP] * 3 + [ANYWHERE],
        out_specs=[ANYWHERE] * 6 + [ON_CHIP],
        scratch_shapes=scratch,
        compiler_params=pltpu.CompilerParams(vmem_limit_bytes=62 << 20, collective_id=3, has_side_effects=True),
        name="recurrent",
    )(y2, ur, rt, wt, keep, targets, valid, state)


FORM = (
    (FILT, 9, 4 * (FILT + 1), CONV_END, CONV_TILES, 32),
    (4 * HID, 24, FILT + HID + 1, 0, 0, 16),
    (4 * HID, 24, 2 * HID + 1, 0, 0, 16),
    (VOCAB, 79, HID + 1, 0, 0, 16),
)


def slab(role, dest, share):
    width, pitch, rows, before, lead, period = FORM[role]
    low = lax.max if not isinstance(dest, int) else max
    high = lax.min if not isinstance(dest, int) else min
    one = (lambda v: v) if isinstance(dest, int) else jnp.int32
    start = low(one(share) * dest - before, one(0))
    first = start // width // period * period
    end = high((share * (dest + 1) - before + width - 1) // width, one(rows))
    count = low((end - first + 15) // 16, one(0)) * pitch
    tile = lead + first // 16 * pitch
    if lead:
        if isinstance(dest, int):
            if dest == 0:
                tile, count = 0, count + lead
        else:
            head = lax.max(1 - dest, 0)
            tile = tile - lead * head
            count = count + lead * head
    return first, tile, count


def slab_pieces(count, size):
    return (count + size - 1) // size


def most_pieces(groups, share, size):
    return max(slab_pieces(slab(role, dest, share)[2], size) for role in range(4) for dest in range(groups))


def gather_sum_call(tiles, bias, loss, groups, share):
    pair = 2
    across = groups // pair
    size = 64 if across <= 4 else 32
    pieces = most_pieces(groups, share, size)
    room = pieces * size
    line = across <= 4
    slots = across + 1 if line else across - 1
    MESH = pl.DeviceIdType.MESH

    def kernel(
        tiles, bias, loss, out, small_out, own, got1, got2, acc, small, got_small,
        own_sem, send1, recv1, send2, recv2, out_sem, small_send, small_recv,
    ):
        role = lax.axis_index("section")
        me = lax.axis_index("dp")
        mine, side = me // pair, lax.rem(me, pair)
        other = mine * pair + (1 - side)

        def at_place(place):
            return {"dp": place * pair + side}

        barrier = pltpu.get_barrier_semaphore()
        pl.semaphore_signal(barrier, inc=1, device_id={"dp": other}, device_id_type=MESH)
        for k in range(1, across):
            peer = at_place(lax.rem(mine + k, across))
            pl.semaphore_signal(barrier, inc=1, device_id=peer, device_id_type=MESH)
        pl.semaphore_wait(barrier, across)

        def part(ref, slot, p):
            return ref.at[slot, pl.ds(pl.multiple_of(p * size, size), size)]

        def span(p):
            return pl.ds(pl.multiple_of(p * size, size), size)

        def loop(count, body):
            def step(p, carry):
                body(p)
                return carry

            lax.fori_loop(0, count, step, 0)

        def small_copy(k):
            if k == 0:
                source, target = small.at[0], {"dp": other}
            else:
                source, target = small.at[1], at_place(lax.rem(mine + k, across))
            return pltpu.make_async_remote_copy(
                source, got_small.at[k], small_send.at[k], small_recv.at[k], device_id=target, device_id_type=MESH
            )

        small[...] = jnp.zeros_like(small)

        @pl.when(role == 0)
        def _():
            row = FILT % LANE % 8
            for at in range(0, FW, LANE):
                small[0, :, pl.ds(at, LANE)] = bias[row : row + 1, pl.ds(at, LANE)]

        @pl.when(role == 3)
        def _():
            small[0, :, pl.ds(FW, LANE)] = loss[...]

        small_copy(0).start()

        def run(shape_of):
            def count_to(place, which):
                return shape_of(place * pair + which)[1]

            def own_copy(place, p):
                tile, _ = shape_of(place * pair + side)
                return pltpu.make_async_copy(
                    tiles.at[pl.ds(tile + p * size, size)], part(own, place, p), own_sem.at[place, p]
                )

            def first_copy(place, p):
                tile, _ = shape_of(place * pair + 1 - side)
                return pltpu.make_async_remote_copy(
                    tiles.at[pl.ds(tile + p * size, size)], part(got1, place, p), send1.at[place, p], recv1.at[place, p],
                    device_id={"dp": other}, device_id_type=MESH,
                )

            def begin(place):
                loop(count_to(place, 1 - side), lambda p: first_copy(place, p).start())
                loop(count_to(place, side), lambda p: own_copy(place, p).start())

            def hop_copy(place, up, p):
                if line:
                    target = mine + 1 if up else mine - 1
                    slot = jnp.where(place == mine + 1, across, place) if up else place
                else:
                    target = place
                    slot = lax.rem(place - mine + across, across) - 1
                return pltpu.make_async_remote_copy(
                    part(own, place, p), part(got2, slot, p), send2.at[place, p], recv2.at[slot, p],
                    device_id=at_place(target), device_id_type=MESH,
                )

            def arrived(slot, p):
                return pltpu.make_async_remote_copy(
                    part(own, 0, p), part(got2, slot, p), send2.at[0, p], recv2.at[slot, p],
                    device_id=at_place(lax.rem(mine + 1, across)), device_id_type=MESH,
                )

            def forward(place, up, has_before):
                def body(p):
                    own_copy(place, p).wait()
                    first_copy(place, p).wait_recv()
                    at = span(p)
                    own[place, at] = (own[place, at].astype(F32) + got1[place, at].astype(F32)).astype(BF16)
                    hop_copy(place, up, p).start()

                def body_sum(p):
                    own_copy(place, p).wait()
                    first_copy(place, p).wait_recv()
                    arrived(place, p).wait_recv()
                    at = span(p)
                    total = own[place, at].astype(F32) + got1[place, at].astype(F32) + got2[place, at].astype(F32)
                    own[place, at] = total.astype(BF16)
                    hop_copy(place, up, p).start()

                count = count_to(place, side)
                if not line:
                    loop(count, body)
                    return

                @pl.when(has_before)
                def _():
                    loop(count, body_sum)

                @pl.when(jnp.logical_not(has_before))
                def _():
                    loop(count, body)

            if line:
                for k in range(across - 1):

                    @pl.when(k < mine)
                    def _(k=k):
                        begin(k)

                    @pl.when(k < across - 1 - mine)
                    def _(k=k):
                        begin(across - 1 - k)

                begin(mine)
                for k in range(across - 1):

                    @pl.when(k < mine)
                    def _(k=k):
                        forward(k, False, mine < across - 1)

                    @pl.when(k < across - 1 - mine)
                    def _(k=k):
                        forward(across - 1 - k, True, mine > 0)

            else:
                for k in range(1, across):
                    begin(lax.rem(mine + k, across))
                begin(mine)
                for k in range(1, across):
                    forward(lax.rem(mine + k, across), True, None)

            small_copy(0).wait_recv()
            small[1] = small[0] + got_small[0]
            for k in range(1, across):
                small_copy(k).start()

            def settle(p):
                own_copy(mine, p).wait()
                first_copy(mine, p).wait_recv()
                at = span(p)
                acc[at] = own[mine, at].astype(F32) + got1[mine, at].astype(F32)

            def add(slot):
                def body(p):
                    arrived(slot, p).wait_recv()
                    at = span(p)
                    acc[at] += got2[slot, at].astype(F32)

                return body

            mine_count = count_to(mine, side)
            loop(mine_count, settle)
            if line:

                @pl.when(mine < across - 1)
                def _():
                    loop(mine_count, add(mine))

                @pl.when(mine > 0)
                def _():
                    loop(mine_count, add(across))

            else:
                for k in range(1, across):
                    loop(mine_count, add(k - 1))

            def out_copy(p):
                return pltpu.make_async_copy(acc.at[span(p)], out.at[span(p)], out_sem.at[p])

            loop(mine_count, lambda p: out_copy(p).start())
            loop(mine_count, lambda p: out_copy(p).wait())
            for place in range(across):
                loop(count_to(place, 1 - side), lambda p, place=place: first_copy(place, p).wait_send())

                @pl.when(place != mine)
                def _(place=place):
                    loop(count_to(place, side), lambda p: hop_copy(place, True, p).wait_send())

        for which in range(4):

            @pl.when(role == which)
            def _(which=which):
                def shape_of(dest):
                    _, tile, count = slab(which, dest, share)
                    return tile, slab_pieces(count, size)

                run(shape_of)

        total = small[1]
        for k in range(1, across):
            small_copy(k).wait_recv()
            total = total + got_small[k]
        small_out[...] = total
        for k in range(across):
            small_copy(k).wait_send()

    sems = pltpu.SemaphoreType.DMA
    return pl.pallas_call(
        kernel,
        out_shape=[
            jax.ShapeDtypeStruct((room, 16, LANE), F32),
            jax.ShapeDtypeStruct((1, FW + LANE), F32),
        ],
        in_specs=[ANYWHERE, ON_CHIP, ON_CHIP],
        out_specs=[ANYWHERE, ON_CHIP],
        scratch_shapes=[
            vmem((across, room, 16, LANE), BF16), vmem((across, room, 16, LANE), BF16),
            vmem((slots, room, 16, LANE), BF16), vmem((room, 16, LANE), F32),
            vmem((2, 1, FW + LANE), F32), vmem((across, 1, FW + LANE), F32),
            sems((across, pieces)), sems((across, pieces)), sems((across, pieces)),
            sems((across, pieces)), sems((slots, pieces)), sems((pieces,)), sems((across,)), sems((across,)),
        ],
        compiler_params=pltpu.CompilerParams(vmem_limit_bytes=62 << 20, collective_id=1, has_side_effects=True),
        name="gather_sum",
    )(tiles, bias, loss)


def sections_sum_call(small):
    count = lax.axis_size("section")

    def kernel(mine, out, held, send, recv):
        me = lax.axis_index("section")
        barrier = pltpu.get_barrier_semaphore()

        def peer(k):
            return {"section": lax.rem(me + k, count)}

        for k in range(1, count):
            pl.semaphore_signal(barrier, inc=1, device_id=peer(k), device_id_type=pl.DeviceIdType.MESH)
        pl.semaphore_wait(barrier, count - 1)
        copies = [
            pltpu.make_async_remote_copy(
                mine, held.at[k], send.at[k], recv.at[k], device_id=peer(k), device_id_type=pl.DeviceIdType.MESH
            )
            for k in range(1, count)
        ]
        for copy in copies:
            copy.start()
        total = mine[...]
        for k, copy in enumerate(copies):
            copy.wait_recv()
            total = total + held[k + 1]
        out[...] = total
        for copy in copies:
            copy.wait_send()

    return pl.pallas_call(
        kernel,
        out_shape=jax.ShapeDtypeStruct(small.shape, F32),
        in_specs=[ON_CHIP],
        out_specs=ON_CHIP,
        scratch_shapes=[vmem((count,) + small.shape, F32), dmas(count), dmas(count)],
        compiler_params=pltpu.CompilerParams(collective_id=2, has_side_effects=True),
        name="sections_sum",
    )(small)


def pack_call(summed, groups, share):
    room = summed.shape[0] * 16
    chunks = share // LANE
    margin = 1280
    slab_rows = 10624
    flat_rows = margin + max(10752, chunks + 1280)

    def kernel(summed, out, rows_v, spaced, flat, sem):
        role = lax.axis_index("section")
        me = lax.axis_index("dp")
        zero = jnp.zeros((64, LANE), F32)

        def clear(i, carry):
            flat[pl.ds(pl.multiple_of(i * 64, 64), 64), :] = zero
            return carry

        copy = pltpu.make_async_copy(summed, rows_v.at[pl.ds(0, room)], sem.at[0])
        copy.start()
        lax.fori_loop(0, flat_rows // 64, clear, 0)
        copy.wait()
        lane = lanes()

        for which in range(4):
            width, pitch, rows, before, lead, period = FORM[which]
            if which == 0:
                blocks, cols, tiles = 1, FILT, 9
            elif which == 3:
                blocks, cols, tiles = 1, VOCAB, 79
            else:
                blocks, cols, tiles = 4, HID, 6
            stride = period * width // LANE
            most = max(slab(which, dest, share)[2] for dest in range(groups))
            groups8 = -(-(-(-most // pitch) * 16) // (8 * period))

            @pl.when(role == which)
            def _(which=which):
                first, _, count = slab(which, me, share)
                skip = lead * lax.max(1 - me, 0)
                step_rows = pitch * 49 + (pitch * 49 + 1) % 2

                def space(rt, carry):
                    for c in range(pitch):
                        for half in range(2):
                            at = pl.multiple_of((skip + rt * pitch + c) * 16 + 8 * half, 8)
                            spaced[pl.ds(rt * step_rows + 49 * c + 24 * half, 8, stride=3), :] = rows_v[pl.ds(at, 8), :]
                    return carry

                lax.fori_loop(0, (count - skip) // pitch, space, 0)
                base = margin + before // LANE + stride * (first // period) - chunks * me

                def row(i, carry):
                    group, n = i // period, lax.rem(i, period)
                    number = first + period * (8 * group + sublanes()) + n
                    keep = number < rows
                    hop = period // 16 * step_rows
                    source = n // 16 * step_rows + 3 * lax.rem(n, 16) + 8 * group * hop
                    step = 27
                    for b in range(blocks):
                        flat_at = before % LANE + width * n + cols * b
                        turn = lax.rem(flat_at, LANE)
                        to = base + flat_at // LANE + stride * 8 * group
                        last = jnp.zeros((8, LANE), F32)
                        for low in range(0, tiles, step):
                            high = min(low + step, tiles)
                            taken = [
                                spaced[pl.ds(source + 49 * (tiles * b + j), 8, stride=hop), :]
                                for j in range(low, high)
                            ]
                            turned = [last] + [pltpu.roll(jnp.where(keep, x, 0.0), turn, 1) for x in taken]
                            for j in range(low, high):
                                value = jnp.where(lane >= turn, turned[j - low + 1], turned[j - low])
                                where = pl.ds(to + j, 8, stride=stride)
                                if j == 0:
                                    value = jnp.where(lane >= turn, value, flat[where, :])
                                flat[where, :] = value
                            last = turned[-1]
                        where = pl.ds(to + tiles, 8, stride=stride)
                        flat[where, :] = jnp.where(lane + LANE * tiles - turn < cols, last, flat[where, :])
                    return carry

                @pl.when(count > 0)
                def _():
                    lax.fori_loop(0, period * groups8, row, 0)

        @pl.when((role == 0) & (me == 0))
        def _():
            lane1 = lanes(1)

            def piece(row_at, flat_at, low, size):
                edge = flat_at - low
                turn = edge % LANE
                to = margin + (edge - turn) // LANE
                first, end = low // LANE, (low + size - 1) // LANE
                last = jnp.zeros((1, LANE), F32)
                for j in range(first, end + 2):
                    least, most = max(low + turn - LANE * j, 0), min(low + size + turn - LANE * j, LANE)
                    here = last
                    if j <= end:
                        here = rows_v[row_at + 16 * j : row_at + 16 * j + 1, :]
                        here = pltpu.roll(here, turn, 1) if turn else here
                    if most > least:
                        value = jnp.where(lane1 >= turn, here, last) if turn else here
                        at = to + j
                        if least > 0 or most < LANE:
                            value = jnp.where((lane1 >= least) & (lane1 < most), value, flat[at : at + 1, :])
                        flat[at : at + 1, :] = value
                    last = here

            for k in range(1, 8):
                n = NFILT[k - 1]
                for i in range(k * D_CHAR + 1):
                    number = i + i // D_CHAR if i < k * D_CHAR else 15
                    piece(number // 16 * 144 + number % 16, KOFF[k - 1] + n * i, COLS[k - 1], n)
            for a in range(CHAR_V):
                piece(72 * 16 + a, D_CHAR * a, 0, D_CHAR)

        copy = pltpu.make_async_copy(flat.at[pl.ds(margin, chunks)], out, sem.at[0])
        copy.start()
        copy.wait()

    return pl.pallas_call(
        kernel,
        out_shape=jax.ShapeDtypeStruct((chunks, LANE), F32),
        in_specs=[ANYWHERE],
        out_specs=ANYWHERE,
        scratch_shapes=[
            vmem((slab_rows, LANE), F32), vmem((31104, LANE), F32), vmem((flat_rows, LANE), F32), dmas(1),
        ],
        compiler_params=pltpu.CompilerParams(vmem_limit_bytes=LIMIT),
        name="pack",
    )(summed.reshape(room, LANE))


def shards(char_ids, target_ids, remaining, resets, start_state, section_params):
    rows, steps = char_ids.shape[:2]
    groups = lax.axis_size("dp")
    packed = section_params.shape[1]
    share = packed // groups
    n = rows * (steps + 1)

    def by_step(x, fill):
        x = jnp.pad(x.T, ((0, 1), (0, 0)), constant_values=fill)
        return jnp.broadcast_to(x.reshape(n, 1), (n, LANE))

    ids = jnp.pad(
        char_ids.transpose(1, 0, 2), ((0, 1), (0, 0), (0, LANE - WORD_CHARS)), constant_values=-1
    ).reshape(n, LANE)
    targets = by_step(target_ids, -1)
    keep = by_step(1.0 - resets.astype(F32), 0.0)
    valid = by_step((jnp.arange(steps, dtype=jnp.int32)[None, :] < remaining[:, None]).astype(F32), 0.0)
    state = jnp.pad(start_state, ((0, 0), (0, 0), (0, 0), (0, GW - HID)))

    km, e8, ab, ur, rt, wt = unpack_all(section_params)
    y2, *char_saved = char_forward_call(ids, km, e8, ab)
    g0, x1, xb, prevs, dz, dl, loss = recurrent_call(y2, ur, rt, wt, keep, targets, valid, state)
    tiles = output_weights_call(xb, dl)
    tiles = lstm_weights_call(2, xb, prevs, dz, tiles)
    tiles = lstm_weights_call(1, x1, prevs, dz, tiles)
    tiles, bias = char_backward_call(ids, g0, km, ab, char_saved, tiles)
    summed, small = gather_sum_call(tiles, bias, loss, groups, share)
    flat = pack_call(summed, groups, share)
    small = sections_sum_call(small)
    mean_loss = small[0, FW] / (groups * rows * steps)
    return mean_loss, flat.reshape(1, share), small[0, :FILT]


def solution(mesh):
    in_specs = (
        P("dp", None, None),
        P("dp", None),
        P("dp"),
        P("dp", None),
        P(None, None, "dp", None),
        P("section", None),
    )
    out_specs = (P(), P("section", "dp"), P())
    return jax.shard_map(shards, mesh=mesh, in_specs=in_specs, out_specs=out_specs, check_vma=False)
```

```python
import functools
import math

import jax
import jax.numpy as jnp
from jax import lax
from jax.experimental import pallas as pl
from jax.experimental.pallas import tpu as pltpu
from jax.sharding import PartitionSpec as P

D_CHAR = 15
CHAR_V = 51
F_UNIT = 50
WORD_CHARS = 21
HID = 650
VOCAB = 10000
FILT = 1100
F32 = jnp.float32
BF16 = jnp.bfloat16

NFILT = [F_UNIT * min(k, 4) for k in range(1, 8)]
COLS = [sum(NFILT[:k]) for k in range(8)]
KOFF = [CHAR_V * D_CHAR + sum((j * D_CHAR + 1) * NFILT[j - 1] for j in range(1, k)) for k in range(1, 9)]
CONV_END = KOFF[7]
HIGH_STRIDE = FILT * (FILT + 1)
FW = 1152
GW = 768
ZW = 4 * GW
VW = 10112
LANE = 128
LENS = (2304, 2688, 2688, 5120)


def roll_lanes(x, shift):
    return pltpu.roll(x, shift, 1)


def lanes(rows=8):
    return lax.broadcasted_iota(jnp.int32, (rows, LANE), 1)


def sublanes():
    return lax.broadcasted_iota(jnp.int32, (8, LANE), 0)


def widen(raw, slot, rows, wide):
    def body(i, carry):
        piece = raw[slot, 0:1, pl.ds(pl.multiple_of(i * 16384, 16384), 16384)]
        wide[pl.ds(pl.multiple_of(i * 128, 128), 128), :] = piece.astype(F32).reshape(128, LANE)
        return carry

    lax.fori_loop(0, rows // 128, body, 0)


def stream_blocks(count, length, total, chunk_of, src, raw, sem, wide, work):
    def start_of(i):
        first = chunk_of(i)
        return jnp.minimum(first // 8 * 8, total - length)

    def copy(i, slot):
        at = pl.multiple_of(start_of(i) * LANE, 8 * LANE)
        return pltpu.make_async_copy(
            src.at[:, pl.ds(at, length * LANE)], raw.at[slot, :, pl.ds(0, length * LANE)], sem.at[slot]
        )

    copy(0, 0).start()

    def body(i, carry):
        slot = lax.rem(i, 2)

        @pl.when(i + 1 < count)
        def _():
            copy(i + 1, 1 - slot).start()

        copy(i, slot).wait()
        widen(raw, slot, length, wide)
        work(i, chunk_of(i) - start_of(i))
        return carry

    lax.fori_loop(0, count, body, 0)


def take_rows(wide, starts, tiles, cols, stride, put):
    step = max(1, 28 // len(starts))
    lane = lanes()
    for low in range(0, tiles, step):
        high = min(tiles, low + step)
        loaded = [
            [wide[pl.ds(first + c, 8, stride=stride), :] for c in range(low, high + 1)] for _, first, _, _ in starts
        ]
        results = []
        for (_, _, shift, keep_row), pieces in zip(starts, loaded):
            turn = lax.rem(LANE - shift, LANE)
            split = lane < LANE - shift
            turned = [roll_lanes(piece, turn) for piece in pieces]
            for c in range(low, high):
                out = jnp.where(split, turned[c - low], turned[c - low + 1])
                keep = keep_row
                if cols - c * LANE < LANE:
                    keep = keep & (lane < cols - c * LANE)
                results.append(jnp.where(keep, out, 0.0))
        at = 0
        for tag, _, _, _ in starts:
            for c in range(low, high):
                put(tag, c, results[at])
                at += 1


def spread(c, n, period):
    return pl.ds((c * period + n) * 25, 8, stride=3)


def collect(dest, c, period):
    return [
        dest[pl.ds((c * period + 8 * m) * 25 + 3 * j, 8, stride=25), :] for j in range(8) for m in range(period // 8)
    ]


def stage_tile(stage, slot, c, blocks):
    for i in range(0, len(blocks), 2):
        pair = jnp.concatenate([blocks[i], blocks[i + 1]], axis=0).astype(BF16)
        stage[slot, pl.ds(8 * i, 16), pl.ds(c * LANE, LANE)] = pair


def unpack_kernel(
    src, km, e8, ab, ur, rt, wt, raw, wide, dest, kstage, stage0, stage1, stage_t, stage3, sem_in, sem_out, sem_t
):
    role = lax.axis_index("section")
    total = src.shape[1] // LANE

    def out_copy(stage, slot, target):
        return pltpu.make_async_copy(stage.at[slot], target, sem_out.at[slot])

    @pl.when(role == 0)
    def _():
        length = 640
        copy = pltpu.make_async_copy(
            src.at[:, pl.ds(0, length * LANE)], raw.at[0, :, pl.ds(0, length * LANE)], sem_in.at[0]
        )
        copy.start()
        copy.wait()
        widen(raw, 0, length, wide)
        lane1 = lanes(1)
        dest[pl.ds(0, 64), :] = jnp.zeros((64, LANE), F32)
        for a in range(CHAR_V):
            flat = D_CHAR * a
            q, s = flat // LANE, flat % LANE
            here = wide[q : q + 1, :]
            out = roll_lanes(here, (LANE - s) % LANE) if s else here
            if s + D_CHAR > LANE:
                out = jnp.where(lane1 < LANE - s, out, roll_lanes(wide[q + 1 : q + 2, :], LANE - s))
            dest[a : a + 1, :] = jnp.where(lane1 < D_CHAR, out, jnp.where(lane1 == D_CHAR, 1.0, 0.0))
        table = dest[pl.ds(0, 64), :]
        for m in range(8):
            kstage[pl.ds(64 * m, 64), pl.ds(0, LANE)] = (
                pltpu.roll(table, 16 * m, 1) if m else table
            ).astype(BF16)
        copy = pltpu.make_async_copy(kstage.at[pl.ds(0, 512), pl.ds(0, LANE)], e8, sem_out.at[0])
        copy.start()
        copy.wait()
        tiles = FW // LANE
        rows = 112
        dest[pl.ds(0, rows * tiles), :] = jnp.zeros((rows * tiles, LANE), F32)

        def kernel_row(k, i, row):
            n, base = NFILT[k - 1], COLS[k - 1]
            edge = KOFF[k - 1] + n * i - base
            q, s = edge // LANE, edge % LANE
            for ct in range(base // LANE, (base + n - 1) // LANE + 1):
                out = wide[q + ct : q + ct + 1, :]
                if s:
                    after = roll_lanes(wide[q + ct + 1 : q + ct + 2, :], LANE - s)
                    out = jnp.where(lane1 < LANE - s, roll_lanes(out, LANE - s), after)
                at = ct * rows + row
                low, high = max(base - ct * LANE, 0), min(base + n - ct * LANE, LANE)
                if low > 0 or high < LANE:
                    out = jnp.where((lane1 >= low) & (lane1 < high), out, dest[at : at + 1, :])
                dest[at : at + 1, :] = out

        for k in range(1, 8):
            for i in range(k * D_CHAR):
                kernel_row(k, i, i + i // D_CHAR)
            kernel_row(k, k * D_CHAR, 15)
        kstage[...] = jnp.zeros_like(kstage)
        for ct in range(tiles):
            kstage[pl.ds(112, rows), pl.ds(ct * LANE, LANE)] = dest[pl.ds(ct * rows, rows), :].astype(BF16)
        copy = pltpu.make_async_copy(kstage.at[pl.ds(0, 368)], km, sem_out.at[0])
        copy.start()
        copy.wait()

        blocks = 5

        def flat_of(i):
            return CONV_END + HIGH_STRIDE * (i // blocks)

        def chunk_of(i):
            return flat_of(i) // LANE + 2200 * lax.rem(i, blocks)

        def target(i):
            return ab.at[i // blocks, pl.ds(pl.multiple_of(lax.rem(i, blocks) * 256, 256), 256)]

        def work(i, extra):
            block = lax.rem(i, blocks)
            inner = lax.rem(flat_of(i), LANE)

            def rows_of(i, carry):
                starts = []
                for n in (2 * i, 2 * i + 1):
                    flat = inner + FILT * n
                    keep = 32 * (8 * block + sublanes()) + n <= FILT
                    starts.append((n, flat // LANE + extra, lax.rem(flat, LANE), keep))

                def put(n, c, value):
                    dest[spread(c, n, 32), :] = value

                take_rows(wide, starts, tiles, FILT, 275, put)
                return carry

            lax.fori_loop(0, 16, rows_of, 0)
            slot = lax.rem(i, 2)

            @pl.when(i >= 2)
            def _():
                out_copy(stage0, slot, target(i - 2)).wait()

            for c in range(tiles):
                stage_tile(stage0, slot, c, collect(dest, c, 32))
            out_copy(stage0, slot, target(i)).start()

        count = 4 * blocks
        stream_blocks(count, LENS[0], total, chunk_of, src, raw, sem_in, wide, work)
        for i in (count - 2, count - 1):
            out_copy(stage0, i % 2, target(i)).wait()

    for layer in (1, 2):

        @pl.when(role == layer)
        def _(layer=layer):
            depth = FILT if layer == 1 else HID
            blocks = -(-depth // 128)
            recurrent = depth * 4 * HID
            count = blocks + 6

            def chunk_of(i):
                return jnp.where(i < blocks, 2600 * i, recurrent // LANE + 2600 * (i - blocks))

            def target(i):
                at = jnp.where(i < blocks, i, i - blocks + 9)
                return ur.at[pl.ds(pl.multiple_of(at * 128, 128), 128)]

            def work(i, extra):
                inner = jnp.where(i < blocks, 0, recurrent % LANE)
                block = jnp.where(i < blocks, i, i - blocks)
                limit = jnp.where(i < blocks, depth, HID + 1)

                def rows_of(n, carry):
                    keep = 16 * (8 * block + sublanes()) + n < limit
                    flats = [inner + 4 * HID * n + HID * b for b in range(4)]

                    def put(b, c, value):
                        dest[spread(6 * b + c, n, 16), :] = value

                    starts = [(b, flat // LANE + extra, lax.rem(flat, LANE), keep) for b, flat in enumerate(flats)]
                    take_rows(wide, starts, 6, HID, 325, put)
                    return carry

                lax.fori_loop(0, 16, rows_of, 0)
                slot = lax.rem(i, 2)

                @pl.when(i >= 2)
                def _():
                    out_copy(stage1, slot, target(i - 2)).wait()

                for c in range(24):
                    stage_tile(stage1, slot, c, collect(dest, c, 16))
                out_copy(stage1, slot, target(i)).start()

                @pl.when(i >= blocks)
                def _():
                    @pl.when(i >= blocks + 2)
                    def _():
                        turned_copy(i - 2).wait()

                    k = LANE * block + lanes(LANE)
                    for c in range(24):
                        turned = jnp.transpose(jnp.concatenate(collect(dest, c, 16), axis=0))
                        stage_t[slot, pl.ds(128 * c, 128), :] = jnp.where(k < HID, turned, 0.0).astype(BF16)
                    turned_copy(i).start()

            def turned_copy(i):
                slot = lax.rem(i, 2)
                at = pl.multiple_of((i - blocks) * LANE, LANE)
                return pltpu.make_async_copy(stage_t.at[slot], rt.at[:, pl.ds(at, LANE)], sem_t.at[slot])

            stream_blocks(count, LENS[1], total, chunk_of, src, raw, sem_in, wide, work)
            for i in (count - 2, count - 1):
                out_copy(stage1, i % 2, target(jnp.int32(i))).wait()
                turned_copy(jnp.int32(i)).wait()

    @pl.when(role == 3)
    def _():
        count = 11
        tiles = VW // LANE

        def chunk_of(i):
            return 5000 * i

        def target(i):
            return wt.at[pl.ds(pl.multiple_of(i * 64, 64), 64)]

        def work(i, extra):
            def rows_of(n, carry):
                flat = VOCAB * n
                keep = 8 * (8 * i + sublanes()) + n < HID + 1

                def put(n, c, value):
                    dest[spread(c, n, 8), :] = value

                take_rows(wide, [(n, flat // LANE + extra, lax.rem(flat, LANE), keep)], tiles, VOCAB, 625, put)
                return carry

            lax.fori_loop(0, 8, rows_of, 0)
            slot = lax.rem(i, 2)

            @pl.when(i >= 2)
            def _():
                out_copy(stage3, slot, target(i - 2)).wait()

            for c in range(tiles):
                stage_tile(stage3, slot, c, collect(dest, c, 8))
            out_copy(stage3, slot, target(i)).start()

        stream_blocks(count, LENS[3], total, chunk_of, src, raw, sem_in, wide, work)
        for i in (count - 2, count - 1):
            out_copy(stage3, i % 2, target(jnp.int32(i))).wait()


def unpack_all(section_params):
    anywhere = pl.BlockSpec(memory_space=pl.ANY)
    return pl.pallas_call(
        unpack_kernel,
        out_shape=[
            jax.ShapeDtypeStruct((368, FW), BF16),
            jax.ShapeDtypeStruct((512, LANE), BF16),
            jax.ShapeDtypeStruct((4, 1280, FW), BF16),
            jax.ShapeDtypeStruct((15 * 128, ZW), BF16),
            jax.ShapeDtypeStruct((ZW, GW), BF16),
            jax.ShapeDtypeStruct((11 * 64, VW), BF16),
        ],
        in_specs=[anywhere],
        out_specs=[anywhere] * 6,
        scratch_shapes=[
            pltpu.VMEM((2, 1, LENS[3] * LANE), BF16),
            pltpu.VMEM((9312, LANE), F32),
            pltpu.VMEM((79 * 200, LANE), F32),
            pltpu.VMEM((512, FW), BF16),
            pltpu.VMEM((2, 256, FW), BF16),
            pltpu.VMEM((2, 128, ZW), BF16),
            pltpu.VMEM((2, ZW, LANE), BF16),
            pltpu.VMEM((2, 64, VW), BF16),
            pltpu.SemaphoreType.DMA((2,)),
            pltpu.SemaphoreType.DMA((2,)),
            pltpu.SemaphoreType.DMA((2,)),
        ],
        compiler_params=pltpu.CompilerParams(vmem_limit_bytes=56 << 20),
        name="unpack",
    )(section_params)


def fblocks(width, step=256):
    return [(at, min(step, width - at)) for at in range(0, width, step)]


def mm(a, b):
    return jnp.dot(a, b, preferred_element_type=F32)


def mm_tn(a, b):
    return lax.dot_general(a, b, (((0,), (0,)), ((), ())), preferred_element_type=F32)


def mm_nt(a, b):
    return lax.dot_general(a, b, (((1,), (1,)), ((), ())), preferred_element_type=F32)


def sigmoid(x):
    return 0.5 * jnp.tanh(0.5 * x) + 0.5


def load(pairs, sem):
    copies = [pltpu.make_async_copy(a, b, sem.at[i]) for i, (a, b) in enumerate(pairs)]
    for copy in copies:
        copy.start()
    for copy in copies:
        copy.wait()


def column_mask(at, width, limit, rows):
    return lax.broadcasted_iota(jnp.int32, (rows, width), 1) + at < limit


def char_onehot(ids, t):
    rows = ids.shape[0]
    lane = lanes(rows)
    pieces = []
    for pair in range(4):
        j = 8 * t + 2 * pair
        left = ids[:, j : j + 1]
        right = ids[:, j + 1 : j + 2]
        hit = jnp.where(lane < 64, left, right) == lax.rem(lane, 64)
        pieces.append(jnp.where(hit, 1.0, 0.0).astype(BF16))
    return jnp.concatenate(pieces, axis=1)


def conv_steps(body):
    def step(p, carry):
        body(p, p // 8, True, lax.rem(p, 8), FILT)
        return carry

    lax.fori_loop(0, 15, step, 0)
    body(15, 1, True, 7, COLS[6])
    for p in range(16, WORD_CHARS):
        body(p, 2, False, p - 16, COLS[WORD_CHARS - p])


def conv_at(emb, km, tile, second, within, at, width):
    first = 112 - 16 * within
    if not isinstance(first, int):
        first = pl.multiple_of(first, 16)
    if second:
        window = jnp.concatenate([emb[tile], emb[tile + 1]], axis=1)
    else:
        window = emb[tile]
    return mm(window, km[pl.ds(first, window.shape[1]), pl.ds(at, width)])


def char_forward(ids, e8, km, ab, emb, total, feats, pres, out):
    rows = ids.shape[0]
    for t in range(3):
        emb[t] = mm(char_onehot(ids, t), e8[...]).astype(BF16)
    total[...] = jnp.zeros_like(total)

    def step(p, tile, second, within, limit):
        for at, width in fblocks(FW):
            if at >= limit:
                continue
            value = jnp.exp(jnp.tanh(conv_at(emb, km, tile, second, within, at, width)))
            if at + width > limit and limit < FILT:
                value = jnp.where(column_mask(at, width, limit, rows), value, 0.0)
            total[:, pl.ds(at, width)] += value

    conv_steps(step)
    for at, width in fblocks(FW):
        col = lax.broadcasted_iota(jnp.int32, (rows, width), 1) + at
        count = jnp.full((rows, width), float(WORD_CHARS), F32)
        for k in range(1, 7):
            count = jnp.where(col >= COLS[k], float(WORD_CHARS - k), count)
        value = jnp.log(total[:, pl.ds(at, width)]) - jnp.log(count)
        value = jnp.where(col < FILT, value, jnp.where(col == FILT, 1.0, 0.0))
        feats[0, :, pl.ds(at, width)] = value.astype(BF16)
    for layer in range(2):
        for at, width in fblocks(FW):
            cols = pl.ds(at, width)
            t_pre = mm(feats[layer], ab[2 * layer, pl.ds(0, FW), cols])
            h_pre = mm(feats[layer], ab[2 * layer + 1, pl.ds(0, FW), cols])
            pres[2 * layer, :, cols] = t_pre
            pres[2 * layer + 1, :, cols] = h_pre
            gate = sigmoid(t_pre)
            y = feats[layer, :, cols].astype(F32)
            value = gate * (h_pre * sigmoid(h_pre)) + (1.0 - gate) * y
            col = lax.broadcasted_iota(jnp.int32, (rows, width), 1) + at
            if layer == 0:
                value = jnp.where(col < FILT, value, jnp.where(col == FILT, 1.0, 0.0))
                feats[1, :, cols] = value.astype(BF16)
            else:
                out[:, cols] = jnp.where(col < FILT, value, 0.0).astype(BF16)


def highway_backward(dy, ab, feats, pres, grad, dpre, share):
    rows = grad.shape[0]
    for at, width in fblocks(FW):
        cols = pl.ds(at, width)
        grad[:, cols] = jnp.where(column_mask(at, width, FILT, rows), dy[:, cols].astype(F32), 0.0)
    for layer in (1, 0):
        for at, width in fblocks(FW):
            cols = pl.ds(at, width)
            g = grad[:, cols]
            gate = sigmoid(pres[2 * layer, :, cols])
            q = pres[2 * layer + 1, :, cols]
            sig = sigmoid(q)
            y = feats[layer, :, cols].astype(F32)
            dpre[2 * layer, :, cols] = (g * (q * sig - y) * gate * (1.0 - gate)).astype(BF16)
            dpre[2 * layer + 1, :, cols] = (g * gate * sig * (1.0 + q * (1.0 - sig))).astype(BF16)
            grad[:, cols] = g * (1.0 - gate)
        share(layer)
        for at, width in fblocks(FW):
            cols = pl.ds(at, width)
            value = (
                grad[:, cols]
                + mm_nt(dpre[2 * layer], ab[2 * layer, cols, :])
                + mm_nt(dpre[2 * layer + 1], ab[2 * layer + 1, cols, :])
            )
            if at + width > FILT:
                value = jnp.where(column_mask(at, width, FILT, rows), value, 0.0)
            grad[:, cols] = value


def conv_backward(ids, km, kt, emb, emb_t, total, grad, dk, demb):
    rows = grad.shape[0]
    kt[...] = jnp.transpose(km[pl.ds(112, LANE), :])
    for t in range(3):
        emb_t[pl.ds(LANE * t, LANE), :] = jnp.transpose(emb[t])
    emb_t[pl.ds(3 * LANE, LANE), :] = jnp.zeros((LANE, rows), BF16)
    dk[...] = jnp.zeros_like(dk)
    demb[...] = jnp.zeros_like(demb)
    for at, width in fblocks(FW):
        cols = pl.ds(at, width)
        grad[:, cols] = grad[:, cols] / total[:, cols]

    def step(p, tile, second, within, limit):
        window_t = emb_t[pl.ds(p * 16 if isinstance(p, int) else pl.multiple_of(p * 16, 16), LANE), :]
        back = jnp.zeros((rows, LANE), F32)
        for at, width in fblocks(FW):
            if at >= limit:
                continue
            cols = pl.ds(at, width)
            act = jnp.tanh(conv_at(emb, km, tile, second, within, at, width))
            dz = grad[:, cols] * jnp.exp(act) * (1.0 - act * act)
            if at + width > limit and limit < FILT:
                dz = jnp.where(column_mask(at, width, limit, rows), dz, 0.0)
            dz = dz.astype(BF16)
            dk[:, cols] += mm(window_t, dz)
            back = back + mm(dz, kt[cols, :])
        lane = lanes(rows)
        back = jnp.where(lane < 112, back, 0.0)
        turned = pltpu.roll(back, 16 * within, 1)
        demb[tile] += jnp.where(lane >= 16 * within, turned, 0.0)
        if second:
            demb[tile + 1] += jnp.where(lane < 16 * within, turned, 0.0)

    conv_steps(step)


def table_backward(ids, demb, table):
    acc = jnp.zeros((64, LANE), F32)
    for t in range(3):
        hot = char_onehot(ids, t)
        value = demb[t]
        high = value.astype(BF16)
        low = (value - high.astype(F32)).astype(BF16)
        grads = mm_tn(hot, high) + mm_tn(hot, low)
        for m in range(8):
            block = grads[64 * m : 64 * m + 64, :]
            acc = acc + (pltpu.roll(block, LANE - 16 * m, 1) if m else block)
    table[...] = acc


def tile_rows(stage, base, value, row_tiles, col_tiles, first_col=0, pitch=None):
    pitch = col_tiles if pitch is None else pitch
    for r in range(row_tiles):
        for c in range(col_tiles):
            stage[base + r * pitch + first_col + c] = value[16 * r : 16 * r + 16, LANE * c : LANE * c + LANE].astype(BF16)


def six(x):
    return jnp.concatenate([x] * 6, axis=1)


ANYWHERE = pl.BlockSpec(memory_space=pl.ANY)
ON_CHIP = pl.BlockSpec(memory_space=pltpu.VMEM)
LIMIT = 56 << 20


def call(kernel, name, ins, specs, outs, scratch, aliases=None):
    return pl.pallas_call(
        kernel,
        out_shape=[jax.ShapeDtypeStruct(shape, dtype) for shape, dtype in outs],
        in_specs=specs,
        out_specs=[ANYWHERE] * len(outs),
        scratch_shapes=scratch,
        input_output_aliases=aliases or {},
        compiler_params=pltpu.CompilerParams(vmem_limit_bytes=LIMIT),
        name=name,
    )(*ins)


def vmem(shape, dtype):
    return pltpu.VMEM(shape, dtype)


def dmas(count):
    return pltpu.SemaphoreType.DMA((count,))


def char_forward_call(ids, km, e8, ab):
    n = ids.shape[0]

    def kernel(ids, km, e8, ab, y2_o, feats_o, pres_o, total_o, emb_o, km_v, e8_v, ab_v, y2, feats, pres, total, emb, sem):
        @pl.when(lax.axis_index("section") == 0)
        def _():
            load([(km, km_v), (e8, e8_v), (ab, ab_v)], sem)
            char_forward(ids, e8_v, km_v, ab_v, emb, total, feats, pres, y2)
            load([(y2, y2_o), (feats, feats_o), (pres, pres_o), (total, total_o), (emb, emb_o)], sem)

    outs = [
        ((n, FW), BF16),
        ((2, n, FW), BF16),
        ((4, n, FW), F32),
        ((n, FW), F32),
        ((3, n, LANE), BF16),
    ]
    scratch = [vmem(km.shape, BF16), vmem(e8.shape, BF16), vmem(ab.shape, BF16)]
    scratch += [vmem(shape, dtype) for shape, dtype in outs] + [dmas(5)]
    return call(kernel, "char_forward", (ids, km, e8, ab), [ON_CHIP] + [ANYWHERE] * 3, outs, scratch)


def char_backward_call(ids, dy, km, ab, saved):
    n = ids.shape[0]
    feats, pres, total, emb = saved
    MESH = pl.DeviceIdType.MESH

    def kernel(
        ids, dy, km, ab, feats, pres, total, emb, tiles_o, bias_o, right_o,
        dy_v, km_v, ab_v, feats_v, pres_v, total_v, emb_v, grad, dpre, kt, emb_t, dk, demb, table, stage, bias, sem,
        send, recv, sem_own,
    ):
        me = lax.axis_index("dp")

        def right_copy(layer, k):
            part = pl.ds(2 * layer, 2)
            return pltpu.make_async_remote_copy(
                dpre.at[part], right_o.at[k - 1, part], send.at[layer, k - 1], recv.at[layer, k - 1],
                device_id={"dp": quad_peer(me, k)}, device_id_type=MESH,
            )

        def right_own(layer):
            part = pl.ds(2 * layer, 2)
            return pltpu.make_async_copy(dpre.at[part], right_o.at[QUAD - 1, part], sem_own.at[layer])

        def share(layer):
            for k in range(1, QUAD):
                right_copy(layer, k).start()
            right_own(layer).start()

        @pl.when(lax.axis_index("section") == 0)
        def _():
            barrier = pltpu.get_barrier_semaphore()
            for k in range(1, QUAD):
                pl.semaphore_signal(barrier, inc=1, device_id={"dp": quad_peer(me, k)}, device_id_type=MESH)
            load(
                [(dy, dy_v), (km, km_v), (ab, ab_v), (feats, feats_v), (pres, pres_v), (total, total_v), (emb, emb_v)],
                sem,
            )
            pl.semaphore_wait(barrier, QUAD - 1)
            highway_backward(dy_v, ab_v, feats_v, pres_v, grad, dpre, share)
            for at, width in fblocks(FW):
                bias[:, pl.ds(at, width)] = jnp.sum(dpre[0, :, pl.ds(at, width)].astype(F32), axis=0, keepdims=True)
            conv_backward(ids, km_v, kt, emb_v, emb_t, total_v, grad, dk, demb)
            table_backward(ids, demb, table)
            tile_rows(stage, 0, dk[...], 8, 9)
            tile_rows(stage, 72, table[...], 4, 1)
            load([(stage, tiles_o), (bias, bias_o)], sem)
            for layer in range(2):
                right_own(layer).wait()
                for k in range(1, QUAD):
                    right_copy(layer, k).wait_send()
                    right_copy(layer, k).wait_recv()

    outs = [((CONV_TILES, 16, LANE), BF16), ((1, FW), F32), ((QUAD, 4, n, FW), BF16)]
    scratch = [
        vmem(dy.shape, BF16), vmem(km.shape, BF16), vmem(ab.shape, BF16), vmem(feats.shape, BF16),
        vmem(pres.shape, F32), vmem(total.shape, F32), vmem(emb.shape, BF16),
        vmem((n, FW), F32), vmem((4, n, FW), BF16), vmem((FW, LANE), BF16), vmem((4 * LANE, n), BF16),
        vmem((LANE, FW), F32), vmem((3, n, LANE), F32), vmem((64, LANE), F32),
        vmem((CONV_TILES, 16, LANE), BF16), vmem((1, FW), F32), dmas(7),
        pltpu.SemaphoreType.DMA((2, QUAD - 1)), pltpu.SemaphoreType.DMA((2, QUAD - 1)), dmas(2),
    ]
    return pl.pallas_call(
        kernel,
        out_shape=[jax.ShapeDtypeStruct(shape, dtype) for shape, dtype in outs],
        in_specs=[ON_CHIP] + [ANYWHERE] * 7,
        out_specs=[ANYWHERE] * 3,
        scratch_shapes=scratch,
        compiler_params=pltpu.CompilerParams(vmem_limit_bytes=LIMIT, collective_id=4, has_side_effects=True),
        name="char_backward",
    )(ids, dy, km, ab, feats, pres, total, emb)


CONV_TILES = 76
TILES = 3648


def turned_tile(left, right, shift):
    rows = right.shape[0]
    if shift:
        mixed = jnp.where(
            lanes(rows) < shift, pltpu.roll(left.astype(F32), shift, 1), pltpu.roll(right.astype(F32), shift, 1)
        )
        right = mixed.astype(BF16)
    return jnp.transpose(right)


def each_vocab(body, step=2048):
    whole = VW // step

    def one(i, carry):
        body(pl.multiple_of(i * step, step), step)
        return carry

    lax.fori_loop(0, whole, one, 0)
    body(whole * step, VW - whole * step)


def output_weights_call(h, dl):
    n = h.shape[0]
    rows = 704
    pitch = VW // LANE

    def kernel(h, dl, tiles_o, h_v, dl_v, h_t, stage, sem):
        @pl.when(lax.axis_index("section") == 3)
        def _():
            load([(h, h_v), (dl, dl_v)], sem)
            lane = lanes(n)
            for c in range(6):
                value = h_v[:, pl.ds(LANE * c, LANE)].astype(F32)
                value = jnp.where(lane + c * LANE == HID, 1.0, value).astype(BF16)
                h_t[pl.ds(LANE * c, LANE), :] = jnp.transpose(value)

            def body(at, width):
                first = at // LANE
                for top, count in fblocks(rows):
                    value = mm(h_t[pl.ds(top, count), :], dl_v[:, pl.ds(at, width)])
                    for r in range(count // 16):
                        for c in range(width // LANE):
                            stage[(top // 16 + r) * pitch + first + c] = value[
                                16 * r : 16 * r + 16, LANE * c : LANE * c + LANE
                            ].astype(BF16)

            each_vocab(body, 256)
            count = rows // 16 * pitch
            load([(stage.at[pl.ds(0, count)], tiles_o.at[pl.ds(0, count)])], sem)

    scratch = [
        vmem((n, GW), BF16), vmem((n, VW), BF16), vmem((6 * LANE, n), BF16),
        vmem((rows // 16 * pitch, 16, LANE), BF16), dmas(2),
    ]
    return call(
        kernel, "output_weights", (h, dl), [ANYWHERE] * 2, [((TILES, 16, LANE), BF16)], scratch
    )[0]


CHUNK = 32
GROUPS_OUT = (3, 3, 2, 1)


def lstm_steps(first, count, keep, carry, r, gates, cells, prevs, hiddens):
    def step(s, carry):
        h, c = carry
        at = pl.ds(pl.multiple_of((first + s) * 8, 8), 8)
        k = six(keep[at, :])
        hp = h * k
        cp = c * k
        prevs[at, :] = hp
        z = gates[at, :] + mm(hp.astype(BF16), r[...])
        i = sigmoid(z[:, 0:GW])
        f = sigmoid(z[:, GW : 2 * GW])
        o = sigmoid(z[:, 2 * GW : 3 * GW])
        g = jnp.tanh(z[:, 3 * GW :])
        c = f * cp + i * g
        h = (o * jnp.tanh(c)).astype(BF16).astype(F32)
        gates[at, :] = jnp.concatenate([i, f, o, g], axis=1)
        cells[at, :] = c
        hiddens[at, :] = h
        return h, c

    return lax.fori_loop(0, count, step, carry)


def lstm_back_steps(first, count, keep, c0, carry, rt, gates, cells, dhs):
    def step(s, carry):
        dh_next, dc_next = carry
        t = first + count - 1 - s
        at = pl.ds(pl.multiple_of(t * 8, 8), 8)
        before = pl.ds(pl.multiple_of(jnp.maximum(t - 1, 0) * 8, 8), 8)
        k = six(keep[at, :])
        saved = gates[at, :]
        i, f, o, g = [saved[:, GW * b : GW * b + GW] for b in range(4)]
        cp = jnp.where(t > 0, cells[before, :], c0[...]) * k
        ct = jnp.tanh(cells[at, :])
        dh = dhs[at, :] + dh_next
        dc = dc_next + dh * o * (1.0 - ct * ct)
        dz = jnp.concatenate(
            [dc * g * i * (1.0 - i), dc * cp * f * (1.0 - f), dh * ct * o * (1.0 - o), dc * i * (1.0 - g * g)], axis=1
        ).astype(BF16)
        gates[at, :] = dz.astype(F32)
        return k * mm(dz, rt[...]), k * dc * f

    return lax.fori_loop(0, count, step, carry)


def output_rows(first, count, h, w, targets, valid, logits, dl, top, part, dh, loss, dh16):
    at_rows = pl.ds(first, count)
    depth = w.shape[0]
    own = pl.ds(0, count)
    top[own, :] = jnp.full((count, LANE), -jnp.inf, F32)

    def forward(at, width):
        z = mm(h[at_rows, pl.ds(0, depth)], w[:, pl.ds(at, width)])
        if isinstance(at, int):
            z = jnp.where(column_mask(at, width, VOCAB, count), z, -jnp.inf)
        logits[own, pl.ds(at, width)] = z
        best = top[own, :]
        for c in range(width // LANE):
            best = jnp.maximum(best, z[:, LANE * c : LANE * c + LANE])
        top[own, :] = best

    each_vocab(forward)
    best = jnp.max(top[own, :], axis=1, keepdims=True)
    part[:, own, :] = jnp.zeros((2, count, LANE), F32)
    wanted = targets[at_rows, :]

    def exponents(at, width):
        z = logits[own, pl.ds(at, width)]
        e = jnp.exp(z - best)
        logits[own, pl.ds(at, width)] = e
        for c in range(width // LANE):
            part[0, own, :] += e[:, LANE * c : LANE * c + LANE]
            hit = lanes(count) + (at + LANE * c) == wanted
            part[1, own, :] += jnp.where(hit, z[:, LANE * c : LANE * c + LANE], 0.0)

    each_vocab(exponents)
    total = jnp.sum(part[0, own, :], axis=1, keepdims=True)
    picked = jnp.sum(part[1, own, :], axis=1, keepdims=True)
    counts = valid[at_rows, :]
    loss[...] += jnp.sum(counts * (best + jnp.log(total) - picked), axis=0, keepdims=True)
    share = counts / total
    dh[own, :] = jnp.zeros((count, depth), F32)

    def backward(at, width):
        e = logits[own, pl.ds(at, width)]
        pieces = []
        for c in range(width // LANE):
            hit = lanes(count) + (at + LANE * c) == wanted
            grad = e[:, LANE * c : LANE * c + LANE] * share - jnp.where(hit, counts, 0.0)
            pieces.append(grad.astype(BF16))
        grad = jnp.concatenate(pieces, axis=1)
        dl[at_rows, pl.ds(at, width)] = grad
        dh[own, :] += mm_nt(grad, w[:, pl.ds(at, width)])

    each_vocab(backward)
    for at, width in fblocks(depth):
        value = dh[own, pl.ds(at, width)]
        dh16[at_rows, pl.ds(at, width)] = jnp.where(column_mask(at, width, HID, count), value, 0.0).astype(BF16)


QUAD = 4
LEFT0 = 35 * LANE
LEFT1 = 14 * LANE
LEFT2 = 11 * LANE
LEFT_ROOM = 41 * LANE


def quad_peer(me, k):
    place = lax.rem(me, QUAD)
    return me - place + lax.rem(place + k, QUAD)


def turn_features(feats, turned):
    n = feats.shape[1]
    zero = jnp.zeros((n, LANE), BF16)
    for segment in range(4):
        start = segment * (FILT + 1)
        shift, first, last = start % LANE, start // LANE, (start + FILT) // LANE
        for c in range(last - first + 1):
            left = feats[segment // 2, :, pl.ds(LANE * (c - 1), LANE)] if c > 0 else zero
            right = feats[segment // 2, :, pl.ds(LANE * c, LANE)] if c < 9 else zero
            tile = turned_tile(left, right, shift)
            at = pl.ds(LANE * (first + c), LANE)
            if c == 0 and segment > 0:
                tile = tile + turned[at, :]
            turned[at, :] = tile


def turn_inputs(x, prevs, depth, turned):
    n = prevs.shape[0]
    first, shift = depth // LANE, depth % LANE
    end = depth + HID
    zero = jnp.zeros((n, LANE), F32)
    lane = lanes(n)
    for c in range(end // LANE + 1):
        if c < first:
            mixed = x[:, pl.ds(LANE * c, LANE)]
        else:
            k = c - first
            left = prevs[:, pl.ds(LANE * (k - 1), LANE)] if 0 < k < 7 else zero
            right = prevs[:, pl.ds(LANE * k, LANE)] if k < 6 else zero
            before = pltpu.roll(left, shift, 1) if k else x[:, pl.ds(LANE * c, LANE)].astype(F32)
            mixed = jnp.where(lane < shift, before, pltpu.roll(right, shift, 1))
            mixed = jnp.where(lane + c * LANE == end, 1.0, mixed).astype(BF16)
        turned[pl.ds(LANE * c, LANE), :] = jnp.transpose(mixed)


def recurrent_call(y2, feats, ur, rt, wt, keep, targets, valid, state):
    n = y2.shape[0]
    chunks = n // CHUNK
    steps = CHUNK // 8
    depth_w = wt.shape[0]
    MESH = pl.DeviceIdType.MESH

    def kernel(
        y2, feats, ur, rt, wt, keep, targets, valid, state,
        dy_o, xb_o, lhs_o, dz_o, dl_o, loss_o,
        feats_v, turned, x1, xb, hb, db, ob, dy, u, r, r_t, w, start, gates, cells, prevs, hs, dhs, dz16,
        logits, dl, top, part, dh, loss,
        sem_in, sem_out, send_y, recv_y, send_f, recv_f, send_b, recv_b, send_d, recv_d,
        send_l, recv_l, send_z, recv_z,
    ):
        role = lax.axis_index("section")
        me = lax.axis_index("dp")
        loss[...] = jnp.zeros_like(loss)

        def to(step, source, target, send, recv):
            return pltpu.make_async_remote_copy(
                source, target, send, recv, device_id={"section": role + step}, device_id_type=MESH
            )

        def span(c):
            return pl.ds(pl.multiple_of(c * CHUNK, CHUNK), CHUNK)

        def forward_copy(c, step):
            return to(step, hb.at[span(c)], xb.at[span(c)], send_f.at[c], recv_f.at[c])

        def backward_copy(c, step):
            return to(step, ob.at[span(c)], db.at[span(c)], send_b.at[c], recv_b.at[c])

        def feature_copy(step):
            return to(step, y2, x1, send_y.at[0], recv_y.at[0])

        def last_copy(step):
            return to(step, dy, dy, send_d.at[0], recv_d.at[0])

        def left_copy(k, rows):
            return pltpu.make_async_remote_copy(
                turned.at[pl.ds(0, rows)], lhs_o.at[k - 1, pl.ds(0, rows)], send_l.at[k - 1], recv_l.at[k - 1],
                device_id={"dp": quad_peer(me, k)}, device_id_type=MESH,
            )

        def left_own(rows):
            return pltpu.make_async_copy(
                turned.at[pl.ds(0, rows)], lhs_o.at[QUAD - 1, pl.ds(0, rows)], send_l.at[QUAD - 1]
            )

        def left_start(rows):
            for k in range(1, QUAD):
                left_copy(k, rows).start()
            left_own(rows).start()

        def left_finish(rows):
            left_own(rows).wait()
            for k in range(1, QUAD):
                left_copy(k, rows).wait_send()
                left_copy(k, rows).wait_recv()

        def right_copy(k, c):
            return pltpu.make_async_remote_copy(
                dz16.at[span(c)], dz_o.at[k - 1, span(c)], send_z.at[k - 1, c], recv_z.at[k - 1, c],
                device_id={"dp": quad_peer(me, k)}, device_id_type=MESH,
            )

        def inputs(which):
            if which == 0:
                pairs = [(feats, feats_v)]
            elif which == 3:
                pairs = [(wt, w)]
            else:
                depth = FW if which == 1 else GW
                pairs = [
                    (ur.at[pl.ds(0, depth)], u.at[pl.ds(0, depth)]),
                    (ur.at[pl.ds(FW, GW)], r),
                    (rt, r_t),
                    (state.at[which - 1], start),
                ]
            return [pltpu.make_async_copy(a, b, sem_in.at[i]) for i, (a, b) in enumerate(pairs)]

        for which in range(4):

            @pl.when(role == which)
            def _(which=which):
                for copy in inputs(which):
                    copy.start()

        barrier = pltpu.get_barrier_semaphore()

        @pl.when(role > 0)
        def _():
            pl.semaphore_signal(barrier, inc=1, device_id={"section": role - 1}, device_id_type=MESH)

        @pl.when(role < 3)
        def _():
            pl.semaphore_signal(barrier, inc=1, device_id={"section": role + 1}, device_id_type=MESH)

        for k in range(1, QUAD):
            pl.semaphore_signal(barrier, inc=1, device_id={"dp": quad_peer(me, k)}, device_id_type=MESH)
        pl.semaphore_wait(barrier, lax.min(role, 1) + lax.min(3 - role, 1) + QUAD - 1)

        @pl.when(role == 0)
        def _():
            feature_copy(1).start()
            for copy in inputs(0):
                copy.wait()
            turn_features(feats_v, turned)
            left_start(LEFT0)
            feature_copy(1).wait_send()
            left_finish(LEFT0)
            last_copy(1).wait_recv()
            copy = pltpu.make_async_copy(dy, dy_o, sem_out.at[0])
            copy.start()
            copy.wait()

        @pl.when((role == 1) | (role == 2))
        def _():
            for which in (1, 2):

                @pl.when(role == which)
                def _(which=which):
                    for copy in inputs(which):
                        copy.wait()

            bias = r[pl.ds(HID, 1), :].astype(F32)

            @pl.when(role == 1)
            def _():
                feature_copy(-1).wait_recv()
                for at, width in fblocks(ZW):
                    cols = pl.ds(at, width)
                    gates[:, cols] = mm(x1[...], u[:, cols]) + bias[:, at : at + width]

            def chunk_forward(c, carry):
                @pl.when(role == 2)
                def _():
                    forward_copy(c, -1).wait_recv()
                    for at, width in fblocks(ZW):
                        cols = pl.ds(at, width)
                        gates[span(c), cols] = mm(xb[span(c), :], u[pl.ds(0, GW), cols]) + bias[:, at : at + width]

                carry = lstm_steps(c * steps, steps, keep, carry, r, gates, cells, prevs, hs)
                hb[span(c), :] = hs[span(c), :].astype(BF16)
                forward_copy(c, 1).start()
                return carry

            h0 = start[0].astype(BF16).astype(F32)
            lax.fori_loop(0, chunks, chunk_forward, (h0, start[1]))

            for which in (1, 2):

                @pl.when(role == which)
                def _(which=which):
                    turn_inputs(x1 if which == 1 else xb, prevs, FILT if which == 1 else HID, turned)
                    left_start(LEFT1 if which == 1 else LEFT2)

            def chunk_backward(i, carry):
                c = chunks - 1 - i
                backward_copy(c, 1).wait_recv()
                dhs[span(c), :] = db[span(c), :].astype(F32)
                carry = lstm_back_steps(c * steps, steps, keep, start.at[1], carry, r_t, gates, cells, dhs)
                dz16[span(c), :] = gates[span(c), :].astype(BF16)
                for k in range(1, QUAD):
                    right_copy(k, c).start()

                @pl.when(role == 2)
                def _():
                    for at, width in fblocks(GW):
                        value = mm_nt(dz16[span(c), :], u[pl.ds(at, width), :])
                        if at + width > HID:
                            value = jnp.where(column_mask(at, width, HID, CHUNK), value, 0.0)
                        ob[span(c), pl.ds(at, width)] = value.astype(BF16)
                    backward_copy(c, -1).start()

                return carry

            zero = jnp.zeros((8, GW), F32)
            lax.fori_loop(0, chunks, chunk_backward, (zero, zero))

            own_right = pltpu.make_async_copy(dz16, dz_o.at[QUAD - 1], sem_out.at[1])
            own_right.start()

            @pl.when(role == 1)
            def _():
                for at, width in fblocks(FW):
                    value = mm_nt(dz16[...], u[pl.ds(at, width), :])
                    if at + width > FILT:
                        value = jnp.where(column_mask(at, width, FILT, n), value, 0.0)
                    dy[:, pl.ds(at, width)] = value.astype(BF16)
                last_copy(-1).start()
                left_finish(LEFT1)
                last_copy(-1).wait_send()

            @pl.when(role == 2)
            def _():
                left_finish(LEFT2)

                def sent(c, carry):
                    backward_copy(c, -1).wait_send()
                    return carry

                lax.fori_loop(0, chunks, sent, 0)

            own_right.wait()

            def sent(c, carry):
                forward_copy(c, 1).wait_send()
                for k in range(1, QUAD):
                    right_copy(k, c).wait_send()
                    right_copy(k, c).wait_recv()
                return carry

            lax.fori_loop(0, chunks, sent, 0)

        @pl.when(role == 3)
        def _():
            for copy in inputs(3):
                copy.wait()
            ob[...] = jnp.zeros_like(ob)
            done = 0
            for count in GROUPS_OUT:
                rows = pl.ds(done * CHUNK, count * CHUNK)
                for c in range(done, done + count):
                    forward_copy(c, -1).wait_recv()
                value = xb[rows, pl.ds(5 * LANE, LANE)].astype(F32)
                value = jnp.where(lanes(count * CHUNK) + 5 * LANE == HID, 1.0, value)
                xb[rows, pl.ds(5 * LANE, LANE)] = value.astype(BF16)
                output_rows(
                    done * CHUNK, count * CHUNK, xb, w, targets, valid, logits, dl, top, part, dh, loss, ob
                )
                for c in range(done, done + count):
                    backward_copy(c, -1).start()
                done += count
            copies = [
                pltpu.make_async_copy(xb, xb_o, sem_out.at[0]),
                pltpu.make_async_copy(dl, dl_o, sem_out.at[1]),
            ]
            for copy in copies:
                copy.start()
            for c in range(chunks):
                backward_copy(c, -1).wait_send()
            for copy in copies:
                copy.wait()

        loss_o[...] = loss[...]

    most = max(GROUPS_OUT) * CHUNK
    outs = [
        ((n, FW), BF16), ((n, GW), BF16), ((QUAD, LEFT_ROOM, n), BF16), ((QUAD, n, ZW), BF16), ((n, VW), BF16),
    ]
    scratch = [
        vmem((2, n, FW), BF16), vmem((LEFT0, n), BF16),
        vmem((n, FW), BF16), vmem((n, GW), BF16), vmem((n, GW), BF16), vmem((n, GW), BF16), vmem((n, GW), BF16),
        vmem((n, FW), BF16), vmem((FW, ZW), BF16), vmem((GW, ZW), BF16), vmem((ZW, GW), BF16), vmem(wt.shape, BF16),
        vmem((2, 8, GW), F32), vmem((n, ZW), F32), vmem((n, GW), F32), vmem((n, GW), F32), vmem((n, GW), F32),
        vmem((n, GW), F32), vmem((n, ZW), BF16),
        vmem((most, VW), F32), vmem((n, VW), BF16), vmem((most, LANE), F32), vmem((2, most, LANE), F32),
        vmem((most, depth_w), F32), vmem((1, LANE), F32),
        dmas(4), dmas(3), dmas(1), dmas(1), dmas(chunks), dmas(chunks), dmas(chunks), dmas(chunks), dmas(1), dmas(1),
        dmas(QUAD), dmas(QUAD - 1), pltpu.SemaphoreType.DMA((QUAD - 1, chunks)), pltpu.SemaphoreType.DMA((QUAD - 1, chunks)),
    ]
    return pl.pallas_call(
        kernel,
        out_shape=[jax.ShapeDtypeStruct(shape, dtype) for shape, dtype in outs]
        + [jax.ShapeDtypeStruct((1, LANE), F32)],
        in_specs=[ANYWHERE] * 5 + [ON_CHIP] * 3 + [ANYWHERE],
        out_specs=[ANYWHERE] * 5 + [ON_CHIP],
        scratch_shapes=scratch,
        compiler_params=pltpu.CompilerParams(vmem_limit_bytes=62 << 20, collective_id=3, has_side_effects=True),
        name="recurrent",
    )(y2, feats, ur, rt, wt, keep, targets, valid, state)


FORM = (
    (FILT, 9, 4 * (FILT + 1), CONV_END, CONV_TILES, 32),
    (4 * HID, 24, FILT + HID + 1, 0, 0, 16),
    (4 * HID, 24, 2 * HID + 1, 0, 0, 16),
    (VOCAB, 79, HID + 1, 0, 0, 16),
)


def slab(role, dest, share):
    width, pitch, rows, before, lead, period = FORM[role]
    low = lax.max if not isinstance(dest, int) else max
    high = lax.min if not isinstance(dest, int) else min
    one = (lambda v: v) if isinstance(dest, int) else jnp.int32
    start = low(one(share) * dest - before, one(0))
    first = start // width // period * period
    end = high((share * (dest + 1) - before + width - 1) // width, one(rows))
    count = low((end - first + 15) // 16, one(0)) * pitch
    tile = lead + first // 16 * pitch
    if lead:
        if isinstance(dest, int):
            if dest == 0:
                tile, count = 0, count + lead
        else:
            head = lax.max(1 - dest, 0)
            tile = tile - lead * head
            count = count + lead * head
    return first, tile, count


def slab_pieces(count, size):
    return (count + size - 1) // size


def gather_sum_call(tiles, groups, share):
    pair = 2
    across = groups // pair
    size = 64 if across <= 4 else 32
    pieces = max(slab_pieces(slab(3, dest, share)[2], size) for dest in range(groups))
    room = pieces * size
    line = across <= 4
    slots = across + 1 if line else across - 1
    MESH = pl.DeviceIdType.MESH

    def kernel(
        tiles, out, own, got1, got2, acc, own_sem, send1, recv1, send2, recv2, out_sem,
    ):
        role = lax.axis_index("section")
        me = lax.axis_index("dp")
        mine, side = me // pair, lax.rem(me, pair)
        other = mine * pair + (1 - side)

        def at_place(place):
            return {"dp": place * pair + side}

        def part(ref, slot, p):
            return ref.at[slot, pl.ds(pl.multiple_of(p * size, size), size)]

        def span(p):
            return pl.ds(pl.multiple_of(p * size, size), size)

        def loop(count, body):
            def step(p, carry):
                body(p)
                return carry

            lax.fori_loop(0, count, step, 0)

        def run(shape_of):
            def count_to(place, which):
                return shape_of(place * pair + which)[1]

            def own_copy(place, p):
                tile, _ = shape_of(place * pair + side)
                return pltpu.make_async_copy(
                    tiles.at[pl.ds(tile + p * size, size)], part(own, place, p), own_sem.at[place, p]
                )

            def first_copy(place, p):
                tile, _ = shape_of(place * pair + 1 - side)
                return pltpu.make_async_remote_copy(
                    tiles.at[pl.ds(tile + p * size, size)], part(got1, place, p), send1.at[place, p], recv1.at[place, p],
                    device_id={"dp": other}, device_id_type=MESH,
                )

            def begin(place):
                loop(count_to(place, 1 - side), lambda p: first_copy(place, p).start())
                loop(count_to(place, side), lambda p: own_copy(place, p).start())

            def hop_copy(place, up, p):
                if line:
                    target = mine + 1 if up else mine - 1
                    slot = jnp.where(place == mine + 1, across, place) if up else place
                else:
                    target = place
                    slot = lax.rem(place - mine + across, across) - 1
                return pltpu.make_async_remote_copy(
                    part(own, place, p), part(got2, slot, p), send2.at[place, p], recv2.at[slot, p],
                    device_id=at_place(target), device_id_type=MESH,
                )

            def arrived(slot, p):
                return pltpu.make_async_remote_copy(
                    part(own, 0, p), part(got2, slot, p), send2.at[0, p], recv2.at[slot, p],
                    device_id=at_place(lax.rem(mine + 1, across)), device_id_type=MESH,
                )

            def forward(place, up, has_before):
                def body(p):
                    own_copy(place, p).wait()
                    first_copy(place, p).wait_recv()
                    at = span(p)
                    own[place, at] = (own[place, at].astype(F32) + got1[place, at].astype(F32)).astype(BF16)
                    hop_copy(place, up, p).start()

                def body_sum(p):
                    own_copy(place, p).wait()
                    first_copy(place, p).wait_recv()
                    arrived(place, p).wait_recv()
                    at = span(p)
                    total = own[place, at].astype(F32) + got1[place, at].astype(F32) + got2[place, at].astype(F32)
                    own[place, at] = total.astype(BF16)
                    hop_copy(place, up, p).start()

                count = count_to(place, side)
                if not line:
                    loop(count, body)
                    return

                @pl.when(has_before)
                def _():
                    loop(count, body_sum)

                @pl.when(jnp.logical_not(has_before))
                def _():
                    loop(count, body)

            if line:
                for k in range(across - 1):

                    @pl.when(k < mine)
                    def _(k=k):
                        begin(k)

                    @pl.when(k < across - 1 - mine)
                    def _(k=k):
                        begin(across - 1 - k)

                begin(mine)
                for k in range(across - 1):

                    @pl.when(k < mine)
                    def _(k=k):
                        forward(k, False, mine < across - 1)

                    @pl.when(k < across - 1 - mine)
                    def _(k=k):
                        forward(across - 1 - k, True, mine > 0)

            else:
                for k in range(1, across):
                    begin(lax.rem(mine + k, across))
                begin(mine)
                for k in range(1, across):
                    forward(lax.rem(mine + k, across), True, None)

            def settle(p):
                own_copy(mine, p).wait()
                first_copy(mine, p).wait_recv()
                at = span(p)
                acc[at] = own[mine, at].astype(F32) + got1[mine, at].astype(F32)

            def add(slot):
                def body(p):
                    arrived(slot, p).wait_recv()
                    at = span(p)
                    acc[at] += got2[slot, at].astype(F32)

                return body

            mine_count = count_to(mine, side)
            loop(mine_count, settle)
            if line:

                @pl.when(mine < across - 1)
                def _():
                    loop(mine_count, add(mine))

                @pl.when(mine > 0)
                def _():
                    loop(mine_count, add(across))

            else:
                for k in range(1, across):
                    loop(mine_count, add(k - 1))

            def out_copy(p):
                return pltpu.make_async_copy(acc.at[span(p)], out.at[span(p)], out_sem.at[p])

            loop(mine_count, lambda p: out_copy(p).start())
            loop(mine_count, lambda p: out_copy(p).wait())
            for place in range(across):
                loop(count_to(place, 1 - side), lambda p, place=place: first_copy(place, p).wait_send())

                @pl.when(place != mine)
                def _(place=place):
                    loop(count_to(place, side), lambda p: hop_copy(place, True, p).wait_send())

        def shape_of(dest):
            _, tile, count = slab(3, dest, share)
            return tile, slab_pieces(count, size)

        @pl.when(role == 3)
        def _():
            barrier = pltpu.get_barrier_semaphore()
            pl.semaphore_signal(barrier, inc=1, device_id={"dp": other}, device_id_type=MESH)
            for k in range(1, across):
                peer = at_place(lax.rem(mine + k, across))
                pl.semaphore_signal(barrier, inc=1, device_id=peer, device_id_type=MESH)
            pl.semaphore_wait(barrier, across)
            run(shape_of)

    sems = pltpu.SemaphoreType.DMA
    return pl.pallas_call(
        kernel,
        out_shape=jax.ShapeDtypeStruct((room, 16, LANE), F32),
        in_specs=[ANYWHERE],
        out_specs=ANYWHERE,
        scratch_shapes=[
            vmem((across, room, 16, LANE), BF16), vmem((across, room, 16, LANE), BF16),
            vmem((slots, room, 16, LANE), BF16), vmem((room, 16, LANE), F32),
            sems((across, pieces)), sems((across, pieces)), sems((across, pieces)),
            sems((across, pieces)), sems((slots, pieces)), sems((pieces,)),
        ],
        compiler_params=pltpu.CompilerParams(vmem_limit_bytes=62 << 20, collective_id=1, has_side_effects=True),
        name="gather_sum",
    )(tiles)


BLOCK_ROWS = (25, 11, 11)


def finish_call(lhs, dz, dpre, conv, bias, loss, groups, share):
    n = lhs.shape[2]
    quads = groups // QUAD
    MESH = pl.DeviceIdType.MESH

    def most_blocks(role):
        width = FORM[role][1]
        lead = FORM[role][4]
        most = 0
        for dest in range(groups):
            count = slab(role, dest, share)[2]
            if lead and dest == 0:
                count -= lead
            most = max(most, -(-(count // width) // BLOCK_ROWS[role]))
        return most

    blocks = [most_blocks(role) for role in range(3)]
    room = max(
        FORM[role][4] + blocks[role] * BLOCK_ROWS[role] * FORM[role][1] for role in range(3)
    )
    left_rows = max(blocks[role] * BLOCK_ROWS[role] * 16 for role in range(3))
    most = max(blocks)

    def kernel(
        lhs, dz, dpre, conv, bias, loss, out, small_out,
        left, dpre_v, sent, got, acc, convs, lead_sum, small, got_small,
        sem_left, sem_right, send, recv, send_c, recv_c, small_send, small_recv, sem_out,
    ):
        role = lax.axis_index("section")
        me = lax.axis_index("dp")
        place, quad = lax.rem(me, QUAD), me // QUAD

        def across_peer(k):
            return {"dp": place + QUAD * lax.rem(quad + k, quads)}

        barrier = pltpu.get_barrier_semaphore()
        for k in range(1, QUAD):
            pl.semaphore_signal(barrier, inc=1, device_id={"dp": quad_peer(me, k)}, device_id_type=MESH)
        for k in range(1, quads):
            pl.semaphore_signal(barrier, inc=1, device_id=across_peer(k), device_id_type=MESH)

        def right_load(b):
            return pltpu.make_async_copy(
                dz.at[:, :, pl.ds(GW * b, GW)], dpre_v.at[:, b, :, pl.ds(0, GW)], sem_right.at[b]
            )

        def right_load0():
            return pltpu.make_async_copy(dpre, dpre_v, sem_right.at[0])

        def conv_load():
            return pltpu.make_async_copy(conv, convs.at[QUAD - 1], sem_right.at[1])

        @pl.when(role == 0)
        def _():
            right_load0().start()
            conv_load().start()

        @pl.when((role == 1) | (role == 2))
        def _():
            for b in range(4):
                right_load(b).start()

        pl.semaphore_wait(barrier, QUAD - 1 + quads - 1)

        small[...] = jnp.zeros_like(small)

        @pl.when(role == 0)
        def _():
            small[0, :, pl.ds(0, FW)] = bias[...]

        @pl.when(role == 3)
        def _():
            small[0, :, pl.ds(FW, LANE)] = loss[...]

        def small_copy(k):
            if k < QUAD:
                source, target = small.at[0], {"dp": quad_peer(me, k)}
            else:
                source, target = small.at[1], across_peer(k - QUAD + 1)
            return pltpu.make_async_remote_copy(
                source, got_small.at[k - 1], small_send.at[k - 1], small_recv.at[k - 1],
                device_id=target, device_id_type=MESH,
            )

        for k in range(1, QUAD):
            small_copy(k).start()

        def conv_copy(slot, target):
            return pltpu.make_async_remote_copy(
                conv, convs.at[slot], send_c.at[slot], recv_c.at[slot], device_id={"dp": target}, device_id_type=MESH
            )

        def run(which):
            width, pitch, rows, _, lead, _ = FORM[which]
            size = BLOCK_ROWS[which]
            block_tiles = size * pitch

            def geometry(k):
                dest = place + QUAD * lax.rem(quad + k, quads)
                first, _, count = slab(which, dest, share)
                if lead:
                    head = lax.max(1 - dest, 0)
                    count = count - lead * head
                else:
                    head = 0
                return first, (count // pitch + size - 1) // size, head

            def left_copy(k):
                height = blocks[which] * size * 16
                first = lax.min(geometry(k)[0], LEFT_ROOM - height)
                span = pl.ds(pl.multiple_of(first, 16), height)
                return pltpu.make_async_copy(
                    lhs.at[:, span], left.at[lax.rem(k, 2), :, pl.ds(0, blocks[which] * size * 16)], sem_left.at[lax.rem(k, 2)]
                )

            def block_copy(k, b):
                span = pl.ds(CONV_TILES + b * block_tiles, block_tiles)
                return pltpu.make_async_remote_copy(
                    sent.at[k - 1, span], got.at[k - 1, span], send.at[k - 1, b], recv.at[k - 1, b],
                    device_id=across_peer(k), device_id_type=MESH,
                )

            def lead_copy(k):
                span = pl.ds(0, CONV_TILES)
                return pltpu.make_async_remote_copy(
                    sent.at[k - 1, span], got.at[k - 1, span], send.at[k - 1, most], recv.at[k - 1, most],
                    device_id=across_peer(k), device_id_type=MESH,
                )

            def put(k, own, at, value):
                if own:
                    acc[at] = value
                else:
                    sent[k - 1, at] = value.astype(BF16)

            def block(k, own, b, first):
                here = pl.ds(pl.multiple_of(b * size * 16, 16), size * 16)
                base = CONV_TILES + b * block_tiles
                if which == 0:
                    row = lax.broadcasted_iota(jnp.int32, (size * 16, n), 0) + first + b * size * 16
                    start = first + b * size * 16
                    low = lax.min(start // (FILT + 1), 3)
                    high = lax.min((start + size * 16 - 1) // (FILT + 1), 3)
                    edge = (FILT + 1) * (low + 1)
                    lefts = [left[lax.rem(k, 2), g, here, :] for g in range(QUAD)]
                    near = [jnp.where(row < edge, x, jnp.zeros_like(x)) for x in lefts]
                    for col, wide in fblocks(FW):
                        value = jnp.zeros((size * 16, wide), F32)
                        for g in range(QUAD):
                            value = value + mm(near[g], dpre_v[g, low, :, pl.ds(col, wide)])
                        for r in range(size):
                            for c in range(wide // LANE):
                                tile = value[16 * r : 16 * r + 16, LANE * c : LANE * c + LANE]
                                put(k, own, base + r * pitch + col // LANE + c, tile)

                    @pl.when(high > low)
                    def _():
                        far = [jnp.where(row < edge, jnp.zeros_like(x), x) for x in lefts]
                        for col, wide in fblocks(FW):
                            value = jnp.zeros((size * 16, wide), F32)
                            for g in range(QUAD):
                                value = value + mm(far[g], dpre_v[g, high, :, pl.ds(col, wide)])
                            for r in range(size):
                                for c in range(wide // LANE):
                                    tile = value[16 * r : 16 * r + 16, LANE * c : LANE * c + LANE]
                                    at = base + r * pitch + col // LANE + c
                                    old = acc[at] if own else sent[k - 1, at].astype(F32)
                                    put(k, own, at, old + tile)

                else:
                    for col, wide in fblocks(ZW):
                        value = jnp.zeros((size * 16, wide), F32)
                        for g in range(QUAD):
                            value = value + mm(left[lax.rem(k, 2), g, here, :], dpre_v[g, col // GW, :, pl.ds(col % GW, wide)])
                        for r in range(size):
                            for c in range(wide // LANE):
                                tile = value[16 * r : 16 * r + 16, LANE * c : LANE * c + LANE]
                                put(k, own, base + r * pitch + col // LANE + c, tile)

            def loop(count, body):
                def step(b, carry):
                    body(b)
                    return carry

                lax.fori_loop(0, count, step, 0)

            left_copy(jnp.int32(1 % quads)).start()
            if which == 0:

                @pl.when(place > 0)
                def _():
                    for k in range(1, QUAD):

                        @pl.when(place == k)
                        def _(k=k):
                            conv_copy(k - 1, me - k).start()

                right_load0().wait()
                conv_load().wait()
            else:
                for b in range(4):
                    right_load(b).wait()

            if which == 0:

                @pl.when(place == 0)
                def _():
                    for k in range(1, QUAD):
                        conv_copy(k - 1, me + k).wait_recv()
                    total = convs[0].astype(F32)
                    for k in range(1, QUAD):
                        total = total + convs[k].astype(F32)
                    lead_sum[...] = total

            def slab_of(k, own):
                left_copy(k).wait()
                if not own:
                    left_copy(lax.rem(k + 1, quads)).start()
                first, count, head = geometry(k)
                if which == 0:

                    @pl.when(head > 0)
                    def _():
                        if own:
                            acc[pl.ds(0, CONV_TILES)] = lead_sum[...]
                        else:
                            sent[k - 1, pl.ds(0, CONV_TILES)] = lead_sum[...].astype(BF16)
                            lead_copy(k).start()

                def work(b):
                    block(k, own, b, first)
                    if not own:
                        block_copy(k, b).start()

                loop(count, work)

            def others(body):
                def step(k, carry):
                    body(k)
                    return carry

                lax.fori_loop(1, quads, step, 0)

            others(lambda k: slab_of(k, False))
            slab_of(jnp.int32(0), True)

            _, mine, head = geometry(0)
            def join(k):
                def add(b):
                    block_copy(k, b).wait_recv()
                    span = pl.ds(CONV_TILES + b * block_tiles, block_tiles)
                    acc[span] += got[k - 1, span].astype(F32)

                loop(mine, add)
                if which == 0:

                    @pl.when(head > 0)
                    def _():
                        lead_copy(k).wait_recv()
                        span = pl.ds(0, CONV_TILES)
                        acc[span] += got[k - 1, span].astype(F32)

            others(join)

            span = blocks[which] * block_tiles
            if which == 0:

                @pl.when(head > 0)
                def _():
                    copy = pltpu.make_async_copy(
                        acc.at[pl.ds(0, CONV_TILES + span)], out.at[pl.ds(0, CONV_TILES + span)], sem_out.at[0]
                    )
                    copy.start()
                    copy.wait()

                @pl.when(head == 0)
                def _():
                    copy = pltpu.make_async_copy(acc.at[pl.ds(CONV_TILES, span)], out.at[pl.ds(0, span)], sem_out.at[0])
                    copy.start()
                    copy.wait()

            else:
                copy = pltpu.make_async_copy(acc.at[pl.ds(CONV_TILES, span)], out.at[pl.ds(0, span)], sem_out.at[0])
                copy.start()
                copy.wait()

            def sent_all(k):
                _, count, head = geometry(k)
                loop(count, lambda b: block_copy(k, b).wait_send())
                if which == 0:

                    @pl.when(head > 0)
                    def _():
                        lead_copy(k).wait_send()

            others(sent_all)

            if which == 0:
                for k in range(1, QUAD):

                    @pl.when(place == k)
                    def _(k=k):
                        conv_copy(k - 1, me - k).wait_send()

        for k in range(1, QUAD):
            small_copy(k).wait_recv()
        small[1] = small[0] + got_small[0] + got_small[1] + got_small[2]
        for k in range(QUAD, QUAD + quads - 1):
            small_copy(k).start()

        for which in range(3):

            @pl.when(role == which)
            def _(which=which):
                run(which)

        total = small[1]
        for k in range(QUAD, QUAD + quads - 1):
            small_copy(k).wait_recv()
            total = total + got_small[k - 1]
        small_out[...] = total
        for k in range(1, QUAD + quads - 1):
            small_copy(k).wait_send()

    sems = pltpu.SemaphoreType.DMA
    full = CONV_TILES + max(blocks[role] * BLOCK_ROWS[role] * FORM[role][1] for role in range(3))
    smalls = QUAD + quads - 2
    return pl.pallas_call(
        kernel,
        out_shape=[jax.ShapeDtypeStruct((full, 16, LANE), F32), jax.ShapeDtypeStruct((1, FW + LANE), F32)],
        in_specs=[ANYWHERE] * 4 + [ON_CHIP] * 2,
        out_specs=[ANYWHERE, ON_CHIP],
        scratch_shapes=[
            vmem((2, QUAD, left_rows, n), BF16), vmem(dpre.shape, BF16),
            vmem((quads - 1, full, 16, LANE), BF16), vmem((quads - 1, full, 16, LANE), BF16),
            vmem((full, 16, LANE), F32), vmem((QUAD, CONV_TILES, 16, LANE), BF16), vmem((CONV_TILES, 16, LANE), F32),
            vmem((2, 1, FW + LANE), F32), vmem((smalls, 1, FW + LANE), F32),
            sems((2,)), sems((4,)), sems((quads - 1, most + 1)), sems((quads - 1, most + 1)),
            sems((QUAD - 1,)), sems((QUAD - 1,)), sems((smalls,)), sems((smalls,)), sems((1,)),
        ],
        compiler_params=pltpu.CompilerParams(vmem_limit_bytes=62 << 20, collective_id=5, has_side_effects=True),
        name="finish",
    )(lhs, dz, dpre, conv, bias, loss)


def sections_sum_call(small):
    count = lax.axis_size("section")

    def kernel(mine, out, held, send, recv):
        me = lax.axis_index("section")
        barrier = pltpu.get_barrier_semaphore()

        def peer(k):
            return {"section": lax.rem(me + k, count)}

        for k in range(1, count):
            pl.semaphore_signal(barrier, inc=1, device_id=peer(k), device_id_type=pl.DeviceIdType.MESH)
        pl.semaphore_wait(barrier, count - 1)
        copies = [
            pltpu.make_async_remote_copy(
                mine, held.at[k], send.at[k], recv.at[k], device_id=peer(k), device_id_type=pl.DeviceIdType.MESH
            )
            for k in range(1, count)
        ]
        for copy in copies:
            copy.start()
        total = mine[...]
        for k, copy in enumerate(copies):
            copy.wait_recv()
            total = total + held[k + 1]
        out[...] = total
        for copy in copies:
            copy.wait_send()

    return pl.pallas_call(
        kernel,
        out_shape=jax.ShapeDtypeStruct(small.shape, F32),
        in_specs=[ON_CHIP],
        out_specs=ON_CHIP,
        scratch_shapes=[vmem((count,) + small.shape, F32), dmas(count), dmas(count)],
        compiler_params=pltpu.CompilerParams(collective_id=2, has_side_effects=True),
        name="sections_sum",
    )(small)


def pack_call(summed, summed3, groups, share):
    rooms = (summed.shape[0] * 16, summed3.shape[0] * 16)
    chunks = share // LANE
    margin = 1280
    slab_rows = 10624
    flat_rows = margin + max(10752, chunks + 1280)

    def kernel(summed, summed3, out, rows_v, spaced, flat, sem):
        role = lax.axis_index("section")
        me = lax.axis_index("dp")
        zero = jnp.zeros((64, LANE), F32)

        def clear(i, carry):
            flat[pl.ds(pl.multiple_of(i * 64, 64), 64), :] = zero
            return carry

        def fetch(source, room):
            return pltpu.make_async_copy(source, rows_v.at[pl.ds(0, room)], sem.at[0])

        @pl.when(role < 3)
        def _():
            fetch(summed, rooms[0]).start()

        @pl.when(role == 3)
        def _():
            fetch(summed3, rooms[1]).start()

        lax.fori_loop(0, flat_rows // 64, clear, 0)

        @pl.when(role < 3)
        def _():
            fetch(summed, rooms[0]).wait()

        @pl.when(role == 3)
        def _():
            fetch(summed3, rooms[1]).wait()

        lane = lanes()

        for which in range(4):
            width, pitch, rows, before, lead, period = FORM[which]
            if which == 0:
                blocks, cols, tiles = 1, FILT, 9
            elif which == 3:
                blocks, cols, tiles = 1, VOCAB, 79
            else:
                blocks, cols, tiles = 4, HID, 6
            stride = period * width // LANE
            most = max(slab(which, dest, share)[2] for dest in range(groups))
            groups8 = -(-(-(-most // pitch) * 16) // (8 * period))

            @pl.when(role == which)
            def _(which=which):
                first, _, count = slab(which, me, share)
                skip = lead * lax.max(1 - me, 0)
                step_rows = pitch * 49 + (pitch * 49 + 1) % 2

                def space(rt, carry):
                    for c in range(pitch):
                        for half in range(2):
                            at = pl.multiple_of((skip + rt * pitch + c) * 16 + 8 * half, 8)
                            spaced[pl.ds(rt * step_rows + 49 * c + 24 * half, 8, stride=3), :] = rows_v[pl.ds(at, 8), :]
                    return carry

                lax.fori_loop(0, (count - skip) // pitch, space, 0)
                base = margin + before // LANE + stride * (first // period) - chunks * me

                def row(i, carry):
                    group, n = i // period, lax.rem(i, period)
                    number = first + period * (8 * group + sublanes()) + n
                    keep = number < rows
                    hop = period // 16 * step_rows
                    source = n // 16 * step_rows + 3 * lax.rem(n, 16) + 8 * group * hop
                    step = 27
                    for b in range(blocks):
                        flat_at = before % LANE + width * n + cols * b
                        turn = lax.rem(flat_at, LANE)
                        to = base + flat_at // LANE + stride * 8 * group
                        last = jnp.zeros((8, LANE), F32)
                        for low in range(0, tiles, step):
                            high = min(low + step, tiles)
                            taken = [
                                spaced[pl.ds(source + 49 * (tiles * b + j), 8, stride=hop), :]
                                for j in range(low, high)
                            ]
                            turned = [last] + [pltpu.roll(jnp.where(keep, x, 0.0), turn, 1) for x in taken]
                            for j in range(low, high):
                                value = jnp.where(lane >= turn, turned[j - low + 1], turned[j - low])
                                where = pl.ds(to + j, 8, stride=stride)
                                if j == 0:
                                    value = jnp.where(lane >= turn, value, flat[where, :])
                                flat[where, :] = value
                            last = turned[-1]
                        where = pl.ds(to + tiles, 8, stride=stride)
                        flat[where, :] = jnp.where(lane + LANE * tiles - turn < cols, last, flat[where, :])
                    return carry

                @pl.when(count > 0)
                def _():
                    lax.fori_loop(0, period * groups8, row, 0)

        @pl.when((role == 0) & (me == 0))
        def _():
            lane1 = lanes(1)

            def piece(row_at, flat_at, low, size):
                edge = flat_at - low
                turn = edge % LANE
                to = margin + (edge - turn) // LANE
                first, end = low // LANE, (low + size - 1) // LANE
                last = jnp.zeros((1, LANE), F32)
                for j in range(first, end + 2):
                    least, most = max(low + turn - LANE * j, 0), min(low + size + turn - LANE * j, LANE)
                    here = last
                    if j <= end:
                        here = rows_v[row_at + 16 * j : row_at + 16 * j + 1, :]
                        here = pltpu.roll(here, turn, 1) if turn else here
                    if most > least:
                        value = jnp.where(lane1 >= turn, here, last) if turn else here
                        at = to + j
                        if least > 0 or most < LANE:
                            value = jnp.where((lane1 >= least) & (lane1 < most), value, flat[at : at + 1, :])
                        flat[at : at + 1, :] = value
                    last = here

            for k in range(1, 8):
                n = NFILT[k - 1]
                for i in range(k * D_CHAR + 1):
                    number = i + i // D_CHAR if i < k * D_CHAR else 15
                    piece(number // 16 * 144 + number % 16, KOFF[k - 1] + n * i, COLS[k - 1], n)
            for a in range(CHAR_V):
                piece(72 * 16 + a, D_CHAR * a, 0, D_CHAR)

        copy = pltpu.make_async_copy(flat.at[pl.ds(margin, chunks)], out, sem.at[0])
        copy.start()
        copy.wait()

    return pl.pallas_call(
        kernel,
        out_shape=jax.ShapeDtypeStruct((chunks, LANE), F32),
        in_specs=[ANYWHERE] * 2,
        out_specs=ANYWHERE,
        scratch_shapes=[
            vmem((slab_rows, LANE), F32), vmem((31104, LANE), F32), vmem((flat_rows, LANE), F32), dmas(1),
        ],
        compiler_params=pltpu.CompilerParams(vmem_limit_bytes=LIMIT),
        name="pack",
    )(summed.reshape(rooms[0], LANE), summed3.reshape(rooms[1], LANE))


def shards(char_ids, target_ids, remaining, resets, start_state, section_params):
    rows, steps = char_ids.shape[:2]
    groups = lax.axis_size("dp")
    packed = section_params.shape[1]
    share = packed // groups
    n = rows * (steps + 1)

    def by_step(x, fill):
        x = jnp.pad(x.T, ((0, 1), (0, 0)), constant_values=fill)
        return jnp.broadcast_to(x.reshape(n, 1), (n, LANE))

    ids = jnp.pad(
        char_ids.transpose(1, 0, 2), ((0, 1), (0, 0), (0, LANE - WORD_CHARS)), constant_values=-1
    ).reshape(n, LANE)
    targets = by_step(target_ids, -1)
    keep = by_step(1.0 - resets.astype(F32), 0.0)
    valid = by_step((jnp.arange(steps, dtype=jnp.int32)[None, :] < remaining[:, None]).astype(F32), 0.0)
    state = jnp.pad(start_state, ((0, 0), (0, 0), (0, 0), (0, GW - HID)))

    km, e8, ab, ur, rt, wt = unpack_all(section_params)
    y2, *char_saved = char_forward_call(ids, km, e8, ab)
    g0, xb, lhs, dz, dl, loss = recurrent_call(y2, char_saved[0], ur, rt, wt, keep, targets, valid, state)
    tiles3 = output_weights_call(xb, dl)
    summed3 = gather_sum_call(tiles3, groups, share)
    conv, bias, dpre = char_backward_call(ids, g0, km, ab, char_saved)
    summed, small = finish_call(lhs, dz, dpre, conv, bias, loss, groups, share)
    flat = pack_call(summed, summed3, groups, share)
    small = sections_sum_call(small)
    mean_loss = small[0, FW] / (groups * rows * steps)
    return mean_loss, flat.reshape(1, share), small[0, :FILT]


def solution(mesh):
    in_specs = (
        P("dp", None, None),
        P("dp", None),
        P("dp"),
        P("dp", None),
        P(None, None, "dp", None),
        P("section", None),
    )
    out_specs = (P(), P("section", "dp"), P())
    return jax.shard_map(shards, mesh=mesh, in_specs=in_specs, out_specs=out_specs, check_vma=False)
```

```python
import functools
import math

import jax
import jax.numpy as jnp
from jax import lax
from jax.experimental import pallas as pl
from jax.experimental.pallas import tpu as pltpu
from jax.sharding import PartitionSpec as P

D_CHAR = 15
CHAR_V = 51
F_UNIT = 50
WORD_CHARS = 21
HID = 650
VOCAB = 10000
FILT = 1100
F32 = jnp.float32
BF16 = jnp.bfloat16

NFILT = [F_UNIT * min(k, 4) for k in range(1, 8)]
COLS = [sum(NFILT[:k]) for k in range(8)]
KOFF = [CHAR_V * D_CHAR + sum((j * D_CHAR + 1) * NFILT[j - 1] for j in range(1, k)) for k in range(1, 9)]
CONV_END = KOFF[7]
HIGH_STRIDE = FILT * (FILT + 1)
FW = 1152
GW = 768
ZW = 4 * GW
VW = 10112
LANE = 128
LENS = (2304, 2688, 2688, 5120)


def roll_lanes(x, shift):
    return pltpu.roll(x, shift, 1)


def lanes(rows=8):
    return lax.broadcasted_iota(jnp.int32, (rows, LANE), 1)


def sublanes():
    return lax.broadcasted_iota(jnp.int32, (8, LANE), 0)


def widen(raw, slot, rows, wide):
    def body(i, carry):
        piece = raw[slot, 0:1, pl.ds(pl.multiple_of(i * 16384, 16384), 16384)]
        wide[pl.ds(pl.multiple_of(i * 128, 128), 128), :] = piece.astype(F32).reshape(128, LANE)
        return carry

    lax.fori_loop(0, rows // 128, body, 0)


def stream_blocks(count, length, total, chunk_of, src, raw, sem, wide, work):
    def start_of(i):
        first = chunk_of(i)
        return jnp.minimum(first // 8 * 8, total - length)

    def copy(i, slot):
        at = pl.multiple_of(start_of(i) * LANE, 8 * LANE)
        return pltpu.make_async_copy(
            src.at[:, pl.ds(at, length * LANE)], raw.at[slot, :, pl.ds(0, length * LANE)], sem.at[slot]
        )

    copy(0, 0).start()

    def body(i, carry):
        slot = lax.rem(i, 2)

        @pl.when(i + 1 < count)
        def _():
            copy(i + 1, 1 - slot).start()

        copy(i, slot).wait()
        widen(raw, slot, length, wide)
        work(i, chunk_of(i) - start_of(i))
        return carry

    lax.fori_loop(0, count, body, 0)


def take_rows(wide, starts, tiles, cols, stride, put):
    step = max(1, 28 // len(starts))
    lane = lanes()
    for low in range(0, tiles, step):
        high = min(tiles, low + step)
        loaded = [
            [wide[pl.ds(first + c, 8, stride=stride), :] for c in range(low, high + 1)] for _, first, _, _ in starts
        ]
        results = []
        for (_, _, shift, keep_row), pieces in zip(starts, loaded):
            turn = lax.rem(LANE - shift, LANE)
            split = lane < LANE - shift
            turned = [roll_lanes(piece, turn) for piece in pieces]
            for c in range(low, high):
                out = jnp.where(split, turned[c - low], turned[c - low + 1])
                keep = keep_row
                if cols - c * LANE < LANE:
                    keep = keep & (lane < cols - c * LANE)
                results.append(jnp.where(keep, out, 0.0))
        at = 0
        for tag, _, _, _ in starts:
            for c in range(low, high):
                put(tag, c, results[at])
                at += 1


def spread(c, n, period):
    return pl.ds((c * period + n) * 25, 8, stride=3)


def collect(dest, c, period):
    return [
        dest[pl.ds((c * period + 8 * m) * 25 + 3 * j, 8, stride=25), :] for j in range(8) for m in range(period // 8)
    ]


def stage_tile(stage, slot, c, blocks):
    for i in range(0, len(blocks), 2):
        pair = jnp.concatenate([blocks[i], blocks[i + 1]], axis=0).astype(BF16)
        stage[slot, pl.ds(8 * i, 16), pl.ds(c * LANE, LANE)] = pair


def unpack_kernel(
    src, km, e8, ab, ur, rt, wt, raw, wide, dest, kstage, stage0, stage1, stage_t, stage3, sem_in, sem_out, sem_t
):
    role = lax.axis_index("section")
    total = src.shape[1] // LANE

    def out_copy(stage, slot, target):
        return pltpu.make_async_copy(stage.at[slot], target, sem_out.at[slot])

    @pl.when(role == 0)
    def _():
        length = 640
        copy = pltpu.make_async_copy(
            src.at[:, pl.ds(0, length * LANE)], raw.at[0, :, pl.ds(0, length * LANE)], sem_in.at[0]
        )
        copy.start()
        copy.wait()
        widen(raw, 0, length, wide)
        lane1 = lanes(1)
        dest[pl.ds(0, 64), :] = jnp.zeros((64, LANE), F32)
        for a in range(CHAR_V):
            flat = D_CHAR * a
            q, s = flat // LANE, flat % LANE
            here = wide[q : q + 1, :]
            out = roll_lanes(here, (LANE - s) % LANE) if s else here
            if s + D_CHAR > LANE:
                out = jnp.where(lane1 < LANE - s, out, roll_lanes(wide[q + 1 : q + 2, :], LANE - s))
            dest[a : a + 1, :] = jnp.where(lane1 < D_CHAR, out, jnp.where(lane1 == D_CHAR, 1.0, 0.0))
        table = dest[pl.ds(0, 64), :]
        for m in range(8):
            kstage[pl.ds(64 * m, 64), pl.ds(0, LANE)] = (
                pltpu.roll(table, 16 * m, 1) if m else table
            ).astype(BF16)
        copy = pltpu.make_async_copy(kstage.at[pl.ds(0, 512), pl.ds(0, LANE)], e8, sem_out.at[0])
        copy.start()
        copy.wait()
        tiles = FW // LANE
        rows = 112
        dest[pl.ds(0, rows * tiles), :] = jnp.zeros((rows * tiles, LANE), F32)

        def kernel_row(k, i, row):
            n, base = NFILT[k - 1], COLS[k - 1]
            edge = KOFF[k - 1] + n * i - base
            q, s = edge // LANE, edge % LANE
            for ct in range(base // LANE, (base + n - 1) // LANE + 1):
                out = wide[q + ct : q + ct + 1, :]
                if s:
                    after = roll_lanes(wide[q + ct + 1 : q + ct + 2, :], LANE - s)
                    out = jnp.where(lane1 < LANE - s, roll_lanes(out, LANE - s), after)
                at = ct * rows + row
                low, high = max(base - ct * LANE, 0), min(base + n - ct * LANE, LANE)
                if low > 0 or high < LANE:
                    out = jnp.where((lane1 >= low) & (lane1 < high), out, dest[at : at + 1, :])
                dest[at : at + 1, :] = out

        for k in range(1, 8):
            for i in range(k * D_CHAR):
                kernel_row(k, i, i + i // D_CHAR)
            kernel_row(k, k * D_CHAR, 15)
        kstage[...] = jnp.zeros_like(kstage)
        for ct in range(tiles):
            kstage[pl.ds(112, rows), pl.ds(ct * LANE, LANE)] = dest[pl.ds(ct * rows, rows), :].astype(BF16)
        copy = pltpu.make_async_copy(kstage.at[pl.ds(0, 368)], km, sem_out.at[0])
        copy.start()
        copy.wait()

        blocks = 5

        def flat_of(i):
            return CONV_END + HIGH_STRIDE * (i // blocks)

        def chunk_of(i):
            return flat_of(i) // LANE + 2200 * lax.rem(i, blocks)

        def target(i):
            return ab.at[i // blocks, pl.ds(pl.multiple_of(lax.rem(i, blocks) * 256, 256), 256)]

        def work(i, extra):
            block = lax.rem(i, blocks)
            inner = lax.rem(flat_of(i), LANE)

            def rows_of(i, carry):
                starts = []
                for n in (2 * i, 2 * i + 1):
                    flat = inner + FILT * n
                    keep = 32 * (8 * block + sublanes()) + n <= FILT
                    starts.append((n, flat // LANE + extra, lax.rem(flat, LANE), keep))

                def put(n, c, value):
                    dest[spread(c, n, 32), :] = value

                take_rows(wide, starts, tiles, FILT, 275, put)
                return carry

            lax.fori_loop(0, 16, rows_of, 0)
            slot = lax.rem(i, 2)

            @pl.when(i >= 2)
            def _():
                out_copy(stage0, slot, target(i - 2)).wait()

            for c in range(tiles):
                stage_tile(stage0, slot, c, collect(dest, c, 32))
            out_copy(stage0, slot, target(i)).start()

        count = 4 * blocks
        stream_blocks(count, LENS[0], total, chunk_of, src, raw, sem_in, wide, work)
        for i in (count - 2, count - 1):
            out_copy(stage0, i % 2, target(i)).wait()

    for layer in (1, 2):

        @pl.when(role == layer)
        def _(layer=layer):
            depth = FILT if layer == 1 else HID
            blocks = -(-depth // 128)
            recurrent = depth * 4 * HID
            count = blocks + 6

            def chunk_of(i):
                return jnp.where(i < blocks, 2600 * i, recurrent // LANE + 2600 * (i - blocks))

            def target(i):
                at = jnp.where(i < blocks, i, i - blocks + 9)
                return ur.at[pl.ds(pl.multiple_of(at * 128, 128), 128)]

            def work(i, extra):
                inner = jnp.where(i < blocks, 0, recurrent % LANE)
                block = jnp.where(i < blocks, i, i - blocks)
                limit = jnp.where(i < blocks, depth, HID + 1)

                def rows_of(n, carry):
                    keep = 16 * (8 * block + sublanes()) + n < limit
                    flats = [inner + 4 * HID * n + HID * b for b in range(4)]

                    def put(b, c, value):
                        dest[spread(6 * b + c, n, 16), :] = value

                    starts = [(b, flat // LANE + extra, lax.rem(flat, LANE), keep) for b, flat in enumerate(flats)]
                    take_rows(wide, starts, 6, HID, 325, put)
                    return carry

                lax.fori_loop(0, 16, rows_of, 0)
                slot = lax.rem(i, 2)

                @pl.when(i >= 2)
                def _():
                    out_copy(stage1, slot, target(i - 2)).wait()

                for c in range(24):
                    stage_tile(stage1, slot, c, collect(dest, c, 16))
                out_copy(stage1, slot, target(i)).start()

                @pl.when(i >= blocks)
                def _():
                    @pl.when(i >= blocks + 2)
                    def _():
                        turned_copy(i - 2).wait()

                    k = LANE * block + lanes(LANE)
                    for c in range(24):
                        turned = jnp.transpose(jnp.concatenate(collect(dest, c, 16), axis=0))
                        stage_t[slot, pl.ds(128 * c, 128), :] = jnp.where(k < HID, turned, 0.0).astype(BF16)
                    turned_copy(i).start()

            def turned_copy(i):
                slot = lax.rem(i, 2)
                at = pl.multiple_of((i - blocks) * LANE, LANE)
                return pltpu.make_async_copy(stage_t.at[slot], rt.at[:, pl.ds(at, LANE)], sem_t.at[slot])

            stream_blocks(count, LENS[1], total, chunk_of, src, raw, sem_in, wide, work)
            for i in (count - 2, count - 1):
                out_copy(stage1, i % 2, target(jnp.int32(i))).wait()
                turned_copy(jnp.int32(i)).wait()

    @pl.when(role == 3)
    def _():
        count = 11
        tiles = VW // LANE

        def chunk_of(i):
            return 5000 * i

        def target(i):
            return wt.at[pl.ds(pl.multiple_of(i * 64, 64), 64)]

        def work(i, extra):
            def rows_of(n, carry):
                flat = VOCAB * n
                keep = 8 * (8 * i + sublanes()) + n < HID + 1

                def put(n, c, value):
                    dest[spread(c, n, 8), :] = value

                take_rows(wide, [(n, flat // LANE + extra, lax.rem(flat, LANE), keep)], tiles, VOCAB, 625, put)
                return carry

            lax.fori_loop(0, 8, rows_of, 0)
            slot = lax.rem(i, 2)

            @pl.when(i >= 2)
            def _():
                out_copy(stage3, slot, target(i - 2)).wait()

            for c in range(tiles):
                stage_tile(stage3, slot, c, collect(dest, c, 8))
            out_copy(stage3, slot, target(i)).start()

        stream_blocks(count, LENS[3], total, chunk_of, src, raw, sem_in, wide, work)
        for i in (count - 2, count - 1):
            out_copy(stage3, i % 2, target(jnp.int32(i))).wait()


def unpack_all(section_params):
    anywhere = pl.BlockSpec(memory_space=pl.ANY)
    return pl.pallas_call(
        unpack_kernel,
        out_shape=[
            jax.ShapeDtypeStruct((368, FW), BF16),
            jax.ShapeDtypeStruct((512, LANE), BF16),
            jax.ShapeDtypeStruct((4, 1280, FW), BF16),
            jax.ShapeDtypeStruct((15 * 128, ZW), BF16),
            jax.ShapeDtypeStruct((ZW, GW), BF16),
            jax.ShapeDtypeStruct((11 * 64, VW), BF16),
        ],
        in_specs=[anywhere],
        out_specs=[anywhere] * 6,
        scratch_shapes=[
            pltpu.VMEM((2, 1, LENS[3] * LANE), BF16),
            pltpu.VMEM((9312, LANE), F32),
            pltpu.VMEM((79 * 200, LANE), F32),
            pltpu.VMEM((512, FW), BF16),
            pltpu.VMEM((2, 256, FW), BF16),
            pltpu.VMEM((2, 128, ZW), BF16),
            pltpu.VMEM((2, ZW, LANE), BF16),
            pltpu.VMEM((2, 64, VW), BF16),
            pltpu.SemaphoreType.DMA((2,)),
            pltpu.SemaphoreType.DMA((2,)),
            pltpu.SemaphoreType.DMA((2,)),
        ],
        compiler_params=pltpu.CompilerParams(vmem_limit_bytes=56 << 20),
        name="unpack",
    )(section_params)


def fblocks(width, step=256):
    return [(at, min(step, width - at)) for at in range(0, width, step)]


def mm(a, b):
    return jnp.dot(a, b, preferred_element_type=F32)


def mm_tn(a, b):
    return lax.dot_general(a, b, (((0,), (0,)), ((), ())), preferred_element_type=F32)


def mm_nt(a, b):
    return lax.dot_general(a, b, (((1,), (1,)), ((), ())), preferred_element_type=F32)


def sigmoid(x):
    return 0.5 * jnp.tanh(0.5 * x) + 0.5


def load(pairs, sem):
    copies = [pltpu.make_async_copy(a, b, sem.at[i]) for i, (a, b) in enumerate(pairs)]
    for copy in copies:
        copy.start()
    for copy in copies:
        copy.wait()


def column_mask(at, width, limit, rows):
    return lax.broadcasted_iota(jnp.int32, (rows, width), 1) + at < limit


def char_onehot(ids, t):
    rows = ids.shape[0]
    lane = lanes(rows)
    pieces = []
    for pair in range(4):
        j = 8 * t + 2 * pair
        left = ids[:, j : j + 1]
        right = ids[:, j + 1 : j + 2]
        hit = jnp.where(lane < 64, left, right) == lax.rem(lane, 64)
        pieces.append(jnp.where(hit, 1.0, 0.0).astype(BF16))
    return jnp.concatenate(pieces, axis=1)


def conv_steps(body):
    def step(p, carry):
        body(p, p // 8, True, lax.rem(p, 8), FILT)
        return carry

    lax.fori_loop(0, 15, step, 0)
    body(15, 1, True, 7, COLS[6])
    for p in range(16, WORD_CHARS):
        body(p, 2, False, p - 16, COLS[WORD_CHARS - p])


def conv_at(emb, km, tile, second, within, at, width):
    first = 112 - 16 * within
    if not isinstance(first, int):
        first = pl.multiple_of(first, 16)
    if second:
        window = jnp.concatenate([emb[tile], emb[tile + 1]], axis=1)
    else:
        window = emb[tile]
    return mm(window, km[pl.ds(first, window.shape[1]), pl.ds(at, width)])


def char_forward(ids, e8, km, ab, emb, total, feats, pres, out):
    rows = ids.shape[0]
    for t in range(3):
        emb[t] = mm(char_onehot(ids, t), e8[...]).astype(BF16)
    total[...] = jnp.zeros_like(total)

    def step(p, tile, second, within, limit):
        for at, width in fblocks(FW):
            if at >= limit:
                continue
            value = jnp.exp(jnp.tanh(conv_at(emb, km, tile, second, within, at, width)))
            if at + width > limit and limit < FILT:
                value = jnp.where(column_mask(at, width, limit, rows), value, 0.0)
            total[:, pl.ds(at, width)] += value

    conv_steps(step)
    for at, width in fblocks(FW):
        col = lax.broadcasted_iota(jnp.int32, (rows, width), 1) + at
        count = jnp.full((rows, width), float(WORD_CHARS), F32)
        for k in range(1, 7):
            count = jnp.where(col >= COLS[k], float(WORD_CHARS - k), count)
        value = jnp.log(total[:, pl.ds(at, width)]) - jnp.log(count)
        value = jnp.where(col < FILT, value, jnp.where(col == FILT, 1.0, 0.0))
        feats[0, :, pl.ds(at, width)] = value.astype(BF16)
    for layer in range(2):
        for at, width in fblocks(FW):
            cols = pl.ds(at, width)
            t_pre = mm(feats[layer], ab[2 * layer, pl.ds(0, FW), cols])
            h_pre = mm(feats[layer], ab[2 * layer + 1, pl.ds(0, FW), cols])
            pres[2 * layer, :, cols] = t_pre
            pres[2 * layer + 1, :, cols] = h_pre
            gate = sigmoid(t_pre)
            y = feats[layer, :, cols].astype(F32)
            value = gate * (h_pre * sigmoid(h_pre)) + (1.0 - gate) * y
            col = lax.broadcasted_iota(jnp.int32, (rows, width), 1) + at
            if layer == 0:
                value = jnp.where(col < FILT, value, jnp.where(col == FILT, 1.0, 0.0))
                feats[1, :, cols] = value.astype(BF16)
            else:
                out[:, cols] = jnp.where(col < FILT, value, 0.0).astype(BF16)


def conv_backward(ids, km, kt, emb, emb_t, total, grad, dk, demb):
    rows = grad.shape[0]
    kt[...] = jnp.transpose(km[pl.ds(112, LANE), :])
    for t in range(3):
        emb_t[pl.ds(LANE * t, LANE), :] = jnp.transpose(emb[t])
    emb_t[pl.ds(3 * LANE, LANE), :] = jnp.zeros((LANE, rows), BF16)
    dk[...] = jnp.zeros_like(dk)
    demb[...] = jnp.zeros_like(demb)
    for at, width in fblocks(FW):
        cols = pl.ds(at, width)
        grad[:, cols] = grad[:, cols] / total[:, cols]

    def step(p, tile, second, within, limit):
        window_t = emb_t[pl.ds(p * 16 if isinstance(p, int) else pl.multiple_of(p * 16, 16), LANE), :]
        back = jnp.zeros((rows, LANE), F32)
        for at, width in fblocks(FW):
            if at >= limit:
                continue
            cols = pl.ds(at, width)
            act = jnp.tanh(conv_at(emb, km, tile, second, within, at, width))
            dz = grad[:, cols] * jnp.exp(act) * (1.0 - act * act)
            if at + width > limit and limit < FILT:
                dz = jnp.where(column_mask(at, width, limit, rows), dz, 0.0)
            dz = dz.astype(BF16)
            dk[:, cols] += mm(window_t, dz)
            back = back + mm(dz, kt[cols, :])
        lane = lanes(rows)
        back = jnp.where(lane < 112, back, 0.0)
        turned = pltpu.roll(back, 16 * within, 1)
        demb[tile] += jnp.where(lane >= 16 * within, turned, 0.0)
        if second:
            demb[tile + 1] += jnp.where(lane < 16 * within, turned, 0.0)

    conv_steps(step)


def table_backward(ids, demb, table):
    acc = jnp.zeros((64, LANE), F32)
    for t in range(3):
        hot = char_onehot(ids, t)
        value = demb[t]
        high = value.astype(BF16)
        low = (value - high.astype(F32)).astype(BF16)
        grads = mm_tn(hot, high) + mm_tn(hot, low)
        for m in range(8):
            block = grads[64 * m : 64 * m + 64, :]
            acc = acc + (pltpu.roll(block, LANE - 16 * m, 1) if m else block)
    table[...] = acc


def tile_rows(stage, base, value, row_tiles, col_tiles, first_col=0, pitch=None):
    pitch = col_tiles if pitch is None else pitch
    for r in range(row_tiles):
        for c in range(col_tiles):
            stage[base + r * pitch + first_col + c] = value[16 * r : 16 * r + 16, LANE * c : LANE * c + LANE].astype(BF16)


def six(x):
    return jnp.concatenate([x] * 6, axis=1)


ANYWHERE = pl.BlockSpec(memory_space=pl.ANY)
ON_CHIP = pl.BlockSpec(memory_space=pltpu.VMEM)
LIMIT = 56 << 20


def call(kernel, name, ins, specs, outs, scratch, aliases=None):
    return pl.pallas_call(
        kernel,
        out_shape=[jax.ShapeDtypeStruct(shape, dtype) for shape, dtype in outs],
        in_specs=specs,
        out_specs=[ANYWHERE] * len(outs),
        scratch_shapes=scratch,
        input_output_aliases=aliases or {},
        compiler_params=pltpu.CompilerParams(vmem_limit_bytes=LIMIT),
        name=name,
    )(*ins)


def vmem(shape, dtype):
    return pltpu.VMEM(shape, dtype)


def dmas(count):
    return pltpu.SemaphoreType.DMA((count,))


def char_forward_call(ids, km, e8, ab):
    n = ids.shape[0]

    def kernel(ids, km, e8, ab, y2_o, feats_o, pres_o, total_o, emb_o, km_v, e8_v, ab_v, y2, feats, pres, total, emb, sem):
        @pl.when(lax.axis_index("section") == 0)
        def _():
            load([(km, km_v), (e8, e8_v), (ab, ab_v)], sem)
            char_forward(ids, e8_v, km_v, ab_v, emb, total, feats, pres, y2)
            load([(y2, y2_o), (feats, feats_o), (pres, pres_o), (total, total_o), (emb, emb_o)], sem)

    outs = [
        ((n, FW), BF16),
        ((2, n, FW), BF16),
        ((4, n, FW), F32),
        ((n, FW), F32),
        ((3, n, LANE), BF16),
    ]
    scratch = [vmem(km.shape, BF16), vmem(e8.shape, BF16), vmem(ab.shape, BF16)]
    scratch += [vmem(shape, dtype) for shape, dtype in outs] + [dmas(5)]
    return call(kernel, "char_forward", (ids, km, e8, ab), [ON_CHIP] + [ANYWHERE] * 3, outs, scratch)


def char_backward_call(ids, grad, km, saved, dpre):
    n = ids.shape[0]
    total, emb = saved
    rows = SPLIT * CHUNK

    def kernel(
        ids, grad, km, total, emb, dpre, tiles_o, right_o,
        grad_v, km_v, total_v, emb_v, kt, emb_t, dk, demb, table, stage, sem, send, recv,
    ):
        me = lax.axis_index("dp")

        def right_copy(k):
            return pltpu.make_async_remote_copy(
                dpre.at[pl.ds(0, rows)], right_o.at[k - 1], send.at[k - 1], recv.at[k - 1],
                device_id={"dp": quad_peer(me, k)}, device_id_type=pl.DeviceIdType.MESH,
            )

        @pl.when(lax.axis_index("section") == 0)
        def _():
            barrier = pltpu.get_barrier_semaphore()
            for k in range(1, QUAD):
                pl.semaphore_signal(
                    barrier, inc=1, device_id={"dp": quad_peer(me, k)}, device_id_type=pl.DeviceIdType.MESH
                )
            pl.semaphore_wait(barrier, QUAD - 1)
            for k in range(1, QUAD):
                right_copy(k).start()
            load([(grad, grad_v), (km, km_v), (total, total_v), (emb, emb_v)], sem)
            conv_backward(ids, km_v, kt, emb_v, emb_t, total_v, grad_v, dk, demb)
            table_backward(ids, demb, table)
            tile_rows(stage, 0, dk[...], 8, 9)
            tile_rows(stage, 72, table[...], 4, 1)
            load([(stage, tiles_o)], sem)
            for k in range(1, QUAD):
                right_copy(k).wait_send()
                right_copy(k).wait_recv()

    outs = [((CONV_TILES, 16, LANE), BF16), ((QUAD - 1, rows, 4 * FW), BF16)]
    scratch = [
        vmem((n, FW), F32), vmem(km.shape, BF16), vmem(total.shape, F32), vmem(emb.shape, BF16),
        vmem((FW, LANE), BF16), vmem((4 * LANE, n), BF16), vmem((LANE, FW), F32), vmem((3, n, LANE), F32),
        vmem((64, LANE), F32), vmem((CONV_TILES, 16, LANE), BF16), dmas(4), dmas(QUAD - 1), dmas(QUAD - 1),
    ]
    return pl.pallas_call(
        kernel,
        out_shape=[jax.ShapeDtypeStruct(shape, dtype) for shape, dtype in outs],
        in_specs=[ON_CHIP] + [ANYWHERE] * 5,
        out_specs=[ANYWHERE] * 2,
        scratch_shapes=scratch,
        compiler_params=pltpu.CompilerParams(vmem_limit_bytes=LIMIT, collective_id=4, has_side_effects=True),
        name="char_backward",
    )(ids, grad, km, total, emb, dpre)


CONV_TILES = 76
TILES = 3648


def turned_tile(left, right, shift):
    rows = right.shape[0]
    if shift:
        mixed = jnp.where(
            lanes(rows) < shift, pltpu.roll(left.astype(F32), shift, 1), pltpu.roll(right.astype(F32), shift, 1)
        )
        right = mixed.astype(BF16)
    return jnp.transpose(right)


def each_vocab(body, step=2048):
    whole = VW // step

    def one(i, carry):
        body(pl.multiple_of(i * step, step), step)
        return carry

    lax.fori_loop(0, whole, one, 0)
    body(whole * step, VW - whole * step)


def output_weights_call(h, dl):
    n = h.shape[0]
    rows = 704
    pitch = VW // LANE

    def kernel(h, dl, tiles_o, h_v, dl_v, h_t, stage, sem):
        @pl.when(lax.axis_index("section") == 3)
        def _():
            load([(h, h_v), (dl, dl_v)], sem)
            lane = lanes(n)
            for c in range(6):
                value = h_v[:, pl.ds(LANE * c, LANE)].astype(F32)
                value = jnp.where(lane + c * LANE == HID, 1.0, value).astype(BF16)
                h_t[pl.ds(LANE * c, LANE), :] = jnp.transpose(value)

            def body(at, width):
                first = at // LANE
                for top, count in fblocks(rows):
                    value = mm(h_t[pl.ds(top, count), :], dl_v[:, pl.ds(at, width)])
                    for r in range(count // 16):
                        for c in range(width // LANE):
                            stage[(top // 16 + r) * pitch + first + c] = value[
                                16 * r : 16 * r + 16, LANE * c : LANE * c + LANE
                            ].astype(BF16)

            each_vocab(body, 256)
            count = rows // 16 * pitch
            load([(stage.at[pl.ds(0, count)], tiles_o.at[pl.ds(0, count)])], sem)

    scratch = [
        vmem((n, GW), BF16), vmem((n, VW), BF16), vmem((6 * LANE, n), BF16),
        vmem((rows // 16 * pitch, 16, LANE), BF16), dmas(2),
    ]
    return call(
        kernel, "output_weights", (h, dl), [ANYWHERE] * 2, [((TILES, 16, LANE), BF16)], scratch
    )[0]


CHUNK = 32
GROUPS_OUT = (3, 3, 2, 1)


def lstm_steps(first, count, keep, carry, r, gates, cells, prevs, hiddens):
    def step(s, carry):
        h, c = carry
        at = pl.ds(pl.multiple_of((first + s) * 8, 8), 8)
        k = six(keep[at, :])
        hp = h * k
        cp = c * k
        prevs[at, :] = hp
        z = gates[at, :] + mm(hp.astype(BF16), r[...])
        i = sigmoid(z[:, 0:GW])
        f = sigmoid(z[:, GW : 2 * GW])
        o = sigmoid(z[:, 2 * GW : 3 * GW])
        g = jnp.tanh(z[:, 3 * GW :])
        c = f * cp + i * g
        h = (o * jnp.tanh(c)).astype(BF16).astype(F32)
        gates[at, :] = jnp.concatenate([i, f, o, g], axis=1)
        cells[at, :] = c
        hiddens[at, :] = h
        return h, c

    return lax.fori_loop(0, count, step, carry)


def lstm_back_steps(first, count, keep, c0, carry, rt, gates, cells, dhs):
    def step(s, carry):
        dh_next, dc_next = carry
        t = first + count - 1 - s
        at = pl.ds(pl.multiple_of(t * 8, 8), 8)
        before = pl.ds(pl.multiple_of(jnp.maximum(t - 1, 0) * 8, 8), 8)
        k = six(keep[at, :])
        saved = gates[at, :]
        i, f, o, g = [saved[:, GW * b : GW * b + GW] for b in range(4)]
        cp = jnp.where(t > 0, cells[before, :], c0[...]) * k
        ct = jnp.tanh(cells[at, :])
        dh = dhs[at, :] + dh_next
        dc = dc_next + dh * o * (1.0 - ct * ct)
        dz = jnp.concatenate(
            [dc * g * i * (1.0 - i), dc * cp * f * (1.0 - f), dh * ct * o * (1.0 - o), dc * i * (1.0 - g * g)], axis=1
        ).astype(BF16)
        gates[at, :] = dz.astype(F32)
        return k * mm(dz, rt[...]), k * dc * f

    return lax.fori_loop(0, count, step, carry)


def output_rows(first, count, h, w, targets, valid, logits, dl, top, part, dh, loss, dh16):
    at_rows = pl.ds(first, count)
    depth = w.shape[0]
    own = pl.ds(0, count)
    top[own, :] = jnp.full((count, LANE), -jnp.inf, F32)

    def forward(at, width):
        z = mm(h[at_rows, pl.ds(0, depth)], w[:, pl.ds(at, width)])
        if isinstance(at, int):
            z = jnp.where(column_mask(at, width, VOCAB, count), z, -jnp.inf)
        logits[own, pl.ds(at, width)] = z
        best = top[own, :]
        for c in range(width // LANE):
            best = jnp.maximum(best, z[:, LANE * c : LANE * c + LANE])
        top[own, :] = best

    each_vocab(forward)
    best = jnp.max(top[own, :], axis=1, keepdims=True)
    part[:, own, :] = jnp.zeros((2, count, LANE), F32)
    wanted = targets[at_rows, :]

    def exponents(at, width):
        z = logits[own, pl.ds(at, width)]
        e = jnp.exp(z - best)
        logits[own, pl.ds(at, width)] = e
        for c in range(width // LANE):
            part[0, own, :] += e[:, LANE * c : LANE * c + LANE]
            hit = lanes(count) + (at + LANE * c) == wanted
            part[1, own, :] += jnp.where(hit, z[:, LANE * c : LANE * c + LANE], 0.0)

    each_vocab(exponents)
    total = jnp.sum(part[0, own, :], axis=1, keepdims=True)
    picked = jnp.sum(part[1, own, :], axis=1, keepdims=True)
    counts = valid[at_rows, :]
    loss[...] += jnp.sum(counts * (best + jnp.log(total) - picked), axis=0, keepdims=True)
    share = counts / total
    dh[own, :] = jnp.zeros((count, depth), F32)

    def backward(at, width):
        e = logits[own, pl.ds(at, width)]
        pieces = []
        for c in range(width // LANE):
            hit = lanes(count) + (at + LANE * c) == wanted
            grad = e[:, LANE * c : LANE * c + LANE] * share - jnp.where(hit, counts, 0.0)
            pieces.append(grad.astype(BF16))
        grad = jnp.concatenate(pieces, axis=1)
        dl[at_rows, pl.ds(at, width)] = grad
        dh[own, :] += mm_nt(grad, w[:, pl.ds(at, width)])

    each_vocab(backward)
    for at, width in fblocks(depth):
        value = dh[own, pl.ds(at, width)]
        dh16[at_rows, pl.ds(at, width)] = jnp.where(column_mask(at, width, HID, count), value, 0.0).astype(BF16)


QUAD = 4
LEFT0 = 35 * LANE
LEFT1 = 14 * LANE
LEFT2 = 11 * LANE
LEFT_ROOM = 41 * LANE


def quad_peer(me, k):
    place = lax.rem(me, QUAD)
    return me - place + lax.rem(place + k, QUAD)


def turn_features(feats, turned):
    n = feats.shape[1]
    zero = jnp.zeros((n, LANE), BF16)
    for segment in range(4):
        start = segment * (FILT + 1)
        shift, first, last = start % LANE, start // LANE, (start + FILT) // LANE
        for c in range(last - first + 1):
            left = feats[segment // 2, :, pl.ds(LANE * (c - 1), LANE)] if c > 0 else zero
            right = feats[segment // 2, :, pl.ds(LANE * c, LANE)] if c < 9 else zero
            tile = turned_tile(left, right, shift)
            at = pl.ds(LANE * (first + c), LANE)
            if c == 0 and segment > 0:
                tile = tile + turned[at, :]
            turned[at, :] = tile


def turn_inputs(x, prevs, depth, turned):
    n = prevs.shape[0]
    first, shift = depth // LANE, depth % LANE
    end = depth + HID
    zero = jnp.zeros((n, LANE), F32)
    lane = lanes(n)
    for c in range(end // LANE + 1):
        if c < first:
            mixed = x[:, pl.ds(LANE * c, LANE)]
        else:
            k = c - first
            left = prevs[:, pl.ds(LANE * (k - 1), LANE)].astype(F32) if 0 < k < 7 else zero
            right = prevs[:, pl.ds(LANE * k, LANE)].astype(F32) if k < 6 else zero
            before = pltpu.roll(left, shift, 1) if k else x[:, pl.ds(LANE * c, LANE)].astype(F32)
            mixed = jnp.where(lane < shift, before, pltpu.roll(right, shift, 1))
            mixed = jnp.where(lane + c * LANE == end, 1.0, mixed).astype(BF16)
        turned[pl.ds(LANE * c, LANE), :] = jnp.transpose(mixed)


SPLIT = 4
AB_PARTS = ((0, 640), (640, 512))


def highway_chunk(rows, slot, dy, feats, pres, grad, dpre, w):
    def cut(m, at, width):
        return pl.ds(m * FW + at, width)

    for at, width in fblocks(FW):
        grad[rows, pl.ds(at, width)] = dy[rows, pl.ds(at, width)].astype(F32)
    for layer in (1, 0):
        own = pl.ds(slot, CHUNK)
        for at, width in fblocks(FW):
            cols = pl.ds(at, width)
            g = grad[rows, cols]
            gate = sigmoid(pres[own, cut(2 * layer, at, width)])
            q = pres[own, cut(2 * layer + 1, at, width)]
            sig = sigmoid(q)
            y = feats[layer, rows, cols].astype(F32)
            dpre[rows, cut(2 * layer, at, width)] = (g * (q * sig - y) * gate * (1.0 - gate)).astype(BF16)
            dpre[rows, cut(2 * layer + 1, at, width)] = (g * gate * sig * (1.0 + q * (1.0 - sig))).astype(BF16)
            grad[rows, cols] = g * (1.0 - gate)
        for half, (row, count) in enumerate(AB_PARTS):
            for at, width in fblocks(count):
                cols = pl.ds(row + at, width)
                value = grad[rows, cols]
                for m in (2 * layer, 2 * layer + 1):
                    part = w[pl.ds(at, width), pl.ds((2 * m + half) * FW, FW)]
                    value = value + mm_nt(dpre[rows, cut(m, 0, FW)], part)
                if row + at + width > FILT:
                    value = jnp.where(column_mask(row + at, width, FILT, CHUNK), value, 0.0)
                grad[rows, cols] = value


def recurrent_call(y2, feats, pres, ab, ur, rt, wt, keep, targets, valid, state):
    n = y2.shape[0]
    chunks = n // CHUNK
    steps = CHUNK // 8
    depth_w = wt.shape[0]
    MESH = pl.DeviceIdType.MESH

    def kernel(
        y2, feats, pres, ab, ur, rt, wt, keep, targets, valid, state,
        grad_o, dpre_o, right_o, xb_o, lhs_o, dz_o, dl_o, x_q, h_q, loss_o, bias_o,
        feats_v, turned, pb, x1, xb, hb, db, ob, dy, u, r, r_t, w, start, gates, cells, prevs, hs, dhs, dz16,
        logits, dl, top, part, dh, loss,
        sem_in, sem_out, send_y, recv_y, send_f, recv_f, send_b, recv_b, send_d, recv_d,
        send_x, recv_x, send_h, recv_h, send_z, recv_z, sem_l, sem_p,
    ):
        role = lax.axis_index("section")
        me = lax.axis_index("dp")
        loss[...] = jnp.zeros_like(loss)
        bias_o[...] = jnp.zeros_like(bias_o)

        def to(step, source, target, send, recv):
            return pltpu.make_async_remote_copy(
                source, target, send, recv, device_id={"section": role + step}, device_id_type=MESH
            )

        def span(c):
            return pl.ds(pl.multiple_of(c * CHUNK, CHUNK), CHUNK)

        def forward_copy(c, step):
            return to(step, hb.at[span(c)], xb.at[span(c)], send_f.at[c], recv_f.at[c])

        def backward_copy(c, step):
            return to(step, ob.at[span(c)], db.at[span(c)], send_b.at[c], recv_b.at[c])

        def feature_copy(step):
            return to(step, y2, x1, send_y.at[0], recv_y.at[0])

        def last_copy(c, step):
            return to(step, dy.at[span(c)], dy.at[span(c)], send_d.at[c], recv_d.at[c])

        def quad_copy(source, target, send, recv, k):
            return pltpu.make_async_remote_copy(
                source, target, send, recv, device_id={"dp": quad_peer(me, k)}, device_id_type=MESH
            )

        def input_copy(k):
            return quad_copy(x1, x_q.at[k - 1, 0], send_x.at[k - 1, 0], recv_x.at[k - 1, 0], k)

        def layer_copy(c, k):
            target = x_q.at[k - 1, 0, span(c), pl.ds(0, GW)]
            return quad_copy(xb.at[span(c)], target, send_x.at[k - 1, c], recv_x.at[k - 1, c], k)

        def feats_copy(k):
            return quad_copy(feats_v, x_q.at[k - 1], send_x.at[k - 1, 0], recv_x.at[k - 1, 0], k)

        def hidden_copy(c, k):
            return quad_copy(pb.at[span(c)], h_q.at[k - 1, span(c)], send_h.at[k - 1, c], recv_h.at[k - 1, c], k)

        def each_peer(body):
            for k in range(1, QUAD):
                body(k)

        def each_chunk(body, first=0):
            def step(c, carry):
                body(c)
                return carry

            lax.fori_loop(first, chunks, step, 0)

        def turned_out(g, rows):
            copy = pltpu.make_async_copy(turned.at[pl.ds(0, rows)], lhs_o.at[g, pl.ds(0, rows)], sem_l.at[0])
            copy.start()
            copy.wait()

        def fetch(source, target):
            copy = pltpu.make_async_copy(source, target, sem_l.at[1])
            copy.start()
            copy.wait()

        def dpre_copy(c, k):
            rows = pl.ds(pl.multiple_of((c - SPLIT) * CHUNK, CHUNK), CHUNK)
            return quad_copy(
                dl.at[span(c), pl.ds(0, 4 * FW)], right_o.at[k - 1, rows], send_z.at[k - 1, c], recv_z.at[k - 1, c], k
            )

        def right_copy(k, c):
            return pltpu.make_async_remote_copy(
                dz16.at[span(c)], dz_o.at[k - 1, span(c)], send_z.at[k - 1, c], recv_z.at[k - 1, c],
                device_id={"dp": quad_peer(me, k)}, device_id_type=MESH,
            )

        def inputs(which):
            if which == 0:
                pairs = [(feats, feats_v)]
                for m in range(4):
                    for half, (row, count) in enumerate(AB_PARTS):
                        target = w.at[pl.ds(0, count), pl.ds((2 * m + half) * FW, FW)]
                        pairs.append((ab.at[m, pl.ds(row, count)], target))
            elif which == 3:
                pairs = [(wt, w)]
            else:
                depth = FW if which == 1 else GW
                pairs = [
                    (ur.at[pl.ds(0, depth)], u.at[pl.ds(0, depth)]),
                    (ur.at[pl.ds(FW, GW)], r),
                    (rt, r_t),
                    (state.at[which - 1], start),
                ]
            return [pltpu.make_async_copy(a, b, sem_in.at[i]) for i, (a, b) in enumerate(pairs)]

        for which in range(4):

            @pl.when(role == which)
            def _(which=which):
                for copy in inputs(which):
                    copy.start()

        barrier = pltpu.get_barrier_semaphore()

        @pl.when(role > 0)
        def _():
            pl.semaphore_signal(barrier, inc=1, device_id={"section": role - 1}, device_id_type=MESH)

        @pl.when(role < 3)
        def _():
            pl.semaphore_signal(barrier, inc=1, device_id={"section": role + 1}, device_id_type=MESH)

        for k in range(1, QUAD):
            pl.semaphore_signal(barrier, inc=1, device_id={"dp": quad_peer(me, k)}, device_id_type=MESH)
        pl.semaphore_wait(barrier, lax.min(role, 1) + lax.min(3 - role, 1) + QUAD - 1)

        @pl.when(role == 0)
        def _():
            feature_copy(1).start()
            for copy in inputs(0):
                copy.wait()
            each_peer(lambda k: feats_copy(k).start())
            turn_features(feats_v, turned)
            turned_out(QUAD - 1, LEFT0)
            feature_copy(1).wait_send()
            each_peer(lambda k: feats_copy(k).wait_send())
            for k in range(1, QUAD):
                feats_copy(k).wait_recv()
                fetch(x_q.at[k - 1], feats_v)
                turn_features(feats_v, turned)
                turned_out(k - 1, LEFT0)
            fetch(feats, feats_v)

            def pres_copy(c, m):
                slot = lax.rem(c, 2)
                target = logits.at[pl.ds(pl.multiple_of(slot * CHUNK, CHUNK), CHUNK), pl.ds(m * FW, FW)]
                return pltpu.make_async_copy(pres.at[m, span(c)], target, sem_p.at[slot, m])

            for m in range(4):
                pres_copy(chunks - 1, m).start()

            def chunk(i, carry):
                c = chunks - 1 - i

                @pl.when(c > 0)
                def _():
                    for m in range(4):
                        pres_copy(c - 1, m).start()

                for m in range(4):
                    pres_copy(c, m).wait()
                last_copy(c, 1).wait_recv()
                highway_chunk(span(c), pl.multiple_of(lax.rem(c, 2) * CHUNK, CHUNK), dy, feats_v, logits, gates, dl, w)

                @pl.when(c >= SPLIT)
                def _():
                    each_peer(lambda k: dpre_copy(c, k).start())

                return carry

            lax.fori_loop(0, chunks, chunk, 0)
            copies = [
                pltpu.make_async_copy(gates.at[:, pl.ds(0, FW)], grad_o, sem_out.at[0]),
                pltpu.make_async_copy(dl.at[:, pl.ds(0, 4 * FW)], dpre_o, sem_out.at[1]),
            ]
            for copy in copies:
                copy.start()
            for at, width in fblocks(FW):
                cols = pl.ds(at, width)
                bias_o[:, cols] = jnp.sum(dl[:, cols].astype(F32), axis=0, keepdims=True)
            for copy in copies:
                copy.wait()

            def settle(c):
                for k in range(1, QUAD):
                    dpre_copy(c, k).wait_send()
                    dpre_copy(c, k).wait_recv()

            each_chunk(settle, SPLIT)

        @pl.when((role == 1) | (role == 2))
        def _():
            for which in (1, 2):

                @pl.when(role == which)
                def _(which=which):
                    for copy in inputs(which):
                        copy.wait()

            bias = r[pl.ds(HID, 1), :].astype(F32)

            @pl.when(role == 1)
            def _():
                feature_copy(-1).wait_recv()
                each_peer(lambda k: input_copy(k).start())
                for at, width in fblocks(ZW):
                    cols = pl.ds(at, width)
                    gates[:, cols] = mm(x1[...], u[:, cols]) + bias[:, at : at + width]

            def chunk_forward(c, carry):
                @pl.when(role == 2)
                def _():
                    forward_copy(c, -1).wait_recv()
                    each_peer(lambda k: layer_copy(c, k).start())
                    for at, width in fblocks(ZW):
                        cols = pl.ds(at, width)
                        gates[span(c), cols] = mm(xb[span(c), :], u[pl.ds(0, GW), cols]) + bias[:, at : at + width]

                carry = lstm_steps(c * steps, steps, keep, carry, r, gates, cells, prevs, hs)
                hb[span(c), :] = hs[span(c), :].astype(BF16)
                forward_copy(c, 1).start()
                pb[span(c), :] = prevs[span(c), :].astype(BF16)
                each_peer(lambda k: hidden_copy(c, k).start())
                return carry

            h0 = start[0].astype(BF16).astype(F32)
            lax.fori_loop(0, chunks, chunk_forward, (h0, start[1]))

            for which in (1, 2):

                @pl.when(role == which)
                def _(which=which):
                    depth, rows = (FILT, LEFT1) if which == 1 else (HID, LEFT2)
                    width = FW if which == 1 else GW
                    turn_inputs(x1 if which == 1 else xb, pb, depth, turned)
                    turned_out(QUAD - 1, rows)
                    if which == 1:
                        each_peer(lambda k: input_copy(k).wait_send())
                        each_peer(lambda k: input_copy(k).wait_recv())
                    else:

                        def moved(c):
                            for k in range(1, QUAD):
                                layer_copy(c, k).wait_send()
                                layer_copy(c, k).wait_recv()

                        each_chunk(moved)

                    def hidden_moved(c):
                        for k in range(1, QUAD):
                            hidden_copy(c, k).wait_send()
                            hidden_copy(c, k).wait_recv()

                    each_chunk(hidden_moved)
                    for g in range(QUAD - 1):
                        fetch(x_q.at[g, 0, :, pl.ds(0, width)], feats_v.at[0, :, pl.ds(0, width)])
                        fetch(h_q.at[g], pb)
                        turn_inputs(feats_v.at[0], pb, depth, turned)
                        turned_out(g, rows)

            def chunk_backward(i, carry):
                c = chunks - 1 - i
                backward_copy(c, 1).wait_recv()
                dhs[span(c), :] = db[span(c), :].astype(F32)
                carry = lstm_back_steps(c * steps, steps, keep, start.at[1], carry, r_t, gates, cells, dhs)
                dz16[span(c), :] = gates[span(c), :].astype(BF16)

                @pl.when(role == 1)
                def _():
                    for at, width in fblocks(FW):
                        value = mm_nt(dz16[span(c), :], u[pl.ds(at, width), :])
                        if at + width > FILT:
                            value = jnp.where(column_mask(at, width, FILT, CHUNK), value, 0.0)
                        dy[span(c), pl.ds(at, width)] = value.astype(BF16)
                    last_copy(c, -1).start()

                @pl.when(role == 2)
                def _():
                    for at, width in fblocks(GW):
                        value = mm_nt(dz16[span(c), :], u[pl.ds(at, width), :])
                        if at + width > HID:
                            value = jnp.where(column_mask(at, width, HID, CHUNK), value, 0.0)
                        ob[span(c), pl.ds(at, width)] = value.astype(BF16)
                    backward_copy(c, -1).start()

                each_peer(lambda k: right_copy(k, c).start())
                return carry

            zero = jnp.zeros((8, GW), F32)
            lax.fori_loop(0, chunks, chunk_backward, (zero, zero))

            own_right = pltpu.make_async_copy(dz16, dz_o.at[QUAD - 1], sem_out.at[1])
            own_right.start()

            @pl.when(role == 1)
            def _():
                each_chunk(lambda c: last_copy(c, -1).wait_send())

            @pl.when(role == 2)
            def _():
                each_chunk(lambda c: backward_copy(c, -1).wait_send())

            own_right.wait()

            def sent(c, carry):
                forward_copy(c, 1).wait_send()
                for k in range(1, QUAD):
                    right_copy(k, c).wait_send()
                    right_copy(k, c).wait_recv()
                return carry

            lax.fori_loop(0, chunks, sent, 0)

        @pl.when(role == 3)
        def _():
            for copy in inputs(3):
                copy.wait()
            ob[...] = jnp.zeros_like(ob)
            done = 0
            for count in GROUPS_OUT:
                rows = pl.ds(done * CHUNK, count * CHUNK)
                for c in range(done, done + count):
                    forward_copy(c, -1).wait_recv()
                value = xb[rows, pl.ds(5 * LANE, LANE)].astype(F32)
                value = jnp.where(lanes(count * CHUNK) + 5 * LANE == HID, 1.0, value)
                xb[rows, pl.ds(5 * LANE, LANE)] = value.astype(BF16)
                output_rows(
                    done * CHUNK, count * CHUNK, xb, w, targets, valid, logits, dl, top, part, dh, loss, ob
                )
                for c in range(done, done + count):
                    backward_copy(c, -1).start()
                done += count
            copies = [
                pltpu.make_async_copy(xb, xb_o, sem_out.at[0]),
                pltpu.make_async_copy(dl, dl_o, sem_out.at[1]),
            ]
            for copy in copies:
                copy.start()
            for c in range(chunks):
                backward_copy(c, -1).wait_send()
            for copy in copies:
                copy.wait()

        loss_o[...] = loss[...]

    most = max(GROUPS_OUT) * CHUNK
    sems = pltpu.SemaphoreType.DMA
    outs = [
        ((n, FW), F32), ((n, 4 * FW), BF16), ((QUAD - 1, n - SPLIT * CHUNK, 4 * FW), BF16), ((n, GW), BF16),
        ((QUAD, LEFT_ROOM, n), BF16), ((QUAD, n, ZW), BF16), ((n, VW), BF16), ((QUAD - 1, 2, n, FW), BF16),
        ((QUAD - 1, n, GW), BF16),
    ]
    scratch = [
        vmem((2, n, FW), BF16), vmem((LEFT0, n), BF16), vmem((n, GW), BF16),
        vmem((n, FW), BF16), vmem((n, GW), BF16), vmem((n, GW), BF16), vmem((n, GW), BF16), vmem((n, GW), BF16),
        vmem((n, FW), BF16), vmem((FW, ZW), BF16), vmem((GW, ZW), BF16), vmem((ZW, GW), BF16), vmem(wt.shape, BF16),
        vmem((2, 8, GW), F32), vmem((n, ZW), F32), vmem((n, GW), F32), vmem((n, GW), F32), vmem((n, GW), F32),
        vmem((n, GW), F32), vmem((n, ZW), BF16),
        vmem((most, VW), F32), vmem((n, VW), BF16), vmem((most, LANE), F32), vmem((2, most, LANE), F32),
        vmem((most, depth_w), F32), vmem((1, LANE), F32),
        dmas(9), dmas(3), dmas(1), dmas(1), dmas(chunks), dmas(chunks), dmas(chunks), dmas(chunks), dmas(chunks), dmas(chunks),
        sems((QUAD - 1, chunks)), sems((QUAD - 1, chunks)), sems((QUAD - 1, chunks)), sems((QUAD - 1, chunks)),
        sems((QUAD - 1, chunks)), sems((QUAD - 1, chunks)), dmas(2), sems((2, 4)),
    ]
    return pl.pallas_call(
        kernel,
        out_shape=[jax.ShapeDtypeStruct(shape, dtype) for shape, dtype in outs]
        + [jax.ShapeDtypeStruct((1, LANE), F32), jax.ShapeDtypeStruct((1, FW), F32)],
        in_specs=[ANYWHERE] * 7 + [ON_CHIP] * 3 + [ANYWHERE],
        out_specs=[ANYWHERE] * 9 + [ON_CHIP] * 2,
        scratch_shapes=scratch,
        compiler_params=pltpu.CompilerParams(vmem_limit_bytes=62 << 20, collective_id=3, has_side_effects=True),
        name="recurrent",
    )(y2, feats, pres, ab, ur, rt, wt, keep, targets, valid, state)


FORM = (
    (FILT, 9, 4 * (FILT + 1), CONV_END, CONV_TILES, 32),
    (4 * HID, 24, FILT + HID + 1, 0, 0, 16),
    (4 * HID, 24, 2 * HID + 1, 0, 0, 16),
    (VOCAB, 79, HID + 1, 0, 0, 16),
)


def slab(role, dest, share):
    width, pitch, rows, before, lead, period = FORM[role]
    low = lax.max if not isinstance(dest, int) else max
    high = lax.min if not isinstance(dest, int) else min
    one = (lambda v: v) if isinstance(dest, int) else jnp.int32
    start = low(one(share) * dest - before, one(0))
    first = start // width // period * period
    end = high((share * (dest + 1) - before + width - 1) // width, one(rows))
    count = low((end - first + 15) // 16, one(0)) * pitch
    tile = lead + first // 16 * pitch
    if lead:
        if isinstance(dest, int):
            if dest == 0:
                tile, count = 0, count + lead
        else:
            head = lax.max(1 - dest, 0)
            tile = tile - lead * head
            count = count + lead * head
    return first, tile, count


def slab_pieces(count, size):
    return (count + size - 1) // size


def gather_sum_call(tiles, groups, share):
    pair = 2
    across = groups // pair
    size = 64 if across <= 4 else 32
    pieces = max(slab_pieces(slab(3, dest, share)[2], size) for dest in range(groups))
    room = pieces * size
    line = across <= 4
    slots = across + 1 if line else across - 1
    MESH = pl.DeviceIdType.MESH

    def kernel(
        tiles, out, own, got1, got2, acc, own_sem, send1, recv1, send2, recv2, out_sem,
    ):
        role = lax.axis_index("section")
        me = lax.axis_index("dp")
        mine, side = me // pair, lax.rem(me, pair)
        other = mine * pair + (1 - side)

        def at_place(place):
            return {"dp": place * pair + side}

        def part(ref, slot, p):
            return ref.at[slot, pl.ds(pl.multiple_of(p * size, size), size)]

        def span(p):
            return pl.ds(pl.multiple_of(p * size, size), size)

        def loop(count, body):
            def step(p, carry):
                body(p)
                return carry

            lax.fori_loop(0, count, step, 0)

        def run(shape_of):
            def count_to(place, which):
                return shape_of(place * pair + which)[1]

            def own_copy(place, p):
                tile, _ = shape_of(place * pair + side)
                return pltpu.make_async_copy(
                    tiles.at[pl.ds(tile + p * size, size)], part(own, place, p), own_sem.at[place, p]
                )

            def first_copy(place, p):
                tile, _ = shape_of(place * pair + 1 - side)
                return pltpu.make_async_remote_copy(
                    tiles.at[pl.ds(tile + p * size, size)], part(got1, place, p), send1.at[place, p], recv1.at[place, p],
                    device_id={"dp": other}, device_id_type=MESH,
                )

            def begin(place):
                loop(count_to(place, 1 - side), lambda p: first_copy(place, p).start())
                loop(count_to(place, side), lambda p: own_copy(place, p).start())

            def hop_copy(place, up, p):
                if line:
                    target = mine + 1 if up else mine - 1
                    slot = jnp.where(place == mine + 1, across, place) if up else place
                else:
                    target = place
                    slot = lax.rem(place - mine + across, across) - 1
                return pltpu.make_async_remote_copy(
                    part(own, place, p), part(got2, slot, p), send2.at[place, p], recv2.at[slot, p],
                    device_id=at_place(target), device_id_type=MESH,
                )

            def arrived(slot, p):
                return pltpu.make_async_remote_copy(
                    part(own, 0, p), part(got2, slot, p), send2.at[0, p], recv2.at[slot, p],
                    device_id=at_place(lax.rem(mine + 1, across)), device_id_type=MESH,
                )

            def forward(place, up, has_before):
                def body(p):
                    own_copy(place, p).wait()
                    first_copy(place, p).wait_recv()
                    at = span(p)
                    own[place, at] = (own[place, at].astype(F32) + got1[place, at].astype(F32)).astype(BF16)
                    hop_copy(place, up, p).start()

                def body_sum(p):
                    own_copy(place, p).wait()
                    first_copy(place, p).wait_recv()
                    arrived(place, p).wait_recv()
                    at = span(p)
                    total = own[place, at].astype(F32) + got1[place, at].astype(F32) + got2[place, at].astype(F32)
                    own[place, at] = total.astype(BF16)
                    hop_copy(place, up, p).start()

                count = count_to(place, side)
                if not line:
                    loop(count, body)
                    return

                @pl.when(has_before)
                def _():
                    loop(count, body_sum)

                @pl.when(jnp.logical_not(has_before))
                def _():
                    loop(count, body)

            if line:
                for k in range(across - 1):

                    @pl.when(k < mine)
                    def _(k=k):
                        begin(k)

                    @pl.when(k < across - 1 - mine)
                    def _(k=k):
                        begin(across - 1 - k)

                begin(mine)
                for k in range(across - 1):

                    @pl.when(k < mine)
                    def _(k=k):
                        forward(k, False, mine < across - 1)

                    @pl.when(k < across - 1 - mine)
                    def _(k=k):
                        forward(across - 1 - k, True, mine > 0)

            else:
                for k in range(1, across):
                    begin(lax.rem(mine + k, across))
                begin(mine)
                for k in range(1, across):
                    forward(lax.rem(mine + k, across), True, None)

            def settle(p):
                own_copy(mine, p).wait()
                first_copy(mine, p).wait_recv()
                at = span(p)
                acc[at] = own[mine, at].astype(F32) + got1[mine, at].astype(F32)

            def add(slot):
                def body(p):
                    arrived(slot, p).wait_recv()
                    at = span(p)
                    acc[at] += got2[slot, at].astype(F32)

                return body

            mine_count = count_to(mine, side)
            loop(mine_count, settle)
            if line:

                @pl.when(mine < across - 1)
                def _():
                    loop(mine_count, add(mine))

                @pl.when(mine > 0)
                def _():
                    loop(mine_count, add(across))

            else:
                for k in range(1, across):
                    loop(mine_count, add(k - 1))

            def out_copy(p):
                return pltpu.make_async_copy(acc.at[span(p)], out.at[span(p)], out_sem.at[p])

            loop(mine_count, lambda p: out_copy(p).start())
            loop(mine_count, lambda p: out_copy(p).wait())
            for place in range(across):
                loop(count_to(place, 1 - side), lambda p, place=place: first_copy(place, p).wait_send())

                @pl.when(place != mine)
                def _(place=place):
                    loop(count_to(place, side), lambda p: hop_copy(place, True, p).wait_send())

        def shape_of(dest):
            _, tile, count = slab(3, dest, share)
            return tile, slab_pieces(count, size)

        @pl.when(role == 3)
        def _():
            barrier = pltpu.get_barrier_semaphore()
            pl.semaphore_signal(barrier, inc=1, device_id={"dp": other}, device_id_type=MESH)
            for k in range(1, across):
                peer = at_place(lax.rem(mine + k, across))
                pl.semaphore_signal(barrier, inc=1, device_id=peer, device_id_type=MESH)
            pl.semaphore_wait(barrier, across)
            run(shape_of)

    sems = pltpu.SemaphoreType.DMA
    return pl.pallas_call(
        kernel,
        out_shape=jax.ShapeDtypeStruct((room, 16, LANE), F32),
        in_specs=[ANYWHERE],
        out_specs=ANYWHERE,
        scratch_shapes=[
            vmem((across, room, 16, LANE), BF16), vmem((across, room, 16, LANE), BF16),
            vmem((slots, room, 16, LANE), BF16), vmem((room, 16, LANE), F32),
            sems((across, pieces)), sems((across, pieces)), sems((across, pieces)),
            sems((across, pieces)), sems((slots, pieces)), sems((pieces,)),
        ],
        compiler_params=pltpu.CompilerParams(vmem_limit_bytes=62 << 20, collective_id=1, has_side_effects=True),
        name="gather_sum",
    )(tiles)


BLOCK_ROWS = (25, 11, 11)


def finish_call(lhs, dz, dpre, rights, conv, bias, loss, after, groups, share):
    n = lhs.shape[2]
    quads = groups // QUAD
    MESH = pl.DeviceIdType.MESH

    def most_blocks(role):
        width = FORM[role][1]
        lead = FORM[role][4]
        most = 0
        for dest in range(groups):
            count = slab(role, dest, share)[2]
            if lead and dest == 0:
                count -= lead
            most = max(most, -(-(count // width) // BLOCK_ROWS[role]))
        return most

    blocks = [most_blocks(role) for role in range(3)]
    room = max(
        FORM[role][4] + blocks[role] * BLOCK_ROWS[role] * FORM[role][1] for role in range(3)
    )
    left_rows = max(blocks[role] * BLOCK_ROWS[role] * 16 for role in range(3))
    most = max(blocks)

    def kernel(
        lhs, dz, dpre, late, early, conv, bias, loss, after, out, small_out,
        left, dpre_v, sent, got, acc, convs, lead_sum, small, got_small,
        sem_left, sem_right, send, recv, send_c, recv_c, small_send, small_recv, sem_out,
    ):
        role = lax.axis_index("section")
        me = lax.axis_index("dp")
        place, quad = lax.rem(me, QUAD), me // QUAD

        def across_peer(k):
            return {"dp": place + QUAD * lax.rem(quad + k, quads)}

        barrier = pltpu.get_barrier_semaphore()
        for k in range(1, QUAD):
            pl.semaphore_signal(barrier, inc=1, device_id={"dp": quad_peer(me, k)}, device_id_type=MESH)
        for k in range(1, quads):
            pl.semaphore_signal(barrier, inc=1, device_id=across_peer(k), device_id_type=MESH)

        def right_load(b):
            return pltpu.make_async_copy(
                dz.at[:, :, pl.ds(GW * b, GW)], dpre_v.at[:, b, :, pl.ds(0, GW)], sem_right.at[b]
            )

        def right_loads0():
            copies = []
            cut = SPLIT * CHUNK
            for b in range(4):
                cols = pl.ds(FW * b, FW)
                pairs = [
                    (early.at[:, :, cols], dpre_v.at[pl.ds(0, QUAD - 1), b, pl.ds(0, cut)]),
                    (late.at[:, :, cols], dpre_v.at[pl.ds(0, QUAD - 1), b, pl.ds(cut, n - cut)]),
                    (dpre.at[:, cols], dpre_v.at[QUAD - 1, b]),
                ]
                copies += [pltpu.make_async_copy(x, y, sem_right.at[4 + 3 * b + i]) for i, (x, y) in enumerate(pairs)]
            return copies

        def conv_load():
            return pltpu.make_async_copy(conv, convs.at[QUAD - 1], sem_right.at[16])

        @pl.when(role == 0)
        def _():
            for copy in right_loads0():
                copy.start()
            conv_load().start()

        @pl.when((role == 1) | (role == 2))
        def _():
            for b in range(4):
                right_load(b).start()

        pl.semaphore_wait(barrier, QUAD - 1 + quads - 1)

        small[...] = jnp.zeros_like(small)

        @pl.when(role == 0)
        def _():
            small[0, :, pl.ds(0, FW)] = bias[...]

        @pl.when(role == 3)
        def _():
            small[0, :, pl.ds(FW, LANE)] = loss[...]

        def small_copy(k):
            if k < QUAD:
                source, target = small.at[0], {"dp": quad_peer(me, k)}
            else:
                source, target = small.at[1], across_peer(k - QUAD + 1)
            return pltpu.make_async_remote_copy(
                source, got_small.at[k - 1], small_send.at[k - 1], small_recv.at[k - 1],
                device_id=target, device_id_type=MESH,
            )

        for k in range(1, QUAD):
            small_copy(k).start()

        def conv_copy(slot, target):
            return pltpu.make_async_remote_copy(
                conv, convs.at[slot], send_c.at[slot], recv_c.at[slot], device_id={"dp": target}, device_id_type=MESH
            )

        def run(which):
            width, pitch, rows, _, lead, _ = FORM[which]
            size = BLOCK_ROWS[which]
            block_tiles = size * pitch

            def geometry(k):
                dest = place + QUAD * lax.rem(quad + k, quads)
                first, _, count = slab(which, dest, share)
                if lead:
                    head = lax.max(1 - dest, 0)
                    count = count - lead * head
                else:
                    head = 0
                return first, (count // pitch + size - 1) // size, head

            def left_copy(k):
                height = blocks[which] * size * 16
                first = lax.min(geometry(k)[0], LEFT_ROOM - height)
                span = pl.ds(pl.multiple_of(first, 16), height)
                return pltpu.make_async_copy(
                    lhs.at[:, span], left.at[lax.rem(k, 2), :, pl.ds(0, blocks[which] * size * 16)], sem_left.at[lax.rem(k, 2)]
                )

            def block_copy(k, b):
                span = pl.ds(CONV_TILES + b * block_tiles, block_tiles)
                return pltpu.make_async_remote_copy(
                    sent.at[k - 1, span], got.at[k - 1, span], send.at[k - 1, b], recv.at[k - 1, b],
                    device_id=across_peer(k), device_id_type=MESH,
                )

            def lead_copy(k):
                span = pl.ds(0, CONV_TILES)
                return pltpu.make_async_remote_copy(
                    sent.at[k - 1, span], got.at[k - 1, span], send.at[k - 1, most], recv.at[k - 1, most],
                    device_id=across_peer(k), device_id_type=MESH,
                )

            def put(k, own, at, value):
                if own:
                    acc[at] = value
                else:
                    sent[k - 1, at] = value.astype(BF16)

            def block(k, own, b, first):
                here = pl.ds(pl.multiple_of(b * size * 16, 16), size * 16)
                base = CONV_TILES + b * block_tiles
                if which == 0:
                    row = lax.broadcasted_iota(jnp.int32, (size * 16, n), 0) + first + b * size * 16
                    start = first + b * size * 16
                    low = lax.min(start // (FILT + 1), 3)
                    high = lax.min((start + size * 16 - 1) // (FILT + 1), 3)
                    edge = (FILT + 1) * (low + 1)
                    lefts = [left[lax.rem(k, 2), g, here, :] for g in range(QUAD)]
                    near = [jnp.where(row < edge, x, jnp.zeros_like(x)) for x in lefts]
                    for col, wide in fblocks(FW):
                        value = jnp.zeros((size * 16, wide), F32)
                        for g in range(QUAD):
                            value = value + mm(near[g], dpre_v[g, low, :, pl.ds(col, wide)])
                        for r in range(size):
                            for c in range(wide // LANE):
                                tile = value[16 * r : 16 * r + 16, LANE * c : LANE * c + LANE]
                                put(k, own, base + r * pitch + col // LANE + c, tile)

                    @pl.when(high > low)
                    def _():
                        far = [jnp.where(row < edge, jnp.zeros_like(x), x) for x in lefts]
                        for col, wide in fblocks(FW):
                            value = jnp.zeros((size * 16, wide), F32)
                            for g in range(QUAD):
                                value = value + mm(far[g], dpre_v[g, high, :, pl.ds(col, wide)])
                            for r in range(size):
                                for c in range(wide // LANE):
                                    tile = value[16 * r : 16 * r + 16, LANE * c : LANE * c + LANE]
                                    at = base + r * pitch + col // LANE + c
                                    old = acc[at] if own else sent[k - 1, at].astype(F32)
                                    put(k, own, at, old + tile)

                else:
                    for col, wide in fblocks(ZW):
                        value = jnp.zeros((size * 16, wide), F32)
                        for g in range(QUAD):
                            value = value + mm(left[lax.rem(k, 2), g, here, :], dpre_v[g, col // GW, :, pl.ds(col % GW, wide)])
                        for r in range(size):
                            for c in range(wide // LANE):
                                tile = value[16 * r : 16 * r + 16, LANE * c : LANE * c + LANE]
                                put(k, own, base + r * pitch + col // LANE + c, tile)

            def loop(count, body):
                def step(b, carry):
                    body(b)
                    return carry

                lax.fori_loop(0, count, step, 0)

            left_copy(jnp.int32(1 % quads)).start()
            if which == 0:

                @pl.when(place > 0)
                def _():
                    for k in range(1, QUAD):

                        @pl.when(place == k)
                        def _(k=k):
                            conv_copy(k - 1, me - k).start()

                for copy in right_loads0():
                    copy.wait()
                conv_load().wait()
            else:
                for b in range(4):
                    right_load(b).wait()

            if which == 0:

                @pl.when(place == 0)
                def _():
                    for k in range(1, QUAD):
                        conv_copy(k - 1, me + k).wait_recv()
                    total = convs[0].astype(F32)
                    for k in range(1, QUAD):
                        total = total + convs[k].astype(F32)
                    lead_sum[...] = total

            def slab_of(k, own):
                left_copy(k).wait()
                if not own:
                    left_copy(lax.rem(k + 1, quads)).start()
                first, count, head = geometry(k)
                if which == 0:

                    @pl.when(head > 0)
                    def _():
                        if own:
                            acc[pl.ds(0, CONV_TILES)] = lead_sum[...]
                        else:
                            sent[k - 1, pl.ds(0, CONV_TILES)] = lead_sum[...].astype(BF16)
                            lead_copy(k).start()

                def work(b):
                    block(k, own, b, first)
                    if not own:
                        block_copy(k, b).start()

                loop(count, work)

            def others(body):
                def step(k, carry):
                    body(k)
                    return carry

                lax.fori_loop(1, quads, step, 0)

            others(lambda k: slab_of(k, False))
            slab_of(jnp.int32(0), True)

            _, mine, head = geometry(0)
            def join(k):
                def add(b):
                    block_copy(k, b).wait_recv()
                    span = pl.ds(CONV_TILES + b * block_tiles, block_tiles)
                    acc[span] += got[k - 1, span].astype(F32)

                loop(mine, add)
                if which == 0:

                    @pl.when(head > 0)
                    def _():
                        lead_copy(k).wait_recv()
                        span = pl.ds(0, CONV_TILES)
                        acc[span] += got[k - 1, span].astype(F32)

            others(join)

            span = blocks[which] * block_tiles
            if which == 0:

                @pl.when(head > 0)
                def _():
                    copy = pltpu.make_async_copy(
                        acc.at[pl.ds(0, CONV_TILES + span)], out.at[pl.ds(0, CONV_TILES + span)], sem_out.at[0]
                    )
                    copy.start()
                    copy.wait()

                @pl.when(head == 0)
                def _():
                    copy = pltpu.make_async_copy(acc.at[pl.ds(CONV_TILES, span)], out.at[pl.ds(0, span)], sem_out.at[0])
                    copy.start()
                    copy.wait()

            else:
                copy = pltpu.make_async_copy(acc.at[pl.ds(CONV_TILES, span)], out.at[pl.ds(0, span)], sem_out.at[0])
                copy.start()
                copy.wait()

            def sent_all(k):
                _, count, head = geometry(k)
                loop(count, lambda b: block_copy(k, b).wait_send())
                if which == 0:

                    @pl.when(head > 0)
                    def _():
                        lead_copy(k).wait_send()

            others(sent_all)

            if which == 0:
                for k in range(1, QUAD):

                    @pl.when(place == k)
                    def _(k=k):
                        conv_copy(k - 1, me - k).wait_send()

        for k in range(1, QUAD):
            small_copy(k).wait_recv()
        small[1] = small[0] + got_small[0] + got_small[1] + got_small[2]
        for k in range(QUAD, QUAD + quads - 1):
            small_copy(k).start()

        for which in range(3):

            @pl.when(role == which)
            def _(which=which):
                run(which)

        total = small[1]
        for k in range(QUAD, QUAD + quads - 1):
            small_copy(k).wait_recv()
            total = total + got_small[k - 1]
        small_out[...] = total
        for k in range(1, QUAD + quads - 1):
            small_copy(k).wait_send()

    sems = pltpu.SemaphoreType.DMA
    full = CONV_TILES + max(blocks[role] * BLOCK_ROWS[role] * FORM[role][1] for role in range(3))
    smalls = QUAD + quads - 2
    return pl.pallas_call(
        kernel,
        out_shape=[jax.ShapeDtypeStruct((full, 16, LANE), F32), jax.ShapeDtypeStruct((1, FW + LANE), F32)],
        in_specs=[ANYWHERE] * 6 + [ON_CHIP] * 2 + [ANYWHERE],
        out_specs=[ANYWHERE, ON_CHIP],
        scratch_shapes=[
            vmem((2, QUAD, left_rows, n), BF16), vmem((QUAD, 4, n, FW), BF16),
            vmem((quads - 1, full, 16, LANE), BF16), vmem((quads - 1, full, 16, LANE), BF16),
            vmem((full, 16, LANE), F32), vmem((QUAD, CONV_TILES, 16, LANE), BF16), vmem((CONV_TILES, 16, LANE), F32),
            vmem((2, 1, FW + LANE), F32), vmem((smalls, 1, FW + LANE), F32),
            sems((2,)), sems((17,)), sems((quads - 1, most + 1)), sems((quads - 1, most + 1)),
            sems((QUAD - 1,)), sems((QUAD - 1,)), sems((smalls,)), sems((smalls,)), sems((1,)),
        ],
        compiler_params=pltpu.CompilerParams(vmem_limit_bytes=62 << 20, collective_id=5, has_side_effects=True),
        name="finish",
    )(lhs, dz, dpre, *rights, conv, bias, loss, after)


def sections_sum_call(small):
    count = lax.axis_size("section")

    def kernel(mine, out, held, send, recv):
        me = lax.axis_index("section")
        barrier = pltpu.get_barrier_semaphore()

        def peer(k):
            return {"section": lax.rem(me + k, count)}

        for k in range(1, count):
            pl.semaphore_signal(barrier, inc=1, device_id=peer(k), device_id_type=pl.DeviceIdType.MESH)
        pl.semaphore_wait(barrier, count - 1)
        copies = [
            pltpu.make_async_remote_copy(
                mine, held.at[k], send.at[k], recv.at[k], device_id=peer(k), device_id_type=pl.DeviceIdType.MESH
            )
            for k in range(1, count)
        ]
        for copy in copies:
            copy.start()
        total = mine[...]
        for k, copy in enumerate(copies):
            copy.wait_recv()
            total = total + held[k + 1]
        out[...] = total
        for copy in copies:
            copy.wait_send()

    return pl.pallas_call(
        kernel,
        out_shape=jax.ShapeDtypeStruct(small.shape, F32),
        in_specs=[ON_CHIP],
        out_specs=ON_CHIP,
        scratch_shapes=[vmem((count,) + small.shape, F32), dmas(count), dmas(count)],
        compiler_params=pltpu.CompilerParams(collective_id=2, has_side_effects=True),
        name="sections_sum",
    )(small)


def pack_call(summed, summed3, groups, share):
    rooms = (summed.shape[0] * 16, summed3.shape[0] * 16)
    chunks = share // LANE
    margin = 1280
    slab_rows = 10624
    flat_rows = margin + max(10752, chunks + 1280)

    def kernel(summed, summed3, out, rows_v, spaced, flat, sem):
        role = lax.axis_index("section")
        me = lax.axis_index("dp")
        zero = jnp.zeros((64, LANE), F32)

        def clear(i, carry):
            flat[pl.ds(pl.multiple_of(i * 64, 64), 64), :] = zero
            return carry

        def fetch(source, room):
            return pltpu.make_async_copy(source, rows_v.at[pl.ds(0, room)], sem.at[0])

        @pl.when(role < 3)
        def _():
            fetch(summed, rooms[0]).start()

        @pl.when(role == 3)
        def _():
            fetch(summed3, rooms[1]).start()

        lax.fori_loop(0, flat_rows // 64, clear, 0)

        @pl.when(role < 3)
        def _():
            fetch(summed, rooms[0]).wait()

        @pl.when(role == 3)
        def _():
            fetch(summed3, rooms[1]).wait()

        lane = lanes()

        for which in range(4):
            width, pitch, rows, before, lead, period = FORM[which]
            if which == 0:
                blocks, cols, tiles = 1, FILT, 9
            elif which == 3:
                blocks, cols, tiles = 1, VOCAB, 79
            else:
                blocks, cols, tiles = 4, HID, 6
            stride = period * width // LANE
            most = max(slab(which, dest, share)[2] for dest in range(groups))
            groups8 = -(-(-(-most // pitch) * 16) // (8 * period))

            @pl.when(role == which)
            def _(which=which):
                first, _, count = slab(which, me, share)
                skip = lead * lax.max(1 - me, 0)
                step_rows = pitch * 49 + (pitch * 49 + 1) % 2

                def space(rt, carry):
                    for c in range(pitch):
                        for half in range(2):
                            at = pl.multiple_of((skip + rt * pitch + c) * 16 + 8 * half, 8)
                            spaced[pl.ds(rt * step_rows + 49 * c + 24 * half, 8, stride=3), :] = rows_v[pl.ds(at, 8), :]
                    return carry

                lax.fori_loop(0, (count - skip) // pitch, space, 0)
                base = margin + before // LANE + stride * (first // period) - chunks * me

                def row(i, carry):
                    group, n = i // period, lax.rem(i, period)
                    number = first + period * (8 * group + sublanes()) + n
                    keep = number < rows
                    hop = period // 16 * step_rows
                    source = n // 16 * step_rows + 3 * lax.rem(n, 16) + 8 * group * hop
                    step = 27
                    for b in range(blocks):
                        flat_at = before % LANE + width * n + cols * b
                        turn = lax.rem(flat_at, LANE)
                        to = base + flat_at // LANE + stride * 8 * group
                        last = jnp.zeros((8, LANE), F32)
                        for low in range(0, tiles, step):
                            high = min(low + step, tiles)
                            taken = [
                                spaced[pl.ds(source + 49 * (tiles * b + j), 8, stride=hop), :]
                                for j in range(low, high)
                            ]
                            turned = [last] + [pltpu.roll(jnp.where(keep, x, 0.0), turn, 1) for x in taken]
                            for j in range(low, high):
                                value = jnp.where(lane >= turn, turned[j - low + 1], turned[j - low])
                                where = pl.ds(to + j, 8, stride=stride)
                                if j == 0:
                                    value = jnp.where(lane >= turn, value, flat[where, :])
                                flat[where, :] = value
                            last = turned[-1]
                        where = pl.ds(to + tiles, 8, stride=stride)
                        flat[where, :] = jnp.where(lane + LANE * tiles - turn < cols, last, flat[where, :])
                    return carry

                @pl.when(count > 0)
                def _():
                    lax.fori_loop(0, period * groups8, row, 0)

        @pl.when((role == 0) & (me == 0))
        def _():
            lane1 = lanes(1)

            def piece(row_at, flat_at, low, size):
                edge = flat_at - low
                turn = edge % LANE
                to = margin + (edge - turn) // LANE
                first, end = low // LANE, (low + size - 1) // LANE
                last = jnp.zeros((1, LANE), F32)
                for j in range(first, end + 2):
                    least, most = max(low + turn - LANE * j, 0), min(low + size + turn - LANE * j, LANE)
                    here = last
                    if j <= end:
                        here = rows_v[row_at + 16 * j : row_at + 16 * j + 1, :]
                        here = pltpu.roll(here, turn, 1) if turn else here
                    if most > least:
                        value = jnp.where(lane1 >= turn, here, last) if turn else here
                        at = to + j
                        if least > 0 or most < LANE:
                            value = jnp.where((lane1 >= least) & (lane1 < most), value, flat[at : at + 1, :])
                        flat[at : at + 1, :] = value
                    last = here

            for k in range(1, 8):
                n = NFILT[k - 1]
                for i in range(k * D_CHAR + 1):
                    number = i + i // D_CHAR if i < k * D_CHAR else 15
                    piece(number // 16 * 144 + number % 16, KOFF[k - 1] + n * i, COLS[k - 1], n)
            for a in range(CHAR_V):
                piece(72 * 16 + a, D_CHAR * a, 0, D_CHAR)

        copy = pltpu.make_async_copy(flat.at[pl.ds(margin, chunks)], out, sem.at[0])
        copy.start()
        copy.wait()

    return pl.pallas_call(
        kernel,
        out_shape=jax.ShapeDtypeStruct((chunks, LANE), F32),
        in_specs=[ANYWHERE] * 2,
        out_specs=ANYWHERE,
        scratch_shapes=[
            vmem((slab_rows, LANE), F32), vmem((31104, LANE), F32), vmem((flat_rows, LANE), F32), dmas(1),
        ],
        compiler_params=pltpu.CompilerParams(vmem_limit_bytes=LIMIT),
        name="pack",
    )(summed.reshape(rooms[0], LANE), summed3.reshape(rooms[1], LANE))


def shards(char_ids, target_ids, remaining, resets, start_state, section_params):
    rows, steps = char_ids.shape[:2]
    groups = lax.axis_size("dp")
    packed = section_params.shape[1]
    share = packed // groups
    n = rows * (steps + 1)

    def by_step(x, fill):
        x = jnp.pad(x.T, ((0, 1), (0, 0)), constant_values=fill)
        return jnp.broadcast_to(x.reshape(n, 1), (n, LANE))

    ids = jnp.pad(
        char_ids.transpose(1, 0, 2), ((0, 1), (0, 0), (0, LANE - WORD_CHARS)), constant_values=-1
    ).reshape(n, LANE)
    targets = by_step(target_ids, -1)
    keep = by_step(1.0 - resets.astype(F32), 0.0)
    valid = by_step((jnp.arange(steps, dtype=jnp.int32)[None, :] < remaining[:, None]).astype(F32), 0.0)
    state = jnp.pad(start_state, ((0, 0), (0, 0), (0, 0), (0, GW - HID)))

    km, e8, ab, ur, rt, wt = unpack_all(section_params)
    y2, *char_saved = char_forward_call(ids, km, e8, ab)
    feats, pres, total, emb = char_saved
    grad, dpre, late, xb, lhs, dz, dl, _, _, loss, bias = recurrent_call(
        y2, feats, pres, ab, ur, rt, wt, keep, targets, valid, state
    )
    tiles3 = output_weights_call(xb, dl)
    summed3 = gather_sum_call(tiles3, groups, share)
    conv, early = char_backward_call(ids, grad, km, (total, emb), dpre)
    summed, small = finish_call(lhs, dz, dpre, (late, early), conv, bias, loss, summed3, groups, share)
    flat = pack_call(summed, summed3, groups, share)
    small = sections_sum_call(small)
    mean_loss = small[0, FW] / (groups * rows * steps)
    return mean_loss, flat.reshape(1, share), small[0, :FILT]


def solution(mesh):
    in_specs = (
        P("dp", None, None),
        P("dp", None),
        P("dp"),
        P("dp", None),
        P(None, None, "dp", None),
        P("section", None),
    )
    out_specs = (P(), P("section", "dp"), P())
    return jax.shard_map(shards, mesh=mesh, in_specs=in_specs, out_specs=out_specs, check_vma=False)
```

```python
import functools
import math

import jax
import jax.numpy as jnp
from jax import lax
from jax.experimental import pallas as pl
from jax.experimental.pallas import tpu as pltpu
from jax.sharding import PartitionSpec as P

D_CHAR = 15
CHAR_V = 51
F_UNIT = 50
WORD_CHARS = 21
HID = 650
VOCAB = 10000
FILT = 1100
F32 = jnp.float32
BF16 = jnp.bfloat16

NFILT = [F_UNIT * min(k, 4) for k in range(1, 8)]
COLS = [sum(NFILT[:k]) for k in range(8)]
KOFF = [CHAR_V * D_CHAR + sum((j * D_CHAR + 1) * NFILT[j - 1] for j in range(1, k)) for k in range(1, 9)]
CONV_END = KOFF[7]
HIGH_STRIDE = FILT * (FILT + 1)
FW = 1152
GW = 768
ZW = 4 * GW
VW = 10112
LANE = 128
LENS = (2304, 2688, 2688, 5120)


def roll_lanes(x, shift):
    return pltpu.roll(x, shift, 1)


def lanes(rows=8):
    return lax.broadcasted_iota(jnp.int32, (rows, LANE), 1)


def sublanes():
    return lax.broadcasted_iota(jnp.int32, (8, LANE), 0)


def widen(raw, slot, rows, wide):
    def body(i, carry):
        piece = raw[slot, 0:1, pl.ds(pl.multiple_of(i * 16384, 16384), 16384)]
        wide[pl.ds(pl.multiple_of(i * 128, 128), 128), :] = piece.astype(F32).reshape(128, LANE)
        return carry

    lax.fori_loop(0, rows // 128, body, 0)


DEPTH = 4


def stream_start(count, length, total, chunk_of, src, raw, sem):
    for i in range(DEPTH - 1):
        stream_copy(jnp.int32(i), length, total, chunk_of, src, raw, sem).start()


def stream_at(i, length, total, chunk_of):
    return jnp.minimum(chunk_of(i) // 8 * 8, total - length)


def stream_copy(i, length, total, chunk_of, src, raw, sem):
    at = pl.multiple_of(stream_at(i, length, total, chunk_of) * LANE, 8 * LANE)
    slot = lax.rem(i, DEPTH)
    return pltpu.make_async_copy(
        src.at[:, pl.ds(at, length * LANE)], raw.at[slot, :, pl.ds(0, length * LANE)], sem.at[slot]
    )


def stream_blocks(count, length, total, chunk_of, src, raw, sem, wide, work):
    def body(i, carry):
        @pl.when(i + DEPTH - 1 < count)
        def _():
            stream_copy(i + DEPTH - 1, length, total, chunk_of, src, raw, sem).start()

        stream_copy(i, length, total, chunk_of, src, raw, sem).wait()
        widen(raw, lax.rem(i, DEPTH), length, wide)
        work(i, chunk_of(i) - stream_at(i, length, total, chunk_of))
        return carry

    lax.fori_loop(0, count, body, 0)


def take_rows(wide, starts, tiles, cols, stride, put):
    step = max(1, 28 // len(starts))
    lane = lanes()
    for low in range(0, tiles, step):
        high = min(tiles, low + step)
        loaded = [
            [wide[pl.ds(first + c, 8, stride=stride), :] for c in range(low, high + 1)] for _, first, _, _ in starts
        ]
        results = []
        for (_, _, shift, keep_row), pieces in zip(starts, loaded):
            turn = lax.rem(LANE - shift, LANE)
            split = lane < LANE - shift
            turned = [roll_lanes(piece, turn) for piece in pieces]
            for c in range(low, high):
                out = jnp.where(split, turned[c - low], turned[c - low + 1])
                keep = keep_row
                if cols - c * LANE < LANE:
                    keep = keep & (lane < cols - c * LANE)
                results.append(jnp.where(keep, out, 0.0))
        at = 0
        for tag, _, _, _ in starts:
            for c in range(low, high):
                put(tag, c, results[at])
                at += 1


def spread(c, n, period):
    return pl.ds((c * period + n) * 25, 8, stride=3)


def collect(dest, c, period):
    return [
        dest[pl.ds((c * period + 8 * m) * 25 + 3 * j, 8, stride=25), :] for j in range(8) for m in range(period // 8)
    ]


def stage_tile(stage, slot, c, blocks):
    for i in range(0, len(blocks), 2):
        pair = jnp.concatenate([blocks[i], blocks[i + 1]], axis=0).astype(BF16)
        stage[slot, pl.ds(8 * i, 16), pl.ds(c * LANE, LANE)] = pair


def unpack_kernel(
    src, km, e8, ab, ur, rt, wt, raw, wide, dest, kstage, stage0, stage1, stage_t, stage3, raw_conv, sem_in, sem_out, sem_t
):
    role = lax.axis_index("section")
    total = src.shape[1] // LANE

    def out_copy(stage, slot, target):
        return pltpu.make_async_copy(stage.at[slot], target, sem_out.at[slot])

    @pl.when(role == 0)
    def _():
        blocks = 5
        count = 4 * blocks

        def flat_of(i):
            return CONV_END + HIGH_STRIDE * (i // blocks)

        def chunk_of(i):
            return flat_of(i) // LANE + 2200 * lax.rem(i, blocks)

        length = 640
        copy = pltpu.make_async_copy(src.at[:, pl.ds(0, length * LANE)], raw_conv.at[0], sem_t.at[0])
        copy.start()
        stream_start(count, LENS[0], total, chunk_of, src, raw, sem_in)
        copy.wait()
        widen(raw_conv, 0, length, wide)
        lane1 = lanes(1)
        dest[pl.ds(0, 64), :] = jnp.zeros((64, LANE), F32)
        for a in range(CHAR_V):
            flat = D_CHAR * a
            q, s = flat // LANE, flat % LANE
            here = wide[q : q + 1, :]
            out = roll_lanes(here, (LANE - s) % LANE) if s else here
            if s + D_CHAR > LANE:
                out = jnp.where(lane1 < LANE - s, out, roll_lanes(wide[q + 1 : q + 2, :], LANE - s))
            dest[a : a + 1, :] = jnp.where(lane1 < D_CHAR, out, jnp.where(lane1 == D_CHAR, 1.0, 0.0))
        table = dest[pl.ds(0, 64), :]
        for m in range(8):
            kstage[pl.ds(64 * m, 64), pl.ds(0, LANE)] = (
                pltpu.roll(table, 16 * m, 1) if m else table
            ).astype(BF16)
        copy = pltpu.make_async_copy(kstage.at[pl.ds(0, 512), pl.ds(0, LANE)], e8, sem_out.at[0])
        copy.start()
        copy.wait()
        tiles = FW // LANE
        rows = 112
        dest[pl.ds(0, rows * tiles), :] = jnp.zeros((rows * tiles, LANE), F32)

        def kernel_row(k, i, row):
            n, base = NFILT[k - 1], COLS[k - 1]
            edge = KOFF[k - 1] + n * i - base
            q, s = edge // LANE, edge % LANE
            for ct in range(base // LANE, (base + n - 1) // LANE + 1):
                out = wide[q + ct : q + ct + 1, :]
                if s:
                    after = roll_lanes(wide[q + ct + 1 : q + ct + 2, :], LANE - s)
                    out = jnp.where(lane1 < LANE - s, roll_lanes(out, LANE - s), after)
                at = ct * rows + row
                low, high = max(base - ct * LANE, 0), min(base + n - ct * LANE, LANE)
                if low > 0 or high < LANE:
                    out = jnp.where((lane1 >= low) & (lane1 < high), out, dest[at : at + 1, :])
                dest[at : at + 1, :] = out

        for k in range(1, 8):
            for i in range(k * D_CHAR):
                kernel_row(k, i, i + i // D_CHAR)
            kernel_row(k, k * D_CHAR, 15)
        kstage[...] = jnp.zeros_like(kstage)
        for ct in range(tiles):
            kstage[pl.ds(112, rows), pl.ds(ct * LANE, LANE)] = dest[pl.ds(ct * rows, rows), :].astype(BF16)
        copy = pltpu.make_async_copy(kstage.at[pl.ds(0, 368)], km, sem_out.at[0])
        copy.start()
        copy.wait()

        def target(i):
            return ab.at[i // blocks, pl.ds(pl.multiple_of(lax.rem(i, blocks) * 256, 256), 256)]

        def work(i, extra):
            block = lax.rem(i, blocks)
            inner = lax.rem(flat_of(i), LANE)

            def rows_of(i, carry):
                starts = []
                for n in (2 * i, 2 * i + 1):
                    flat = inner + FILT * n
                    keep = 32 * (8 * block + sublanes()) + n <= FILT
                    starts.append((n, flat // LANE + extra, lax.rem(flat, LANE), keep))

                def put(n, c, value):
                    dest[spread(c, n, 32), :] = value

                take_rows(wide, starts, tiles, FILT, 275, put)
                return carry

            lax.fori_loop(0, 16, rows_of, 0)
            slot = lax.rem(i, 2)

            @pl.when(i >= 2)
            def _():
                out_copy(stage0, slot, target(i - 2)).wait()

            for c in range(tiles):
                stage_tile(stage0, slot, c, collect(dest, c, 32))
            out_copy(stage0, slot, target(i)).start()

        stream_blocks(count, LENS[0], total, chunk_of, src, raw, sem_in, wide, work)
        for i in (count - 2, count - 1):
            out_copy(stage0, i % 2, target(i)).wait()

    for layer in (1, 2):

        @pl.when(role == layer)
        def _(layer=layer):
            depth = FILT if layer == 1 else HID
            blocks = -(-depth // 128)
            recurrent = depth * 4 * HID
            count = blocks + 6

            def chunk_of(i):
                return jnp.where(i < blocks, 2600 * i, recurrent // LANE + 2600 * (i - blocks))

            stream_start(count, LENS[1], total, chunk_of, src, raw, sem_in)

            def target(i):
                at = jnp.where(i < blocks, i, i - blocks + 9)
                return ur.at[pl.ds(pl.multiple_of(at * 128, 128), 128)]

            def work(i, extra):
                inner = jnp.where(i < blocks, 0, recurrent % LANE)
                block = jnp.where(i < blocks, i, i - blocks)
                limit = jnp.where(i < blocks, depth, HID + 1)

                def rows_of(n, carry):
                    keep = 16 * (8 * block + sublanes()) + n < limit
                    flats = [inner + 4 * HID * n + HID * b for b in range(4)]

                    def put(b, c, value):
                        dest[spread(6 * b + c, n, 16), :] = value

                    starts = [(b, flat // LANE + extra, lax.rem(flat, LANE), keep) for b, flat in enumerate(flats)]
                    take_rows(wide, starts, 6, HID, 325, put)
                    return carry

                lax.fori_loop(0, 16, rows_of, 0)
                slot = lax.rem(i, 2)

                @pl.when(i >= 2)
                def _():
                    out_copy(stage1, slot, target(i - 2)).wait()

                for c in range(24):
                    stage_tile(stage1, slot, c, collect(dest, c, 16))
                out_copy(stage1, slot, target(i)).start()

                @pl.when(i >= blocks)
                def _():
                    @pl.when(i >= blocks + 2)
                    def _():
                        turned_copy(i - 2).wait()

                    k = LANE * block + lanes(LANE)
                    for c in range(24):
                        turned = jnp.transpose(jnp.concatenate(collect(dest, c, 16), axis=0))
                        stage_t[slot, pl.ds(128 * c, 128), :] = jnp.where(k < HID, turned, 0.0).astype(BF16)
                    turned_copy(i).start()

            def turned_copy(i):
                slot = lax.rem(i, 2)
                at = pl.multiple_of((i - blocks) * LANE, LANE)
                return pltpu.make_async_copy(stage_t.at[slot], rt.at[:, pl.ds(at, LANE)], sem_t.at[slot])

            stream_blocks(count, LENS[1], total, chunk_of, src, raw, sem_in, wide, work)
            for i in (count - 2, count - 1):
                out_copy(stage1, i % 2, target(jnp.int32(i))).wait()
                turned_copy(jnp.int32(i)).wait()

    @pl.when(role == 3)
    def _():
        count = 11
        tiles = VW // LANE

        def chunk_of(i):
            return 5000 * i

        stream_start(count, LENS[3], total, chunk_of, src, raw, sem_in)

        def target(i):
            return wt.at[pl.ds(pl.multiple_of(i * 64, 64), 64)]

        def work(i, extra):
            def rows_of(n, carry):
                flat = VOCAB * n
                keep = 8 * (8 * i + sublanes()) + n < HID + 1

                def put(n, c, value):
                    dest[spread(c, n, 8), :] = value

                take_rows(wide, [(n, flat // LANE + extra, lax.rem(flat, LANE), keep)], tiles, VOCAB, 625, put)
                return carry

            lax.fori_loop(0, 8, rows_of, 0)
            slot = lax.rem(i, 2)

            @pl.when(i >= 2)
            def _():
                out_copy(stage3, slot, target(i - 2)).wait()

            for c in range(tiles):
                stage_tile(stage3, slot, c, collect(dest, c, 8))
            out_copy(stage3, slot, target(i)).start()

        stream_blocks(count, LENS[3], total, chunk_of, src, raw, sem_in, wide, work)
        for i in (count - 2, count - 1):
            out_copy(stage3, i % 2, target(jnp.int32(i))).wait()


def unpack_all(section_params):
    anywhere = pl.BlockSpec(memory_space=pl.ANY)
    return pl.pallas_call(
        unpack_kernel,
        out_shape=[
            jax.ShapeDtypeStruct((368, FW), BF16),
            jax.ShapeDtypeStruct((512, LANE), BF16),
            jax.ShapeDtypeStruct((4, 1280, FW), BF16),
            jax.ShapeDtypeStruct((15 * 128, ZW), BF16),
            jax.ShapeDtypeStruct((ZW, GW), BF16),
            jax.ShapeDtypeStruct((11 * 64, VW), BF16),
        ],
        in_specs=[anywhere],
        out_specs=[anywhere] * 6,
        scratch_shapes=[
            pltpu.VMEM((DEPTH, 1, LENS[3] * LANE), BF16),
            pltpu.VMEM((9312, LANE), F32),
            pltpu.VMEM((79 * 200, LANE), F32),
            pltpu.VMEM((512, FW), BF16),
            pltpu.VMEM((2, 256, FW), BF16),
            pltpu.VMEM((2, 128, ZW), BF16),
            pltpu.VMEM((2, ZW, LANE), BF16),
            pltpu.VMEM((2, 64, VW), BF16),
            pltpu.VMEM((1, 1, 640 * LANE), BF16),
            pltpu.SemaphoreType.DMA((DEPTH,)),
            pltpu.SemaphoreType.DMA((2,)),
            pltpu.SemaphoreType.DMA((2,)),
        ],
        compiler_params=pltpu.CompilerParams(vmem_limit_bytes=56 << 20),
        name="unpack",
    )(section_params)


def fblocks(width, step=256):
    return [(at, min(step, width - at)) for at in range(0, width, step)]


def mm(a, b):
    return jnp.dot(a, b, preferred_element_type=F32)


def mm_tn(a, b):
    return lax.dot_general(a, b, (((0,), (0,)), ((), ())), preferred_element_type=F32)


def mm_nt(a, b):
    return lax.dot_general(a, b, (((1,), (1,)), ((), ())), preferred_element_type=F32)


def mm_nt_few(a, b):
    return jnp.transpose(mm_nt(b, a))


def sigmoid(x):
    return 0.5 * jnp.tanh(0.5 * x) + 0.5


def load(pairs, sem):
    copies = [pltpu.make_async_copy(a, b, sem.at[i]) for i, (a, b) in enumerate(pairs)]
    for copy in copies:
        copy.start()
    for copy in copies:
        copy.wait()


def column_mask(at, width, limit, rows):
    return lax.broadcasted_iota(jnp.int32, (rows, width), 1) + at < limit


def char_onehot(ids, t):
    rows = ids.shape[0]
    lane = lanes(rows)
    pieces = []
    for pair in range(4):
        j = 8 * t + 2 * pair
        left = ids[:, j : j + 1]
        right = ids[:, j + 1 : j + 2]
        hit = jnp.where(lane < 64, left, right) == lax.rem(lane, 64)
        pieces.append(jnp.where(hit, 1.0, 0.0).astype(BF16))
    return jnp.concatenate(pieces, axis=1)


def conv_steps(body):
    def step(p, carry):
        body(p, p // 8, True, lax.rem(p, 8), FILT)
        return carry

    lax.fori_loop(0, 15, step, 0)
    body(15, 1, True, 7, COLS[6])
    for p in range(16, WORD_CHARS):
        body(p, 2, False, p - 16, COLS[WORD_CHARS - p])


def conv_at(emb, km, tile, second, within, at, width):
    first = 112 - 16 * within
    if not isinstance(first, int):
        first = pl.multiple_of(first, 16)
    if second:
        window = jnp.concatenate([emb[tile], emb[tile + 1]], axis=1)
    else:
        window = emb[tile]
    return mm(window, km[pl.ds(first, window.shape[1]), pl.ds(at, width)])


def char_forward(ids, e8, km, ab, emb, total, feats, pres, out):
    rows = ids.shape[0]
    for t in range(3):
        emb[t] = mm(char_onehot(ids, t), e8[...]).astype(BF16)
    total[...] = jnp.zeros_like(total)

    def step(p, tile, second, within, limit):
        for at, width in fblocks(FW):
            if at >= limit:
                continue
            value = jnp.exp(jnp.tanh(conv_at(emb, km, tile, second, within, at, width)))
            if at + width > limit and limit < FILT:
                value = jnp.where(column_mask(at, width, limit, rows), value, 0.0)
            total[:, pl.ds(at, width)] += value

    conv_steps(step)
    for at, width in fblocks(FW):
        col = lax.broadcasted_iota(jnp.int32, (rows, width), 1) + at
        count = jnp.full((rows, width), float(WORD_CHARS), F32)
        for k in range(1, 7):
            count = jnp.where(col >= COLS[k], float(WORD_CHARS - k), count)
        value = jnp.log(total[:, pl.ds(at, width)]) - jnp.log(count)
        value = jnp.where(col < FILT, value, jnp.where(col == FILT, 1.0, 0.0))
        feats[0, :, pl.ds(at, width)] = value.astype(BF16)
    for layer in range(2):
        for at, width in fblocks(FW):
            cols = pl.ds(at, width)
            t_pre = mm(feats[layer], ab[2 * layer, pl.ds(0, FW), cols])
            h_pre = mm(feats[layer], ab[2 * layer + 1, pl.ds(0, FW), cols])
            pres[2 * layer, :, cols] = t_pre
            pres[2 * layer + 1, :, cols] = h_pre
            gate = sigmoid(t_pre)
            y = feats[layer, :, cols].astype(F32)
            value = gate * (h_pre * sigmoid(h_pre)) + (1.0 - gate) * y
            col = lax.broadcasted_iota(jnp.int32, (rows, width), 1) + at
            if layer == 0:
                value = jnp.where(col < FILT, value, jnp.where(col == FILT, 1.0, 0.0))
                feats[1, :, cols] = value.astype(BF16)
            else:
                out[:, cols] = jnp.where(col < FILT, value, 0.0).astype(BF16)


def conv_backward(km, kt, emb, emb_t, slopes, held, sem, grad, dk, demb):
    rows = grad.shape[0]

    def fetch(p, slot):
        return pltpu.make_async_copy(slopes.at[p], held.at[slot], sem.at[slot])

    fetch(0, 0).start()
    kt[...] = jnp.transpose(km[pl.ds(112, LANE), :])
    for t in range(3):
        emb_t[pl.ds(LANE * t, LANE), :] = jnp.transpose(emb[t])
    emb_t[pl.ds(3 * LANE, LANE), :] = jnp.zeros((LANE, rows), BF16)
    dk[...] = jnp.zeros_like(dk)
    demb[...] = jnp.zeros_like(demb)

    def step(p, tile, second, within, limit):
        slot = p % 2 if isinstance(p, int) else lax.rem(p, 2)
        if not isinstance(p, int) or p + 1 < WORD_CHARS:
            fetch(p + 1, 1 - slot).start()
        fetch(p, slot).wait()
        window_t = emb_t[pl.ds(p * 16 if isinstance(p, int) else pl.multiple_of(p * 16, 16), LANE), :]
        back = jnp.zeros((rows, LANE), F32)
        for at, width in fblocks(FW):
            if at >= limit:
                continue
            cols = pl.ds(at, width)
            dz = (grad[:, cols] * held[slot, :, cols]).astype(BF16)
            dk[:, cols] += mm(window_t, dz)
            back = back + mm(dz, kt[cols, :])
        lane = lanes(rows)
        back = jnp.where(lane < 112, back, 0.0)
        turned = pltpu.roll(back, 16 * within, 1)
        demb[tile] += jnp.where(lane >= 16 * within, turned, 0.0)
        if second:
            demb[tile + 1] += jnp.where(lane < 16 * within, turned, 0.0)

    conv_steps(step)


def table_backward(ids, demb, table):
    acc = jnp.zeros((64, LANE), F32)
    for t in range(3):
        hot = char_onehot(ids, t)
        value = demb[t]
        high = value.astype(BF16)
        low = (value - high.astype(F32)).astype(BF16)
        grads = mm_tn(hot, high) + mm_tn(hot, low)
        for m in range(8):
            block = grads[64 * m : 64 * m + 64, :]
            acc = acc + (pltpu.roll(block, LANE - 16 * m, 1) if m else block)
    table[...] = acc


def tile_rows(stage, base, value, row_tiles, col_tiles, first_col=0, pitch=None):
    pitch = col_tiles if pitch is None else pitch
    for r in range(row_tiles):
        for c in range(col_tiles):
            stage[base + r * pitch + first_col + c] = value[16 * r : 16 * r + 16, LANE * c : LANE * c + LANE].astype(BF16)


def six(x):
    return jnp.concatenate([x] * 6, axis=1)


ANYWHERE = pl.BlockSpec(memory_space=pl.ANY)
ON_CHIP = pl.BlockSpec(memory_space=pltpu.VMEM)
LIMIT = 56 << 20


def call(kernel, name, ins, specs, outs, scratch, aliases=None):
    return pl.pallas_call(
        kernel,
        out_shape=[jax.ShapeDtypeStruct(shape, dtype) for shape, dtype in outs],
        in_specs=specs,
        out_specs=[ANYWHERE] * len(outs),
        scratch_shapes=scratch,
        input_output_aliases=aliases or {},
        compiler_params=pltpu.CompilerParams(vmem_limit_bytes=LIMIT),
        name=name,
    )(*ins)


def vmem(shape, dtype):
    return pltpu.VMEM(shape, dtype)


def dmas(count):
    return pltpu.SemaphoreType.DMA((count,))


def char_forward_call(ids, km, e8, ab):
    n = ids.shape[0]

    def kernel(ids, km, e8, ab, y2_o, feats_o, pres_o, total_o, emb_o, km_v, e8_v, ab_v, y2, feats, pres, total, emb, sem):
        @pl.when(lax.axis_index("section") == 0)
        def _():
            load([(km, km_v), (e8, e8_v), (ab, ab_v)], sem)
            char_forward(ids, e8_v, km_v, ab_v, emb, total, feats, pres, y2)
            load([(y2, y2_o), (feats, feats_o), (pres, pres_o), (total, total_o), (emb, emb_o)], sem)

    outs = [
        ((n, FW), BF16),
        ((2, n, FW), BF16),
        ((4, n, FW), F32),
        ((n, FW), F32),
        ((3, n, LANE), BF16),
    ]
    scratch = [vmem(km.shape, BF16), vmem(e8.shape, BF16), vmem(ab.shape, BF16)]
    scratch += [vmem(shape, dtype) for shape, dtype in outs] + [dmas(5)]
    return call(kernel, "char_forward", (ids, km, e8, ab), [ON_CHIP] + [ANYWHERE] * 3, outs, scratch)


def char_backward_call(ids, grad, km, emb, slopes, dpre):
    n = ids.shape[0]
    rows = SPLIT * CHUNK

    def kernel(
        ids, grad, km, emb, slopes, dpre, tiles_o, right_o,
        grad_v, km_v, emb_v, held, sem_s, kt, emb_t, dk, demb, table, stage, sem, send, recv,
    ):
        me = lax.axis_index("dp")

        def right_copy(k):
            return pltpu.make_async_remote_copy(
                dpre.at[pl.ds(0, rows)], right_o.at[k - 1], send.at[k - 1], recv.at[k - 1],
                device_id={"dp": quad_peer(me, k)}, device_id_type=pl.DeviceIdType.MESH,
            )

        @pl.when(lax.axis_index("section") == 0)
        def _():
            barrier = pltpu.get_barrier_semaphore()
            for k in range(1, QUAD):
                pl.semaphore_signal(
                    barrier, inc=1, device_id={"dp": quad_peer(me, k)}, device_id_type=pl.DeviceIdType.MESH
                )
            pl.semaphore_wait(barrier, QUAD - 1)
            for k in range(1, QUAD):
                right_copy(k).start()
            load([(grad, grad_v), (km, km_v), (emb, emb_v)], sem)
            conv_backward(km_v, kt, emb_v, emb_t, slopes, held, sem_s, grad_v, dk, demb)
            table_backward(ids, demb, table)
            tile_rows(stage, 0, dk[...], 8, 9)
            tile_rows(stage, 72, table[...], 4, 1)
            load([(stage, tiles_o)], sem)
            for k in range(1, QUAD):
                right_copy(k).wait_send()
                right_copy(k).wait_recv()

    outs = [((CONV_TILES, 16, LANE), BF16), ((QUAD - 1, rows, 4 * FW), BF16)]
    scratch = [
        vmem((n, FW), F32), vmem(km.shape, BF16), vmem(emb.shape, BF16), vmem((2, n, FW), F32), dmas(2),
        vmem((FW, LANE), BF16), vmem((4 * LANE, n), BF16), vmem((LANE, FW), F32), vmem((3, n, LANE), F32),
        vmem((64, LANE), F32), vmem((CONV_TILES, 16, LANE), BF16), dmas(4), dmas(QUAD - 1), dmas(QUAD - 1),
    ]
    return pl.pallas_call(
        kernel,
        out_shape=[jax.ShapeDtypeStruct(shape, dtype) for shape, dtype in outs],
        in_specs=[ON_CHIP] + [ANYWHERE] * 5,
        out_specs=[ANYWHERE] * 2,
        scratch_shapes=scratch,
        compiler_params=pltpu.CompilerParams(vmem_limit_bytes=LIMIT, collective_id=4, has_side_effects=True),
        name="char_backward",
    )(ids, grad, km, emb, slopes, dpre)


CONV_TILES = 76
TILES = 3648


def turned_tile(left, right, shift):
    rows = right.shape[0]
    if shift:
        mixed = jnp.where(
            lanes(rows) < shift, pltpu.roll(left.astype(F32), shift, 1), pltpu.roll(right.astype(F32), shift, 1)
        )
        right = mixed.astype(BF16)
    return jnp.transpose(right)


def each_vocab(body, step=2048):
    whole = VW // step

    def one(i, carry):
        body(pl.multiple_of(i * step, step), step)
        return carry

    lax.fori_loop(0, whole, one, 0)
    body(whole * step, VW - whole * step)


def output_weights_call(h, dl):
    n = h.shape[0]
    rows = 704
    pitch = VW // LANE

    def kernel(h, dl, tiles_o, h_v, dl_v, h_t, stage, sem):
        @pl.when(lax.axis_index("section") == 3)
        def _():
            load([(h, h_v), (dl, dl_v)], sem)
            lane = lanes(n)
            for c in range(6):
                value = h_v[:, pl.ds(LANE * c, LANE)].astype(F32)
                value = jnp.where(lane + c * LANE == HID, 1.0, value).astype(BF16)
                h_t[pl.ds(LANE * c, LANE), :] = jnp.transpose(value)

            def body(at, width):
                first = at // LANE
                for top, count in fblocks(rows):
                    value = mm(h_t[pl.ds(top, count), :], dl_v[:, pl.ds(at, width)])
                    for r in range(count // 16):
                        for c in range(width // LANE):
                            stage[(top // 16 + r) * pitch + first + c] = value[
                                16 * r : 16 * r + 16, LANE * c : LANE * c + LANE
                            ].astype(BF16)

            each_vocab(body, 256)
            count = rows // 16 * pitch
            load([(stage.at[pl.ds(0, count)], tiles_o.at[pl.ds(0, count)])], sem)

    scratch = [
        vmem((n, GW), BF16), vmem((n, VW), BF16), vmem((6 * LANE, n), BF16),
        vmem((rows // 16 * pitch, 16, LANE), BF16), dmas(2),
    ]
    return call(
        kernel, "output_weights", (h, dl), [ANYWHERE] * 2, [((TILES, 16, LANE), BF16)], scratch
    )[0]


CHUNK = 32
GROUPS_OUT = (3, 3, 2, 1)


def lstm_steps(first, count, keep, carry, r, gates, cells, prevs, hiddens):
    def step(s, carry):
        h, c = carry
        at = pl.ds(pl.multiple_of((first + s) * 8, 8), 8)
        k = six(keep[at, :])
        hp = h * k
        cp = c * k
        prevs[at, :] = hp
        z = gates[at, :] + mm(hp.astype(BF16), r[...])
        i = sigmoid(z[:, 0:GW])
        f = sigmoid(z[:, GW : 2 * GW])
        o = sigmoid(z[:, 2 * GW : 3 * GW])
        g = jnp.tanh(z[:, 3 * GW :])
        c = f * cp + i * g
        h = (o * jnp.tanh(c)).astype(BF16).astype(F32)
        gates[at, :] = jnp.concatenate([i, f, o, g], axis=1)
        cells[at, :] = c
        hiddens[at, :] = h
        return h, c

    return lax.fori_loop(0, count, step, carry)


def lstm_back_steps(first, count, keep, c0, carry, rt, gates, cells, dhs):
    def step(s, carry):
        dh_next, dc_next = carry
        t = first + count - 1 - s
        at = pl.ds(pl.multiple_of(t * 8, 8), 8)
        before = pl.ds(pl.multiple_of(jnp.maximum(t - 1, 0) * 8, 8), 8)
        k = six(keep[at, :])
        saved = gates[at, :]
        i, f, o, g = [saved[:, GW * b : GW * b + GW] for b in range(4)]
        cp = jnp.where(t > 0, cells[before, :], c0[...]) * k
        ct = jnp.tanh(cells[at, :])
        dh = dhs[at, :] + dh_next
        dc = dc_next + dh * o * (1.0 - ct * ct)
        dz = jnp.concatenate(
            [dc * g * i * (1.0 - i), dc * cp * f * (1.0 - f), dh * ct * o * (1.0 - o), dc * i * (1.0 - g * g)], axis=1
        ).astype(BF16)
        gates[at, :] = dz.astype(F32)
        return k * mm(dz, rt[...]), k * dc * f

    return lax.fori_loop(0, count, step, carry)


def output_rows(first, count, h, w, targets, valid, logits, dl, top, part, dh, loss, dh16):
    at_rows = pl.ds(first, count)
    depth = w.shape[0]
    own = pl.ds(0, count)
    top[own, :] = jnp.full((count, LANE), -jnp.inf, F32)

    def forward(at, width):
        z = mm(h[at_rows, pl.ds(0, depth)], w[:, pl.ds(at, width)])
        if isinstance(at, int):
            z = jnp.where(column_mask(at, width, VOCAB, count), z, -jnp.inf)
        logits[own, pl.ds(at, width)] = z
        best = top[own, :]
        for c in range(width // LANE):
            best = jnp.maximum(best, z[:, LANE * c : LANE * c + LANE])
        top[own, :] = best

    each_vocab(forward)
    best = jnp.max(top[own, :], axis=1, keepdims=True)
    part[:, own, :] = jnp.zeros((2, count, LANE), F32)
    wanted = targets[at_rows, :]

    def exponents(at, width):
        z = logits[own, pl.ds(at, width)]
        e = jnp.exp(z - best)
        logits[own, pl.ds(at, width)] = e
        for c in range(width // LANE):
            part[0, own, :] += e[:, LANE * c : LANE * c + LANE]
            hit = lanes(count) + (at + LANE * c) == wanted
            part[1, own, :] += jnp.where(hit, z[:, LANE * c : LANE * c + LANE], 0.0)

    each_vocab(exponents)
    total = jnp.sum(part[0, own, :], axis=1, keepdims=True)
    picked = jnp.sum(part[1, own, :], axis=1, keepdims=True)
    counts = valid[at_rows, :]
    loss[...] += jnp.sum(counts * (best + jnp.log(total) - picked), axis=0, keepdims=True)
    share = counts / total
    dh[:, own] = jnp.zeros((depth, count), F32)

    def backward(at, width):
        e = logits[own, pl.ds(at, width)]
        pieces = []
        for c in range(width // LANE):
            hit = lanes(count) + (at + LANE * c) == wanted
            grad = e[:, LANE * c : LANE * c + LANE] * share - jnp.where(hit, counts, 0.0)
            pieces.append(grad.astype(BF16))
        grad = jnp.concatenate(pieces, axis=1)
        dl[at_rows, pl.ds(at, width)] = grad
        dh[:, own] += mm_nt(w[:, pl.ds(at, width)], grad)

    each_vocab(backward)
    for at, width in fblocks(depth):
        value = jnp.transpose(dh[pl.ds(at, width), own])
        dh16[at_rows, pl.ds(at, width)] = jnp.where(column_mask(at, width, HID, count), value, 0.0).astype(BF16)


QUAD = 4
LEFT0 = 35 * LANE
LEFT1 = 14 * LANE
LEFT2 = 11 * LANE
LEFT_ROOM = 41 * LANE


def quad_peer(me, k):
    place = lax.rem(me, QUAD)
    return me - place + lax.rem(place + k, QUAD)


def turn_features(feats, turned):
    n = feats.shape[1]
    zero = jnp.zeros((n, LANE), BF16)
    for segment in range(4):
        start = segment * (FILT + 1)
        shift, first, last = start % LANE, start // LANE, (start + FILT) // LANE
        for c in range(last - first + 1):
            left = feats[segment // 2, :, pl.ds(LANE * (c - 1), LANE)] if c > 0 else zero
            right = feats[segment // 2, :, pl.ds(LANE * c, LANE)] if c < 9 else zero
            tile = turned_tile(left, right, shift)
            at = pl.ds(LANE * (first + c), LANE)
            if c == 0 and segment > 0:
                tile = tile + turned[at, :]
            turned[at, :] = tile


def turn_inputs(x, prevs, depth, turned):
    n = prevs.shape[0]
    first, shift = depth // LANE, depth % LANE
    end = depth + HID
    zero = jnp.zeros((n, LANE), F32)
    lane = lanes(n)
    for c in range(end // LANE + 1):
        if c < first:
            mixed = x[:, pl.ds(LANE * c, LANE)]
        else:
            k = c - first
            left = prevs[:, pl.ds(LANE * (k - 1), LANE)].astype(F32) if 0 < k < 7 else zero
            right = prevs[:, pl.ds(LANE * k, LANE)].astype(F32) if k < 6 else zero
            before = pltpu.roll(left, shift, 1) if k else x[:, pl.ds(LANE * c, LANE)].astype(F32)
            mixed = jnp.where(lane < shift, before, pltpu.roll(right, shift, 1))
            mixed = jnp.where(lane + c * LANE == end, 1.0, mixed).astype(BF16)
        turned[pl.ds(LANE * c, LANE), :] = jnp.transpose(mixed)


SPLIT = 4
AB_PARTS = ((0, 640), (640, 512))


def highway_chunk(rows, slot, dy, feats, pres, grad, dpre, w):
    def cut(m, at, width):
        return pl.ds(m * FW + at, width)

    for at, width in fblocks(FW):
        grad[rows, pl.ds(at, width)] = dy[rows, pl.ds(at, width)].astype(F32)
    for layer in (1, 0):
        own = pl.ds(slot, CHUNK)
        for at, width in fblocks(FW):
            cols = pl.ds(at, width)
            g = grad[rows, cols]
            gate = sigmoid(pres[own, cut(2 * layer, at, width)])
            q = pres[own, cut(2 * layer + 1, at, width)]
            sig = sigmoid(q)
            y = feats[layer, rows, cols].astype(F32)
            dpre[rows, cut(2 * layer, at, width)] = (g * (q * sig - y) * gate * (1.0 - gate)).astype(BF16)
            dpre[rows, cut(2 * layer + 1, at, width)] = (g * gate * sig * (1.0 + q * (1.0 - sig))).astype(BF16)
            grad[rows, cols] = g * (1.0 - gate)
        for half, (row, count) in enumerate(AB_PARTS):
            for at, width in fblocks(count):
                cols = pl.ds(row + at, width)
                value = grad[rows, cols]
                for m in (2 * layer, 2 * layer + 1):
                    part = w[pl.ds(at, width), pl.ds((2 * m + half) * FW, FW)]
                    value = value + mm_nt_few(dpre[rows, cut(m, 0, FW)], part)
                if row + at + width > FILT:
                    value = jnp.where(column_mask(row + at, width, FILT, CHUNK), value, 0.0)
                grad[rows, cols] = value


def recurrent_call(y2, feats, pres, ab, km, emb, total, ur, rt, wt, resets, target_ids, remaining, state):
    n = y2.shape[0]
    real_steps = resets.shape[1]
    chunks = n // CHUNK
    steps = CHUNK // 8
    depth_w = wt.shape[0]
    MESH = pl.DeviceIdType.MESH

    def kernel(
        y2, feats, pres, ab, km, emb, total, ur, rt, wt, resets, target_ids, remaining, state,
        slopes_o, grad_o, dpre_o, right_o, xb_o, lhs_o, dz_o, dl_o, x_q, h_q, loss_o, bias_o,
        emb_v, keep, valid, targets, feats_v, turned, pb, x1, xb, hb, db, ob, dy, u, r, r_t, w, start, gates, cells, prevs, hs, dhs, dz16,
        logits, dl, top, part, dh, loss,
        sem_in, sem_out, send_y, recv_y, send_f, recv_f, send_b, recv_b, send_d, recv_d,
        send_x, recv_x, send_h, recv_h, send_z, recv_z, sem_l, sem_p, sem_s,
    ):
        role = lax.axis_index("section")
        me = lax.axis_index("dp")
        loss[...] = jnp.zeros_like(loss)
        bias_o[...] = jnp.zeros_like(bias_o)

        def to(step, source, target, send, recv):
            return pltpu.make_async_remote_copy(
                source, target, send, recv, device_id={"section": role + step}, device_id_type=MESH
            )

        def span(c):
            return pl.ds(pl.multiple_of(c * CHUNK, CHUNK), CHUNK)

        def forward_copy(c, step):
            return to(step, hb.at[span(c)], xb.at[span(c)], send_f.at[c], recv_f.at[c])

        def backward_copy(c, step):
            return to(step, ob.at[span(c)], db.at[span(c)], send_b.at[c], recv_b.at[c])

        def feature_copy(step):
            return to(step, y2, x1, send_y.at[0], recv_y.at[0])

        def last_copy(c, step):
            return to(step, dy.at[span(c)], dy.at[span(c)], send_d.at[c], recv_d.at[c])

        def quad_copy(source, target, send, recv, k):
            return pltpu.make_async_remote_copy(
                source, target, send, recv, device_id={"dp": quad_peer(me, k)}, device_id_type=MESH
            )

        def input_copy(k):
            return quad_copy(x1, x_q.at[k - 1, 0], send_x.at[k - 1, 0], recv_x.at[k - 1, 0], k)

        def layer_copy(c, k):
            target = x_q.at[k - 1, 0, span(c), pl.ds(0, GW)]
            return quad_copy(xb.at[span(c)], target, send_x.at[k - 1, c], recv_x.at[k - 1, c], k)

        def feats_copy(k):
            return quad_copy(feats_v, x_q.at[k - 1], send_x.at[k - 1, 0], recv_x.at[k - 1, 0], k)

        def hidden_copy(c, k):
            return quad_copy(pb.at[span(c)], h_q.at[k - 1, span(c)], send_h.at[k - 1, c], recv_h.at[k - 1, c], k)

        def each_peer(body):
            for k in range(1, QUAD):
                body(k)

        def each_chunk(body, first=0):
            def step(c, carry):
                body(c)
                return carry

            lax.fori_loop(first, chunks, step, 0)

        def turned_out(g, rows):
            copy = pltpu.make_async_copy(turned.at[pl.ds(0, rows)], lhs_o.at[g, pl.ds(0, rows)], sem_l.at[0])
            copy.start()
            copy.wait()

        def fetch(source, target):
            copy = pltpu.make_async_copy(source, target, sem_l.at[1])
            copy.start()
            copy.wait()

        def dpre_copy(c, k):
            rows = pl.ds(pl.multiple_of((c - SPLIT) * CHUNK, CHUNK), CHUNK)
            return quad_copy(
                dl.at[span(c), pl.ds(0, 4 * FW)], right_o.at[k - 1, rows], send_z.at[k - 1, c], recv_z.at[k - 1, c], k
            )

        def right_copy(k, c):
            return pltpu.make_async_remote_copy(
                dz16.at[span(c)], dz_o.at[k - 1, span(c)], send_z.at[k - 1, c], recv_z.at[k - 1, c],
                device_id={"dp": quad_peer(me, k)}, device_id_type=MESH,
            )

        def inputs(which):
            if which == 0:
                pairs = [
                    (feats, feats_v),
                    (emb, emb_v),
                    (km, u.at[pl.ds(0, km.shape[0]), pl.ds(0, FW)]),
                    (total, gates.at[:, pl.ds(FW, FW)]),
                ]
                for m in range(4):
                    for half, (row, count) in enumerate(AB_PARTS):
                        target = w.at[pl.ds(0, count), pl.ds((2 * m + half) * FW, FW)]
                        pairs.append((ab.at[m, pl.ds(row, count)], target))
            elif which == 3:
                pairs = [(wt, w)]
            else:
                depth = FW if which == 1 else GW
                pairs = [
                    (ur.at[pl.ds(0, depth)], u.at[pl.ds(0, depth)]),
                    (ur.at[pl.ds(FW, GW)], r),
                    (rt, r_t),
                ]
            return [pltpu.make_async_copy(a, b, sem_in.at[i]) for i, (a, b) in enumerate(pairs)]

        for which in range(4):

            @pl.when(role == which)
            def _(which=which):
                for copy in inputs(which):
                    copy.start()

        @pl.when((role == 1) | (role == 2))
        def _():
            start[...] = jnp.zeros_like(start)
            for which in (1, 2):

                @pl.when(role == which)
                def _(which=which):
                    for half in range(2):
                        start[half, :, pl.ds(0, HID)] = state[which - 1, half]

            for t in range(n // 8):
                rows = pl.ds(8 * t, 8)
                kept = jnp.zeros((8, LANE), F32)
                if t < real_steps:
                    kept = 1.0 - jnp.broadcast_to(resets[:, t : t + 1], (8, LANE)).astype(F32)
                keep[rows, :] = kept

        @pl.when(role == 3)
        def _():
            left_words = jnp.broadcast_to(remaining[...], (8, LANE))
            for t in range(n // 8):
                rows = pl.ds(8 * t, 8)
                if t < real_steps:
                    valid[rows, :] = jnp.where(left_words > t, 1.0, 0.0)
                    targets[rows, :] = jnp.broadcast_to(target_ids[:, t : t + 1], (8, LANE))
                else:
                    valid[rows, :] = jnp.zeros((8, LANE), F32)
                    targets[rows, :] = jnp.full((8, LANE), -1, jnp.int32)

        barrier = pltpu.get_barrier_semaphore()

        @pl.when(role > 0)
        def _():
            pl.semaphore_signal(barrier, inc=1, device_id={"section": role - 1}, device_id_type=MESH)

        @pl.when(role < 3)
        def _():
            pl.semaphore_signal(barrier, inc=1, device_id={"section": role + 1}, device_id_type=MESH)

        for k in range(1, QUAD):
            pl.semaphore_signal(barrier, inc=1, device_id={"dp": quad_peer(me, k)}, device_id_type=MESH)
        pl.semaphore_wait(barrier, lax.min(role, 1) + lax.min(3 - role, 1) + QUAD - 1)

        @pl.when(role == 0)
        def _():
            feature_copy(1).start()
            for copy in inputs(0):
                copy.wait()
            each_peer(lambda k: feats_copy(k).start())
            turn_features(feats_v, turned)
            turned_out(QUAD - 1, LEFT0)
            feature_copy(1).wait_send()
            each_peer(lambda k: feats_copy(k).wait_send())
            for k in range(1, QUAD):
                feats_copy(k).wait_recv()
                fetch(x_q.at[k - 1], feats_v)
                turn_features(feats_v, turned)
                turned_out(k - 1, LEFT0)
            fetch(feats, feats_v)
            stages = ((cells, prevs), (hs, dhs))

            def slope_copies(p, slot):
                left, right = stages[slot]
                return [
                    pltpu.make_async_copy(left, slopes_o.at[p, :, pl.ds(0, GW)], sem_s.at[slot, 0]),
                    pltpu.make_async_copy(
                        right.at[:, pl.ds(0, FW - GW)], slopes_o.at[p, :, pl.ds(GW, FW - GW)], sem_s.at[slot, 1]
                    ),
                ]

            def slopes(p, slot, tile, second, within, limit):
                left, right = stages[slot]
                for at, width in fblocks(FW):
                    target, to_col = (left, at) if at < GW else (right, at - GW)
                    if at >= limit:
                        target[:, pl.ds(to_col, width)] = jnp.zeros((n, width), F32)
                        continue
                    act = jnp.tanh(conv_at(emb_v, u, tile, second, within, at, width))
                    value = jnp.exp(act) * (1.0 - act * act) / gates[:, pl.ds(FW + at, width)]
                    if at + width > limit and limit < FILT:
                        value = jnp.where(column_mask(at, width, limit, n), value, 0.0)
                    target[:, pl.ds(to_col, width)] = value
                for copy in slope_copies(p, slot):
                    copy.start()

            def finish_slopes(p, slot):
                for copy in slope_copies(p, slot):
                    copy.wait()

            def slope_pair(i, carry):
                for slot in range(2):
                    p = 2 * i + slot

                    @pl.when(i > 0)
                    def _(p=p, slot=slot):
                        finish_slopes(p - 2, slot)

                    slopes(p, slot, p // 8, True, lax.rem(p, 8), FILT)
                return carry

            lax.fori_loop(0, 7, slope_pair, 0)
            for p in range(14, WORD_CHARS):
                finish_slopes(p - 2, p % 2)
                tile, within = (1, p - 8) if p < 16 else (2, p - 16)
                slopes(p, p % 2, tile, p < 16, within, FILT if p < 15 else COLS[WORD_CHARS - p])
            for p in (WORD_CHARS - 2, WORD_CHARS - 1):
                finish_slopes(p, p % 2)

            def pres_copy(c, m):
                slot = lax.rem(c, 2)
                target = logits.at[pl.ds(pl.multiple_of(slot * CHUNK, CHUNK), CHUNK), pl.ds(m * FW, FW)]
                return pltpu.make_async_copy(pres.at[m, span(c)], target, sem_p.at[slot, m])

            for m in range(4):
                pres_copy(chunks - 1, m).start()

            def chunk(i, carry):
                c = chunks - 1 - i

                @pl.when(c > 0)
                def _():
                    for m in range(4):
                        pres_copy(c - 1, m).start()

                for m in range(4):
                    pres_copy(c, m).wait()
                last_copy(c, 1).wait_recv()
                highway_chunk(span(c), pl.multiple_of(lax.rem(c, 2) * CHUNK, CHUNK), dy, feats_v, logits, gates, dl, w)

                @pl.when(c >= SPLIT)
                def _():
                    each_peer(lambda k: dpre_copy(c, k).start())

                return carry

            lax.fori_loop(0, chunks, chunk, 0)
            copies = [
                pltpu.make_async_copy(gates.at[:, pl.ds(0, FW)], grad_o, sem_out.at[0]),
                pltpu.make_async_copy(dl.at[:, pl.ds(0, 4 * FW)], dpre_o, sem_out.at[1]),
            ]
            for copy in copies:
                copy.start()
            for at, width in fblocks(FW):
                cols = pl.ds(at, width)
                bias_o[:, cols] = jnp.sum(dl[:, cols].astype(F32), axis=0, keepdims=True)
            for copy in copies:
                copy.wait()

            def settle(c):
                for k in range(1, QUAD):
                    dpre_copy(c, k).wait_send()
                    dpre_copy(c, k).wait_recv()

            each_chunk(settle, SPLIT)

        @pl.when((role == 1) | (role == 2))
        def _():
            for which in (1, 2):

                @pl.when(role == which)
                def _(which=which):
                    for copy in inputs(which):
                        copy.wait()

            bias = r[pl.ds(HID, 1), :].astype(F32)

            @pl.when(role == 1)
            def _():
                feature_copy(-1).wait_recv()
                each_peer(lambda k: input_copy(k).start())
                for at, width in fblocks(ZW):
                    cols = pl.ds(at, width)
                    gates[:, cols] = mm(x1[...], u[:, cols]) + bias[:, at : at + width]

            def chunk_forward(c, carry):
                @pl.when(role == 2)
                def _():
                    forward_copy(c, -1).wait_recv()
                    each_peer(lambda k: layer_copy(c, k).start())
                    for at, width in fblocks(ZW):
                        cols = pl.ds(at, width)
                        gates[span(c), cols] = mm(xb[span(c), :], u[pl.ds(0, GW), cols]) + bias[:, at : at + width]

                carry = lstm_steps(c * steps, steps, keep, carry, r, gates, cells, prevs, hs)
                hb[span(c), :] = hs[span(c), :].astype(BF16)
                forward_copy(c, 1).start()
                pb[span(c), :] = prevs[span(c), :].astype(BF16)
                each_peer(lambda k: hidden_copy(c, k).start())
                return carry

            h0 = start[0].astype(BF16).astype(F32)
            lax.fori_loop(0, chunks, chunk_forward, (h0, start[1]))

            for which in (1, 2):

                @pl.when(role == which)
                def _(which=which):
                    depth, rows = (FILT, LEFT1) if which == 1 else (HID, LEFT2)
                    width = FW if which == 1 else GW
                    turn_inputs(x1 if which == 1 else xb, pb, depth, turned)
                    turned_out(QUAD - 1, rows)
                    if which == 1:
                        each_peer(lambda k: input_copy(k).wait_send())
                        each_peer(lambda k: input_copy(k).wait_recv())
                    else:

                        def moved(c):
                            for k in range(1, QUAD):
                                layer_copy(c, k).wait_send()
                                layer_copy(c, k).wait_recv()

                        each_chunk(moved)

                    def hidden_moved(c):
                        for k in range(1, QUAD):
                            hidden_copy(c, k).wait_send()
                            hidden_copy(c, k).wait_recv()

                    each_chunk(hidden_moved)
                    for g in range(QUAD - 1):
                        fetch(x_q.at[g, 0, :, pl.ds(0, width)], feats_v.at[0, :, pl.ds(0, width)])
                        fetch(h_q.at[g], pb)
                        turn_inputs(feats_v.at[0], pb, depth, turned)
                        turned_out(g, rows)

            def chunk_backward(i, carry):
                c = chunks - 1 - i
                backward_copy(c, 1).wait_recv()
                dhs[span(c), :] = db[span(c), :].astype(F32)
                carry = lstm_back_steps(c * steps, steps, keep, start.at[1], carry, r_t, gates, cells, dhs)
                dz16[span(c), :] = gates[span(c), :].astype(BF16)

                @pl.when(role == 1)
                def _():
                    for at, width in fblocks(FW):
                        value = mm_nt_few(dz16[span(c), :], u[pl.ds(at, width), :])
                        if at + width > FILT:
                            value = jnp.where(column_mask(at, width, FILT, CHUNK), value, 0.0)
                        dy[span(c), pl.ds(at, width)] = value.astype(BF16)
                    last_copy(c, -1).start()

                @pl.when(role == 2)
                def _():
                    for at, width in fblocks(GW):
                        value = mm_nt_few(dz16[span(c), :], u[pl.ds(at, width), :])
                        if at + width > HID:
                            value = jnp.where(column_mask(at, width, HID, CHUNK), value, 0.0)
                        ob[span(c), pl.ds(at, width)] = value.astype(BF16)
                    backward_copy(c, -1).start()

                each_peer(lambda k: right_copy(k, c).start())
                return carry

            zero = jnp.zeros((8, GW), F32)
            lax.fori_loop(0, chunks, chunk_backward, (zero, zero))

            own_right = pltpu.make_async_copy(dz16, dz_o.at[QUAD - 1], sem_out.at[1])
            own_right.start()

            @pl.when(role == 1)
            def _():
                each_chunk(lambda c: last_copy(c, -1).wait_send())

            @pl.when(role == 2)
            def _():
                each_chunk(lambda c: backward_copy(c, -1).wait_send())

            own_right.wait()

            def sent(c, carry):
                forward_copy(c, 1).wait_send()
                for k in range(1, QUAD):
                    right_copy(k, c).wait_send()
                    right_copy(k, c).wait_recv()
                return carry

            lax.fori_loop(0, chunks, sent, 0)

        @pl.when(role == 3)
        def _():
            for copy in inputs(3):
                copy.wait()
            ob[...] = jnp.zeros_like(ob)
            done = 0
            for count in GROUPS_OUT:
                rows = pl.ds(done * CHUNK, count * CHUNK)
                for c in range(done, done + count):
                    forward_copy(c, -1).wait_recv()
                value = xb[rows, pl.ds(5 * LANE, LANE)].astype(F32)
                value = jnp.where(lanes(count * CHUNK) + 5 * LANE == HID, 1.0, value)
                xb[rows, pl.ds(5 * LANE, LANE)] = value.astype(BF16)
                output_rows(
                    done * CHUNK, count * CHUNK, xb, w, targets, valid, logits, dl, top, part, dh, loss, ob
                )
                for c in range(done, done + count):
                    backward_copy(c, -1).start()
                done += count
            copies = [
                pltpu.make_async_copy(xb, xb_o, sem_out.at[0]),
                pltpu.make_async_copy(dl, dl_o, sem_out.at[1]),
            ]
            for copy in copies:
                copy.start()
            for c in range(chunks):
                backward_copy(c, -1).wait_send()
            for copy in copies:
                copy.wait()

        loss_o[...] = loss[...]

    most = max(GROUPS_OUT) * CHUNK
    sems = pltpu.SemaphoreType.DMA
    outs = [
        ((WORD_CHARS, n, FW), F32), ((n, FW), F32), ((n, 4 * FW), BF16), ((QUAD - 1, n - SPLIT * CHUNK, 4 * FW), BF16), ((n, GW), BF16),
        ((QUAD, LEFT_ROOM, n), BF16), ((QUAD, n, ZW), BF16), ((n, VW), BF16), ((QUAD - 1, 2, n, FW), BF16),
        ((QUAD - 1, n, GW), BF16),
    ]
    scratch = [
        vmem((3, n, LANE), BF16), vmem((n, LANE), F32), vmem((n, LANE), F32), vmem((n, LANE), jnp.int32),
        vmem((2, n, FW), BF16), vmem((LEFT0, n), BF16), vmem((n, GW), BF16),
        vmem((n, FW), BF16), vmem((n, GW), BF16), vmem((n, GW), BF16), vmem((n, GW), BF16), vmem((n, GW), BF16),
        vmem((n, FW), BF16), vmem((FW, ZW), BF16), vmem((GW, ZW), BF16), vmem((ZW, GW), BF16), vmem(wt.shape, BF16),
        vmem((2, 8, GW), F32), vmem((n, ZW), F32), vmem((n, GW), F32), vmem((n, GW), F32), vmem((n, GW), F32),
        vmem((n, GW), F32), vmem((n, ZW), BF16),
        vmem((most, VW), F32), vmem((n, VW), BF16), vmem((most, LANE), F32), vmem((2, most, LANE), F32),
        vmem((depth_w, LANE), F32), vmem((1, LANE), F32),
        dmas(12), dmas(3), dmas(1), dmas(1), dmas(chunks), dmas(chunks), dmas(chunks), dmas(chunks), dmas(chunks), dmas(chunks),
        sems((QUAD - 1, chunks)), sems((QUAD - 1, chunks)), sems((QUAD - 1, chunks)), sems((QUAD - 1, chunks)),
        sems((QUAD - 1, chunks)), sems((QUAD - 1, chunks)), dmas(2), sems((2, 4)), sems((2, 2)),
    ]
    return pl.pallas_call(
        kernel,
        out_shape=[jax.ShapeDtypeStruct(shape, dtype) for shape, dtype in outs]
        + [jax.ShapeDtypeStruct((1, LANE), F32), jax.ShapeDtypeStruct((1, FW), F32)],
        in_specs=[ANYWHERE] * 10 + [ON_CHIP] * 4,
        out_specs=[ANYWHERE] * 10 + [ON_CHIP] * 2,
        scratch_shapes=scratch,
        compiler_params=pltpu.CompilerParams(vmem_limit_bytes=62 << 20, collective_id=3, has_side_effects=True),
        name="recurrent",
    )(y2, feats, pres, ab, km, emb, total, ur, rt, wt, resets, target_ids, remaining, state)


FORM = (
    (FILT, 9, 4 * (FILT + 1), CONV_END, CONV_TILES, 32),
    (4 * HID, 24, FILT + HID + 1, 0, 0, 16),
    (4 * HID, 24, 2 * HID + 1, 0, 0, 16),
    (VOCAB, 79, HID + 1, 0, 0, 16),
)


def slab(role, dest, share):
    width, pitch, rows, before, lead, period = FORM[role]
    low = lax.max if not isinstance(dest, int) else max
    high = lax.min if not isinstance(dest, int) else min
    one = (lambda v: v) if isinstance(dest, int) else jnp.int32
    start = low(one(share) * dest - before, one(0))
    first = start // width // period * period
    end = high((share * (dest + 1) - before + width - 1) // width, one(rows))
    count = low((end - first + 15) // 16, one(0)) * pitch
    tile = lead + first // 16 * pitch
    if lead:
        if isinstance(dest, int):
            if dest == 0:
                tile, count = 0, count + lead
        else:
            head = lax.max(1 - dest, 0)
            tile = tile - lead * head
            count = count + lead * head
    return first, tile, count


def slab_pieces(count, size):
    return (count + size - 1) // size


def gather_sum_call(tiles, groups, share):
    pair = 2
    across = groups // pair
    size = 64 if across <= 4 else 32
    pieces = max(slab_pieces(slab(3, dest, share)[2], size) for dest in range(groups))
    room = pieces * size
    line = across <= 4
    slots = across + 1 if line else across - 1
    MESH = pl.DeviceIdType.MESH

    def kernel(
        tiles, out, own, got1, got2, acc, own_sem, send1, recv1, send2, recv2, out_sem,
    ):
        role = lax.axis_index("section")
        me = lax.axis_index("dp")
        mine, side = me // pair, lax.rem(me, pair)
        other = mine * pair + (1 - side)

        def at_place(place):
            return {"dp": place * pair + side}

        def part(ref, slot, p):
            return ref.at[slot, pl.ds(pl.multiple_of(p * size, size), size)]

        def span(p):
            return pl.ds(pl.multiple_of(p * size, size), size)

        def loop(count, body):
            def step(p, carry):
                body(p)
                return carry

            lax.fori_loop(0, count, step, 0)

        def run(shape_of):
            def count_to(place, which):
                return shape_of(place * pair + which)[1]

            def own_copy(place, p):
                tile, _ = shape_of(place * pair + side)
                return pltpu.make_async_copy(
                    tiles.at[pl.ds(tile + p * size, size)], part(own, place, p), own_sem.at[place, p]
                )

            def first_copy(place, p):
                tile, _ = shape_of(place * pair + 1 - side)
                return pltpu.make_async_remote_copy(
                    tiles.at[pl.ds(tile + p * size, size)], part(got1, place, p), send1.at[place, p], recv1.at[place, p],
                    device_id={"dp": other}, device_id_type=MESH,
                )

            def begin(place):
                loop(count_to(place, 1 - side), lambda p: first_copy(place, p).start())
                loop(count_to(place, side), lambda p: own_copy(place, p).start())

            def hop_copy(place, up, p):
                if line:
                    target = mine + 1 if up else mine - 1
                    slot = jnp.where(place == mine + 1, across, place) if up else place
                else:
                    target = place
                    slot = lax.rem(place - mine + across, across) - 1
                return pltpu.make_async_remote_copy(
                    part(own, place, p), part(got2, slot, p), send2.at[place, p], recv2.at[slot, p],
                    device_id=at_place(target), device_id_type=MESH,
                )

            def arrived(slot, p):
                return pltpu.make_async_remote_copy(
                    part(own, 0, p), part(got2, slot, p), send2.at[0, p], recv2.at[slot, p],
                    device_id=at_place(lax.rem(mine + 1, across)), device_id_type=MESH,
                )

            def forward(place, up, has_before):
                def body(p):
                    own_copy(place, p).wait()
                    first_copy(place, p).wait_recv()
                    at = span(p)
                    own[place, at] = (own[place, at].astype(F32) + got1[place, at].astype(F32)).astype(BF16)
                    hop_copy(place, up, p).start()

                def body_sum(p):
                    own_copy(place, p).wait()
                    first_copy(place, p).wait_recv()
                    arrived(place, p).wait_recv()
                    at = span(p)
                    total = own[place, at].astype(F32) + got1[place, at].astype(F32) + got2[place, at].astype(F32)
                    own[place, at] = total.astype(BF16)
                    hop_copy(place, up, p).start()

                count = count_to(place, side)
                if not line:
                    loop(count, body)
                    return

                @pl.when(has_before)
                def _():
                    loop(count, body_sum)

                @pl.when(jnp.logical_not(has_before))
                def _():
                    loop(count, body)

            if line:
                for k in range(across - 1):

                    @pl.when(k < mine)
                    def _(k=k):
                        begin(k)

                    @pl.when(k < across - 1 - mine)
                    def _(k=k):
                        begin(across - 1 - k)

                begin(mine)
                for k in range(across - 1):

                    @pl.when(k < mine)
                    def _(k=k):
                        forward(k, False, mine < across - 1)

                    @pl.when(k < across - 1 - mine)
                    def _(k=k):
                        forward(across - 1 - k, True, mine > 0)

            else:
                for k in range(1, across):
                    begin(lax.rem(mine + k, across))
                begin(mine)
                for k in range(1, across):
                    forward(lax.rem(mine + k, across), True, None)

            def settle(p):
                own_copy(mine, p).wait()
                first_copy(mine, p).wait_recv()
                at = span(p)
                acc[at] = own[mine, at].astype(F32) + got1[mine, at].astype(F32)

            def add(slot):
                def body(p):
                    arrived(slot, p).wait_recv()
                    at = span(p)
                    acc[at] += got2[slot, at].astype(F32)

                return body

            mine_count = count_to(mine, side)
            loop(mine_count, settle)
            if line:

                @pl.when(mine < across - 1)
                def _():
                    loop(mine_count, add(mine))

                @pl.when(mine > 0)
                def _():
                    loop(mine_count, add(across))

            else:
                for k in range(1, across):
                    loop(mine_count, add(k - 1))

            def out_copy(p):
                return pltpu.make_async_copy(acc.at[span(p)], out.at[span(p)], out_sem.at[p])

            loop(mine_count, lambda p: out_copy(p).start())
            loop(mine_count, lambda p: out_copy(p).wait())
            for place in range(across):
                loop(count_to(place, 1 - side), lambda p, place=place: first_copy(place, p).wait_send())

                @pl.when(place != mine)
                def _(place=place):
                    loop(count_to(place, side), lambda p: hop_copy(place, True, p).wait_send())

        def shape_of(dest):
            _, tile, count = slab(3, dest, share)
            return tile, slab_pieces(count, size)

        @pl.when(role == 3)
        def _():
            barrier = pltpu.get_barrier_semaphore()
            pl.semaphore_signal(barrier, inc=1, device_id={"dp": other}, device_id_type=MESH)
            for k in range(1, across):
                peer = at_place(lax.rem(mine + k, across))
                pl.semaphore_signal(barrier, inc=1, device_id=peer, device_id_type=MESH)
            pl.semaphore_wait(barrier, across)
            run(shape_of)

    sems = pltpu.SemaphoreType.DMA
    return pl.pallas_call(
        kernel,
        out_shape=jax.ShapeDtypeStruct((room, 16, LANE), F32),
        in_specs=[ANYWHERE],
        out_specs=ANYWHERE,
        scratch_shapes=[
            vmem((across, room, 16, LANE), BF16), vmem((across, room, 16, LANE), BF16),
            vmem((slots, room, 16, LANE), BF16), vmem((room, 16, LANE), F32),
            sems((across, pieces)), sems((across, pieces)), sems((across, pieces)),
            sems((across, pieces)), sems((slots, pieces)), sems((pieces,)),
        ],
        compiler_params=pltpu.CompilerParams(vmem_limit_bytes=62 << 20, collective_id=1, has_side_effects=True),
        name="gather_sum",
    )(tiles)


BLOCK_ROWS = (25, 11, 11)


def finish_call(lhs, dz, dpre, rights, conv, bias, loss, after, groups, share):
    n = lhs.shape[2]
    quads = groups // QUAD
    MESH = pl.DeviceIdType.MESH

    def most_blocks(role):
        width = FORM[role][1]
        lead = FORM[role][4]
        most = 0
        for dest in range(groups):
            count = slab(role, dest, share)[2]
            if lead and dest == 0:
                count -= lead
            most = max(most, -(-(count // width) // BLOCK_ROWS[role]))
        return most

    blocks = [most_blocks(role) for role in range(3)]
    room = max(
        FORM[role][4] + blocks[role] * BLOCK_ROWS[role] * FORM[role][1] for role in range(3)
    )
    left_rows = max(blocks[role] * BLOCK_ROWS[role] * 16 for role in range(3))
    most = max(blocks)

    def kernel(
        lhs, dz, dpre, late, early, conv, bias, loss, after, out, small_out,
        left, dpre_v, sent, got, acc, convs, lead_sum, small, got_small,
        sem_left, sem_right, send, recv, send_c, recv_c, small_send, small_recv, sem_out,
    ):
        role = lax.axis_index("section")
        me = lax.axis_index("dp")
        place, quad = lax.rem(me, QUAD), me // QUAD

        def across_peer(k):
            return {"dp": place + QUAD * lax.rem(quad + k, quads)}

        barrier = pltpu.get_barrier_semaphore()
        for k in range(1, QUAD):
            pl.semaphore_signal(barrier, inc=1, device_id={"dp": quad_peer(me, k)}, device_id_type=MESH)
        for k in range(1, quads):
            pl.semaphore_signal(barrier, inc=1, device_id=across_peer(k), device_id_type=MESH)

        def right_load(b):
            return pltpu.make_async_copy(
                dz.at[:, :, pl.ds(GW * b, GW)], dpre_v.at[:, b, :, pl.ds(0, GW)], sem_right.at[b]
            )

        def right_loads0():
            copies = []
            cut = SPLIT * CHUNK
            for b in range(4):
                cols = pl.ds(FW * b, FW)
                pairs = [
                    (early.at[:, :, cols], dpre_v.at[pl.ds(0, QUAD - 1), b, pl.ds(0, cut)]),
                    (late.at[:, :, cols], dpre_v.at[pl.ds(0, QUAD - 1), b, pl.ds(cut, n - cut)]),
                    (dpre.at[:, cols], dpre_v.at[QUAD - 1, b]),
                ]
                copies += [pltpu.make_async_copy(x, y, sem_right.at[4 + 3 * b + i]) for i, (x, y) in enumerate(pairs)]
            return copies

        def conv_load():
            return pltpu.make_async_copy(conv, convs.at[QUAD - 1], sem_right.at[16])

        @pl.when(role == 0)
        def _():
            for copy in right_loads0():
                copy.start()
            conv_load().start()

        @pl.when((role == 1) | (role == 2))
        def _():
            for b in range(4):
                right_load(b).start()

        pl.semaphore_wait(barrier, QUAD - 1 + quads - 1)

        small[...] = jnp.zeros_like(small)

        @pl.when(role == 0)
        def _():
            small[0, :, pl.ds(0, FW)] = bias[...]

        @pl.when(role == 3)
        def _():
            small[0, :, pl.ds(FW, LANE)] = loss[...]

        def small_copy(k):
            if k < QUAD:
                source, target = small.at[0], {"dp": quad_peer(me, k)}
            else:
                source, target = small.at[1], across_peer(k - QUAD + 1)
            return pltpu.make_async_remote_copy(
                source, got_small.at[k - 1], small_send.at[k - 1], small_recv.at[k - 1],
                device_id=target, device_id_type=MESH,
            )

        for k in range(1, QUAD):
            small_copy(k).start()

        def conv_copy(slot, target):
            return pltpu.make_async_remote_copy(
                conv, convs.at[slot], send_c.at[slot], recv_c.at[slot], device_id={"dp": target}, device_id_type=MESH
            )

        def run(which):
            width, pitch, rows, _, lead, _ = FORM[which]
            size = BLOCK_ROWS[which]
            block_tiles = size * pitch

            def geometry(k):
                dest = place + QUAD * lax.rem(quad + k, quads)
                first, _, count = slab(which, dest, share)
                if lead:
                    head = lax.max(1 - dest, 0)
                    count = count - lead * head
                else:
                    head = 0
                return first, (count // pitch + size - 1) // size, head

            def left_copy(k):
                height = blocks[which] * size * 16
                first = lax.min(geometry(k)[0], LEFT_ROOM - height)
                span = pl.ds(pl.multiple_of(first, 16), height)
                return pltpu.make_async_copy(
                    lhs.at[:, span], left.at[lax.rem(k, 2), :, pl.ds(0, blocks[which] * size * 16)], sem_left.at[lax.rem(k, 2)]
                )

            def block_copy(k, b):
                span = pl.ds(CONV_TILES + b * block_tiles, block_tiles)
                return pltpu.make_async_remote_copy(
                    sent.at[k - 1, span], got.at[k - 1, span], send.at[k - 1, b], recv.at[k - 1, b],
                    device_id=across_peer(k), device_id_type=MESH,
                )

            def lead_copy(k):
                span = pl.ds(0, CONV_TILES)
                return pltpu.make_async_remote_copy(
                    sent.at[k - 1, span], got.at[k - 1, span], send.at[k - 1, most], recv.at[k - 1, most],
                    device_id=across_peer(k), device_id_type=MESH,
                )

            def put(k, own, at, value):
                if own:
                    acc[at] = value
                else:
                    sent[k - 1, at] = value.astype(BF16)

            def block(k, own, b, first):
                here = pl.ds(pl.multiple_of(b * size * 16, 16), size * 16)
                base = CONV_TILES + b * block_tiles
                if which == 0:
                    row = lax.broadcasted_iota(jnp.int32, (size * 16, n), 0) + first + b * size * 16
                    start = first + b * size * 16
                    low = lax.min(start // (FILT + 1), 3)
                    high = lax.min((start + size * 16 - 1) // (FILT + 1), 3)
                    edge = (FILT + 1) * (low + 1)
                    lefts = [left[lax.rem(k, 2), g, here, :] for g in range(QUAD)]
                    near = [jnp.where(row < edge, x, jnp.zeros_like(x)) for x in lefts]
                    for col, wide in fblocks(FW):
                        value = jnp.zeros((size * 16, wide), F32)
                        for g in range(QUAD):
                            value = value + mm(near[g], dpre_v[g, low, :, pl.ds(col, wide)])
                        for r in range(size):
                            for c in range(wide // LANE):
                                tile = value[16 * r : 16 * r + 16, LANE * c : LANE * c + LANE]
                                put(k, own, base + r * pitch + col // LANE + c, tile)

                    @pl.when(high > low)
                    def _():
                        far = [jnp.where(row < edge, jnp.zeros_like(x), x) for x in lefts]
                        for col, wide in fblocks(FW):
                            value = jnp.zeros((size * 16, wide), F32)
                            for g in range(QUAD):
                                value = value + mm(far[g], dpre_v[g, high, :, pl.ds(col, wide)])
                            for r in range(size):
                                for c in range(wide // LANE):
                                    tile = value[16 * r : 16 * r + 16, LANE * c : LANE * c + LANE]
                                    at = base + r * pitch + col // LANE + c
                                    old = acc[at] if own else sent[k - 1, at].astype(F32)
                                    put(k, own, at, old + tile)

                else:
                    for col, wide in fblocks(ZW):
                        value = jnp.zeros((size * 16, wide), F32)
                        for g in range(QUAD):
                            value = value + mm(left[lax.rem(k, 2), g, here, :], dpre_v[g, col // GW, :, pl.ds(col % GW, wide)])
                        for r in range(size):
                            for c in range(wide // LANE):
                                tile = value[16 * r : 16 * r + 16, LANE * c : LANE * c + LANE]
                                put(k, own, base + r * pitch + col // LANE + c, tile)

            def loop(count, body):
                def step(b, carry):
                    body(b)
                    return carry

                lax.fori_loop(0, count, step, 0)

            left_copy(jnp.int32(1 % quads)).start()
            if which == 0:

                @pl.when(place > 0)
                def _():
                    for k in range(1, QUAD):

                        @pl.when(place == k)
                        def _(k=k):
                            conv_copy(k - 1, me - k).start()

                for copy in right_loads0():
                    copy.wait()
                conv_load().wait()
            else:
                for b in range(4):
                    right_load(b).wait()

            if which == 0:

                @pl.when(place == 0)
                def _():
                    for k in range(1, QUAD):
                        conv_copy(k - 1, me + k).wait_recv()
                    total = convs[0].astype(F32)
                    for k in range(1, QUAD):
                        total = total + convs[k].astype(F32)
                    lead_sum[...] = total

            def slab_of(k, own):
                left_copy(k).wait()
                if not own:
                    left_copy(lax.rem(k + 1, quads)).start()
                first, count, head = geometry(k)
                if which == 0:

                    @pl.when(head > 0)
                    def _():
                        if own:
                            acc[pl.ds(0, CONV_TILES)] = lead_sum[...]
                        else:
                            sent[k - 1, pl.ds(0, CONV_TILES)] = lead_sum[...].astype(BF16)
                            lead_copy(k).start()

                def work(b):
                    block(k, own, b, first)
                    if not own:
                        block_copy(k, b).start()

                loop(count, work)

            def others(body):
                def step(k, carry):
                    body(k)
                    return carry

                lax.fori_loop(1, quads, step, 0)

            others(lambda k: slab_of(k, False))
            slab_of(jnp.int32(0), True)

            _, mine, head = geometry(0)
            def join(k):
                def add(b):
                    block_copy(k, b).wait_recv()
                    span = pl.ds(CONV_TILES + b * block_tiles, block_tiles)
                    acc[span] += got[k - 1, span].astype(F32)

                loop(mine, add)
                if which == 0:

                    @pl.when(head > 0)
                    def _():
                        lead_copy(k).wait_recv()
                        span = pl.ds(0, CONV_TILES)
                        acc[span] += got[k - 1, span].astype(F32)

            others(join)

            span = blocks[which] * block_tiles
            if which == 0:

                @pl.when(head > 0)
                def _():
                    copy = pltpu.make_async_copy(
                        acc.at[pl.ds(0, CONV_TILES + span)], out.at[pl.ds(0, CONV_TILES + span)], sem_out.at[0]
                    )
                    copy.start()
                    copy.wait()

                @pl.when(head == 0)
                def _():
                    copy = pltpu.make_async_copy(acc.at[pl.ds(CONV_TILES, span)], out.at[pl.ds(0, span)], sem_out.at[0])
                    copy.start()
                    copy.wait()

            else:
                copy = pltpu.make_async_copy(acc.at[pl.ds(CONV_TILES, span)], out.at[pl.ds(0, span)], sem_out.at[0])
                copy.start()
                copy.wait()

            def sent_all(k):
                _, count, head = geometry(k)
                loop(count, lambda b: block_copy(k, b).wait_send())
                if which == 0:

                    @pl.when(head > 0)
                    def _():
                        lead_copy(k).wait_send()

            others(sent_all)

            if which == 0:
                for k in range(1, QUAD):

                    @pl.when(place == k)
                    def _(k=k):
                        conv_copy(k - 1, me - k).wait_send()

        for k in range(1, QUAD):
            small_copy(k).wait_recv()
        small[1] = small[0] + got_small[0] + got_small[1] + got_small[2]
        for k in range(QUAD, QUAD + quads - 1):
            small_copy(k).start()

        for which in range(3):

            @pl.when(role == which)
            def _(which=which):
                run(which)

        total = small[1]
        for k in range(QUAD, QUAD + quads - 1):
            small_copy(k).wait_recv()
            total = total + got_small[k - 1]
        small_out[...] = total
        for k in range(1, QUAD + quads - 1):
            small_copy(k).wait_send()

    sems = pltpu.SemaphoreType.DMA
    full = CONV_TILES + max(blocks[role] * BLOCK_ROWS[role] * FORM[role][1] for role in range(3))
    smalls = QUAD + quads - 2
    return pl.pallas_call(
        kernel,
        out_shape=[jax.ShapeDtypeStruct((full, 16, LANE), F32), jax.ShapeDtypeStruct((1, FW + LANE), F32)],
        in_specs=[ANYWHERE] * 6 + [ON_CHIP] * 2 + [ANYWHERE],
        out_specs=[ANYWHERE, ON_CHIP],
        scratch_shapes=[
            vmem((2, QUAD, left_rows, n), BF16), vmem((QUAD, 4, n, FW), BF16),
            vmem((quads - 1, full, 16, LANE), BF16), vmem((quads - 1, full, 16, LANE), BF16),
            vmem((full, 16, LANE), F32), vmem((QUAD, CONV_TILES, 16, LANE), BF16), vmem((CONV_TILES, 16, LANE), F32),
            vmem((2, 1, FW + LANE), F32), vmem((smalls, 1, FW + LANE), F32),
            sems((2,)), sems((17,)), sems((quads - 1, most + 1)), sems((quads - 1, most + 1)),
            sems((QUAD - 1,)), sems((QUAD - 1,)), sems((smalls,)), sems((smalls,)), sems((1,)),
        ],
        compiler_params=pltpu.CompilerParams(vmem_limit_bytes=62 << 20, collective_id=5, has_side_effects=True),
        name="finish",
    )(lhs, dz, dpre, *rights, conv, bias, loss, after)


def sections_sum_call(small):
    count = lax.axis_size("section")

    def kernel(mine, out, held, send, recv):
        me = lax.axis_index("section")
        barrier = pltpu.get_barrier_semaphore()

        def peer(k):
            return {"section": lax.rem(me + k, count)}

        for k in range(1, count):
            pl.semaphore_signal(barrier, inc=1, device_id=peer(k), device_id_type=pl.DeviceIdType.MESH)
        pl.semaphore_wait(barrier, count - 1)
        copies = [
            pltpu.make_async_remote_copy(
                mine, held.at[k], send.at[k], recv.at[k], device_id=peer(k), device_id_type=pl.DeviceIdType.MESH
            )
            for k in range(1, count)
        ]
        for copy in copies:
            copy.start()
        total = mine[...]
        for k, copy in enumerate(copies):
            copy.wait_recv()
            total = total + held[k + 1]
        out[...] = total
        for copy in copies:
            copy.wait_send()

    return pl.pallas_call(
        kernel,
        out_shape=jax.ShapeDtypeStruct(small.shape, F32),
        in_specs=[ON_CHIP],
        out_specs=ON_CHIP,
        scratch_shapes=[vmem((count,) + small.shape, F32), dmas(count), dmas(count)],
        compiler_params=pltpu.CompilerParams(collective_id=2, has_side_effects=True),
        name="sections_sum",
    )(small)


def pack_call(summed, summed3, groups, share):
    rooms = (summed.shape[0] * 16, summed3.shape[0] * 16)
    chunks = share // LANE
    margin = 1280
    slab_rows = 10624
    flat_rows = margin + max(10752, chunks + 1280)

    def kernel(summed, summed3, out, rows_v, spaced, flat, sem):
        role = lax.axis_index("section")
        me = lax.axis_index("dp")
        zero = jnp.zeros((64, LANE), F32)

        def clear(i, carry):
            flat[pl.ds(pl.multiple_of(i * 64, 64), 64), :] = zero
            return carry

        def fetch(source, room):
            return pltpu.make_async_copy(source, rows_v.at[pl.ds(0, room)], sem.at[0])

        @pl.when(role < 3)
        def _():
            fetch(summed, rooms[0]).start()

        @pl.when(role == 3)
        def _():
            fetch(summed3, rooms[1]).start()

        lax.fori_loop(0, flat_rows // 64, clear, 0)

        @pl.when(role < 3)
        def _():
            fetch(summed, rooms[0]).wait()

        @pl.when(role == 3)
        def _():
            fetch(summed3, rooms[1]).wait()

        lane = lanes()

        for which in range(4):
            width, pitch, rows, before, lead, period = FORM[which]
            if which == 0:
                blocks, cols, tiles = 1, FILT, 9
            elif which == 3:
                blocks, cols, tiles = 1, VOCAB, 79
            else:
                blocks, cols, tiles = 4, HID, 6
            stride = period * width // LANE
            most = max(slab(which, dest, share)[2] for dest in range(groups))
            groups8 = -(-(-(-most // pitch) * 16) // (8 * period))

            @pl.when(role == which)
            def _(which=which):
                first, _, count = slab(which, me, share)
                skip = lead * lax.max(1 - me, 0)
                step_rows = pitch * 49 + (pitch * 49 + 1) % 2

                def space(rt, carry):
                    for c in range(pitch):
                        for half in range(2):
                            at = pl.multiple_of((skip + rt * pitch + c) * 16 + 8 * half, 8)
                            spaced[pl.ds(rt * step_rows + 49 * c + 24 * half, 8, stride=3), :] = rows_v[pl.ds(at, 8), :]
                    return carry

                lax.fori_loop(0, (count - skip) // pitch, space, 0)
                base = margin + before // LANE + stride * (first // period) - chunks * me

                def row(i, carry):
                    group, n = i // period, lax.rem(i, period)
                    number = first + period * (8 * group + sublanes()) + n
                    keep = number < rows
                    hop = period // 16 * step_rows
                    source = n // 16 * step_rows + 3 * lax.rem(n, 16) + 8 * group * hop
                    step = 27
                    for b in range(blocks):
                        flat_at = before % LANE + width * n + cols * b
                        turn = lax.rem(flat_at, LANE)
                        to = base + flat_at // LANE + stride * 8 * group
                        last = jnp.zeros((8, LANE), F32)
                        for low in range(0, tiles, step):
                            high = min(low + step, tiles)
                            taken = [
                                spaced[pl.ds(source + 49 * (tiles * b + j), 8, stride=hop), :]
                                for j in range(low, high)
                            ]
                            turned = [last] + [pltpu.roll(jnp.where(keep, x, 0.0), turn, 1) for x in taken]
                            for j in range(low, high):
                                value = jnp.where(lane >= turn, turned[j - low + 1], turned[j - low])
                                where = pl.ds(to + j, 8, stride=stride)
                                if j == 0:
                                    value = jnp.where(lane >= turn, value, flat[where, :])
                                flat[where, :] = value
                            last = turned[-1]
                        where = pl.ds(to + tiles, 8, stride=stride)
                        flat[where, :] = jnp.where(lane + LANE * tiles - turn < cols, last, flat[where, :])
                    return carry

                @pl.when(count > 0)
                def _():
                    lax.fori_loop(0, period * groups8, row, 0)

        @pl.when((role == 0) & (me == 0))
        def _():
            lane1 = lanes(1)

            def piece(row_at, flat_at, low, size):
                edge = flat_at - low
                turn = edge % LANE
                to = margin + (edge - turn) // LANE
                first, end = low // LANE, (low + size - 1) // LANE
                last = jnp.zeros((1, LANE), F32)
                for j in range(first, end + 2):
                    least, most = max(low + turn - LANE * j, 0), min(low + size + turn - LANE * j, LANE)
                    here = last
                    if j <= end:
                        here = rows_v[row_at + 16 * j : row_at + 16 * j + 1, :]
                        here = pltpu.roll(here, turn, 1) if turn else here
                    if most > least:
                        value = jnp.where(lane1 >= turn, here, last) if turn else here
                        at = to + j
                        if least > 0 or most < LANE:
                            value = jnp.where((lane1 >= least) & (lane1 < most), value, flat[at : at + 1, :])
                        flat[at : at + 1, :] = value
                    last = here

            for k in range(1, 8):
                n = NFILT[k - 1]
                for i in range(k * D_CHAR + 1):
                    number = i + i // D_CHAR if i < k * D_CHAR else 15
                    piece(number // 16 * 144 + number % 16, KOFF[k - 1] + n * i, COLS[k - 1], n)
            for a in range(CHAR_V):
                piece(72 * 16 + a, D_CHAR * a, 0, D_CHAR)

        copy = pltpu.make_async_copy(flat.at[pl.ds(margin, chunks)], out, sem.at[0])
        copy.start()
        copy.wait()

    return pl.pallas_call(
        kernel,
        out_shape=jax.ShapeDtypeStruct((chunks, LANE), F32),
        in_specs=[ANYWHERE] * 2,
        out_specs=ANYWHERE,
        scratch_shapes=[
            vmem((slab_rows, LANE), F32), vmem((31104, LANE), F32), vmem((flat_rows, LANE), F32), dmas(1),
        ],
        compiler_params=pltpu.CompilerParams(vmem_limit_bytes=LIMIT),
        name="pack",
    )(summed.reshape(rooms[0], LANE), summed3.reshape(rooms[1], LANE))


def shards(char_ids, target_ids, remaining, resets, start_state, section_params):
    rows, steps = char_ids.shape[:2]
    groups = lax.axis_size("dp")
    packed = section_params.shape[1]
    share = packed // groups
    n = rows * (steps + 1)

    ids = jnp.pad(
        char_ids.transpose(1, 0, 2), ((0, 1), (0, 0), (0, LANE - WORD_CHARS)), constant_values=-1
    ).reshape(n, LANE)
    km, e8, ab, ur, rt, wt = unpack_all(section_params)
    y2, *char_saved = char_forward_call(ids, km, e8, ab)
    feats, pres, total, emb = char_saved
    slopes, grad, dpre, late, xb, lhs, dz, dl, _, _, loss, bias = recurrent_call(
        y2, feats, pres, ab, km, emb, total, ur, rt, wt, resets, target_ids, remaining.reshape(rows, 1), start_state
    )
    tiles3 = output_weights_call(xb, dl)
    summed3 = gather_sum_call(tiles3, groups, share)
    conv, early = char_backward_call(ids, grad, km, emb, slopes, dpre)
    summed, small = finish_call(lhs, dz, dpre, (late, early), conv, bias, loss, summed3, groups, share)
    flat = pack_call(summed, summed3, groups, share)
    small = sections_sum_call(small)
    mean_loss = small[0, FW] / (groups * rows * steps)
    return mean_loss, flat.reshape(1, share), small[0, :FILT]


def solution(mesh):
    in_specs = (
        P("dp", None, None),
        P("dp", None),
        P("dp"),
        P("dp", None),
        P(None, None, "dp", None),
        P("section", None),
    )
    out_specs = (P(), P("section", "dp"), P())
    return jax.shard_map(shards, mesh=mesh, in_specs=in_specs, out_specs=out_specs, check_vma=False)
```

```python
import functools
import math

import jax
import jax.numpy as jnp
from jax import lax
from jax.experimental import pallas as pl
from jax.experimental.pallas import tpu as pltpu
from jax.sharding import PartitionSpec as P

D_CHAR = 15
CHAR_V = 51
F_UNIT = 50
WORD_CHARS = 21
HID = 650
VOCAB = 10000
FILT = 1100
F32 = jnp.float32
BF16 = jnp.bfloat16

NFILT = [F_UNIT * min(k, 4) for k in range(1, 8)]
COLS = [sum(NFILT[:k]) for k in range(8)]
KOFF = [CHAR_V * D_CHAR + sum((j * D_CHAR + 1) * NFILT[j - 1] for j in range(1, k)) for k in range(1, 9)]
CONV_END = KOFF[7]
HIGH_STRIDE = FILT * (FILT + 1)
FW = 1152
GW = 768
ZW = 4 * GW
VW = 10112
LANE = 128
LENS = (2304, 2688, 2688, 5120)


def roll_lanes(x, shift):
    return pltpu.roll(x, shift, 1)


def lanes(rows=8):
    return lax.broadcasted_iota(jnp.int32, (rows, LANE), 1)


def sublanes():
    return lax.broadcasted_iota(jnp.int32, (8, LANE), 0)


def widen(raw, slot, rows, wide):
    def body(i, carry):
        piece = raw[slot, 0:1, pl.ds(pl.multiple_of(i * 16384, 16384), 16384)]
        wide[pl.ds(pl.multiple_of(i * 128, 128), 128), :] = piece.astype(F32).reshape(128, LANE)
        return carry

    lax.fori_loop(0, rows // 128, body, 0)


DEPTH = 4


def stream_start(count, length, total, chunk_of, src, raw, sem):
    for i in range(DEPTH - 1):
        stream_copy(jnp.int32(i), length, total, chunk_of, src, raw, sem).start()


def stream_at(i, length, total, chunk_of):
    return jnp.minimum(chunk_of(i) // 8 * 8, total - length)


def stream_copy(i, length, total, chunk_of, src, raw, sem):
    at = pl.multiple_of(stream_at(i, length, total, chunk_of) * LANE, 8 * LANE)
    slot = lax.rem(i, DEPTH)
    return pltpu.make_async_copy(
        src.at[:, pl.ds(at, length * LANE)], raw.at[slot, :, pl.ds(0, length * LANE)], sem.at[slot]
    )


def stream_blocks(count, length, total, chunk_of, src, raw, sem, wide, work):
    def body(i, carry):
        @pl.when(i + DEPTH - 1 < count)
        def _():
            stream_copy(i + DEPTH - 1, length, total, chunk_of, src, raw, sem).start()

        stream_copy(i, length, total, chunk_of, src, raw, sem).wait()
        widen(raw, lax.rem(i, DEPTH), length, wide)
        work(i, chunk_of(i) - stream_at(i, length, total, chunk_of))
        return carry

    lax.fori_loop(0, count, body, 0)


def take_rows(wide, starts, tiles, cols, stride, put):
    step = max(6, 40 // len(starts))
    lane = lanes()
    for low in range(0, tiles, step):
        high = min(tiles, low + step)
        loaded = [
            [wide[pl.ds(first + c, 8, stride=stride), :] for c in range(low, high + 1)] for _, first, _, _ in starts
        ]
        results = []
        for (_, _, shift, keep_row), pieces in zip(starts, loaded):
            turn = lax.rem(LANE - shift, LANE)
            split = lane < LANE - shift
            turned = [roll_lanes(piece, turn) for piece in pieces]
            for c in range(low, high):
                out = jnp.where(split, turned[c - low], turned[c - low + 1])
                keep = keep_row
                if cols - c * LANE < LANE:
                    keep = keep & (lane < cols - c * LANE)
                results.append(jnp.where(keep, out, 0.0))
        at = 0
        for tag, _, _, _ in starts:
            for c in range(low, high):
                put(tag, c, results[at])
                at += 1


def spread(c, n, period):
    return pl.ds((c * period + n) * 25, 8, stride=3)


def collect(dest, c, period):
    return [
        dest[pl.ds((c * period + 8 * m) * 25 + 3 * j, 8, stride=25), :] for j in range(8) for m in range(period // 8)
    ]


def stage_tile(stage, slot, c, blocks):
    for i in range(0, len(blocks), 2):
        pair = jnp.concatenate([blocks[i], blocks[i + 1]], axis=0).astype(BF16)
        stage[slot, pl.ds(8 * i, 16), pl.ds(c * LANE, LANE)] = pair


def unpack_kernel(
    src, km, e8, ab, ur, rt, wt, raw, wide, dest, kstage, stage0, stage1, stage_t, stage3, raw_conv, sem_in, sem_out, sem_t
):
    role = lax.axis_index("section")
    total = src.shape[1] // LANE

    def out_copy(stage, slot, target):
        return pltpu.make_async_copy(stage.at[slot], target, sem_out.at[slot])

    @pl.when(role == 0)
    def _():
        blocks = 5
        count = 4 * blocks

        def flat_of(i):
            return CONV_END + HIGH_STRIDE * (i // blocks)

        def chunk_of(i):
            return flat_of(i) // LANE + 2200 * lax.rem(i, blocks)

        length = 640
        copy = pltpu.make_async_copy(src.at[:, pl.ds(0, length * LANE)], raw_conv.at[0], sem_t.at[0])
        copy.start()
        stream_start(count, LENS[0], total, chunk_of, src, raw, sem_in)
        copy.wait()
        widen(raw_conv, 0, length, wide)
        lane1 = lanes(1)
        dest[pl.ds(0, 64), :] = jnp.zeros((64, LANE), F32)
        for a in range(CHAR_V):
            flat = D_CHAR * a
            q, s = flat // LANE, flat % LANE
            here = wide[q : q + 1, :]
            out = roll_lanes(here, (LANE - s) % LANE) if s else here
            if s + D_CHAR > LANE:
                out = jnp.where(lane1 < LANE - s, out, roll_lanes(wide[q + 1 : q + 2, :], LANE - s))
            dest[a : a + 1, :] = jnp.where(lane1 < D_CHAR, out, jnp.where(lane1 == D_CHAR, 1.0, 0.0))
        table = dest[pl.ds(0, 64), :]
        for m in range(8):
            kstage[pl.ds(64 * m, 64), pl.ds(0, LANE)] = (
                pltpu.roll(table, 16 * m, 1) if m else table
            ).astype(BF16)
        copy = pltpu.make_async_copy(kstage.at[pl.ds(0, 512), pl.ds(0, LANE)], e8, sem_out.at[0])
        copy.start()
        copy.wait()
        tiles = FW // LANE
        rows = 112
        dest[pl.ds(0, rows * tiles), :] = jnp.zeros((rows * tiles, LANE), F32)

        def kernel_row(k, i, row):
            n, base = NFILT[k - 1], COLS[k - 1]
            edge = KOFF[k - 1] + n * i - base
            q, s = edge // LANE, edge % LANE
            for ct in range(base // LANE, (base + n - 1) // LANE + 1):
                out = wide[q + ct : q + ct + 1, :]
                if s:
                    after = roll_lanes(wide[q + ct + 1 : q + ct + 2, :], LANE - s)
                    out = jnp.where(lane1 < LANE - s, roll_lanes(out, LANE - s), after)
                at = ct * rows + row
                low, high = max(base - ct * LANE, 0), min(base + n - ct * LANE, LANE)
                if low > 0 or high < LANE:
                    out = jnp.where((lane1 >= low) & (lane1 < high), out, dest[at : at + 1, :])
                dest[at : at + 1, :] = out

        for k in range(1, 8):
            for i in range(k * D_CHAR):
                kernel_row(k, i, i + i // D_CHAR)
            kernel_row(k, k * D_CHAR, 15)
        kstage[...] = jnp.zeros_like(kstage)
        for ct in range(tiles):
            kstage[pl.ds(112, rows), pl.ds(ct * LANE, LANE)] = dest[pl.ds(ct * rows, rows), :].astype(BF16)
        copy = pltpu.make_async_copy(kstage.at[pl.ds(0, 368)], km, sem_out.at[0])
        copy.start()
        copy.wait()

        def target(i):
            return ab.at[i // blocks, pl.ds(pl.multiple_of(lax.rem(i, blocks) * 256, 256), 256)]

        def work(i, extra):
            block = lax.rem(i, blocks)
            inner = lax.rem(flat_of(i), LANE)

            def rows_of(i, carry):
                starts = []
                for n in range(4):
                    n = 4 * i + n
                    flat = inner + FILT * n
                    keep = 32 * (8 * block + sublanes()) + n <= FILT
                    starts.append((n, flat // LANE + extra, lax.rem(flat, LANE), keep))

                def put(n, c, value):
                    dest[spread(c, n, 32), :] = value

                take_rows(wide, starts, tiles, FILT, 275, put)
                return carry

            lax.fori_loop(0, 8, rows_of, 0)
            slot = lax.rem(i, 2)

            @pl.when(i >= 2)
            def _():
                out_copy(stage0, slot, target(i - 2)).wait()

            for c in range(tiles):
                stage_tile(stage0, slot, c, collect(dest, c, 32))
            out_copy(stage0, slot, target(i)).start()

        stream_blocks(count, LENS[0], total, chunk_of, src, raw, sem_in, wide, work)
        for i in (count - 2, count - 1):
            out_copy(stage0, i % 2, target(i)).wait()

    for layer in (1, 2):

        @pl.when(role == layer)
        def _(layer=layer):
            depth = FILT if layer == 1 else HID
            blocks = -(-depth // 128)
            recurrent = depth * 4 * HID
            count = blocks + 6

            def chunk_of(i):
                return jnp.where(i < blocks, 2600 * i, recurrent // LANE + 2600 * (i - blocks))

            stream_start(count, LENS[1], total, chunk_of, src, raw, sem_in)

            def target(i):
                at = jnp.where(i < blocks, i, i - blocks + 9)
                return ur.at[pl.ds(pl.multiple_of(at * 128, 128), 128)]

            def work(i, extra):
                inner = jnp.where(i < blocks, 0, recurrent % LANE)
                block = jnp.where(i < blocks, i, i - blocks)
                limit = jnp.where(i < blocks, depth, HID + 1)

                def rows_of(i, carry):
                    starts = []
                    for n in (2 * i, 2 * i + 1):
                        keep = 16 * (8 * block + sublanes()) + n < limit
                        for b in range(4):
                            flat = inner + 4 * HID * n + HID * b
                            starts.append(((n, b), flat // LANE + extra, lax.rem(flat, LANE), keep))

                    def put(tag, c, value):
                        dest[spread(6 * tag[1] + c, tag[0], 16), :] = value

                    take_rows(wide, starts, 6, HID, 325, put)
                    return carry

                lax.fori_loop(0, 8, rows_of, 0)
                slot = lax.rem(i, 2)

                @pl.when(i >= 2)
                def _():
                    out_copy(stage1, slot, target(i - 2)).wait()

                for c in range(24):
                    stage_tile(stage1, slot, c, collect(dest, c, 16))
                out_copy(stage1, slot, target(i)).start()

                @pl.when(i >= blocks)
                def _():
                    @pl.when(i >= blocks + 2)
                    def _():
                        turned_copy(i - 2).wait()

                    k = LANE * block + lanes(LANE)
                    for c in range(24):
                        turned = jnp.transpose(jnp.concatenate(collect(dest, c, 16), axis=0))
                        stage_t[slot, pl.ds(128 * c, 128), :] = jnp.where(k < HID, turned, 0.0).astype(BF16)
                    turned_copy(i).start()

            def turned_copy(i):
                slot = lax.rem(i, 2)
                at = pl.multiple_of((i - blocks) * LANE, LANE)
                return pltpu.make_async_copy(stage_t.at[slot], rt.at[:, pl.ds(at, LANE)], sem_t.at[slot])

            stream_blocks(count, LENS[1], total, chunk_of, src, raw, sem_in, wide, work)
            for i in (count - 2, count - 1):
                out_copy(stage1, i % 2, target(jnp.int32(i))).wait()
                turned_copy(jnp.int32(i)).wait()

    @pl.when(role == 3)
    def _():
        count = 11
        tiles = VW // LANE

        def chunk_of(i):
            return 5000 * i

        stream_start(count, LENS[3], total, chunk_of, src, raw, sem_in)

        def target(i):
            return wt.at[pl.ds(pl.multiple_of(i * 64, 64), 64)]

        def work(i, extra):
            def rows_of(n, carry):
                flat = VOCAB * n
                keep = 8 * (8 * i + sublanes()) + n < HID + 1

                def put(n, c, value):
                    dest[spread(c, n, 8), :] = value

                take_rows(wide, [(n, flat // LANE + extra, lax.rem(flat, LANE), keep)], tiles, VOCAB, 625, put)
                return carry

            lax.fori_loop(0, 8, rows_of, 0)
            slot = lax.rem(i, 2)

            @pl.when(i >= 2)
            def _():
                out_copy(stage3, slot, target(i - 2)).wait()

            for c in range(tiles):
                stage_tile(stage3, slot, c, collect(dest, c, 8))
            out_copy(stage3, slot, target(i)).start()

        stream_blocks(count, LENS[3], total, chunk_of, src, raw, sem_in, wide, work)
        for i in (count - 2, count - 1):
            out_copy(stage3, i % 2, target(jnp.int32(i))).wait()


def unpack_all(section_params):
    anywhere = pl.BlockSpec(memory_space=pl.ANY)
    return pl.pallas_call(
        unpack_kernel,
        out_shape=[
            jax.ShapeDtypeStruct((368, FW), BF16),
            jax.ShapeDtypeStruct((512, LANE), BF16),
            jax.ShapeDtypeStruct((4, 1280, FW), BF16),
            jax.ShapeDtypeStruct((15 * 128, ZW), BF16),
            jax.ShapeDtypeStruct((ZW, GW), BF16),
            jax.ShapeDtypeStruct((11 * 64, VW), BF16),
        ],
        in_specs=[anywhere],
        out_specs=[anywhere] * 6,
        scratch_shapes=[
            pltpu.VMEM((DEPTH, 1, LENS[3] * LANE), BF16),
            pltpu.VMEM((9312, LANE), F32),
            pltpu.VMEM((79 * 200, LANE), F32),
            pltpu.VMEM((512, FW), BF16),
            pltpu.VMEM((2, 256, FW), BF16),
            pltpu.VMEM((2, 128, ZW), BF16),
            pltpu.VMEM((2, ZW, LANE), BF16),
            pltpu.VMEM((2, 64, VW), BF16),
            pltpu.VMEM((1, 1, 640 * LANE), BF16),
            pltpu.SemaphoreType.DMA((DEPTH,)),
            pltpu.SemaphoreType.DMA((2,)),
            pltpu.SemaphoreType.DMA((2,)),
        ],
        compiler_params=pltpu.CompilerParams(vmem_limit_bytes=56 << 20),
        name="unpack",
    )(section_params)


def fblocks(width, step=256):
    return [(at, min(step, width - at)) for at in range(0, width, step)]


def mm(a, b):
    return jnp.dot(a, b, preferred_element_type=F32)


def mm_tn(a, b):
    return lax.dot_general(a, b, (((0,), (0,)), ((), ())), preferred_element_type=F32)


def mm_nt(a, b):
    return lax.dot_general(a, b, (((1,), (1,)), ((), ())), preferred_element_type=F32)


def mm_nt_few(a, b):
    return jnp.transpose(mm_nt(b, a))


def sigmoid(x):
    return 0.5 * jnp.tanh(0.5 * x) + 0.5


def load(pairs, sem):
    copies = [pltpu.make_async_copy(a, b, sem.at[i]) for i, (a, b) in enumerate(pairs)]
    for copy in copies:
        copy.start()
    for copy in copies:
        copy.wait()


def column_mask(at, width, limit, rows):
    return lax.broadcasted_iota(jnp.int32, (rows, width), 1) + at < limit


def char_onehot(ids, t):
    rows = ids.shape[0]
    lane = lanes(rows)
    pieces = []
    for pair in range(4):
        j = 8 * t + 2 * pair
        left = ids[:, j : j + 1]
        right = ids[:, j + 1 : j + 2]
        hit = jnp.where(lane < 64, left, right) == lax.rem(lane, 64)
        pieces.append(jnp.where(hit, 1.0, 0.0).astype(BF16))
    return jnp.concatenate(pieces, axis=1)


def conv_steps(body):
    def step(p, carry):
        body(p, p // 8, True, lax.rem(p, 8), FILT)
        return carry

    lax.fori_loop(0, 15, step, 0)
    body(15, 1, True, 7, COLS[6])
    for p in range(16, WORD_CHARS):
        body(p, 2, False, p - 16, COLS[WORD_CHARS - p])


def conv_at(emb, km, tile, second, within, at, width):
    first = 112 - 16 * within
    if not isinstance(first, int):
        first = pl.multiple_of(first, 16)
    if second:
        window = jnp.concatenate([emb[tile], emb[tile + 1]], axis=1)
    else:
        window = emb[tile]
    return mm(window, km[pl.ds(first, window.shape[1]), pl.ds(at, width)])


def char_forward(ids, e8, km, ab, emb, total, feats, pres, out):
    rows = ids.shape[0]
    for t in range(3):
        emb[t] = mm(char_onehot(ids, t), e8[...]).astype(BF16)
    total[...] = jnp.zeros_like(total)

    def step(p, tile, second, within, limit):
        for at, width in fblocks(FW):
            if at >= limit:
                continue
            value = jnp.exp(jnp.tanh(conv_at(emb, km, tile, second, within, at, width)))
            if at + width > limit and limit < FILT:
                value = jnp.where(column_mask(at, width, limit, rows), value, 0.0)
            total[:, pl.ds(at, width)] += value

    conv_steps(step)
    for at, width in fblocks(FW):
        col = lax.broadcasted_iota(jnp.int32, (rows, width), 1) + at
        count = jnp.full((rows, width), float(WORD_CHARS), F32)
        for k in range(1, 7):
            count = jnp.where(col >= COLS[k], float(WORD_CHARS - k), count)
        value = jnp.log(total[:, pl.ds(at, width)]) - jnp.log(count)
        value = jnp.where(col < FILT, value, jnp.where(col == FILT, 1.0, 0.0))
        feats[0, :, pl.ds(at, width)] = value.astype(BF16)
    for layer in range(2):
        for at, width in fblocks(FW):
            cols = pl.ds(at, width)
            t_pre = mm(feats[layer], ab[2 * layer, pl.ds(0, FW), cols])
            h_pre = mm(feats[layer], ab[2 * layer + 1, pl.ds(0, FW), cols])
            pres[2 * layer, :, cols] = t_pre
            pres[2 * layer + 1, :, cols] = h_pre
            gate = sigmoid(t_pre)
            y = feats[layer, :, cols].astype(F32)
            value = gate * (h_pre * sigmoid(h_pre)) + (1.0 - gate) * y
            col = lax.broadcasted_iota(jnp.int32, (rows, width), 1) + at
            if layer == 0:
                value = jnp.where(col < FILT, value, jnp.where(col == FILT, 1.0, 0.0))
                feats[1, :, cols] = value.astype(BF16)
            else:
                out[:, cols] = jnp.where(col < FILT, value, 0.0).astype(BF16)


def conv_backward(km, kt, emb, emb_t, slopes, held, sem, grad, dk, demb):
    rows = grad.shape[0]

    def fetch(p, slot):
        return pltpu.make_async_copy(slopes.at[p], held.at[slot], sem.at[slot])

    fetch(0, 0).start()
    kt[...] = jnp.transpose(km[pl.ds(112, LANE), :])
    for t in range(3):
        emb_t[pl.ds(LANE * t, LANE), :] = jnp.transpose(emb[t])
    emb_t[pl.ds(3 * LANE, LANE), :] = jnp.zeros((LANE, rows), BF16)
    dk[...] = jnp.zeros_like(dk)
    demb[...] = jnp.zeros_like(demb)

    def step(p, tile, second, within, limit):
        slot = p % 2 if isinstance(p, int) else lax.rem(p, 2)
        if not isinstance(p, int) or p + 1 < WORD_CHARS:
            fetch(p + 1, 1 - slot).start()
        fetch(p, slot).wait()
        window_t = emb_t[pl.ds(p * 16 if isinstance(p, int) else pl.multiple_of(p * 16, 16), LANE), :]
        back = jnp.zeros((rows, LANE), F32)
        for at, width in fblocks(FW):
            if at >= limit:
                continue
            cols = pl.ds(at, width)
            dz = (grad[:, cols] * held[slot, :, cols]).astype(BF16)
            dk[:, cols] += mm(window_t, dz)
            back = back + mm(dz, kt[cols, :])
        lane = lanes(rows)
        back = jnp.where(lane < 112, back, 0.0)
        turned = pltpu.roll(back, 16 * within, 1)
        demb[tile] += jnp.where(lane >= 16 * within, turned, 0.0)
        if second:
            demb[tile + 1] += jnp.where(lane < 16 * within, turned, 0.0)

    conv_steps(step)


def table_backward(ids, demb, table):
    acc = jnp.zeros((64, LANE), F32)
    for t in range(3):
        hot = char_onehot(ids, t)
        value = demb[t]
        high = value.astype(BF16)
        low = (value - high.astype(F32)).astype(BF16)
        grads = mm_tn(hot, high) + mm_tn(hot, low)
        for m in range(8):
            block = grads[64 * m : 64 * m + 64, :]
            acc = acc + (pltpu.roll(block, LANE - 16 * m, 1) if m else block)
    table[...] = acc


def tile_rows(stage, base, value, row_tiles, col_tiles, first_col=0, pitch=None):
    pitch = col_tiles if pitch is None else pitch
    for r in range(row_tiles):
        for c in range(col_tiles):
            stage[base + r * pitch + first_col + c] = value[16 * r : 16 * r + 16, LANE * c : LANE * c + LANE].astype(BF16)


def six(x):
    return jnp.concatenate([x] * 6, axis=1)


ANYWHERE = pl.BlockSpec(memory_space=pl.ANY)
ON_CHIP = pl.BlockSpec(memory_space=pltpu.VMEM)
LIMIT = 56 << 20


def call(kernel, name, ins, specs, outs, scratch, aliases=None):
    return pl.pallas_call(
        kernel,
        out_shape=[jax.ShapeDtypeStruct(shape, dtype) for shape, dtype in outs],
        in_specs=specs,
        out_specs=[ANYWHERE] * len(outs),
        scratch_shapes=scratch,
        input_output_aliases=aliases or {},
        compiler_params=pltpu.CompilerParams(vmem_limit_bytes=LIMIT),
        name=name,
    )(*ins)


def vmem(shape, dtype):
    return pltpu.VMEM(shape, dtype)


def dmas(count):
    return pltpu.SemaphoreType.DMA((count,))


def char_forward_call(ids, km, e8, ab):
    n = ids.shape[0]

    def kernel(ids, km, e8, ab, y2_o, feats_o, pres_o, total_o, emb_o, km_v, e8_v, ab_v, y2, feats, pres, total, emb, sem):
        @pl.when(lax.axis_index("section") == 0)
        def _():
            load([(km, km_v), (e8, e8_v), (ab, ab_v)], sem)
            char_forward(ids, e8_v, km_v, ab_v, emb, total, feats, pres, y2)
            load([(y2, y2_o), (feats, feats_o), (pres, pres_o), (total, total_o), (emb, emb_o)], sem)

    outs = [
        ((n, FW), BF16),
        ((2, n, FW), BF16),
        ((4, n, FW), F32),
        ((n, FW), F32),
        ((3, n, LANE), BF16),
    ]
    scratch = [vmem(km.shape, BF16), vmem(e8.shape, BF16), vmem(ab.shape, BF16)]
    scratch += [vmem(shape, dtype) for shape, dtype in outs] + [dmas(5)]
    return call(kernel, "char_forward", (ids, km, e8, ab), [ON_CHIP] + [ANYWHERE] * 3, outs, scratch)


def char_backward_call(ids, grad, km, emb, slopes, dpre):
    n = ids.shape[0]
    rows = SPLIT * CHUNK

    def kernel(
        ids, grad, km, emb, slopes, dpre, tiles_o, right_o,
        grad_v, km_v, emb_v, held, sem_s, kt, emb_t, dk, demb, table, stage, sem, send, recv,
    ):
        me = lax.axis_index("dp")

        def right_copy(k):
            return pltpu.make_async_remote_copy(
                dpre.at[pl.ds(0, rows)], right_o.at[k - 1], send.at[k - 1], recv.at[k - 1],
                device_id={"dp": quad_peer(me, k)}, device_id_type=pl.DeviceIdType.MESH,
            )

        @pl.when(lax.axis_index("section") == 0)
        def _():
            barrier = pltpu.get_barrier_semaphore()
            for k in range(1, QUAD):
                pl.semaphore_signal(
                    barrier, inc=1, device_id={"dp": quad_peer(me, k)}, device_id_type=pl.DeviceIdType.MESH
                )
            pl.semaphore_wait(barrier, QUAD - 1)
            for k in range(1, QUAD):
                right_copy(k).start()
            load([(grad, grad_v), (km, km_v), (emb, emb_v)], sem)
            conv_backward(km_v, kt, emb_v, emb_t, slopes, held, sem_s, grad_v, dk, demb)
            table_backward(ids, demb, table)
            tile_rows(stage, 0, dk[...], 8, 9)
            tile_rows(stage, 72, table[...], 4, 1)
            load([(stage, tiles_o)], sem)
            for k in range(1, QUAD):
                right_copy(k).wait_send()
                right_copy(k).wait_recv()

    outs = [((CONV_TILES, 16, LANE), BF16), ((QUAD - 1, rows, 4 * FW), BF16)]
    scratch = [
        vmem((n, FW), F32), vmem(km.shape, BF16), vmem(emb.shape, BF16), vmem((2, n, FW), F32), dmas(2),
        vmem((FW, LANE), BF16), vmem((4 * LANE, n), BF16), vmem((LANE, FW), F32), vmem((3, n, LANE), F32),
        vmem((64, LANE), F32), vmem((CONV_TILES, 16, LANE), BF16), dmas(4), dmas(QUAD - 1), dmas(QUAD - 1),
    ]
    return pl.pallas_call(
        kernel,
        out_shape=[jax.ShapeDtypeStruct(shape, dtype) for shape, dtype in outs],
        in_specs=[ON_CHIP] + [ANYWHERE] * 5,
        out_specs=[ANYWHERE] * 2,
        scratch_shapes=scratch,
        compiler_params=pltpu.CompilerParams(vmem_limit_bytes=LIMIT, collective_id=4, has_side_effects=True),
        name="char_backward",
    )(ids, grad, km, emb, slopes, dpre)


CONV_TILES = 76
TILES = 3648


def turned_tile(left, right, shift):
    rows = right.shape[0]
    if shift:
        mixed = jnp.where(
            lanes(rows) < shift, pltpu.roll(left.astype(F32), shift, 1), pltpu.roll(right.astype(F32), shift, 1)
        )
        right = mixed.astype(BF16)
    return jnp.transpose(right)


def each_vocab(body, step=2048):
    whole = VW // step

    def one(i, carry):
        body(pl.multiple_of(i * step, step), step)
        return carry

    lax.fori_loop(0, whole, one, 0)
    body(whole * step, VW - whole * step)


def output_weights_call(h, dl):
    n = h.shape[0]
    rows = 704
    pitch = VW // LANE

    def kernel(h, dl, tiles_o, h_v, dl_v, h_t, stage, sem):
        @pl.when(lax.axis_index("section") == 3)
        def _():
            load([(h, h_v), (dl, dl_v)], sem)
            lane = lanes(n)
            for c in range(6):
                value = h_v[:, pl.ds(LANE * c, LANE)].astype(F32)
                value = jnp.where(lane + c * LANE == HID, 1.0, value).astype(BF16)
                h_t[pl.ds(LANE * c, LANE), :] = jnp.transpose(value)

            def body(at, width):
                first = at // LANE
                for top, count in fblocks(rows):
                    value = mm(h_t[pl.ds(top, count), :], dl_v[:, pl.ds(at, width)])
                    for r in range(count // 16):
                        for c in range(width // LANE):
                            stage[(top // 16 + r) * pitch + first + c] = value[
                                16 * r : 16 * r + 16, LANE * c : LANE * c + LANE
                            ].astype(BF16)

            each_vocab(body, 256)
            count = rows // 16 * pitch
            load([(stage.at[pl.ds(0, count)], tiles_o.at[pl.ds(0, count)])], sem)

    scratch = [
        vmem((n, GW), BF16), vmem((n, VW), BF16), vmem((6 * LANE, n), BF16),
        vmem((rows // 16 * pitch, 16, LANE), BF16), dmas(2),
    ]
    return call(
        kernel, "output_weights", (h, dl), [ANYWHERE] * 2, [((TILES, 16, LANE), BF16)], scratch
    )[0]


CHUNK = 32
GROUPS_OUT = (3, 3, 2, 1)


def lstm_steps(first, count, keep, carry, r, gates, cells, prevs, hiddens):
    def step(s, carry):
        h, c = carry
        at = pl.ds(pl.multiple_of((first + s) * 8, 8), 8)
        k = six(keep[at, :])
        hp = h * k
        cp = c * k
        prevs[at, :] = hp
        z = gates[at, :] + mm(hp.astype(BF16), r[...])
        i = sigmoid(z[:, 0:GW])
        f = sigmoid(z[:, GW : 2 * GW])
        o = sigmoid(z[:, 2 * GW : 3 * GW])
        g = jnp.tanh(z[:, 3 * GW :])
        c = f * cp + i * g
        h = (o * jnp.tanh(c)).astype(BF16).astype(F32)
        gates[at, :] = jnp.concatenate([i, f, o, g], axis=1)
        cells[at, :] = c
        hiddens[at, :] = h
        return h, c

    return lax.fori_loop(0, count, step, carry)


def lstm_back_steps(first, count, keep, c0, carry, rt, gates, cells, dhs):
    def step(s, carry):
        dh_next, dc_next = carry
        t = first + count - 1 - s
        at = pl.ds(pl.multiple_of(t * 8, 8), 8)
        before = pl.ds(pl.multiple_of(jnp.maximum(t - 1, 0) * 8, 8), 8)
        k = six(keep[at, :])
        saved = gates[at, :]
        i, f, o, g = [saved[:, GW * b : GW * b + GW] for b in range(4)]
        cp = jnp.where(t > 0, cells[before, :], c0[...]) * k
        ct = jnp.tanh(cells[at, :])
        dh = dhs[at, :] + dh_next
        dc = dc_next + dh * o * (1.0 - ct * ct)
        dz = jnp.concatenate(
            [dc * g * i * (1.0 - i), dc * cp * f * (1.0 - f), dh * ct * o * (1.0 - o), dc * i * (1.0 - g * g)], axis=1
        ).astype(BF16)
        gates[at, :] = dz.astype(F32)
        return k * mm(dz, rt[...]), k * dc * f

    return lax.fori_loop(0, count, step, carry)


def output_rows(first, count, h, w, targets, valid, logits, dl, top, part, dh, loss, dh16):
    at_rows = pl.ds(first, count)
    depth = w.shape[0]
    own = pl.ds(0, count)
    top[own, :] = jnp.full((count, LANE), -jnp.inf, F32)

    def forward(at, width):
        z = mm(h[at_rows, pl.ds(0, depth)], w[:, pl.ds(at, width)])
        if isinstance(at, int):
            z = jnp.where(column_mask(at, width, VOCAB, count), z, -jnp.inf)
        logits[own, pl.ds(at, width)] = z
        best = top[own, :]
        for c in range(width // LANE):
            best = jnp.maximum(best, z[:, LANE * c : LANE * c + LANE])
        top[own, :] = best

    each_vocab(forward)
    best = jnp.max(top[own, :], axis=1, keepdims=True)
    part[:, own, :] = jnp.zeros((2, count, LANE), F32)
    wanted = targets[at_rows, :]

    def exponents(at, width):
        z = logits[own, pl.ds(at, width)]
        e = jnp.exp(z - best)
        logits[own, pl.ds(at, width)] = e
        for c in range(width // LANE):
            part[0, own, :] += e[:, LANE * c : LANE * c + LANE]
            hit = lanes(count) + (at + LANE * c) == wanted
            part[1, own, :] += jnp.where(hit, z[:, LANE * c : LANE * c + LANE], 0.0)

    each_vocab(exponents)
    total = jnp.sum(part[0, own, :], axis=1, keepdims=True)
    picked = jnp.sum(part[1, own, :], axis=1, keepdims=True)
    counts = valid[at_rows, :]
    loss[...] += jnp.sum(counts * (best + jnp.log(total) - picked), axis=0, keepdims=True)
    share = counts / total
    dh[:, own] = jnp.zeros((depth, count), F32)

    def backward(at, width):
        e = logits[own, pl.ds(at, width)]
        pieces = []
        for c in range(width // LANE):
            hit = lanes(count) + (at + LANE * c) == wanted
            grad = e[:, LANE * c : LANE * c + LANE] * share - jnp.where(hit, counts, 0.0)
            pieces.append(grad.astype(BF16))
        grad = jnp.concatenate(pieces, axis=1)
        dl[at_rows, pl.ds(at, width)] = grad
        dh[:, own] += mm_nt(w[:, pl.ds(at, width)], grad)

    each_vocab(backward)
    for at, width in fblocks(depth):
        value = jnp.transpose(dh[pl.ds(at, width), own])
        dh16[at_rows, pl.ds(at, width)] = jnp.where(column_mask(at, width, HID, count), value, 0.0).astype(BF16)


QUAD = 4
LEFT0 = 35 * LANE
LEFT1 = 14 * LANE
LEFT2 = 11 * LANE
LEFT_ROOM = 41 * LANE


def quad_peer(me, k):
    place = lax.rem(me, QUAD)
    return me - place + lax.rem(place + k, QUAD)


def turn_features(feats, turned):
    n = feats.shape[1]
    zero = jnp.zeros((n, LANE), BF16)
    for segment in range(4):
        start = segment * (FILT + 1)
        shift, first, last = start % LANE, start // LANE, (start + FILT) // LANE
        for c in range(last - first + 1):
            left = feats[segment // 2, :, pl.ds(LANE * (c - 1), LANE)] if c > 0 else zero
            right = feats[segment // 2, :, pl.ds(LANE * c, LANE)] if c < 9 else zero
            tile = turned_tile(left, right, shift)
            at = pl.ds(LANE * (first + c), LANE)
            if c == 0 and segment > 0:
                tile = tile + turned[at, :]
            turned[at, :] = tile


def turn_inputs(x, prevs, depth, turned):
    n = prevs.shape[0]
    first, shift = depth // LANE, depth % LANE
    end = depth + HID
    zero = jnp.zeros((n, LANE), F32)
    lane = lanes(n)
    for c in range(end // LANE + 1):
        if c < first:
            mixed = x[:, pl.ds(LANE * c, LANE)]
        else:
            k = c - first
            left = prevs[:, pl.ds(LANE * (k - 1), LANE)].astype(F32) if 0 < k < 7 else zero
            right = prevs[:, pl.ds(LANE * k, LANE)].astype(F32) if k < 6 else zero
            before = pltpu.roll(left, shift, 1) if k else x[:, pl.ds(LANE * c, LANE)].astype(F32)
            mixed = jnp.where(lane < shift, before, pltpu.roll(right, shift, 1))
            mixed = jnp.where(lane + c * LANE == end, 1.0, mixed).astype(BF16)
        turned[pl.ds(LANE * c, LANE), :] = jnp.transpose(mixed)


SPLIT = 6
AB_PARTS = ((0, 640), (640, 512))


def highway_chunk(rows, slot, dy, feats, pres, grad, dpre, w):
    def cut(m, at, width):
        return pl.ds(m * FW + at, width)

    for at, width in fblocks(FW):
        grad[rows, pl.ds(at, width)] = dy[rows, pl.ds(at, width)].astype(F32)
    for layer in (1, 0):
        own = pl.ds(slot, CHUNK)
        for at, width in fblocks(FW):
            cols = pl.ds(at, width)
            g = grad[rows, cols]
            gate = sigmoid(pres[own, cut(2 * layer, at, width)])
            q = pres[own, cut(2 * layer + 1, at, width)]
            sig = sigmoid(q)
            y = feats[layer, rows, cols].astype(F32)
            dpre[rows, cut(2 * layer, at, width)] = (g * (q * sig - y) * gate * (1.0 - gate)).astype(BF16)
            dpre[rows, cut(2 * layer + 1, at, width)] = (g * gate * sig * (1.0 + q * (1.0 - sig))).astype(BF16)
            grad[rows, cols] = g * (1.0 - gate)
        for half, (row, count) in enumerate(AB_PARTS):
            for at, width in fblocks(count):
                cols = pl.ds(row + at, width)
                value = grad[rows, cols]
                for m in (2 * layer, 2 * layer + 1):
                    part = w[pl.ds(at, width), pl.ds((2 * m + half) * FW, FW)]
                    value = value + mm_nt_few(dpre[rows, cut(m, 0, FW)], part)
                if row + at + width > FILT:
                    value = jnp.where(column_mask(row + at, width, FILT, CHUNK), value, 0.0)
                grad[rows, cols] = value


def recurrent_call(y2, feats, pres, ab, km, emb, total, ur, rt, wt, resets, target_ids, remaining, state):
    n = y2.shape[0]
    real_steps = resets.shape[1]
    chunks = n // CHUNK
    steps = CHUNK // 8
    depth_w = wt.shape[0]
    MESH = pl.DeviceIdType.MESH

    def kernel(
        y2, feats, pres, ab, km, emb, total, ur, rt, wt, resets, target_ids, remaining, state,
        slopes_o, grad_o, dpre_o, right_o, xb_o, lhs_o, dz_o, dl_o, x_q, h_q, loss_o, bias_o,
        emb_v, keep, valid, targets, feats_v, turned, pb, x1, xb, hb, db, ob, dy, u, r, r_t, w, start, gates, cells, prevs, hs, dhs, dz16,
        logits, dl, top, part, dh, loss,
        sem_in, sem_out, send_y, recv_y, send_f, recv_f, send_b, recv_b, send_d, recv_d,
        send_x, recv_x, send_h, recv_h, send_z, recv_z, sem_l, sem_p, sem_s,
    ):
        role = lax.axis_index("section")
        me = lax.axis_index("dp")
        loss[...] = jnp.zeros_like(loss)
        bias_o[...] = jnp.zeros_like(bias_o)

        def to(step, source, target, send, recv):
            return pltpu.make_async_remote_copy(
                source, target, send, recv, device_id={"section": role + step}, device_id_type=MESH
            )

        def span(c):
            return pl.ds(pl.multiple_of(c * CHUNK, CHUNK), CHUNK)

        def forward_copy(c, step):
            return to(step, hb.at[span(c)], xb.at[span(c)], send_f.at[c], recv_f.at[c])

        def backward_copy(c, step):
            return to(step, ob.at[span(c)], db.at[span(c)], send_b.at[c], recv_b.at[c])

        def feature_copy(step):
            return to(step, y2, x1, send_y.at[0], recv_y.at[0])

        def last_copy(c, step):
            return to(step, dy.at[span(c)], dy.at[span(c)], send_d.at[c], recv_d.at[c])

        def quad_copy(source, target, send, recv, k):
            return pltpu.make_async_remote_copy(
                source, target, send, recv, device_id={"dp": quad_peer(me, k)}, device_id_type=MESH
            )

        def input_copy(k):
            return quad_copy(x1, x_q.at[k - 1, 0], send_x.at[k - 1, 0], recv_x.at[k - 1, 0], k)

        def layer_copy(c, k):
            target = x_q.at[k - 1, 0, span(c), pl.ds(0, GW)]
            return quad_copy(xb.at[span(c)], target, send_x.at[k - 1, c], recv_x.at[k - 1, c], k)

        def feats_copy(k):
            return quad_copy(feats_v, x_q.at[k - 1], send_x.at[k - 1, 0], recv_x.at[k - 1, 0], k)

        def hidden_copy(c, k):
            return quad_copy(pb.at[span(c)], h_q.at[k - 1, span(c)], send_h.at[k - 1, c], recv_h.at[k - 1, c], k)

        def each_peer(body):
            for k in range(1, QUAD):
                body(k)

        def each_chunk(body, first=0):
            def step(c, carry):
                body(c)
                return carry

            lax.fori_loop(first, chunks, step, 0)

        def turned_out(g, rows):
            copy = pltpu.make_async_copy(turned.at[pl.ds(0, rows)], lhs_o.at[g, pl.ds(0, rows)], sem_l.at[0])
            copy.start()
            copy.wait()

        def fetch(source, target):
            copy = pltpu.make_async_copy(source, target, sem_l.at[1])
            copy.start()
            copy.wait()

        def dpre_copy(c, k):
            rows = pl.ds(pl.multiple_of((c - SPLIT) * CHUNK, CHUNK), CHUNK)
            return quad_copy(
                dl.at[span(c), pl.ds(0, 4 * FW)], right_o.at[k - 1, rows], send_z.at[k - 1, c], recv_z.at[k - 1, c], k
            )

        def right_copy(k, c):
            return pltpu.make_async_remote_copy(
                dz16.at[span(c)], dz_o.at[k - 1, span(c)], send_z.at[k - 1, c], recv_z.at[k - 1, c],
                device_id={"dp": quad_peer(me, k)}, device_id_type=MESH,
            )

        def inputs(which):
            if which == 0:
                pairs = [
                    (feats, feats_v),
                    (emb, emb_v),
                    (km, u.at[pl.ds(0, km.shape[0]), pl.ds(0, FW)]),
                    (total, gates.at[:, pl.ds(FW, FW)]),
                ]
                for m in range(4):
                    for half, (row, count) in enumerate(AB_PARTS):
                        target = w.at[pl.ds(0, count), pl.ds((2 * m + half) * FW, FW)]
                        pairs.append((ab.at[m, pl.ds(row, count)], target))
            elif which == 3:
                pairs = [(wt, w)]
            else:
                depth = FW if which == 1 else GW
                pairs = [
                    (ur.at[pl.ds(0, depth)], u.at[pl.ds(0, depth)]),
                    (ur.at[pl.ds(FW, GW)], r),
                    (rt, r_t),
                ]
            return [pltpu.make_async_copy(a, b, sem_in.at[i]) for i, (a, b) in enumerate(pairs)]

        for which in range(4):

            @pl.when(role == which)
            def _(which=which):
                for copy in inputs(which):
                    copy.start()

        @pl.when((role == 1) | (role == 2))
        def _():
            start[...] = jnp.zeros_like(start)
            for which in (1, 2):

                @pl.when(role == which)
                def _(which=which):
                    for half in range(2):
                        start[half, :, pl.ds(0, HID)] = state[which - 1, half]

            for t in range(n // 8):
                rows = pl.ds(8 * t, 8)
                kept = jnp.zeros((8, LANE), F32)
                if t < real_steps:
                    kept = 1.0 - jnp.broadcast_to(resets[:, t : t + 1], (8, LANE)).astype(F32)
                keep[rows, :] = kept

        @pl.when(role == 3)
        def _():
            left_words = jnp.broadcast_to(remaining[...], (8, LANE))
            for t in range(n // 8):
                rows = pl.ds(8 * t, 8)
                if t < real_steps:
                    valid[rows, :] = jnp.where(left_words > t, 1.0, 0.0)
                    targets[rows, :] = jnp.broadcast_to(target_ids[:, t : t + 1], (8, LANE))
                else:
                    valid[rows, :] = jnp.zeros((8, LANE), F32)
                    targets[rows, :] = jnp.full((8, LANE), -1, jnp.int32)

        barrier = pltpu.get_barrier_semaphore()

        @pl.when(role > 0)
        def _():
            pl.semaphore_signal(barrier, inc=1, device_id={"section": role - 1}, device_id_type=MESH)

        @pl.when(role < 3)
        def _():
            pl.semaphore_signal(barrier, inc=1, device_id={"section": role + 1}, device_id_type=MESH)

        for k in range(1, QUAD):
            pl.semaphore_signal(barrier, inc=1, device_id={"dp": quad_peer(me, k)}, device_id_type=MESH)
        pl.semaphore_wait(barrier, lax.min(role, 1) + lax.min(3 - role, 1) + QUAD - 1)

        @pl.when(role == 0)
        def _():
            feature_copy(1).start()
            for copy in inputs(0):
                copy.wait()
            each_peer(lambda k: feats_copy(k).start())
            turn_features(feats_v, turned)
            turned_out(QUAD - 1, LEFT0)
            feature_copy(1).wait_send()
            each_peer(lambda k: feats_copy(k).wait_send())
            for k in range(1, QUAD):
                feats_copy(k).wait_recv()
                fetch(x_q.at[k - 1], feats_v)
                turn_features(feats_v, turned)
                turned_out(k - 1, LEFT0)
            fetch(feats, feats_v)
            stages = ((cells, prevs), (hs, dhs))

            def slope_copies(p, slot):
                left, right = stages[slot]
                return [
                    pltpu.make_async_copy(left, slopes_o.at[p, :, pl.ds(0, GW)], sem_s.at[slot, 0]),
                    pltpu.make_async_copy(
                        right.at[:, pl.ds(0, FW - GW)], slopes_o.at[p, :, pl.ds(GW, FW - GW)], sem_s.at[slot, 1]
                    ),
                ]

            def slopes(p, slot, tile, second, within, limit):
                left, right = stages[slot]
                for at, width in fblocks(FW):
                    target, to_col = (left, at) if at < GW else (right, at - GW)
                    if at >= limit:
                        target[:, pl.ds(to_col, width)] = jnp.zeros((n, width), F32)
                        continue
                    act = jnp.tanh(conv_at(emb_v, u, tile, second, within, at, width))
                    value = jnp.exp(act) * (1.0 - act * act) / gates[:, pl.ds(FW + at, width)]
                    if at + width > limit and limit < FILT:
                        value = jnp.where(column_mask(at, width, limit, n), value, 0.0)
                    target[:, pl.ds(to_col, width)] = value
                for copy in slope_copies(p, slot):
                    copy.start()

            def finish_slopes(p, slot):
                for copy in slope_copies(p, slot):
                    copy.wait()

            def slope_pair(i, carry):
                for slot in range(2):
                    p = 2 * i + slot

                    @pl.when(i > 0)
                    def _(p=p, slot=slot):
                        finish_slopes(p - 2, slot)

                    slopes(p, slot, p // 8, True, lax.rem(p, 8), FILT)
                return carry

            lax.fori_loop(0, 7, slope_pair, 0)
            for p in range(14, WORD_CHARS):
                finish_slopes(p - 2, p % 2)
                tile, within = (1, p - 8) if p < 16 else (2, p - 16)
                slopes(p, p % 2, tile, p < 16, within, FILT if p < 15 else COLS[WORD_CHARS - p])
            for p in (WORD_CHARS - 2, WORD_CHARS - 1):
                finish_slopes(p, p % 2)

            def pres_copy(c, m):
                slot = lax.rem(c, 2)
                target = logits.at[pl.ds(pl.multiple_of(slot * CHUNK, CHUNK), CHUNK), pl.ds(m * FW, FW)]
                return pltpu.make_async_copy(pres.at[m, span(c)], target, sem_p.at[slot, m])

            for m in range(4):
                pres_copy(chunks - 1, m).start()

            def chunk(i, carry):
                c = chunks - 1 - i

                @pl.when(c > 0)
                def _():
                    for m in range(4):
                        pres_copy(c - 1, m).start()

                for m in range(4):
                    pres_copy(c, m).wait()
                last_copy(c, 1).wait_recv()
                highway_chunk(span(c), pl.multiple_of(lax.rem(c, 2) * CHUNK, CHUNK), dy, feats_v, logits, gates, dl, w)

                @pl.when(c >= SPLIT)
                def _():
                    each_peer(lambda k: dpre_copy(c, k).start())

                return carry

            lax.fori_loop(0, chunks, chunk, 0)
            copies = [
                pltpu.make_async_copy(gates.at[:, pl.ds(0, FW)], grad_o, sem_out.at[0]),
                pltpu.make_async_copy(dl.at[:, pl.ds(0, 4 * FW)], dpre_o, sem_out.at[1]),
            ]
            for copy in copies:
                copy.start()
            for at, width in fblocks(FW):
                cols = pl.ds(at, width)
                bias_o[:, cols] = jnp.sum(dl[:, cols].astype(F32), axis=0, keepdims=True)
            for copy in copies:
                copy.wait()

            def settle(c):
                for k in range(1, QUAD):
                    dpre_copy(c, k).wait_send()
                    dpre_copy(c, k).wait_recv()

            each_chunk(settle, SPLIT)

        @pl.when((role == 1) | (role == 2))
        def _():
            for which in (1, 2):

                @pl.when(role == which)
                def _(which=which):
                    for copy in inputs(which):
                        copy.wait()

            bias = r[pl.ds(HID, 1), :].astype(F32)

            @pl.when(role == 1)
            def _():
                feature_copy(-1).wait_recv()
                each_peer(lambda k: input_copy(k).start())
                for at, width in fblocks(ZW):
                    cols = pl.ds(at, width)
                    gates[:, cols] = mm(x1[...], u[:, cols]) + bias[:, at : at + width]

            def chunk_forward(c, carry):
                @pl.when(role == 2)
                def _():
                    forward_copy(c, -1).wait_recv()
                    each_peer(lambda k: layer_copy(c, k).start())
                    for at, width in fblocks(ZW):
                        cols = pl.ds(at, width)
                        gates[span(c), cols] = mm(xb[span(c), :], u[pl.ds(0, GW), cols]) + bias[:, at : at + width]

                carry = lstm_steps(c * steps, steps, keep, carry, r, gates, cells, prevs, hs)
                hb[span(c), :] = hs[span(c), :].astype(BF16)
                forward_copy(c, 1).start()
                pb[span(c), :] = prevs[span(c), :].astype(BF16)
                each_peer(lambda k: hidden_copy(c, k).start())
                return carry

            h0 = start[0].astype(BF16).astype(F32)
            lax.fori_loop(0, chunks, chunk_forward, (h0, start[1]))

            def turn_all(which):
                depth, rows = (FILT, LEFT1) if which == 1 else (HID, LEFT2)
                width = FW if which == 1 else GW
                turn_inputs(x1 if which == 1 else xb, pb, depth, turned)
                turned_out(QUAD - 1, rows)
                if which == 1:
                    each_peer(lambda k: input_copy(k).wait_send())
                    each_peer(lambda k: input_copy(k).wait_recv())
                else:

                    def moved(c):
                        for k in range(1, QUAD):
                            layer_copy(c, k).wait_send()
                            layer_copy(c, k).wait_recv()

                    each_chunk(moved)

                def hidden_moved(c):
                    for k in range(1, QUAD):
                        hidden_copy(c, k).wait_send()
                        hidden_copy(c, k).wait_recv()

                each_chunk(hidden_moved)
                for g in range(QUAD - 1):
                    fetch(x_q.at[g, 0, :, pl.ds(0, width)], feats_v.at[0, :, pl.ds(0, width)])
                    fetch(h_q.at[g], pb)
                    turn_inputs(feats_v.at[0], pb, depth, turned)
                    turned_out(g, rows)

            @pl.when(role == 1)
            def _():
                turn_all(1)

            def chunk_backward(i, carry):
                c = chunks - 1 - i
                backward_copy(c, 1).wait_recv()
                dhs[span(c), :] = db[span(c), :].astype(F32)
                carry = lstm_back_steps(c * steps, steps, keep, start.at[1], carry, r_t, gates, cells, dhs)
                dz16[span(c), :] = gates[span(c), :].astype(BF16)

                @pl.when(role == 1)
                def _():
                    for at, width in fblocks(FW):
                        value = mm_nt_few(dz16[span(c), :], u[pl.ds(at, width), :])
                        if at + width > FILT:
                            value = jnp.where(column_mask(at, width, FILT, CHUNK), value, 0.0)
                        dy[span(c), pl.ds(at, width)] = value.astype(BF16)
                    last_copy(c, -1).start()

                @pl.when(role == 2)
                def _():
                    for at, width in fblocks(GW):
                        value = mm_nt_few(dz16[span(c), :], u[pl.ds(at, width), :])
                        if at + width > HID:
                            value = jnp.where(column_mask(at, width, HID, CHUNK), value, 0.0)
                        ob[span(c), pl.ds(at, width)] = value.astype(BF16)
                    backward_copy(c, -1).start()

                each_peer(lambda k: right_copy(k, c).start())
                return carry

            zero = jnp.zeros((8, GW), F32)
            lax.fori_loop(0, chunks, chunk_backward, (zero, zero))

            own_right = pltpu.make_async_copy(dz16, dz_o.at[QUAD - 1], sem_out.at[1])
            own_right.start()

            @pl.when(role == 1)
            def _():
                each_chunk(lambda c: last_copy(c, -1).wait_send())

            @pl.when(role == 2)
            def _():
                turn_all(2)
                each_chunk(lambda c: backward_copy(c, -1).wait_send())

            own_right.wait()

            def sent(c, carry):
                forward_copy(c, 1).wait_send()
                for k in range(1, QUAD):
                    right_copy(k, c).wait_send()
                    right_copy(k, c).wait_recv()
                return carry

            lax.fori_loop(0, chunks, sent, 0)

        @pl.when(role == 3)
        def _():
            for copy in inputs(3):
                copy.wait()
            ob[...] = jnp.zeros_like(ob)
            done = 0
            for count in GROUPS_OUT:
                rows = pl.ds(done * CHUNK, count * CHUNK)
                for c in range(done, done + count):
                    forward_copy(c, -1).wait_recv()
                value = xb[rows, pl.ds(5 * LANE, LANE)].astype(F32)
                value = jnp.where(lanes(count * CHUNK) + 5 * LANE == HID, 1.0, value)
                xb[rows, pl.ds(5 * LANE, LANE)] = value.astype(BF16)
                output_rows(
                    done * CHUNK, count * CHUNK, xb, w, targets, valid, logits, dl, top, part, dh, loss, ob
                )
                for c in range(done, done + count):
                    backward_copy(c, -1).start()
                done += count
            copies = [
                pltpu.make_async_copy(xb, xb_o, sem_out.at[0]),
                pltpu.make_async_copy(dl, dl_o, sem_out.at[1]),
            ]
            for copy in copies:
                copy.start()
            for c in range(chunks):
                backward_copy(c, -1).wait_send()
            for copy in copies:
                copy.wait()

        loss_o[...] = loss[...]

    most = max(GROUPS_OUT) * CHUNK
    sems = pltpu.SemaphoreType.DMA
    outs = [
        ((WORD_CHARS, n, FW), F32), ((n, FW), F32), ((n, 4 * FW), BF16), ((QUAD - 1, n - SPLIT * CHUNK, 4 * FW), BF16), ((n, GW), BF16),
        ((QUAD, LEFT_ROOM, n), BF16), ((QUAD, n, ZW), BF16), ((n, VW), BF16), ((QUAD - 1, 2, n, FW), BF16),
        ((QUAD - 1, n, GW), BF16),
    ]
    scratch = [
        vmem((3, n, LANE), BF16), vmem((n, LANE), F32), vmem((n, LANE), F32), vmem((n, LANE), jnp.int32),
        vmem((2, n, FW), BF16), vmem((LEFT0, n), BF16), vmem((n, GW), BF16),
        vmem((n, FW), BF16), vmem((n, GW), BF16), vmem((n, GW), BF16), vmem((n, GW), BF16), vmem((n, GW), BF16),
        vmem((n, FW), BF16), vmem((FW, ZW), BF16), vmem((GW, ZW), BF16), vmem((ZW, GW), BF16), vmem(wt.shape, BF16),
        vmem((2, 8, GW), F32), vmem((n, ZW), F32), vmem((n, GW), F32), vmem((n, GW), F32), vmem((n, GW), F32),
        vmem((n, GW), F32), vmem((n, ZW), BF16),
        vmem((most, VW), F32), vmem((n, VW), BF16), vmem((most, LANE), F32), vmem((2, most, LANE), F32),
        vmem((depth_w, LANE), F32), vmem((1, LANE), F32),
        dmas(12), dmas(3), dmas(1), dmas(1), dmas(chunks), dmas(chunks), dmas(chunks), dmas(chunks), dmas(chunks), dmas(chunks),
        sems((QUAD - 1, chunks)), sems((QUAD - 1, chunks)), sems((QUAD - 1, chunks)), sems((QUAD - 1, chunks)),
        sems((QUAD - 1, chunks)), sems((QUAD - 1, chunks)), dmas(2), sems((2, 4)), sems((2, 2)),
    ]
    return pl.pallas_call(
        kernel,
        out_shape=[jax.ShapeDtypeStruct(shape, dtype) for shape, dtype in outs]
        + [jax.ShapeDtypeStruct((1, LANE), F32), jax.ShapeDtypeStruct((1, FW), F32)],
        in_specs=[ANYWHERE] * 10 + [ON_CHIP] * 4,
        out_specs=[ANYWHERE] * 10 + [ON_CHIP] * 2,
        scratch_shapes=scratch,
        compiler_params=pltpu.CompilerParams(vmem_limit_bytes=62 << 20, collective_id=3, has_side_effects=True),
        name="recurrent",
    )(y2, feats, pres, ab, km, emb, total, ur, rt, wt, resets, target_ids, remaining, state)


FORM = (
    (FILT, 9, 4 * (FILT + 1), CONV_END, CONV_TILES, 32),
    (4 * HID, 24, FILT + HID + 1, 0, 0, 16),
    (4 * HID, 24, 2 * HID + 1, 0, 0, 16),
    (VOCAB, 79, HID + 1, 0, 0, 16),
)


def slab(role, dest, share):
    width, pitch, rows, before, lead, period = FORM[role]
    low = lax.max if not isinstance(dest, int) else max
    high = lax.min if not isinstance(dest, int) else min
    one = (lambda v: v) if isinstance(dest, int) else jnp.int32
    start = low(one(share) * dest - before, one(0))
    first = start // width // period * period
    end = high((share * (dest + 1) - before + width - 1) // width, one(rows))
    count = low((end - first + 15) // 16, one(0)) * pitch
    tile = lead + first // 16 * pitch
    if lead:
        if isinstance(dest, int):
            if dest == 0:
                tile, count = 0, count + lead
        else:
            head = lax.max(1 - dest, 0)
            tile = tile - lead * head
            count = count + lead * head
    return first, tile, count


def slab_pieces(count, size):
    return (count + size - 1) // size


def gather_sum_call(tiles, groups, share):
    pair = 2
    across = groups // pair
    size = 64 if across <= 4 else 32
    pieces = max(slab_pieces(slab(3, dest, share)[2], size) for dest in range(groups))
    room = pieces * size
    line = across <= 4
    slots = across + 1 if line else across - 1
    MESH = pl.DeviceIdType.MESH

    def kernel(
        tiles, out, own, got1, got2, acc, own_sem, send1, recv1, send2, recv2, out_sem,
    ):
        role = lax.axis_index("section")
        me = lax.axis_index("dp")
        mine, side = me // pair, lax.rem(me, pair)
        other = mine * pair + (1 - side)

        def at_place(place):
            return {"dp": place * pair + side}

        def part(ref, slot, p):
            return ref.at[slot, pl.ds(pl.multiple_of(p * size, size), size)]

        def span(p):
            return pl.ds(pl.multiple_of(p * size, size), size)

        def loop(count, body):
            def step(p, carry):
                body(p)
                return carry

            lax.fori_loop(0, count, step, 0)

        def run(shape_of):
            def count_to(place, which):
                return shape_of(place * pair + which)[1]

            def own_copy(place, p):
                tile, _ = shape_of(place * pair + side)
                return pltpu.make_async_copy(
                    tiles.at[pl.ds(tile + p * size, size)], part(own, place, p), own_sem.at[place, p]
                )

            def first_copy(place, p):
                tile, _ = shape_of(place * pair + 1 - side)
                return pltpu.make_async_remote_copy(
                    tiles.at[pl.ds(tile + p * size, size)], part(got1, place, p), send1.at[place, p], recv1.at[place, p],
                    device_id={"dp": other}, device_id_type=MESH,
                )

            def begin(place):
                loop(count_to(place, 1 - side), lambda p: first_copy(place, p).start())
                loop(count_to(place, side), lambda p: own_copy(place, p).start())

            def hop_copy(place, up, p):
                if line:
                    target = mine + 1 if up else mine - 1
                    slot = jnp.where(place == mine + 1, across, place) if up else place
                else:
                    target = place
                    slot = lax.rem(place - mine + across, across) - 1
                return pltpu.make_async_remote_copy(
                    part(own, place, p), part(got2, slot, p), send2.at[place, p], recv2.at[slot, p],
                    device_id=at_place(target), device_id_type=MESH,
                )

            def arrived(slot, p):
                return pltpu.make_async_remote_copy(
                    part(own, 0, p), part(got2, slot, p), send2.at[0, p], recv2.at[slot, p],
                    device_id=at_place(lax.rem(mine + 1, across)), device_id_type=MESH,
                )

            def forward(place, up, has_before):
                def body(p):
                    own_copy(place, p).wait()
                    first_copy(place, p).wait_recv()
                    at = span(p)
                    own[place, at] = (own[place, at].astype(F32) + got1[place, at].astype(F32)).astype(BF16)
                    hop_copy(place, up, p).start()

                def body_sum(p):
                    own_copy(place, p).wait()
                    first_copy(place, p).wait_recv()
                    arrived(place, p).wait_recv()
                    at = span(p)
                    total = own[place, at].astype(F32) + got1[place, at].astype(F32) + got2[place, at].astype(F32)
                    own[place, at] = total.astype(BF16)
                    hop_copy(place, up, p).start()

                count = count_to(place, side)
                if not line:
                    loop(count, body)
                    return

                @pl.when(has_before)
                def _():
                    loop(count, body_sum)

                @pl.when(jnp.logical_not(has_before))
                def _():
                    loop(count, body)

            if line:
                for k in range(across - 1):

                    @pl.when(k < mine)
                    def _(k=k):
                        begin(k)

                    @pl.when(k < across - 1 - mine)
                    def _(k=k):
                        begin(across - 1 - k)

                begin(mine)
                for k in range(across - 1):

                    @pl.when(k < mine)
                    def _(k=k):
                        forward(k, False, mine < across - 1)

                    @pl.when(k < across - 1 - mine)
                    def _(k=k):
                        forward(across - 1 - k, True, mine > 0)

            else:
                for k in range(1, across):
                    begin(lax.rem(mine + k, across))
                begin(mine)
                for k in range(1, across):
                    forward(lax.rem(mine + k, across), True, None)

            def settle(p):
                own_copy(mine, p).wait()
                first_copy(mine, p).wait_recv()
                at = span(p)
                acc[at] = own[mine, at].astype(F32) + got1[mine, at].astype(F32)

            def add(slot):
                def body(p):
                    arrived(slot, p).wait_recv()
                    at = span(p)
                    acc[at] += got2[slot, at].astype(F32)

                return body

            mine_count = count_to(mine, side)
            loop(mine_count, settle)
            if line:

                @pl.when(mine < across - 1)
                def _():
                    loop(mine_count, add(mine))

                @pl.when(mine > 0)
                def _():
                    loop(mine_count, add(across))

            else:
                for k in range(1, across):
                    loop(mine_count, add(k - 1))

            def out_copy(p):
                return pltpu.make_async_copy(acc.at[span(p)], out.at[span(p)], out_sem.at[p])

            loop(mine_count, lambda p: out_copy(p).start())
            loop(mine_count, lambda p: out_copy(p).wait())
            for place in range(across):
                loop(count_to(place, 1 - side), lambda p, place=place: first_copy(place, p).wait_send())

                @pl.when(place != mine)
                def _(place=place):
                    loop(count_to(place, side), lambda p: hop_copy(place, True, p).wait_send())

        def shape_of(dest):
            _, tile, count = slab(3, dest, share)
            return tile, slab_pieces(count, size)

        @pl.when(role == 3)
        def _():
            barrier = pltpu.get_barrier_semaphore()
            pl.semaphore_signal(barrier, inc=1, device_id={"dp": other}, device_id_type=MESH)
            for k in range(1, across):
                peer = at_place(lax.rem(mine + k, across))
                pl.semaphore_signal(barrier, inc=1, device_id=peer, device_id_type=MESH)
            pl.semaphore_wait(barrier, across)
            run(shape_of)

    sems = pltpu.SemaphoreType.DMA
    return pl.pallas_call(
        kernel,
        out_shape=jax.ShapeDtypeStruct((room, 16, LANE), F32),
        in_specs=[ANYWHERE],
        out_specs=ANYWHERE,
        scratch_shapes=[
            vmem((across, room, 16, LANE), BF16), vmem((across, room, 16, LANE), BF16),
            vmem((slots, room, 16, LANE), BF16), vmem((room, 16, LANE), F32),
            sems((across, pieces)), sems((across, pieces)), sems((across, pieces)),
            sems((across, pieces)), sems((slots, pieces)), sems((pieces,)),
        ],
        compiler_params=pltpu.CompilerParams(vmem_limit_bytes=62 << 20, collective_id=1, has_side_effects=True),
        name="gather_sum",
    )(tiles)


BLOCK_ROWS = (25, 11, 11)


def finish_call(lhs, dz, dpre, rights, conv, bias, loss, after, groups, share):
    n = lhs.shape[2]
    quads = groups // QUAD
    MESH = pl.DeviceIdType.MESH

    def most_blocks(role):
        width = FORM[role][1]
        lead = FORM[role][4]
        most = 0
        for dest in range(groups):
            count = slab(role, dest, share)[2]
            if lead and dest == 0:
                count -= lead
            most = max(most, -(-(count // width) // BLOCK_ROWS[role]))
        return most

    blocks = [most_blocks(role) for role in range(3)]
    room = max(
        FORM[role][4] + blocks[role] * BLOCK_ROWS[role] * FORM[role][1] for role in range(3)
    )
    left_rows = max(blocks[role] * BLOCK_ROWS[role] * 16 for role in range(3))
    most = max(blocks)

    def kernel(
        lhs, dz, dpre, late, early, conv, bias, loss, after, out, small_out,
        left, dpre_v, sent, got, acc, convs, lead_sum, small, got_small,
        sem_left, sem_right, send, recv, send_c, recv_c, small_send, small_recv, sem_out,
        shared, shared_send, shared_recv,
    ):
        role = lax.axis_index("section")
        me = lax.axis_index("dp")
        place, quad = lax.rem(me, QUAD), me // QUAD

        def across_peer(k):
            return {"dp": place + QUAD * lax.rem(quad + k, quads)}

        barrier = pltpu.get_barrier_semaphore()
        for k in range(1, QUAD):
            pl.semaphore_signal(barrier, inc=1, device_id={"dp": quad_peer(me, k)}, device_id_type=MESH)
        for k in range(1, quads):
            pl.semaphore_signal(barrier, inc=1, device_id=across_peer(k), device_id_type=MESH)

        for source in (0, 3):

            @pl.when(role != source)
            def _(source=source):
                pl.semaphore_signal(barrier, inc=1, device_id={"section": source}, device_id_type=MESH)

        def right_load(b):
            return pltpu.make_async_copy(
                dz.at[:, :, pl.ds(GW * b, GW)], dpre_v.at[:, b, :, pl.ds(0, GW)], sem_right.at[b]
            )

        def right_loads0():
            copies = []
            cut = SPLIT * CHUNK
            for b in range(4):
                cols = pl.ds(FW * b, FW)
                pairs = [
                    (early.at[:, :, cols], dpre_v.at[pl.ds(0, QUAD - 1), b, pl.ds(0, cut)]),
                    (late.at[:, :, cols], dpre_v.at[pl.ds(0, QUAD - 1), b, pl.ds(cut, n - cut)]),
                    (dpre.at[:, cols], dpre_v.at[QUAD - 1, b]),
                ]
                copies += [pltpu.make_async_copy(x, y, sem_right.at[4 + 3 * b + i]) for i, (x, y) in enumerate(pairs)]
            return copies

        def conv_load():
            return pltpu.make_async_copy(conv, convs.at[QUAD - 1], sem_right.at[16])

        @pl.when(role == 0)
        def _():
            for copy in right_loads0():
                copy.start()
            conv_load().start()

        @pl.when((role == 1) | (role == 2))
        def _():
            for b in range(4):
                right_load(b).start()

        ends = lax.max(1 - role, 0) + lax.max(role - 2, 0)
        pl.semaphore_wait(barrier, QUAD - 1 + quads - 1 + 3 * ends)

        small[...] = jnp.zeros_like(small)

        @pl.when(role == 0)
        def _():
            small[0, :, pl.ds(0, FW)] = bias[...]

        @pl.when(role == 3)
        def _():
            small[0, :, pl.ds(FW, LANE)] = loss[...]

        def small_copy(k):
            if k < QUAD:
                source, target = small.at[0], {"dp": quad_peer(me, k)}
            else:
                source, target = small.at[1], across_peer(k - QUAD + 1)
            return pltpu.make_async_remote_copy(
                source, got_small.at[k - 1], small_send.at[k - 1], small_recv.at[k - 1],
                device_id=target, device_id_type=MESH,
            )

        for k in range(1, QUAD):
            small_copy(k).start()

        def across_small():
            for k in range(1, QUAD):
                small_copy(k).wait_recv()
            small[1] = small[0] + got_small[0] + got_small[1] + got_small[2]
            for k in range(QUAD, QUAD + quads - 1):
                small_copy(k).start()

        def share_copy(slot, k):
            return pltpu.make_async_remote_copy(
                small.at[0], shared.at[slot], shared_send.at[slot, k - 1], shared_recv.at[slot],
                device_id={"section": lax.rem(role + k, 4)}, device_id_type=MESH,
            )

        def share_small():
            total = small[1]
            for k in range(QUAD, QUAD + quads - 1):
                small_copy(k).wait_recv()
                total = total + got_small[k - 1]
            for k in range(1, QUAD):
                small_copy(k).wait_send()
            small[0] = total
            for slot, source in enumerate((0, 3)):

                @pl.when(role == source)
                def _(slot=slot):
                    for k in range(1, 4):
                        share_copy(slot, k).start()

        def conv_copy(slot, target):
            return pltpu.make_async_remote_copy(
                conv, convs.at[slot], send_c.at[slot], recv_c.at[slot], device_id={"dp": target}, device_id_type=MESH
            )

        def run(which):
            width, pitch, rows, _, lead, _ = FORM[which]
            size = BLOCK_ROWS[which]
            block_tiles = size * pitch

            def geometry(k):
                dest = place + QUAD * lax.rem(quad + k, quads)
                first, _, count = slab(which, dest, share)
                if lead:
                    head = lax.max(1 - dest, 0)
                    count = count - lead * head
                else:
                    head = 0
                return first, (count // pitch + size - 1) // size, head

            def left_copy(k):
                height = blocks[which] * size * 16
                first = lax.min(geometry(k)[0], LEFT_ROOM - height)
                span = pl.ds(pl.multiple_of(first, 16), height)
                return pltpu.make_async_copy(
                    lhs.at[:, span], left.at[lax.rem(k, 2), :, pl.ds(0, blocks[which] * size * 16)], sem_left.at[lax.rem(k, 2)]
                )

            def block_copy(k, b):
                span = pl.ds(CONV_TILES + b * block_tiles, block_tiles)
                return pltpu.make_async_remote_copy(
                    sent.at[k - 1, span], got.at[k - 1, span], send.at[k - 1, b], recv.at[k - 1, b],
                    device_id=across_peer(k), device_id_type=MESH,
                )

            def lead_copy(k):
                span = pl.ds(0, CONV_TILES)
                return pltpu.make_async_remote_copy(
                    sent.at[k - 1, span], got.at[k - 1, span], send.at[k - 1, most], recv.at[k - 1, most],
                    device_id=across_peer(k), device_id_type=MESH,
                )

            def put(k, own, at, value):
                if own:
                    acc[at] = value
                else:
                    sent[k - 1, at] = value.astype(BF16)

            def block(k, own, b, first):
                here = pl.ds(pl.multiple_of(b * size * 16, 16), size * 16)
                base = CONV_TILES + b * block_tiles
                if which == 0:
                    row = lax.broadcasted_iota(jnp.int32, (size * 16, n), 0) + first + b * size * 16
                    start = first + b * size * 16
                    low = lax.min(start // (FILT + 1), 3)
                    high = lax.min((start + size * 16 - 1) // (FILT + 1), 3)
                    edge = (FILT + 1) * (low + 1)
                    lefts = [left[lax.rem(k, 2), g, here, :] for g in range(QUAD)]
                    near = [jnp.where(row < edge, x, jnp.zeros_like(x)) for x in lefts]
                    for col, wide in fblocks(FW):
                        value = jnp.zeros((size * 16, wide), F32)
                        for g in range(QUAD):
                            value = value + mm(near[g], dpre_v[g, low, :, pl.ds(col, wide)])
                        for r in range(size):
                            for c in range(wide // LANE):
                                tile = value[16 * r : 16 * r + 16, LANE * c : LANE * c + LANE]
                                put(k, own, base + r * pitch + col // LANE + c, tile)

                    @pl.when(high > low)
                    def _():
                        far = [jnp.where(row < edge, jnp.zeros_like(x), x) for x in lefts]
                        for col, wide in fblocks(FW):
                            value = jnp.zeros((size * 16, wide), F32)
                            for g in range(QUAD):
                                value = value + mm(far[g], dpre_v[g, high, :, pl.ds(col, wide)])
                            for r in range(size):
                                for c in range(wide // LANE):
                                    tile = value[16 * r : 16 * r + 16, LANE * c : LANE * c + LANE]
                                    at = base + r * pitch + col // LANE + c
                                    old = acc[at] if own else sent[k - 1, at].astype(F32)
                                    put(k, own, at, old + tile)

                else:
                    for col, wide in fblocks(ZW):
                        value = jnp.zeros((size * 16, wide), F32)
                        for g in range(QUAD):
                            value = value + mm(left[lax.rem(k, 2), g, here, :], dpre_v[g, col // GW, :, pl.ds(col % GW, wide)])
                        for r in range(size):
                            for c in range(wide // LANE):
                                tile = value[16 * r : 16 * r + 16, LANE * c : LANE * c + LANE]
                                put(k, own, base + r * pitch + col // LANE + c, tile)

            def loop(count, body):
                def step(b, carry):
                    body(b)
                    return carry

                lax.fori_loop(0, count, step, 0)

            left_copy(jnp.int32(1 % quads)).start()
            if which == 0:

                @pl.when(place > 0)
                def _():
                    for k in range(1, QUAD):

                        @pl.when(place == k)
                        def _(k=k):
                            conv_copy(k - 1, me - k).start()

                for copy in right_loads0():
                    copy.wait()
                conv_load().wait()
            else:
                for b in range(4):
                    right_load(b).wait()

            if which == 0:

                @pl.when(place == 0)
                def _():
                    for k in range(1, QUAD):
                        conv_copy(k - 1, me + k).wait_recv()
                    total = convs[0].astype(F32)
                    for k in range(1, QUAD):
                        total = total + convs[k].astype(F32)
                    lead_sum[...] = total

            def slab_of(k, own):
                left_copy(k).wait()
                if not own:
                    left_copy(lax.rem(k + 1, quads)).start()
                first, count, head = geometry(k)
                if which == 0:

                    @pl.when(head > 0)
                    def _():
                        if own:
                            acc[pl.ds(0, CONV_TILES)] = lead_sum[...]
                        else:
                            sent[k - 1, pl.ds(0, CONV_TILES)] = lead_sum[...].astype(BF16)
                            lead_copy(k).start()

                def work(b):
                    block(k, own, b, first)
                    if not own:
                        block_copy(k, b).start()

                loop(count, work)

            def others(body):
                def step(k, carry):
                    body(k)
                    return carry

                lax.fori_loop(1, quads, step, 0)

            others(lambda k: slab_of(k, False))
            across_small()
            slab_of(jnp.int32(0), True)
            share_small()

            _, mine, head = geometry(0)
            def join(k):
                def add(b):
                    block_copy(k, b).wait_recv()
                    span = pl.ds(CONV_TILES + b * block_tiles, block_tiles)
                    acc[span] += got[k - 1, span].astype(F32)

                loop(mine, add)
                if which == 0:

                    @pl.when(head > 0)
                    def _():
                        lead_copy(k).wait_recv()
                        span = pl.ds(0, CONV_TILES)
                        acc[span] += got[k - 1, span].astype(F32)

            others(join)

            span = blocks[which] * block_tiles
            if which == 0:

                @pl.when(head > 0)
                def _():
                    copy = pltpu.make_async_copy(
                        acc.at[pl.ds(0, CONV_TILES + span)], out.at[pl.ds(0, CONV_TILES + span)], sem_out.at[0]
                    )
                    copy.start()
                    copy.wait()

                @pl.when(head == 0)
                def _():
                    copy = pltpu.make_async_copy(acc.at[pl.ds(CONV_TILES, span)], out.at[pl.ds(0, span)], sem_out.at[0])
                    copy.start()
                    copy.wait()

            else:
                copy = pltpu.make_async_copy(acc.at[pl.ds(CONV_TILES, span)], out.at[pl.ds(0, span)], sem_out.at[0])
                copy.start()
                copy.wait()

            def sent_all(k):
                _, count, head = geometry(k)
                loop(count, lambda b: block_copy(k, b).wait_send())
                if which == 0:

                    @pl.when(head > 0)
                    def _():
                        lead_copy(k).wait_send()

            others(sent_all)

            if which == 0:
                for k in range(1, QUAD):

                    @pl.when(place == k)
                    def _(k=k):
                        conv_copy(k - 1, me - k).wait_send()

        for which in range(3):

            @pl.when(role == which)
            def _(which=which):
                run(which)

        @pl.when(role == 3)
        def _():
            across_small()
            share_small()

        result = jnp.zeros((1, FW + LANE), F32)
        for slot, source in enumerate((0, 3)):

            @pl.when(role == source)
            def _(slot=slot):
                shared[slot] = small[0]

            @pl.when(role != source)
            def _(slot=slot):
                share_copy(slot, 1).wait_recv()

            result = result + shared[slot]
        small_out[...] = result
        for slot, source in enumerate((0, 3)):

            @pl.when(role == source)
            def _(slot=slot):
                for k in range(1, 4):
                    share_copy(slot, k).wait_send()

        for k in range(QUAD, QUAD + quads - 1):
            small_copy(k).wait_send()

    sems = pltpu.SemaphoreType.DMA
    full = CONV_TILES + max(blocks[role] * BLOCK_ROWS[role] * FORM[role][1] for role in range(3))
    smalls = QUAD + quads - 2
    return pl.pallas_call(
        kernel,
        out_shape=[jax.ShapeDtypeStruct((full, 16, LANE), F32), jax.ShapeDtypeStruct((1, FW + LANE), F32)],
        in_specs=[ANYWHERE] * 6 + [ON_CHIP] * 2 + [ANYWHERE],
        out_specs=[ANYWHERE, ON_CHIP],
        scratch_shapes=[
            vmem((2, QUAD, left_rows, n), BF16), vmem((QUAD, 4, n, FW), BF16),
            vmem((quads - 1, full, 16, LANE), BF16), vmem((quads - 1, full, 16, LANE), BF16),
            vmem((full, 16, LANE), F32), vmem((QUAD, CONV_TILES, 16, LANE), BF16), vmem((CONV_TILES, 16, LANE), F32),
            vmem((2, 1, FW + LANE), F32), vmem((smalls, 1, FW + LANE), F32),
            sems((2,)), sems((17,)), sems((quads - 1, most + 1)), sems((quads - 1, most + 1)),
            sems((QUAD - 1,)), sems((QUAD - 1,)), sems((smalls,)), sems((smalls,)), sems((1,)),
            vmem((2, 1, FW + LANE), F32), sems((2, 3)), sems((2,)),
        ],
        compiler_params=pltpu.CompilerParams(vmem_limit_bytes=62 << 20, collective_id=5, has_side_effects=True),
        name="finish",
    )(lhs, dz, dpre, *rights, conv, bias, loss, after)


def pack_call(summed, summed3, groups, share):
    rooms = (summed.shape[0] * 16, summed3.shape[0] * 16)
    chunks = share // LANE
    margin = 1280
    slab_rows = 10624
    flat_rows = margin + max(10752, chunks + 1280)

    def kernel(summed, summed3, out, rows_v, spaced, flat, sem):
        role = lax.axis_index("section")
        me = lax.axis_index("dp")
        zero = jnp.zeros((64, LANE), F32)

        def clear(i, carry):
            flat[pl.ds(pl.multiple_of(i * 64, 64), 64), :] = zero
            return carry

        def fetch(source, room):
            return pltpu.make_async_copy(source, rows_v.at[pl.ds(0, room)], sem.at[0])

        @pl.when(role < 3)
        def _():
            fetch(summed, rooms[0]).start()

        @pl.when(role == 3)
        def _():
            fetch(summed3, rooms[1]).start()

        lax.fori_loop(0, flat_rows // 64, clear, 0)

        @pl.when(role < 3)
        def _():
            fetch(summed, rooms[0]).wait()

        @pl.when(role == 3)
        def _():
            fetch(summed3, rooms[1]).wait()

        lane = lanes()

        for which in range(4):
            width, pitch, rows, before, lead, period = FORM[which]
            if which == 0:
                blocks, cols, tiles = 1, FILT, 9
            elif which == 3:
                blocks, cols, tiles = 1, VOCAB, 79
            else:
                blocks, cols, tiles = 4, HID, 6
            stride = period * width // LANE
            most = max(slab(which, dest, share)[2] for dest in range(groups))
            groups8 = -(-(-(-most // pitch) * 16) // (8 * period))

            @pl.when(role == which)
            def _(which=which):
                first, _, count = slab(which, me, share)
                skip = lead * lax.max(1 - me, 0)
                step_rows = pitch * 49 + (pitch * 49 + 1) % 2

                def space(rt, carry):
                    for c in range(pitch):
                        for half in range(2):
                            at = pl.multiple_of((skip + rt * pitch + c) * 16 + 8 * half, 8)
                            spaced[pl.ds(rt * step_rows + 49 * c + 24 * half, 8, stride=3), :] = rows_v[pl.ds(at, 8), :]
                    return carry

                lax.fori_loop(0, (count - skip) // pitch, space, 0)
                base = margin + before // LANE + stride * (first // period) - chunks * me

                hop = period // 16 * step_rows
                half = period // 2

                def place(group, n, b):
                    number = first + period * (8 * group + sublanes()) + n
                    flat_at = before % LANE + width * n + cols * b
                    source = n // 16 * step_rows + 3 * lax.rem(n, 16) + 8 * group * hop + 49 * tiles * b
                    to = base + flat_at // LANE + stride * 8 * group
                    return number < rows, lax.rem(flat_at, LANE), source, to

                def run(places, low, high, lasts):
                    taken = [
                        [spaced[pl.ds(source + 49 * j, 8, stride=hop), :] for j in range(low, min(high, tiles))]
                        for _, _, source, _ in places
                    ]
                    edges = [j for j in range(low, high) if j == 0 or j >= tiles - 1]
                    old = [
                        {j: flat[pl.ds(to + j, 8, stride=stride), :] for j in edges} for _, _, _, to in places
                    ]
                    values, ends = [], []
                    for (keep, turn, _, _), pieces, olds, last in zip(places, taken, old, lasts):
                        turned = [last] + [pltpu.roll(jnp.where(keep, x, 0.0), turn, 1) for x in pieces]
                        for j in range(low, high):
                            here = turned[j - low + 1] if j < tiles else turned[-1]
                            value = here if j == tiles else jnp.where(lane >= turn, here, turned[j - low])
                            if j in olds:
                                at = lane + LANE * j - turn
                                value = jnp.where((at >= 0) & (at < cols), value, olds[j])
                            values.append(value)
                        ends.append(turned[-1])
                    at = 0
                    for _, _, _, to in places:
                        for j in range(low, high):
                            flat[pl.ds(to + j, 8, stride=stride), :] = values[at]
                            at += 1
                    return ends

                def row(i, carry):
                    group, n = i // half, lax.rem(i, half)
                    zero = jnp.zeros((8, LANE), F32)
                    if blocks == 4:
                        for b in range(2):
                            places = [place(group, m, c) for m in (n, n + half) for c in (b, b + 2)]
                            run(places, 0, tiles + 1, [zero] * 4)
                    else:
                        places = [place(group, m, 0) for m in (n, n + half)]
                        ends = [zero] * 2
                        for low in range(0, tiles + 1, 20):
                            ends = run(places, low, min(low + 20, tiles + 1), ends)
                    return carry

                @pl.when(count > 0)
                def _():
                    lax.fori_loop(0, half * groups8, row, 0)

        @pl.when((role == 0) & (me == 0))
        def _():
            lane1 = lanes(1)

            def piece(row_at, flat_at, low, size):
                edge = flat_at - low
                turn = edge % LANE
                to = margin + (edge - turn) // LANE
                first, end = low // LANE, (low + size - 1) // LANE
                last = jnp.zeros((1, LANE), F32)
                for j in range(first, end + 2):
                    least, most = max(low + turn - LANE * j, 0), min(low + size + turn - LANE * j, LANE)
                    here = last
                    if j <= end:
                        here = rows_v[row_at + 16 * j : row_at + 16 * j + 1, :]
                        here = pltpu.roll(here, turn, 1) if turn else here
                    if most > least:
                        value = jnp.where(lane1 >= turn, here, last) if turn else here
                        at = to + j
                        if least > 0 or most < LANE:
                            value = jnp.where((lane1 >= least) & (lane1 < most), value, flat[at : at + 1, :])
                        flat[at : at + 1, :] = value
                    last = here

            for k in range(1, 8):
                n = NFILT[k - 1]
                for i in range(k * D_CHAR + 1):
                    number = i + i // D_CHAR if i < k * D_CHAR else 15
                    piece(number // 16 * 144 + number % 16, KOFF[k - 1] + n * i, COLS[k - 1], n)
            for a in range(CHAR_V):
                piece(72 * 16 + a, D_CHAR * a, 0, D_CHAR)

        copy = pltpu.make_async_copy(flat.at[pl.ds(margin, chunks)], out, sem.at[0])
        copy.start()
        copy.wait()

    return pl.pallas_call(
        kernel,
        out_shape=jax.ShapeDtypeStruct((chunks, LANE), F32),
        in_specs=[ANYWHERE] * 2,
        out_specs=ANYWHERE,
        scratch_shapes=[
            vmem((slab_rows, LANE), F32), vmem((31104, LANE), F32), vmem((flat_rows, LANE), F32), dmas(1),
        ],
        compiler_params=pltpu.CompilerParams(vmem_limit_bytes=LIMIT),
        name="pack",
    )(summed.reshape(rooms[0], LANE), summed3.reshape(rooms[1], LANE))


def shards(char_ids, target_ids, remaining, resets, start_state, section_params):
    rows, steps = char_ids.shape[:2]
    groups = lax.axis_size("dp")
    packed = section_params.shape[1]
    share = packed // groups
    n = rows * (steps + 1)

    ids = jnp.pad(
        char_ids.transpose(1, 0, 2), ((0, 1), (0, 0), (0, LANE - WORD_CHARS)), constant_values=-1
    ).reshape(n, LANE)
    km, e8, ab, ur, rt, wt = unpack_all(section_params)
    y2, *char_saved = char_forward_call(ids, km, e8, ab)
    feats, pres, total, emb = char_saved
    slopes, grad, dpre, late, xb, lhs, dz, dl, _, _, loss, bias = recurrent_call(
        y2, feats, pres, ab, km, emb, total, ur, rt, wt, resets, target_ids, remaining.reshape(rows, 1), start_state
    )
    tiles3 = output_weights_call(xb, dl)
    summed3 = gather_sum_call(tiles3, groups, share)
    conv, early = char_backward_call(ids, grad, km, emb, slopes, dpre)
    summed, small = finish_call(lhs, dz, dpre, (late, early), conv, bias, loss, summed3, groups, share)
    flat = pack_call(summed, summed3, groups, share)
    mean_loss = small[0, FW] / (groups * rows * steps)
    return mean_loss, flat.reshape(1, share), small[0, :FILT]


def solution(mesh):
    in_specs = (
        P("dp", None, None),
        P("dp", None),
        P("dp"),
        P("dp", None),
        P(None, None, "dp", None),
        P("section", None),
    )
    out_specs = (P(), P("section", "dp"), P())
    return jax.shard_map(shards, mesh=mesh, in_specs=in_specs, out_specs=out_specs, check_vma=False)
```

```python
import functools
import math

import jax
import jax.numpy as jnp
from jax import lax
from jax.experimental import pallas as pl
from jax.experimental.pallas import tpu as pltpu
from jax.sharding import PartitionSpec as P

D_CHAR = 15
CHAR_V = 51
F_UNIT = 50
WORD_CHARS = 21
HID = 650
VOCAB = 10000
FILT = 1100
F32 = jnp.float32
BF16 = jnp.bfloat16

NFILT = [F_UNIT * min(k, 4) for k in range(1, 8)]
COLS = [sum(NFILT[:k]) for k in range(8)]
KOFF = [CHAR_V * D_CHAR + sum((j * D_CHAR + 1) * NFILT[j - 1] for j in range(1, k)) for k in range(1, 9)]
CONV_END = KOFF[7]
HIGH_STRIDE = FILT * (FILT + 1)
FW = 1152
GW = 768
ZW = 4 * GW
VW = 10112
LANE = 128
LENS = (2304, 2688, 2688, 5120)


def roll_lanes(x, shift):
    return pltpu.roll(x, shift, 1)


def lanes(rows=8):
    return lax.broadcasted_iota(jnp.int32, (rows, LANE), 1)


def sublanes():
    return lax.broadcasted_iota(jnp.int32, (8, LANE), 0)


def widen(raw, slot, rows, wide):
    def body(i, carry):
        piece = raw[slot, 0:1, pl.ds(pl.multiple_of(i * 16384, 16384), 16384)]
        wide[pl.ds(pl.multiple_of(i * 128, 128), 128), :] = piece.astype(F32).reshape(128, LANE)
        return carry

    lax.fori_loop(0, rows // 128, body, 0)


DEPTH = 4


def stream_start(count, length, total, chunk_of, src, raw, sem):
    for i in range(DEPTH - 1):
        stream_copy(jnp.int32(i), length, total, chunk_of, src, raw, sem).start()


def stream_at(i, length, total, chunk_of):
    return jnp.minimum(chunk_of(i) // 8 * 8, total - length)


def stream_copy(i, length, total, chunk_of, src, raw, sem):
    at = pl.multiple_of(stream_at(i, length, total, chunk_of) * LANE, 8 * LANE)
    slot = lax.rem(i, DEPTH)
    return pltpu.make_async_copy(
        src.at[:, pl.ds(at, length * LANE)], raw.at[slot, :, pl.ds(0, length * LANE)], sem.at[slot]
    )


def stream_blocks(count, length, total, chunk_of, src, raw, sem, wide, work):
    def body(i, carry):
        @pl.when(i + DEPTH - 1 < count)
        def _():
            stream_copy(i + DEPTH - 1, length, total, chunk_of, src, raw, sem).start()

        stream_copy(i, length, total, chunk_of, src, raw, sem).wait()
        widen(raw, lax.rem(i, DEPTH), length, wide)
        work(i, chunk_of(i) - stream_at(i, length, total, chunk_of))
        return carry

    lax.fori_loop(0, count, body, 0)


def take_rows(wide, starts, tiles, cols, stride, put):
    step = max(6, 40 // len(starts))
    lane = lanes()
    for low in range(0, tiles, step):
        high = min(tiles, low + step)
        loaded = [
            [wide[pl.ds(first + c, 8, stride=stride), :] for c in range(low, high + 1)] for _, first, _, _ in starts
        ]
        results = []
        for (_, _, shift, keep_row), pieces in zip(starts, loaded):
            turn = lax.rem(LANE - shift, LANE)
            split = lane < LANE - shift
            turned = [roll_lanes(piece, turn) for piece in pieces]
            for c in range(low, high):
                out = jnp.where(split, turned[c - low], turned[c - low + 1])
                keep = keep_row
                if cols - c * LANE < LANE:
                    keep = keep & (lane < cols - c * LANE)
                results.append(jnp.where(keep, out, 0.0))
        at = 0
        for tag, _, _, _ in starts:
            for c in range(low, high):
                put(tag, c, results[at])
                at += 1


def spread(c, n, period):
    return pl.ds((c * period + n) * 25, 8, stride=3)


def collect(dest, c, period):
    return [
        dest[pl.ds((c * period + 8 * m) * 25 + 3 * j, 8, stride=25), :] for j in range(8) for m in range(period // 8)
    ]


def stage_tile(stage, slot, c, blocks):
    for i in range(0, len(blocks), 2):
        pair = jnp.concatenate([blocks[i], blocks[i + 1]], axis=0).astype(BF16)
        stage[slot, pl.ds(8 * i, 16), pl.ds(c * LANE, LANE)] = pair


def unpack_kernel(
    src, km, e8, ab, ur, rt, wt, raw, wide, dest, kstage, stage0, stage1, stage_t, stage3, raw_conv, sem_in, sem_out, sem_t
):
    role = lax.axis_index("section")
    total = src.shape[1] // LANE

    def out_copy(stage, slot, target):
        return pltpu.make_async_copy(stage.at[slot], target, sem_out.at[slot])

    @pl.when(role == 0)
    def _():
        blocks = 5
        count = 4 * blocks

        def flat_of(i):
            return CONV_END + HIGH_STRIDE * (i // blocks)

        def chunk_of(i):
            return flat_of(i) // LANE + 2200 * lax.rem(i, blocks)

        length = 640
        copy = pltpu.make_async_copy(src.at[:, pl.ds(0, length * LANE)], raw_conv.at[0], sem_t.at[0])
        copy.start()
        stream_start(count, LENS[0], total, chunk_of, src, raw, sem_in)
        copy.wait()
        widen(raw_conv, 0, length, wide)
        lane1 = lanes(1)
        dest[pl.ds(0, 64), :] = jnp.zeros((64, LANE), F32)
        for a in range(CHAR_V):
            flat = D_CHAR * a
            q, s = flat // LANE, flat % LANE
            here = wide[q : q + 1, :]
            out = roll_lanes(here, (LANE - s) % LANE) if s else here
            if s + D_CHAR > LANE:
                out = jnp.where(lane1 < LANE - s, out, roll_lanes(wide[q + 1 : q + 2, :], LANE - s))
            dest[a : a + 1, :] = jnp.where(lane1 < D_CHAR, out, jnp.where(lane1 == D_CHAR, 1.0, 0.0))
        table = dest[pl.ds(0, 64), :]
        for m in range(8):
            kstage[pl.ds(64 * m, 64), pl.ds(0, LANE)] = (
                pltpu.roll(table, 16 * m, 1) if m else table
            ).astype(BF16)
        copy = pltpu.make_async_copy(kstage.at[pl.ds(0, 512), pl.ds(0, LANE)], e8, sem_out.at[0])
        copy.start()
        copy.wait()
        tiles = FW // LANE
        rows = 112
        dest[pl.ds(0, rows * tiles), :] = jnp.zeros((rows * tiles, LANE), F32)

        def kernel_row(k, i, row):
            n, base = NFILT[k - 1], COLS[k - 1]
            edge = KOFF[k - 1] + n * i - base
            q, s = edge // LANE, edge % LANE
            for ct in range(base // LANE, (base + n - 1) // LANE + 1):
                out = wide[q + ct : q + ct + 1, :]
                if s:
                    after = roll_lanes(wide[q + ct + 1 : q + ct + 2, :], LANE - s)
                    out = jnp.where(lane1 < LANE - s, roll_lanes(out, LANE - s), after)
                at = ct * rows + row
                low, high = max(base - ct * LANE, 0), min(base + n - ct * LANE, LANE)
                if low > 0 or high < LANE:
                    out = jnp.where((lane1 >= low) & (lane1 < high), out, dest[at : at + 1, :])
                dest[at : at + 1, :] = out

        for k in range(1, 8):
            for i in range(k * D_CHAR):
                kernel_row(k, i, i + i // D_CHAR)
            kernel_row(k, k * D_CHAR, 15)
        kstage[...] = jnp.zeros_like(kstage)
        for ct in range(tiles):
            kstage[pl.ds(112, rows), pl.ds(ct * LANE, LANE)] = dest[pl.ds(ct * rows, rows), :].astype(BF16)
        copy = pltpu.make_async_copy(kstage.at[pl.ds(0, 368)], km, sem_out.at[0])
        copy.start()
        copy.wait()

        def target(i):
            return ab.at[i // blocks, pl.ds(pl.multiple_of(lax.rem(i, blocks) * 256, 256), 256)]

        def work(i, extra):
            block = lax.rem(i, blocks)
            inner = lax.rem(flat_of(i), LANE)

            def rows_of(i, carry):
                starts = []
                for n in range(4):
                    n = 4 * i + n
                    flat = inner + FILT * n
                    keep = 32 * (8 * block + sublanes()) + n <= FILT
                    starts.append((n, flat // LANE + extra, lax.rem(flat, LANE), keep))

                def put(n, c, value):
                    dest[spread(c, n, 32), :] = value

                take_rows(wide, starts, tiles, FILT, 275, put)
                return carry

            lax.fori_loop(0, 8, rows_of, 0)
            slot = lax.rem(i, 2)

            @pl.when(i >= 2)
            def _():
                out_copy(stage0, slot, target(i - 2)).wait()

            for c in range(tiles):
                stage_tile(stage0, slot, c, collect(dest, c, 32))
            out_copy(stage0, slot, target(i)).start()

        stream_blocks(count, LENS[0], total, chunk_of, src, raw, sem_in, wide, work)
        for i in (count - 2, count - 1):
            out_copy(stage0, i % 2, target(i)).wait()

    for layer in (1, 2):

        @pl.when(role == layer)
        def _(layer=layer):
            depth = FILT if layer == 1 else HID
            blocks = -(-depth // 128)
            recurrent = depth * 4 * HID
            count = blocks + 6

            def chunk_of(i):
                return jnp.where(i < blocks, 2600 * i, recurrent // LANE + 2600 * (i - blocks))

            stream_start(count, LENS[1], total, chunk_of, src, raw, sem_in)

            def target(i):
                at = jnp.where(i < blocks, i, i - blocks + 9)
                return ur.at[pl.ds(pl.multiple_of(at * 128, 128), 128)]

            def work(i, extra):
                inner = jnp.where(i < blocks, 0, recurrent % LANE)
                block = jnp.where(i < blocks, i, i - blocks)
                limit = jnp.where(i < blocks, depth, HID + 1)

                def rows_of(i, carry):
                    starts = []
                    for n in (2 * i, 2 * i + 1):
                        keep = 16 * (8 * block + sublanes()) + n < limit
                        for b in range(4):
                            flat = inner + 4 * HID * n + HID * b
                            starts.append(((n, b), flat // LANE + extra, lax.rem(flat, LANE), keep))

                    def put(tag, c, value):
                        dest[spread(6 * tag[1] + c, tag[0], 16), :] = value

                    take_rows(wide, starts, 6, HID, 325, put)
                    return carry

                lax.fori_loop(0, 8, rows_of, 0)
                slot = lax.rem(i, 2)

                @pl.when(i >= 2)
                def _():
                    out_copy(stage1, slot, target(i - 2)).wait()

                for c in range(24):
                    stage_tile(stage1, slot, c, collect(dest, c, 16))
                out_copy(stage1, slot, target(i)).start()

                @pl.when(i >= blocks)
                def _():
                    @pl.when(i >= blocks + 2)
                    def _():
                        turned_copy(i - 2).wait()

                    k = LANE * block + lanes(LANE)
                    for c in range(24):
                        turned = jnp.transpose(jnp.concatenate(collect(dest, c, 16), axis=0))
                        stage_t[slot, pl.ds(128 * c, 128), :] = jnp.where(k < HID, turned, 0.0).astype(BF16)
                    turned_copy(i).start()

            def turned_copy(i):
                slot = lax.rem(i, 2)
                at = pl.multiple_of((i - blocks) * LANE, LANE)
                return pltpu.make_async_copy(stage_t.at[slot], rt.at[:, pl.ds(at, LANE)], sem_t.at[slot])

            stream_blocks(count, LENS[1], total, chunk_of, src, raw, sem_in, wide, work)
            for i in (count - 2, count - 1):
                out_copy(stage1, i % 2, target(jnp.int32(i))).wait()
                turned_copy(jnp.int32(i)).wait()

    @pl.when(role == 3)
    def _():
        count = 11
        tiles = VW // LANE

        def chunk_of(i):
            return 5000 * i

        stream_start(count, LENS[3], total, chunk_of, src, raw, sem_in)

        def target(i):
            return wt.at[pl.ds(pl.multiple_of(i * 64, 64), 64)]

        def work(i, extra):
            def rows_of(n, carry):
                flat = VOCAB * n
                keep = 8 * (8 * i + sublanes()) + n < HID + 1

                def put(n, c, value):
                    dest[spread(c, n, 8), :] = value

                take_rows(wide, [(n, flat // LANE + extra, lax.rem(flat, LANE), keep)], tiles, VOCAB, 625, put)
                return carry

            lax.fori_loop(0, 8, rows_of, 0)
            slot = lax.rem(i, 2)

            @pl.when(i >= 2)
            def _():
                out_copy(stage3, slot, target(i - 2)).wait()

            for c in range(tiles):
                stage_tile(stage3, slot, c, collect(dest, c, 8))
            out_copy(stage3, slot, target(i)).start()

        stream_blocks(count, LENS[3], total, chunk_of, src, raw, sem_in, wide, work)
        for i in (count - 2, count - 1):
            out_copy(stage3, i % 2, target(jnp.int32(i))).wait()


def unpack_all(section_params):
    anywhere = pl.BlockSpec(memory_space=pl.ANY)
    return pl.pallas_call(
        unpack_kernel,
        out_shape=[
            jax.ShapeDtypeStruct((368, FW), BF16),
            jax.ShapeDtypeStruct((512, LANE), BF16),
            jax.ShapeDtypeStruct((4, 1280, FW), BF16),
            jax.ShapeDtypeStruct((15 * 128, ZW), BF16),
            jax.ShapeDtypeStruct((ZW, GW), BF16),
            jax.ShapeDtypeStruct((11 * 64, VW), BF16),
        ],
        in_specs=[anywhere],
        out_specs=[anywhere] * 6,
        scratch_shapes=[
            pltpu.VMEM((DEPTH, 1, LENS[3] * LANE), BF16),
            pltpu.VMEM((9312, LANE), F32),
            pltpu.VMEM((79 * 200, LANE), F32),
            pltpu.VMEM((512, FW), BF16),
            pltpu.VMEM((2, 256, FW), BF16),
            pltpu.VMEM((2, 128, ZW), BF16),
            pltpu.VMEM((2, ZW, LANE), BF16),
            pltpu.VMEM((2, 64, VW), BF16),
            pltpu.VMEM((1, 1, 640 * LANE), BF16),
            pltpu.SemaphoreType.DMA((DEPTH,)),
            pltpu.SemaphoreType.DMA((2,)),
            pltpu.SemaphoreType.DMA((2,)),
        ],
        compiler_params=pltpu.CompilerParams(vmem_limit_bytes=56 << 20),
        name="unpack",
    )(section_params)


def fblocks(width, step=256):
    return [(at, min(step, width - at)) for at in range(0, width, step)]


def mm(a, b):
    return jnp.dot(a, b, preferred_element_type=F32)


def mm_tn(a, b):
    return lax.dot_general(a, b, (((0,), (0,)), ((), ())), preferred_element_type=F32)


def mm_nt(a, b):
    return lax.dot_general(a, b, (((1,), (1,)), ((), ())), preferred_element_type=F32)


def sigmoid(x):
    return 0.5 * jnp.tanh(0.5 * x) + 0.5


def load(pairs, sem):
    copies = [pltpu.make_async_copy(a, b, sem.at[i]) for i, (a, b) in enumerate(pairs)]
    for copy in copies:
        copy.start()
    for copy in copies:
        copy.wait()


def column_mask(at, width, limit, rows):
    return lax.broadcasted_iota(jnp.int32, (rows, width), 1) + at < limit


def char_onehot(ids, t):
    rows = ids.shape[0]
    lane = lanes(rows)
    pieces = []
    for pair in range(4):
        j = 8 * t + 2 * pair
        left = ids[:, j : j + 1]
        right = ids[:, j + 1 : j + 2]
        hit = jnp.where(lane < 64, left, right) == lax.rem(lane, 64)
        pieces.append(jnp.where(hit, 1.0, 0.0).astype(BF16))
    return jnp.concatenate(pieces, axis=1)


def conv_steps(body):
    def step(p, carry):
        body(p, p // 8, True, lax.rem(p, 8), FILT)
        return carry

    lax.fori_loop(0, 15, step, 0)
    body(15, 1, True, 7, COLS[6])
    for p in range(16, WORD_CHARS):
        body(p, 2, False, p - 16, COLS[WORD_CHARS - p])


def conv_at(emb, km, tile, second, within, at, width):
    first = 112 - 16 * within
    if not isinstance(first, int):
        first = pl.multiple_of(first, 16)
    if second:
        window = jnp.concatenate([emb[tile], emb[tile + 1]], axis=1)
    else:
        window = emb[tile]
    return mm(window, km[pl.ds(first, window.shape[1]), pl.ds(at, width)])


def char_forward(ids, e8, km, ab, emb, total, feats, pres, out):
    rows = ids.shape[0]
    for t in range(3):
        emb[t] = mm(char_onehot(ids, t), e8[...]).astype(BF16)
    total[...] = jnp.zeros_like(total)

    def step(p, tile, second, within, limit):
        for at, width in fblocks(FW):
            if at >= limit:
                continue
            value = jnp.exp(jnp.tanh(conv_at(emb, km, tile, second, within, at, width)))
            if at + width > limit and limit < FILT:
                value = jnp.where(column_mask(at, width, limit, rows), value, 0.0)
            total[:, pl.ds(at, width)] += value

    conv_steps(step)
    for at, width in fblocks(FW):
        col = lax.broadcasted_iota(jnp.int32, (rows, width), 1) + at
        count = jnp.full((rows, width), float(WORD_CHARS), F32)
        for k in range(1, 7):
            count = jnp.where(col >= COLS[k], float(WORD_CHARS - k), count)
        value = jnp.log(total[:, pl.ds(at, width)]) - jnp.log(count)
        value = jnp.where(col < FILT, value, jnp.where(col == FILT, 1.0, 0.0))
        feats[0, :, pl.ds(at, width)] = value.astype(BF16)
    for layer in range(2):
        for at, width in fblocks(FW):
            cols = pl.ds(at, width)
            t_pre = mm(feats[layer], ab[2 * layer, pl.ds(0, FW), cols])
            h_pre = mm(feats[layer], ab[2 * layer + 1, pl.ds(0, FW), cols])
            pres[2 * layer, :, cols] = t_pre
            pres[2 * layer + 1, :, cols] = h_pre
            gate = sigmoid(t_pre)
            y = feats[layer, :, cols].astype(F32)
            value = gate * (h_pre * sigmoid(h_pre)) + (1.0 - gate) * y
            col = lax.broadcasted_iota(jnp.int32, (rows, width), 1) + at
            if layer == 0:
                value = jnp.where(col < FILT, value, jnp.where(col == FILT, 1.0, 0.0))
                feats[1, :, cols] = value.astype(BF16)
            else:
                out[:, cols] = jnp.where(col < FILT, value, 0.0).astype(BF16)


def conv_backward(km, kt, emb, emb_t, total, grad, dk, demb, relay):
    rows = grad.shape[0]
    kt[...] = jnp.transpose(km[pl.ds(112, LANE), :])
    for t in range(3):
        emb_t[pl.ds(LANE * t, LANE), :] = jnp.transpose(emb[t])
    emb_t[pl.ds(3 * LANE, LANE), :] = jnp.zeros((LANE, rows), BF16)
    dk[...] = jnp.zeros_like(dk)
    demb[...] = jnp.zeros_like(demb)
    for at, width in fblocks(FW):
        cols = pl.ds(at, width)
        grad[:, cols] = grad[:, cols] / total[:, cols]

    def step(p, tile, second, within, limit):
        relay(p)
        window_t = emb_t[pl.ds(p * 16 if isinstance(p, int) else pl.multiple_of(p * 16, 16), LANE), :]
        back = jnp.zeros((rows, LANE), F32)
        for at, width in fblocks(FW):
            if at >= limit:
                continue
            cols = pl.ds(at, width)
            act = jnp.tanh(conv_at(emb, km, tile, second, within, at, width))
            dz = grad[:, cols] * jnp.exp(act) * (1.0 - act * act)
            if at + width > limit and limit < FILT:
                dz = jnp.where(column_mask(at, width, limit, rows), dz, 0.0)
            dz = dz.astype(BF16)
            dk[:, cols] += mm(window_t, dz)
            back = back + mm(dz, kt[cols, :])
        lane = lanes(rows)
        back = jnp.where(lane < 112, back, 0.0)
        turned = pltpu.roll(back, 16 * within, 1)
        demb[tile] += jnp.where(lane >= 16 * within, turned, 0.0)
        if second:
            demb[tile + 1] += jnp.where(lane < 16 * within, turned, 0.0)

    conv_steps(step)


def table_backward(ids, demb, table):
    acc = jnp.zeros((64, LANE), F32)
    for t in range(3):
        hot = char_onehot(ids, t)
        value = demb[t]
        high = value.astype(BF16)
        low = (value - high.astype(F32)).astype(BF16)
        grads = mm_tn(hot, high) + mm_tn(hot, low)
        for m in range(8):
            block = grads[64 * m : 64 * m + 64, :]
            acc = acc + (pltpu.roll(block, LANE - 16 * m, 1) if m else block)
    table[...] = acc


def tile_rows(stage, base, value, row_tiles, col_tiles, first_col=0, pitch=None):
    pitch = col_tiles if pitch is None else pitch
    for r in range(row_tiles):
        for c in range(col_tiles):
            stage[base + r * pitch + first_col + c] = value[16 * r : 16 * r + 16, LANE * c : LANE * c + LANE].astype(BF16)


def six(x):
    return jnp.concatenate([x] * 6, axis=1)


ANYWHERE = pl.BlockSpec(memory_space=pl.ANY)
ON_CHIP = pl.BlockSpec(memory_space=pltpu.VMEM)
LIMIT = 56 << 20


def call(kernel, name, ins, specs, outs, scratch, aliases=None):
    return pl.pallas_call(
        kernel,
        out_shape=[jax.ShapeDtypeStruct(shape, dtype) for shape, dtype in outs],
        in_specs=specs,
        out_specs=[ANYWHERE] * len(outs),
        scratch_shapes=scratch,
        input_output_aliases=aliases or {},
        compiler_params=pltpu.CompilerParams(vmem_limit_bytes=LIMIT),
        name=name,
    )(*ins)


def vmem(shape, dtype):
    return pltpu.VMEM(shape, dtype)


def dmas(count):
    return pltpu.SemaphoreType.DMA((count,))


def char_forward_call(ids, km, e8, ab):
    n = ids.shape[0]

    def kernel(ids, km, e8, ab, y2_o, feats_o, pres_o, total_o, emb_o, km_v, e8_v, ab_v, y2, feats, pres, total, emb, sem):
        @pl.when(lax.axis_index("section") == 0)
        def _():
            load([(km, km_v), (e8, e8_v), (ab, ab_v)], sem)
            char_forward(ids, e8_v, km_v, ab_v, emb, total, feats, pres, y2)
            load([(y2, y2_o), (feats, feats_o), (pres, pres_o), (total, total_o), (emb, emb_o)], sem)

    outs = [
        ((n, FW), BF16),
        ((2, n, FW), BF16),
        ((4, n, FW), F32),
        ((n, FW), F32),
        ((3, n, LANE), BF16),
    ]
    scratch = [vmem(km.shape, BF16), vmem(e8.shape, BF16), vmem(ab.shape, BF16)]
    scratch += [vmem(shape, dtype) for shape, dtype in outs] + [dmas(5)]
    return call(kernel, "char_forward", (ids, km, e8, ab), [ON_CHIP] + [ANYWHERE] * 3, outs, scratch)


def char_backward_call(ids, grad, km, saved, dpre):
    n = ids.shape[0]
    total, emb = saved
    rows = SPLIT * CHUNK
    sems = pltpu.SemaphoreType.DMA

    def kernel(
        ids, grad, km, total, emb, dpre, tiles_o, right_o,
        grad_v, km_v, total_v, emb_v, kt, emb_t, dk, demb, table, stage, sem, send, recv,
    ):
        me = lax.axis_index("dp")

        def right_copy(k, i):
            span = pl.ds(pl.multiple_of(i * CHUNK, CHUNK), CHUNK)
            source = right_o.at[1, span] if k == 3 else dpre.at[span]
            return pltpu.make_async_remote_copy(
                source, right_o.at[k - 1, span], send.at[k - 1, i], recv.at[k - 1, i],
                device_id={"dp": quad_peer(me, 1 if k == 3 else k)}, device_id_type=pl.DeviceIdType.MESH,
            )

        def relay(p):
            if isinstance(p, int):
                return
            i = p // 3 - 1

            @pl.when((lax.rem(p, 3) == 0) & (p > 0) & (i < SPLIT))
            def _():
                right_copy(2, i).wait_recv()
                right_copy(3, i).start()

        @pl.when(lax.axis_index("section") == 0)
        def _():
            barrier = pltpu.get_barrier_semaphore()
            for k in range(1, QUAD):
                pl.semaphore_signal(
                    barrier, inc=1, device_id={"dp": quad_peer(me, k)}, device_id_type=pl.DeviceIdType.MESH
                )
            pl.semaphore_wait(barrier, QUAD - 1)
            for i in range(SPLIT):
                right_copy(2, i).start()
                right_copy(1, i).start()
            load([(grad, grad_v), (km, km_v), (total, total_v), (emb, emb_v)], sem)
            conv_backward(km_v, kt, emb_v, emb_t, total_v, grad_v, dk, demb, relay)
            table_backward(ids, demb, table)
            tile_rows(stage, 0, dk[...], 8, 9)
            tile_rows(stage, 72, table[...], 4, 1)
            load([(stage, tiles_o)], sem)
            for i in range(SPLIT):
                for k in range(1, QUAD):
                    right_copy(k, i).wait_send()
                    if k != 2:
                        right_copy(k, i).wait_recv()

    outs = [((CONV_TILES, 16, LANE), BF16), ((QUAD - 1, rows, 4 * FW), BF16)]
    scratch = [
        vmem((n, FW), F32), vmem(km.shape, BF16), vmem(total.shape, F32), vmem(emb.shape, BF16),
        vmem((FW, LANE), BF16), vmem((4 * LANE, n), BF16), vmem((LANE, FW), F32), vmem((3, n, LANE), F32),
        vmem((64, LANE), F32), vmem((CONV_TILES, 16, LANE), BF16), dmas(4), sems((QUAD - 1, SPLIT)), sems((QUAD - 1, SPLIT)),
    ]
    return pl.pallas_call(
        kernel,
        out_shape=[jax.ShapeDtypeStruct(shape, dtype) for shape, dtype in outs],
        in_specs=[ON_CHIP] + [ANYWHERE] * 5,
        out_specs=[ANYWHERE] * 2,
        scratch_shapes=scratch,
        compiler_params=pltpu.CompilerParams(vmem_limit_bytes=LIMIT, collective_id=4, has_side_effects=True),
        name="char_backward",
    )(ids, grad, km, total, emb, dpre)


CONV_TILES = 76
TILES = 3648


def turned_tile(left, right, shift):
    rows = right.shape[0]
    if shift:
        mixed = jnp.where(
            lanes(rows) < shift, pltpu.roll(left.astype(F32), shift, 1), pltpu.roll(right.astype(F32), shift, 1)
        )
        right = mixed.astype(BF16)
    return jnp.transpose(right)


def each_vocab(body, step=2048):
    whole = VW // step

    def one(i, carry):
        body(pl.multiple_of(i * step, step), step)
        return carry

    lax.fori_loop(0, whole, one, 0)
    body(whole * step, VW - whole * step)


def output_weights_call(h, dl):
    n = h.shape[0]
    rows = 704
    pitch = VW // LANE

    def kernel(h, dl, tiles_o, h_v, dl_v, h_t, stage, sem):
        @pl.when(lax.axis_index("section") == 3)
        def _():
            load([(h, h_v), (dl, dl_v)], sem)
            lane = lanes(n)
            for c in range(6):
                value = h_v[:, pl.ds(LANE * c, LANE)].astype(F32)
                value = jnp.where(lane + c * LANE == HID, 1.0, value).astype(BF16)
                h_t[pl.ds(LANE * c, LANE), :] = jnp.transpose(value)

            def body(at, width):
                first = at // LANE
                for top, count in fblocks(rows):
                    value = mm(h_t[pl.ds(top, count), :], dl_v[:, pl.ds(at, width)])
                    for r in range(count // 16):
                        for c in range(width // LANE):
                            stage[(top // 16 + r) * pitch + first + c] = value[
                                16 * r : 16 * r + 16, LANE * c : LANE * c + LANE
                            ].astype(BF16)

            each_vocab(body, 256)
            count = rows // 16 * pitch
            load([(stage.at[pl.ds(0, count)], tiles_o.at[pl.ds(0, count)])], sem)

    scratch = [
        vmem((n, GW), BF16), vmem((n, VW), BF16), vmem((6 * LANE, n), BF16),
        vmem((rows // 16 * pitch, 16, LANE), BF16), dmas(2),
    ]
    return call(
        kernel, "output_weights", (h, dl), [ANYWHERE] * 2, [((TILES, 16, LANE), BF16)], scratch
    )[0]


CHUNK = 32
GROUPS_OUT = (3, 3, 2, 1)


def lstm_steps(first, count, keep, carry, r, gates, cells, prevs, hiddens):
    def step(s, carry):
        h, c = carry
        at = pl.ds(pl.multiple_of((first + s) * 8, 8), 8)
        k = six(keep[at, :])
        hp = h * k
        cp = c * k
        prevs[at, :] = hp
        z = gates[at, :] + mm(hp.astype(BF16), r[...])
        i = sigmoid(z[:, 0:GW])
        f = sigmoid(z[:, GW : 2 * GW])
        o = sigmoid(z[:, 2 * GW : 3 * GW])
        g = jnp.tanh(z[:, 3 * GW :])
        c = f * cp + i * g
        h = (o * jnp.tanh(c)).astype(BF16).astype(F32)
        gates[at, :] = jnp.concatenate([i, f, o, g], axis=1)
        cells[at, :] = c
        hiddens[at, :] = h
        return h, c

    return lax.fori_loop(0, count, step, carry)


def lstm_back_steps(first, count, keep, c0, carry, rt, gates, cells, dhs):
    def step(s, carry):
        dh_next, dc_next = carry
        t = first + count - 1 - s
        at = pl.ds(pl.multiple_of(t * 8, 8), 8)
        before = pl.ds(pl.multiple_of(jnp.maximum(t - 1, 0) * 8, 8), 8)
        k = six(keep[at, :])
        saved = gates[at, :]
        i, f, o, g = [saved[:, GW * b : GW * b + GW] for b in range(4)]
        cp = jnp.where(t > 0, cells[before, :], c0[...]) * k
        ct = jnp.tanh(cells[at, :])
        dh = dhs[at, :] + dh_next
        dc = dc_next + dh * o * (1.0 - ct * ct)
        dz = jnp.concatenate(
            [dc * g * i * (1.0 - i), dc * cp * f * (1.0 - f), dh * ct * o * (1.0 - o), dc * i * (1.0 - g * g)], axis=1
        ).astype(BF16)
        gates[at, :] = dz.astype(F32)
        return k * mm(dz, rt[...]), k * dc * f

    return lax.fori_loop(0, count, step, carry)


def output_rows(first, count, h, w, targets, valid, logits, dl, top, part, dh, loss, dh16):
    at_rows = pl.ds(first, count)
    depth = w.shape[0]
    own = pl.ds(0, count)
    top[own, :] = jnp.full((count, LANE), -jnp.inf, F32)

    def forward(at, width):
        z = mm(h[at_rows, pl.ds(0, depth)], w[:, pl.ds(at, width)])
        if isinstance(at, int):
            z = jnp.where(column_mask(at, width, VOCAB, count), z, -jnp.inf)
        logits[own, pl.ds(at, width)] = z
        best = top[own, :]
        for c in range(width // LANE):
            best = jnp.maximum(best, z[:, LANE * c : LANE * c + LANE])
        top[own, :] = best

    each_vocab(forward)
    best = jnp.max(top[own, :], axis=1, keepdims=True)
    part[:, own, :] = jnp.zeros((2, count, LANE), F32)
    wanted = targets[at_rows, :]

    def exponents(at, width):
        z = logits[own, pl.ds(at, width)]
        e = jnp.exp(z - best)
        logits[own, pl.ds(at, width)] = e
        for c in range(width // LANE):
            part[0, own, :] += e[:, LANE * c : LANE * c + LANE]
            hit = lanes(count) + (at + LANE * c) == wanted
            part[1, own, :] += jnp.where(hit, z[:, LANE * c : LANE * c + LANE], 0.0)

    each_vocab(exponents)
    total = jnp.sum(part[0, own, :], axis=1, keepdims=True)
    picked = jnp.sum(part[1, own, :], axis=1, keepdims=True)
    counts = valid[at_rows, :]
    loss[...] += jnp.sum(counts * (best + jnp.log(total) - picked), axis=0, keepdims=True)
    share = counts / total
    dh[:, own] = jnp.zeros((depth, count), F32)

    def backward(at, width):
        e = logits[own, pl.ds(at, width)]
        pieces = []
        for c in range(width // LANE):
            hit = lanes(count) + (at + LANE * c) == wanted
            grad = e[:, LANE * c : LANE * c + LANE] * share - jnp.where(hit, counts, 0.0)
            pieces.append(grad.astype(BF16))
        grad = jnp.concatenate(pieces, axis=1)
        dl[at_rows, pl.ds(at, width)] = grad
        dh[:, own] += mm_nt(w[:, pl.ds(at, width)], grad)

    each_vocab(backward)
    for at, width in fblocks(depth):
        value = jnp.transpose(dh[pl.ds(at, width), own])
        dh16[at_rows, pl.ds(at, width)] = jnp.where(column_mask(at, width, HID, count), value, 0.0).astype(BF16)


QUAD = 4
LEFT0 = 35 * LANE
LEFT1 = 14 * LANE
LEFT2 = 11 * LANE
LEFT_ROOM = 41 * LANE


def quad_peer(me, k):
    place = lax.rem(me, QUAD)
    pair, side = place // 2, lax.rem(place, 2)
    return me + (k % 2) * (1 - 2 * side) + (k // 2) * (2 - 4 * pair)


def turn_features(feats, turned):
    n = feats.shape[1]
    zero = jnp.zeros((n, LANE), BF16)
    for segment in range(4):
        start = segment * (FILT + 1)
        shift, first, last = start % LANE, start // LANE, (start + FILT) // LANE
        for c in range(last - first + 1):
            left = feats[segment // 2, :, pl.ds(LANE * (c - 1), LANE)] if c > 0 else zero
            right = feats[segment // 2, :, pl.ds(LANE * c, LANE)] if c < 9 else zero
            tile = turned_tile(left, right, shift)
            at = pl.ds(LANE * (first + c), LANE)
            if c == 0 and segment > 0:
                tile = tile + turned[at, :]
            turned[at, :] = tile


def turn_inputs(x, prevs, depth, turned):
    n = prevs.shape[0]
    first, shift = depth // LANE, depth % LANE
    end = depth + HID
    zero = jnp.zeros((n, LANE), F32)
    lane = lanes(n)
    for c in range(end // LANE + 1):
        if c < first:
            mixed = x[:, pl.ds(LANE * c, LANE)]
        else:
            k = c - first
            left = prevs[:, pl.ds(LANE * (k - 1), LANE)].astype(F32) if 0 < k < 7 else zero
            right = prevs[:, pl.ds(LANE * k, LANE)].astype(F32) if k < 6 else zero
            before = pltpu.roll(left, shift, 1) if k else x[:, pl.ds(LANE * c, LANE)].astype(F32)
            mixed = jnp.where(lane < shift, before, pltpu.roll(right, shift, 1))
            mixed = jnp.where(lane + c * LANE == end, 1.0, mixed).astype(BF16)
        turned[pl.ds(LANE * c, LANE), :] = jnp.transpose(mixed)


SPLIT = 3
AB_PARTS = ((0, 640), (640, 512))


def highway_chunk(rows, slot, dy, feats, pres, grad, dpre, w):
    def cut(m, at, width):
        return pl.ds(m * FW + at, width)

    for at, width in fblocks(FW):
        grad[rows, pl.ds(at, width)] = dy[rows, pl.ds(at, width)].astype(F32)
    for layer in (1, 0):
        own = pl.ds(slot, CHUNK)
        for at, width in fblocks(FW):
            cols = pl.ds(at, width)
            g = grad[rows, cols]
            gate = sigmoid(pres[own, cut(2 * layer, at, width)])
            q = pres[own, cut(2 * layer + 1, at, width)]
            sig = sigmoid(q)
            y = feats[layer, rows, cols].astype(F32)
            dpre[rows, cut(2 * layer, at, width)] = (g * (q * sig - y) * gate * (1.0 - gate)).astype(BF16)
            dpre[rows, cut(2 * layer + 1, at, width)] = (g * gate * sig * (1.0 + q * (1.0 - sig))).astype(BF16)
            grad[rows, cols] = g * (1.0 - gate)
        turned = [jnp.transpose(dpre[rows, cut(2 * layer + i, 0, FW)]) for i in range(2)]
        for half, (row, count) in enumerate(AB_PARTS):
            for at, width in fblocks(count):
                cols = pl.ds(row + at, width)
                back = jnp.zeros((width, CHUNK), F32)
                for i in range(2):
                    part = w[pl.ds(at, width), pl.ds((2 * (2 * layer + i) + half) * FW, FW)]
                    back = back + mm(part, turned[i])
                value = grad[rows, cols] + jnp.transpose(back)
                if row + at + width > FILT:
                    value = jnp.where(column_mask(row + at, width, FILT, CHUNK), value, 0.0)
                grad[rows, cols] = value


def recurrent_call(y2, feats, pres, ab, ur, rt, wt, resets, target_ids, remaining, state):
    n = y2.shape[0]
    real_steps = resets.shape[1]
    chunks = n // CHUNK
    steps = CHUNK // 8
    depth_w = wt.shape[0]
    MESH = pl.DeviceIdType.MESH

    def kernel(
        y2, feats, pres, ab, ur, rt, wt, resets, target_ids, remaining, state,
        grad_o, dpre_o, right_o, xb_o, lhs_o, dz_o, dl_o, x_q, h_q, loss_o, bias_o,
        keep, valid, targets, feats_v, turned, pb, x1, xb, hb, db, ob, dy, u, r, r_t, w, start, gates, cells, prevs, hs, dhs, dz16,
        logits, dl, top, part, dh, loss,
        sem_in, sem_out, send_y, recv_y, send_f, recv_f, send_b, recv_b, send_d, recv_d,
        send_x, recv_x, send_h, recv_h, send_z, recv_z, sem_l, sem_p,
    ):
        role = lax.axis_index("section")
        me = lax.axis_index("dp")
        loss[...] = jnp.zeros_like(loss)
        bias_o[...] = jnp.zeros_like(bias_o)

        def to(step, source, target, send, recv):
            return pltpu.make_async_remote_copy(
                source, target, send, recv, device_id={"section": role + step}, device_id_type=MESH
            )

        def span(c):
            return pl.ds(pl.multiple_of(c * CHUNK, CHUNK), CHUNK)

        def forward_copy(c, step):
            return to(step, hb.at[span(c)], xb.at[span(c)], send_f.at[c], recv_f.at[c])

        def backward_copy(c, step):
            return to(step, ob.at[span(c)], db.at[span(c)], send_b.at[c], recv_b.at[c])

        def feature_copy(step):
            return to(step, y2, x1, send_y.at[0], recv_y.at[0])

        def last_copy(c, step):
            return to(step, dy.at[span(c)], dy.at[span(c)], send_d.at[c], recv_d.at[c])

        def quad_copy(source, target, send, recv, k):
            return pltpu.make_async_remote_copy(
                source, target, send, recv, device_id={"dp": quad_peer(me, k)}, device_id_type=MESH
            )

        def input_copy(k):
            return quad_copy(x1, x_q.at[k - 1, 0], send_x.at[k - 1, 0], recv_x.at[k - 1, 0], k)

        def layer_copy(c, k):
            target = x_q.at[k - 1, 0, span(c), pl.ds(0, GW)]
            return quad_copy(xb.at[span(c)], target, send_x.at[k - 1, c], recv_x.at[k - 1, c], k)

        def feats_copy(k):
            return quad_copy(feats_v, x_q.at[k - 1], send_x.at[k - 1, 0], recv_x.at[k - 1, 0], k)

        def hidden_copy(c, k):
            return quad_copy(pb.at[span(c)], h_q.at[k - 1, span(c)], send_h.at[k - 1, c], recv_h.at[k - 1, c], k)

        def each_peer(body):
            for k in range(1, QUAD):
                body(k)

        def each_chunk(body, first=0):
            def step(c, carry):
                body(c)
                return carry

            lax.fori_loop(first, chunks, step, 0)

        def turned_out(g, rows):
            copy = pltpu.make_async_copy(turned.at[pl.ds(0, rows)], lhs_o.at[g, pl.ds(0, rows)], sem_l.at[0])
            copy.start()
            copy.wait()

        def fetch(source, target):
            copy = pltpu.make_async_copy(source, target, sem_l.at[1])
            copy.start()
            copy.wait()

        def dpre_copy(c, k):
            rows = pl.ds(pl.multiple_of((c - SPLIT) * CHUNK, CHUNK), CHUNK)
            source = right_o.at[1, rows] if k == 3 else dl.at[span(c), pl.ds(0, 4 * FW)]
            return quad_copy(
                source, right_o.at[k - 1, rows], send_z.at[k - 1, c], recv_z.at[k - 1, c], 1 if k == 3 else k
            )

        def right_copy(k, c):
            source = dz_o.at[1, span(c)] if k == 3 else dz16.at[span(c)]
            return quad_copy(
                source, dz_o.at[k - 1, span(c)], send_z.at[k - 1, c], recv_z.at[k - 1, c], 1 if k == 3 else k
            )

        def exchange(copy, c, first):
            @pl.when(c >= first)
            def _():
                copy(c, 2).start()
                copy(c, 1).start()

            @pl.when((c < chunks - 1) & (c + 1 >= first))
            def _():
                copy(c + 1, 2).wait_recv()
                copy(c + 1, 3).start()

        def exchanged(copy, first):
            if first == 0:
                copy(0, 2).wait_recv()
                copy(0, 3).start()

            def settle(c):
                for k in range(1, QUAD):
                    copy(c, k).wait_send()
                    if k != 2:
                        copy(c, k).wait_recv()

            each_chunk(settle, first)

        def inputs(which):
            if which == 0:
                pairs = [(feats, feats_v)]
                for m in range(4):
                    for half, (row, count) in enumerate(AB_PARTS):
                        target = w.at[pl.ds(0, count), pl.ds((2 * m + half) * FW, FW)]
                        pairs.append((ab.at[m, pl.ds(row, count)], target))
            elif which == 3:
                pairs = [(wt, w)]
            else:
                depth = FW if which == 1 else GW
                pairs = [
                    (ur.at[pl.ds(0, depth)], u.at[pl.ds(0, depth)]),
                    (ur.at[pl.ds(FW, GW)], r),
                    (rt, r_t),
                ]
            return [pltpu.make_async_copy(a, b, sem_in.at[i]) for i, (a, b) in enumerate(pairs)]

        for which in range(4):

            @pl.when(role == which)
            def _(which=which):
                for copy in inputs(which):
                    copy.start()

        @pl.when((role == 1) | (role == 2))
        def _():
            start[...] = jnp.zeros_like(start)
            for which in (1, 2):

                @pl.when(role == which)
                def _(which=which):
                    for half in range(2):
                        start[half, :, pl.ds(0, HID)] = state[which - 1, half]

            for t in range(n // 8):
                rows = pl.ds(8 * t, 8)
                kept = jnp.zeros((8, LANE), F32)
                if t < real_steps:
                    kept = 1.0 - jnp.broadcast_to(resets[:, t : t + 1], (8, LANE)).astype(F32)
                keep[rows, :] = kept

        @pl.when(role == 3)
        def _():
            left_words = jnp.broadcast_to(remaining[...], (8, LANE))
            for t in range(n // 8):
                rows = pl.ds(8 * t, 8)
                if t < real_steps:
                    valid[rows, :] = jnp.where(left_words > t, 1.0, 0.0)
                    targets[rows, :] = jnp.broadcast_to(target_ids[:, t : t + 1], (8, LANE))
                else:
                    valid[rows, :] = jnp.zeros((8, LANE), F32)
                    targets[rows, :] = jnp.full((8, LANE), -1, jnp.int32)

        barrier = pltpu.get_barrier_semaphore()

        @pl.when(role > 0)
        def _():
            pl.semaphore_signal(barrier, inc=1, device_id={"section": role - 1}, device_id_type=MESH)

        @pl.when(role < 3)
        def _():
            pl.semaphore_signal(barrier, inc=1, device_id={"section": role + 1}, device_id_type=MESH)

        for k in range(1, QUAD):
            pl.semaphore_signal(barrier, inc=1, device_id={"dp": quad_peer(me, k)}, device_id_type=MESH)
        pl.semaphore_wait(barrier, lax.min(role, 1) + lax.min(3 - role, 1) + QUAD - 1)

        @pl.when(role == 0)
        def _():
            feature_copy(1).start()
            for copy in inputs(0):
                copy.wait()
            each_peer(lambda k: feats_copy(k).start())
            turn_features(feats_v, turned)
            turned_out(QUAD - 1, LEFT0)
            feature_copy(1).wait_send()
            each_peer(lambda k: feats_copy(k).wait_send())
            for k in range(1, QUAD):
                feats_copy(k).wait_recv()
                fetch(x_q.at[k - 1], feats_v)
                turn_features(feats_v, turned)
                turned_out(k - 1, LEFT0)
            fetch(feats, feats_v)

            def pres_copy(c, m):
                slot = lax.rem(c, 2)
                target = logits.at[pl.ds(pl.multiple_of(slot * CHUNK, CHUNK), CHUNK), pl.ds(m * FW, FW)]
                return pltpu.make_async_copy(pres.at[m, span(c)], target, sem_p.at[slot, m])

            for m in range(4):
                pres_copy(chunks - 1, m).start()

            def chunk(i, carry):
                c = chunks - 1 - i

                @pl.when(c > 0)
                def _():
                    for m in range(4):
                        pres_copy(c - 1, m).start()

                for m in range(4):
                    pres_copy(c, m).wait()
                last_copy(c, 1).wait_recv()
                highway_chunk(span(c), pl.multiple_of(lax.rem(c, 2) * CHUNK, CHUNK), dy, feats_v, logits, gates, dl, w)

                exchange(dpre_copy, c, SPLIT)
                return carry

            lax.fori_loop(0, chunks, chunk, 0)
            copies = [
                pltpu.make_async_copy(gates.at[:, pl.ds(0, FW)], grad_o, sem_out.at[0]),
                pltpu.make_async_copy(dl.at[:, pl.ds(0, 4 * FW)], dpre_o, sem_out.at[1]),
            ]
            for copy in copies:
                copy.start()
            for at, width in fblocks(FW):
                cols = pl.ds(at, width)
                bias_o[:, cols] = jnp.sum(dl[:, cols].astype(F32), axis=0, keepdims=True)
            for copy in copies:
                copy.wait()

            exchanged(dpre_copy, SPLIT)

        @pl.when((role == 1) | (role == 2))
        def _():
            for which in (1, 2):

                @pl.when(role == which)
                def _(which=which):
                    for copy in inputs(which):
                        copy.wait()

            bias = r[pl.ds(HID, 1), :].astype(F32)

            @pl.when(role == 1)
            def _():
                feature_copy(-1).wait_recv()
                each_peer(lambda k: input_copy(k).start())
                for at, width in fblocks(ZW):
                    cols = pl.ds(at, width)
                    gates[:, cols] = mm(x1[...], u[:, cols]) + bias[:, at : at + width]

            def chunk_forward(c, carry):
                @pl.when(role == 2)
                def _():
                    forward_copy(c, -1).wait_recv()
                    each_peer(lambda k: layer_copy(c, k).start())
                    for at, width in fblocks(ZW):
                        cols = pl.ds(at, width)
                        gates[span(c), cols] = mm(xb[span(c), :], u[pl.ds(0, GW), cols]) + bias[:, at : at + width]

                carry = lstm_steps(c * steps, steps, keep, carry, r, gates, cells, prevs, hs)
                hb[span(c), :] = hs[span(c), :].astype(BF16)
                forward_copy(c, 1).start()
                pb[span(c), :] = prevs[span(c), :].astype(BF16)
                each_peer(lambda k: hidden_copy(c, k).start())
                return carry

            h0 = start[0].astype(BF16).astype(F32)
            lax.fori_loop(0, chunks, chunk_forward, (h0, start[1]))

            def turn_all(which):
                depth, rows = (FILT, LEFT1) if which == 1 else (HID, LEFT2)
                width = FW if which == 1 else GW
                turn_inputs(x1 if which == 1 else xb, pb, depth, turned)
                turned_out(QUAD - 1, rows)
                if which == 1:
                    each_peer(lambda k: input_copy(k).wait_send())
                    each_peer(lambda k: input_copy(k).wait_recv())
                else:

                    def moved(c):
                        for k in range(1, QUAD):
                            layer_copy(c, k).wait_send()
                            layer_copy(c, k).wait_recv()

                    each_chunk(moved)

                def hidden_moved(c):
                    for k in range(1, QUAD):
                        hidden_copy(c, k).wait_send()
                        hidden_copy(c, k).wait_recv()

                each_chunk(hidden_moved)
                for g in range(QUAD - 1):
                    fetch(x_q.at[g, 0, :, pl.ds(0, width)], feats_v.at[0, :, pl.ds(0, width)])
                    fetch(h_q.at[g], pb)
                    turn_inputs(feats_v.at[0], pb, depth, turned)
                    turned_out(g, rows)

            @pl.when(role == 1)
            def _():
                turn_all(1)

            def chunk_backward(i, carry):
                c = chunks - 1 - i
                backward_copy(c, 1).wait_recv()
                dhs[span(c), :] = db[span(c), :].astype(F32)
                carry = lstm_back_steps(c * steps, steps, keep, start.at[1], carry, r_t, gates, cells, dhs)
                dz16[span(c), :] = gates[span(c), :].astype(BF16)

                dz_t = jnp.transpose(dz16[span(c), :])

                @pl.when(role == 1)
                def _():
                    for at, width in fblocks(FW):
                        value = jnp.transpose(mm(u[pl.ds(at, width), :], dz_t))
                        if at + width > FILT:
                            value = jnp.where(column_mask(at, width, FILT, CHUNK), value, 0.0)
                        dy[span(c), pl.ds(at, width)] = value.astype(BF16)
                    last_copy(c, -1).start()

                @pl.when(role == 2)
                def _():
                    for at, width in fblocks(GW):
                        value = jnp.transpose(mm(u[pl.ds(at, width), :], dz_t))
                        if at + width > HID:
                            value = jnp.where(column_mask(at, width, HID, CHUNK), value, 0.0)
                        ob[span(c), pl.ds(at, width)] = value.astype(BF16)
                    backward_copy(c, -1).start()

                exchange(lambda c, k: right_copy(k, c), c, 0)
                return carry

            zero = jnp.zeros((8, GW), F32)
            lax.fori_loop(0, chunks, chunk_backward, (zero, zero))

            own_right = pltpu.make_async_copy(dz16, dz_o.at[QUAD - 1], sem_out.at[1])
            own_right.start()

            @pl.when(role == 1)
            def _():
                each_chunk(lambda c: last_copy(c, -1).wait_send())

            @pl.when(role == 2)
            def _():
                turn_all(2)
                each_chunk(lambda c: backward_copy(c, -1).wait_send())

            own_right.wait()
            exchanged(lambda c, k: right_copy(k, c), 0)

            def sent(c, carry):
                forward_copy(c, 1).wait_send()
                return carry

            lax.fori_loop(0, chunks, sent, 0)

        @pl.when(role == 3)
        def _():
            for copy in inputs(3):
                copy.wait()
            ob[...] = jnp.zeros_like(ob)
            done = 0
            for count in GROUPS_OUT:
                rows = pl.ds(done * CHUNK, count * CHUNK)
                for c in range(done, done + count):
                    forward_copy(c, -1).wait_recv()
                value = xb[rows, pl.ds(5 * LANE, LANE)].astype(F32)
                value = jnp.where(lanes(count * CHUNK) + 5 * LANE == HID, 1.0, value)
                xb[rows, pl.ds(5 * LANE, LANE)] = value.astype(BF16)
                output_rows(
                    done * CHUNK, count * CHUNK, xb, w, targets, valid, logits, dl, top, part, dh, loss, ob
                )
                for c in range(done, done + count):
                    backward_copy(c, -1).start()
                done += count
            copies = [
                pltpu.make_async_copy(xb, xb_o, sem_out.at[0]),
                pltpu.make_async_copy(dl, dl_o, sem_out.at[1]),
            ]
            for copy in copies:
                copy.start()
            for c in range(chunks):
                backward_copy(c, -1).wait_send()
            for copy in copies:
                copy.wait()

        loss_o[...] = loss[...]

    most = max(GROUPS_OUT) * CHUNK
    sems = pltpu.SemaphoreType.DMA
    outs = [
        ((n, FW), F32), ((n, 4 * FW), BF16), ((QUAD - 1, n - SPLIT * CHUNK, 4 * FW), BF16), ((n, GW), BF16),
        ((QUAD, LEFT_ROOM, n), BF16), ((QUAD, n, ZW), BF16), ((n, VW), BF16), ((QUAD - 1, 2, n, FW), BF16),
        ((QUAD - 1, n, GW), BF16),
    ]
    scratch = [
        vmem((n, LANE), F32), vmem((n, LANE), F32), vmem((n, LANE), jnp.int32),
        vmem((2, n, FW), BF16), vmem((LEFT0, n), BF16), vmem((n, GW), BF16),
        vmem((n, FW), BF16), vmem((n, GW), BF16), vmem((n, GW), BF16), vmem((n, GW), BF16), vmem((n, GW), BF16),
        vmem((n, FW), BF16), vmem((FW, ZW), BF16), vmem((GW, ZW), BF16), vmem((ZW, GW), BF16), vmem(wt.shape, BF16),
        vmem((2, 8, GW), F32), vmem((n, ZW), F32), vmem((n, GW), F32), vmem((n, GW), F32), vmem((n, GW), F32),
        vmem((n, GW), F32), vmem((n, ZW), BF16),
        vmem((most, VW), F32), vmem((n, VW), BF16), vmem((most, LANE), F32), vmem((2, most, LANE), F32),
        vmem((depth_w, LANE), F32), vmem((1, LANE), F32),
        dmas(12), dmas(3), dmas(1), dmas(1), dmas(chunks), dmas(chunks), dmas(chunks), dmas(chunks), dmas(chunks), dmas(chunks),
        sems((QUAD - 1, chunks)), sems((QUAD - 1, chunks)), sems((QUAD - 1, chunks)), sems((QUAD - 1, chunks)),
        sems((QUAD - 1, chunks)), sems((QUAD - 1, chunks)), dmas(2), sems((2, 4)),
    ]
    return pl.pallas_call(
        kernel,
        out_shape=[jax.ShapeDtypeStruct(shape, dtype) for shape, dtype in outs]
        + [jax.ShapeDtypeStruct((1, LANE), F32), jax.ShapeDtypeStruct((1, FW), F32)],
        in_specs=[ANYWHERE] * 7 + [ON_CHIP] * 4,
        out_specs=[ANYWHERE] * 9 + [ON_CHIP] * 2,
        scratch_shapes=scratch,
        compiler_params=pltpu.CompilerParams(vmem_limit_bytes=62 << 20, collective_id=3, has_side_effects=True),
        name="recurrent",
    )(y2, feats, pres, ab, ur, rt, wt, resets, target_ids, remaining, state)


FORM = (
    (FILT, 9, 4 * (FILT + 1), CONV_END, CONV_TILES, 32),
    (4 * HID, 24, FILT + HID + 1, 0, 0, 16),
    (4 * HID, 24, 2 * HID + 1, 0, 0, 16),
    (VOCAB, 79, HID + 1, 0, 0, 16),
)


def slab(role, dest, share):
    width, pitch, rows, before, lead, period = FORM[role]
    low = lax.max if not isinstance(dest, int) else max
    high = lax.min if not isinstance(dest, int) else min
    one = (lambda v: v) if isinstance(dest, int) else jnp.int32
    start = low(one(share) * dest - before, one(0))
    first = start // width // period * period
    end = high((share * (dest + 1) - before + width - 1) // width, one(rows))
    count = low((end - first + 15) // 16, one(0)) * pitch
    tile = lead + first // 16 * pitch
    if lead:
        if isinstance(dest, int):
            if dest == 0:
                tile, count = 0, count + lead
        else:
            head = lax.max(1 - dest, 0)
            tile = tile - lead * head
            count = count + lead * head
    return first, tile, count


def slab_pieces(count, size):
    return (count + size - 1) // size


def gather_sum_call(tiles, groups, share):
    pair = 2
    across = groups // pair
    size = 64 if across <= 4 else 32
    pieces = max(slab_pieces(slab(3, dest, share)[2], size) for dest in range(groups))
    room = pieces * size
    line = across <= 4
    slots = across + 1 if line else across - 1
    MESH = pl.DeviceIdType.MESH

    def kernel(
        tiles, out, own, got1, got2, acc, own_sem, send1, recv1, send2, recv2, out_sem,
    ):
        role = lax.axis_index("section")
        me = lax.axis_index("dp")
        mine, side = me // pair, lax.rem(me, pair)
        other = mine * pair + (1 - side)

        def at_place(place):
            return {"dp": place * pair + side}

        def part(ref, slot, p):
            return ref.at[slot, pl.ds(pl.multiple_of(p * size, size), size)]

        def span(p):
            return pl.ds(pl.multiple_of(p * size, size), size)

        def loop(count, body):
            def step(p, carry):
                body(p)
                return carry

            lax.fori_loop(0, count, step, 0)

        def run(shape_of):
            def count_to(place, which):
                return shape_of(place * pair + which)[1]

            def own_copy(place, p):
                tile, _ = shape_of(place * pair + side)
                return pltpu.make_async_copy(
                    tiles.at[pl.ds(tile + p * size, size)], part(own, place, p), own_sem.at[place, p]
                )

            def first_copy(place, p):
                tile, _ = shape_of(place * pair + 1 - side)
                return pltpu.make_async_remote_copy(
                    tiles.at[pl.ds(tile + p * size, size)], part(got1, place, p), send1.at[place, p], recv1.at[place, p],
                    device_id={"dp": other}, device_id_type=MESH,
                )

            def begin(place):
                loop(count_to(place, 1 - side), lambda p: first_copy(place, p).start())
                loop(count_to(place, side), lambda p: own_copy(place, p).start())

            def hop_copy(place, up, p):
                if line:
                    target = mine + 1 if up else mine - 1
                    slot = jnp.where(place == mine + 1, across, place) if up else place
                else:
                    target = place
                    slot = lax.rem(place - mine + across, across) - 1
                return pltpu.make_async_remote_copy(
                    part(own, place, p), part(got2, slot, p), send2.at[place, p], recv2.at[slot, p],
                    device_id=at_place(target), device_id_type=MESH,
                )

            def arrived(slot, p):
                return pltpu.make_async_remote_copy(
                    part(own, 0, p), part(got2, slot, p), send2.at[0, p], recv2.at[slot, p],
                    device_id=at_place(lax.rem(mine + 1, across)), device_id_type=MESH,
                )

            def forward(place, up, has_before):
                def body(p):
                    own_copy(place, p).wait()
                    first_copy(place, p).wait_recv()
                    at = span(p)
                    own[place, at] = (own[place, at].astype(F32) + got1[place, at].astype(F32)).astype(BF16)
                    hop_copy(place, up, p).start()

                def body_sum(p):
                    own_copy(place, p).wait()
                    first_copy(place, p).wait_recv()
                    arrived(place, p).wait_recv()
                    at = span(p)
                    total = own[place, at].astype(F32) + got1[place, at].astype(F32) + got2[place, at].astype(F32)
                    own[place, at] = total.astype(BF16)
                    hop_copy(place, up, p).start()

                count = count_to(place, side)
                if not line:
                    loop(count, body)
                    return

                @pl.when(has_before)
                def _():
                    loop(count, body_sum)

                @pl.when(jnp.logical_not(has_before))
                def _():
                    loop(count, body)

            if line:
                for k in range(across - 1):

                    @pl.when(k < mine)
                    def _(k=k):
                        begin(k)

                    @pl.when(k < across - 1 - mine)
                    def _(k=k):
                        begin(across - 1 - k)

                begin(mine)
                for k in range(across - 1):

                    @pl.when(k < mine)
                    def _(k=k):
                        forward(k, False, mine < across - 1)

                    @pl.when(k < across - 1 - mine)
                    def _(k=k):
                        forward(across - 1 - k, True, mine > 0)

            else:
                for k in range(1, across):
                    begin(lax.rem(mine + k, across))
                begin(mine)
                for k in range(1, across):
                    forward(lax.rem(mine + k, across), True, None)

            def settle(p):
                own_copy(mine, p).wait()
                first_copy(mine, p).wait_recv()
                at = span(p)
                acc[at] = own[mine, at].astype(F32) + got1[mine, at].astype(F32)

            def add(slot):
                def body(p):
                    arrived(slot, p).wait_recv()
                    at = span(p)
                    acc[at] += got2[slot, at].astype(F32)

                return body

            mine_count = count_to(mine, side)
            loop(mine_count, settle)
            if line:

                @pl.when(mine < across - 1)
                def _():
                    loop(mine_count, add(mine))

                @pl.when(mine > 0)
                def _():
                    loop(mine_count, add(across))

            else:
                for k in range(1, across):
                    loop(mine_count, add(k - 1))

            def out_copy(p):
                return pltpu.make_async_copy(acc.at[span(p)], out.at[span(p)], out_sem.at[p])

            loop(mine_count, lambda p: out_copy(p).start())
            loop(mine_count, lambda p: out_copy(p).wait())
            for place in range(across):
                loop(count_to(place, 1 - side), lambda p, place=place: first_copy(place, p).wait_send())

                @pl.when(place != mine)
                def _(place=place):
                    loop(count_to(place, side), lambda p: hop_copy(place, True, p).wait_send())

        def shape_of(dest):
            _, tile, count = slab(3, dest, share)
            return tile, slab_pieces(count, size)

        @pl.when(role == 3)
        def _():
            barrier = pltpu.get_barrier_semaphore()
            pl.semaphore_signal(barrier, inc=1, device_id={"dp": other}, device_id_type=MESH)
            for k in range(1, across):
                peer = at_place(lax.rem(mine + k, across))
                pl.semaphore_signal(barrier, inc=1, device_id=peer, device_id_type=MESH)
            pl.semaphore_wait(barrier, across)
            run(shape_of)

    sems = pltpu.SemaphoreType.DMA
    return pl.pallas_call(
        kernel,
        out_shape=jax.ShapeDtypeStruct((room, 16, LANE), F32),
        in_specs=[ANYWHERE],
        out_specs=ANYWHERE,
        scratch_shapes=[
            vmem((across, room, 16, LANE), BF16), vmem((across, room, 16, LANE), BF16),
            vmem((slots, room, 16, LANE), BF16), vmem((room, 16, LANE), F32),
            sems((across, pieces)), sems((across, pieces)), sems((across, pieces)),
            sems((across, pieces)), sems((slots, pieces)), sems((pieces,)),
        ],
        compiler_params=pltpu.CompilerParams(vmem_limit_bytes=62 << 20, collective_id=1, has_side_effects=True),
        name="gather_sum",
    )(tiles)


BLOCK_ROWS = (25, 11, 11)


def finish_call(lhs, dz, dpre, rights, conv, bias, loss, after, groups, share):
    n = lhs.shape[2]
    quads = groups // QUAD
    MESH = pl.DeviceIdType.MESH

    def most_blocks(role):
        width = FORM[role][1]
        lead = FORM[role][4]
        most = 0
        for dest in range(groups):
            count = slab(role, dest, share)[2]
            if lead and dest == 0:
                count -= lead
            most = max(most, -(-(count // width) // BLOCK_ROWS[role]))
        return most

    blocks = [most_blocks(role) for role in range(3)]
    room = max(
        FORM[role][4] + blocks[role] * BLOCK_ROWS[role] * FORM[role][1] for role in range(3)
    )
    left_rows = max(blocks[role] * BLOCK_ROWS[role] * 16 for role in range(3))
    most = max(blocks)

    def kernel(
        lhs, dz, dpre, late, early, conv, bias, loss, after, out, small_out,
        left, dpre_v, sent, got, acc, convs, lead_sum, small, got_small,
        sem_left, sem_right, send, recv, send_c, recv_c, small_send, small_recv, sem_out,
        shared, shared_send, shared_recv,
    ):
        role = lax.axis_index("section")
        me = lax.axis_index("dp")
        place, quad = lax.rem(me, QUAD), me // QUAD

        def across_peer(k):
            return {"dp": place + QUAD * lax.rem(quad + k, quads)}

        barrier = pltpu.get_barrier_semaphore()
        for k in range(1, QUAD):
            pl.semaphore_signal(barrier, inc=1, device_id={"dp": quad_peer(me, k)}, device_id_type=MESH)
        for k in range(1, quads):
            pl.semaphore_signal(barrier, inc=1, device_id=across_peer(k), device_id_type=MESH)

        for source in (0, 3):

            @pl.when(role != source)
            def _(source=source):
                pl.semaphore_signal(barrier, inc=1, device_id={"section": source}, device_id_type=MESH)

        def right_load(b):
            return pltpu.make_async_copy(
                dz.at[:, :, pl.ds(GW * b, GW)], dpre_v.at[:, b, :, pl.ds(0, GW)], sem_right.at[b]
            )

        def right_loads0():
            copies = []
            cut = SPLIT * CHUNK
            for b in range(4):
                cols = pl.ds(FW * b, FW)
                pairs = [
                    (early.at[:, :, cols], dpre_v.at[pl.ds(0, QUAD - 1), b, pl.ds(0, cut)]),
                    (late.at[:, :, cols], dpre_v.at[pl.ds(0, QUAD - 1), b, pl.ds(cut, n - cut)]),
                    (dpre.at[:, cols], dpre_v.at[QUAD - 1, b]),
                ]
                copies += [pltpu.make_async_copy(x, y, sem_right.at[4 + 3 * b + i]) for i, (x, y) in enumerate(pairs)]
            return copies

        def conv_load():
            return pltpu.make_async_copy(conv, convs.at[QUAD - 1], sem_right.at[16])

        @pl.when(role == 0)
        def _():
            for copy in right_loads0():
                copy.start()
            conv_load().start()

        @pl.when((role == 1) | (role == 2))
        def _():
            for b in range(4):
                right_load(b).start()

        ends = lax.max(1 - role, 0) + lax.max(role - 2, 0)
        pl.semaphore_wait(barrier, QUAD - 1 + quads - 1 + 3 * ends)

        small[...] = jnp.zeros_like(small)

        @pl.when(role == 0)
        def _():
            small[0, :, pl.ds(0, FW)] = bias[...]

        @pl.when(role == 3)
        def _():
            small[0, :, pl.ds(FW, LANE)] = loss[...]

        def small_copy(k):
            if k < QUAD:
                source, target = small.at[0], {"dp": quad_peer(me, k)}
            else:
                source, target = small.at[1], across_peer(k - QUAD + 1)
            return pltpu.make_async_remote_copy(
                source, got_small.at[k - 1], small_send.at[k - 1], small_recv.at[k - 1],
                device_id=target, device_id_type=MESH,
            )

        for k in range(1, QUAD):
            small_copy(k).start()

        def across_small():
            for k in range(1, QUAD):
                small_copy(k).wait_recv()
            small[1] = small[0] + got_small[0] + got_small[1] + got_small[2]
            for k in range(QUAD, QUAD + quads - 1):
                small_copy(k).start()

        def share_copy(slot, k):
            return pltpu.make_async_remote_copy(
                small.at[0], shared.at[slot], shared_send.at[slot, k - 1], shared_recv.at[slot],
                device_id={"section": lax.rem(role + k, 4)}, device_id_type=MESH,
            )

        def share_small():
            total = small[1]
            for k in range(QUAD, QUAD + quads - 1):
                small_copy(k).wait_recv()
                total = total + got_small[k - 1]
            for k in range(1, QUAD):
                small_copy(k).wait_send()
            small[0] = total
            for slot, source in enumerate((0, 3)):

                @pl.when(role == source)
                def _(slot=slot):
                    for k in range(1, 4):
                        share_copy(slot, k).start()

        def conv_copy(slot, target):
            return pltpu.make_async_remote_copy(
                conv, convs.at[slot], send_c.at[slot], recv_c.at[slot], device_id={"dp": target}, device_id_type=MESH
            )

        def run(which):
            width, pitch, rows, _, lead, _ = FORM[which]
            size = BLOCK_ROWS[which]
            block_tiles = size * pitch

            def geometry(k):
                dest = place + QUAD * lax.rem(quad + k, quads)
                first, _, count = slab(which, dest, share)
                if lead:
                    head = lax.max(1 - dest, 0)
                    count = count - lead * head
                else:
                    head = 0
                return first, (count // pitch + size - 1) // size, head

            def left_copy(k):
                height = blocks[which] * size * 16
                first = lax.min(geometry(k)[0], LEFT_ROOM - height)
                span = pl.ds(pl.multiple_of(first, 16), height)
                return pltpu.make_async_copy(
                    lhs.at[:, span], left.at[lax.rem(k, 2), :, pl.ds(0, blocks[which] * size * 16)], sem_left.at[lax.rem(k, 2)]
                )

            def block_copy(k, b):
                span = pl.ds(CONV_TILES + b * block_tiles, block_tiles)
                return pltpu.make_async_remote_copy(
                    sent.at[k - 1, span], got.at[k - 1, span], send.at[k - 1, b], recv.at[k - 1, b],
                    device_id=across_peer(k), device_id_type=MESH,
                )

            def lead_copy(k):
                span = pl.ds(0, CONV_TILES)
                return pltpu.make_async_remote_copy(
                    sent.at[k - 1, span], got.at[k - 1, span], send.at[k - 1, most], recv.at[k - 1, most],
                    device_id=across_peer(k), device_id_type=MESH,
                )

            def put(k, own, at, value):
                if own:
                    acc[at] = value
                else:
                    sent[k - 1, at] = value.astype(BF16)

            def block(k, own, b, first):
                here = pl.ds(pl.multiple_of(b * size * 16, 16), size * 16)
                base = CONV_TILES + b * block_tiles
                if which == 0:
                    row = lax.broadcasted_iota(jnp.int32, (size * 16, n), 0) + first + b * size * 16
                    start = first + b * size * 16
                    low = lax.min(start // (FILT + 1), 3)
                    high = lax.min((start + size * 16 - 1) // (FILT + 1), 3)
                    edge = (FILT + 1) * (low + 1)
                    lefts = [left[lax.rem(k, 2), g, here, :] for g in range(QUAD)]
                    near = [jnp.where(row < edge, x, jnp.zeros_like(x)) for x in lefts]
                    for col, wide in fblocks(FW):
                        value = jnp.zeros((size * 16, wide), F32)
                        for g in range(QUAD):
                            value = value + mm(near[g], dpre_v[g, low, :, pl.ds(col, wide)])
                        for r in range(size):
                            for c in range(wide // LANE):
                                tile = value[16 * r : 16 * r + 16, LANE * c : LANE * c + LANE]
                                put(k, own, base + r * pitch + col // LANE + c, tile)

                    @pl.when(high > low)
                    def _():
                        far = [jnp.where(row < edge, jnp.zeros_like(x), x) for x in lefts]
                        for col, wide in fblocks(FW):
                            value = jnp.zeros((size * 16, wide), F32)
                            for g in range(QUAD):
                                value = value + mm(far[g], dpre_v[g, high, :, pl.ds(col, wide)])
                            for r in range(size):
                                for c in range(wide // LANE):
                                    tile = value[16 * r : 16 * r + 16, LANE * c : LANE * c + LANE]
                                    at = base + r * pitch + col // LANE + c
                                    old = acc[at] if own else sent[k - 1, at].astype(F32)
                                    put(k, own, at, old + tile)

                else:
                    for col, wide in fblocks(ZW):
                        value = jnp.zeros((size * 16, wide), F32)
                        for g in range(QUAD):
                            value = value + mm(left[lax.rem(k, 2), g, here, :], dpre_v[g, col // GW, :, pl.ds(col % GW, wide)])
                        for r in range(size):
                            for c in range(wide // LANE):
                                tile = value[16 * r : 16 * r + 16, LANE * c : LANE * c + LANE]
                                put(k, own, base + r * pitch + col // LANE + c, tile)

            def loop(count, body):
                def step(b, carry):
                    body(b)
                    return carry

                lax.fori_loop(0, count, step, 0)

            left_copy(jnp.int32(1 % quads)).start()
            if which == 0:

                @pl.when(place > 0)
                def _():
                    for k in range(1, QUAD):

                        @pl.when(place == k)
                        def _(k=k):
                            conv_copy(k - 1, me - k).start()

                for copy in right_loads0():
                    copy.wait()
                conv_load().wait()
            else:
                for b in range(4):
                    right_load(b).wait()

            if which == 0:

                @pl.when(place == 0)
                def _():
                    for k in range(1, QUAD):
                        conv_copy(k - 1, me + k).wait_recv()
                    total = convs[0].astype(F32)
                    for k in range(1, QUAD):
                        total = total + convs[k].astype(F32)
                    lead_sum[...] = total

            def slab_of(k, own):
                left_copy(k).wait()
                if not own:
                    left_copy(lax.rem(k + 1, quads)).start()
                first, count, head = geometry(k)
                if which == 0:

                    @pl.when(head > 0)
                    def _():
                        if own:
                            acc[pl.ds(0, CONV_TILES)] = lead_sum[...]
                        else:
                            sent[k - 1, pl.ds(0, CONV_TILES)] = lead_sum[...].astype(BF16)
                            lead_copy(k).start()

                def work(b):
                    block(k, own, b, first)
                    if not own:
                        block_copy(k, b).start()

                loop(count, work)

            def others(body):
                def step(k, carry):
                    body(k)
                    return carry

                lax.fori_loop(1, quads, step, 0)

            others(lambda k: slab_of(k, False))
            across_small()
            slab_of(jnp.int32(0), True)
            share_small()

            _, mine, head = geometry(0)
            def join(k):
                def add(b):
                    block_copy(k, b).wait_recv()
                    span = pl.ds(CONV_TILES + b * block_tiles, block_tiles)
                    acc[span] += got[k - 1, span].astype(F32)

                loop(mine, add)
                if which == 0:

                    @pl.when(head > 0)
                    def _():
                        lead_copy(k).wait_recv()
                        span = pl.ds(0, CONV_TILES)
                        acc[span] += got[k - 1, span].astype(F32)

            others(join)

            span = blocks[which] * block_tiles
            if which == 0:

                @pl.when(head > 0)
                def _():
                    copy = pltpu.make_async_copy(
                        acc.at[pl.ds(0, CONV_TILES + span)], out.at[pl.ds(0, CONV_TILES + span)], sem_out.at[0]
                    )
                    copy.start()
                    copy.wait()

                @pl.when(head == 0)
                def _():
                    copy = pltpu.make_async_copy(acc.at[pl.ds(CONV_TILES, span)], out.at[pl.ds(0, span)], sem_out.at[0])
                    copy.start()
                    copy.wait()

            else:
                copy = pltpu.make_async_copy(acc.at[pl.ds(CONV_TILES, span)], out.at[pl.ds(0, span)], sem_out.at[0])
                copy.start()
                copy.wait()

            def sent_all(k):
                _, count, head = geometry(k)
                loop(count, lambda b: block_copy(k, b).wait_send())
                if which == 0:

                    @pl.when(head > 0)
                    def _():
                        lead_copy(k).wait_send()

            others(sent_all)

            if which == 0:
                for k in range(1, QUAD):

                    @pl.when(place == k)
                    def _(k=k):
                        conv_copy(k - 1, me - k).wait_send()

        for which in range(3):

            @pl.when(role == which)
            def _(which=which):
                run(which)

        @pl.when(role == 3)
        def _():
            across_small()
            share_small()

        result = jnp.zeros((1, FW + LANE), F32)
        for slot, source in enumerate((0, 3)):

            @pl.when(role == source)
            def _(slot=slot):
                shared[slot] = small[0]

            @pl.when(role != source)
            def _(slot=slot):
                share_copy(slot, 1).wait_recv()

            result = result + shared[slot]
        small_out[...] = result
        for slot, source in enumerate((0, 3)):

            @pl.when(role == source)
            def _(slot=slot):
                for k in range(1, 4):
                    share_copy(slot, k).wait_send()

        for k in range(QUAD, QUAD + quads - 1):
            small_copy(k).wait_send()

    sems = pltpu.SemaphoreType.DMA
    full = CONV_TILES + max(blocks[role] * BLOCK_ROWS[role] * FORM[role][1] for role in range(3))
    smalls = QUAD + quads - 2
    return pl.pallas_call(
        kernel,
        out_shape=[jax.ShapeDtypeStruct((full, 16, LANE), F32), jax.ShapeDtypeStruct((1, FW + LANE), F32)],
        in_specs=[ANYWHERE] * 6 + [ON_CHIP] * 2 + [ANYWHERE],
        out_specs=[ANYWHERE, ON_CHIP],
        scratch_shapes=[
            vmem((2, QUAD, left_rows, n), BF16), vmem((QUAD, 4, n, FW), BF16),
            vmem((quads - 1, full, 16, LANE), BF16), vmem((quads - 1, full, 16, LANE), BF16),
            vmem((full, 16, LANE), F32), vmem((QUAD, CONV_TILES, 16, LANE), BF16), vmem((CONV_TILES, 16, LANE), F32),
            vmem((2, 1, FW + LANE), F32), vmem((smalls, 1, FW + LANE), F32),
            sems((2,)), sems((17,)), sems((quads - 1, most + 1)), sems((quads - 1, most + 1)),
            sems((QUAD - 1,)), sems((QUAD - 1,)), sems((smalls,)), sems((smalls,)), sems((1,)),
            vmem((2, 1, FW + LANE), F32), sems((2, 3)), sems((2,)),
        ],
        compiler_params=pltpu.CompilerParams(vmem_limit_bytes=62 << 20, collective_id=5, has_side_effects=True),
        name="finish",
    )(lhs, dz, dpre, *rights, conv, bias, loss, after)


def pack_call(summed, summed3, groups, share):
    rooms = (summed.shape[0] * 16, summed3.shape[0] * 16)
    chunks = share // LANE
    margin = 1280
    slab_rows = 10624
    flat_rows = margin + max(10752, chunks + 1280)

    def kernel(summed, summed3, out, rows_v, spaced, flat, sem):
        role = lax.axis_index("section")
        me = lax.axis_index("dp")
        zero = jnp.zeros((64, LANE), F32)

        def clear(i, carry):
            flat[pl.ds(pl.multiple_of(i * 64, 64), 64), :] = zero
            return carry

        def fetch(source, room):
            return pltpu.make_async_copy(source, rows_v.at[pl.ds(0, room)], sem.at[0])

        @pl.when(role < 3)
        def _():
            fetch(summed, rooms[0]).start()

        @pl.when(role == 3)
        def _():
            fetch(summed3, rooms[1]).start()

        lax.fori_loop(0, flat_rows // 64, clear, 0)

        @pl.when(role < 3)
        def _():
            fetch(summed, rooms[0]).wait()

        @pl.when(role == 3)
        def _():
            fetch(summed3, rooms[1]).wait()

        lane = lanes()

        for which in range(4):
            width, pitch, rows, before, lead, period = FORM[which]
            if which == 0:
                blocks, cols, tiles = 1, FILT, 9
            elif which == 3:
                blocks, cols, tiles = 1, VOCAB, 79
            else:
                blocks, cols, tiles = 4, HID, 6
            stride = period * width // LANE
            most = max(slab(which, dest, share)[2] for dest in range(groups))
            groups8 = -(-(-(-most // pitch) * 16) // (8 * period))

            @pl.when(role == which)
            def _(which=which):
                first, _, count = slab(which, me, share)
                skip = lead * lax.max(1 - me, 0)
                step_rows = pitch * 49 + (pitch * 49 + 1) % 2

                def space(rt, carry):
                    for c in range(pitch):
                        for half in range(2):
                            at = pl.multiple_of((skip + rt * pitch + c) * 16 + 8 * half, 8)
                            spaced[pl.ds(rt * step_rows + 49 * c + 24 * half, 8, stride=3), :] = rows_v[pl.ds(at, 8), :]
                    return carry

                lax.fori_loop(0, (count - skip) // pitch, space, 0)
                base = margin + before // LANE + stride * (first // period) - chunks * me

                hop = period // 16 * step_rows
                half = period // 2

                def place(group, n, b):
                    number = first + period * (8 * group + sublanes()) + n
                    flat_at = before % LANE + width * n + cols * b
                    source = n // 16 * step_rows + 3 * lax.rem(n, 16) + 8 * group * hop + 49 * tiles * b
                    to = base + flat_at // LANE + stride * 8 * group
                    return number < rows, lax.rem(flat_at, LANE), source, to

                def run(places, low, high, lasts):
                    taken = [
                        [spaced[pl.ds(source + 49 * j, 8, stride=hop), :] for j in range(low, min(high, tiles))]
                        for _, _, source, _ in places
                    ]
                    edges = [j for j in range(low, high) if j == 0 or j >= tiles - 1]
                    old = [
                        {j: flat[pl.ds(to + j, 8, stride=stride), :] for j in edges} for _, _, _, to in places
                    ]
                    values, ends = [], []
                    for (keep, turn, _, _), pieces, olds, last in zip(places, taken, old, lasts):
                        turned = [last] + [pltpu.roll(jnp.where(keep, x, 0.0), turn, 1) for x in pieces]
                        for j in range(low, high):
                            here = turned[j - low + 1] if j < tiles else turned[-1]
                            value = here if j == tiles else jnp.where(lane >= turn, here, turned[j - low])
                            if j in olds:
                                at = lane + LANE * j - turn
                                value = jnp.where((at >= 0) & (at < cols), value, olds[j])
                            values.append(value)
                        ends.append(turned[-1])
                    at = 0
                    for _, _, _, to in places:
                        for j in range(low, high):
                            flat[pl.ds(to + j, 8, stride=stride), :] = values[at]
                            at += 1
                    return ends

                def row(i, carry):
                    group, n = i // half, lax.rem(i, half)
                    zero = jnp.zeros((8, LANE), F32)
                    if blocks == 4:
                        for b in range(2):
                            places = [place(group, m, c) for m in (n, n + half) for c in (b, b + 2)]
                            run(places, 0, tiles + 1, [zero] * 4)
                    else:
                        places = [place(group, m, 0) for m in (n, n + half)]
                        ends = [zero] * 2
                        for low in range(0, tiles + 1, 20):
                            ends = run(places, low, min(low + 20, tiles + 1), ends)
                    return carry

                @pl.when(count > 0)
                def _():
                    lax.fori_loop(0, half * groups8, row, 0)

        @pl.when((role == 0) & (me == 0))
        def _():
            lane1 = lanes(1)

            def piece(row_at, flat_at, low, size):
                edge = flat_at - low
                turn = edge % LANE
                to = margin + (edge - turn) // LANE
                first, end = low // LANE, (low + size - 1) // LANE
                last = jnp.zeros((1, LANE), F32)
                for j in range(first, end + 2):
                    least, most = max(low + turn - LANE * j, 0), min(low + size + turn - LANE * j, LANE)
                    here = last
                    if j <= end:
                        here = rows_v[row_at + 16 * j : row_at + 16 * j + 1, :]
                        here = pltpu.roll(here, turn, 1) if turn else here
                    if most > least:
                        value = jnp.where(lane1 >= turn, here, last) if turn else here
                        at = to + j
                        if least > 0 or most < LANE:
                            value = jnp.where((lane1 >= least) & (lane1 < most), value, flat[at : at + 1, :])
                        flat[at : at + 1, :] = value
                    last = here

            for k in range(1, 8):
                n = NFILT[k - 1]
                for i in range(k * D_CHAR + 1):
                    number = i + i // D_CHAR if i < k * D_CHAR else 15
                    piece(number // 16 * 144 + number % 16, KOFF[k - 1] + n * i, COLS[k - 1], n)
            for a in range(CHAR_V):
                piece(72 * 16 + a, D_CHAR * a, 0, D_CHAR)

        copy = pltpu.make_async_copy(flat.at[pl.ds(margin, chunks)], out, sem.at[0])
        copy.start()
        copy.wait()

    return pl.pallas_call(
        kernel,
        out_shape=jax.ShapeDtypeStruct((chunks, LANE), F32),
        in_specs=[ANYWHERE] * 2,
        out_specs=ANYWHERE,
        scratch_shapes=[
            vmem((slab_rows, LANE), F32), vmem((31104, LANE), F32), vmem((flat_rows, LANE), F32), dmas(1),
        ],
        compiler_params=pltpu.CompilerParams(vmem_limit_bytes=LIMIT),
        name="pack",
    )(summed.reshape(rooms[0], LANE), summed3.reshape(rooms[1], LANE))


def shards(char_ids, target_ids, remaining, resets, start_state, section_params):
    rows, steps = char_ids.shape[:2]
    groups = lax.axis_size("dp")
    packed = section_params.shape[1]
    share = packed // groups
    n = rows * (steps + 1)

    ids = jnp.pad(
        char_ids.transpose(1, 0, 2), ((0, 1), (0, 0), (0, LANE - WORD_CHARS)), constant_values=-1
    ).reshape(n, LANE)
    km, e8, ab, ur, rt, wt = unpack_all(section_params)
    y2, *char_saved = char_forward_call(ids, km, e8, ab)
    feats, pres, total, emb = char_saved
    grad, dpre, late, xb, lhs, dz, dl, _, _, loss, bias = recurrent_call(
        y2, feats, pres, ab, ur, rt, wt, resets, target_ids, remaining.reshape(rows, 1), start_state
    )
    tiles3 = output_weights_call(xb, dl)
    summed3 = gather_sum_call(tiles3, groups, share)
    conv, early = char_backward_call(ids, grad, km, (total, emb), dpre)
    summed, small = finish_call(lhs, dz, dpre, (late, early), conv, bias, loss, summed3, groups, share)
    flat = pack_call(summed, summed3, groups, share)
    mean_loss = small[0, FW] / (groups * rows * steps)
    return mean_loss, flat.reshape(1, share), small[0, :FILT]


def solution(mesh):
    in_specs = (
        P("dp", None, None),
        P("dp", None),
        P("dp"),
        P("dp", None),
        P(None, None, "dp", None),
        P("section", None),
    )
    out_specs = (P(), P("section", "dp"), P())
    return jax.shard_map(shards, mesh=mesh, in_specs=in_specs, out_specs=out_specs, check_vma=False)
```

```python
import functools
import math

import jax
import jax.numpy as jnp
from jax import lax
from jax.experimental import pallas as pl
from jax.experimental.pallas import tpu as pltpu
from jax.sharding import PartitionSpec as P

D_CHAR = 15
CHAR_V = 51
F_UNIT = 50
WORD_CHARS = 21
HID = 650
VOCAB = 10000
FILT = 1100
F32 = jnp.float32
BF16 = jnp.bfloat16

NFILT = [F_UNIT * min(k, 4) for k in range(1, 8)]
COLS = [sum(NFILT[:k]) for k in range(8)]
KOFF = [CHAR_V * D_CHAR + sum((j * D_CHAR + 1) * NFILT[j - 1] for j in range(1, k)) for k in range(1, 9)]
CONV_END = KOFF[7]
HIGH_STRIDE = FILT * (FILT + 1)
FW = 1152
GW = 768
ZW = 4 * GW
VW = 10112
LANE = 128
LENS = (2304, 2688, 2688, 5120)


def roll_lanes(x, shift):
    return pltpu.roll(x, shift, 1)


def lanes(rows=8):
    return lax.broadcasted_iota(jnp.int32, (rows, LANE), 1)


def sublanes():
    return lax.broadcasted_iota(jnp.int32, (8, LANE), 0)


def widen(raw, slot, rows, wide):
    def body(i, carry):
        piece = raw[slot, 0:1, pl.ds(pl.multiple_of(i * 16384, 16384), 16384)]
        wide[pl.ds(pl.multiple_of(i * 128, 128), 128), :] = piece.astype(F32).reshape(128, LANE)
        return carry

    lax.fori_loop(0, rows // 128, body, 0)


DEPTH = 4


def stream_start(count, length, total, chunk_of, src, raw, sem):
    for i in range(DEPTH - 1):
        stream_copy(jnp.int32(i), length, total, chunk_of, src, raw, sem).start()


def stream_at(i, length, total, chunk_of):
    return jnp.minimum(chunk_of(i) // 8 * 8, total - length)


def stream_copy(i, length, total, chunk_of, src, raw, sem):
    at = pl.multiple_of(stream_at(i, length, total, chunk_of) * LANE, 8 * LANE)
    slot = lax.rem(i, DEPTH)
    return pltpu.make_async_copy(
        src.at[:, pl.ds(at, length * LANE)], raw.at[slot, :, pl.ds(0, length * LANE)], sem.at[slot]
    )


def stream_blocks(count, length, total, chunk_of, src, raw, sem, wide, work):
    def body(i, carry):
        @pl.when(i + DEPTH - 1 < count)
        def _():
            stream_copy(i + DEPTH - 1, length, total, chunk_of, src, raw, sem).start()

        stream_copy(i, length, total, chunk_of, src, raw, sem).wait()
        widen(raw, lax.rem(i, DEPTH), length, wide)
        work(i, chunk_of(i) - stream_at(i, length, total, chunk_of))
        return carry

    lax.fori_loop(0, count, body, 0)


def take_rows(wide, starts, tiles, cols, stride, put):
    step = max(6, 40 // len(starts))
    lane = lanes()
    for low in range(0, tiles, step):
        high = min(tiles, low + step)
        loaded = [
            [wide[pl.ds(first + c, 8, stride=stride), :] for c in range(low, high + 1)] for _, first, _, _ in starts
        ]
        results = []
        for (_, _, shift, keep_row), pieces in zip(starts, loaded):
            turn = lax.rem(LANE - shift, LANE)
            split = lane < LANE - shift
            turned = [roll_lanes(piece, turn) for piece in pieces]
            for c in range(low, high):
                out = jnp.where(split, turned[c - low], turned[c - low + 1])
                keep = keep_row
                if cols - c * LANE < LANE:
                    keep = keep & (lane < cols - c * LANE)
                results.append(jnp.where(keep, out, 0.0))
        at = 0
        for tag, _, _, _ in starts:
            for c in range(low, high):
                put(tag, c, results[at])
                at += 1


def spread(c, n, period):
    return pl.ds((c * period + n) * 25, 8, stride=3)


def collect(dest, c, period):
    return [
        dest[pl.ds((c * period + 8 * m) * 25 + 3 * j, 8, stride=25), :] for j in range(8) for m in range(period // 8)
    ]


def stage_tile(stage, slot, c, blocks):
    for i in range(0, len(blocks), 2):
        pair = jnp.concatenate([blocks[i], blocks[i + 1]], axis=0).astype(BF16)
        stage[slot, pl.ds(8 * i, 16), pl.ds(c * LANE, LANE)] = pair


def unpack_kernel(
    src, km, e8, ab, ur, rt, wt, raw, wide, dest, kstage, stage0, stage1, stage_t, stage3, raw_conv, sem_in, sem_out, sem_t
):
    role = lax.axis_index("section")
    total = src.shape[1] // LANE

    def out_copy(stage, slot, target):
        return pltpu.make_async_copy(stage.at[slot], target, sem_out.at[slot])

    @pl.when(role == 0)
    def _():
        blocks = 5
        count = 4 * blocks

        def flat_of(i):
            return CONV_END + HIGH_STRIDE * (i // blocks)

        def chunk_of(i):
            return flat_of(i) // LANE + 2200 * lax.rem(i, blocks)

        length = 640
        copy = pltpu.make_async_copy(src.at[:, pl.ds(0, length * LANE)], raw_conv.at[0], sem_t.at[0])
        copy.start()
        stream_start(count, LENS[0], total, chunk_of, src, raw, sem_in)
        copy.wait()
        widen(raw_conv, 0, length, wide)
        lane1 = lanes(1)
        dest[pl.ds(0, 64), :] = jnp.zeros((64, LANE), F32)
        for a in range(CHAR_V):
            flat = D_CHAR * a
            q, s = flat // LANE, flat % LANE
            here = wide[q : q + 1, :]
            out = roll_lanes(here, (LANE - s) % LANE) if s else here
            if s + D_CHAR > LANE:
                out = jnp.where(lane1 < LANE - s, out, roll_lanes(wide[q + 1 : q + 2, :], LANE - s))
            dest[a : a + 1, :] = jnp.where(lane1 < D_CHAR, out, jnp.where(lane1 == D_CHAR, 1.0, 0.0))
        table = dest[pl.ds(0, 64), :]
        for m in range(8):
            kstage[pl.ds(64 * m, 64), pl.ds(0, LANE)] = (
                pltpu.roll(table, 16 * m, 1) if m else table
            ).astype(BF16)
        copy = pltpu.make_async_copy(kstage.at[pl.ds(0, 512), pl.ds(0, LANE)], e8, sem_out.at[0])
        copy.start()
        copy.wait()
        tiles = FW // LANE
        rows = 112
        dest[pl.ds(0, rows * tiles), :] = jnp.zeros((rows * tiles, LANE), F32)

        def kernel_row(k, i, row):
            n, base = NFILT[k - 1], COLS[k - 1]
            edge = KOFF[k - 1] + n * i - base
            q, s = edge // LANE, edge % LANE
            for ct in range(base // LANE, (base + n - 1) // LANE + 1):
                out = wide[q + ct : q + ct + 1, :]
                if s:
                    after = roll_lanes(wide[q + ct + 1 : q + ct + 2, :], LANE - s)
                    out = jnp.where(lane1 < LANE - s, roll_lanes(out, LANE - s), after)
                at = ct * rows + row
                low, high = max(base - ct * LANE, 0), min(base + n - ct * LANE, LANE)
                if low > 0 or high < LANE:
                    out = jnp.where((lane1 >= low) & (lane1 < high), out, dest[at : at + 1, :])
                dest[at : at + 1, :] = out

        for k in range(1, 8):
            for i in range(k * D_CHAR):
                kernel_row(k, i, i + i // D_CHAR)
            kernel_row(k, k * D_CHAR, 15)
        kstage[...] = jnp.zeros_like(kstage)
        for ct in range(tiles):
            kstage[pl.ds(112, rows), pl.ds(ct * LANE, LANE)] = dest[pl.ds(ct * rows, rows), :].astype(BF16)
        copy = pltpu.make_async_copy(kstage.at[pl.ds(0, 368)], km, sem_out.at[0])
        copy.start()
        copy.wait()

        def target(i):
            return ab.at[i // blocks, pl.ds(pl.multiple_of(lax.rem(i, blocks) * 256, 256), 256)]

        def work(i, extra):
            block = lax.rem(i, blocks)
            inner = lax.rem(flat_of(i), LANE)

            def rows_of(i, carry):
                starts = []
                for n in range(4):
                    n = 4 * i + n
                    flat = inner + FILT * n
                    keep = 32 * (8 * block + sublanes()) + n <= FILT
                    starts.append((n, flat // LANE + extra, lax.rem(flat, LANE), keep))

                def put(n, c, value):
                    dest[spread(c, n, 32), :] = value

                take_rows(wide, starts, tiles, FILT, 275, put)
                return carry

            lax.fori_loop(0, 8, rows_of, 0)
            slot = lax.rem(i, 2)

            @pl.when(i >= 2)
            def _():
                out_copy(stage0, slot, target(i - 2)).wait()

            for c in range(tiles):
                stage_tile(stage0, slot, c, collect(dest, c, 32))
            out_copy(stage0, slot, target(i)).start()

        stream_blocks(count, LENS[0], total, chunk_of, src, raw, sem_in, wide, work)
        for i in (count - 2, count - 1):
            out_copy(stage0, i % 2, target(i)).wait()

    for layer in (1, 2):

        @pl.when(role == layer)
        def _(layer=layer):
            depth = FILT if layer == 1 else HID
            blocks = -(-depth // 128)
            recurrent = depth * 4 * HID
            count = blocks + 6

            def chunk_of(i):
                return jnp.where(i < blocks, 2600 * i, recurrent // LANE + 2600 * (i - blocks))

            stream_start(count, LENS[1], total, chunk_of, src, raw, sem_in)

            def target(i):
                at = jnp.where(i < blocks, i, i - blocks + 9)
                return ur.at[pl.ds(pl.multiple_of(at * 128, 128), 128)]

            def work(i, extra):
                inner = jnp.where(i < blocks, 0, recurrent % LANE)
                block = jnp.where(i < blocks, i, i - blocks)
                limit = jnp.where(i < blocks, depth, HID + 1)

                def rows_of(i, carry):
                    starts = []
                    for n in (2 * i, 2 * i + 1):
                        keep = 16 * (8 * block + sublanes()) + n < limit
                        for b in range(4):
                            flat = inner + 4 * HID * n + HID * b
                            starts.append(((n, b), flat // LANE + extra, lax.rem(flat, LANE), keep))

                    def put(tag, c, value):
                        dest[spread(6 * tag[1] + c, tag[0], 16), :] = value

                    take_rows(wide, starts, 6, HID, 325, put)
                    return carry

                lax.fori_loop(0, 8, rows_of, 0)
                slot = lax.rem(i, 2)

                @pl.when(i >= 2)
                def _():
                    out_copy(stage1, slot, target(i - 2)).wait()

                for c in range(24):
                    stage_tile(stage1, slot, c, collect(dest, c, 16))
                out_copy(stage1, slot, target(i)).start()

                @pl.when(i >= blocks)
                def _():
                    @pl.when(i >= blocks + 2)
                    def _():
                        turned_copy(i - 2).wait()

                    k = LANE * block + lanes(LANE)
                    for c in range(24):
                        turned = jnp.transpose(jnp.concatenate(collect(dest, c, 16), axis=0))
                        stage_t[slot, pl.ds(128 * c, 128), :] = jnp.where(k < HID, turned, 0.0).astype(BF16)
                    turned_copy(i).start()

            def turned_copy(i):
                slot = lax.rem(i, 2)
                at = pl.multiple_of((i - blocks) * LANE, LANE)
                return pltpu.make_async_copy(stage_t.at[slot], rt.at[:, pl.ds(at, LANE)], sem_t.at[slot])

            stream_blocks(count, LENS[1], total, chunk_of, src, raw, sem_in, wide, work)
            for i in (count - 2, count - 1):
                out_copy(stage1, i % 2, target(jnp.int32(i))).wait()
                turned_copy(jnp.int32(i)).wait()

    @pl.when(role == 3)
    def _():
        count = 11
        tiles = VW // LANE

        def chunk_of(i):
            return 5000 * i

        stream_start(count, LENS[3], total, chunk_of, src, raw, sem_in)

        def target(i):
            return wt.at[pl.ds(pl.multiple_of(i * 64, 64), 64)]

        def work(i, extra):
            def rows_of(n, carry):
                flat = VOCAB * n
                keep = 8 * (8 * i + sublanes()) + n < HID + 1

                def put(n, c, value):
                    dest[spread(c, n, 8), :] = value

                take_rows(wide, [(n, flat // LANE + extra, lax.rem(flat, LANE), keep)], tiles, VOCAB, 625, put)
                return carry

            lax.fori_loop(0, 8, rows_of, 0)
            slot = lax.rem(i, 2)

            @pl.when(i >= 2)
            def _():
                out_copy(stage3, slot, target(i - 2)).wait()

            for c in range(tiles):
                stage_tile(stage3, slot, c, collect(dest, c, 8))
            out_copy(stage3, slot, target(i)).start()

        stream_blocks(count, LENS[3], total, chunk_of, src, raw, sem_in, wide, work)
        for i in (count - 2, count - 1):
            out_copy(stage3, i % 2, target(jnp.int32(i))).wait()


def unpack_all(section_params):
    anywhere = pl.BlockSpec(memory_space=pl.ANY)
    return pl.pallas_call(
        unpack_kernel,
        out_shape=[
            jax.ShapeDtypeStruct((368, FW), BF16),
            jax.ShapeDtypeStruct((512, LANE), BF16),
            jax.ShapeDtypeStruct((4, 1280, FW), BF16),
            jax.ShapeDtypeStruct((15 * 128, ZW), BF16),
            jax.ShapeDtypeStruct((ZW, GW), BF16),
            jax.ShapeDtypeStruct((11 * 64, VW), BF16),
        ],
        in_specs=[anywhere],
        out_specs=[anywhere] * 6,
        scratch_shapes=[
            pltpu.VMEM((DEPTH, 1, LENS[3] * LANE), BF16),
            pltpu.VMEM((9312, LANE), F32),
            pltpu.VMEM((79 * 200, LANE), F32),
            pltpu.VMEM((512, FW), BF16),
            pltpu.VMEM((2, 256, FW), BF16),
            pltpu.VMEM((2, 128, ZW), BF16),
            pltpu.VMEM((2, ZW, LANE), BF16),
            pltpu.VMEM((2, 64, VW), BF16),
            pltpu.VMEM((1, 1, 640 * LANE), BF16),
            pltpu.SemaphoreType.DMA((DEPTH,)),
            pltpu.SemaphoreType.DMA((2,)),
            pltpu.SemaphoreType.DMA((2,)),
        ],
        compiler_params=pltpu.CompilerParams(vmem_limit_bytes=56 << 20),
        name="unpack",
    )(section_params)


def fblocks(width, step=256):
    return [(at, min(step, width - at)) for at in range(0, width, step)]


def mm(a, b):
    return jnp.dot(a, b, preferred_element_type=F32)


def mm_tn(a, b):
    return lax.dot_general(a, b, (((0,), (0,)), ((), ())), preferred_element_type=F32)


def mm_nt(a, b):
    return lax.dot_general(a, b, (((1,), (1,)), ((), ())), preferred_element_type=F32)


def sigmoid(x):
    return 0.5 * jnp.tanh(0.5 * x) + 0.5


def load(pairs, sem):
    copies = [pltpu.make_async_copy(a, b, sem.at[i]) for i, (a, b) in enumerate(pairs)]
    for copy in copies:
        copy.start()
    for copy in copies:
        copy.wait()


def column_mask(at, width, limit, rows):
    return lax.broadcasted_iota(jnp.int32, (rows, width), 1) + at < limit


def char_onehot(ids, t):
    rows = ids.shape[0]
    lane = lanes(rows)
    pieces = []
    for pair in range(4):
        j = 8 * t + 2 * pair
        left = ids[:, j : j + 1]
        right = ids[:, j + 1 : j + 2]
        hit = jnp.where(lane < 64, left, right) == lax.rem(lane, 64)
        pieces.append(jnp.where(hit, 1.0, 0.0).astype(BF16))
    return jnp.concatenate(pieces, axis=1)


def conv_steps(body):
    def step(p, carry):
        body(p, p // 8, True, lax.rem(p, 8), FILT)
        return carry

    lax.fori_loop(0, 15, step, 0)
    body(15, 1, True, 7, COLS[6])
    for p in range(16, WORD_CHARS):
        body(p, 2, False, p - 16, COLS[WORD_CHARS - p])


def conv_at(emb, km, tile, second, within, at, width):
    first = 112 - 16 * within
    if not isinstance(first, int):
        first = pl.multiple_of(first, 16)
    if second:
        window = jnp.concatenate([emb[tile], emb[tile + 1]], axis=1)
    else:
        window = emb[tile]
    return mm(window, km[pl.ds(first, window.shape[1]), pl.ds(at, width)])


def char_forward(ids, e8, km, ab, emb, total, feats, pres, out):
    rows = ids.shape[0]
    for t in range(3):
        emb[t] = mm(char_onehot(ids, t), e8[...]).astype(BF16)
    total[...] = jnp.zeros_like(total)

    def step(p, tile, second, within, limit):
        for at, width in fblocks(FW):
            if at >= limit:
                continue
            value = jnp.exp(jnp.tanh(conv_at(emb, km, tile, second, within, at, width)))
            if at + width > limit and limit < FILT:
                value = jnp.where(column_mask(at, width, limit, rows), value, 0.0)
            total[:, pl.ds(at, width)] += value

    conv_steps(step)
    for at, width in fblocks(FW):
        col = lax.broadcasted_iota(jnp.int32, (rows, width), 1) + at
        count = jnp.full((rows, width), float(WORD_CHARS), F32)
        for k in range(1, 7):
            count = jnp.where(col >= COLS[k], float(WORD_CHARS - k), count)
        value = jnp.log(total[:, pl.ds(at, width)]) - jnp.log(count)
        value = jnp.where(col < FILT, value, jnp.where(col == FILT, 1.0, 0.0))
        feats[0, :, pl.ds(at, width)] = value.astype(BF16)
    for layer in range(2):
        for at, width in fblocks(FW):
            cols = pl.ds(at, width)
            t_pre = mm(feats[layer], ab[2 * layer, pl.ds(0, FW), cols])
            h_pre = mm(feats[layer], ab[2 * layer + 1, pl.ds(0, FW), cols])
            pres[2 * layer, :, cols] = t_pre
            pres[2 * layer + 1, :, cols] = h_pre
            gate = sigmoid(t_pre)
            y = feats[layer, :, cols].astype(F32)
            value = gate * (h_pre * sigmoid(h_pre)) + (1.0 - gate) * y
            col = lax.broadcasted_iota(jnp.int32, (rows, width), 1) + at
            if layer == 0:
                value = jnp.where(col < FILT, value, jnp.where(col == FILT, 1.0, 0.0))
                feats[1, :, cols] = value.astype(BF16)
            else:
                out[:, cols] = jnp.where(col < FILT, value, 0.0).astype(BF16)


def conv_backward(km, kt, emb, emb_t, total, grad, dk, demb, relay):
    rows = grad.shape[0]
    kt[...] = jnp.transpose(km[pl.ds(112, LANE), :])
    for t in range(3):
        emb_t[pl.ds(LANE * t, LANE), :] = jnp.transpose(emb[t])
    emb_t[pl.ds(3 * LANE, LANE), :] = jnp.zeros((LANE, rows), BF16)
    dk[...] = jnp.zeros_like(dk)
    demb[...] = jnp.zeros_like(demb)
    for at, width in fblocks(FW):
        cols = pl.ds(at, width)
        grad[:, cols] = grad[:, cols] / total[:, cols]

    def step(p, tile, second, within, limit):
        relay(p)
        window_t = emb_t[pl.ds(p * 16 if isinstance(p, int) else pl.multiple_of(p * 16, 16), LANE), :]
        back = jnp.zeros((rows, LANE), F32)
        for at, width in fblocks(FW):
            if at >= limit:
                continue
            cols = pl.ds(at, width)
            act = jnp.tanh(conv_at(emb, km, tile, second, within, at, width))
            dz = grad[:, cols] * jnp.exp(act) * (1.0 - act * act)
            if at + width > limit and limit < FILT:
                dz = jnp.where(column_mask(at, width, limit, rows), dz, 0.0)
            dz = dz.astype(BF16)
            dk[:, cols] += mm(window_t, dz)
            back = back + mm(dz, kt[cols, :])
        lane = lanes(rows)
        back = jnp.where(lane < 112, back, 0.0)
        turned = pltpu.roll(back, 16 * within, 1)
        demb[tile] += jnp.where(lane >= 16 * within, turned, 0.0)
        if second:
            demb[tile + 1] += jnp.where(lane < 16 * within, turned, 0.0)

    conv_steps(step)


def table_backward(ids, demb, table):
    acc = jnp.zeros((64, LANE), F32)
    for t in range(3):
        hot = char_onehot(ids, t)
        value = demb[t]
        high = value.astype(BF16)
        low = (value - high.astype(F32)).astype(BF16)
        grads = mm_tn(hot, high) + mm_tn(hot, low)
        for m in range(8):
            block = grads[64 * m : 64 * m + 64, :]
            acc = acc + (pltpu.roll(block, LANE - 16 * m, 1) if m else block)
    table[...] = acc


def tile_rows(stage, base, value, row_tiles, col_tiles, first_col=0, pitch=None):
    pitch = col_tiles if pitch is None else pitch
    for r in range(row_tiles):
        for c in range(col_tiles):
            stage[base + r * pitch + first_col + c] = value[16 * r : 16 * r + 16, LANE * c : LANE * c + LANE].astype(BF16)


def six(x):
    return jnp.concatenate([x] * 6, axis=1)


ANYWHERE = pl.BlockSpec(memory_space=pl.ANY)
ON_CHIP = pl.BlockSpec(memory_space=pltpu.VMEM)
LIMIT = 56 << 20


def call(kernel, name, ins, specs, outs, scratch, aliases=None):
    return pl.pallas_call(
        kernel,
        out_shape=[jax.ShapeDtypeStruct(shape, dtype) for shape, dtype in outs],
        in_specs=specs,
        out_specs=[ANYWHERE] * len(outs),
        scratch_shapes=scratch,
        input_output_aliases=aliases or {},
        compiler_params=pltpu.CompilerParams(vmem_limit_bytes=LIMIT),
        name=name,
    )(*ins)


def vmem(shape, dtype):
    return pltpu.VMEM(shape, dtype)


def dmas(count):
    return pltpu.SemaphoreType.DMA((count,))


def char_forward_call(ids, km, e8, ab):
    n = ids.shape[0]

    def kernel(ids, km, e8, ab, y2_o, feats_o, pres_o, total_o, emb_o, km_v, e8_v, ab_v, y2, feats, pres, total, emb, sem):
        @pl.when(lax.axis_index("section") == 0)
        def _():
            load([(km, km_v), (e8, e8_v), (ab, ab_v)], sem)
            char_forward(ids, e8_v, km_v, ab_v, emb, total, feats, pres, y2)
            load([(y2, y2_o), (feats, feats_o), (pres, pres_o), (total, total_o), (emb, emb_o)], sem)

    outs = [
        ((n, FW), BF16),
        ((2, n, FW), BF16),
        ((4, n, FW), F32),
        ((n, FW), F32),
        ((3, n, LANE), BF16),
    ]
    scratch = [vmem(km.shape, BF16), vmem(e8.shape, BF16), vmem(ab.shape, BF16)]
    scratch += [vmem(shape, dtype) for shape, dtype in outs] + [dmas(5)]
    return call(kernel, "char_forward", (ids, km, e8, ab), [ON_CHIP] + [ANYWHERE] * 3, outs, scratch)


def char_backward_call(ids, grad, km, saved, dpre):
    n = ids.shape[0]
    total, emb = saved
    rows = SPLIT * CHUNK
    sems = pltpu.SemaphoreType.DMA

    def kernel(
        ids, grad, km, total, emb, dpre, tiles_o, right_o,
        grad_v, km_v, total_v, emb_v, kt, emb_t, dk, demb, table, stage, sem, send, recv,
    ):
        me = lax.axis_index("dp")

        def right_copy(k, i):
            span = pl.ds(pl.multiple_of(i * CHUNK, CHUNK), CHUNK)
            source = right_o.at[1, span] if k == 3 else dpre.at[span]
            return pltpu.make_async_remote_copy(
                source, right_o.at[k - 1, span], send.at[k - 1, i], recv.at[k - 1, i],
                device_id={"dp": quad_peer(me, 1 if k == 3 else k)}, device_id_type=pl.DeviceIdType.MESH,
            )

        def relay(p):
            if isinstance(p, int):
                return
            i = p // 3 - 1

            @pl.when((lax.rem(p, 3) == 0) & (p > 0) & (i < SPLIT))
            def _():
                right_copy(2, i).wait_recv()
                right_copy(3, i).start()

        @pl.when(lax.axis_index("section") == 0)
        def _():
            barrier = pltpu.get_barrier_semaphore()
            for k in range(1, QUAD):
                pl.semaphore_signal(
                    barrier, inc=1, device_id={"dp": quad_peer(me, k)}, device_id_type=pl.DeviceIdType.MESH
                )
            pl.semaphore_wait(barrier, QUAD - 1)
            for i in range(SPLIT):
                right_copy(2, i).start()
                right_copy(1, i).start()
            load([(grad, grad_v), (km, km_v), (total, total_v), (emb, emb_v)], sem)
            conv_backward(km_v, kt, emb_v, emb_t, total_v, grad_v, dk, demb, relay)
            table_backward(ids, demb, table)
            tile_rows(stage, 0, dk[...], 8, 9)
            tile_rows(stage, 72, table[...], 4, 1)
            load([(stage, tiles_o)], sem)
            for i in range(SPLIT):
                for k in range(1, QUAD):
                    right_copy(k, i).wait_send()
                    if k != 2:
                        right_copy(k, i).wait_recv()

    outs = [((CONV_TILES, 16, LANE), BF16), ((QUAD - 1, rows, 4 * FW), BF16)]
    scratch = [
        vmem((n, FW), F32), vmem(km.shape, BF16), vmem(total.shape, F32), vmem(emb.shape, BF16),
        vmem((FW, LANE), BF16), vmem((4 * LANE, n), BF16), vmem((LANE, FW), F32), vmem((3, n, LANE), F32),
        vmem((64, LANE), F32), vmem((CONV_TILES, 16, LANE), BF16), dmas(4), sems((QUAD - 1, SPLIT)), sems((QUAD - 1, SPLIT)),
    ]
    return pl.pallas_call(
        kernel,
        out_shape=[jax.ShapeDtypeStruct(shape, dtype) for shape, dtype in outs],
        in_specs=[ON_CHIP] + [ANYWHERE] * 5,
        out_specs=[ANYWHERE] * 2,
        scratch_shapes=scratch,
        compiler_params=pltpu.CompilerParams(vmem_limit_bytes=LIMIT, collective_id=4, has_side_effects=True),
        name="char_backward",
    )(ids, grad, km, total, emb, dpre)


CONV_TILES = 76
TILES = 3648


def turned_tile(left, right, shift):
    rows = right.shape[0]
    if shift:
        mixed = jnp.where(
            lanes(rows) < shift, pltpu.roll(left.astype(F32), shift, 1), pltpu.roll(right.astype(F32), shift, 1)
        )
        right = mixed.astype(BF16)
    return jnp.transpose(right)


def each_vocab(body, step=2048):
    whole = VW // step

    def one(i, carry):
        body(pl.multiple_of(i * step, step), step)
        return carry

    lax.fori_loop(0, whole, one, 0)
    body(whole * step, VW - whole * step)


def output_weights_call(h, dl):
    n = h.shape[0]
    rows = 704
    pitch = VW // LANE

    def kernel(h, dl, tiles_o, h_v, dl_v, h_t, stage, sem):
        @pl.when(lax.axis_index("section") == 3)
        def _():
            load([(h, h_v), (dl, dl_v)], sem)
            lane = lanes(n)
            for c in range(6):
                value = h_v[:, pl.ds(LANE * c, LANE)].astype(F32)
                value = jnp.where(lane + c * LANE == HID, 1.0, value).astype(BF16)
                h_t[pl.ds(LANE * c, LANE), :] = jnp.transpose(value)

            def body(at, width):
                first = at // LANE
                for top, count in fblocks(rows):
                    value = mm(h_t[pl.ds(top, count), :], dl_v[:, pl.ds(at, width)])
                    for r in range(count // 16):
                        for c in range(width // LANE):
                            stage[(top // 16 + r) * pitch + first + c] = value[
                                16 * r : 16 * r + 16, LANE * c : LANE * c + LANE
                            ].astype(BF16)

            each_vocab(body, 256)
            count = rows // 16 * pitch
            load([(stage.at[pl.ds(0, count)], tiles_o.at[pl.ds(0, count)])], sem)

    scratch = [
        vmem((n, GW), BF16), vmem((n, VW), BF16), vmem((6 * LANE, n), BF16),
        vmem((rows // 16 * pitch, 16, LANE), BF16), dmas(2),
    ]
    return call(
        kernel, "output_weights", (h, dl), [ANYWHERE] * 2, [((TILES, 16, LANE), BF16)], scratch
    )[0]


CHUNK = 32
GROUPS_OUT = (3, 3, 2, 1)


def lstm_steps(first, count, keep, carry, r, gates, cells, prevs, hiddens):
    def step(s, carry):
        h, c = carry
        at = pl.ds(pl.multiple_of((first + s) * 8, 8), 8)
        k = six(keep[at, :])
        hp = h * k
        cp = c * k
        prevs[at, :] = hp
        z = gates[at, :] + mm(hp.astype(BF16), r[...])
        i = sigmoid(z[:, 0:GW])
        f = sigmoid(z[:, GW : 2 * GW])
        o = sigmoid(z[:, 2 * GW : 3 * GW])
        g = jnp.tanh(z[:, 3 * GW :])
        c = f * cp + i * g
        h = (o * jnp.tanh(c)).astype(BF16).astype(F32)
        gates[at, :] = jnp.concatenate([i, f, o, g], axis=1)
        cells[at, :] = c
        hiddens[at, :] = h
        return h, c

    return lax.fori_loop(0, count, step, carry)


def lstm_back_steps(first, count, keep, c0, carry, rt, gates, cells, dhs):
    def step(s, carry):
        dh_next, dc_next = carry
        t = first + count - 1 - s
        at = pl.ds(pl.multiple_of(t * 8, 8), 8)
        before = pl.ds(pl.multiple_of(jnp.maximum(t - 1, 0) * 8, 8), 8)
        k = six(keep[at, :])
        saved = gates[at, :]
        i, f, o, g = [saved[:, GW * b : GW * b + GW] for b in range(4)]
        cp = jnp.where(t > 0, cells[before, :], c0[...]) * k
        ct = jnp.tanh(cells[at, :])
        dh = dhs[at, :] + dh_next
        dc = dc_next + dh * o * (1.0 - ct * ct)
        dz = jnp.concatenate(
            [dc * g * i * (1.0 - i), dc * cp * f * (1.0 - f), dh * ct * o * (1.0 - o), dc * i * (1.0 - g * g)], axis=1
        ).astype(BF16)
        gates[at, :] = dz.astype(F32)
        return k * mm(dz, rt[...]), k * dc * f

    return lax.fori_loop(0, count, step, carry)


def output_rows(first, count, h, w, targets, valid, logits, dl, top, part, dh, loss, dh16):
    at_rows = pl.ds(first, count)
    depth = w.shape[0]
    own = pl.ds(0, count)
    top[own, :] = jnp.full((count, LANE), -jnp.inf, F32)

    def forward(at, width):
        z = mm(h[at_rows, pl.ds(0, depth)], w[:, pl.ds(at, width)])
        if isinstance(at, int):
            z = jnp.where(column_mask(at, width, VOCAB, count), z, -jnp.inf)
        logits[own, pl.ds(at, width)] = z
        best = top[own, :]
        for c in range(width // LANE):
            best = jnp.maximum(best, z[:, LANE * c : LANE * c + LANE])
        top[own, :] = best

    each_vocab(forward)
    best = jnp.max(top[own, :], axis=1, keepdims=True)
    part[:, own, :] = jnp.zeros((2, count, LANE), F32)
    wanted = targets[at_rows, :]

    def exponents(at, width):
        z = logits[own, pl.ds(at, width)]
        e = jnp.exp(z - best)
        logits[own, pl.ds(at, width)] = e
        for c in range(width // LANE):
            part[0, own, :] += e[:, LANE * c : LANE * c + LANE]
            hit = lanes(count) + (at + LANE * c) == wanted
            part[1, own, :] += jnp.where(hit, z[:, LANE * c : LANE * c + LANE], 0.0)

    each_vocab(exponents)
    total = jnp.sum(part[0, own, :], axis=1, keepdims=True)
    picked = jnp.sum(part[1, own, :], axis=1, keepdims=True)
    counts = valid[at_rows, :]
    loss[...] += jnp.sum(counts * (best + jnp.log(total) - picked), axis=0, keepdims=True)
    share = counts / total
    dh[:, own] = jnp.zeros((depth, count), F32)

    def backward(at, width):
        e = logits[own, pl.ds(at, width)]
        pieces = []
        for c in range(width // LANE):
            hit = lanes(count) + (at + LANE * c) == wanted
            grad = e[:, LANE * c : LANE * c + LANE] * share - jnp.where(hit, counts, 0.0)
            pieces.append(grad.astype(BF16))
        grad = jnp.concatenate(pieces, axis=1)
        dl[at_rows, pl.ds(at, width)] = grad
        dh[:, own] += mm_nt(w[:, pl.ds(at, width)], grad)

    each_vocab(backward)
    for at, width in fblocks(depth):
        value = jnp.transpose(dh[pl.ds(at, width), own])
        dh16[at_rows, pl.ds(at, width)] = jnp.where(column_mask(at, width, HID, count), value, 0.0).astype(BF16)


QUAD = 4
LEFT0 = 35 * LANE
LEFT1 = 14 * LANE
LEFT2 = 11 * LANE
LEFT_ROOM = 41 * LANE


def quad_peer(me, k):
    place = lax.rem(me, QUAD)
    pair, side = place // 2, lax.rem(place, 2)
    return me + (k % 2) * (1 - 2 * side) + (k // 2) * (2 - 4 * pair)


def turn_features(feats, turned):
    n = feats.shape[1]
    zero = jnp.zeros((n, LANE), BF16)
    for segment in range(4):
        start = segment * (FILT + 1)
        shift, first, last = start % LANE, start // LANE, (start + FILT) // LANE
        for c in range(last - first + 1):
            left = feats[segment // 2, :, pl.ds(LANE * (c - 1), LANE)] if c > 0 else zero
            right = feats[segment // 2, :, pl.ds(LANE * c, LANE)] if c < 9 else zero
            tile = turned_tile(left, right, shift)
            at = pl.ds(LANE * (first + c), LANE)
            if c == 0 and segment > 0:
                tile = tile + turned[at, :]
            turned[at, :] = tile


def turn_inputs(x, prevs, depth, turned):
    n = prevs.shape[0]
    first, shift = depth // LANE, depth % LANE
    end = depth + HID
    zero = jnp.zeros((n, LANE), F32)
    lane = lanes(n)
    for c in range(end // LANE + 1):
        if c < first:
            mixed = x[:, pl.ds(LANE * c, LANE)]
        else:
            k = c - first
            left = prevs[:, pl.ds(LANE * (k - 1), LANE)].astype(F32) if 0 < k < 7 else zero
            right = prevs[:, pl.ds(LANE * k, LANE)].astype(F32) if k < 6 else zero
            before = pltpu.roll(left, shift, 1) if k else x[:, pl.ds(LANE * c, LANE)].astype(F32)
            mixed = jnp.where(lane < shift, before, pltpu.roll(right, shift, 1))
            mixed = jnp.where(lane + c * LANE == end, 1.0, mixed).astype(BF16)
        turned[pl.ds(LANE * c, LANE), :] = jnp.transpose(mixed)


SPLIT = 3
AB_PARTS = ((0, 640), (640, 512))


def highway_chunk(rows, slot, dy, feats, pres, grad, dpre, w):
    def cut(m, at, width):
        return pl.ds(m * FW + at, width)

    for at, width in fblocks(FW):
        grad[rows, pl.ds(at, width)] = dy[rows, pl.ds(at, width)].astype(F32)
    for layer in (1, 0):
        own = pl.ds(slot, CHUNK)
        for at, width in fblocks(FW):
            cols = pl.ds(at, width)
            g = grad[rows, cols]
            gate = sigmoid(pres[own, cut(2 * layer, at, width)])
            q = pres[own, cut(2 * layer + 1, at, width)]
            sig = sigmoid(q)
            y = feats[layer, rows, cols].astype(F32)
            dpre[rows, cut(2 * layer, at, width)] = (g * (q * sig - y) * gate * (1.0 - gate)).astype(BF16)
            dpre[rows, cut(2 * layer + 1, at, width)] = (g * gate * sig * (1.0 + q * (1.0 - sig))).astype(BF16)
            grad[rows, cols] = g * (1.0 - gate)
        turned = [jnp.transpose(dpre[rows, cut(2 * layer + i, 0, FW)]) for i in range(2)]
        for half, (row, count) in enumerate(AB_PARTS):
            for at, width in fblocks(count):
                cols = pl.ds(row + at, width)
                back = jnp.zeros((width, CHUNK), F32)
                for i in range(2):
                    part = w[pl.ds(at, width), pl.ds((2 * (2 * layer + i) + half) * FW, FW)]
                    back = back + mm(part, turned[i])
                value = grad[rows, cols] + jnp.transpose(back)
                if row + at + width > FILT:
                    value = jnp.where(column_mask(row + at, width, FILT, CHUNK), value, 0.0)
                grad[rows, cols] = value


def recurrent_call(y2, feats, pres, ab, ur, rt, wt, resets, target_ids, remaining, state):
    n = y2.shape[0]
    real_steps = resets.shape[1]
    chunks = n // CHUNK
    steps = CHUNK // 8
    depth_w = wt.shape[0]
    MESH = pl.DeviceIdType.MESH

    def kernel(
        y2, feats, pres, ab, ur, rt, wt, resets, target_ids, remaining, state,
        grad_o, dpre_o, right_o, xb_o, lhs_o, dz_o, dl_o, x_q, h_q, loss_o, bias_o,
        keep, valid, targets, feats_v, turned, pb, x1, xb, hb, db, ob, dy, u, r, r_t, w, start, gates, cells, prevs, hs, dhs, dz16,
        logits, dl, top, part, dh, loss,
        sem_in, sem_out, send_y, recv_y, send_f, recv_f, send_b, recv_b, send_d, recv_d,
        send_x, recv_x, send_h, recv_h, send_z, recv_z, sem_l, sem_p,
    ):
        role = lax.axis_index("section")
        me = lax.axis_index("dp")
        loss[...] = jnp.zeros_like(loss)
        bias_o[...] = jnp.zeros_like(bias_o)

        def to(step, source, target, send, recv):
            return pltpu.make_async_remote_copy(
                source, target, send, recv, device_id={"section": role + step}, device_id_type=MESH
            )

        def span(c):
            return pl.ds(pl.multiple_of(c * CHUNK, CHUNK), CHUNK)

        def forward_copy(c, step):
            return to(step, hb.at[span(c)], xb.at[span(c)], send_f.at[c], recv_f.at[c])

        def backward_copy(c, step):
            return to(step, ob.at[span(c)], db.at[span(c)], send_b.at[c], recv_b.at[c])

        def feature_copy(step):
            return to(step, y2, x1, send_y.at[0], recv_y.at[0])

        def last_copy(c, step):
            return to(step, dy.at[span(c)], dy.at[span(c)], send_d.at[c], recv_d.at[c])

        def quad_copy(source, target, send, recv, k):
            return pltpu.make_async_remote_copy(
                source, target, send, recv, device_id={"dp": quad_peer(me, k)}, device_id_type=MESH
            )

        def input_copy(k):
            return quad_copy(x1, x_q.at[k - 1, 0], send_x.at[k - 1, 0], recv_x.at[k - 1, 0], k)

        def layer_copy(k):
            return quad_copy(
                xb, x_q.at[k - 1, 0, :, pl.ds(0, GW)], send_x.at[k - 1, 0], recv_x.at[k - 1, 0], k
            )

        def feats_copy(k):
            return quad_copy(feats_v, x_q.at[k - 1], send_x.at[k - 1, 0], recv_x.at[k - 1, 0], k)

        def hidden_copy(k):
            return quad_copy(pb, h_q.at[k - 1], send_h.at[k - 1, 0], recv_h.at[k - 1, 0], k)

        def each_peer(body):
            for k in range(1, QUAD):
                body(k)

        def each_chunk(body, first=0):
            def step(c, carry):
                body(c)
                return carry

            lax.fori_loop(first, chunks, step, 0)

        def turned_out(g, rows):
            copy = pltpu.make_async_copy(turned.at[pl.ds(0, rows)], lhs_o.at[g, pl.ds(0, rows)], sem_l.at[0])
            copy.start()
            copy.wait()

        def fetch(source, target):
            copy = pltpu.make_async_copy(source, target, sem_l.at[1])
            copy.start()
            copy.wait()

        def dpre_copy(c, k):
            rows = pl.ds(pl.multiple_of((c - SPLIT) * CHUNK, CHUNK), CHUNK)
            source = right_o.at[1, rows] if k == 3 else dl.at[span(c), pl.ds(0, 4 * FW)]
            return quad_copy(
                source, right_o.at[k - 1, rows], send_z.at[k - 1, c], recv_z.at[k - 1, c], 1 if k == 3 else k
            )

        def right_copy(k):
            return quad_copy(dz16, dz_o.at[k - 1], send_z.at[k - 1, 0], recv_z.at[k - 1, 0], k)

        def exchange(copy, c, first):
            @pl.when(c >= first)
            def _():
                copy(c, 2).start()
                copy(c, 1).start()

            @pl.when((c < chunks - 1) & (c + 1 >= first))
            def _():
                copy(c + 1, 2).wait_recv()
                copy(c + 1, 3).start()

        def exchanged(copy, first):
            if first == 0:
                copy(0, 2).wait_recv()
                copy(0, 3).start()

            def settle(c):
                for k in range(1, QUAD):
                    copy(c, k).wait_send()
                    if k != 2:
                        copy(c, k).wait_recv()

            each_chunk(settle, first)

        def inputs(which):
            if which == 0:
                pairs = [(feats, feats_v)]
                for m in range(4):
                    for half, (row, count) in enumerate(AB_PARTS):
                        target = w.at[pl.ds(0, count), pl.ds((2 * m + half) * FW, FW)]
                        pairs.append((ab.at[m, pl.ds(row, count)], target))
            elif which == 3:
                pairs = [(wt, w)]
            else:
                depth = FW if which == 1 else GW
                pairs = [
                    (ur.at[pl.ds(0, depth)], u.at[pl.ds(0, depth)]),
                    (ur.at[pl.ds(FW, GW)], r),
                    (rt, r_t),
                ]
            return [pltpu.make_async_copy(a, b, sem_in.at[i]) for i, (a, b) in enumerate(pairs)]

        for which in range(4):

            @pl.when(role == which)
            def _(which=which):
                for copy in inputs(which):
                    copy.start()

        @pl.when((role == 1) | (role == 2))
        def _():
            start[...] = jnp.zeros_like(start)
            for which in (1, 2):

                @pl.when(role == which)
                def _(which=which):
                    for half in range(2):
                        start[half, :, pl.ds(0, HID)] = state[which - 1, half]

            for t in range(n // 8):
                rows = pl.ds(8 * t, 8)
                kept = jnp.zeros((8, LANE), F32)
                if t < real_steps:
                    kept = 1.0 - jnp.broadcast_to(resets[:, t : t + 1], (8, LANE)).astype(F32)
                keep[rows, :] = kept

        @pl.when(role == 3)
        def _():
            left_words = jnp.broadcast_to(remaining[...], (8, LANE))
            for t in range(n // 8):
                rows = pl.ds(8 * t, 8)
                if t < real_steps:
                    valid[rows, :] = jnp.where(left_words > t, 1.0, 0.0)
                    targets[rows, :] = jnp.broadcast_to(target_ids[:, t : t + 1], (8, LANE))
                else:
                    valid[rows, :] = jnp.zeros((8, LANE), F32)
                    targets[rows, :] = jnp.full((8, LANE), -1, jnp.int32)

        barrier = pltpu.get_barrier_semaphore()

        @pl.when(role > 0)
        def _():
            pl.semaphore_signal(barrier, inc=1, device_id={"section": role - 1}, device_id_type=MESH)

        @pl.when(role < 3)
        def _():
            pl.semaphore_signal(barrier, inc=1, device_id={"section": role + 1}, device_id_type=MESH)

        for k in range(1, QUAD):
            pl.semaphore_signal(barrier, inc=1, device_id={"dp": quad_peer(me, k)}, device_id_type=MESH)
        pl.semaphore_wait(barrier, lax.min(role, 1) + lax.min(3 - role, 1) + QUAD - 1)

        @pl.when(role == 0)
        def _():
            feature_copy(1).start()
            for copy in inputs(0):
                copy.wait()
            each_peer(lambda k: feats_copy(k).start())
            turn_features(feats_v, turned)
            turned_out(QUAD - 1, LEFT0)
            feature_copy(1).wait_send()
            each_peer(lambda k: feats_copy(k).wait_send())
            for k in range(1, QUAD):
                feats_copy(k).wait_recv()
                fetch(x_q.at[k - 1], feats_v)
                turn_features(feats_v, turned)
                turned_out(k - 1, LEFT0)
            fetch(feats, feats_v)

            def pres_copy(c, m):
                slot = lax.rem(c, 2)
                target = logits.at[pl.ds(pl.multiple_of(slot * CHUNK, CHUNK), CHUNK), pl.ds(m * FW, FW)]
                return pltpu.make_async_copy(pres.at[m, span(c)], target, sem_p.at[slot, m])

            for m in range(4):
                pres_copy(chunks - 1, m).start()

            def chunk(i, carry):
                c = chunks - 1 - i

                @pl.when(c > 0)
                def _():
                    for m in range(4):
                        pres_copy(c - 1, m).start()

                for m in range(4):
                    pres_copy(c, m).wait()
                last_copy(c, 1).wait_recv()
                highway_chunk(span(c), pl.multiple_of(lax.rem(c, 2) * CHUNK, CHUNK), dy, feats_v, logits, gates, dl, w)

                exchange(dpre_copy, c, SPLIT)
                return carry

            lax.fori_loop(0, chunks, chunk, 0)
            copies = [
                pltpu.make_async_copy(gates.at[:, pl.ds(0, FW)], grad_o, sem_out.at[0]),
                pltpu.make_async_copy(dl.at[:, pl.ds(0, 4 * FW)], dpre_o, sem_out.at[1]),
            ]
            for copy in copies:
                copy.start()
            for at, width in fblocks(FW):
                cols = pl.ds(at, width)
                bias_o[:, cols] = jnp.sum(dl[:, cols].astype(F32), axis=0, keepdims=True)
            for copy in copies:
                copy.wait()

            exchanged(dpre_copy, SPLIT)

        @pl.when((role == 1) | (role == 2))
        def _():
            for which in (1, 2):

                @pl.when(role == which)
                def _(which=which):
                    for copy in inputs(which):
                        copy.wait()

            bias = r[pl.ds(HID, 1), :].astype(F32)

            @pl.when(role == 1)
            def _():
                feature_copy(-1).wait_recv()
                for at, width in fblocks(ZW):
                    cols = pl.ds(at, width)
                    gates[:, cols] = mm(x1[...], u[:, cols]) + bias[:, at : at + width]

            def chunk_forward(c, carry):
                @pl.when(role == 2)
                def _():
                    forward_copy(c, -1).wait_recv()
                    for at, width in fblocks(ZW):
                        cols = pl.ds(at, width)
                        gates[span(c), cols] = mm(xb[span(c), :], u[pl.ds(0, GW), cols]) + bias[:, at : at + width]

                carry = lstm_steps(c * steps, steps, keep, carry, r, gates, cells, prevs, hs)
                hb[span(c), :] = hs[span(c), :].astype(BF16)
                forward_copy(c, 1).start()
                return carry

            h0 = start[0].astype(BF16).astype(F32)
            lax.fori_loop(0, chunks, chunk_forward, (h0, start[1]))

            def turn_all(which):
                depth, rows = (FILT, LEFT1) if which == 1 else (HID, LEFT2)
                width = FW if which == 1 else GW
                copies = (input_copy if which == 1 else layer_copy, hidden_copy)
                pb[...] = prevs[...].astype(BF16)
                each_peer(lambda k: [copy(k).start() for copy in copies])
                turn_inputs(x1 if which == 1 else xb, pb, depth, turned)
                turned_out(QUAD - 1, rows)
                for g in range(QUAD - 1):
                    for copy in copies:
                        copy(g + 1).wait_recv()
                    fetch(x_q.at[g, 0, :, pl.ds(0, width)], feats_v.at[0, :, pl.ds(0, width)])
                    fetch(h_q.at[g], ob)
                    turn_inputs(feats_v.at[0], ob, depth, turned)
                    turned_out(g, rows)
                each_peer(lambda k: [copy(k).wait_send() for copy in copies])

            @pl.when(role == 1)
            def _():
                turn_all(1)

            def chunk_backward(i, carry):
                c = chunks - 1 - i
                backward_copy(c, 1).wait_recv()
                dhs[span(c), :] = db[span(c), :].astype(F32)
                carry = lstm_back_steps(c * steps, steps, keep, start.at[1], carry, r_t, gates, cells, dhs)
                dz16[span(c), :] = gates[span(c), :].astype(BF16)

                dz_t = jnp.transpose(dz16[span(c), :])

                @pl.when(role == 1)
                def _():
                    for at, width in fblocks(FW):
                        value = jnp.transpose(mm(u[pl.ds(at, width), :], dz_t))
                        if at + width > FILT:
                            value = jnp.where(column_mask(at, width, FILT, CHUNK), value, 0.0)
                        dy[span(c), pl.ds(at, width)] = value.astype(BF16)
                    last_copy(c, -1).start()

                @pl.when(role == 2)
                def _():
                    for at, width in fblocks(GW):
                        value = jnp.transpose(mm(u[pl.ds(at, width), :], dz_t))
                        if at + width > HID:
                            value = jnp.where(column_mask(at, width, HID, CHUNK), value, 0.0)
                        ob[span(c), pl.ds(at, width)] = value.astype(BF16)
                    backward_copy(c, -1).start()

                return carry

            zero = jnp.zeros((8, GW), F32)
            lax.fori_loop(0, chunks, chunk_backward, (zero, zero))

            own_right = pltpu.make_async_copy(dz16, dz_o.at[QUAD - 1], sem_out.at[1])
            own_right.start()
            each_peer(lambda k: right_copy(k).start())

            @pl.when(role == 1)
            def _():
                each_chunk(lambda c: last_copy(c, -1).wait_send())

            @pl.when(role == 2)
            def _():
                each_chunk(lambda c: backward_copy(c, -1).wait_send())
                turn_all(2)

            own_right.wait()
            each_peer(lambda k: right_copy(k).wait_send())
            each_peer(lambda k: right_copy(k).wait_recv())

            def sent(c, carry):
                forward_copy(c, 1).wait_send()
                return carry

            lax.fori_loop(0, chunks, sent, 0)

        @pl.when(role == 3)
        def _():
            for copy in inputs(3):
                copy.wait()
            ob[...] = jnp.zeros_like(ob)
            done = 0
            for count in GROUPS_OUT:
                rows = pl.ds(done * CHUNK, count * CHUNK)
                for c in range(done, done + count):
                    forward_copy(c, -1).wait_recv()
                value = xb[rows, pl.ds(5 * LANE, LANE)].astype(F32)
                value = jnp.where(lanes(count * CHUNK) + 5 * LANE == HID, 1.0, value)
                xb[rows, pl.ds(5 * LANE, LANE)] = value.astype(BF16)
                output_rows(
                    done * CHUNK, count * CHUNK, xb, w, targets, valid, logits, dl, top, part, dh, loss, ob
                )
                for c in range(done, done + count):
                    backward_copy(c, -1).start()
                done += count
            copies = [
                pltpu.make_async_copy(xb, xb_o, sem_out.at[0]),
                pltpu.make_async_copy(dl, dl_o, sem_out.at[1]),
            ]
            for copy in copies:
                copy.start()
            for c in range(chunks):
                backward_copy(c, -1).wait_send()
            for copy in copies:
                copy.wait()

        loss_o[...] = loss[...]

    most = max(GROUPS_OUT) * CHUNK
    sems = pltpu.SemaphoreType.DMA
    outs = [
        ((n, FW), F32), ((n, 4 * FW), BF16), ((QUAD - 1, n - SPLIT * CHUNK, 4 * FW), BF16), ((n, GW), BF16),
        ((QUAD, LEFT_ROOM, n), BF16), ((QUAD, n, ZW), BF16), ((n, VW), BF16), ((QUAD - 1, 2, n, FW), BF16),
        ((QUAD - 1, n, GW), BF16),
    ]
    scratch = [
        vmem((n, LANE), F32), vmem((n, LANE), F32), vmem((n, LANE), jnp.int32),
        vmem((2, n, FW), BF16), vmem((LEFT0, n), BF16), vmem((n, GW), BF16),
        vmem((n, FW), BF16), vmem((n, GW), BF16), vmem((n, GW), BF16), vmem((n, GW), BF16), vmem((n, GW), BF16),
        vmem((n, FW), BF16), vmem((FW, ZW), BF16), vmem((GW, ZW), BF16), vmem((ZW, GW), BF16), vmem(wt.shape, BF16),
        vmem((2, 8, GW), F32), vmem((n, ZW), F32), vmem((n, GW), F32), vmem((n, GW), F32), vmem((n, GW), F32),
        vmem((n, GW), F32), vmem((n, ZW), BF16),
        vmem((most, VW), F32), vmem((n, VW), BF16), vmem((most, LANE), F32), vmem((2, most, LANE), F32),
        vmem((depth_w, LANE), F32), vmem((1, LANE), F32),
        dmas(12), dmas(3), dmas(1), dmas(1), dmas(chunks), dmas(chunks), dmas(chunks), dmas(chunks), dmas(chunks), dmas(chunks),
        sems((QUAD - 1, chunks)), sems((QUAD - 1, chunks)), sems((QUAD - 1, chunks)), sems((QUAD - 1, chunks)),
        sems((QUAD - 1, chunks)), sems((QUAD - 1, chunks)), dmas(2), sems((2, 4)),
    ]
    return pl.pallas_call(
        kernel,
        out_shape=[jax.ShapeDtypeStruct(shape, dtype) for shape, dtype in outs]
        + [jax.ShapeDtypeStruct((1, LANE), F32), jax.ShapeDtypeStruct((1, FW), F32)],
        in_specs=[ANYWHERE] * 7 + [ON_CHIP] * 4,
        out_specs=[ANYWHERE] * 9 + [ON_CHIP] * 2,
        scratch_shapes=scratch,
        compiler_params=pltpu.CompilerParams(vmem_limit_bytes=62 << 20, collective_id=3, has_side_effects=True),
        name="recurrent",
    )(y2, feats, pres, ab, ur, rt, wt, resets, target_ids, remaining, state)


FORM = (
    (FILT, 9, 4 * (FILT + 1), CONV_END, CONV_TILES, 32),
    (4 * HID, 24, FILT + HID + 1, 0, 0, 16),
    (4 * HID, 24, 2 * HID + 1, 0, 0, 16),
    (VOCAB, 79, HID + 1, 0, 0, 16),
)


def slab(role, dest, share):
    width, pitch, rows, before, lead, period = FORM[role]
    low = lax.max if not isinstance(dest, int) else max
    high = lax.min if not isinstance(dest, int) else min
    one = (lambda v: v) if isinstance(dest, int) else jnp.int32
    start = low(one(share) * dest - before, one(0))
    first = start // width // period * period
    end = high((share * (dest + 1) - before + width - 1) // width, one(rows))
    count = low((end - first + 15) // 16, one(0)) * pitch
    tile = lead + first // 16 * pitch
    if lead:
        if isinstance(dest, int):
            if dest == 0:
                tile, count = 0, count + lead
        else:
            head = lax.max(1 - dest, 0)
            tile = tile - lead * head
            count = count + lead * head
    return first, tile, count


def slab_pieces(count, size):
    return (count + size - 1) // size


def gather_sum_call(tiles, groups, share):
    pair = 2
    across = groups // pair
    size = 64 if across <= 4 else 32
    pieces = max(slab_pieces(slab(3, dest, share)[2], size) for dest in range(groups))
    room = pieces * size
    line = across <= 4
    slots = across + 1 if line else across - 1
    MESH = pl.DeviceIdType.MESH

    def kernel(
        tiles, out, own, got1, got2, acc, own_sem, send1, recv1, send2, recv2, out_sem,
    ):
        role = lax.axis_index("section")
        me = lax.axis_index("dp")
        mine, side = me // pair, lax.rem(me, pair)
        other = mine * pair + (1 - side)

        def at_place(place):
            return {"dp": place * pair + side}

        def part(ref, slot, p):
            return ref.at[slot, pl.ds(pl.multiple_of(p * size, size), size)]

        def span(p):
            return pl.ds(pl.multiple_of(p * size, size), size)

        def loop(count, body):
            def step(p, carry):
                body(p)
                return carry

            lax.fori_loop(0, count, step, 0)

        def run(shape_of):
            def count_to(place, which):
                return shape_of(place * pair + which)[1]

            def own_copy(place, p):
                tile, _ = shape_of(place * pair + side)
                return pltpu.make_async_copy(
                    tiles.at[pl.ds(tile + p * size, size)], part(own, place, p), own_sem.at[place, p]
                )

            def first_copy(place, p):
                tile, _ = shape_of(place * pair + 1 - side)
                return pltpu.make_async_remote_copy(
                    tiles.at[pl.ds(tile + p * size, size)], part(got1, place, p), send1.at[place, p], recv1.at[place, p],
                    device_id={"dp": other}, device_id_type=MESH,
                )

            def begin(place):
                loop(count_to(place, 1 - side), lambda p: first_copy(place, p).start())
                loop(count_to(place, side), lambda p: own_copy(place, p).start())

            def hop_copy(place, up, p):
                if line:
                    target = mine + 1 if up else mine - 1
                    slot = jnp.where(place == mine + 1, across, place) if up else place
                else:
                    target = place
                    slot = lax.rem(place - mine + across, across) - 1
                return pltpu.make_async_remote_copy(
                    part(own, place, p), part(got2, slot, p), send2.at[place, p], recv2.at[slot, p],
                    device_id=at_place(target), device_id_type=MESH,
                )

            def arrived(slot, p):
                return pltpu.make_async_remote_copy(
                    part(own, 0, p), part(got2, slot, p), send2.at[0, p], recv2.at[slot, p],
                    device_id=at_place(lax.rem(mine + 1, across)), device_id_type=MESH,
                )

            def forward(place, up, has_before):
                def body(p):
                    own_copy(place, p).wait()
                    first_copy(place, p).wait_recv()
                    at = span(p)
                    own[place, at] = (own[place, at].astype(F32) + got1[place, at].astype(F32)).astype(BF16)
                    hop_copy(place, up, p).start()

                def body_sum(p):
                    own_copy(place, p).wait()
                    first_copy(place, p).wait_recv()
                    arrived(place, p).wait_recv()
                    at = span(p)
                    total = own[place, at].astype(F32) + got1[place, at].astype(F32) + got2[place, at].astype(F32)
                    own[place, at] = total.astype(BF16)
                    hop_copy(place, up, p).start()

                count = count_to(place, side)
                if not line:
                    loop(count, body)
                    return

                @pl.when(has_before)
                def _():
                    loop(count, body_sum)

                @pl.when(jnp.logical_not(has_before))
                def _():
                    loop(count, body)

            if line:
                for k in range(across - 1):

                    @pl.when(k < mine)
                    def _(k=k):
                        begin(k)

                    @pl.when(k < across - 1 - mine)
                    def _(k=k):
                        begin(across - 1 - k)

                begin(mine)
                for k in range(across - 1):

                    @pl.when(k < mine)
                    def _(k=k):
                        forward(k, False, mine < across - 1)

                    @pl.when(k < across - 1 - mine)
                    def _(k=k):
                        forward(across - 1 - k, True, mine > 0)

            else:
                for k in range(1, across):
                    begin(lax.rem(mine + k, across))
                begin(mine)
                for k in range(1, across):
                    forward(lax.rem(mine + k, across), True, None)

            def settle(p):
                own_copy(mine, p).wait()
                first_copy(mine, p).wait_recv()
                at = span(p)
                acc[at] = own[mine, at].astype(F32) + got1[mine, at].astype(F32)

            def add(slot):
                def body(p):
                    arrived(slot, p).wait_recv()
                    at = span(p)
                    acc[at] += got2[slot, at].astype(F32)

                return body

            mine_count = count_to(mine, side)
            loop(mine_count, settle)
            if line:

                @pl.when(mine < across - 1)
                def _():
                    loop(mine_count, add(mine))

                @pl.when(mine > 0)
                def _():
                    loop(mine_count, add(across))

            else:
                for k in range(1, across):
                    loop(mine_count, add(k - 1))

            def out_copy(p):
                return pltpu.make_async_copy(acc.at[span(p)], out.at[span(p)], out_sem.at[p])

            loop(mine_count, lambda p: out_copy(p).start())
            loop(mine_count, lambda p: out_copy(p).wait())
            for place in range(across):
                loop(count_to(place, 1 - side), lambda p, place=place: first_copy(place, p).wait_send())

                @pl.when(place != mine)
                def _(place=place):
                    loop(count_to(place, side), lambda p: hop_copy(place, True, p).wait_send())

        def shape_of(dest):
            _, tile, count = slab(3, dest, share)
            return tile, slab_pieces(count, size)

        @pl.when(role == 3)
        def _():
            barrier = pltpu.get_barrier_semaphore()
            pl.semaphore_signal(barrier, inc=1, device_id={"dp": other}, device_id_type=MESH)
            for k in range(1, across):
                peer = at_place(lax.rem(mine + k, across))
                pl.semaphore_signal(barrier, inc=1, device_id=peer, device_id_type=MESH)
            pl.semaphore_wait(barrier, across)
            run(shape_of)

    sems = pltpu.SemaphoreType.DMA
    return pl.pallas_call(
        kernel,
        out_shape=jax.ShapeDtypeStruct((room, 16, LANE), F32),
        in_specs=[ANYWHERE],
        out_specs=ANYWHERE,
        scratch_shapes=[
            vmem((across, room, 16, LANE), BF16), vmem((across, room, 16, LANE), BF16),
            vmem((slots, room, 16, LANE), BF16), vmem((room, 16, LANE), F32),
            sems((across, pieces)), sems((across, pieces)), sems((across, pieces)),
            sems((across, pieces)), sems((slots, pieces)), sems((pieces,)),
        ],
        compiler_params=pltpu.CompilerParams(vmem_limit_bytes=62 << 20, collective_id=1, has_side_effects=True),
        name="gather_sum",
    )(tiles)


BLOCK_ROWS = (25, 11, 11)


def finish_call(lhs, dz, dpre, rights, conv, bias, loss, after, groups, share):
    n = lhs.shape[2]
    quads = groups // QUAD
    MESH = pl.DeviceIdType.MESH

    def most_blocks(role):
        width = FORM[role][1]
        lead = FORM[role][4]
        most = 0
        for dest in range(groups):
            count = slab(role, dest, share)[2]
            if lead and dest == 0:
                count -= lead
            most = max(most, -(-(count // width) // BLOCK_ROWS[role]))
        return most

    blocks = [most_blocks(role) for role in range(3)]
    room = max(
        FORM[role][4] + blocks[role] * BLOCK_ROWS[role] * FORM[role][1] for role in range(3)
    )
    left_rows = max(blocks[role] * BLOCK_ROWS[role] * 16 for role in range(3))
    most = max(blocks)

    def kernel(
        lhs, dz, dpre, late, early, conv, bias, loss, after, out, small_out,
        left, dpre_v, sent, got, acc, convs, lead_sum, small, got_small,
        sem_left, sem_right, send, recv, send_c, recv_c, small_send, small_recv, sem_out,
        shared, shared_send, shared_recv,
    ):
        role = lax.axis_index("section")
        me = lax.axis_index("dp")
        place, quad = lax.rem(me, QUAD), me // QUAD

        def across_peer(k):
            return {"dp": place + QUAD * lax.rem(quad + k, quads)}

        barrier = pltpu.get_barrier_semaphore()
        for k in range(1, QUAD):
            pl.semaphore_signal(barrier, inc=1, device_id={"dp": quad_peer(me, k)}, device_id_type=MESH)
        for k in range(1, quads):
            pl.semaphore_signal(barrier, inc=1, device_id=across_peer(k), device_id_type=MESH)

        for source in (0, 3):

            @pl.when(role != source)
            def _(source=source):
                pl.semaphore_signal(barrier, inc=1, device_id={"section": source}, device_id_type=MESH)

        def right_load(b):
            return pltpu.make_async_copy(
                dz.at[:, :, pl.ds(GW * b, GW)], dpre_v.at[:, b, :, pl.ds(0, GW)], sem_right.at[b]
            )

        def right_loads0():
            copies = []
            cut = SPLIT * CHUNK
            for b in range(4):
                cols = pl.ds(FW * b, FW)
                pairs = [
                    (early.at[:, :, cols], dpre_v.at[pl.ds(0, QUAD - 1), b, pl.ds(0, cut)]),
                    (late.at[:, :, cols], dpre_v.at[pl.ds(0, QUAD - 1), b, pl.ds(cut, n - cut)]),
                    (dpre.at[:, cols], dpre_v.at[QUAD - 1, b]),
                ]
                copies += [pltpu.make_async_copy(x, y, sem_right.at[4 + 3 * b + i]) for i, (x, y) in enumerate(pairs)]
            return copies

        def conv_load():
            return pltpu.make_async_copy(conv, convs.at[QUAD - 1], sem_right.at[16])

        @pl.when(role == 0)
        def _():
            for copy in right_loads0():
                copy.start()
            conv_load().start()

        @pl.when((role == 1) | (role == 2))
        def _():
            for b in range(4):
                right_load(b).start()

        ends = lax.max(1 - role, 0) + lax.max(role - 2, 0)
        pl.semaphore_wait(barrier, QUAD - 1 + quads - 1 + 3 * ends)

        small[...] = jnp.zeros_like(small)

        @pl.when(role == 0)
        def _():
            small[0, :, pl.ds(0, FW)] = bias[...]

        @pl.when(role == 3)
        def _():
            small[0, :, pl.ds(FW, LANE)] = loss[...]

        def small_copy(k):
            if k < QUAD:
                source, target = small.at[0], {"dp": quad_peer(me, k)}
            else:
                source, target = small.at[1], across_peer(k - QUAD + 1)
            return pltpu.make_async_remote_copy(
                source, got_small.at[k - 1], small_send.at[k - 1], small_recv.at[k - 1],
                device_id=target, device_id_type=MESH,
            )

        for k in range(1, QUAD):
            small_copy(k).start()

        def across_small():
            for k in range(1, QUAD):
                small_copy(k).wait_recv()
            small[1] = small[0] + got_small[0] + got_small[1] + got_small[2]
            for k in range(QUAD, QUAD + quads - 1):
                small_copy(k).start()

        def share_copy(slot, k):
            return pltpu.make_async_remote_copy(
                small.at[0], shared.at[slot], shared_send.at[slot, k - 1], shared_recv.at[slot],
                device_id={"section": lax.rem(role + k, 4)}, device_id_type=MESH,
            )

        def share_small():
            total = small[1]
            for k in range(QUAD, QUAD + quads - 1):
                small_copy(k).wait_recv()
                total = total + got_small[k - 1]
            for k in range(1, QUAD):
                small_copy(k).wait_send()
            small[0] = total
            for slot, source in enumerate((0, 3)):

                @pl.when(role == source)
                def _(slot=slot):
                    for k in range(1, 4):
                        share_copy(slot, k).start()

        def conv_copy(slot, target):
            return pltpu.make_async_remote_copy(
                conv, convs.at[slot], send_c.at[slot], recv_c.at[slot], device_id={"dp": target}, device_id_type=MESH
            )

        def run(which):
            width, pitch, rows, _, lead, _ = FORM[which]
            size = BLOCK_ROWS[which]
            block_tiles = size * pitch

            def geometry(k):
                dest = place + QUAD * lax.rem(quad + k, quads)
                first, _, count = slab(which, dest, share)
                if lead:
                    head = lax.max(1 - dest, 0)
                    count = count - lead * head
                else:
                    head = 0
                return first, (count // pitch + size - 1) // size, head

            def left_copy(k):
                height = blocks[which] * size * 16
                first = lax.min(geometry(k)[0], LEFT_ROOM - height)
                span = pl.ds(pl.multiple_of(first, 16), height)
                return pltpu.make_async_copy(
                    lhs.at[:, span], left.at[lax.rem(k, 2), :, pl.ds(0, blocks[which] * size * 16)], sem_left.at[lax.rem(k, 2)]
                )

            def block_copy(k, b):
                span = pl.ds(CONV_TILES + b * block_tiles, block_tiles)
                return pltpu.make_async_remote_copy(
                    sent.at[k - 1, span], got.at[k - 1, span], send.at[k - 1, b], recv.at[k - 1, b],
                    device_id=across_peer(k), device_id_type=MESH,
                )

            def lead_copy(k):
                span = pl.ds(0, CONV_TILES)
                return pltpu.make_async_remote_copy(
                    sent.at[k - 1, span], got.at[k - 1, span], send.at[k - 1, most], recv.at[k - 1, most],
                    device_id=across_peer(k), device_id_type=MESH,
                )

            def put(k, own, at, value):
                if own:
                    acc[at] = value
                else:
                    sent[k - 1, at] = value.astype(BF16)

            def block(k, own, b, first):
                here = pl.ds(pl.multiple_of(b * size * 16, 16), size * 16)
                base = CONV_TILES + b * block_tiles
                if which == 0:
                    row = lax.broadcasted_iota(jnp.int32, (size * 16, n), 0) + first + b * size * 16
                    start = first + b * size * 16
                    low = lax.min(start // (FILT + 1), 3)
                    high = lax.min((start + size * 16 - 1) // (FILT + 1), 3)
                    edge = (FILT + 1) * (low + 1)
                    lefts = [left[lax.rem(k, 2), g, here, :] for g in range(QUAD)]
                    near = [jnp.where(row < edge, x, jnp.zeros_like(x)) for x in lefts]
                    for col, wide in fblocks(FW):
                        value = jnp.zeros((size * 16, wide), F32)
                        for g in range(QUAD):
                            value = value + mm(near[g], dpre_v[g, low, :, pl.ds(col, wide)])
                        for r in range(size):
                            for c in range(wide // LANE):
                                tile = value[16 * r : 16 * r + 16, LANE * c : LANE * c + LANE]
                                put(k, own, base + r * pitch + col // LANE + c, tile)

                    @pl.when(high > low)
                    def _():
                        far = [jnp.where(row < edge, jnp.zeros_like(x), x) for x in lefts]
                        for col, wide in fblocks(FW):
                            value = jnp.zeros((size * 16, wide), F32)
                            for g in range(QUAD):
                                value = value + mm(far[g], dpre_v[g, high, :, pl.ds(col, wide)])
                            for r in range(size):
                                for c in range(wide // LANE):
                                    tile = value[16 * r : 16 * r + 16, LANE * c : LANE * c + LANE]
                                    at = base + r * pitch + col // LANE + c
                                    old = acc[at] if own else sent[k - 1, at].astype(F32)
                                    put(k, own, at, old + tile)

                else:
                    for col, wide in fblocks(ZW):
                        value = jnp.zeros((size * 16, wide), F32)
                        for g in range(QUAD):
                            value = value + mm(left[lax.rem(k, 2), g, here, :], dpre_v[g, col // GW, :, pl.ds(col % GW, wide)])
                        for r in range(size):
                            for c in range(wide // LANE):
                                tile = value[16 * r : 16 * r + 16, LANE * c : LANE * c + LANE]
                                put(k, own, base + r * pitch + col // LANE + c, tile)

            def loop(count, body):
                def step(b, carry):
                    body(b)
                    return carry

                lax.fori_loop(0, count, step, 0)

            left_copy(jnp.int32(1 % quads)).start()
            if which == 0:

                @pl.when(place > 0)
                def _():
                    for k in range(1, QUAD):

                        @pl.when(place == k)
                        def _(k=k):
                            conv_copy(k - 1, me - k).start()

                for copy in right_loads0():
                    copy.wait()
                conv_load().wait()
            else:
                for b in range(4):
                    right_load(b).wait()

            if which == 0:

                @pl.when(place == 0)
                def _():
                    for k in range(1, QUAD):
                        conv_copy(k - 1, me + k).wait_recv()
                    total = convs[0].astype(F32)
                    for k in range(1, QUAD):
                        total = total + convs[k].astype(F32)
                    lead_sum[...] = total

            def slab_of(k, own):
                left_copy(k).wait()
                if not own:
                    left_copy(lax.rem(k + 1, quads)).start()
                first, count, head = geometry(k)
                if which == 0:

                    @pl.when(head > 0)
                    def _():
                        if own:
                            acc[pl.ds(0, CONV_TILES)] = lead_sum[...]
                        else:
                            sent[k - 1, pl.ds(0, CONV_TILES)] = lead_sum[...].astype(BF16)
                            lead_copy(k).start()

                def work(b):
                    block(k, own, b, first)
                    if not own:
                        block_copy(k, b).start()

                loop(count, work)

            def others(body):
                def step(k, carry):
                    body(k)
                    return carry

                lax.fori_loop(1, quads, step, 0)

            others(lambda k: slab_of(k, False))
            across_small()
            slab_of(jnp.int32(0), True)
            share_small()

            _, mine, head = geometry(0)
            def join(k):
                def add(b):
                    block_copy(k, b).wait_recv()
                    span = pl.ds(CONV_TILES + b * block_tiles, block_tiles)
                    acc[span] += got[k - 1, span].astype(F32)

                loop(mine, add)
                if which == 0:

                    @pl.when(head > 0)
                    def _():
                        lead_copy(k).wait_recv()
                        span = pl.ds(0, CONV_TILES)
                        acc[span] += got[k - 1, span].astype(F32)

            others(join)

            span = blocks[which] * block_tiles
            if which == 0:

                @pl.when(head > 0)
                def _():
                    copy = pltpu.make_async_copy(
                        acc.at[pl.ds(0, CONV_TILES + span)], out.at[pl.ds(0, CONV_TILES + span)], sem_out.at[0]
                    )
                    copy.start()
                    copy.wait()

                @pl.when(head == 0)
                def _():
                    copy = pltpu.make_async_copy(acc.at[pl.ds(CONV_TILES, span)], out.at[pl.ds(0, span)], sem_out.at[0])
                    copy.start()
                    copy.wait()

            else:
                copy = pltpu.make_async_copy(acc.at[pl.ds(CONV_TILES, span)], out.at[pl.ds(0, span)], sem_out.at[0])
                copy.start()
                copy.wait()

            def sent_all(k):
                _, count, head = geometry(k)
                loop(count, lambda b: block_copy(k, b).wait_send())
                if which == 0:

                    @pl.when(head > 0)
                    def _():
                        lead_copy(k).wait_send()

            others(sent_all)

            if which == 0:
                for k in range(1, QUAD):

                    @pl.when(place == k)
                    def _(k=k):
                        conv_copy(k - 1, me - k).wait_send()

        for which in range(3):

            @pl.when(role == which)
            def _(which=which):
                run(which)

        @pl.when(role == 3)
        def _():
            across_small()
            share_small()

        result = jnp.zeros((1, FW + LANE), F32)
        for slot, source in enumerate((0, 3)):

            @pl.when(role == source)
            def _(slot=slot):
                shared[slot] = small[0]

            @pl.when(role != source)
            def _(slot=slot):
                share_copy(slot, 1).wait_recv()

            result = result + shared[slot]
        small_out[...] = result
        for slot, source in enumerate((0, 3)):

            @pl.when(role == source)
            def _(slot=slot):
                for k in range(1, 4):
                    share_copy(slot, k).wait_send()

        for k in range(QUAD, QUAD + quads - 1):
            small_copy(k).wait_send()

    sems = pltpu.SemaphoreType.DMA
    full = CONV_TILES + max(blocks[role] * BLOCK_ROWS[role] * FORM[role][1] for role in range(3))
    smalls = QUAD + quads - 2
    return pl.pallas_call(
        kernel,
        out_shape=[jax.ShapeDtypeStruct((full, 16, LANE), F32), jax.ShapeDtypeStruct((1, FW + LANE), F32)],
        in_specs=[ANYWHERE] * 6 + [ON_CHIP] * 2 + [ANYWHERE],
        out_specs=[ANYWHERE, ON_CHIP],
        scratch_shapes=[
            vmem((2, QUAD, left_rows, n), BF16), vmem((QUAD, 4, n, FW), BF16),
            vmem((quads - 1, full, 16, LANE), BF16), vmem((quads - 1, full, 16, LANE), BF16),
            vmem((full, 16, LANE), F32), vmem((QUAD, CONV_TILES, 16, LANE), BF16), vmem((CONV_TILES, 16, LANE), F32),
            vmem((2, 1, FW + LANE), F32), vmem((smalls, 1, FW + LANE), F32),
            sems((2,)), sems((17,)), sems((quads - 1, most + 1)), sems((quads - 1, most + 1)),
            sems((QUAD - 1,)), sems((QUAD - 1,)), sems((smalls,)), sems((smalls,)), sems((1,)),
            vmem((2, 1, FW + LANE), F32), sems((2, 3)), sems((2,)),
        ],
        compiler_params=pltpu.CompilerParams(vmem_limit_bytes=62 << 20, collective_id=5, has_side_effects=True),
        name="finish",
    )(lhs, dz, dpre, *rights, conv, bias, loss, after)


def pack_call(summed, summed3, groups, share):
    rooms = (summed.shape[0] * 16, summed3.shape[0] * 16)
    chunks = share // LANE
    margin = 1280
    slab_rows = 10624
    flat_rows = margin + max(10752, chunks + 1280)

    def kernel(summed, summed3, out, rows_v, spaced, flat, sem):
        role = lax.axis_index("section")
        me = lax.axis_index("dp")
        zero = jnp.zeros((64, LANE), F32)

        def clear(i, carry):
            flat[pl.ds(pl.multiple_of(i * 64, 64), 64), :] = zero
            return carry

        def fetch(source, room):
            return pltpu.make_async_copy(source, rows_v.at[pl.ds(0, room)], sem.at[0])

        @pl.when(role < 3)
        def _():
            fetch(summed, rooms[0]).start()

        @pl.when(role == 3)
        def _():
            fetch(summed3, rooms[1]).start()

        lax.fori_loop(0, flat_rows // 64, clear, 0)

        @pl.when(role < 3)
        def _():
            fetch(summed, rooms[0]).wait()

        @pl.when(role == 3)
        def _():
            fetch(summed3, rooms[1]).wait()

        lane = lanes()

        for which in range(4):
            width, pitch, rows, before, lead, period = FORM[which]
            if which == 0:
                blocks, cols, tiles = 1, FILT, 9
            elif which == 3:
                blocks, cols, tiles = 1, VOCAB, 79
            else:
                blocks, cols, tiles = 4, HID, 6
            stride = period * width // LANE
            most = max(slab(which, dest, share)[2] for dest in range(groups))
            groups8 = -(-(-(-most // pitch) * 16) // (8 * period))

            @pl.when(role == which)
            def _(which=which):
                first, _, count = slab(which, me, share)
                skip = lead * lax.max(1 - me, 0)
                step_rows = pitch * 49 + (pitch * 49 + 1) % 2

                def space(rt, carry):
                    for c in range(pitch):
                        for half in range(2):
                            at = pl.multiple_of((skip + rt * pitch + c) * 16 + 8 * half, 8)
                            spaced[pl.ds(rt * step_rows + 49 * c + 24 * half, 8, stride=3), :] = rows_v[pl.ds(at, 8), :]
                    return carry

                lax.fori_loop(0, (count - skip) // pitch, space, 0)
                base = margin + before // LANE + stride * (first // period) - chunks * me

                hop = period // 16 * step_rows
                half = period // 2

                def place(group, n, b):
                    number = first + period * (8 * group + sublanes()) + n
                    flat_at = before % LANE + width * n + cols * b
                    source = n // 16 * step_rows + 3 * lax.rem(n, 16) + 8 * group * hop + 49 * tiles * b
                    to = base + flat_at // LANE + stride * 8 * group
                    return number < rows, lax.rem(flat_at, LANE), source, to

                def run(places, low, high, lasts):
                    taken = [
                        [spaced[pl.ds(source + 49 * j, 8, stride=hop), :] for j in range(low, min(high, tiles))]
                        for _, _, source, _ in places
                    ]
                    edges = [j for j in range(low, high) if j == 0 or j >= tiles - 1]
                    old = [
                        {j: flat[pl.ds(to + j, 8, stride=stride), :] for j in edges} for _, _, _, to in places
                    ]
                    values, ends = [], []
                    for (keep, turn, _, _), pieces, olds, last in zip(places, taken, old, lasts):
                        turned = [last] + [pltpu.roll(jnp.where(keep, x, 0.0), turn, 1) for x in pieces]
                        for j in range(low, high):
                            here = turned[j - low + 1] if j < tiles else turned[-1]
                            value = here if j == tiles else jnp.where(lane >= turn, here, turned[j - low])
                            if j in olds:
                                at = lane + LANE * j - turn
                                value = jnp.where((at >= 0) & (at < cols), value, olds[j])
                            values.append(value)
                        ends.append(turned[-1])
                    at = 0
                    for _, _, _, to in places:
                        for j in range(low, high):
                            flat[pl.ds(to + j, 8, stride=stride), :] = values[at]
                            at += 1
                    return ends

                def row(i, carry):
                    group, n = i // half, lax.rem(i, half)
                    zero = jnp.zeros((8, LANE), F32)
                    if blocks == 4:
                        for b in range(2):
                            places = [place(group, m, c) for m in (n, n + half) for c in (b, b + 2)]
                            run(places, 0, tiles + 1, [zero] * 4)
                    else:
                        places = [place(group, m, 0) for m in (n, n + half)]
                        ends = [zero] * 2
                        for low in range(0, tiles + 1, 20):
                            ends = run(places, low, min(low + 20, tiles + 1), ends)
                    return carry

                @pl.when(count > 0)
                def _():
                    lax.fori_loop(0, half * groups8, row, 0)

        @pl.when((role == 0) & (me == 0))
        def _():
            lane1 = lanes(1)

            def piece(row_at, flat_at, low, size):
                edge = flat_at - low
                turn = edge % LANE
                to = margin + (edge - turn) // LANE
                first, end = low // LANE, (low + size - 1) // LANE
                last = jnp.zeros((1, LANE), F32)
                for j in range(first, end + 2):
                    least, most = max(low + turn - LANE * j, 0), min(low + size + turn - LANE * j, LANE)
                    here = last
                    if j <= end:
                        here = rows_v[row_at + 16 * j : row_at + 16 * j + 1, :]
                        here = pltpu.roll(here, turn, 1) if turn else here
                    if most > least:
                        value = jnp.where(lane1 >= turn, here, last) if turn else here
                        at = to + j
                        if least > 0 or most < LANE:
                            value = jnp.where((lane1 >= least) & (lane1 < most), value, flat[at : at + 1, :])
                        flat[at : at + 1, :] = value
                    last = here

            for k in range(1, 8):
                n = NFILT[k - 1]
                for i in range(k * D_CHAR + 1):
                    number = i + i // D_CHAR if i < k * D_CHAR else 15
                    piece(number // 16 * 144 + number % 16, KOFF[k - 1] + n * i, COLS[k - 1], n)
            for a in range(CHAR_V):
                piece(72 * 16 + a, D_CHAR * a, 0, D_CHAR)

        copy = pltpu.make_async_copy(flat.at[pl.ds(margin, chunks)], out, sem.at[0])
        copy.start()
        copy.wait()

    return pl.pallas_call(
        kernel,
        out_shape=jax.ShapeDtypeStruct((chunks, LANE), F32),
        in_specs=[ANYWHERE] * 2,
        out_specs=ANYWHERE,
        scratch_shapes=[
            vmem((slab_rows, LANE), F32), vmem((31104, LANE), F32), vmem((flat_rows, LANE), F32), dmas(1),
        ],
        compiler_params=pltpu.CompilerParams(vmem_limit_bytes=LIMIT),
        name="pack",
    )(summed.reshape(rooms[0], LANE), summed3.reshape(rooms[1], LANE))


def shards(char_ids, target_ids, remaining, resets, start_state, section_params):
    rows, steps = char_ids.shape[:2]
    groups = lax.axis_size("dp")
    packed = section_params.shape[1]
    share = packed // groups
    n = rows * (steps + 1)

    ids = jnp.pad(
        char_ids.transpose(1, 0, 2), ((0, 1), (0, 0), (0, LANE - WORD_CHARS)), constant_values=-1
    ).reshape(n, LANE)
    km, e8, ab, ur, rt, wt = unpack_all(section_params)
    y2, *char_saved = char_forward_call(ids, km, e8, ab)
    feats, pres, total, emb = char_saved
    grad, dpre, late, xb, lhs, dz, dl, _, _, loss, bias = recurrent_call(
        y2, feats, pres, ab, ur, rt, wt, resets, target_ids, remaining.reshape(rows, 1), start_state
    )
    tiles3 = output_weights_call(xb, dl)
    summed3 = gather_sum_call(tiles3, groups, share)
    conv, early = char_backward_call(ids, grad, km, (total, emb), dpre)
    summed, small = finish_call(lhs, dz, dpre, (late, early), conv, bias, loss, summed3, groups, share)
    flat = pack_call(summed, summed3, groups, share)
    mean_loss = small[0, FW] / (groups * rows * steps)
    return mean_loss, flat.reshape(1, share), small[0, :FILT]


def solution(mesh):
    in_specs = (
        P("dp", None, None),
        P("dp", None),
        P("dp"),
        P("dp", None),
        P(None, None, "dp", None),
        P("section", None),
    )
    out_specs = (P(), P("section", "dp"), P())
    return jax.shard_map(shards, mesh=mesh, in_specs=in_specs, out_specs=out_specs, check_vma=False)
```

```python
import functools
import math

import jax
import jax.numpy as jnp
from jax import lax
from jax.experimental import pallas as pl
from jax.experimental.pallas import tpu as pltpu
from jax.sharding import PartitionSpec as P

D_CHAR = 15
CHAR_V = 51
F_UNIT = 50
WORD_CHARS = 21
HID = 650
VOCAB = 10000
FILT = 1100
F32 = jnp.float32
BF16 = jnp.bfloat16

NFILT = [F_UNIT * min(k, 4) for k in range(1, 8)]
COLS = [sum(NFILT[:k]) for k in range(8)]
KOFF = [CHAR_V * D_CHAR + sum((j * D_CHAR + 1) * NFILT[j - 1] for j in range(1, k)) for k in range(1, 9)]
CONV_END = KOFF[7]
HIGH_STRIDE = FILT * (FILT + 1)
FW = 1152
GW = 768
ZW = 4 * GW
VW = 10112
LANE = 128
LENS = (2304, 2688, 2688, 5120)


def roll_lanes(x, shift):
    return pltpu.roll(x, shift, 1)


def lanes(rows=8):
    return lax.broadcasted_iota(jnp.int32, (rows, LANE), 1)


def sublanes():
    return lax.broadcasted_iota(jnp.int32, (8, LANE), 0)


def widen(raw, slot, rows, wide):
    def body(i, carry):
        piece = raw[slot, 0:1, pl.ds(pl.multiple_of(i * 16384, 16384), 16384)]
        wide[pl.ds(pl.multiple_of(i * 128, 128), 128), :] = piece.astype(F32).reshape(128, LANE)
        return carry

    lax.fori_loop(0, rows // 128, body, 0)


DEPTH = 4


def stream_start(count, length, total, chunk_of, src, raw, sem):
    for i in range(DEPTH - 1):
        stream_copy(jnp.int32(i), length, total, chunk_of, src, raw, sem).start()


def stream_at(i, length, total, chunk_of):
    return jnp.minimum(chunk_of(i) // 8 * 8, total - length)


def stream_copy(i, length, total, chunk_of, src, raw, sem):
    at = pl.multiple_of(stream_at(i, length, total, chunk_of) * LANE, 8 * LANE)
    slot = lax.rem(i, DEPTH)
    return pltpu.make_async_copy(
        src.at[:, pl.ds(at, length * LANE)], raw.at[slot, :, pl.ds(0, length * LANE)], sem.at[slot]
    )


def stream_blocks(count, length, total, chunk_of, src, raw, sem, wide, work):
    def body(i, carry):
        @pl.when(i + DEPTH - 1 < count)
        def _():
            stream_copy(i + DEPTH - 1, length, total, chunk_of, src, raw, sem).start()

        stream_copy(i, length, total, chunk_of, src, raw, sem).wait()
        widen(raw, lax.rem(i, DEPTH), length, wide)
        work(i, chunk_of(i) - stream_at(i, length, total, chunk_of))
        return carry

    lax.fori_loop(0, count, body, 0)


def take_rows(wide, starts, tiles, cols, stride, put):
    step = max(6, 40 // len(starts))
    lane = lanes()
    for low in range(0, tiles, step):
        high = min(tiles, low + step)
        loaded = [
            [wide[pl.ds(first + c, 8, stride=stride), :] for c in range(low, high + 1)] for _, first, _, _ in starts
        ]
        results = []
        for (_, _, shift, keep_row), pieces in zip(starts, loaded):
            turn = lax.rem(LANE - shift, LANE)
            split = lane < LANE - shift
            turned = [roll_lanes(piece, turn) for piece in pieces]
            for c in range(low, high):
                out = jnp.where(split, turned[c - low], turned[c - low + 1])
                keep = keep_row
                if cols - c * LANE < LANE:
                    keep = keep & (lane < cols - c * LANE)
                results.append(jnp.where(keep, out, 0.0))
        at = 0
        for tag, _, _, _ in starts:
            for c in range(low, high):
                put(tag, c, results[at])
                at += 1


def spread(c, n, period):
    return pl.ds((c * period + n) * 25, 8, stride=3)


def collect(dest, c, period):
    return [
        dest[pl.ds((c * period + 8 * m) * 25 + 3 * j, 8, stride=25), :] for j in range(8) for m in range(period // 8)
    ]


def stage_tile(stage, slot, c, blocks):
    for i in range(0, len(blocks), 2):
        pair = jnp.concatenate([blocks[i], blocks[i + 1]], axis=0).astype(BF16)
        stage[slot, pl.ds(8 * i, 16), pl.ds(c * LANE, LANE)] = pair


def unpack_kernel(
    src, km, e8, ab, ur, rt, wt, raw, wide, dest, kstage, stage0, stage1, stage_t, stage3, raw_conv, sem_in, sem_out, sem_t
):
    role = lax.axis_index("section")
    total = src.shape[1] // LANE

    def out_copy(stage, slot, target):
        return pltpu.make_async_copy(stage.at[slot], target, sem_out.at[slot])

    @pl.when(role == 0)
    def _():
        blocks = 5
        count = 4 * blocks

        def flat_of(i):
            return CONV_END + HIGH_STRIDE * (i // blocks)

        def chunk_of(i):
            return flat_of(i) // LANE + 2200 * lax.rem(i, blocks)

        length = 640
        copy = pltpu.make_async_copy(src.at[:, pl.ds(0, length * LANE)], raw_conv.at[0], sem_t.at[0])
        copy.start()
        stream_start(count, LENS[0], total, chunk_of, src, raw, sem_in)
        copy.wait()
        widen(raw_conv, 0, length, wide)
        lane1 = lanes(1)
        dest[pl.ds(0, 64), :] = jnp.zeros((64, LANE), F32)
        for a in range(CHAR_V):
            flat = D_CHAR * a
            q, s = flat // LANE, flat % LANE
            here = wide[q : q + 1, :]
            out = roll_lanes(here, (LANE - s) % LANE) if s else here
            if s + D_CHAR > LANE:
                out = jnp.where(lane1 < LANE - s, out, roll_lanes(wide[q + 1 : q + 2, :], LANE - s))
            dest[a : a + 1, :] = jnp.where(lane1 < D_CHAR, out, jnp.where(lane1 == D_CHAR, 1.0, 0.0))
        table = dest[pl.ds(0, 64), :]
        for m in range(8):
            kstage[pl.ds(64 * m, 64), pl.ds(0, LANE)] = (
                pltpu.roll(table, 16 * m, 1) if m else table
            ).astype(BF16)
        copy = pltpu.make_async_copy(kstage.at[pl.ds(0, 512), pl.ds(0, LANE)], e8, sem_out.at[0])
        copy.start()
        copy.wait()
        tiles = FW // LANE
        rows = 112
        dest[pl.ds(0, rows * tiles), :] = jnp.zeros((rows * tiles, LANE), F32)

        def kernel_row(k, i, row):
            n, base = NFILT[k - 1], COLS[k - 1]
            edge = KOFF[k - 1] + n * i - base
            q, s = edge // LANE, edge % LANE
            for ct in range(base // LANE, (base + n - 1) // LANE + 1):
                out = wide[q + ct : q + ct + 1, :]
                if s:
                    after = roll_lanes(wide[q + ct + 1 : q + ct + 2, :], LANE - s)
                    out = jnp.where(lane1 < LANE - s, roll_lanes(out, LANE - s), after)
                at = ct * rows + row
                low, high = max(base - ct * LANE, 0), min(base + n - ct * LANE, LANE)
                if low > 0 or high < LANE:
                    out = jnp.where((lane1 >= low) & (lane1 < high), out, dest[at : at + 1, :])
                dest[at : at + 1, :] = out

        for k in range(1, 8):
            for i in range(k * D_CHAR):
                kernel_row(k, i, i + i // D_CHAR)
            kernel_row(k, k * D_CHAR, 15)
        kstage[...] = jnp.zeros_like(kstage)
        for ct in range(tiles):
            kstage[pl.ds(112, rows), pl.ds(ct * LANE, LANE)] = dest[pl.ds(ct * rows, rows), :].astype(BF16)
        copy = pltpu.make_async_copy(kstage.at[pl.ds(0, 368)], km, sem_out.at[0])
        copy.start()
        copy.wait()

        def target(i):
            return ab.at[i // blocks, pl.ds(pl.multiple_of(lax.rem(i, blocks) * 256, 256), 256)]

        def work(i, extra):
            block = lax.rem(i, blocks)
            inner = lax.rem(flat_of(i), LANE)

            def rows_of(i, carry):
                starts = []
                for n in range(4):
                    n = 4 * i + n
                    flat = inner + FILT * n
                    keep = 32 * (8 * block + sublanes()) + n <= FILT
                    starts.append((n, flat // LANE + extra, lax.rem(flat, LANE), keep))

                def put(n, c, value):
                    dest[spread(c, n, 32), :] = value

                take_rows(wide, starts, tiles, FILT, 275, put)
                return carry

            lax.fori_loop(0, 8, rows_of, 0)
            slot = lax.rem(i, 2)

            @pl.when(i >= 2)
            def _():
                out_copy(stage0, slot, target(i - 2)).wait()

            for c in range(tiles):
                stage_tile(stage0, slot, c, collect(dest, c, 32))
            out_copy(stage0, slot, target(i)).start()

        stream_blocks(count, LENS[0], total, chunk_of, src, raw, sem_in, wide, work)
        for i in (count - 2, count - 1):
            out_copy(stage0, i % 2, target(i)).wait()

    for layer in (1, 2):

        @pl.when(role == layer)
        def _(layer=layer):
            depth = FILT if layer == 1 else HID
            blocks = -(-depth // 128)
            recurrent = depth * 4 * HID
            count = blocks + 6

            def chunk_of(i):
                return jnp.where(i < blocks, 2600 * i, recurrent // LANE + 2600 * (i - blocks))

            stream_start(count, LENS[1], total, chunk_of, src, raw, sem_in)

            def target(i):
                at = jnp.where(i < blocks, i, i - blocks + 9)
                return ur.at[pl.ds(pl.multiple_of(at * 128, 128), 128)]

            def work(i, extra):
                inner = jnp.where(i < blocks, 0, recurrent % LANE)
                block = jnp.where(i < blocks, i, i - blocks)
                limit = jnp.where(i < blocks, depth, HID + 1)

                def rows_of(i, carry):
                    starts = []
                    for n in (2 * i, 2 * i + 1):
                        keep = 16 * (8 * block + sublanes()) + n < limit
                        for b in range(4):
                            flat = inner + 4 * HID * n + HID * b
                            starts.append(((n, b), flat // LANE + extra, lax.rem(flat, LANE), keep))

                    def put(tag, c, value):
                        dest[spread(6 * tag[1] + c, tag[0], 16), :] = value

                    take_rows(wide, starts, 6, HID, 325, put)
                    return carry

                lax.fori_loop(0, 8, rows_of, 0)
                slot = lax.rem(i, 2)

                @pl.when(i >= 2)
                def _():
                    out_copy(stage1, slot, target(i - 2)).wait()

                for c in range(24):
                    stage_tile(stage1, slot, c, collect(dest, c, 16))
                out_copy(stage1, slot, target(i)).start()

                @pl.when(i >= blocks)
                def _():
                    @pl.when(i >= blocks + 2)
                    def _():
                        turned_copy(i - 2).wait()

                    k = LANE * block + lanes(LANE)
                    for c in range(24):
                        turned = jnp.transpose(jnp.concatenate(collect(dest, c, 16), axis=0))
                        stage_t[slot, pl.ds(128 * c, 128), :] = jnp.where(k < HID, turned, 0.0).astype(BF16)
                    turned_copy(i).start()

            def turned_copy(i):
                slot = lax.rem(i, 2)
                at = pl.multiple_of((i - blocks) * LANE, LANE)
                return pltpu.make_async_copy(stage_t.at[slot], rt.at[:, pl.ds(at, LANE)], sem_t.at[slot])

            stream_blocks(count, LENS[1], total, chunk_of, src, raw, sem_in, wide, work)
            for i in (count - 2, count - 1):
                out_copy(stage1, i % 2, target(jnp.int32(i))).wait()
                turned_copy(jnp.int32(i)).wait()

    @pl.when(role == 3)
    def _():
        count = 11
        tiles = VW // LANE

        def chunk_of(i):
            return 5000 * i

        stream_start(count, LENS[3], total, chunk_of, src, raw, sem_in)

        def target(i):
            return wt.at[pl.ds(pl.multiple_of(i * 64, 64), 64)]

        def work(i, extra):
            def rows_of(n, carry):
                flat = VOCAB * n
                keep = 8 * (8 * i + sublanes()) + n < HID + 1

                def put(n, c, value):
                    dest[spread(c, n, 8), :] = value

                take_rows(wide, [(n, flat // LANE + extra, lax.rem(flat, LANE), keep)], tiles, VOCAB, 625, put)
                return carry

            lax.fori_loop(0, 8, rows_of, 0)
            slot = lax.rem(i, 2)

            @pl.when(i >= 2)
            def _():
                out_copy(stage3, slot, target(i - 2)).wait()

            for c in range(tiles):
                stage_tile(stage3, slot, c, collect(dest, c, 8))
            out_copy(stage3, slot, target(i)).start()

        stream_blocks(count, LENS[3], total, chunk_of, src, raw, sem_in, wide, work)
        for i in (count - 2, count - 1):
            out_copy(stage3, i % 2, target(jnp.int32(i))).wait()


def unpack_all(section_params):
    anywhere = pl.BlockSpec(memory_space=pl.ANY)
    return pl.pallas_call(
        unpack_kernel,
        out_shape=[
            jax.ShapeDtypeStruct((368, FW), BF16),
            jax.ShapeDtypeStruct((512, LANE), BF16),
            jax.ShapeDtypeStruct((4, 1280, FW), BF16),
            jax.ShapeDtypeStruct((15 * 128, ZW), BF16),
            jax.ShapeDtypeStruct((ZW, GW), BF16),
            jax.ShapeDtypeStruct((11 * 64, VW), BF16),
        ],
        in_specs=[anywhere],
        out_specs=[anywhere] * 6,
        scratch_shapes=[
            pltpu.VMEM((DEPTH, 1, LENS[3] * LANE), BF16),
            pltpu.VMEM((9312, LANE), F32),
            pltpu.VMEM((79 * 200, LANE), F32),
            pltpu.VMEM((512, FW), BF16),
            pltpu.VMEM((2, 256, FW), BF16),
            pltpu.VMEM((2, 128, ZW), BF16),
            pltpu.VMEM((2, ZW, LANE), BF16),
            pltpu.VMEM((2, 64, VW), BF16),
            pltpu.VMEM((1, 1, 640 * LANE), BF16),
            pltpu.SemaphoreType.DMA((DEPTH,)),
            pltpu.SemaphoreType.DMA((2,)),
            pltpu.SemaphoreType.DMA((2,)),
        ],
        compiler_params=pltpu.CompilerParams(vmem_limit_bytes=56 << 20),
        name="unpack",
    )(section_params)


def fblocks(width, step=256):
    return [(at, min(step, width - at)) for at in range(0, width, step)]


def mm(a, b):
    return jnp.dot(a, b, preferred_element_type=F32)


def mm_tn(a, b):
    return lax.dot_general(a, b, (((0,), (0,)), ((), ())), preferred_element_type=F32)


def mm_nt(a, b):
    return lax.dot_general(a, b, (((1,), (1,)), ((), ())), preferred_element_type=F32)


def sigmoid(x):
    return 0.5 * jnp.tanh(0.5 * x) + 0.5


def load(pairs, sem):
    copies = [pltpu.make_async_copy(a, b, sem.at[i]) for i, (a, b) in enumerate(pairs)]
    for copy in copies:
        copy.start()
    for copy in copies:
        copy.wait()


def column_mask(at, width, limit, rows):
    return lax.broadcasted_iota(jnp.int32, (rows, width), 1) + at < limit


def char_onehot(ids, t):
    rows = ids.shape[0]
    lane = lanes(rows)
    pieces = []
    for pair in range(4):
        j = 8 * t + 2 * pair
        left = ids[:, j : j + 1]
        right = ids[:, j + 1 : j + 2]
        hit = jnp.where(lane < 64, left, right) == lax.rem(lane, 64)
        pieces.append(jnp.where(hit, 1.0, 0.0).astype(BF16))
    return jnp.concatenate(pieces, axis=1)


def conv_steps(body):
    def step(p, carry):
        body(p, p // 8, True, lax.rem(p, 8), FILT)
        return carry

    lax.fori_loop(0, 15, step, 0)
    body(15, 1, True, 7, COLS[6])
    for p in range(16, WORD_CHARS):
        body(p, 2, False, p - 16, COLS[WORD_CHARS - p])


def conv_at(emb, km, tile, second, within, at, width):
    first = 112 - 16 * within
    if not isinstance(first, int):
        first = pl.multiple_of(first, 16)
    if second:
        window = jnp.concatenate([emb[tile], emb[tile + 1]], axis=1)
    else:
        window = emb[tile]
    return mm(window, km[pl.ds(first, window.shape[1]), pl.ds(at, width)])


def char_forward(ids, e8, km, ab, emb, total, feats, pres, out):
    rows = ids.shape[0]
    for t in range(3):
        emb[t] = mm(char_onehot(ids, t), e8[...]).astype(BF16)
    total[...] = jnp.zeros_like(total)

    def step(p, tile, second, within, limit):
        for at, width in fblocks(FW):
            if at >= limit:
                continue
            value = jnp.exp(jnp.tanh(conv_at(emb, km, tile, second, within, at, width)))
            if at + width > limit and limit < FILT:
                value = jnp.where(column_mask(at, width, limit, rows), value, 0.0)
            total[:, pl.ds(at, width)] += value

    conv_steps(step)
    for at, width in fblocks(FW):
        col = lax.broadcasted_iota(jnp.int32, (rows, width), 1) + at
        count = jnp.full((rows, width), float(WORD_CHARS), F32)
        for k in range(1, 7):
            count = jnp.where(col >= COLS[k], float(WORD_CHARS - k), count)
        value = jnp.log(total[:, pl.ds(at, width)]) - jnp.log(count)
        value = jnp.where(col < FILT, value, jnp.where(col == FILT, 1.0, 0.0))
        feats[0, :, pl.ds(at, width)] = value.astype(BF16)
    for layer in range(2):
        for at, width in fblocks(FW):
            cols = pl.ds(at, width)
            t_pre = mm(feats[layer], ab[2 * layer, pl.ds(0, FW), cols])
            h_pre = mm(feats[layer], ab[2 * layer + 1, pl.ds(0, FW), cols])
            pres[2 * layer, :, cols] = t_pre
            pres[2 * layer + 1, :, cols] = h_pre
            gate = sigmoid(t_pre)
            y = feats[layer, :, cols].astype(F32)
            value = gate * (h_pre * sigmoid(h_pre)) + (1.0 - gate) * y
            col = lax.broadcasted_iota(jnp.int32, (rows, width), 1) + at
            if layer == 0:
                value = jnp.where(col < FILT, value, jnp.where(col == FILT, 1.0, 0.0))
                feats[1, :, cols] = value.astype(BF16)
            else:
                out[:, cols] = jnp.where(col < FILT, value, 0.0).astype(BF16)


def conv_backward(km, kt, emb, emb_t, total, grad, dk, demb, relay):
    rows = grad.shape[0]
    kt[...] = jnp.transpose(km[pl.ds(112, LANE), :])
    for t in range(3):
        emb_t[pl.ds(LANE * t, LANE), :] = jnp.transpose(emb[t])
    emb_t[pl.ds(3 * LANE, LANE), :] = jnp.zeros((LANE, rows), BF16)
    dk[...] = jnp.zeros_like(dk)
    demb[...] = jnp.zeros_like(demb)
    for at, width in fblocks(FW):
        cols = pl.ds(at, width)
        grad[:, cols] = grad[:, cols] / total[:, cols]

    def step(p, tile, second, within, limit):
        relay(p)
        window_t = emb_t[pl.ds(p * 16 if isinstance(p, int) else pl.multiple_of(p * 16, 16), LANE), :]
        back = jnp.zeros((rows, LANE), F32)
        for at, width in fblocks(FW):
            if at >= limit:
                continue
            cols = pl.ds(at, width)
            act = jnp.tanh(conv_at(emb, km, tile, second, within, at, width))
            dz = grad[:, cols] * jnp.exp(act) * (1.0 - act * act)
            if at + width > limit and limit < FILT:
                dz = jnp.where(column_mask(at, width, limit, rows), dz, 0.0)
            dz = dz.astype(BF16)
            dk[:, cols] += mm(window_t, dz)
            back = back + mm(dz, kt[cols, :])
        lane = lanes(rows)
        back = jnp.where(lane < 112, back, 0.0)
        turned = pltpu.roll(back, 16 * within, 1)
        demb[tile] += jnp.where(lane >= 16 * within, turned, 0.0)
        if second:
            demb[tile + 1] += jnp.where(lane < 16 * within, turned, 0.0)

    conv_steps(step)


def table_backward(ids, demb, table):
    acc = jnp.zeros((64, LANE), F32)
    for t in range(3):
        hot = char_onehot(ids, t)
        value = demb[t]
        high = value.astype(BF16)
        low = (value - high.astype(F32)).astype(BF16)
        grads = mm_tn(hot, high) + mm_tn(hot, low)
        for m in range(8):
            block = grads[64 * m : 64 * m + 64, :]
            acc = acc + (pltpu.roll(block, LANE - 16 * m, 1) if m else block)
    table[...] = acc


def tile_rows(stage, base, value, row_tiles, col_tiles, first_col=0, pitch=None):
    pitch = col_tiles if pitch is None else pitch
    for r in range(row_tiles):
        for c in range(col_tiles):
            stage[base + r * pitch + first_col + c] = value[16 * r : 16 * r + 16, LANE * c : LANE * c + LANE].astype(BF16)


def six(x):
    return jnp.concatenate([x] * 6, axis=1)


ANYWHERE = pl.BlockSpec(memory_space=pl.ANY)
ON_CHIP = pl.BlockSpec(memory_space=pltpu.VMEM)
LIMIT = 56 << 20


def call(kernel, name, ins, specs, outs, scratch, aliases=None):
    return pl.pallas_call(
        kernel,
        out_shape=[jax.ShapeDtypeStruct(shape, dtype) for shape, dtype in outs],
        in_specs=specs,
        out_specs=[ANYWHERE] * len(outs),
        scratch_shapes=scratch,
        input_output_aliases=aliases or {},
        compiler_params=pltpu.CompilerParams(vmem_limit_bytes=LIMIT),
        name=name,
    )(*ins)


def vmem(shape, dtype):
    return pltpu.VMEM(shape, dtype)


def dmas(count):
    return pltpu.SemaphoreType.DMA((count,))


def char_forward_call(ids, km, e8, ab):
    n = ids.shape[0]

    def kernel(ids, km, e8, ab, y2_o, feats_o, pres_o, total_o, emb_o, km_v, e8_v, ab_v, y2, feats, pres, total, emb, sem):
        @pl.when(lax.axis_index("section") == 0)
        def _():
            load([(km, km_v), (e8, e8_v), (ab, ab_v)], sem)
            char_forward(ids, e8_v, km_v, ab_v, emb, total, feats, pres, y2)
            load([(y2, y2_o), (feats, feats_o), (pres, pres_o), (total, total_o), (emb, emb_o)], sem)

    outs = [
        ((n, FW), BF16),
        ((2, n, FW), BF16),
        ((4, n, FW), F32),
        ((n, FW), F32),
        ((3, n, LANE), BF16),
    ]
    scratch = [vmem(km.shape, BF16), vmem(e8.shape, BF16), vmem(ab.shape, BF16)]
    scratch += [vmem(shape, dtype) for shape, dtype in outs] + [dmas(5)]
    return call(kernel, "char_forward", (ids, km, e8, ab), [ON_CHIP] + [ANYWHERE] * 3, outs, scratch)


def char_backward_call(ids, grad, km, saved, dpre):
    n = ids.shape[0]
    total, emb = saved
    rows = SPLIT * CHUNK
    sems = pltpu.SemaphoreType.DMA

    def kernel(
        ids, grad, km, total, emb, dpre, tiles_o, right_o,
        grad_v, km_v, total_v, emb_v, kt, emb_t, dk, demb, table, stage, sem, send, recv,
    ):
        me = lax.axis_index("dp")

        def right_copy(k, i):
            span = pl.ds(pl.multiple_of(i * CHUNK, CHUNK), CHUNK)
            source = right_o.at[1, span] if k == 3 else dpre.at[span]
            return pltpu.make_async_remote_copy(
                source, right_o.at[k - 1, span], send.at[k - 1, i], recv.at[k - 1, i],
                device_id={"dp": quad_peer(me, 1 if k == 3 else k)}, device_id_type=pl.DeviceIdType.MESH,
            )

        def relay(p):
            if isinstance(p, int):
                return
            i = p // 3 - 1

            @pl.when((lax.rem(p, 3) == 0) & (p > 0) & (i < SPLIT))
            def _():
                right_copy(2, i).wait_recv()
                right_copy(3, i).start()

        @pl.when(lax.axis_index("section") == 0)
        def _():
            barrier = pltpu.get_barrier_semaphore()
            for k in range(1, QUAD):
                pl.semaphore_signal(
                    barrier, inc=1, device_id={"dp": quad_peer(me, k)}, device_id_type=pl.DeviceIdType.MESH
                )
            pl.semaphore_wait(barrier, QUAD - 1)
            for i in range(SPLIT):
                right_copy(2, i).start()
                right_copy(1, i).start()
            load([(grad, grad_v), (km, km_v), (total, total_v), (emb, emb_v)], sem)
            conv_backward(km_v, kt, emb_v, emb_t, total_v, grad_v, dk, demb, relay)
            table_backward(ids, demb, table)
            tile_rows(stage, 0, dk[...], 8, 9)
            tile_rows(stage, 72, table[...], 4, 1)
            load([(stage, tiles_o)], sem)
            for i in range(SPLIT):
                for k in range(1, QUAD):
                    right_copy(k, i).wait_send()
                    if k != 2:
                        right_copy(k, i).wait_recv()

    outs = [((CONV_TILES, 16, LANE), BF16), ((QUAD - 1, rows, 4 * FW), BF16)]
    scratch = [
        vmem((n, FW), F32), vmem(km.shape, BF16), vmem(total.shape, F32), vmem(emb.shape, BF16),
        vmem((FW, LANE), BF16), vmem((4 * LANE, n), BF16), vmem((LANE, FW), F32), vmem((3, n, LANE), F32),
        vmem((64, LANE), F32), vmem((CONV_TILES, 16, LANE), BF16), dmas(4), sems((QUAD - 1, SPLIT)), sems((QUAD - 1, SPLIT)),
    ]
    return pl.pallas_call(
        kernel,
        out_shape=[jax.ShapeDtypeStruct(shape, dtype) for shape, dtype in outs],
        in_specs=[ON_CHIP] + [ANYWHERE] * 5,
        out_specs=[ANYWHERE] * 2,
        scratch_shapes=scratch,
        compiler_params=pltpu.CompilerParams(vmem_limit_bytes=LIMIT, collective_id=4, has_side_effects=True),
        name="char_backward",
    )(ids, grad, km, total, emb, dpre)


CONV_TILES = 76
TILES = 3648


def turned_tile(left, right, shift):
    rows = right.shape[0]
    if shift:
        mixed = jnp.where(
            lanes(rows) < shift, pltpu.roll(left.astype(F32), shift, 1), pltpu.roll(right.astype(F32), shift, 1)
        )
        right = mixed.astype(BF16)
    return jnp.transpose(right)


def each_vocab(body, step=2048):
    whole = VW // step

    def one(i, carry):
        body(pl.multiple_of(i * step, step), step)
        return carry

    lax.fori_loop(0, whole, one, 0)
    body(whole * step, VW - whole * step)


def output_weights_call(h, dl):
    n = h.shape[0]
    rows = 704
    pitch = VW // LANE

    def kernel(h, dl, tiles_o, h_v, dl_v, h_t, stage, sem):
        @pl.when(lax.axis_index("section") == 3)
        def _():
            load([(h, h_v), (dl, dl_v)], sem)
            lane = lanes(n)
            for c in range(6):
                value = h_v[:, pl.ds(LANE * c, LANE)].astype(F32)
                value = jnp.where(lane + c * LANE == HID, 1.0, value).astype(BF16)
                h_t[pl.ds(LANE * c, LANE), :] = jnp.transpose(value)

            def body(at, width):
                first = at // LANE
                for top, count in fblocks(rows):
                    value = mm(h_t[pl.ds(top, count), :], dl_v[:, pl.ds(at, width)])
                    for r in range(count // 16):
                        for c in range(width // LANE):
                            stage[(top // 16 + r) * pitch + first + c] = value[
                                16 * r : 16 * r + 16, LANE * c : LANE * c + LANE
                            ].astype(BF16)

            each_vocab(body, 256)
            count = rows // 16 * pitch
            load([(stage.at[pl.ds(0, count)], tiles_o.at[pl.ds(0, count)])], sem)

    scratch = [
        vmem((n, GW), BF16), vmem((n, VW), BF16), vmem((6 * LANE, n), BF16),
        vmem((rows // 16 * pitch, 16, LANE), BF16), dmas(2),
    ]
    return call(
        kernel, "output_weights", (h, dl), [ANYWHERE] * 2, [((TILES, 16, LANE), BF16)], scratch
    )[0]


CHUNK = 32
GROUPS_OUT = (3, 3, 2, 1)


def lstm_steps(first, count, keep, carry, r, gates, cells, prevs, hiddens):
    def step(s, carry):
        h, c = carry
        at = pl.ds(pl.multiple_of((first + s) * 8, 8), 8)
        k = six(keep[at, :])
        hp = h * k
        cp = c * k
        prevs[at, :] = hp
        z = gates[at, :] + mm(hp.astype(BF16), r[...])
        i = sigmoid(z[:, 0:GW])
        f = sigmoid(z[:, GW : 2 * GW])
        o = sigmoid(z[:, 2 * GW : 3 * GW])
        g = jnp.tanh(z[:, 3 * GW :])
        c = f * cp + i * g
        h = (o * jnp.tanh(c)).astype(BF16).astype(F32)
        gates[at, :] = jnp.concatenate([i, f, o, g], axis=1)
        cells[at, :] = c
        hiddens[at, :] = h
        return h, c

    return lax.fori_loop(0, count, step, carry)


def lstm_back_steps(first, count, keep, c0, carry, rt, gates, cells, dhs):
    def step(s, carry):
        dh_next, dc_next = carry
        t = first + count - 1 - s
        at = pl.ds(pl.multiple_of(t * 8, 8), 8)
        before = pl.ds(pl.multiple_of(jnp.maximum(t - 1, 0) * 8, 8), 8)
        k = six(keep[at, :])
        saved = gates[at, :]
        i, f, o, g = [saved[:, GW * b : GW * b + GW] for b in range(4)]
        cp = jnp.where(t > 0, cells[before, :], c0[...]) * k
        ct = jnp.tanh(cells[at, :])
        dh = dhs[at, :] + dh_next
        dc = dc_next + dh * o * (1.0 - ct * ct)
        dz = jnp.concatenate(
            [dc * g * i * (1.0 - i), dc * cp * f * (1.0 - f), dh * ct * o * (1.0 - o), dc * i * (1.0 - g * g)], axis=1
        ).astype(BF16)
        gates[at, :] = dz.astype(F32)
        return k * mm(dz, rt[...]), k * dc * f

    return lax.fori_loop(0, count, step, carry)


def output_rows(first, count, h, w, targets, valid, logits, dl, top, part, dh, loss, dh16):
    at_rows = pl.ds(first, count)
    depth = w.shape[0]
    own = pl.ds(0, count)
    top[own, :] = jnp.full((count, LANE), -jnp.inf, F32)

    def forward(at, width):
        z = mm(h[at_rows, pl.ds(0, depth)], w[:, pl.ds(at, width)])
        if isinstance(at, int):
            z = jnp.where(column_mask(at, width, VOCAB, count), z, -jnp.inf)
        logits[own, pl.ds(at, width)] = z
        best = top[own, :]
        for c in range(width // LANE):
            best = jnp.maximum(best, z[:, LANE * c : LANE * c + LANE])
        top[own, :] = best

    each_vocab(forward)
    best = jnp.max(top[own, :], axis=1, keepdims=True)
    part[:, own, :] = jnp.zeros((2, count, LANE), F32)
    wanted = targets[at_rows, :]

    def exponents(at, width):
        z = logits[own, pl.ds(at, width)]
        e = jnp.exp(z - best)
        logits[own, pl.ds(at, width)] = e
        for c in range(width // LANE):
            part[0, own, :] += e[:, LANE * c : LANE * c + LANE]
            hit = lanes(count) + (at + LANE * c) == wanted
            part[1, own, :] += jnp.where(hit, z[:, LANE * c : LANE * c + LANE], 0.0)

    each_vocab(exponents)
    total = jnp.sum(part[0, own, :], axis=1, keepdims=True)
    picked = jnp.sum(part[1, own, :], axis=1, keepdims=True)
    counts = valid[at_rows, :]
    loss[...] += jnp.sum(counts * (best + jnp.log(total) - picked), axis=0, keepdims=True)
    share = counts / total
    dh[:, own] = jnp.zeros((depth, count), F32)

    def backward(at, width):
        e = logits[own, pl.ds(at, width)]
        pieces = []
        for c in range(width // LANE):
            hit = lanes(count) + (at + LANE * c) == wanted
            grad = e[:, LANE * c : LANE * c + LANE] * share - jnp.where(hit, counts, 0.0)
            pieces.append(grad.astype(BF16))
        grad = jnp.concatenate(pieces, axis=1)
        dl[at_rows, pl.ds(at, width)] = grad
        dh[:, own] += mm_nt(w[:, pl.ds(at, width)], grad)

    each_vocab(backward)
    for at, width in fblocks(depth):
        value = jnp.transpose(dh[pl.ds(at, width), own])
        dh16[at_rows, pl.ds(at, width)] = jnp.where(column_mask(at, width, HID, count), value, 0.0).astype(BF16)


QUAD = 4
LEFT0 = 35 * LANE
LEFT1 = 14 * LANE
LEFT2 = 11 * LANE
LEFT_ROOM = 41 * LANE


def quad_peer(me, k):
    place = lax.rem(me, QUAD)
    pair, side = place // 2, lax.rem(place, 2)
    return me + (k % 2) * (1 - 2 * side) + (k // 2) * (2 - 4 * pair)


def turn_features(feats, turned):
    n = feats.shape[1]
    zero = jnp.zeros((n, LANE), BF16)
    for segment in range(4):
        start = segment * (FILT + 1)
        shift, first, last = start % LANE, start // LANE, (start + FILT) // LANE
        for c in range(last - first + 1):
            left = feats[segment // 2, :, pl.ds(LANE * (c - 1), LANE)] if c > 0 else zero
            right = feats[segment // 2, :, pl.ds(LANE * c, LANE)] if c < 9 else zero
            tile = turned_tile(left, right, shift)
            at = pl.ds(LANE * (first + c), LANE)
            if c == 0 and segment > 0:
                tile = tile + turned[at, :]
            turned[at, :] = tile


def turn_inputs(x, prevs, depth, turned):
    n = prevs.shape[0]
    first, shift = depth // LANE, depth % LANE
    end = depth + HID
    zero = jnp.zeros((n, LANE), F32)
    lane = lanes(n)
    for c in range(end // LANE + 1):
        if c < first:
            mixed = x[:, pl.ds(LANE * c, LANE)]
        else:
            k = c - first
            left = prevs[:, pl.ds(LANE * (k - 1), LANE)].astype(F32) if 0 < k < 7 else zero
            right = prevs[:, pl.ds(LANE * k, LANE)].astype(F32) if k < 6 else zero
            before = pltpu.roll(left, shift, 1) if k else x[:, pl.ds(LANE * c, LANE)].astype(F32)
            mixed = jnp.where(lane < shift, before, pltpu.roll(right, shift, 1))
            mixed = jnp.where(lane + c * LANE == end, 1.0, mixed).astype(BF16)
        turned[pl.ds(LANE * c, LANE), :] = jnp.transpose(mixed)


SPLIT = 3
AB_PARTS = ((0, 640), (640, 512))


def highway_chunk(rows, slot, dy, feats, pres, grad, dpre, w):
    def cut(m, at, width):
        return pl.ds(m * FW + at, width)

    for at, width in fblocks(FW):
        grad[rows, pl.ds(at, width)] = dy[rows, pl.ds(at, width)].astype(F32)
    for layer in (1, 0):
        own = pl.ds(slot, CHUNK)
        for at, width in fblocks(FW):
            cols = pl.ds(at, width)
            g = grad[rows, cols]
            gate = sigmoid(pres[own, cut(2 * layer, at, width)])
            q = pres[own, cut(2 * layer + 1, at, width)]
            sig = sigmoid(q)
            y = feats[layer, rows, cols].astype(F32)
            dpre[rows, cut(2 * layer, at, width)] = (g * (q * sig - y) * gate * (1.0 - gate)).astype(BF16)
            dpre[rows, cut(2 * layer + 1, at, width)] = (g * gate * sig * (1.0 + q * (1.0 - sig))).astype(BF16)
            grad[rows, cols] = g * (1.0 - gate)
        turned = [jnp.transpose(dpre[rows, cut(2 * layer + i, 0, FW)]) for i in range(2)]
        for half, (row, count) in enumerate(AB_PARTS):
            for at, width in fblocks(count):
                cols = pl.ds(row + at, width)
                back = jnp.zeros((width, CHUNK), F32)
                for i in range(2):
                    part = w[pl.ds(at, width), pl.ds((2 * (2 * layer + i) + half) * FW, FW)]
                    back = back + mm(part, turned[i])
                value = grad[rows, cols] + jnp.transpose(back)
                if row + at + width > FILT:
                    value = jnp.where(column_mask(row + at, width, FILT, CHUNK), value, 0.0)
                grad[rows, cols] = value


def recurrent_call(y2, feats, pres, ab, ur, rt, wt, resets, target_ids, remaining, state):
    n = y2.shape[0]
    real_steps = resets.shape[1]
    chunks = n // CHUNK
    steps = CHUNK // 8
    depth_w = wt.shape[0]
    MESH = pl.DeviceIdType.MESH

    def kernel(
        y2, feats, pres, ab, ur, rt, wt, resets, target_ids, remaining, state,
        grad_o, dpre_o, right_o, xb_o, lhs_o, dz_o, dl_o, x_q, h_q, loss_o, bias_o,
        keep, valid, targets, feats_v, turned, pb, x1, xb, hb, db, ob, dy, u, r, r_t, w, start, gates, cells, prevs, hs, dhs, dz16,
        logits, dl, top, part, dh, loss,
        sem_in, sem_out, send_y, recv_y, send_f, recv_f, send_b, recv_b, send_d, recv_d,
        send_x, recv_x, send_h, recv_h, send_z, recv_z, sem_l, sem_p, send_g, recv_g,
    ):
        role = lax.axis_index("section")
        me = lax.axis_index("dp")
        loss[...] = jnp.zeros_like(loss)
        bias_o[...] = jnp.zeros_like(bias_o)

        def to(step, source, target, send, recv):
            return pltpu.make_async_remote_copy(
                source, target, send, recv, device_id={"section": role + step}, device_id_type=MESH
            )

        def span(c):
            return pl.ds(pl.multiple_of(c * CHUNK, CHUNK), CHUNK)

        def forward_copy(c, step):
            return to(step, hb.at[span(c)], xb.at[span(c)], send_f.at[c], recv_f.at[c])

        def backward_copy(c, step):
            return to(step, ob.at[span(c)], db.at[span(c)], send_b.at[c], recv_b.at[c])

        def feature_copy(step):
            return to(step, y2, x1, send_y.at[0], recv_y.at[0])

        def last_copy(c, step):
            return to(step, dy.at[span(c)], dy.at[span(c)], send_d.at[c], recv_d.at[c])

        def quad_copy(source, target, send, recv, k):
            return pltpu.make_async_remote_copy(
                source, target, send, recv, device_id={"dp": quad_peer(me, k)}, device_id_type=MESH
            )

        def input_copy(k):
            return quad_copy(x1, x_q.at[k - 1, 0], send_x.at[k - 1, 0], recv_x.at[k - 1, 0], k)

        def layer_copy(k):
            return quad_copy(
                xb, x_q.at[k - 1, 0, :, pl.ds(0, GW)], send_x.at[k - 1, 0], recv_x.at[k - 1, 0], k
            )

        def feats_copy(k):
            return quad_copy(feats_v, x_q.at[k - 1], send_x.at[k - 1, 0], recv_x.at[k - 1, 0], k)

        def hidden_copy(k):
            return quad_copy(pb, h_q.at[k - 1], send_h.at[k - 1, 0], recv_h.at[k - 1, 0], k)

        def each_peer(body):
            for k in range(1, QUAD):
                body(k)

        def each_chunk(body, first=0):
            def step(c, carry):
                body(c)
                return carry

            lax.fori_loop(first, chunks, step, 0)

        def turned_out(g, rows):
            copy = pltpu.make_async_copy(turned.at[pl.ds(0, rows)], lhs_o.at[g, pl.ds(0, rows)], sem_l.at[0])
            copy.start()
            copy.wait()

        def fetch(source, target):
            copy = pltpu.make_async_copy(source, target, sem_l.at[1])
            copy.start()
            copy.wait()

        def dpre_copy(c, k):
            rows = pl.ds(pl.multiple_of((c - SPLIT) * CHUNK, CHUNK), CHUNK)
            source = right_o.at[1, rows] if k == 3 else dl.at[span(c), pl.ds(0, 4 * FW)]
            return quad_copy(
                source, right_o.at[k - 1, rows], send_z.at[k - 1, c], recv_z.at[k - 1, c], 1 if k == 3 else k
            )

        def right_copy(k):
            return quad_copy(dz16, dz_o.at[k - 1], send_z.at[k - 1, 0], recv_z.at[k - 1, 0], k)

        def hand_copy(c, step):
            return to(step, dz16.at[span(c)], dz16.at[span(c)], send_g.at[c], recv_g.at[c])

        def handed_copy(c, k):
            return pltpu.make_async_remote_copy(
                dz16.at[span(c)], dz_o.at[k - 1, span(c)], send_h.at[k - 1, c], recv_z.at[k - 1, c],
                device_id={"dp": quad_peer(me, k), "section": 1}, device_id_type=MESH,
            )

        def exchange(copy, c, first):
            @pl.when(c >= first)
            def _():
                copy(c, 2).start()
                copy(c, 1).start()

            @pl.when((c < chunks - 1) & (c + 1 >= first))
            def _():
                copy(c + 1, 2).wait_recv()
                copy(c + 1, 3).start()

        def exchanged(copy, first):
            if first == 0:
                copy(0, 2).wait_recv()
                copy(0, 3).start()

            def settle(c):
                for k in range(1, QUAD):
                    copy(c, k).wait_send()
                    if k != 2:
                        copy(c, k).wait_recv()

            each_chunk(settle, first)

        def inputs(which):
            if which == 0:
                pairs = [(feats, feats_v)]
                for m in range(4):
                    for half, (row, count) in enumerate(AB_PARTS):
                        target = w.at[pl.ds(0, count), pl.ds((2 * m + half) * FW, FW)]
                        pairs.append((ab.at[m, pl.ds(row, count)], target))
            elif which == 3:
                pairs = [(wt, w)]
            else:
                depth = FW if which == 1 else GW
                pairs = [
                    (ur.at[pl.ds(0, depth)], u.at[pl.ds(0, depth)]),
                    (ur.at[pl.ds(FW, GW)], r),
                    (rt, r_t),
                ]
            return [pltpu.make_async_copy(a, b, sem_in.at[i]) for i, (a, b) in enumerate(pairs)]

        for which in range(4):

            @pl.when(role == which)
            def _(which=which):
                for copy in inputs(which):
                    copy.start()

        @pl.when((role == 1) | (role == 2))
        def _():
            start[...] = jnp.zeros_like(start)
            for which in (1, 2):

                @pl.when(role == which)
                def _(which=which):
                    for half in range(2):
                        start[half, :, pl.ds(0, HID)] = state[which - 1, half]

            for t in range(n // 8):
                rows = pl.ds(8 * t, 8)
                kept = jnp.zeros((8, LANE), F32)
                if t < real_steps:
                    kept = 1.0 - jnp.broadcast_to(resets[:, t : t + 1], (8, LANE)).astype(F32)
                keep[rows, :] = kept

        @pl.when(role == 3)
        def _():
            left_words = jnp.broadcast_to(remaining[...], (8, LANE))
            for t in range(n // 8):
                rows = pl.ds(8 * t, 8)
                if t < real_steps:
                    valid[rows, :] = jnp.where(left_words > t, 1.0, 0.0)
                    targets[rows, :] = jnp.broadcast_to(target_ids[:, t : t + 1], (8, LANE))
                else:
                    valid[rows, :] = jnp.zeros((8, LANE), F32)
                    targets[rows, :] = jnp.full((8, LANE), -1, jnp.int32)

        barrier = pltpu.get_barrier_semaphore()

        @pl.when(role > 0)
        def _():
            pl.semaphore_signal(barrier, inc=1, device_id={"section": role - 1}, device_id_type=MESH)

        @pl.when(role < 3)
        def _():
            pl.semaphore_signal(barrier, inc=1, device_id={"section": role + 1}, device_id_type=MESH)

        for k in range(1, QUAD):
            pl.semaphore_signal(barrier, inc=1, device_id={"dp": quad_peer(me, k)}, device_id_type=MESH)

        @pl.when(role == 1)
        def _():
            for k in range(1, QUAD):
                pl.semaphore_signal(
                    barrier, inc=1, device_id={"dp": quad_peer(me, k), "section": 0}, device_id_type=MESH
                )

        handed = (QUAD - 1) * lax.max(1 - role, 0)
        pl.semaphore_wait(barrier, lax.min(role, 1) + lax.min(3 - role, 1) + QUAD - 1 + handed)

        @pl.when(role == 0)
        def _():
            feature_copy(1).start()
            for copy in inputs(0):
                copy.wait()
            each_peer(lambda k: feats_copy(k).start())
            turn_features(feats_v, turned)
            turned_out(QUAD - 1, LEFT0)
            feature_copy(1).wait_send()
            each_peer(lambda k: feats_copy(k).wait_send())
            for k in range(1, QUAD):
                feats_copy(k).wait_recv()
                fetch(x_q.at[k - 1], feats_v)
                turn_features(feats_v, turned)
                turned_out(k - 1, LEFT0)
            fetch(feats, feats_v)

            def pres_copy(c, m):
                slot = lax.rem(c, 2)
                target = logits.at[pl.ds(pl.multiple_of(slot * CHUNK, CHUNK), CHUNK), pl.ds(m * FW, FW)]
                return pltpu.make_async_copy(pres.at[m, span(c)], target, sem_p.at[slot, m])

            for m in range(4):
                pres_copy(chunks - 1, m).start()

            def chunk(i, carry):
                c = chunks - 1 - i

                @pl.when(c > 0)
                def _():
                    for m in range(4):
                        pres_copy(c - 1, m).start()

                for m in range(4):
                    pres_copy(c, m).wait()
                hand_copy(c, 1).wait_recv()
                each_peer(lambda k: handed_copy(c, k).start())
                last_copy(c, 1).wait_recv()
                highway_chunk(span(c), pl.multiple_of(lax.rem(c, 2) * CHUNK, CHUNK), dy, feats_v, logits, gates, dl, w)

                exchange(dpre_copy, c, SPLIT)
                return carry

            lax.fori_loop(0, chunks, chunk, 0)
            copies = [
                pltpu.make_async_copy(gates.at[:, pl.ds(0, FW)], grad_o, sem_out.at[0]),
                pltpu.make_async_copy(dl.at[:, pl.ds(0, 4 * FW)], dpre_o, sem_out.at[1]),
            ]
            for copy in copies:
                copy.start()
            for at, width in fblocks(FW):
                cols = pl.ds(at, width)
                bias_o[:, cols] = jnp.sum(dl[:, cols].astype(F32), axis=0, keepdims=True)
            for copy in copies:
                copy.wait()

            exchanged(dpre_copy, SPLIT)
            each_chunk(lambda c: each_peer(lambda k: handed_copy(c, k).wait_send()))

        @pl.when((role == 1) | (role == 2))
        def _():
            for which in (1, 2):

                @pl.when(role == which)
                def _(which=which):
                    for copy in inputs(which):
                        copy.wait()

            bias = r[pl.ds(HID, 1), :].astype(F32)

            @pl.when(role == 1)
            def _():
                feature_copy(-1).wait_recv()
                for at, width in fblocks(ZW):
                    cols = pl.ds(at, width)
                    gates[:, cols] = mm(x1[...], u[:, cols]) + bias[:, at : at + width]

            def chunk_forward(c, carry):
                @pl.when(role == 2)
                def _():
                    forward_copy(c, -1).wait_recv()
                    for at, width in fblocks(ZW):
                        cols = pl.ds(at, width)
                        gates[span(c), cols] = mm(xb[span(c), :], u[pl.ds(0, GW), cols]) + bias[:, at : at + width]

                carry = lstm_steps(c * steps, steps, keep, carry, r, gates, cells, prevs, hs)
                hb[span(c), :] = hs[span(c), :].astype(BF16)
                forward_copy(c, 1).start()
                return carry

            h0 = start[0].astype(BF16).astype(F32)
            lax.fori_loop(0, chunks, chunk_forward, (h0, start[1]))

            def turn_all(which):
                depth, rows = (FILT, LEFT1) if which == 1 else (HID, LEFT2)
                width = FW if which == 1 else GW
                copies = (input_copy if which == 1 else layer_copy, hidden_copy)
                turn_inputs(x1 if which == 1 else xb, pb, depth, turned)
                turned_out(QUAD - 1, rows)
                for g in range(QUAD - 1):
                    for copy in copies:
                        copy(g + 1).wait_recv()
                    fetch(x_q.at[g, 0, :, pl.ds(0, width)], feats_v.at[0, :, pl.ds(0, width)])
                    fetch(h_q.at[g], ob)
                    turn_inputs(feats_v.at[0], ob, depth, turned)
                    turned_out(g, rows)
                each_peer(lambda k: [copy(k).wait_send() for copy in copies])

            pb[...] = prevs[...].astype(BF16)
            each_peer(lambda k: hidden_copy(k).start())

            @pl.when(role == 1)
            def _():
                each_peer(lambda k: input_copy(k).start())
                turn_all(1)

            @pl.when(role == 2)
            def _():
                each_peer(lambda k: layer_copy(k).start())

            def chunk_backward(i, carry):
                c = chunks - 1 - i
                backward_copy(c, 1).wait_recv()
                dhs[span(c), :] = db[span(c), :].astype(F32)
                carry = lstm_back_steps(c * steps, steps, keep, start.at[1], carry, r_t, gates, cells, dhs)
                dz16[span(c), :] = gates[span(c), :].astype(BF16)

                dz_t = jnp.transpose(dz16[span(c), :])

                @pl.when(role == 1)
                def _():
                    for at, width in fblocks(FW):
                        value = jnp.transpose(mm(u[pl.ds(at, width), :], dz_t))
                        if at + width > FILT:
                            value = jnp.where(column_mask(at, width, FILT, CHUNK), value, 0.0)
                        dy[span(c), pl.ds(at, width)] = value.astype(BF16)
                    last_copy(c, -1).start()
                    hand_copy(c, -1).start()

                @pl.when(role == 2)
                def _():
                    for at, width in fblocks(GW):
                        value = jnp.transpose(mm(u[pl.ds(at, width), :], dz_t))
                        if at + width > HID:
                            value = jnp.where(column_mask(at, width, HID, CHUNK), value, 0.0)
                        ob[span(c), pl.ds(at, width)] = value.astype(BF16)
                    backward_copy(c, -1).start()

                return carry

            zero = jnp.zeros((8, GW), F32)
            lax.fori_loop(0, chunks, chunk_backward, (zero, zero))

            own_right = pltpu.make_async_copy(dz16, dz_o.at[QUAD - 1], sem_out.at[1])
            own_right.start()

            @pl.when(role == 2)
            def _():
                each_peer(lambda k: right_copy(k).start())

            @pl.when(role == 1)
            def _():
                each_chunk(lambda c: last_copy(c, -1).wait_send())
                each_chunk(lambda c: hand_copy(c, -1).wait_send())
                each_chunk(lambda c: each_peer(lambda k: handed_copy(c, k).wait_recv()))

            @pl.when(role == 2)
            def _():
                each_chunk(lambda c: backward_copy(c, -1).wait_send())
                turn_all(2)

            own_right.wait()

            @pl.when(role == 2)
            def _():
                each_peer(lambda k: right_copy(k).wait_send())
                each_peer(lambda k: right_copy(k).wait_recv())


            def sent(c, carry):
                forward_copy(c, 1).wait_send()
                return carry

            lax.fori_loop(0, chunks, sent, 0)

        @pl.when(role == 3)
        def _():
            for copy in inputs(3):
                copy.wait()
            ob[...] = jnp.zeros_like(ob)
            done = 0
            for count in GROUPS_OUT:
                rows = pl.ds(done * CHUNK, count * CHUNK)
                for c in range(done, done + count):
                    forward_copy(c, -1).wait_recv()
                value = xb[rows, pl.ds(5 * LANE, LANE)].astype(F32)
                value = jnp.where(lanes(count * CHUNK) + 5 * LANE == HID, 1.0, value)
                xb[rows, pl.ds(5 * LANE, LANE)] = value.astype(BF16)
                output_rows(
                    done * CHUNK, count * CHUNK, xb, w, targets, valid, logits, dl, top, part, dh, loss, ob
                )
                for c in range(done, done + count):
                    backward_copy(c, -1).start()
                done += count
            copies = [
                pltpu.make_async_copy(xb, xb_o, sem_out.at[0]),
                pltpu.make_async_copy(dl, dl_o, sem_out.at[1]),
            ]
            for copy in copies:
                copy.start()
            for c in range(chunks):
                backward_copy(c, -1).wait_send()
            for copy in copies:
                copy.wait()

        loss_o[...] = loss[...]

    most = max(GROUPS_OUT) * CHUNK
    sems = pltpu.SemaphoreType.DMA
    outs = [
        ((n, FW), F32), ((n, 4 * FW), BF16), ((QUAD - 1, n - SPLIT * CHUNK, 4 * FW), BF16), ((n, GW), BF16),
        ((QUAD, LEFT_ROOM, n), BF16), ((QUAD, n, ZW), BF16), ((n, VW), BF16), ((QUAD - 1, 2, n, FW), BF16),
        ((QUAD - 1, n, GW), BF16),
    ]
    scratch = [
        vmem((n, LANE), F32), vmem((n, LANE), F32), vmem((n, LANE), jnp.int32),
        vmem((2, n, FW), BF16), vmem((LEFT0, n), BF16), vmem((n, GW), BF16),
        vmem((n, FW), BF16), vmem((n, GW), BF16), vmem((n, GW), BF16), vmem((n, GW), BF16), vmem((n, GW), BF16),
        vmem((n, FW), BF16), vmem((FW, ZW), BF16), vmem((GW, ZW), BF16), vmem((ZW, GW), BF16), vmem(wt.shape, BF16),
        vmem((2, 8, GW), F32), vmem((n, ZW), F32), vmem((n, GW), F32), vmem((n, GW), F32), vmem((n, GW), F32),
        vmem((n, GW), F32), vmem((n, ZW), BF16),
        vmem((most, VW), F32), vmem((n, VW), BF16), vmem((most, LANE), F32), vmem((2, most, LANE), F32),
        vmem((depth_w, LANE), F32), vmem((1, LANE), F32),
        dmas(12), dmas(3), dmas(1), dmas(1), dmas(chunks), dmas(chunks), dmas(chunks), dmas(chunks), dmas(chunks), dmas(chunks),
        sems((QUAD - 1, chunks)), sems((QUAD - 1, chunks)), sems((QUAD - 1, chunks)), sems((QUAD - 1, chunks)),
        sems((QUAD - 1, chunks)), sems((QUAD - 1, chunks)), dmas(2), sems((2, 4)), dmas(chunks), dmas(chunks),
    ]
    return pl.pallas_call(
        kernel,
        out_shape=[jax.ShapeDtypeStruct(shape, dtype) for shape, dtype in outs]
        + [jax.ShapeDtypeStruct((1, LANE), F32), jax.ShapeDtypeStruct((1, FW), F32)],
        in_specs=[ANYWHERE] * 7 + [ON_CHIP] * 4,
        out_specs=[ANYWHERE] * 9 + [ON_CHIP] * 2,
        scratch_shapes=scratch,
        compiler_params=pltpu.CompilerParams(vmem_limit_bytes=62 << 20, collective_id=3, has_side_effects=True),
        name="recurrent",
    )(y2, feats, pres, ab, ur, rt, wt, resets, target_ids, remaining, state)


FORM = (
    (FILT, 9, 4 * (FILT + 1), CONV_END, CONV_TILES, 32),
    (4 * HID, 24, FILT + HID + 1, 0, 0, 16),
    (4 * HID, 24, 2 * HID + 1, 0, 0, 16),
    (VOCAB, 79, HID + 1, 0, 0, 16),
)


def slab(role, dest, share):
    width, pitch, rows, before, lead, period = FORM[role]
    low = lax.max if not isinstance(dest, int) else max
    high = lax.min if not isinstance(dest, int) else min
    one = (lambda v: v) if isinstance(dest, int) else jnp.int32
    start = low(one(share) * dest - before, one(0))
    first = start // width // period * period
    end = high((share * (dest + 1) - before + width - 1) // width, one(rows))
    count = low((end - first + 15) // 16, one(0)) * pitch
    tile = lead + first // 16 * pitch
    if lead:
        if isinstance(dest, int):
            if dest == 0:
                tile, count = 0, count + lead
        else:
            head = lax.max(1 - dest, 0)
            tile = tile - lead * head
            count = count + lead * head
    return first, tile, count


def slab_pieces(count, size):
    return (count + size - 1) // size


def gather_sum_call(tiles, groups, share):
    pair = 2
    across = groups // pair
    size = 80 if across <= 4 else 32
    pieces = max(slab_pieces(slab(3, dest, share)[2], size) for dest in range(groups))
    room = pieces * size
    line = across <= 4
    slots = across + 1 if line else across - 1
    MESH = pl.DeviceIdType.MESH

    def kernel(
        tiles, out, own, got1, got2, acc, own_sem, send1, recv1, send2, recv2, out_sem,
    ):
        role = lax.axis_index("section")
        me = lax.axis_index("dp")
        mine, side = me // pair, lax.rem(me, pair)
        other = mine * pair + (1 - side)

        def at_place(place):
            return {"dp": place * pair + side}

        def part(ref, slot, p):
            return ref.at[slot, pl.ds(pl.multiple_of(p * size, size), size)]

        def span(p):
            return pl.ds(pl.multiple_of(p * size, size), size)

        def loop(count, body):
            def step(p, carry):
                body(p)
                return carry

            lax.fori_loop(0, count, step, 0)

        def run(shape_of):
            def count_to(place, which):
                return shape_of(place * pair + which)[1]

            def own_copy(place, p):
                tile, _ = shape_of(place * pair + side)
                return pltpu.make_async_copy(
                    tiles.at[pl.ds(tile + p * size, size)], part(own, place, p), own_sem.at[place, p]
                )

            def first_copy(place, p):
                tile, _ = shape_of(place * pair + 1 - side)
                return pltpu.make_async_remote_copy(
                    tiles.at[pl.ds(tile + p * size, size)], part(got1, place, p), send1.at[place, p], recv1.at[place, p],
                    device_id={"dp": other}, device_id_type=MESH,
                )

            def begin(place):
                loop(count_to(place, 1 - side), lambda p: first_copy(place, p).start())
                loop(count_to(place, side), lambda p: own_copy(place, p).start())

            def hop_copy(place, up, p):
                if line:
                    target = mine + 1 if up else mine - 1
                    slot = jnp.where(place == mine + 1, across, place) if up else place
                else:
                    target = place
                    slot = lax.rem(place - mine + across, across) - 1
                return pltpu.make_async_remote_copy(
                    part(own, place, p), part(got2, slot, p), send2.at[place, p], recv2.at[slot, p],
                    device_id=at_place(target), device_id_type=MESH,
                )

            def arrived(slot, p):
                return pltpu.make_async_remote_copy(
                    part(own, 0, p), part(got2, slot, p), send2.at[0, p], recv2.at[slot, p],
                    device_id=at_place(lax.rem(mine + 1, across)), device_id_type=MESH,
                )

            def forward(place, up, has_before):
                def body(p):
                    own_copy(place, p).wait()
                    first_copy(place, p).wait_recv()
                    at = span(p)
                    own[place, at] = (own[place, at].astype(F32) + got1[place, at].astype(F32)).astype(BF16)
                    hop_copy(place, up, p).start()

                def body_sum(p):
                    own_copy(place, p).wait()
                    first_copy(place, p).wait_recv()
                    arrived(place, p).wait_recv()
                    at = span(p)
                    total = own[place, at].astype(F32) + got1[place, at].astype(F32) + got2[place, at].astype(F32)
                    own[place, at] = total.astype(BF16)
                    hop_copy(place, up, p).start()

                count = count_to(place, side)
                if not line:
                    loop(count, body)
                    return

                @pl.when(has_before)
                def _():
                    loop(count, body_sum)

                @pl.when(jnp.logical_not(has_before))
                def _():
                    loop(count, body)

            if line:
                for k in range(across - 1):

                    @pl.when(k < mine)
                    def _(k=k):
                        begin(k)

                    @pl.when(k < across - 1 - mine)
                    def _(k=k):
                        begin(across - 1 - k)

                begin(mine)
                for k in range(across - 1):

                    @pl.when(k < mine)
                    def _(k=k):
                        forward(k, False, mine < across - 1)

                    @pl.when(k < across - 1 - mine)
                    def _(k=k):
                        forward(across - 1 - k, True, mine > 0)

            else:
                for k in range(1, across):
                    begin(lax.rem(mine + k, across))
                begin(mine)
                for k in range(1, across):
                    forward(lax.rem(mine + k, across), True, None)

            def settle(p):
                own_copy(mine, p).wait()
                first_copy(mine, p).wait_recv()
                at = span(p)
                acc[at] = own[mine, at].astype(F32) + got1[mine, at].astype(F32)

            def add(slot):
                def body(p):
                    arrived(slot, p).wait_recv()
                    at = span(p)
                    acc[at] += got2[slot, at].astype(F32)

                return body

            mine_count = count_to(mine, side)
            loop(mine_count, settle)
            if line:

                @pl.when(mine < across - 1)
                def _():
                    loop(mine_count, add(mine))

                @pl.when(mine > 0)
                def _():
                    loop(mine_count, add(across))

            else:
                for k in range(1, across):
                    loop(mine_count, add(k - 1))

            def out_copy(p):
                return pltpu.make_async_copy(acc.at[span(p)], out.at[span(p)], out_sem.at[p])

            loop(mine_count, lambda p: out_copy(p).start())
            loop(mine_count, lambda p: out_copy(p).wait())
            for place in range(across):
                loop(count_to(place, 1 - side), lambda p, place=place: first_copy(place, p).wait_send())

                @pl.when(place != mine)
                def _(place=place):
                    loop(count_to(place, side), lambda p: hop_copy(place, True, p).wait_send())

        def shape_of(dest):
            _, tile, count = slab(3, dest, share)
            return tile, slab_pieces(count, size)

        @pl.when(role == 3)
        def _():
            barrier = pltpu.get_barrier_semaphore()
            pl.semaphore_signal(barrier, inc=1, device_id={"dp": other}, device_id_type=MESH)
            for k in range(1, across):
                peer = at_place(lax.rem(mine + k, across))
                pl.semaphore_signal(barrier, inc=1, device_id=peer, device_id_type=MESH)
            pl.semaphore_wait(barrier, across)
            run(shape_of)

    sems = pltpu.SemaphoreType.DMA
    return pl.pallas_call(
        kernel,
        out_shape=jax.ShapeDtypeStruct((room, 16, LANE), F32),
        in_specs=[ANYWHERE],
        out_specs=ANYWHERE,
        scratch_shapes=[
            vmem((across, room, 16, LANE), BF16), vmem((across, room, 16, LANE), BF16),
            vmem((slots, room, 16, LANE), BF16), vmem((room, 16, LANE), F32),
            sems((across, pieces)), sems((across, pieces)), sems((across, pieces)),
            sems((across, pieces)), sems((slots, pieces)), sems((pieces,)),
        ],
        compiler_params=pltpu.CompilerParams(vmem_limit_bytes=62 << 20, collective_id=1, has_side_effects=True),
        name="gather_sum",
    )(tiles)


BLOCK_ROWS = (25, 11, 11)


def finish_call(lhs, dz, dpre, rights, conv, bias, loss, after, groups, share):
    n = lhs.shape[2]
    quads = groups // QUAD
    MESH = pl.DeviceIdType.MESH

    def most_blocks(role):
        width = FORM[role][1]
        lead = FORM[role][4]
        most = 0
        for dest in range(groups):
            count = slab(role, dest, share)[2]
            if lead and dest == 0:
                count -= lead
            most = max(most, -(-(count // width) // BLOCK_ROWS[role]))
        return most

    blocks = [most_blocks(role) for role in range(3)]
    room = max(
        FORM[role][4] + blocks[role] * BLOCK_ROWS[role] * FORM[role][1] for role in range(3)
    )
    left_rows = max(blocks[role] * BLOCK_ROWS[role] * 16 for role in range(3))
    most = max(blocks)

    def kernel(
        lhs, dz, dpre, late, early, conv, bias, loss, after, out, small_out,
        left, dpre_v, sent, got, acc, convs, lead_sum, small, got_small,
        sem_left, sem_right, send, recv, send_c, recv_c, small_send, small_recv, sem_out,
    ):
        role = lax.axis_index("section")
        me = lax.axis_index("dp")
        place, quad = lax.rem(me, QUAD), me // QUAD

        def across_peer(k):
            return {"dp": place + QUAD * lax.rem(quad + k, quads)}

        barrier = pltpu.get_barrier_semaphore()
        for k in range(1, QUAD):
            pl.semaphore_signal(barrier, inc=1, device_id={"dp": quad_peer(me, k)}, device_id_type=MESH)
        for k in range(1, quads):
            pl.semaphore_signal(barrier, inc=1, device_id=across_peer(k), device_id_type=MESH)

        def right_load(b):
            return pltpu.make_async_copy(
                dz.at[:, :, pl.ds(GW * b, GW)], dpre_v.at[:, b, :, pl.ds(0, GW)], sem_right.at[b]
            )

        def right_loads0():
            copies = []
            cut = SPLIT * CHUNK
            for b in range(4):
                cols = pl.ds(FW * b, FW)
                pairs = [
                    (early.at[:, :, cols], dpre_v.at[pl.ds(0, QUAD - 1), b, pl.ds(0, cut)]),
                    (late.at[:, :, cols], dpre_v.at[pl.ds(0, QUAD - 1), b, pl.ds(cut, n - cut)]),
                    (dpre.at[:, cols], dpre_v.at[QUAD - 1, b]),
                ]
                copies += [pltpu.make_async_copy(x, y, sem_right.at[4 + 3 * b + i]) for i, (x, y) in enumerate(pairs)]
            return copies

        def conv_load():
            return pltpu.make_async_copy(conv, convs.at[QUAD - 1], sem_right.at[16])

        @pl.when(role == 0)
        def _():
            for copy in right_loads0():
                copy.start()
            conv_load().start()

        @pl.when((role == 1) | (role == 2))
        def _():
            for b in range(4):
                right_load(b).start()

        pl.semaphore_wait(barrier, QUAD - 1 + quads - 1)

        small[...] = jnp.zeros_like(small)

        @pl.when(role == 0)
        def _():
            small[0, :, pl.ds(0, FW)] = bias[...]

        @pl.when(role == 3)
        def _():
            small[0, :, pl.ds(FW, LANE)] = loss[...]

        def small_copy(k):
            if k < QUAD:
                source, target = small.at[0], {"dp": quad_peer(me, k)}
            else:
                source, target = small.at[1], across_peer(k - QUAD + 1)
            return pltpu.make_async_remote_copy(
                source, got_small.at[k - 1], small_send.at[k - 1], small_recv.at[k - 1],
                device_id=target, device_id_type=MESH,
            )

        for k in range(1, QUAD):
            small_copy(k).start()

        def across_small():
            for k in range(1, QUAD):
                small_copy(k).wait_recv()
            small[1] = small[0] + got_small[0] + got_small[1] + got_small[2]
            for k in range(QUAD, QUAD + quads - 1):
                small_copy(k).start()

        def share_small():
            total = small[1]
            for k in range(QUAD, QUAD + quads - 1):
                small_copy(k).wait_recv()
                total = total + got_small[k - 1]
            for k in range(1, QUAD):
                small_copy(k).wait_send()
            small_out[...] = total

        def conv_copy(slot, target):
            return pltpu.make_async_remote_copy(
                conv, convs.at[slot], send_c.at[slot], recv_c.at[slot], device_id={"dp": target}, device_id_type=MESH
            )

        def run(which):
            width, pitch, rows, _, lead, _ = FORM[which]
            size = BLOCK_ROWS[which]
            block_tiles = size * pitch

            def geometry(k):
                dest = place + QUAD * lax.rem(quad + k, quads)
                first, _, count = slab(which, dest, share)
                if lead:
                    head = lax.max(1 - dest, 0)
                    count = count - lead * head
                else:
                    head = 0
                return first, (count // pitch + size - 1) // size, head

            def left_copy(k):
                height = blocks[which] * size * 16
                first = lax.min(geometry(k)[0], LEFT_ROOM - height)
                span = pl.ds(pl.multiple_of(first, 16), height)
                return pltpu.make_async_copy(
                    lhs.at[:, span], left.at[lax.rem(k, 2), :, pl.ds(0, blocks[which] * size * 16)], sem_left.at[lax.rem(k, 2)]
                )

            def block_copy(k, b):
                span = pl.ds(CONV_TILES + b * block_tiles, block_tiles)
                return pltpu.make_async_remote_copy(
                    sent.at[k - 1, span], got.at[k - 1, span], send.at[k - 1, b], recv.at[k - 1, b],
                    device_id=across_peer(k), device_id_type=MESH,
                )

            def lead_copy(k):
                span = pl.ds(0, CONV_TILES)
                return pltpu.make_async_remote_copy(
                    sent.at[k - 1, span], got.at[k - 1, span], send.at[k - 1, most], recv.at[k - 1, most],
                    device_id=across_peer(k), device_id_type=MESH,
                )

            def put(k, own, at, value):
                if own:
                    acc[at] = value
                else:
                    sent[k - 1, at] = value.astype(BF16)

            def block(k, own, b, first):
                here = pl.ds(pl.multiple_of(b * size * 16, 16), size * 16)
                base = CONV_TILES + b * block_tiles
                if which == 0:
                    row = lax.broadcasted_iota(jnp.int32, (size * 16, n), 0) + first + b * size * 16
                    start = first + b * size * 16
                    low = lax.min(start // (FILT + 1), 3)
                    high = lax.min((start + size * 16 - 1) // (FILT + 1), 3)
                    edge = (FILT + 1) * (low + 1)
                    lefts = [left[lax.rem(k, 2), g, here, :] for g in range(QUAD)]
                    near = [jnp.where(row < edge, x, jnp.zeros_like(x)) for x in lefts]
                    for col, wide in fblocks(FW):
                        value = jnp.zeros((size * 16, wide), F32)
                        for g in range(QUAD):
                            value = value + mm(near[g], dpre_v[g, low, :, pl.ds(col, wide)])
                        for r in range(size):
                            for c in range(wide // LANE):
                                tile = value[16 * r : 16 * r + 16, LANE * c : LANE * c + LANE]
                                put(k, own, base + r * pitch + col // LANE + c, tile)

                    @pl.when(high > low)
                    def _():
                        far = [jnp.where(row < edge, jnp.zeros_like(x), x) for x in lefts]
                        for col, wide in fblocks(FW):
                            value = jnp.zeros((size * 16, wide), F32)
                            for g in range(QUAD):
                                value = value + mm(far[g], dpre_v[g, high, :, pl.ds(col, wide)])
                            for r in range(size):
                                for c in range(wide // LANE):
                                    tile = value[16 * r : 16 * r + 16, LANE * c : LANE * c + LANE]
                                    at = base + r * pitch + col // LANE + c
                                    old = acc[at] if own else sent[k - 1, at].astype(F32)
                                    put(k, own, at, old + tile)

                else:
                    for col, wide in fblocks(ZW):
                        value = jnp.zeros((size * 16, wide), F32)
                        for g in range(QUAD):
                            value = value + mm(left[lax.rem(k, 2), g, here, :], dpre_v[g, col // GW, :, pl.ds(col % GW, wide)])
                        for r in range(size):
                            for c in range(wide // LANE):
                                tile = value[16 * r : 16 * r + 16, LANE * c : LANE * c + LANE]
                                put(k, own, base + r * pitch + col // LANE + c, tile)

            def loop(count, body):
                def step(b, carry):
                    body(b)
                    return carry

                lax.fori_loop(0, count, step, 0)

            left_copy(jnp.int32(1 % quads)).start()
            if which == 0:

                @pl.when(place > 0)
                def _():
                    for k in range(1, QUAD):

                        @pl.when(place == k)
                        def _(k=k):
                            conv_copy(k - 1, me - k).start()

                for copy in right_loads0():
                    copy.wait()
                conv_load().wait()
            else:
                for b in range(4):
                    right_load(b).wait()

            if which == 0:

                @pl.when(place == 0)
                def _():
                    for k in range(1, QUAD):
                        conv_copy(k - 1, me + k).wait_recv()
                    total = convs[0].astype(F32)
                    for k in range(1, QUAD):
                        total = total + convs[k].astype(F32)
                    lead_sum[...] = total

            def slab_of(k, own):
                left_copy(k).wait()
                if not own:
                    left_copy(lax.rem(k + 1, quads)).start()
                first, count, head = geometry(k)
                if which == 0:

                    @pl.when(head > 0)
                    def _():
                        if own:
                            acc[pl.ds(0, CONV_TILES)] = lead_sum[...]
                        else:
                            sent[k - 1, pl.ds(0, CONV_TILES)] = lead_sum[...].astype(BF16)
                            lead_copy(k).start()

                def work(b):
                    block(k, own, b, first)
                    if not own:
                        block_copy(k, b).start()

                loop(count, work)

            def others(body):
                def step(k, carry):
                    body(k)
                    return carry

                lax.fori_loop(1, quads, step, 0)

            others(lambda k: slab_of(k, False))
            across_small()
            slab_of(jnp.int32(0), True)
            share_small()

            _, mine, head = geometry(0)
            def join(k):
                def add(b):
                    block_copy(k, b).wait_recv()
                    span = pl.ds(CONV_TILES + b * block_tiles, block_tiles)
                    acc[span] += got[k - 1, span].astype(F32)

                loop(mine, add)
                if which == 0:

                    @pl.when(head > 0)
                    def _():
                        lead_copy(k).wait_recv()
                        span = pl.ds(0, CONV_TILES)
                        acc[span] += got[k - 1, span].astype(F32)

            others(join)

            span = blocks[which] * block_tiles
            if which == 0:

                @pl.when(head > 0)
                def _():
                    copy = pltpu.make_async_copy(
                        acc.at[pl.ds(0, CONV_TILES + span)], out.at[pl.ds(0, CONV_TILES + span)], sem_out.at[0]
                    )
                    copy.start()
                    copy.wait()

                @pl.when(head == 0)
                def _():
                    copy = pltpu.make_async_copy(acc.at[pl.ds(CONV_TILES, span)], out.at[pl.ds(0, span)], sem_out.at[0])
                    copy.start()
                    copy.wait()

            else:
                copy = pltpu.make_async_copy(acc.at[pl.ds(CONV_TILES, span)], out.at[pl.ds(0, span)], sem_out.at[0])
                copy.start()
                copy.wait()

            def sent_all(k):
                _, count, head = geometry(k)
                loop(count, lambda b: block_copy(k, b).wait_send())
                if which == 0:

                    @pl.when(head > 0)
                    def _():
                        lead_copy(k).wait_send()

            others(sent_all)

            if which == 0:
                for k in range(1, QUAD):

                    @pl.when(place == k)
                    def _(k=k):
                        conv_copy(k - 1, me - k).wait_send()

        for which in range(3):

            @pl.when(role == which)
            def _(which=which):
                run(which)

        @pl.when(role == 3)
        def _():
            across_small()
            share_small()

        for k in range(QUAD, QUAD + quads - 1):
            small_copy(k).wait_send()

    sems = pltpu.SemaphoreType.DMA
    full = CONV_TILES + max(blocks[role] * BLOCK_ROWS[role] * FORM[role][1] for role in range(3))
    smalls = QUAD + quads - 2
    return pl.pallas_call(
        kernel,
        out_shape=[jax.ShapeDtypeStruct((full, 16, LANE), F32), jax.ShapeDtypeStruct((1, FW + LANE), F32)],
        in_specs=[ANYWHERE] * 6 + [ON_CHIP] * 2 + [ANYWHERE],
        out_specs=[ANYWHERE, ON_CHIP],
        scratch_shapes=[
            vmem((2, QUAD, left_rows, n), BF16), vmem((QUAD, 4, n, FW), BF16),
            vmem((quads - 1, full, 16, LANE), BF16), vmem((quads - 1, full, 16, LANE), BF16),
            vmem((full, 16, LANE), F32), vmem((QUAD, CONV_TILES, 16, LANE), BF16), vmem((CONV_TILES, 16, LANE), F32),
            vmem((2, 1, FW + LANE), F32), vmem((smalls, 1, FW + LANE), F32),
            sems((2,)), sems((17,)), sems((quads - 1, most + 1)), sems((quads - 1, most + 1)),
            sems((QUAD - 1,)), sems((QUAD - 1,)), sems((smalls,)), sems((smalls,)), sems((1,)),
        ],
        compiler_params=pltpu.CompilerParams(vmem_limit_bytes=62 << 20, collective_id=5, has_side_effects=True),
        name="finish",
    )(lhs, dz, dpre, *rights, conv, bias, loss, after)


def sections_sum_call(small):
    count = lax.axis_size("section")

    def kernel(mine, out, held, send, recv):
        me = lax.axis_index("section")
        barrier = pltpu.get_barrier_semaphore()

        def peer(k):
            return {"section": lax.rem(me + k, count)}

        for k in range(1, count):
            pl.semaphore_signal(barrier, inc=1, device_id=peer(k), device_id_type=pl.DeviceIdType.MESH)
        pl.semaphore_wait(barrier, count - 1)
        copies = [
            pltpu.make_async_remote_copy(
                mine, held.at[k], send.at[k], recv.at[k], device_id=peer(k), device_id_type=pl.DeviceIdType.MESH
            )
            for k in range(1, count)
        ]
        for copy in copies:
            copy.start()
        total = mine[...]
        for k, copy in enumerate(copies):
            copy.wait_recv()
            total = total + held[k + 1]
        out[...] = total
        for copy in copies:
            copy.wait_send()

    return pl.pallas_call(
        kernel,
        out_shape=jax.ShapeDtypeStruct(small.shape, F32),
        in_specs=[ON_CHIP],
        out_specs=ON_CHIP,
        scratch_shapes=[vmem((count,) + small.shape, F32), dmas(count), dmas(count)],
        compiler_params=pltpu.CompilerParams(collective_id=2, has_side_effects=True),
        name="sections_sum",
    )(small)


def pack_call(summed, summed3, groups, share):
    rooms = (summed.shape[0] * 16, summed3.shape[0] * 16)
    chunks = share // LANE
    margin = 1280
    slab_rows = 10624
    flat_rows = margin + max(10752, chunks + 1280)

    def kernel(summed, summed3, out, rows_v, spaced, flat, sem):
        role = lax.axis_index("section")
        me = lax.axis_index("dp")
        zero = jnp.zeros((64, LANE), F32)

        def clear(i, carry):
            flat[pl.ds(pl.multiple_of(i * 64, 64), 64), :] = zero
            return carry

        def fetch(source, room):
            return pltpu.make_async_copy(source, rows_v.at[pl.ds(0, room)], sem.at[0])

        @pl.when(role < 3)
        def _():
            fetch(summed, rooms[0]).start()

        @pl.when(role == 3)
        def _():
            fetch(summed3, rooms[1]).start()

        lax.fori_loop(0, flat_rows // 64, clear, 0)

        @pl.when(role < 3)
        def _():
            fetch(summed, rooms[0]).wait()

        @pl.when(role == 3)
        def _():
            fetch(summed3, rooms[1]).wait()

        lane = lanes()

        for which in range(4):
            width, pitch, rows, before, lead, period = FORM[which]
            if which == 0:
                blocks, cols, tiles = 1, FILT, 9
            elif which == 3:
                blocks, cols, tiles = 1, VOCAB, 79
            else:
                blocks, cols, tiles = 4, HID, 6
            stride = period * width // LANE
            most = max(slab(which, dest, share)[2] for dest in range(groups))
            groups8 = -(-(-(-most // pitch) * 16) // (8 * period))

            @pl.when(role == which)
            def _(which=which):
                first, _, count = slab(which, me, share)
                skip = lead * lax.max(1 - me, 0)
                step_rows = pitch * 49 + (pitch * 49 + 1) % 2

                def space(rt, carry):
                    for c in range(pitch):
                        for half in range(2):
                            at = pl.multiple_of((skip + rt * pitch + c) * 16 + 8 * half, 8)
                            spaced[pl.ds(rt * step_rows + 49 * c + 24 * half, 8, stride=3), :] = rows_v[pl.ds(at, 8), :]
                    return carry

                lax.fori_loop(0, (count - skip) // pitch, space, 0)
                base = margin + before // LANE + stride * (first // period) - chunks * me

                hop = period // 16 * step_rows
                half = period // 2

                def place(group, n, b):
                    number = first + period * (8 * group + sublanes()) + n
                    flat_at = before % LANE + width * n + cols * b
                    source = n // 16 * step_rows + 3 * lax.rem(n, 16) + 8 * group * hop + 49 * tiles * b
                    to = base + flat_at // LANE + stride * 8 * group
                    return number < rows, lax.rem(flat_at, LANE), source, to

                def run(places, low, high, lasts):
                    taken = [
                        [spaced[pl.ds(source + 49 * j, 8, stride=hop), :] for j in range(low, min(high, tiles))]
                        for _, _, source, _ in places
                    ]
                    edges = [j for j in range(low, high) if j == 0 or j >= tiles - 1]
                    old = [
                        {j: flat[pl.ds(to + j, 8, stride=stride), :] for j in edges} for _, _, _, to in places
                    ]
                    values, ends = [], []
                    for (keep, turn, _, _), pieces, olds, last in zip(places, taken, old, lasts):
                        turned = [last] + [pltpu.roll(jnp.where(keep, x, 0.0), turn, 1) for x in pieces]
                        for j in range(low, high):
                            here = turned[j - low + 1] if j < tiles else turned[-1]
                            value = here if j == tiles else jnp.where(lane >= turn, here, turned[j - low])
                            if j in olds:
                                at = lane + LANE * j - turn
                                value = jnp.where((at >= 0) & (at < cols), value, olds[j])
                            values.append(value)
                        ends.append(turned[-1])
                    at = 0
                    for _, _, _, to in places:
                        for j in range(low, high):
                            flat[pl.ds(to + j, 8, stride=stride), :] = values[at]
                            at += 1
                    return ends

                def row(i, carry):
                    group, n = i // half, lax.rem(i, half)
                    zero = jnp.zeros((8, LANE), F32)
                    if blocks == 4:
                        for b in range(2):
                            places = [place(group, m, c) for m in (n, n + half) for c in (b, b + 2)]
                            run(places, 0, tiles + 1, [zero] * 4)
                    else:
                        places = [place(group, m, 0) for m in (n, n + half)]
                        ends = [zero] * 2
                        for low in range(0, tiles + 1, 20):
                            ends = run(places, low, min(low + 20, tiles + 1), ends)
                    return carry

                @pl.when(count > 0)
                def _():
                    lax.fori_loop(0, half * groups8, row, 0)

        @pl.when((role == 0) & (me == 0))
        def _():
            lane1 = lanes(1)

            def piece(row_at, flat_at, low, size):
                edge = flat_at - low
                turn = edge % LANE
                to = margin + (edge - turn) // LANE
                first, end = low // LANE, (low + size - 1) // LANE
                last = jnp.zeros((1, LANE), F32)
                for j in range(first, end + 2):
                    least, most = max(low + turn - LANE * j, 0), min(low + size + turn - LANE * j, LANE)
                    here = last
                    if j <= end:
                        here = rows_v[row_at + 16 * j : row_at + 16 * j + 1, :]
                        here = pltpu.roll(here, turn, 1) if turn else here
                    if most > least:
                        value = jnp.where(lane1 >= turn, here, last) if turn else here
                        at = to + j
                        if least > 0 or most < LANE:
                            value = jnp.where((lane1 >= least) & (lane1 < most), value, flat[at : at + 1, :])
                        flat[at : at + 1, :] = value
                    last = here

            for k in range(1, 8):
                n = NFILT[k - 1]
                for i in range(k * D_CHAR + 1):
                    number = i + i // D_CHAR if i < k * D_CHAR else 15
                    piece(number // 16 * 144 + number % 16, KOFF[k - 1] + n * i, COLS[k - 1], n)
            for a in range(CHAR_V):
                piece(72 * 16 + a, D_CHAR * a, 0, D_CHAR)

        copy = pltpu.make_async_copy(flat.at[pl.ds(margin, chunks)], out, sem.at[0])
        copy.start()
        copy.wait()

    return pl.pallas_call(
        kernel,
        out_shape=jax.ShapeDtypeStruct((chunks, LANE), F32),
        in_specs=[ANYWHERE] * 2,
        out_specs=ANYWHERE,
        scratch_shapes=[
            vmem((slab_rows, LANE), F32), vmem((31104, LANE), F32), vmem((flat_rows, LANE), F32), dmas(1),
        ],
        compiler_params=pltpu.CompilerParams(vmem_limit_bytes=LIMIT),
        name="pack",
    )(summed.reshape(rooms[0], LANE), summed3.reshape(rooms[1], LANE))


def shards(char_ids, target_ids, remaining, resets, start_state, section_params):
    rows, steps = char_ids.shape[:2]
    groups = lax.axis_size("dp")
    packed = section_params.shape[1]
    share = packed // groups
    n = rows * (steps + 1)

    ids = jnp.pad(
        char_ids.transpose(1, 0, 2), ((0, 1), (0, 0), (0, LANE - WORD_CHARS)), constant_values=-1
    ).reshape(n, LANE)
    km, e8, ab, ur, rt, wt = unpack_all(section_params)
    y2, *char_saved = char_forward_call(ids, km, e8, ab)
    feats, pres, total, emb = char_saved
    grad, dpre, late, xb, lhs, dz, dl, _, _, loss, bias = recurrent_call(
        y2, feats, pres, ab, ur, rt, wt, resets, target_ids, remaining.reshape(rows, 1), start_state
    )
    tiles3 = output_weights_call(xb, dl)
    summed3 = gather_sum_call(tiles3, groups, share)
    conv, early = char_backward_call(ids, grad, km, (total, emb), dpre)
    summed, small = finish_call(lhs, dz, dpre, (late, early), conv, bias, loss, summed3, groups, share)
    small = sections_sum_call(small)
    flat = pack_call(summed, summed3, groups, share)
    mean_loss = small[0, FW] / (groups * rows * steps)
    return mean_loss, flat.reshape(1, share), small[0, :FILT]


def solution(mesh):
    in_specs = (
        P("dp", None, None),
        P("dp", None),
        P("dp"),
        P("dp", None),
        P(None, None, "dp", None),
        P("section", None),
    )
    out_specs = (P(), P("section", "dp"), P())
    return jax.shard_map(shards, mesh=mesh, in_specs=in_specs, out_specs=out_specs, check_vma=False)
```

```python
import functools
import math

import jax
import jax.numpy as jnp
from jax import lax
from jax.experimental import pallas as pl
from jax.experimental.pallas import tpu as pltpu
from jax.sharding import PartitionSpec as P

D_CHAR = 15
CHAR_V = 51
F_UNIT = 50
WORD_CHARS = 21
HID = 650
VOCAB = 10000
FILT = 1100
F32 = jnp.float32
BF16 = jnp.bfloat16

NFILT = [F_UNIT * min(k, 4) for k in range(1, 8)]
COLS = [sum(NFILT[:k]) for k in range(8)]
KOFF = [CHAR_V * D_CHAR + sum((j * D_CHAR + 1) * NFILT[j - 1] for j in range(1, k)) for k in range(1, 9)]
CONV_END = KOFF[7]
HIGH_STRIDE = FILT * (FILT + 1)
FW = 1152
GW = 768
ZW = 4 * GW
VW = 10112
LANE = 128
LENS = (2304, 2688, 2688, 5120)


def roll_lanes(x, shift):
    return pltpu.roll(x, shift, 1)


def lanes(rows=8):
    return lax.broadcasted_iota(jnp.int32, (rows, LANE), 1)


def sublanes():
    return lax.broadcasted_iota(jnp.int32, (8, LANE), 0)


def widen(raw, slot, rows, wide):
    def body(i, carry):
        piece = raw[slot, 0:1, pl.ds(pl.multiple_of(i * 16384, 16384), 16384)]
        wide[pl.ds(pl.multiple_of(i * 128, 128), 128), :] = piece.astype(F32).reshape(128, LANE)
        return carry

    lax.fori_loop(0, rows // 128, body, 0)


DEPTH = 4


def stream_start(count, length, total, chunk_of, src, raw, sem):
    for i in range(DEPTH - 1):
        stream_copy(jnp.int32(i), length, total, chunk_of, src, raw, sem).start()


def stream_at(i, length, total, chunk_of):
    return jnp.minimum(chunk_of(i) // 8 * 8, total - length)


def stream_copy(i, length, total, chunk_of, src, raw, sem):
    at = pl.multiple_of(stream_at(i, length, total, chunk_of) * LANE, 8 * LANE)
    slot = lax.rem(i, DEPTH)
    return pltpu.make_async_copy(
        src.at[:, pl.ds(at, length * LANE)], raw.at[slot, :, pl.ds(0, length * LANE)], sem.at[slot]
    )


def stream_blocks(count, length, total, chunk_of, src, raw, sem, wide, work):
    def body(i, carry):
        @pl.when(i + DEPTH - 1 < count)
        def _():
            stream_copy(i + DEPTH - 1, length, total, chunk_of, src, raw, sem).start()

        stream_copy(i, length, total, chunk_of, src, raw, sem).wait()
        widen(raw, lax.rem(i, DEPTH), length, wide)
        work(i, chunk_of(i) - stream_at(i, length, total, chunk_of))
        return carry

    lax.fori_loop(0, count, body, 0)


def take_rows(wide, starts, tiles, cols, stride, put):
    step = max(6, 40 // len(starts))
    lane = lanes()
    for low in range(0, tiles, step):
        high = min(tiles, low + step)
        loaded = [
            [wide[pl.ds(first + c, 8, stride=stride), :] for c in range(low, high + 1)] for _, first, _, _ in starts
        ]
        results = []
        for (_, _, shift, keep_row), pieces in zip(starts, loaded):
            turn = lax.rem(LANE - shift, LANE)
            split = lane < LANE - shift
            turned = [roll_lanes(piece, turn) for piece in pieces]
            for c in range(low, high):
                out = jnp.where(split, turned[c - low], turned[c - low + 1])
                keep = keep_row
                if cols - c * LANE < LANE:
                    keep = keep & (lane < cols - c * LANE)
                results.append(jnp.where(keep, out, 0.0))
        at = 0
        for tag, _, _, _ in starts:
            for c in range(low, high):
                put(tag, c, results[at])
                at += 1


def spread(c, n, period):
    return pl.ds((c * period + n) * 25, 8, stride=3)


def collect(dest, c, period):
    return [
        dest[pl.ds((c * period + 8 * m) * 25 + 3 * j, 8, stride=25), :] for j in range(8) for m in range(period // 8)
    ]


def stage_tile(stage, slot, c, blocks):
    for i in range(0, len(blocks), 2):
        pair = jnp.concatenate([blocks[i], blocks[i + 1]], axis=0).astype(BF16)
        stage[slot, pl.ds(8 * i, 16), pl.ds(c * LANE, LANE)] = pair


def unpack_kernel(
    src, km, e8, ab, ur, rt, wt, raw, wide, dest, kstage, stage0, stage1, stage_t, stage3, raw_conv, sem_in, sem_out, sem_t
):
    role = lax.axis_index("section")
    total = src.shape[1] // LANE

    def out_copy(stage, slot, target):
        return pltpu.make_async_copy(stage.at[slot], target, sem_out.at[slot])

    @pl.when(role == 0)
    def _():
        blocks = 5
        count = 4 * blocks

        def flat_of(i):
            return CONV_END + HIGH_STRIDE * (i // blocks)

        def chunk_of(i):
            return flat_of(i) // LANE + 2200 * lax.rem(i, blocks)

        length = 640
        copy = pltpu.make_async_copy(src.at[:, pl.ds(0, length * LANE)], raw_conv.at[0], sem_t.at[0])
        copy.start()
        stream_start(count, LENS[0], total, chunk_of, src, raw, sem_in)
        copy.wait()
        widen(raw_conv, 0, length, wide)
        lane1 = lanes(1)
        dest[pl.ds(0, 64), :] = jnp.zeros((64, LANE), F32)
        for a in range(CHAR_V):
            flat = D_CHAR * a
            q, s = flat // LANE, flat % LANE
            here = wide[q : q + 1, :]
            out = roll_lanes(here, (LANE - s) % LANE) if s else here
            if s + D_CHAR > LANE:
                out = jnp.where(lane1 < LANE - s, out, roll_lanes(wide[q + 1 : q + 2, :], LANE - s))
            dest[a : a + 1, :] = jnp.where(lane1 < D_CHAR, out, jnp.where(lane1 == D_CHAR, 1.0, 0.0))
        table = dest[pl.ds(0, 64), :]
        for m in range(8):
            kstage[pl.ds(64 * m, 64), pl.ds(0, LANE)] = (
                pltpu.roll(table, 16 * m, 1) if m else table
            ).astype(BF16)
        copy = pltpu.make_async_copy(kstage.at[pl.ds(0, 512), pl.ds(0, LANE)], e8, sem_out.at[0])
        copy.start()
        copy.wait()
        tiles = FW // LANE
        rows = 112
        dest[pl.ds(0, rows * tiles), :] = jnp.zeros((rows * tiles, LANE), F32)

        def kernel_row(k, i, row):
            n, base = NFILT[k - 1], COLS[k - 1]
            edge = KOFF[k - 1] + n * i - base
            q, s = edge // LANE, edge % LANE
            for ct in range(base // LANE, (base + n - 1) // LANE + 1):
                out = wide[q + ct : q + ct + 1, :]
                if s:
                    after = roll_lanes(wide[q + ct + 1 : q + ct + 2, :], LANE - s)
                    out = jnp.where(lane1 < LANE - s, roll_lanes(out, LANE - s), after)
                at = ct * rows + row
                low, high = max(base - ct * LANE, 0), min(base + n - ct * LANE, LANE)
                if low > 0 or high < LANE:
                    out = jnp.where((lane1 >= low) & (lane1 < high), out, dest[at : at + 1, :])
                dest[at : at + 1, :] = out

        for k in range(1, 8):
            for i in range(k * D_CHAR):
                kernel_row(k, i, i + i // D_CHAR)
            kernel_row(k, k * D_CHAR, 15)
        kstage[...] = jnp.zeros_like(kstage)
        for ct in range(tiles):
            kstage[pl.ds(112, rows), pl.ds(ct * LANE, LANE)] = dest[pl.ds(ct * rows, rows), :].astype(BF16)
        copy = pltpu.make_async_copy(kstage.at[pl.ds(0, 368)], km, sem_out.at[0])
        copy.start()
        copy.wait()

        def target(i):
            return ab.at[i // blocks, pl.ds(pl.multiple_of(lax.rem(i, blocks) * 256, 256), 256)]

        def work(i, extra):
            block = lax.rem(i, blocks)
            inner = lax.rem(flat_of(i), LANE)

            def rows_of(i, carry):
                starts = []
                for n in range(4):
                    n = 4 * i + n
                    flat = inner + FILT * n
                    keep = 32 * (8 * block + sublanes()) + n <= FILT
                    starts.append((n, flat // LANE + extra, lax.rem(flat, LANE), keep))

                def put(n, c, value):
                    dest[spread(c, n, 32), :] = value

                take_rows(wide, starts, tiles, FILT, 275, put)
                return carry

            lax.fori_loop(0, 8, rows_of, 0)
            slot = lax.rem(i, 2)

            @pl.when(i >= 2)
            def _():
                out_copy(stage0, slot, target(i - 2)).wait()

            for c in range(tiles):
                stage_tile(stage0, slot, c, collect(dest, c, 32))
            out_copy(stage0, slot, target(i)).start()

        stream_blocks(count, LENS[0], total, chunk_of, src, raw, sem_in, wide, work)
        for i in (count - 2, count - 1):
            out_copy(stage0, i % 2, target(i)).wait()

    for layer in (1, 2):

        @pl.when(role == layer)
        def _(layer=layer):
            depth = FILT if layer == 1 else HID
            blocks = -(-depth // 128)
            recurrent = depth * 4 * HID
            count = blocks + 6

            def chunk_of(i):
                return jnp.where(i < blocks, 2600 * i, recurrent // LANE + 2600 * (i - blocks))

            stream_start(count, LENS[1], total, chunk_of, src, raw, sem_in)

            def target(i):
                at = jnp.where(i < blocks, i, i - blocks + 9)
                return ur.at[pl.ds(pl.multiple_of(at * 128, 128), 128)]

            def work(i, extra):
                inner = jnp.where(i < blocks, 0, recurrent % LANE)
                block = jnp.where(i < blocks, i, i - blocks)
                limit = jnp.where(i < blocks, depth, HID + 1)

                def rows_of(i, carry):
                    starts = []
                    for n in (2 * i, 2 * i + 1):
                        keep = 16 * (8 * block + sublanes()) + n < limit
                        for b in range(4):
                            flat = inner + 4 * HID * n + HID * b
                            starts.append(((n, b), flat // LANE + extra, lax.rem(flat, LANE), keep))

                    def put(tag, c, value):
                        dest[spread(6 * tag[1] + c, tag[0], 16), :] = value

                    take_rows(wide, starts, 6, HID, 325, put)
                    return carry

                lax.fori_loop(0, 8, rows_of, 0)
                slot = lax.rem(i, 2)

                @pl.when(i >= 2)
                def _():
                    out_copy(stage1, slot, target(i - 2)).wait()

                for c in range(24):
                    stage_tile(stage1, slot, c, collect(dest, c, 16))
                out_copy(stage1, slot, target(i)).start()

                @pl.when(i >= blocks)
                def _():
                    @pl.when(i >= blocks + 2)
                    def _():
                        turned_copy(i - 2).wait()

                    k = LANE * block + lanes(LANE)
                    for c in range(24):
                        turned = jnp.transpose(jnp.concatenate(collect(dest, c, 16), axis=0))
                        stage_t[slot, pl.ds(128 * c, 128), :] = jnp.where(k < HID, turned, 0.0).astype(BF16)
                    turned_copy(i).start()

            def turned_copy(i):
                slot = lax.rem(i, 2)
                at = pl.multiple_of((i - blocks) * LANE, LANE)
                return pltpu.make_async_copy(stage_t.at[slot], rt.at[:, pl.ds(at, LANE)], sem_t.at[slot])

            stream_blocks(count, LENS[1], total, chunk_of, src, raw, sem_in, wide, work)
            for i in (count - 2, count - 1):
                out_copy(stage1, i % 2, target(jnp.int32(i))).wait()
                turned_copy(jnp.int32(i)).wait()

    @pl.when(role == 3)
    def _():
        count = 11
        tiles = VW // LANE

        def chunk_of(i):
            return 5000 * i

        stream_start(count, LENS[3], total, chunk_of, src, raw, sem_in)

        def target(i):
            return wt.at[pl.ds(pl.multiple_of(i * 64, 64), 64)]

        def work(i, extra):
            def rows_of(n, carry):
                flat = VOCAB * n
                keep = 8 * (8 * i + sublanes()) + n < HID + 1

                def put(n, c, value):
                    dest[spread(c, n, 8), :] = value

                take_rows(wide, [(n, flat // LANE + extra, lax.rem(flat, LANE), keep)], tiles, VOCAB, 625, put)
                return carry

            lax.fori_loop(0, 8, rows_of, 0)
            slot = lax.rem(i, 2)

            @pl.when(i >= 2)
            def _():
                out_copy(stage3, slot, target(i - 2)).wait()

            for c in range(tiles):
                stage_tile(stage3, slot, c, collect(dest, c, 8))
            out_copy(stage3, slot, target(i)).start()

        stream_blocks(count, LENS[3], total, chunk_of, src, raw, sem_in, wide, work)
        for i in (count - 2, count - 1):
            out_copy(stage3, i % 2, target(jnp.int32(i))).wait()


def unpack_all(section_params):
    anywhere = pl.BlockSpec(memory_space=pl.ANY)
    return pl.pallas_call(
        unpack_kernel,
        out_shape=[
            jax.ShapeDtypeStruct((368, FW), BF16),
            jax.ShapeDtypeStruct((512, LANE), BF16),
            jax.ShapeDtypeStruct((4, 1280, FW), BF16),
            jax.ShapeDtypeStruct((15 * 128, ZW), BF16),
            jax.ShapeDtypeStruct((ZW, GW), BF16),
            jax.ShapeDtypeStruct((11 * 64, VW), BF16),
        ],
        in_specs=[anywhere],
        out_specs=[anywhere] * 6,
        scratch_shapes=[
            pltpu.VMEM((DEPTH, 1, LENS[3] * LANE), BF16),
            pltpu.VMEM((9312, LANE), F32),
            pltpu.VMEM((79 * 200, LANE), F32),
            pltpu.VMEM((512, FW), BF16),
            pltpu.VMEM((2, 256, FW), BF16),
            pltpu.VMEM((2, 128, ZW), BF16),
            pltpu.VMEM((2, ZW, LANE), BF16),
            pltpu.VMEM((2, 64, VW), BF16),
            pltpu.VMEM((1, 1, 640 * LANE), BF16),
            pltpu.SemaphoreType.DMA((DEPTH,)),
            pltpu.SemaphoreType.DMA((2,)),
            pltpu.SemaphoreType.DMA((2,)),
        ],
        compiler_params=pltpu.CompilerParams(vmem_limit_bytes=56 << 20),
        name="unpack",
    )(section_params)


def fblocks(width, step=256):
    return [(at, min(step, width - at)) for at in range(0, width, step)]


def mm(a, b):
    return jnp.dot(a, b, preferred_element_type=F32)


def mm_tn(a, b):
    return lax.dot_general(a, b, (((0,), (0,)), ((), ())), preferred_element_type=F32)


def mm_nt(a, b):
    return lax.dot_general(a, b, (((1,), (1,)), ((), ())), preferred_element_type=F32)


def sigmoid(x):
    return 0.5 * jnp.tanh(0.5 * x) + 0.5


def load(pairs, sem):
    copies = [pltpu.make_async_copy(a, b, sem.at[i]) for i, (a, b) in enumerate(pairs)]
    for copy in copies:
        copy.start()
    for copy in copies:
        copy.wait()


def column_mask(at, width, limit, rows):
    return lax.broadcasted_iota(jnp.int32, (rows, width), 1) + at < limit


def char_onehot(ids, t):
    rows = ids.shape[0]
    lane = lanes(rows)
    pieces = []
    for pair in range(4):
        j = 8 * t + 2 * pair
        left = ids[:, j : j + 1]
        right = ids[:, j + 1 : j + 2]
        hit = jnp.where(lane < 64, left, right) == lax.rem(lane, 64)
        pieces.append(jnp.where(hit, 1.0, 0.0).astype(BF16))
    return jnp.concatenate(pieces, axis=1)


def conv_steps(body):
    def step(p, carry):
        body(p, p // 8, True, lax.rem(p, 8), FILT)
        return carry

    lax.fori_loop(0, 15, step, 0)
    body(15, 1, True, 7, COLS[6])
    for p in range(16, WORD_CHARS):
        body(p, 2, False, p - 16, COLS[WORD_CHARS - p])


def conv_at(emb, km, tile, second, within, at, width):
    first = 112 - 16 * within
    if not isinstance(first, int):
        first = pl.multiple_of(first, 16)
    if second:
        window = jnp.concatenate([emb[tile], emb[tile + 1]], axis=1)
    else:
        window = emb[tile]
    return mm(window, km[pl.ds(first, window.shape[1]), pl.ds(at, width)])


def char_forward(ids, e8, km, ab, emb, total, feats, pres, out):
    rows = ids.shape[0]
    for t in range(3):
        emb[t] = mm(char_onehot(ids, t), e8[...]).astype(BF16)
    total[...] = jnp.zeros_like(total)

    def step(p, tile, second, within, limit):
        for at, width in fblocks(FW):
            if at >= limit:
                continue
            value = jnp.exp(jnp.tanh(conv_at(emb, km, tile, second, within, at, width)))
            if at + width > limit and limit < FILT:
                value = jnp.where(column_mask(at, width, limit, rows), value, 0.0)
            total[:, pl.ds(at, width)] += value

    conv_steps(step)
    for at, width in fblocks(FW):
        col = lax.broadcasted_iota(jnp.int32, (rows, width), 1) + at
        count = jnp.full((rows, width), float(WORD_CHARS), F32)
        for k in range(1, 7):
            count = jnp.where(col >= COLS[k], float(WORD_CHARS - k), count)
        value = jnp.log(total[:, pl.ds(at, width)]) - jnp.log(count)
        value = jnp.where(col < FILT, value, jnp.where(col == FILT, 1.0, 0.0))
        feats[0, :, pl.ds(at, width)] = value.astype(BF16)
    for layer in range(2):
        for at, width in fblocks(FW):
            cols = pl.ds(at, width)
            t_pre = mm(feats[layer], ab[2 * layer, pl.ds(0, FW), cols])
            h_pre = mm(feats[layer], ab[2 * layer + 1, pl.ds(0, FW), cols])
            pres[2 * layer, :, cols] = t_pre
            pres[2 * layer + 1, :, cols] = h_pre
            gate = sigmoid(t_pre)
            y = feats[layer, :, cols].astype(F32)
            value = gate * (h_pre * sigmoid(h_pre)) + (1.0 - gate) * y
            col = lax.broadcasted_iota(jnp.int32, (rows, width), 1) + at
            if layer == 0:
                value = jnp.where(col < FILT, value, jnp.where(col == FILT, 1.0, 0.0))
                feats[1, :, cols] = value.astype(BF16)
            else:
                out[:, cols] = jnp.where(col < FILT, value, 0.0).astype(BF16)


def conv_backward(km, kt, emb, emb_t, total, grad, dk, demb, relay):
    rows = grad.shape[0]
    kt[...] = jnp.transpose(km[pl.ds(112, LANE), :])
    for t in range(3):
        emb_t[pl.ds(LANE * t, LANE), :] = jnp.transpose(emb[t])
    emb_t[pl.ds(3 * LANE, LANE), :] = jnp.zeros((LANE, rows), BF16)
    dk[...] = jnp.zeros_like(dk)
    demb[...] = jnp.zeros_like(demb)
    for at, width in fblocks(FW):
        cols = pl.ds(at, width)
        grad[:, cols] = grad[:, cols] / total[:, cols]

    def step(p, tile, second, within, limit):
        relay(p)
        window_t = emb_t[pl.ds(p * 16 if isinstance(p, int) else pl.multiple_of(p * 16, 16), LANE), :]
        back = jnp.zeros((rows, LANE), F32)
        for at, width in fblocks(FW):
            if at >= limit:
                continue
            cols = pl.ds(at, width)
            act = jnp.tanh(conv_at(emb, km, tile, second, within, at, width))
            dz = grad[:, cols] * jnp.exp(act) * (1.0 - act * act)
            if at + width > limit and limit < FILT:
                dz = jnp.where(column_mask(at, width, limit, rows), dz, 0.0)
            dz = dz.astype(BF16)
            dk[:, cols] += mm(window_t, dz)
            back = back + mm(dz, kt[cols, :])
        lane = lanes(rows)
        back = jnp.where(lane < 112, back, 0.0)
        turned = pltpu.roll(back, 16 * within, 1)
        demb[tile] += jnp.where(lane >= 16 * within, turned, 0.0)
        if second:
            demb[tile + 1] += jnp.where(lane < 16 * within, turned, 0.0)

    conv_steps(step)


def table_backward(ids, demb, table):
    acc = jnp.zeros((64, LANE), F32)
    for t in range(3):
        hot = char_onehot(ids, t)
        value = demb[t]
        high = value.astype(BF16)
        low = (value - high.astype(F32)).astype(BF16)
        grads = mm_tn(hot, high) + mm_tn(hot, low)
        for m in range(8):
            block = grads[64 * m : 64 * m + 64, :]
            acc = acc + (pltpu.roll(block, LANE - 16 * m, 1) if m else block)
    table[...] = acc


def tile_rows(stage, base, value, row_tiles, col_tiles, first_col=0, pitch=None):
    pitch = col_tiles if pitch is None else pitch
    for r in range(row_tiles):
        for c in range(col_tiles):
            stage[base + r * pitch + first_col + c] = value[16 * r : 16 * r + 16, LANE * c : LANE * c + LANE].astype(BF16)


def six(x):
    return jnp.concatenate([x] * 6, axis=1)


ANYWHERE = pl.BlockSpec(memory_space=pl.ANY)
ON_CHIP = pl.BlockSpec(memory_space=pltpu.VMEM)
LIMIT = 56 << 20


def call(kernel, name, ins, specs, outs, scratch, aliases=None):
    return pl.pallas_call(
        kernel,
        out_shape=[jax.ShapeDtypeStruct(shape, dtype) for shape, dtype in outs],
        in_specs=specs,
        out_specs=[ANYWHERE] * len(outs),
        scratch_shapes=scratch,
        input_output_aliases=aliases or {},
        compiler_params=pltpu.CompilerParams(vmem_limit_bytes=LIMIT),
        name=name,
    )(*ins)


def vmem(shape, dtype):
    return pltpu.VMEM(shape, dtype)


def dmas(count):
    return pltpu.SemaphoreType.DMA((count,))


def char_forward_call(ids, km, e8, ab):
    n = ids.shape[0]

    def kernel(ids, km, e8, ab, y2_o, feats_o, pres_o, total_o, emb_o, km_v, e8_v, ab_v, y2, feats, pres, total, emb, sem):
        @pl.when(lax.axis_index("section") == 0)
        def _():
            load([(km, km_v), (e8, e8_v), (ab, ab_v)], sem)
            char_forward(ids, e8_v, km_v, ab_v, emb, total, feats, pres, y2)
            load([(y2, y2_o), (feats, feats_o), (pres, pres_o), (total, total_o), (emb, emb_o)], sem)

    outs = [
        ((n, FW), BF16),
        ((2, n, FW), BF16),
        ((4, n, FW), F32),
        ((n, FW), F32),
        ((3, n, LANE), BF16),
    ]
    scratch = [vmem(km.shape, BF16), vmem(e8.shape, BF16), vmem(ab.shape, BF16)]
    scratch += [vmem(shape, dtype) for shape, dtype in outs] + [dmas(5)]
    return call(kernel, "char_forward", (ids, km, e8, ab), [ON_CHIP] + [ANYWHERE] * 3, outs, scratch)


def char_backward_call(ids, grad, km, saved, dpre):
    n = ids.shape[0]
    total, emb = saved
    rows = SPLIT * CHUNK
    sems = pltpu.SemaphoreType.DMA

    def kernel(
        ids, grad, km, total, emb, dpre, tiles_o, right_o,
        grad_v, km_v, total_v, emb_v, kt, emb_t, dk, demb, table, stage, sem, send, recv,
    ):
        me = lax.axis_index("dp")

        def right_copy(k, i):
            span = pl.ds(pl.multiple_of(i * CHUNK, CHUNK), CHUNK)
            source = right_o.at[1, span] if k == 3 else dpre.at[span]
            return pltpu.make_async_remote_copy(
                source, right_o.at[k - 1, span], send.at[k - 1, i], recv.at[k - 1, i],
                device_id={"dp": quad_peer(me, 1 if k == 3 else k)}, device_id_type=pl.DeviceIdType.MESH,
            )

        def relay(p):
            if isinstance(p, int):
                return
            i = p // 3 - 1

            @pl.when((lax.rem(p, 3) == 0) & (p > 0) & (i < SPLIT))
            def _():
                right_copy(2, i).wait_recv()
                right_copy(3, i).start()

        @pl.when(lax.axis_index("section") == 0)
        def _():
            barrier = pltpu.get_barrier_semaphore()
            for k in range(1, QUAD):
                pl.semaphore_signal(
                    barrier, inc=1, device_id={"dp": quad_peer(me, k)}, device_id_type=pl.DeviceIdType.MESH
                )
            pl.semaphore_wait(barrier, QUAD - 1)
            for i in range(SPLIT):
                right_copy(2, i).start()
                right_copy(1, i).start()
            load([(grad, grad_v), (km, km_v), (total, total_v), (emb, emb_v)], sem)
            conv_backward(km_v, kt, emb_v, emb_t, total_v, grad_v, dk, demb, relay)
            table_backward(ids, demb, table)
            tile_rows(stage, 0, dk[...], 8, 9)
            tile_rows(stage, 72, table[...], 4, 1)
            load([(stage, tiles_o)], sem)
            for i in range(SPLIT):
                for k in range(1, QUAD):
                    right_copy(k, i).wait_send()
                    if k != 2:
                        right_copy(k, i).wait_recv()

    outs = [((CONV_TILES, 16, LANE), BF16), ((QUAD - 1, rows, 4 * FW), BF16)]
    scratch = [
        vmem((n, FW), F32), vmem(km.shape, BF16), vmem(total.shape, F32), vmem(emb.shape, BF16),
        vmem((FW, LANE), BF16), vmem((4 * LANE, n), BF16), vmem((LANE, FW), F32), vmem((3, n, LANE), F32),
        vmem((64, LANE), F32), vmem((CONV_TILES, 16, LANE), BF16), dmas(4), sems((QUAD - 1, SPLIT)), sems((QUAD - 1, SPLIT)),
    ]
    return pl.pallas_call(
        kernel,
        out_shape=[jax.ShapeDtypeStruct(shape, dtype) for shape, dtype in outs],
        in_specs=[ON_CHIP] + [ANYWHERE] * 5,
        out_specs=[ANYWHERE] * 2,
        scratch_shapes=scratch,
        compiler_params=pltpu.CompilerParams(vmem_limit_bytes=LIMIT, collective_id=4, has_side_effects=True),
        name="char_backward",
    )(ids, grad, km, total, emb, dpre)


CONV_TILES = 76
TILES = 3648


def turned_tile(left, right, shift):
    rows = right.shape[0]
    if shift:
        mixed = jnp.where(
            lanes(rows) < shift, pltpu.roll(left.astype(F32), shift, 1), pltpu.roll(right.astype(F32), shift, 1)
        )
        right = mixed.astype(BF16)
    return jnp.transpose(right)


def each_vocab(body, step=2048):
    whole = VW // step

    def one(i, carry):
        body(pl.multiple_of(i * step, step), step)
        return carry

    lax.fori_loop(0, whole, one, 0)
    body(whole * step, VW - whole * step)


def output_weights_call(h, dl):
    n = h.shape[0]
    rows = 704
    pitch = VW // LANE

    def kernel(h, dl, tiles_o, h_v, dl_v, h_t, stage, sem):
        @pl.when(lax.axis_index("section") == 3)
        def _():
            load([(h, h_v), (dl, dl_v)], sem)
            lane = lanes(n)
            for c in range(6):
                value = h_v[:, pl.ds(LANE * c, LANE)].astype(F32)
                value = jnp.where(lane + c * LANE == HID, 1.0, value).astype(BF16)
                h_t[pl.ds(LANE * c, LANE), :] = jnp.transpose(value)

            def body(at, width):
                first = at // LANE
                for top, count in fblocks(rows):
                    value = mm(h_t[pl.ds(top, count), :], dl_v[:, pl.ds(at, width)])
                    for r in range(count // 16):
                        for c in range(width // LANE):
                            stage[(top // 16 + r) * pitch + first + c] = value[
                                16 * r : 16 * r + 16, LANE * c : LANE * c + LANE
                            ].astype(BF16)

            each_vocab(body, 256)
            count = rows // 16 * pitch
            load([(stage.at[pl.ds(0, count)], tiles_o.at[pl.ds(0, count)])], sem)

    scratch = [
        vmem((n, GW), BF16), vmem((n, VW), BF16), vmem((6 * LANE, n), BF16),
        vmem((rows // 16 * pitch, 16, LANE), BF16), dmas(2),
    ]
    return call(
        kernel, "output_weights", (h, dl), [ANYWHERE] * 2, [((TILES, 16, LANE), BF16)], scratch
    )[0]


CHUNK = 32
GROUPS_OUT = (3, 3, 2, 1)


def lstm_steps(first, count, keep, carry, r, gates, cells, prevs, hiddens):
    def step(s, carry):
        h, c = carry
        at = pl.ds(pl.multiple_of((first + s) * 8, 8), 8)
        k = six(keep[at, :])
        hp = h * k
        cp = c * k
        prevs[at, :] = hp
        z = gates[at, :] + mm(hp.astype(BF16), r[...])
        i = sigmoid(z[:, 0:GW])
        f = sigmoid(z[:, GW : 2 * GW])
        o = sigmoid(z[:, 2 * GW : 3 * GW])
        g = jnp.tanh(z[:, 3 * GW :])
        c = f * cp + i * g
        h = (o * jnp.tanh(c)).astype(BF16).astype(F32)
        gates[at, :] = jnp.concatenate([i, f, o, g], axis=1)
        cells[at, :] = c
        hiddens[at, :] = h
        return h, c

    return lax.fori_loop(0, count, step, carry)


def lstm_back_steps(first, count, keep, c0, carry, rt, gates, cells, dhs):
    def step(s, carry):
        dh_next, dc_next = carry
        t = first + count - 1 - s
        at = pl.ds(pl.multiple_of(t * 8, 8), 8)
        before = pl.ds(pl.multiple_of(jnp.maximum(t - 1, 0) * 8, 8), 8)
        k = six(keep[at, :])
        saved = gates[at, :]
        i, f, o, g = [saved[:, GW * b : GW * b + GW] for b in range(4)]
        cp = jnp.where(t > 0, cells[before, :], c0[...]) * k
        ct = jnp.tanh(cells[at, :])
        dh = dhs[at, :] + dh_next
        dc = dc_next + dh * o * (1.0 - ct * ct)
        dz = jnp.concatenate(
            [dc * g * i * (1.0 - i), dc * cp * f * (1.0 - f), dh * ct * o * (1.0 - o), dc * i * (1.0 - g * g)], axis=1
        ).astype(BF16)
        gates[at, :] = dz.astype(F32)
        return k * mm(dz, rt[...]), k * dc * f

    return lax.fori_loop(0, count, step, carry)


def output_rows(first, count, h, w, targets, valid, logits, dl, top, part, dh, loss, dh16):
    at_rows = pl.ds(first, count)
    depth = w.shape[0]
    own = pl.ds(0, count)
    top[own, :] = jnp.full((count, LANE), -jnp.inf, F32)

    def forward(at, width):
        z = mm(h[at_rows, pl.ds(0, depth)], w[:, pl.ds(at, width)])
        if isinstance(at, int):
            z = jnp.where(column_mask(at, width, VOCAB, count), z, -jnp.inf)
        logits[own, pl.ds(at, width)] = z
        best = top[own, :]
        for c in range(width // LANE):
            best = jnp.maximum(best, z[:, LANE * c : LANE * c + LANE])
        top[own, :] = best

    each_vocab(forward)
    best = jnp.max(top[own, :], axis=1, keepdims=True)
    part[:, own, :] = jnp.zeros((2, count, LANE), F32)
    wanted = targets[at_rows, :]

    def exponents(at, width):
        z = logits[own, pl.ds(at, width)]
        e = jnp.exp(z - best)
        logits[own, pl.ds(at, width)] = e
        for c in range(width // LANE):
            part[0, own, :] += e[:, LANE * c : LANE * c + LANE]
            hit = lanes(count) + (at + LANE * c) == wanted
            part[1, own, :] += jnp.where(hit, z[:, LANE * c : LANE * c + LANE], 0.0)

    each_vocab(exponents)
    total = jnp.sum(part[0, own, :], axis=1, keepdims=True)
    picked = jnp.sum(part[1, own, :], axis=1, keepdims=True)
    counts = valid[at_rows, :]
    loss[...] += jnp.sum(counts * (best + jnp.log(total) - picked), axis=0, keepdims=True)
    share = counts / total
    dh[:, own] = jnp.zeros((depth, count), F32)

    def backward(at, width):
        e = logits[own, pl.ds(at, width)]
        pieces = []
        for c in range(width // LANE):
            hit = lanes(count) + (at + LANE * c) == wanted
            grad = e[:, LANE * c : LANE * c + LANE] * share - jnp.where(hit, counts, 0.0)
            pieces.append(grad.astype(BF16))
        grad = jnp.concatenate(pieces, axis=1)
        dl[at_rows, pl.ds(at, width)] = grad
        dh[:, own] += mm_nt(w[:, pl.ds(at, width)], grad)

    each_vocab(backward)
    for at, width in fblocks(depth):
        value = jnp.transpose(dh[pl.ds(at, width), own])
        dh16[at_rows, pl.ds(at, width)] = jnp.where(column_mask(at, width, HID, count), value, 0.0).astype(BF16)


QUAD = 4
LEFT0 = 35 * LANE
LEFT1 = 14 * LANE
LEFT2 = 11 * LANE
LEFT_ROOM = 41 * LANE


def quad_peer(me, k):
    place = lax.rem(me, QUAD)
    pair, side = place // 2, lax.rem(place, 2)
    return me + (k % 2) * (1 - 2 * side) + (k // 2) * (2 - 4 * pair)


def turn_features(feats, turned):
    n = feats.shape[1]
    zero = jnp.zeros((n, LANE), BF16)
    for segment in range(4):
        start = segment * (FILT + 1)
        shift, first, last = start % LANE, start // LANE, (start + FILT) // LANE
        for c in range(last - first + 1):
            left = feats[segment // 2, :, pl.ds(LANE * (c - 1), LANE)] if c > 0 else zero
            right = feats[segment // 2, :, pl.ds(LANE * c, LANE)] if c < 9 else zero
            tile = turned_tile(left, right, shift)
            at = pl.ds(LANE * (first + c), LANE)
            if c == 0 and segment > 0:
                tile = tile + turned[at, :]
            turned[at, :] = tile


def turn_inputs(x, prevs, depth, turned):
    n = prevs.shape[0]
    first, shift = depth // LANE, depth % LANE
    end = depth + HID
    zero = jnp.zeros((n, LANE), F32)
    lane = lanes(n)
    for c in range(end // LANE + 1):
        if c < first:
            mixed = x[:, pl.ds(LANE * c, LANE)]
        else:
            k = c - first
            left = prevs[:, pl.ds(LANE * (k - 1), LANE)].astype(F32) if 0 < k < 7 else zero
            right = prevs[:, pl.ds(LANE * k, LANE)].astype(F32) if k < 6 else zero
            before = pltpu.roll(left, shift, 1) if k else x[:, pl.ds(LANE * c, LANE)].astype(F32)
            mixed = jnp.where(lane < shift, before, pltpu.roll(right, shift, 1))
            mixed = jnp.where(lane + c * LANE == end, 1.0, mixed).astype(BF16)
        turned[pl.ds(LANE * c, LANE), :] = jnp.transpose(mixed)


SPLIT = 3
AB_PARTS = ((0, 640), (640, 512))


def highway_chunk(rows, slot, dy, feats, pres, grad, dpre, w):
    def cut(m, at, width):
        return pl.ds(m * FW + at, width)

    for at, width in fblocks(FW):
        grad[rows, pl.ds(at, width)] = dy[rows, pl.ds(at, width)].astype(F32)
    for layer in (1, 0):
        own = pl.ds(slot, CHUNK)
        for at, width in fblocks(FW):
            cols = pl.ds(at, width)
            g = grad[rows, cols]
            gate = sigmoid(pres[own, cut(2 * layer, at, width)])
            q = pres[own, cut(2 * layer + 1, at, width)]
            sig = sigmoid(q)
            y = feats[layer, rows, cols].astype(F32)
            dpre[rows, cut(2 * layer, at, width)] = (g * (q * sig - y) * gate * (1.0 - gate)).astype(BF16)
            dpre[rows, cut(2 * layer + 1, at, width)] = (g * gate * sig * (1.0 + q * (1.0 - sig))).astype(BF16)
            grad[rows, cols] = g * (1.0 - gate)
        turned = [jnp.transpose(dpre[rows, cut(2 * layer + i, 0, FW)]) for i in range(2)]
        for half, (row, count) in enumerate(AB_PARTS):
            for at, width in fblocks(count):
                cols = pl.ds(row + at, width)
                back = jnp.zeros((width, CHUNK), F32)
                for i in range(2):
                    part = w[pl.ds(at, width), pl.ds((2 * (2 * layer + i) + half) * FW, FW)]
                    back = back + mm(part, turned[i])
                value = grad[rows, cols] + jnp.transpose(back)
                if row + at + width > FILT:
                    value = jnp.where(column_mask(row + at, width, FILT, CHUNK), value, 0.0)
                grad[rows, cols] = value


def recurrent_call(y2, feats, pres, ab, ur, rt, wt, resets, target_ids, remaining, state):
    n = y2.shape[0]
    real_steps = resets.shape[1]
    chunks = n // CHUNK
    steps = CHUNK // 8
    depth_w = wt.shape[0]
    MESH = pl.DeviceIdType.MESH

    def kernel(
        y2, feats, pres, ab, ur, rt, wt, resets, target_ids, remaining, state,
        grad_o, dpre_o, right_o, xb_o, lhs_o, dz_o, dl_o, x_q, h_q, loss_o, bias_o,
        keep, valid, targets, feats_v, turned, pb, x1, xb, hb, db, ob, dy, u, r, r_t, w, start, gates, cells, prevs, hs, dhs, dz16,
        logits, dl, top, part, dh, loss,
        sem_in, sem_out, send_y, recv_y, send_f, recv_f, send_b, recv_b, send_d, recv_d,
        send_x, recv_x, send_h, recv_h, send_z, recv_z, sem_l, sem_p,
    ):
        role = lax.axis_index("section")
        me = lax.axis_index("dp")
        loss[...] = jnp.zeros_like(loss)
        bias_o[...] = jnp.zeros_like(bias_o)

        def to(step, source, target, send, recv):
            return pltpu.make_async_remote_copy(
                source, target, send, recv, device_id={"section": role + step}, device_id_type=MESH
            )

        def span(c):
            return pl.ds(pl.multiple_of(c * CHUNK, CHUNK), CHUNK)

        def forward_copy(c, step):
            return to(step, hb.at[span(c)], xb.at[span(c)], send_f.at[c], recv_f.at[c])

        def backward_copy(c, step):
            return to(step, ob.at[span(c)], db.at[span(c)], send_b.at[c], recv_b.at[c])

        def feature_copy(step):
            return to(step, y2, x1, send_y.at[0], recv_y.at[0])

        def last_copy(c, step):
            return to(step, dy.at[span(c)], dy.at[span(c)], send_d.at[c], recv_d.at[c])

        def quad_copy(source, target, send, recv, k):
            return pltpu.make_async_remote_copy(
                source, target, send, recv, device_id={"dp": quad_peer(me, k)}, device_id_type=MESH
            )

        def input_copy(k):
            return quad_copy(x1, x_q.at[k - 1, 0], send_x.at[k - 1, 0], recv_x.at[k - 1, 0], k)

        def layer_copy(k):
            return quad_copy(
                xb, x_q.at[k - 1, 0, :, pl.ds(0, GW)], send_x.at[k - 1, 0], recv_x.at[k - 1, 0], k
            )

        def feats_copy(k):
            return quad_copy(feats_v, x_q.at[k - 1], send_x.at[k - 1, 0], recv_x.at[k - 1, 0], k)

        def hidden_copy(k):
            return quad_copy(pb, h_q.at[k - 1], send_h.at[k - 1, 0], recv_h.at[k - 1, 0], k)

        def each_peer(body):
            for k in range(1, QUAD):
                body(k)

        def each_chunk(body, first=0):
            def step(c, carry):
                body(c)
                return carry

            lax.fori_loop(first, chunks, step, 0)

        def turned_out(g, rows):
            copy = pltpu.make_async_copy(turned.at[pl.ds(0, rows)], lhs_o.at[g, pl.ds(0, rows)], sem_l.at[0])
            copy.start()
            copy.wait()

        def fetch(source, target):
            copy = pltpu.make_async_copy(source, target, sem_l.at[1])
            copy.start()
            copy.wait()

        def dpre_copy(c, k):
            rows = pl.ds(pl.multiple_of((c - SPLIT) * CHUNK, CHUNK), CHUNK)
            source = right_o.at[1, rows] if k == 3 else dl.at[span(c), pl.ds(0, 4 * FW)]
            return quad_copy(
                source, right_o.at[k - 1, rows], send_z.at[k - 1, c], recv_z.at[k - 1, c], 1 if k == 3 else k
            )

        def right_copy(k):
            return quad_copy(dz16, dz_o.at[k - 1], send_z.at[k - 1, 0], recv_z.at[k - 1, 0], k)

        def exchange(copy, c, first):
            @pl.when(c >= first)
            def _():
                copy(c, 2).start()
                copy(c, 1).start()

            @pl.when((c < chunks - 1) & (c + 1 >= first))
            def _():
                copy(c + 1, 2).wait_recv()
                copy(c + 1, 3).start()

        def exchanged(copy, first):
            if first == 0:
                copy(0, 2).wait_recv()
                copy(0, 3).start()

            def settle(c):
                for k in range(1, QUAD):
                    copy(c, k).wait_send()
                    if k != 2:
                        copy(c, k).wait_recv()

            each_chunk(settle, first)

        def inputs(which):
            if which == 0:
                pairs = [(feats, feats_v)]
                for m in range(4):
                    for half, (row, count) in enumerate(AB_PARTS):
                        target = w.at[pl.ds(0, count), pl.ds((2 * m + half) * FW, FW)]
                        pairs.append((ab.at[m, pl.ds(row, count)], target))
            elif which == 3:
                pairs = [(wt, w)]
            else:
                depth = FW if which == 1 else GW
                pairs = [
                    (ur.at[pl.ds(0, depth)], u.at[pl.ds(0, depth)]),
                    (ur.at[pl.ds(FW, GW)], r),
                    (rt, r_t),
                ]
            return [pltpu.make_async_copy(a, b, sem_in.at[i]) for i, (a, b) in enumerate(pairs)]

        for which in range(4):

            @pl.when(role == which)
            def _(which=which):
                for copy in inputs(which):
                    copy.start()

        @pl.when((role == 1) | (role == 2))
        def _():
            start[...] = jnp.zeros_like(start)
            for which in (1, 2):

                @pl.when(role == which)
                def _(which=which):
                    for half in range(2):
                        start[half, :, pl.ds(0, HID)] = state[which - 1, half]

            for t in range(n // 8):
                rows = pl.ds(8 * t, 8)
                kept = jnp.zeros((8, LANE), F32)
                if t < real_steps:
                    kept = 1.0 - jnp.broadcast_to(resets[:, t : t + 1], (8, LANE)).astype(F32)
                keep[rows, :] = kept

        @pl.when(role == 3)
        def _():
            left_words = jnp.broadcast_to(remaining[...], (8, LANE))
            for t in range(n // 8):
                rows = pl.ds(8 * t, 8)
                if t < real_steps:
                    valid[rows, :] = jnp.where(left_words > t, 1.0, 0.0)
                    targets[rows, :] = jnp.broadcast_to(target_ids[:, t : t + 1], (8, LANE))
                else:
                    valid[rows, :] = jnp.zeros((8, LANE), F32)
                    targets[rows, :] = jnp.full((8, LANE), -1, jnp.int32)

        barrier = pltpu.get_barrier_semaphore()

        @pl.when(role > 0)
        def _():
            pl.semaphore_signal(barrier, inc=1, device_id={"section": role - 1}, device_id_type=MESH)

        @pl.when(role < 3)
        def _():
            pl.semaphore_signal(barrier, inc=1, device_id={"section": role + 1}, device_id_type=MESH)

        for k in range(1, QUAD):
            pl.semaphore_signal(barrier, inc=1, device_id={"dp": quad_peer(me, k)}, device_id_type=MESH)
        pl.semaphore_wait(barrier, lax.min(role, 1) + lax.min(3 - role, 1) + QUAD - 1)

        @pl.when(role == 0)
        def _():
            feature_copy(1).start()
            for copy in inputs(0):
                copy.wait()
            each_peer(lambda k: feats_copy(k).start())
            turn_features(feats_v, turned)
            turned_out(QUAD - 1, LEFT0)
            feature_copy(1).wait_send()
            each_peer(lambda k: feats_copy(k).wait_send())
            for k in range(1, QUAD):
                feats_copy(k).wait_recv()
                fetch(x_q.at[k - 1], feats_v)
                turn_features(feats_v, turned)
                turned_out(k - 1, LEFT0)
            fetch(feats, feats_v)

            def pres_copy(c, m):
                slot = lax.rem(c, 2)
                target = logits.at[pl.ds(pl.multiple_of(slot * CHUNK, CHUNK), CHUNK), pl.ds(m * FW, FW)]
                return pltpu.make_async_copy(pres.at[m, span(c)], target, sem_p.at[slot, m])

            for m in range(4):
                pres_copy(chunks - 1, m).start()

            def chunk(i, carry):
                c = chunks - 1 - i

                @pl.when(c > 0)
                def _():
                    for m in range(4):
                        pres_copy(c - 1, m).start()

                for m in range(4):
                    pres_copy(c, m).wait()
                last_copy(c, 1).wait_recv()
                highway_chunk(span(c), pl.multiple_of(lax.rem(c, 2) * CHUNK, CHUNK), dy, feats_v, logits, gates, dl, w)

                exchange(dpre_copy, c, SPLIT)
                return carry

            lax.fori_loop(0, chunks, chunk, 0)
            copies = [
                pltpu.make_async_copy(gates.at[:, pl.ds(0, FW)], grad_o, sem_out.at[0]),
                pltpu.make_async_copy(dl.at[:, pl.ds(0, 4 * FW)], dpre_o, sem_out.at[1]),
            ]
            for copy in copies:
                copy.start()
            for at, width in fblocks(FW):
                cols = pl.ds(at, width)
                bias_o[:, cols] = jnp.sum(dl[:, cols].astype(F32), axis=0, keepdims=True)
            for copy in copies:
                copy.wait()

            exchanged(dpre_copy, SPLIT)

        @pl.when((role == 1) | (role == 2))
        def _():
            for which in (1, 2):

                @pl.when(role == which)
                def _(which=which):
                    for copy in inputs(which):
                        copy.wait()

            bias = r[pl.ds(HID, 1), :].astype(F32)

            @pl.when(role == 1)
            def _():
                feature_copy(-1).wait_recv()
                for at, width in fblocks(ZW):
                    cols = pl.ds(at, width)
                    gates[:, cols] = mm(x1[...], u[:, cols]) + bias[:, at : at + width]

            def chunk_forward(c, carry):
                @pl.when(role == 2)
                def _():
                    forward_copy(c, -1).wait_recv()
                    for at, width in fblocks(ZW):
                        cols = pl.ds(at, width)
                        gates[span(c), cols] = mm(xb[span(c), :], u[pl.ds(0, GW), cols]) + bias[:, at : at + width]

                carry = lstm_steps(c * steps, steps, keep, carry, r, gates, cells, prevs, hs)
                hb[span(c), :] = hs[span(c), :].astype(BF16)
                forward_copy(c, 1).start()
                return carry

            h0 = start[0].astype(BF16).astype(F32)
            lax.fori_loop(0, chunks, chunk_forward, (h0, start[1]))

            def turn_all(which):
                depth, rows = (FILT, LEFT1) if which == 1 else (HID, LEFT2)
                width = FW if which == 1 else GW
                copies = (input_copy if which == 1 else layer_copy, hidden_copy)
                turn_inputs(x1 if which == 1 else xb, pb, depth, turned)
                turned_out(QUAD - 1, rows)
                for g in range(QUAD - 1):
                    for copy in copies:
                        copy(g + 1).wait_recv()
                    fetch(x_q.at[g, 0, :, pl.ds(0, width)], feats_v.at[0, :, pl.ds(0, width)])
                    fetch(h_q.at[g], ob)
                    turn_inputs(feats_v.at[0], ob, depth, turned)
                    turned_out(g, rows)
                each_peer(lambda k: [copy(k).wait_send() for copy in copies])

            pb[...] = prevs[...].astype(BF16)
            each_peer(lambda k: hidden_copy(k).start())

            @pl.when(role == 1)
            def _():
                each_peer(lambda k: input_copy(k).start())
                turn_all(1)

            @pl.when(role == 2)
            def _():
                each_peer(lambda k: layer_copy(k).start())

            def chunk_backward(i, carry):
                c = chunks - 1 - i
                backward_copy(c, 1).wait_recv()
                dhs[span(c), :] = db[span(c), :].astype(F32)
                carry = lstm_back_steps(c * steps, steps, keep, start.at[1], carry, r_t, gates, cells, dhs)
                dz16[span(c), :] = gates[span(c), :].astype(BF16)

                dz_t = jnp.transpose(dz16[span(c), :])

                @pl.when(role == 1)
                def _():
                    for at, width in fblocks(FW):
                        value = jnp.transpose(mm(u[pl.ds(at, width), :], dz_t))
                        if at + width > FILT:
                            value = jnp.where(column_mask(at, width, FILT, CHUNK), value, 0.0)
                        dy[span(c), pl.ds(at, width)] = value.astype(BF16)
                    last_copy(c, -1).start()

                @pl.when(role == 2)
                def _():
                    for at, width in fblocks(GW):
                        value = jnp.transpose(mm(u[pl.ds(at, width), :], dz_t))
                        if at + width > HID:
                            value = jnp.where(column_mask(at, width, HID, CHUNK), value, 0.0)
                        ob[span(c), pl.ds(at, width)] = value.astype(BF16)
                    backward_copy(c, -1).start()

                return carry

            zero = jnp.zeros((8, GW), F32)
            lax.fori_loop(0, chunks, chunk_backward, (zero, zero))

            own_right = pltpu.make_async_copy(dz16, dz_o.at[QUAD - 1], sem_out.at[1])
            own_right.start()
            each_peer(lambda k: right_copy(k).start())

            @pl.when(role == 1)
            def _():
                each_chunk(lambda c: last_copy(c, -1).wait_send())

            @pl.when(role == 2)
            def _():
                each_chunk(lambda c: backward_copy(c, -1).wait_send())
                turn_all(2)

            own_right.wait()
            each_peer(lambda k: right_copy(k).wait_send())
            each_peer(lambda k: right_copy(k).wait_recv())

            def sent(c, carry):
                forward_copy(c, 1).wait_send()
                return carry

            lax.fori_loop(0, chunks, sent, 0)

        @pl.when(role == 3)
        def _():
            for copy in inputs(3):
                copy.wait()
            ob[...] = jnp.zeros_like(ob)
            done = 0
            for count in GROUPS_OUT:
                rows = pl.ds(done * CHUNK, count * CHUNK)
                for c in range(done, done + count):
                    forward_copy(c, -1).wait_recv()
                value = xb[rows, pl.ds(5 * LANE, LANE)].astype(F32)
                value = jnp.where(lanes(count * CHUNK) + 5 * LANE == HID, 1.0, value)
                xb[rows, pl.ds(5 * LANE, LANE)] = value.astype(BF16)
                output_rows(
                    done * CHUNK, count * CHUNK, xb, w, targets, valid, logits, dl, top, part, dh, loss, ob
                )
                for c in range(done, done + count):
                    backward_copy(c, -1).start()
                done += count
            copies = [
                pltpu.make_async_copy(xb, xb_o, sem_out.at[0]),
                pltpu.make_async_copy(dl, dl_o, sem_out.at[1]),
            ]
            for copy in copies:
                copy.start()
            for c in range(chunks):
                backward_copy(c, -1).wait_send()
            for copy in copies:
                copy.wait()

        loss_o[...] = loss[...]

    most = max(GROUPS_OUT) * CHUNK
    sems = pltpu.SemaphoreType.DMA
    outs = [
        ((n, FW), F32), ((n, 4 * FW), BF16), ((QUAD - 1, n - SPLIT * CHUNK, 4 * FW), BF16), ((n, GW), BF16),
        ((QUAD, LEFT_ROOM, n), BF16), ((QUAD, n, ZW), BF16), ((n, VW), BF16), ((QUAD - 1, 2, n, FW), BF16),
        ((QUAD - 1, n, GW), BF16),
    ]
    scratch = [
        vmem((n, LANE), F32), vmem((n, LANE), F32), vmem((n, LANE), jnp.int32),
        vmem((2, n, FW), BF16), vmem((LEFT0, n), BF16), vmem((n, GW), BF16),
        vmem((n, FW), BF16), vmem((n, GW), BF16), vmem((n, GW), BF16), vmem((n, GW), BF16), vmem((n, GW), BF16),
        vmem((n, FW), BF16), vmem((FW, ZW), BF16), vmem((GW, ZW), BF16), vmem((ZW, GW), BF16), vmem(wt.shape, BF16),
        vmem((2, 8, GW), F32), vmem((n, ZW), F32), vmem((n, GW), F32), vmem((n, GW), F32), vmem((n, GW), F32),
        vmem((n, GW), F32), vmem((n, ZW), BF16),
        vmem((most, VW), F32), vmem((n, VW), BF16), vmem((most, LANE), F32), vmem((2, most, LANE), F32),
        vmem((depth_w, LANE), F32), vmem((1, LANE), F32),
        dmas(12), dmas(3), dmas(1), dmas(1), dmas(chunks), dmas(chunks), dmas(chunks), dmas(chunks), dmas(chunks), dmas(chunks),
        sems((QUAD - 1, chunks)), sems((QUAD - 1, chunks)), sems((QUAD - 1, chunks)), sems((QUAD - 1, chunks)),
        sems((QUAD - 1, chunks)), sems((QUAD - 1, chunks)), dmas(2), sems((2, 4)),
    ]
    return pl.pallas_call(
        kernel,
        out_shape=[jax.ShapeDtypeStruct(shape, dtype) for shape, dtype in outs]
        + [jax.ShapeDtypeStruct((1, LANE), F32), jax.ShapeDtypeStruct((1, FW), F32)],
        in_specs=[ANYWHERE] * 7 + [ON_CHIP] * 4,
        out_specs=[ANYWHERE] * 9 + [ON_CHIP] * 2,
        scratch_shapes=scratch,
        compiler_params=pltpu.CompilerParams(vmem_limit_bytes=62 << 20, collective_id=3, has_side_effects=True),
        name="recurrent",
    )(y2, feats, pres, ab, ur, rt, wt, resets, target_ids, remaining, state)


FORM = (
    (FILT, 9, 4 * (FILT + 1), CONV_END, CONV_TILES, 32),
    (4 * HID, 24, FILT + HID + 1, 0, 0, 16),
    (4 * HID, 24, 2 * HID + 1, 0, 0, 16),
    (VOCAB, 79, HID + 1, 0, 0, 16),
)


def slab(role, dest, share):
    width, pitch, rows, before, lead, period = FORM[role]
    low = lax.max if not isinstance(dest, int) else max
    high = lax.min if not isinstance(dest, int) else min
    one = (lambda v: v) if isinstance(dest, int) else jnp.int32
    start = low(one(share) * dest - before, one(0))
    first = start // width // period * period
    end = high((share * (dest + 1) - before + width - 1) // width, one(rows))
    count = low((end - first + 15) // 16, one(0)) * pitch
    tile = lead + first // 16 * pitch
    if lead:
        if isinstance(dest, int):
            if dest == 0:
                tile, count = 0, count + lead
        else:
            head = lax.max(1 - dest, 0)
            tile = tile - lead * head
            count = count + lead * head
    return first, tile, count


def slab_pieces(count, size):
    return (count + size - 1) // size


def gather_sum_call(tiles, groups, share):
    pair = 2
    across = groups // pair
    size = 80 if across <= 4 else 32
    pieces = max(slab_pieces(slab(3, dest, share)[2], size) for dest in range(groups))
    room = pieces * size
    line = across <= 4
    slots = across + 1 if line else across - 1
    MESH = pl.DeviceIdType.MESH

    def kernel(
        tiles, out, own, got1, got2, acc, own_sem, send1, recv1, send2, recv2, out_sem,
    ):
        role = lax.axis_index("section")
        me = lax.axis_index("dp")
        mine, side = me // pair, lax.rem(me, pair)
        other = mine * pair + (1 - side)

        def at_place(place):
            return {"dp": place * pair + side}

        def part(ref, slot, p):
            return ref.at[slot, pl.ds(pl.multiple_of(p * size, size), size)]

        def span(p):
            return pl.ds(pl.multiple_of(p * size, size), size)

        def loop(count, body):
            def step(p, carry):
                body(p)
                return carry

            lax.fori_loop(0, count, step, 0)

        def run(shape_of):
            def count_to(place, which):
                return shape_of(place * pair + which)[1]

            def own_copy(place, p):
                tile, _ = shape_of(place * pair + side)
                return pltpu.make_async_copy(
                    tiles.at[pl.ds(tile + p * size, size)], part(own, place, p), own_sem.at[place, p]
                )

            def first_copy(place, p):
                tile, _ = shape_of(place * pair + 1 - side)
                return pltpu.make_async_remote_copy(
                    tiles.at[pl.ds(tile + p * size, size)], part(got1, place, p), send1.at[place, p], recv1.at[place, p],
                    device_id={"dp": other}, device_id_type=MESH,
                )

            def begin(place):
                loop(count_to(place, 1 - side), lambda p: first_copy(place, p).start())
                loop(count_to(place, side), lambda p: own_copy(place, p).start())

            def hop_copy(place, up, p):
                if line:
                    target = mine + 1 if up else mine - 1
                    slot = jnp.where(place == mine + 1, across, place) if up else place
                else:
                    target = place
                    slot = lax.rem(place - mine + across, across) - 1
                return pltpu.make_async_remote_copy(
                    part(own, place, p), part(got2, slot, p), send2.at[place, p], recv2.at[slot, p],
                    device_id=at_place(target), device_id_type=MESH,
                )

            def arrived(slot, p):
                return pltpu.make_async_remote_copy(
                    part(own, 0, p), part(got2, slot, p), send2.at[0, p], recv2.at[slot, p],
                    device_id=at_place(lax.rem(mine + 1, across)), device_id_type=MESH,
                )

            def forward(place, up, has_before):
                def body(p):
                    own_copy(place, p).wait()
                    first_copy(place, p).wait_recv()
                    at = span(p)
                    own[place, at] = (own[place, at].astype(F32) + got1[place, at].astype(F32)).astype(BF16)
                    hop_copy(place, up, p).start()

                def body_sum(p):
                    own_copy(place, p).wait()
                    first_copy(place, p).wait_recv()
                    arrived(place, p).wait_recv()
                    at = span(p)
                    total = own[place, at].astype(F32) + got1[place, at].astype(F32) + got2[place, at].astype(F32)
                    own[place, at] = total.astype(BF16)
                    hop_copy(place, up, p).start()

                count = count_to(place, side)
                if not line:
                    loop(count, body)
                    return

                @pl.when(has_before)
                def _():
                    loop(count, body_sum)

                @pl.when(jnp.logical_not(has_before))
                def _():
                    loop(count, body)

            if line:
                for k in range(across - 1):

                    @pl.when(k < mine)
                    def _(k=k):
                        begin(k)

                    @pl.when(k < across - 1 - mine)
                    def _(k=k):
                        begin(across - 1 - k)

                begin(mine)
                for k in range(across - 1):

                    @pl.when(k < mine)
                    def _(k=k):
                        forward(k, False, mine < across - 1)

                    @pl.when(k < across - 1 - mine)
                    def _(k=k):
                        forward(across - 1 - k, True, mine > 0)

            else:
                for k in range(1, across):
                    begin(lax.rem(mine + k, across))
                begin(mine)
                for k in range(1, across):
                    forward(lax.rem(mine + k, across), True, None)

            def settle(p):
                own_copy(mine, p).wait()
                first_copy(mine, p).wait_recv()
                at = span(p)
                acc[at] = own[mine, at].astype(F32) + got1[mine, at].astype(F32)

            def add(slot):
                def body(p):
                    arrived(slot, p).wait_recv()
                    at = span(p)
                    acc[at] += got2[slot, at].astype(F32)

                return body

            mine_count = count_to(mine, side)
            loop(mine_count, settle)
            if line:

                @pl.when(mine < across - 1)
                def _():
                    loop(mine_count, add(mine))

                @pl.when(mine > 0)
                def _():
                    loop(mine_count, add(across))

            else:
                for k in range(1, across):
                    loop(mine_count, add(k - 1))

            def out_copy(p):
                return pltpu.make_async_copy(acc.at[span(p)], out.at[span(p)], out_sem.at[p])

            loop(mine_count, lambda p: out_copy(p).start())
            loop(mine_count, lambda p: out_copy(p).wait())
            for place in range(across):
                loop(count_to(place, 1 - side), lambda p, place=place: first_copy(place, p).wait_send())

                @pl.when(place != mine)
                def _(place=place):
                    loop(count_to(place, side), lambda p: hop_copy(place, True, p).wait_send())

        def shape_of(dest):
            _, tile, count = slab(3, dest, share)
            return tile, slab_pieces(count, size)

        @pl.when(role == 3)
        def _():
            barrier = pltpu.get_barrier_semaphore()
            pl.semaphore_signal(barrier, inc=1, device_id={"dp": other}, device_id_type=MESH)
            for k in range(1, across):
                peer = at_place(lax.rem(mine + k, across))
                pl.semaphore_signal(barrier, inc=1, device_id=peer, device_id_type=MESH)
            pl.semaphore_wait(barrier, across)
            run(shape_of)

    sems = pltpu.SemaphoreType.DMA
    return pl.pallas_call(
        kernel,
        out_shape=jax.ShapeDtypeStruct((room, 16, LANE), F32),
        in_specs=[ANYWHERE],
        out_specs=ANYWHERE,
        scratch_shapes=[
            vmem((across, room, 16, LANE), BF16), vmem((across, room, 16, LANE), BF16),
            vmem((slots, room, 16, LANE), BF16), vmem((room, 16, LANE), F32),
            sems((across, pieces)), sems((across, pieces)), sems((across, pieces)),
            sems((across, pieces)), sems((slots, pieces)), sems((pieces,)),
        ],
        compiler_params=pltpu.CompilerParams(vmem_limit_bytes=62 << 20, collective_id=1, has_side_effects=True),
        name="gather_sum",
    )(tiles)


BLOCK_ROWS = (7, 7, 7)


def finish_call(lhs, dz, dpre, rights, conv, bias, loss, after, groups, share):
    n = lhs.shape[2]
    quads = groups // QUAD
    MESH = pl.DeviceIdType.MESH

    def most_blocks(role):
        width = FORM[role][1]
        lead = FORM[role][4]
        most = 0
        for dest in range(groups):
            count = slab(role, dest, share)[2]
            if lead and dest == 0:
                count -= lead
            most = max(most, -(-(count // width) // BLOCK_ROWS[role]))
        return most

    blocks = [most_blocks(role) for role in range(3)]
    room = max(
        FORM[role][4] + blocks[role] * BLOCK_ROWS[role] * FORM[role][1] for role in range(3)
    )
    left_rows = max(blocks[role] * BLOCK_ROWS[role] * 16 for role in range(3))
    most = max(blocks)

    def kernel(
        lhs, dz, dpre, late, early, conv, bias, loss, after, out, small_out,
        left, dpre_v, sent, got, acc, convs, lead_sum, small, got_small,
        sem_left, sem_right, send, recv, send_c, recv_c, small_send, small_recv, sem_out,
    ):
        role = lax.axis_index("section")
        me = lax.axis_index("dp")
        place, quad = lax.rem(me, QUAD), me // QUAD

        def across_peer(k):
            return {"dp": place + QUAD * lax.rem(quad + k, quads)}

        barrier = pltpu.get_barrier_semaphore()
        for k in range(1, QUAD):
            pl.semaphore_signal(barrier, inc=1, device_id={"dp": quad_peer(me, k)}, device_id_type=MESH)
        for k in range(1, quads):
            pl.semaphore_signal(barrier, inc=1, device_id=across_peer(k), device_id_type=MESH)

        def right_load(b):
            return pltpu.make_async_copy(
                dz.at[:, :, pl.ds(GW * b, GW)], dpre_v.at[:, b, :, pl.ds(0, GW)], sem_right.at[b]
            )

        def right_loads0():
            copies = []
            cut = SPLIT * CHUNK
            for b in range(4):
                cols = pl.ds(FW * b, FW)
                pairs = [
                    (early.at[:, :, cols], dpre_v.at[pl.ds(0, QUAD - 1), b, pl.ds(0, cut)]),
                    (late.at[:, :, cols], dpre_v.at[pl.ds(0, QUAD - 1), b, pl.ds(cut, n - cut)]),
                    (dpre.at[:, cols], dpre_v.at[QUAD - 1, b]),
                ]
                copies += [pltpu.make_async_copy(x, y, sem_right.at[4 + 3 * b + i]) for i, (x, y) in enumerate(pairs)]
            return copies

        def conv_load():
            return pltpu.make_async_copy(conv, convs.at[QUAD - 1], sem_right.at[16])

        @pl.when(role == 0)
        def _():
            for copy in right_loads0():
                copy.start()
            conv_load().start()

        @pl.when((role == 1) | (role == 2))
        def _():
            for b in range(4):
                right_load(b).start()

        pl.semaphore_wait(barrier, QUAD - 1 + quads - 1)

        small[...] = jnp.zeros_like(small)

        @pl.when(role == 0)
        def _():
            small[0, :, pl.ds(0, FW)] = bias[...]

        @pl.when(role == 3)
        def _():
            small[0, :, pl.ds(FW, LANE)] = loss[...]

        def small_copy(k):
            if k < QUAD:
                source, target = small.at[0], {"dp": quad_peer(me, k)}
            else:
                source, target = small.at[1], across_peer(k - QUAD + 1)
            return pltpu.make_async_remote_copy(
                source, got_small.at[k - 1], small_send.at[k - 1], small_recv.at[k - 1],
                device_id=target, device_id_type=MESH,
            )

        for k in range(1, QUAD):
            small_copy(k).start()

        def across_small():
            for k in range(1, QUAD):
                small_copy(k).wait_recv()
            small[1] = small[0] + got_small[0] + got_small[1] + got_small[2]
            for k in range(QUAD, QUAD + quads - 1):
                small_copy(k).start()

        def share_small():
            total = small[1]
            for k in range(QUAD, QUAD + quads - 1):
                small_copy(k).wait_recv()
                total = total + got_small[k - 1]
            for k in range(1, QUAD):
                small_copy(k).wait_send()
            small_out[...] = total

        def conv_copy(slot, target):
            return pltpu.make_async_remote_copy(
                conv, convs.at[slot], send_c.at[slot], recv_c.at[slot], device_id={"dp": target}, device_id_type=MESH
            )

        def run(which):
            width, pitch, rows, _, lead, _ = FORM[which]
            size = BLOCK_ROWS[which]
            block_tiles = size * pitch

            def geometry(k):
                dest = place + QUAD * lax.rem(quad + k, quads)
                first, _, count = slab(which, dest, share)
                if lead:
                    head = lax.max(1 - dest, 0)
                    count = count - lead * head
                else:
                    head = 0
                return first, (count // pitch + size - 1) // size, head

            def left_copy(k):
                height = blocks[which] * size * 16
                first = lax.min(geometry(k)[0], LEFT_ROOM - height)
                span = pl.ds(pl.multiple_of(first, 16), height)
                return pltpu.make_async_copy(
                    lhs.at[:, span], left.at[lax.rem(k, 2), :, pl.ds(0, blocks[which] * size * 16)], sem_left.at[lax.rem(k, 2)]
                )

            def block_copy(k, b):
                span = pl.ds(CONV_TILES + b * block_tiles, block_tiles)
                return pltpu.make_async_remote_copy(
                    sent.at[k - 1, span], got.at[k - 1, span], send.at[k - 1, b], recv.at[k - 1, b],
                    device_id=across_peer(k), device_id_type=MESH,
                )

            def lead_copy(k):
                span = pl.ds(0, CONV_TILES)
                return pltpu.make_async_remote_copy(
                    sent.at[k - 1, span], got.at[k - 1, span], send.at[k - 1, most], recv.at[k - 1, most],
                    device_id=across_peer(k), device_id_type=MESH,
                )

            def put(k, own, at, value):
                if own:
                    acc[at] = value
                else:
                    sent[k - 1, at] = value.astype(BF16)

            def block(k, own, b, first):
                here = pl.ds(pl.multiple_of(b * size * 16, 16), size * 16)
                base = CONV_TILES + b * block_tiles
                if which == 0:
                    row = lax.broadcasted_iota(jnp.int32, (size * 16, n), 0) + first + b * size * 16
                    start = first + b * size * 16
                    low = lax.min(start // (FILT + 1), 3)
                    high = lax.min((start + size * 16 - 1) // (FILT + 1), 3)
                    edge = (FILT + 1) * (low + 1)
                    lefts = [left[lax.rem(k, 2), g, here, :] for g in range(QUAD)]
                    near = [jnp.where(row < edge, x, jnp.zeros_like(x)) for x in lefts]
                    for col, wide in fblocks(FW):
                        value = jnp.zeros((size * 16, wide), F32)
                        for g in range(QUAD):
                            value = value + mm(near[g], dpre_v[g, low, :, pl.ds(col, wide)])
                        for r in range(size):
                            for c in range(wide // LANE):
                                tile = value[16 * r : 16 * r + 16, LANE * c : LANE * c + LANE]
                                put(k, own, base + r * pitch + col // LANE + c, tile)

                    @pl.when(high > low)
                    def _():
                        far = [jnp.where(row < edge, jnp.zeros_like(x), x) for x in lefts]
                        for col, wide in fblocks(FW):
                            value = jnp.zeros((size * 16, wide), F32)
                            for g in range(QUAD):
                                value = value + mm(far[g], dpre_v[g, high, :, pl.ds(col, wide)])
                            for r in range(size):
                                for c in range(wide // LANE):
                                    tile = value[16 * r : 16 * r + 16, LANE * c : LANE * c + LANE]
                                    at = base + r * pitch + col // LANE + c
                                    old = acc[at] if own else sent[k - 1, at].astype(F32)
                                    put(k, own, at, old + tile)

                else:
                    for col, wide in fblocks(ZW):
                        value = jnp.zeros((size * 16, wide), F32)
                        for g in range(QUAD):
                            value = value + mm(left[lax.rem(k, 2), g, here, :], dpre_v[g, col // GW, :, pl.ds(col % GW, wide)])
                        for r in range(size):
                            for c in range(wide // LANE):
                                tile = value[16 * r : 16 * r + 16, LANE * c : LANE * c + LANE]
                                put(k, own, base + r * pitch + col // LANE + c, tile)

            def loop(count, body):
                def step(b, carry):
                    body(b)
                    return carry

                lax.fori_loop(0, count, step, 0)

            left_copy(jnp.int32(1 % quads)).start()
            if which == 0:

                @pl.when(place > 0)
                def _():
                    for k in range(1, QUAD):

                        @pl.when(place == k)
                        def _(k=k):
                            conv_copy(k - 1, me - k).start()

                for copy in right_loads0():
                    copy.wait()
                conv_load().wait()
            else:
                for b in range(4):
                    right_load(b).wait()

            if which == 0:

                @pl.when(place == 0)
                def _():
                    for k in range(1, QUAD):
                        conv_copy(k - 1, me + k).wait_recv()
                    total = convs[0].astype(F32)
                    for k in range(1, QUAD):
                        total = total + convs[k].astype(F32)
                    lead_sum[...] = total

            def slab_of(k, own):
                left_copy(k).wait()
                if not own:
                    left_copy(lax.rem(k + 1, quads)).start()
                first, count, head = geometry(k)
                if which == 0:

                    @pl.when(head > 0)
                    def _():
                        if own:
                            acc[pl.ds(0, CONV_TILES)] = lead_sum[...]
                        else:
                            sent[k - 1, pl.ds(0, CONV_TILES)] = lead_sum[...].astype(BF16)
                            lead_copy(k).start()

                def work(b):
                    block(k, own, b, first)
                    if not own:
                        block_copy(k, b).start()

                loop(count, work)

            def others(body):
                def step(k, carry):
                    body(k)
                    return carry

                lax.fori_loop(1, quads, step, 0)

            others(lambda k: slab_of(k, False))
            across_small()
            slab_of(jnp.int32(0), True)
            share_small()

            _, mine, head = geometry(0)
            def join(k):
                def add(b):
                    block_copy(k, b).wait_recv()
                    span = pl.ds(CONV_TILES + b * block_tiles, block_tiles)
                    acc[span] += got[k - 1, span].astype(F32)

                loop(mine, add)
                if which == 0:

                    @pl.when(head > 0)
                    def _():
                        lead_copy(k).wait_recv()
                        span = pl.ds(0, CONV_TILES)
                        acc[span] += got[k - 1, span].astype(F32)

            others(join)

            span = blocks[which] * block_tiles
            if which == 0:

                @pl.when(head > 0)
                def _():
                    copy = pltpu.make_async_copy(
                        acc.at[pl.ds(0, CONV_TILES + span)], out.at[pl.ds(0, CONV_TILES + span)], sem_out.at[0]
                    )
                    copy.start()
                    copy.wait()

                @pl.when(head == 0)
                def _():
                    copy = pltpu.make_async_copy(acc.at[pl.ds(CONV_TILES, span)], out.at[pl.ds(0, span)], sem_out.at[0])
                    copy.start()
                    copy.wait()

            else:
                copy = pltpu.make_async_copy(acc.at[pl.ds(CONV_TILES, span)], out.at[pl.ds(0, span)], sem_out.at[0])
                copy.start()
                copy.wait()

            def sent_all(k):
                _, count, head = geometry(k)
                loop(count, lambda b: block_copy(k, b).wait_send())
                if which == 0:

                    @pl.when(head > 0)
                    def _():
                        lead_copy(k).wait_send()

            others(sent_all)

            if which == 0:
                for k in range(1, QUAD):

                    @pl.when(place == k)
                    def _(k=k):
                        conv_copy(k - 1, me - k).wait_send()

        for which in range(3):

            @pl.when(role == which)
            def _(which=which):
                run(which)

        @pl.when(role == 3)
        def _():
            across_small()
            share_small()

        for k in range(QUAD, QUAD + quads - 1):
            small_copy(k).wait_send()

    sems = pltpu.SemaphoreType.DMA
    full = CONV_TILES + max(blocks[role] * BLOCK_ROWS[role] * FORM[role][1] for role in range(3))
    smalls = QUAD + quads - 2
    return pl.pallas_call(
        kernel,
        out_shape=[jax.ShapeDtypeStruct((full, 16, LANE), F32), jax.ShapeDtypeStruct((1, FW + LANE), F32)],
        in_specs=[ANYWHERE] * 6 + [ON_CHIP] * 2 + [ANYWHERE],
        out_specs=[ANYWHERE, ON_CHIP],
        scratch_shapes=[
            vmem((2, QUAD, left_rows, n), BF16), vmem((QUAD, 4, n, FW), BF16),
            vmem((quads - 1, full, 16, LANE), BF16), vmem((quads - 1, full, 16, LANE), BF16),
            vmem((full, 16, LANE), F32), vmem((QUAD, CONV_TILES, 16, LANE), BF16), vmem((CONV_TILES, 16, LANE), F32),
            vmem((2, 1, FW + LANE), F32), vmem((smalls, 1, FW + LANE), F32),
            sems((2,)), sems((17,)), sems((quads - 1, most + 1)), sems((quads - 1, most + 1)),
            sems((QUAD - 1,)), sems((QUAD - 1,)), sems((smalls,)), sems((smalls,)), sems((1,)),
        ],
        compiler_params=pltpu.CompilerParams(vmem_limit_bytes=62 << 20, collective_id=5, has_side_effects=True),
        name="finish",
    )(lhs, dz, dpre, *rights, conv, bias, loss, after)


def sections_sum_call(small):
    count = lax.axis_size("section")

    def kernel(mine, out, held, send, recv):
        me = lax.axis_index("section")
        barrier = pltpu.get_barrier_semaphore()

        def peer(k):
            return {"section": lax.rem(me + k, count)}

        for k in range(1, count):
            pl.semaphore_signal(barrier, inc=1, device_id=peer(k), device_id_type=pl.DeviceIdType.MESH)
        pl.semaphore_wait(barrier, count - 1)
        copies = [
            pltpu.make_async_remote_copy(
                mine, held.at[k], send.at[k], recv.at[k], device_id=peer(k), device_id_type=pl.DeviceIdType.MESH
            )
            for k in range(1, count)
        ]
        for copy in copies:
            copy.start()
        total = mine[...]
        for k, copy in enumerate(copies):
            copy.wait_recv()
            total = total + held[k + 1]
        out[...] = total
        for copy in copies:
            copy.wait_send()

    return pl.pallas_call(
        kernel,
        out_shape=jax.ShapeDtypeStruct(small.shape, F32),
        in_specs=[ON_CHIP],
        out_specs=ON_CHIP,
        scratch_shapes=[vmem((count,) + small.shape, F32), dmas(count), dmas(count)],
        compiler_params=pltpu.CompilerParams(collective_id=2, has_side_effects=True),
        name="sections_sum",
    )(small)


def pack_call(summed, summed3, groups, share):
    rooms = (summed.shape[0] * 16, summed3.shape[0] * 16)
    chunks = share // LANE
    margin = 1280
    slab_rows = 10624
    flat_rows = margin + max(10752, chunks + 1280)

    def kernel(summed, summed3, out, rows_v, spaced, flat, sem):
        role = lax.axis_index("section")
        me = lax.axis_index("dp")
        zero = jnp.zeros((64, LANE), F32)

        def clear(i, carry):
            flat[pl.ds(pl.multiple_of(i * 64, 64), 64), :] = zero
            return carry

        def fetch(source, room):
            return pltpu.make_async_copy(source, rows_v.at[pl.ds(0, room)], sem.at[0])

        @pl.when(role < 3)
        def _():
            fetch(summed, rooms[0]).start()

        @pl.when(role == 3)
        def _():
            fetch(summed3, rooms[1]).start()

        lax.fori_loop(0, flat_rows // 64, clear, 0)

        @pl.when(role < 3)
        def _():
            fetch(summed, rooms[0]).wait()

        @pl.when(role == 3)
        def _():
            fetch(summed3, rooms[1]).wait()

        lane = lanes()

        for which in range(4):
            width, pitch, rows, before, lead, period = FORM[which]
            if which == 0:
                blocks, cols, tiles = 1, FILT, 9
            elif which == 3:
                blocks, cols, tiles = 1, VOCAB, 79
            else:
                blocks, cols, tiles = 4, HID, 6
            stride = period * width // LANE
            most = max(slab(which, dest, share)[2] for dest in range(groups))
            groups8 = -(-(-(-most // pitch) * 16) // (8 * period))

            @pl.when(role == which)
            def _(which=which):
                first, _, count = slab(which, me, share)
                skip = lead * lax.max(1 - me, 0)
                step_rows = pitch * 49 + (pitch * 49 + 1) % 2

                def space(rt, carry):
                    for c in range(pitch):
                        for half in range(2):
                            at = pl.multiple_of((skip + rt * pitch + c) * 16 + 8 * half, 8)
                            spaced[pl.ds(rt * step_rows + 49 * c + 24 * half, 8, stride=3), :] = rows_v[pl.ds(at, 8), :]
                    return carry

                lax.fori_loop(0, (count - skip) // pitch, space, 0)
                base = margin + before // LANE + stride * (first // period) - chunks * me

                hop = period // 16 * step_rows
                half = period // 2

                def place(group, n, b):
                    number = first + period * (8 * group + sublanes()) + n
                    flat_at = before % LANE + width * n + cols * b
                    source = n // 16 * step_rows + 3 * lax.rem(n, 16) + 8 * group * hop + 49 * tiles * b
                    to = base + flat_at // LANE + stride * 8 * group
                    return number < rows, lax.rem(flat_at, LANE), source, to

                def run(places, low, high, lasts):
                    taken = [
                        [spaced[pl.ds(source + 49 * j, 8, stride=hop), :] for j in range(low, min(high, tiles))]
                        for _, _, source, _ in places
                    ]
                    edges = [j for j in range(low, high) if j == 0 or j >= tiles - 1]
                    old = [
                        {j: flat[pl.ds(to + j, 8, stride=stride), :] for j in edges} for _, _, _, to in places
                    ]
                    values, ends = [], []
                    for (keep, turn, _, _), pieces, olds, last in zip(places, taken, old, lasts):
                        turned = [last] + [pltpu.roll(jnp.where(keep, x, 0.0), turn, 1) for x in pieces]
                        for j in range(low, high):
                            here = turned[j - low + 1] if j < tiles else turned[-1]
                            value = here if j == tiles else jnp.where(lane >= turn, here, turned[j - low])
                            if j in olds:
                                at = lane + LANE * j - turn
                                value = jnp.where((at >= 0) & (at < cols), value, olds[j])
                            values.append(value)
                        ends.append(turned[-1])
                    at = 0
                    for _, _, _, to in places:
                        for j in range(low, high):
                            flat[pl.ds(to + j, 8, stride=stride), :] = values[at]
                            at += 1
                    return ends

                def row(i, carry):
                    group, n = i // half, lax.rem(i, half)
                    zero = jnp.zeros((8, LANE), F32)
                    if blocks == 4:
                        for b in range(2):
                            places = [place(group, m, c) for m in (n, n + half) for c in (b, b + 2)]
                            run(places, 0, tiles + 1, [zero] * 4)
                    else:
                        places = [place(group, m, 0) for m in (n, n + half)]
                        ends = [zero] * 2
                        for low in range(0, tiles + 1, 20):
                            ends = run(places, low, min(low + 20, tiles + 1), ends)
                    return carry

                @pl.when(count > 0)
                def _():
                    lax.fori_loop(0, half * groups8, row, 0)

        @pl.when((role == 0) & (me == 0))
        def _():
            lane1 = lanes(1)

            def piece(row_at, flat_at, low, size):
                edge = flat_at - low
                turn = edge % LANE
                to = margin + (edge - turn) // LANE
                first, end = low // LANE, (low + size - 1) // LANE
                last = jnp.zeros((1, LANE), F32)
                for j in range(first, end + 2):
                    least, most = max(low + turn - LANE * j, 0), min(low + size + turn - LANE * j, LANE)
                    here = last
                    if j <= end:
                        here = rows_v[row_at + 16 * j : row_at + 16 * j + 1, :]
                        here = pltpu.roll(here, turn, 1) if turn else here
                    if most > least:
                        value = jnp.where(lane1 >= turn, here, last) if turn else here
                        at = to + j
                        if least > 0 or most < LANE:
                            value = jnp.where((lane1 >= least) & (lane1 < most), value, flat[at : at + 1, :])
                        flat[at : at + 1, :] = value
                    last = here

            for k in range(1, 8):
                n = NFILT[k - 1]
                for i in range(k * D_CHAR + 1):
                    number = i + i // D_CHAR if i < k * D_CHAR else 15
                    piece(number // 16 * 144 + number % 16, KOFF[k - 1] + n * i, COLS[k - 1], n)
            for a in range(CHAR_V):
                piece(72 * 16 + a, D_CHAR * a, 0, D_CHAR)

        copy = pltpu.make_async_copy(flat.at[pl.ds(margin, chunks)], out, sem.at[0])
        copy.start()
        copy.wait()

    return pl.pallas_call(
        kernel,
        out_shape=jax.ShapeDtypeStruct((chunks, LANE), F32),
        in_specs=[ANYWHERE] * 2,
        out_specs=ANYWHERE,
        scratch_shapes=[
            vmem((slab_rows, LANE), F32), vmem((31104, LANE), F32), vmem((flat_rows, LANE), F32), dmas(1),
        ],
        compiler_params=pltpu.CompilerParams(vmem_limit_bytes=LIMIT),
        name="pack",
    )(summed.reshape(rooms[0], LANE), summed3.reshape(rooms[1], LANE))


def shards(char_ids, target_ids, remaining, resets, start_state, section_params):
    rows, steps = char_ids.shape[:2]
    groups = lax.axis_size("dp")
    packed = section_params.shape[1]
    share = packed // groups
    n = rows * (steps + 1)

    ids = jnp.pad(
        char_ids.transpose(1, 0, 2), ((0, 1), (0, 0), (0, LANE - WORD_CHARS)), constant_values=-1
    ).reshape(n, LANE)
    km, e8, ab, ur, rt, wt = unpack_all(section_params)
    y2, *char_saved = char_forward_call(ids, km, e8, ab)
    feats, pres, total, emb = char_saved
    grad, dpre, late, xb, lhs, dz, dl, _, _, loss, bias = recurrent_call(
        y2, feats, pres, ab, ur, rt, wt, resets, target_ids, remaining.reshape(rows, 1), start_state
    )
    tiles3 = output_weights_call(xb, dl)
    summed3 = gather_sum_call(tiles3, groups, share)
    conv, early = char_backward_call(ids, grad, km, (total, emb), dpre)
    summed, small = finish_call(lhs, dz, dpre, (late, early), conv, bias, loss, summed3, groups, share)
    small = sections_sum_call(small)
    flat = pack_call(summed, summed3, groups, share)
    mean_loss = small[0, FW] / (groups * rows * steps)
    return mean_loss, flat.reshape(1, share), small[0, :FILT]


def solution(mesh):
    in_specs = (
        P("dp", None, None),
        P("dp", None),
        P("dp"),
        P("dp", None),
        P(None, None, "dp", None),
        P("section", None),
    )
    out_specs = (P(), P("section", "dp"), P())
    return jax.shard_map(shards, mesh=mesh, in_specs=in_specs, out_specs=out_specs, check_vma=False)
```
